32 devices in a mesh: dp: 32 (over z, y, x, core).
Axes of the slice: x: 2, y: 2, z: 4, core: 2. Of those that a mesh axis runs over, the one named last changes fastest.
Arguments:
- inputs: bfloat16 [32768, 768], P('dp'), may hold values from -6 to 6
- cotangent: bfloat16 [32768, 768], P('dp'), may hold values from -6 to 6
- counts: int32 [32, 3], P('dp'), may hold values from 0 to 4, as said below
- lengths: int32 [32, 8], P('dp'), may hold values from 0 to 512, as said below
- owners: int32 [12], replicated, may hold values from 0 to 31, as said below
- tile_master: float32 [32, 2, 768, 768], P('dp'), may hold values from -1.1547005 to 1.1547005
- tile_first: float32 [32, 2, 768, 768], P('dp'), may hold values from -1.8 to 1.8
- tile_second: float32 [32, 2, 768, 768], P('dp'), may hold values from 0.02 to 0.4
- tile_ema: float32 [32, 2, 768, 768], P('dp'), may hold values from -1.1547005 to 1.1547005
- bias_vals: float32 [10, 768], replicated, may hold values from -1.2 to 1.2
- gain_vals: float32 [2, 768], replicated, may hold values from 0.5 to 1.5
- vector_first: float32 [12, 768], replicated, may hold values from -1.8 to 1.8
- vector_second: float32 [12, 768], replicated, may hold values from 0.02 to 0.4
- vector_ema: float32 [12, 768], replicated, may hold values from -3 to 3
Outputs:
- mixed: bfloat16 [32768, 768], P('dp')
- input_grad: float32 [32768, 768], P('dp')
- tile_weight: float32 [32, 2, 768, 768], P('dp')
- tile_first_new: float32 [32, 2, 768, 768], P('dp')
- tile_second_new: float32 [32, 2, 768, 768], P('dp')
- tile_ema_new: float32 [32, 2, 768, 768], P('dp')
- tile_copy: bfloat16 [32, 2, 768, 768], P('dp')
- vector_weight: float32 [12, 768], replicated
- vector_first_new: float32 [12, 768], replicated
- vector_second_new: float32 [12, 768], replicated
- vector_ema_new: float32 [12, 768], replicated
The draws below stay inside these ranges and needn't reach their ends.
Inputs may be any that keep to these rules, and one draw needn't show every extreme that they name: counts[d] gives device d's passages of 512, 256 and 128 slots; every device has one or more of the first kind, and its passages take half of its 1024 slots or more; on some device the counts are 1, 0 and 4. lengths[d, p] is the length of device d's passage p, passages in the order of the counts; each from a quarter of its passage's slots to all of them, 0 past the last passage; each device's first passage is full. owners[t] is the device that holds tile t; no device holds more than 2 tiles, and some device holds 2.
All inputs are finite; a program needn't handle non-finite values.
Results may differ from the reference program's by a relative error of at most 0.014.
The reference program's roundings to bfloat16 on the way count: a program that leaves them out, or rounds other values in their place, can miss the bound.
Values may be sent and summed in bfloat16 or wider, within the bound.
A program may use at most 192 MiB of HBM per device.

```python
import math
import jax
import jax.numpy as jnp
from jax import lax

D = 768
HEADS = 12
HEAD_DIM = 64
FF = 3072
TOK_DEV = 1024
BUCKET = 128
SLOTS = 2
TILES = 12
VROWS = 12
STEP = 5
TOKENS = 32768
N_DP = 32


def owner_table(key):
    key = jax.random.fold_in(key, 101)
    others = jax.random.permutation(key, N_DP - 1)
    distinct = jnp.concatenate([jnp.array([N_DP - 1], jnp.int32), others[:TILES - 2].astype(jnp.int32)])
    distinct = distinct[jax.random.permutation(jax.random.fold_in(key, 5), TILES - 1)]
    picks = jnp.concatenate([distinct[:1], distinct])
    shuffle = jax.random.permutation(jax.random.fold_in(key, 7), TILES)
    return picks[shuffle].astype(jnp.int32)


def slot_scales(owners):
    fans = jnp.array([D, D, D, max(D // 64, 1), D, D, D, D, FF, FF, FF, FF], jnp.float32)
    tile_scale = fans ** (-0.5)
    order = jnp.arange(TILES)
    slot_number = jnp.sum(((owners[:, None] == owners[None, :]) & (order[None, :] < order[:, None])).astype(jnp.int32), 1)
    hits = ((owners[None, None, :] == jnp.arange(N_DP)[:, None, None]) & (slot_number[None, None, :] == jnp.arange(SLOTS)[None, :, None])).astype(jnp.float32)
    return jnp.sum(hits * tile_scale[None, None, :], -1) + (1.0 - jnp.sum(hits, -1)) * float(D) ** (-0.5)


def bucket_plan(key):
    key = jax.random.fold_in(key, 202)
    units = TOK_DEV // BUCKET
    subkeys = jax.random.split(key, 5)
    chosen = jax.random.randint(subkeys[4], (), 0, N_DP)
    forced = jnp.arange(N_DP) == chosen
    used_units = jax.random.randint(subkeys[0], (N_DP,), max(units // 2, 4), units + 1)
    used_units = jnp.where(forced, units, used_units)
    big_count = jax.random.randint(subkeys[1], (N_DP,), 1, used_units // 4 + 1)
    big_count = jnp.where(forced, 1, big_count)
    remaining = used_units - 4 * big_count
    mid_count = jax.random.randint(subkeys[2], (N_DP,), 0, remaining // 2 + 1)
    mid_count = jnp.where(forced, 0, mid_count)
    small_count = remaining - 2 * mid_count
    counts = jnp.stack([big_count, mid_count, small_count], 1).astype(jnp.int32)
    order = jnp.arange(units)[None, :]
    slot_sizes = jnp.where(order < big_count[:, None], 4 * BUCKET, jnp.where(order < (big_count + mid_count)[:, None], 2 * BUCKET, jnp.where(order < (big_count + mid_count + small_count)[:, None], BUCKET, 0)))
    drawn = jax.random.randint(subkeys[3], (N_DP, units), slot_sizes // 4, slot_sizes + 1)
    lengths = jnp.where(order == 0, slot_sizes, drawn).astype(jnp.int32)
    return (counts, lengths)


def draw_counts(key, part):
    return bucket_plan(key)[0]


def draw_lengths(key, part):
    return bucket_plan(key)[1]


def draw_owners(key, part):
    return owner_table(key)


def draw_tile_master(key, part):
    scales = slot_scales(owner_table(key))
    key = jax.random.fold_in(key, 11)
    values = jax.random.truncated_normal(key, -4.0, 4.0, (N_DP, SLOTS, D, D), jnp.float32)
    return values * scales[:, :, None, None]


def draw_tile_ema(key, part):
    scales = slot_scales(owner_table(key))
    key = jax.random.fold_in(key, 12)
    values = jax.random.truncated_normal(key, -4.0, 4.0, (N_DP, SLOTS, D, D), jnp.float32)
    return values * scales[:, :, None, None]


def level_of(rng, shape, shards, smallest, largest):
    level, own = 1.0, jax.random.fold_in(rng, 6)
    for axis_at, parts in shards:
        steps = jnp.exp(jax.random.uniform(jax.random.fold_in(own, axis_at), (parts,), jnp.float32, smallest / len(shards), largest / len(shards)))
        level = level * jnp.repeat(steps, shape[axis_at] // parts).reshape([-1 if axis == axis_at else 1 for axis in range(len(shape))])
    return level


def scatter_about(stream_key, shape, deviation, limit, cuts=(), kind=jnp.bfloat16):
    result = jax.random.normal(stream_key, shape, jnp.float32) * deviation
    if len(cuts) > 0:
        result = level_of(stream_key, shape, cuts, -0.22, 0.18) * result
    return jnp.clip(result, min=-limit, max=limit).astype(kind)


def setup_inputs(seed: int = 0) -> dict:
    seeds = jax.random.split(jax.random.key(seed), 15)
    inputs = scatter_about(seeds[0], (TOKENS, D), 1.0, 6.0, ((0, 32),))
    cotangent = scatter_about(seeds[1], (TOKENS, D), 1.0, 6.0, ((0, 32),))
    counts = draw_counts(jax.random.fold_in(seeds[14], 71), 0)
    lengths = draw_lengths(jax.random.fold_in(seeds[14], 71), 0)
    owners = draw_owners(jax.random.fold_in(seeds[14], 71), 0)
    tile_master = draw_tile_master(jax.random.fold_in(seeds[14], 71), 0)
    tile_first = scatter_about(seeds[6], (N_DP, SLOTS, D, D), 0.3, 1.8, ((0, 32),), jnp.float32)
    tile_second = jnp.clip(jnp.exp(math.log(0.4) - 2.9957323 * jax.random.uniform(seeds[7], (N_DP, SLOTS, D, D), jnp.float32) ** level_of(seeds[7], (N_DP, SLOTS, D, D), ((0, 32),), -0.2, 0.2)), 0.02, 0.4)
    tile_ema = draw_tile_ema(jax.random.fold_in(seeds[14], 71), 0)
    bias_vals = scatter_about(seeds[9], (10, D), 0.2, 1.2, (), jnp.float32)
    gain_vals = jnp.clip(1.0 + 0.1 * jax.random.normal(seeds[10], (2, D), jnp.float32), 0.5, 1.5)
    vector_first = scatter_about(seeds[11], (VROWS, D), 0.3, 1.8, (), jnp.float32)
    vector_second = jnp.clip(jnp.exp(jax.random.uniform(seeds[12], (VROWS, D), jnp.float32, math.log(0.02), math.log(0.4))), 0.02, 0.4)
    vector_ema = scatter_about(seeds[13], (VROWS, D), 0.5, 3.0, (), jnp.float32)
    return dict(inputs=inputs, cotangent=cotangent, counts=counts, lengths=lengths, owners=owners, tile_master=tile_master, tile_first=tile_first, tile_second=tile_second, tile_ema=tile_ema, bias_vals=bias_vals, gain_vals=gain_vals, vector_first=vector_first, vector_second=vector_second, vector_ema=vector_ema)


@jax.custom_vjp
def low(v):
    return lax.optimization_barrier(v.astype(jnp.bfloat16)).astype(jnp.float32)

@jax.custom_vjp
def low_back(v):
    return v

def low_keep(v):
    return (low(v), None)

def low_pass(kept, grad):
    return (grad,)

def back_keep(v):
    return (v, None)

def back_low(kept, grad):
    return (low(grad),)
low.defvjp(low_keep, low_pass)
low_back.defvjp(back_keep, back_low)
highest = lax.Precision.HIGHEST
norm_epsilon = 1e-12
tile_rate = 0.03
vector_rate = 0.2
first_decay = 0.5
second_decay = 0.5
adam_epsilon = 1e-08
weight_decay = 0.01
average_rate = 0.9

def passage_layout(counts, lengths, tokens, bucket):
    places = lengths.shape[0]
    order = jnp.arange(places, dtype=jnp.int32)
    big_end = counts[0]
    mid_end = big_end + counts[1]
    all_end = mid_end + counts[2]
    slot_sizes = jnp.where(order < big_end, 4 * bucket, jnp.where(order < mid_end, 2 * bucket, jnp.where(order < all_end, bucket, 0))).astype(jnp.int32)
    starts = (jnp.cumsum(slot_sizes) - slot_sizes).astype(jnp.int32)
    position = jnp.arange(tokens, dtype=jnp.int32)[:, None]
    inside = (position >= starts[None, :]) & (position < (starts + slot_sizes)[None, :])
    live_mask = inside & (position < (starts + lengths)[None, :])
    usable = lax.optimization_barrier(jnp.sum(live_mask.astype(jnp.int32), 1)).astype(jnp.int32)
    member = lax.optimization_barrier(jnp.sum(jnp.where(inside, order[None, :] + 1, 0), 1)).astype(jnp.int32)
    passage_ids = jnp.where(member > 0, member - 1, places + position[:, 0] // bucket)
    return (usable, passage_ids.astype(jnp.int32))

def tile_slots(owners):
    order = jnp.arange(owners.shape[0], dtype=jnp.int32)
    same = owners[:, None] == owners[None, :]
    earlier = order[None, :] < order[:, None]
    return lax.optimization_barrier(jnp.sum((same & earlier).astype(jnp.int32), 1)).astype(jnp.int32)

def block_mask(usable, passage_ids, blocks, block_rows):
    usable_rows = usable.reshape(blocks, block_rows)
    id_rows = passage_ids.reshape(blocks, block_rows)
    diagonal = jnp.arange(block_rows)[:, None] == jnp.arange(block_rows)[None, :]
    return (id_rows[:, :, None] == id_rows[:, None, :]) & ((usable_rows[:, None, :] == 1) | diagonal[None])

def layer_norm(values, gain, shift):
    center = lax.optimization_barrier(jnp.mean(values, -1, keepdims=True))
    centered = values - center
    spread = lax.optimization_barrier(jnp.mean(centered * centered, -1, keepdims=True))
    return centered * lax.rsqrt(spread + norm_epsilon) * gain + shift

def adam_update(param, grad, first, second, rate):
    first_new = first_decay * first + (1.0 - first_decay) * grad
    second_new = second_decay * second + (1.0 - second_decay) * grad * grad
    first_hat = first_new / (1.0 - first_decay ** STEP)
    second_hat = second_new / (1.0 - second_decay ** STEP)
    param_new = param - rate * (first_hat / (jnp.sqrt(second_hat) + adam_epsilon) + weight_decay * param)
    return (param_new, first_new, second_new)

def attend_block(block_items):
    query, keyed, valued, allowed = block_items
    raw_scores = jnp.einsum('qhd,khd->hqk', query, keyed, precision=highest)
    scores = low_back(raw_scores * HEAD_DIM ** (-0.5))
    masked = jnp.where(allowed[None], scores, -1000000000.0)
    highest_score = lax.optimization_barrier(jnp.max(masked, -1, keepdims=True))
    exponent = jnp.exp(masked - highest_score)
    probability = low(exponent / lax.optimization_barrier(jnp.sum(exponent, -1, keepdims=True)))
    return jnp.einsum('hqk,khd->qhd', probability, valued, precision=highest)

def device_layer(x_dev, usable, passage_ids, weights, vectors):
    w_query, w_key, w_value, w_out, w_up, w_down = weights
    tokens = x_dev.shape[0]
    block_rows = 4 * BUCKET
    blocks = tokens // block_rows
    query = low(low_back(jnp.dot(x_dev, w_query, precision=highest) + vectors[0]))
    keyed = low(low_back(jnp.dot(x_dev, w_key, precision=highest)))
    valued = low(low_back(jnp.dot(x_dev, w_value, precision=highest) + vectors[1]))
    allowed = block_mask(usable, passage_ids, blocks, block_rows)

    def split_heads(values):
        return values.reshape(blocks, block_rows, HEADS, HEAD_DIM)
    context = lax.map(jax.checkpoint(attend_block), (split_heads(query), split_heads(keyed), split_heads(valued), allowed))
    context = low(low_back(context.reshape(tokens, D)))
    branch = low_back(jnp.dot(context, w_out, precision=highest) + vectors[2])
    hidden = layer_norm(x_dev + branch, vectors[10], vectors[8])
    upward = low_back(jnp.dot(low(hidden), w_up, precision=highest) + vectors[3:7].reshape(FF))
    active = low(jax.nn.gelu(upward, approximate=False))
    downward = low_back(jnp.dot(active, w_down, precision=highest) + vectors[7])
    normed = layer_norm(hidden + downward, vectors[11], vectors[9])
    return normed * usable.astype(jnp.float32)[:, None]

def reference(inputs, cotangent, counts, lengths, owners, tile_master, tile_first, tile_second, tile_ema, bias_vals, gain_vals, vector_first, vector_second, vector_ema):
    slots = tile_slots(owners)
    tiles = tile_master[owners, slots]
    vectors = jnp.concatenate([bias_vals, gain_vals], 0)
    usable, passage_ids = jax.vmap(passage_layout, in_axes=(0, 0, None, None))(counts, lengths, TOK_DEV, BUCKET)
    x_all = inputs.astype(jnp.float32).reshape(N_DP, TOK_DEV, D)

    def forward(x_all, tiles, vectors):
        low_tiles = [low(tiles[tile_number]) for tile_number in range(TILES)]
        weights = (low_tiles[0], low_tiles[1], low_tiles[2], low_tiles[3], jnp.concatenate(low_tiles[4:8], 1), jnp.concatenate(low_tiles[8:12], 0))
        layer = jax.checkpoint(device_layer)

        def step(carry, items):
            return (carry, layer(items[0], items[1], items[2], weights, vectors))
        carry_out, outputs = lax.scan(step, jnp.zeros((), jnp.float32), (x_all, usable, passage_ids))
        return outputs
    outputs, pullback = jax.vjp(forward, x_all, tiles, vectors)
    grad_inputs, grad_tiles, grad_vectors = pullback(cotangent.astype(jnp.float32).reshape(N_DP, TOK_DEV, D))
    gain_scale = float(TOKENS) ** (-0.5)
    grad_slots = jnp.zeros(tile_master.shape, jnp.float32).at[owners, slots].set(grad_tiles * gain_scale)
    tile_weight, tile_first_new, tile_second_new = adam_update(tile_master, grad_slots, tile_first, tile_second, tile_rate)
    tile_ema_new = average_rate * tile_ema + (1.0 - average_rate) * tile_weight
    vector_weight, vector_first_new, vector_second_new = adam_update(vectors, grad_vectors * gain_scale, vector_first, vector_second, vector_rate)
    vector_ema_new = average_rate * vector_ema + (1.0 - average_rate) * vector_weight
    return (outputs.reshape(TOKENS, D).astype(jnp.bfloat16), grad_inputs.reshape(TOKENS, D), tile_weight, tile_first_new, tile_second_new, tile_ema_new, tile_weight.astype(jnp.bfloat16), vector_weight, vector_first_new, vector_second_new, vector_ema_new)
```

```python
import jax
import jax.numpy as jnp
from jax import lax
from jax.experimental import pallas as pl
from jax.experimental.pallas import tpu as pltpu
from jax.sharding import PartitionSpec as P

HEADS = 12
BUCKET = 128
SLOTS = 2
TILES = 12
VROWS = 12
STEP = 5


highest = lax.Precision.HIGHEST
norm_epsilon = 1e-12
tile_rate = 0.03
vector_rate = 0.2
first_decay = 0.5
second_decay = 0.5
adam_epsilon = 1e-08
weight_decay = 0.01
average_rate = 0.9


def from_root(block, axis, holder):
    block = jnp.where(lax.axis_index(axis) == holder, block, jnp.zeros_like(block))
    return lax.psum(block, axis)


def passage_layout(counts, lengths, tokens, bucket):
    places = lengths.shape[0]
    order = jnp.arange(places, dtype=jnp.int32)
    big_end = counts[0]
    mid_end = big_end + counts[1]
    all_end = mid_end + counts[2]
    slot_sizes = jnp.where(
        order < big_end,
        4 * bucket,
        jnp.where(order < mid_end, 2 * bucket, jnp.where(order < all_end, bucket, 0)),
    ).astype(jnp.int32)
    starts = jnp.cumsum(slot_sizes) - slot_sizes
    position = jnp.arange(tokens, dtype=jnp.int32)[:, None]
    inside = (position >= starts[None, :]) & (position < (starts + slot_sizes)[None, :])
    live_mask = inside & (position < (starts + lengths)[None, :])
    usable = jnp.sum(live_mask.astype(jnp.int32), 1)
    member = jnp.sum(jnp.where(inside, order[None, :] + 1, 0), 1)
    passage_ids = jnp.where(member > 0, member - 1, places + position[:, 0] // bucket)
    return (usable, passage_ids)


def tile_slots(owners):
    order = jnp.arange(owners.shape[0], dtype=jnp.int32)
    same = owners[:, None] == owners[None, :]
    earlier = order[None, :] < order[:, None]
    return jnp.sum((same & earlier).astype(jnp.int32), 1)


def block_mask(usable, passage_ids, blocks, block_rows):
    usable_rows = usable.reshape(blocks, block_rows)
    id_rows = passage_ids.reshape(blocks, block_rows)
    diagonal = jnp.arange(block_rows)[:, None] == jnp.arange(block_rows)[None, :]
    return (id_rows[:, :, None] == id_rows[:, None, :]) & (
        (usable_rows[:, None, :] == 1) | diagonal[None]
    )


def layer_norm(values, gain, shift):
    center = jnp.mean(values, -1, keepdims=True)
    centered = values - center
    spread = jnp.mean(centered * centered, -1, keepdims=True)
    return centered * lax.rsqrt(spread + norm_epsilon) * gain + shift


def exact_gelu(values):
    return jax.nn.gelu(values, approximate=False)


def adam_update(param, grad, first, second, rate):
    first_new = first_decay * first + (1.0 - first_decay) * grad
    second_new = second_decay * second + (1.0 - second_decay) * grad * grad
    first_hat = first_new / (1.0 - first_decay**STEP)
    second_hat = second_new / (1.0 - second_decay**STEP)
    param_new = param - rate * (
        first_hat / (jnp.sqrt(second_hat) + adam_epsilon) + weight_decay * param
    )
    return (param_new, first_new, second_new)


def fetch_forward(tile_master, slots, owners, tile_number):
    local = lax.dynamic_index_in_dim(tile_master[0], slots[tile_number], 0, keepdims=False).astype(
        jnp.bfloat16
    )
    return from_root(local, "dp", owners[tile_number])


MESH = pl.DeviceIdType.MESH
GROUP = 32
CHIPS = 16
SPAN = 48
HALF = 384
PAIRS = TILES // 2


def remote(src, dst, send, recv, device):
    return pltpu.make_async_remote_copy(
        src_ref=src, dst_ref=dst, send_sem=send, recv_sem=recv, device_id=(device,), device_id_type=MESH
    )


def place(device):
    core = lax.rem(device, 2)
    x = lax.rem(device // 2, 2)
    y = lax.rem(device // 4, 2)
    z = device // 8
    return z, y, x, core


def greet_all(me):
    barrier = pltpu.get_barrier_semaphore()

    def greet(step, carry):
        pl.semaphore_signal(
            barrier, inc=1, device_id=(lax.rem(me + step, GROUP),), device_id_type=MESH
        )
        return carry

    lax.fori_loop(1, GROUP, greet, 0)
    pl.semaphore_wait(barrier, GROUP - 1)


def lanes(core):
    return pl.ds(pl.multiple_of(core * HALF, HALF), HALF)


def span(z):
    return pl.ds(pl.multiple_of(z * SPAN, 16), SPAN)


def gather_tiles(
    picks,
    slot_ref,
    w_ref,
    stage,
    chunk,
    swap_send,
    swap_recv,
    own_sem,
    z_send,
    z_recv,
    mid_send,
    mid_recv,
    far_send,
    far_recv,
    core_send,
    core_recv,
):
    me = lax.axis_index("dp")
    z, y, x, core = place(me)
    sibling = me + 1 - 2 * core
    x_peer = me + 2 - 4 * x
    y_peer = me + 4 - 8 * y
    cols = lanes(core)
    rows = span(z)
    greet_all(me)

    def swap(step, carry):
        target = lax.rem(me + step, GROUP)
        tz, ty, tx, tc = place(target)
        remote(
            slot_ref.at[:, tx, ty, span(tz), lanes(tc)],
            stage.at[pl.ds(2 * me, 2)],
            swap_send,
            swap_recv,
            target,
        ).start()
        return carry

    lax.fori_loop(1, GROUP, swap, 0)
    mine = pltpu.make_async_copy(
        slot_ref.at[:, x, y, rows, cols], stage.at[pl.ds(2 * me, 2)], own_sem.at[0]
    )
    mine.start()
    mine.wait()
    most = stage.at[pl.ds(0, 2 * GROUP - 2)]
    pltpu.make_async_copy(most, most, swap_recv).wait()
    for tile in range(TILES):
        chunk[tile] = stage[picks[tile]]

    keep = [
        pltpu.make_async_copy(
            chunk.at[pl.ds(2 * pair, 2)],
            w_ref.at[pl.ds(2 * pair, 2), x, y, rows, cols],
            own_sem.at[1 + pair],
        )
        for pair in range(PAIRS)
    ]
    z_copies = []
    for pair in range(PAIRS):
        keep[pair].start()
        group = []
        for hop in range(1, 4):
            target = lax.rem(z + hop, 4) * 8 + lax.rem(me, 8)
            copy = remote(
                chunk.at[pl.ds(2 * pair, 2)],
                w_ref.at[pl.ds(2 * pair, 2), x, y, rows, cols],
                z_send.at[pair, hop - 1],
                z_recv.at[pair, hop - 1],
                target,
            )
            copy.start()
            group.append(copy)
        z_copies.append(group)

    def mid(pair):
        a, b = 2 * pair, 2 * pair + 1
        block_a = w_ref.at[a, x, y, :, cols]
        block_b = w_ref.at[b, x, y, :, cols]
        return [
            remote(block_a, block_a, mid_send.at[a], mid_recv.at[a], y_peer),
            remote(block_b, block_b, mid_send.at[b], mid_recv.at[b], x_peer),
        ]

    def far(pair):
        a, b = 2 * pair, 2 * pair + 1
        block_a = w_ref.at[a, x, :, :, cols]
        block_b = w_ref.at[b, :, y, :, cols]
        return [
            remote(block_a, block_a, far_send.at[a], far_recv.at[a], x_peer),
            remote(block_b, block_b, far_send.at[b], far_recv.at[b], y_peer),
        ]

    def near(pair, last):
        a, b = 2 * pair, 2 * pair + 1
        if last:
            block_a = w_ref.at[a, 1 - x, :, :, cols]
            block_b = w_ref.at[b, :, 1 - y, :, cols]
        else:
            block_a = w_ref.at[a, x, :, :, cols]
            block_b = w_ref.at[b, :, y, :, cols]
        at = 1 if last else 0
        return [
            remote(block_a, block_a, core_send.at[a, at], core_recv.at[a, at], sibling),
            remote(block_b, block_b, core_send.at[b, at], core_recv.at[b, at], sibling),
        ]

    mids, fars, nears = {}, {}, {}
    for step in range(PAIRS + 2):
        if step < PAIRS:
            keep[step].wait()
            for copy in z_copies[step]:
                copy.wait_recv()
            mids[step] = mid(step)
            for copy in mids[step]:
                copy.start()
        if 0 <= step - 1 < PAIRS:
            for copy in mids[step - 1]:
                copy.wait_recv()
            fars[step - 1] = far(step - 1)
            nears[step - 1] = near(step - 1, False)
            for copy in fars[step - 1] + nears[step - 1]:
                copy.start()
        if 0 <= step - 2 < PAIRS:
            for copy in fars[step - 2]:
                copy.wait_recv()
            late = near(step - 2, True)
            for copy in late:
                copy.start()
            nears[step - 2] += late
    for pair in range(PAIRS):
        for copy in nears[pair]:
            copy.wait_recv()
    for pair in range(PAIRS):
        for copy in z_copies[pair] + mids[pair] + fars[pair] + nears[pair]:
            copy.wait_send()
    pltpu.make_async_copy(most, most, swap_send).wait()


def gathered_tiles(tile_low, picks):
    any_space = pl.BlockSpec(memory_space=pl.ANY)
    dma = pltpu.SemaphoreType.DMA
    low = jnp.bfloat16
    return pl.pallas_call(
        gather_tiles,
        out_shape=jax.ShapeDtypeStruct((TILES, 2, 2, 4 * SPAN, 2 * HALF), low),
        in_specs=[pl.BlockSpec(memory_space=pltpu.SMEM), any_space],
        out_specs=any_space,
        scratch_shapes=[
            pltpu.VMEM((2 * GROUP, SPAN, HALF), low),
            pltpu.VMEM((TILES, SPAN, HALF), low),
            dma,
            dma,
            dma((1 + PAIRS,)),
            dma((PAIRS, 3)),
            dma((PAIRS, 3)),
            dma((TILES,)),
            dma((TILES,)),
            dma((TILES,)),
            dma((TILES,)),
            dma((TILES, 2)),
            dma((TILES, 2)),
        ],
        compiler_params=pltpu.CompilerParams(collective_id=0, has_side_effects=True),
        name="gather_tiles",
    )(picks, tile_low.reshape(2, 2, 2, 4 * SPAN, 2 * HALF))


def reduce_tiles(
    holds,
    keep_slot,
    part_ref,
    vec_ref,
    slot_grad,
    vec_out,
    mine,
    from_core,
    from_far,
    from_mid,
    from_z,
    outbox,
    vec_now,
    vec_in,
    own_sem,
    core_send,
    core_recv,
    far_send,
    far_recv,
    mid_send,
    mid_recv,
    z_send,
    z_recv,
    vec_send,
    vec_recv,
    swap_send,
    swap_recv,
):
    me = lax.axis_index("dp")
    z, y, x, core = place(me)
    sibling = me + 1 - 2 * core
    x_peer = me + 2 - 4 * x
    y_peer = me + 4 - 8 * y
    cols = lanes(core)
    rows = span(z)
    greet_all(me)

    own, to_core = [], []
    for pair in range(PAIRS):
        two = pl.ds(2 * pair, 2)
        own.append(pltpu.make_async_copy(part_ref.at[two, :, :, :, cols], mine.at[two], own_sem.at[pair]))
        to_core.append(
            remote(
                part_ref.at[two, :, :, :, lanes(1 - core)],
                from_core.at[two],
                core_send.at[pair],
                core_recv.at[pair],
                sibling,
            )
        )
        to_core[pair].start()
        own[pair].start()

    vec_copies = []

    def vec_step(number, device):
        copy = remote(vec_now.at[number], vec_in.at[number], vec_send.at[number], vec_recv.at[number], device)
        copy.start()
        vec_copies.append(copy)

    vec_now[0] = vec_ref[...]
    vec_step(0, sibling)

    def far(pair):
        a, b = 2 * pair, 2 * pair + 1
        return [
            remote(mine.at[a, 1 - x], from_far.at[a], far_send.at[a], far_recv.at[a], x_peer),
            remote(mine.at[b, :, 1 - y], from_far.at[b], far_send.at[b], far_recv.at[b], y_peer),
        ]

    def mid(pair):
        a, b = 2 * pair, 2 * pair + 1
        return [
            remote(mine.at[a, x, 1 - y], from_mid.at[a], mid_send.at[a], mid_recv.at[a], y_peer),
            remote(mine.at[b, 1 - x, y], from_mid.at[b], mid_send.at[b], mid_recv.at[b], x_peer),
        ]

    def along_z(pair):
        two = pl.ds(2 * pair, 2)
        copies = []
        for hop in range(1, 4):
            tz = lax.rem(z + hop, 4)
            copies.append(
                remote(
                    mine.at[two, x, y, span(tz)],
                    from_z.at[hop - 1, two],
                    z_send.at[pair, hop - 1],
                    z_recv.at[pair, hop - 1],
                    tz * 8 + lax.rem(me, 8),
                )
            )
        return copies

    fars, mids, zs = {}, {}, {}
    for step in range(PAIRS + 3):
        if step < PAIRS:
            pair = step
            own[pair].wait()
            to_core[pair].wait_recv()
            for tile in (2 * pair, 2 * pair + 1):
                mine[tile] = mine[tile] + from_core[tile]
            fars[pair] = far(pair)
            for copy in fars[pair]:
                copy.start()
        if 0 <= step - 1 < PAIRS:
            pair = step - 1
            a, b = 2 * pair, 2 * pair + 1
            for copy in fars[pair]:
                copy.wait_recv()
            mine[a, x] = mine[a, x] + from_far[a]
            mine[b, :, y] = mine[b, :, y] + from_far[b]
            mids[pair] = mid(pair)
            for copy in mids[pair]:
                copy.start()
        if 0 <= step - 2 < PAIRS:
            pair = step - 2
            a, b = 2 * pair, 2 * pair + 1
            for copy in mids[pair]:
                copy.wait_recv()
            mine[a, x, y] = mine[a, x, y] + from_mid[a]
            mine[b, x, y] = mine[b, x, y] + from_mid[b]
            zs[pair] = along_z(pair)
            for copy in zs[pair]:
                copy.start()
        if 0 <= step - 3 < PAIRS:
            pair = step - 3
            for copy in zs[pair]:
                copy.wait_recv()
            for tile in (2 * pair, 2 * pair + 1):
                total = mine[tile, x, y, rows].astype(jnp.float32)
                for hop in range(3):
                    total = total + from_z[hop, tile].astype(jnp.float32)
                from_z[0, tile] = total.astype(jnp.bfloat16)
        if step == 1:
            vec_copies[0].wait_recv()
            vec_now[1] = vec_now[0] + vec_in[0]
            vec_step(1, x_peer)
        if step == 2:
            vec_copies[1].wait_recv()
            vec_now[2] = vec_now[1] + vec_in[1]
            vec_step(2, y_peer)
        if step == 4:
            vec_copies[2].wait_recv()
            vec_now[3] = vec_now[2] + vec_in[2]
            for hop in range(1, 4):
                copy = remote(
                    vec_now.at[3],
                    vec_in.at[2 + hop],
                    vec_send.at[2 + hop],
                    vec_recv.at[2 + hop],
                    lax.rem(z + hop, 4) * 8 + lax.rem(me, 8),
                )
                copy.start()
                vec_copies.append(copy)

    for copy in vec_copies[3:]:
        copy.wait_recv()
    total = jnp.zeros_like(vec_out)
    for source in range(4):
        hop = lax.rem(z - source + 4, 4)
        total = total + jnp.where(hop == 0, vec_now[3], vec_in[2 + jnp.maximum(hop, 1)])
    vec_out[...] = total

    def fill(at, carry):
        tile = holds[at]
        value = from_z[0, tile]
        outbox[at] = jnp.where(keep_slot[at] > 0, value, jnp.zeros_like(value))
        return carry

    lax.fori_loop(0, 2 * GROUP, fill, 0)
    local = pltpu.make_async_copy(
        outbox.at[pl.ds(2 * me, 2)], slot_grad.at[:, x, y, rows, cols], own_sem.at[PAIRS]
    )
    local.start()

    def swap(step, carry):
        target = lax.rem(me + step, GROUP)
        remote(
            outbox.at[pl.ds(2 * target, 2)],
            slot_grad.at[:, x, y, rows, cols],
            swap_send,
            swap_recv,
            target,
        ).start()
        return carry

    lax.fori_loop(1, GROUP, swap, 0)
    local.wait()
    for group in [to_core] + list(fars.values()) + list(mids.values()) + list(zs.values()) + [vec_copies]:
        for copy in group:
            copy.wait_send()
    most = outbox.at[pl.ds(0, 2 * GROUP - 2)]
    pltpu.make_async_copy(most, most, swap_recv).wait()
    pltpu.make_async_copy(most, most, swap_send).wait()


def reduced_tiles(parts, vector_terms, holds, keep_slot):
    any_space = pl.BlockSpec(memory_space=pl.ANY)
    vmem = pl.BlockSpec(memory_space=pltpu.VMEM)
    smem = pl.BlockSpec(memory_space=pltpu.SMEM)
    dma = pltpu.SemaphoreType.DMA
    low = jnp.bfloat16
    vec_rows = vector_terms.shape[0]
    return pl.pallas_call(
        reduce_tiles,
        out_shape=(
            jax.ShapeDtypeStruct((SLOTS, 2, 2, 4 * SPAN, 2 * HALF), low),
            jax.ShapeDtypeStruct(vector_terms.shape, jnp.float32),
        ),
        in_specs=[smem, smem, any_space, vmem],
        out_specs=(any_space, vmem),
        scratch_shapes=[
            pltpu.VMEM((TILES, 2, 2, 4 * SPAN, HALF), low),
            pltpu.VMEM((TILES, 2, 2, 4 * SPAN, HALF), low),
            pltpu.VMEM((TILES, 2, 4 * SPAN, HALF), low),
            pltpu.VMEM((TILES, 4 * SPAN, HALF), low),
            pltpu.VMEM((3, TILES, SPAN, HALF), low),
            pltpu.VMEM((2 * GROUP, SPAN, HALF), low),
            pltpu.VMEM((4, vec_rows, 2 * HALF), jnp.float32),
            pltpu.VMEM((6, vec_rows, 2 * HALF), jnp.float32),
            dma((PAIRS + 1,)),
            dma((PAIRS,)),
            dma((PAIRS,)),
            dma((TILES,)),
            dma((TILES,)),
            dma((TILES,)),
            dma((TILES,)),
            dma((PAIRS, 3)),
            dma((PAIRS, 3)),
            dma((6,)),
            dma((6,)),
            dma,
            dma,
        ],
        compiler_params=pltpu.CompilerParams(
            collective_id=1, has_side_effects=True, vmem_limit_bytes=56 * 2**20
        ),
        name="reduce_tiles",
    )(holds, keep_slot, parts.reshape(TILES, 2, 2, 4 * SPAN, 2 * HALF), vector_terms)


def assemble(tiles):
    return (
        tiles[0],
        tiles[1],
        tiles[2],
        tiles[3],
        jnp.concatenate(tiles[4:8], 1),
        jnp.concatenate(tiles[8:12], 0),
    )


def attend_block(block_items, score_scale):
    query, keyed, valued, allowed = block_items
    raw_scores = (
        jnp.einsum("qhd,khd->hqk", query, keyed, preferred_element_type=jnp.float32) * score_scale
    )
    masked = jnp.where(allowed[None], raw_scores, -1000000000.0)
    highest_score = jnp.max(masked, -1, keepdims=True)
    exponent = jnp.exp(masked - highest_score)
    totals = jnp.sum(exponent, -1, keepdims=True)
    probability = (exponent / totals).astype(jnp.bfloat16)
    context = jnp.einsum("hqk,khd->qhd", probability, valued, preferred_element_type=jnp.float32)
    return (context, highest_score[..., 0] + jnp.log(totals[..., 0]))


def attend_back(block_items, score_scale):
    query, keyed, valued, allowed, grad_context, log_totals = block_items
    raw_scores = (
        jnp.einsum("qhd,khd->hqk", query, keyed, preferred_element_type=jnp.float32) * score_scale
    )
    masked = jnp.where(allowed[None], raw_scores, -1000000000.0)
    probability = jnp.exp(masked - log_totals[..., None])
    grad_valued = jnp.einsum(
        "hqk,qhd->khd",
        probability.astype(jnp.bfloat16),
        grad_context,
        preferred_element_type=jnp.float32,
    )
    grad_prob = jnp.einsum("qhd,khd->hqk", grad_context, valued, preferred_element_type=jnp.float32)
    row_total = jnp.sum(probability * grad_prob, -1, keepdims=True)
    grad_scores = (probability * (grad_prob - row_total)).astype(jnp.bfloat16)
    grad_query = (
        jnp.einsum("hqk,khd->qhd", grad_scores, keyed, preferred_element_type=jnp.float32)
        * score_scale
    )
    grad_keyed = (
        jnp.einsum("hqk,qhd->khd", grad_scores, query, preferred_element_type=jnp.float32)
        * score_scale
    )
    return (grad_query, grad_keyed, grad_valued)


def outer(left, right):
    return lax.dot_general(
        left, right, (((0,), (0,)), ((), ())), preferred_element_type=jnp.float32
    )


def summed_over_slice(stacked, vector_terms, owners, slots, gain_scale):
    model_width = stacked.shape[1]
    summed_rows = lax.psum_scatter(stacked, "dp", scatter_dimension=0, tiled=True)
    full_rows = lax.all_gather(summed_rows, "dp", axis=0, tiled=True)
    tile_grads = full_rows.reshape(TILES, model_width, model_width) * gain_scale
    myself = lax.axis_index("dp")
    slot_list = []
    for slot_number in range(SLOTS):
        select = ((owners == myself) & (slots == slot_number)).astype(jnp.float32)
        slot_list.append(jnp.tensordot(select, tile_grads, 1, precision=highest))
    return jnp.stack(slot_list, 0)[None], lax.psum(vector_terms, "dp")


def body(
    inputs,
    cotangent,
    counts,
    lengths,
    owners,
    tile_master,
    tile_first,
    tile_second,
    tile_ema,
    bias_vals,
    gain_vals,
    vector_first,
    vector_second,
    vector_ema,
):
    tokens, model_width = inputs.shape
    head_dim = model_width // HEADS
    block_rows = 4 * BUCKET
    blocks = tokens // block_rows
    score_scale = head_dim ** (-0.5)
    usable, passage_ids = passage_layout(counts[0], lengths[0], tokens, BUCKET)
    live_rows = usable.astype(jnp.float32)[:, None]
    allowed = block_mask(usable, passage_ids, blocks, block_rows)
    slots = tile_slots(owners)
    vectors = jnp.concatenate([bias_vals, gain_vals], 0)

    def split_heads(values):
        return values.reshape(blocks, block_rows, HEADS, head_dim)

    def merge_heads(values):
        return values.reshape(tokens, model_width)

    small = lax.axis_size("dp") == GROUP
    if small:
        gathered = gathered_tiles(tile_master[0].astype(jnp.bfloat16), owners * SLOTS + slots)
        gathered = gathered.reshape(TILES, model_width, model_width)
        forward_tiles = [gathered[tile_number] for tile_number in range(TILES)]
    else:
        forward_tiles = [
            fetch_forward(tile_master, slots, owners, tile_number) for tile_number in range(TILES)
        ]
    w_query, w_key, w_value, w_out, w_up, w_down = assemble(forward_tiles)
    query = (jnp.dot(inputs, w_query, preferred_element_type=jnp.float32) + vectors[0]).astype(
        jnp.bfloat16
    )
    keyed = jnp.dot(inputs, w_key, preferred_element_type=jnp.float32).astype(jnp.bfloat16)
    valued = (jnp.dot(inputs, w_value, preferred_element_type=jnp.float32) + vectors[1]).astype(
        jnp.bfloat16
    )
    context, log_totals = lax.map(
        lambda block_items: attend_block(block_items, score_scale),
        (split_heads(query), split_heads(keyed), split_heads(valued), allowed),
    )
    context_low = merge_heads(context).astype(jnp.bfloat16)
    branch = jnp.dot(context_low, w_out, preferred_element_type=jnp.float32) + vectors[2]
    hidden, norm_one_back = jax.vjp(
        layer_norm, inputs.astype(jnp.float32) + branch, vectors[10], vectors[8]
    )
    hidden_low = hidden.astype(jnp.bfloat16)
    upward = jnp.dot(hidden_low, w_up, preferred_element_type=jnp.float32) + vectors[3:7].reshape(
        -1
    )
    active, gelu_back = jax.vjp(exact_gelu, upward)
    active_low = active.astype(jnp.bfloat16)
    downward = jnp.dot(active_low, w_down, preferred_element_type=jnp.float32) + vectors[7]
    normed, norm_two_back = jax.vjp(layer_norm, hidden + downward, vectors[11], vectors[9])
    mixed = (normed * live_rows).astype(jnp.bfloat16)
    grad_second, grad_gain_two, grad_shift_two = norm_two_back(
        cotangent.astype(jnp.float32) * live_rows
    )
    grad_down = grad_second.astype(jnp.bfloat16)
    grad_active = jnp.einsum("nd,fd->nf", grad_down, w_down, preferred_element_type=jnp.float32)
    grad_up = gelu_back(grad_active)[0].astype(jnp.bfloat16)
    grad_hidden = grad_second + jnp.einsum(
        "nf,df->nd", grad_up, w_up, preferred_element_type=jnp.float32
    )
    grad_first, grad_gain_one, grad_shift_one = norm_one_back(grad_hidden)
    grad_branch = grad_first.astype(jnp.bfloat16)
    grad_context = jnp.einsum(
        "nd,ed->ne", grad_branch, w_out, preferred_element_type=jnp.float32
    ).astype(jnp.bfloat16)
    grad_query, grad_keyed, grad_valued = lax.map(
        lambda block_items: attend_back(block_items, score_scale),
        (
            split_heads(query),
            split_heads(keyed),
            split_heads(valued),
            allowed,
            split_heads(grad_context),
            log_totals,
        ),
    )
    grad_query = merge_heads(grad_query).astype(jnp.bfloat16)
    grad_keyed = merge_heads(grad_keyed).astype(jnp.bfloat16)
    grad_valued = merge_heads(grad_valued).astype(jnp.bfloat16)
    input_grad = grad_first + jnp.einsum(
        "nd,ed->ne", grad_query, w_query, preferred_element_type=jnp.float32
    )
    input_grad = input_grad + jnp.einsum(
        "nd,ed->ne", grad_keyed, w_key, preferred_element_type=jnp.float32
    )
    input_grad = input_grad + jnp.einsum(
        "nd,ed->ne", grad_valued, w_value, preferred_element_type=jnp.float32
    )
    pieces = [
        outer(inputs, grad_query),
        outer(inputs, grad_keyed),
        outer(inputs, grad_valued),
        outer(context_low, grad_branch),
    ]
    pieces += [
        outer(hidden_low, grad_up[:, column * model_width : (column + 1) * model_width])
        for column in range(4)
    ]
    pieces.append(outer(active_low, grad_down))
    column_sums = [
        jnp.sum(grad_query, 0, dtype=jnp.float32)[None],
        jnp.sum(grad_valued, 0, dtype=jnp.float32)[None],
        jnp.sum(grad_branch, 0, dtype=jnp.float32)[None],
        jnp.sum(grad_up, 0, dtype=jnp.float32).reshape(4, model_width),
        jnp.sum(grad_down, 0, dtype=jnp.float32)[None],
        grad_shift_one[None],
        grad_shift_two[None],
        grad_gain_one[None],
        grad_gain_two[None],
    ]
    gain_scale = float(tokens * lax.axis_size("dp")) ** (-0.5)
    if small:
        stacked = jnp.concatenate([piece.astype(jnp.bfloat16) for piece in pieces], 0)
        vector_terms = jnp.concatenate(
            column_sums + [jnp.zeros((16 - VROWS, model_width), jnp.float32)], 0
        )
        places = jnp.arange(SLOTS * GROUP, dtype=jnp.int32)
        match = (owners * SLOTS + slots)[None, :] == places[:, None]
        holds = jnp.sum(jnp.where(match, jnp.arange(TILES, dtype=jnp.int32)[None, :], 0), 1)
        keep_slot = jnp.sum(match.astype(jnp.int32), 1)
        slot_sums, full_vector = reduced_tiles(stacked, vector_terms, holds, keep_slot)
        slot_grads = slot_sums.reshape(tile_master.shape).astype(jnp.float32) * gain_scale
        full_vector = full_vector[:VROWS]
    else:
        slot_grads, full_vector = summed_over_slice(
            jnp.concatenate(pieces, 0), jnp.concatenate(column_sums, 0), owners, slots, gain_scale
        )
    tile_weight, tile_first_new, tile_second_new = adam_update(
        tile_master, slot_grads, tile_first, tile_second, tile_rate
    )
    tile_ema_new = average_rate * tile_ema + (1.0 - average_rate) * tile_weight
    vector_grads = full_vector * gain_scale
    vector_weight, vector_first_new, vector_second_new = adam_update(
        vectors, vector_grads, vector_first, vector_second, vector_rate
    )
    vector_ema_new = average_rate * vector_ema + (1.0 - average_rate) * vector_weight
    return (
        mixed,
        input_grad,
        tile_weight,
        tile_first_new,
        tile_second_new,
        tile_ema_new,
        tile_weight.astype(jnp.bfloat16),
        vector_weight,
        vector_first_new,
        vector_second_new,
        vector_ema_new,
    )


def solution(mesh):
    placed = (
        P("dp", None),
        P("dp", None),
        P("dp", None),
        P("dp", None),
        P(),
        P("dp", None, None, None),
        P("dp", None, None, None),
        P("dp", None, None, None),
        P("dp", None, None, None),
        P(),
        P(),
        P(),
        P(),
        P(),
    )
    return jax.shard_map(
        body,
        mesh=mesh,
        in_specs=placed,
        out_specs=(
            P("dp", None),
            P("dp", None),
            P("dp", None, None, None),
            P("dp", None, None, None),
            P("dp", None, None, None),
            P("dp", None, None, None),
            P("dp", None, None, None),
            P(),
            P(),
            P(),
            P(),
        ),
        check_vma=False,
    )
```

```python
import functools

import jax
import jax.numpy as jnp
from jax import lax
from jax.experimental import pallas as pl
from jax.experimental.pallas import tpu as pltpu
from jax.sharding import PartitionSpec as P

HEADS = 12
BUCKET = 128
SLOTS = 2
TILES = 12
VROWS = 12
STEP = 5

norm_epsilon = 1e-12
tile_rate = 0.03
vector_rate = 0.2
first_decay = 0.5
second_decay = 0.5
adam_epsilon = 1e-08
weight_decay = 0.01
average_rate = 0.9


def tile_slots(owners):
    order = jnp.arange(owners.shape[0], dtype=jnp.int32)
    same = owners[:, None] == owners[None, :]
    earlier = order[None, :] < order[:, None]
    return jnp.sum((same & earlier).astype(jnp.int32), 1)


def adam_update(param, grad, first, second, rate):
    first_new = first_decay * first + (1.0 - first_decay) * grad
    second_new = second_decay * second + (1.0 - second_decay) * grad * grad
    first_hat = first_new / (1.0 - first_decay**STEP)
    second_hat = second_new / (1.0 - second_decay**STEP)
    param_new = param - rate * (
        first_hat / (jnp.sqrt(second_hat) + adam_epsilon) + weight_decay * param
    )
    return (param_new, first_new, second_new)


MESH = pl.DeviceIdType.MESH
GROUP = 32
CHIPS = 16
SPAN = 48
HALF = 384
PAIRS = TILES // 2


def remote(src, dst, send, recv, device):
    return pltpu.make_async_remote_copy(
        src_ref=src, dst_ref=dst, send_sem=send, recv_sem=recv, device_id=(device,), device_id_type=MESH
    )


def place(device):
    core = lax.rem(device, 2)
    x = lax.rem(device // 2, 2)
    y = lax.rem(device // 4, 2)
    z = device // 8
    return z, y, x, core


def greet_all(me):
    barrier = pltpu.get_barrier_semaphore()

    def greet(step, carry):
        pl.semaphore_signal(
            barrier, inc=1, device_id=(lax.rem(me + step, GROUP),), device_id_type=MESH
        )
        return carry

    lax.fori_loop(1, GROUP, greet, 0)
    pl.semaphore_wait(barrier, GROUP - 1)


def lanes(core):
    return pl.ds(pl.multiple_of(core * HALF, HALF), HALF)


def span(z):
    return pl.ds(pl.multiple_of(z * SPAN, 16), SPAN)


def gather_tiles(
    picks,
    slot_ref,
    w_ref,
    stage,
    chunk,
    swap_send,
    swap_recv,
    own_sem,
    z_send,
    z_recv,
    mid_send,
    mid_recv,
    far_send,
    far_recv,
    core_send,
    core_recv,
):
    me = lax.axis_index("dp")
    z, y, x, core = place(me)
    sibling = me + 1 - 2 * core
    x_peer = me + 2 - 4 * x
    y_peer = me + 4 - 8 * y
    cols = lanes(core)
    rows = span(z)
    greet_all(me)

    def swap(step, carry):
        target = lax.rem(me + step, GROUP)
        tz, ty, tx, tc = place(target)
        remote(
            slot_ref.at[:, tx, ty, span(tz), lanes(tc)],
            stage.at[pl.ds(2 * me, 2)],
            swap_send,
            swap_recv,
            target,
        ).start()
        return carry

    lax.fori_loop(1, GROUP, swap, 0)
    mine = pltpu.make_async_copy(
        slot_ref.at[:, x, y, rows, cols], stage.at[pl.ds(2 * me, 2)], own_sem.at[0]
    )
    mine.start()
    mine.wait()
    most = stage.at[pl.ds(0, 2 * GROUP - 2)]
    pltpu.make_async_copy(most, most, swap_recv).wait()
    for tile in range(TILES):
        chunk[tile] = stage[picks[tile]]

    keep = [
        pltpu.make_async_copy(
            chunk.at[pl.ds(2 * pair, 2)],
            w_ref.at[pl.ds(2 * pair, 2), x, y, rows, cols],
            own_sem.at[1 + pair],
        )
        for pair in range(PAIRS)
    ]
    z_copies = []
    for pair in range(PAIRS):
        keep[pair].start()
        group = []
        for hop in range(1, 4):
            target = lax.rem(z + hop, 4) * 8 + lax.rem(me, 8)
            copy = remote(
                chunk.at[pl.ds(2 * pair, 2)],
                w_ref.at[pl.ds(2 * pair, 2), x, y, rows, cols],
                z_send.at[pair, hop - 1],
                z_recv.at[pair, hop - 1],
                target,
            )
            copy.start()
            group.append(copy)
        z_copies.append(group)

    def mid(pair):
        a, b = 2 * pair, 2 * pair + 1
        block_a = w_ref.at[a, x, y, :, cols]
        block_b = w_ref.at[b, x, y, :, cols]
        return [
            remote(block_a, block_a, mid_send.at[a], mid_recv.at[a], y_peer),
            remote(block_b, block_b, mid_send.at[b], mid_recv.at[b], x_peer),
        ]

    def far(pair):
        a, b = 2 * pair, 2 * pair + 1
        block_a = w_ref.at[a, x, :, :, cols]
        block_b = w_ref.at[b, :, y, :, cols]
        return [
            remote(block_a, block_a, far_send.at[a], far_recv.at[a], x_peer),
            remote(block_b, block_b, far_send.at[b], far_recv.at[b], y_peer),
        ]

    def near(pair, last):
        a, b = 2 * pair, 2 * pair + 1
        if last:
            block_a = w_ref.at[a, 1 - x, :, :, cols]
            block_b = w_ref.at[b, :, 1 - y, :, cols]
        else:
            block_a = w_ref.at[a, x, :, :, cols]
            block_b = w_ref.at[b, :, y, :, cols]
        at = 1 if last else 0
        return [
            remote(block_a, block_a, core_send.at[a, at], core_recv.at[a, at], sibling),
            remote(block_b, block_b, core_send.at[b, at], core_recv.at[b, at], sibling),
        ]

    mids, fars, nears = {}, {}, {}
    for step in range(PAIRS + 2):
        if step < PAIRS:
            keep[step].wait()
            for copy in z_copies[step]:
                copy.wait_recv()
            mids[step] = mid(step)
            for copy in mids[step]:
                copy.start()
        if 0 <= step - 1 < PAIRS:
            for copy in mids[step - 1]:
                copy.wait_recv()
            fars[step - 1] = far(step - 1)
            nears[step - 1] = near(step - 1, False)
            for copy in fars[step - 1] + nears[step - 1]:
                copy.start()
        if 0 <= step - 2 < PAIRS:
            for copy in fars[step - 2]:
                copy.wait_recv()
            late = near(step - 2, True)
            for copy in late:
                copy.start()
            nears[step - 2] += late
    for pair in range(PAIRS):
        for copy in nears[pair]:
            copy.wait_recv()
    for pair in range(PAIRS):
        for copy in z_copies[pair] + mids[pair] + fars[pair] + nears[pair]:
            copy.wait_send()
    pltpu.make_async_copy(most, most, swap_send).wait()


def gathered_tiles(tile_low, picks):
    any_space = pl.BlockSpec(memory_space=pl.ANY)
    dma = pltpu.SemaphoreType.DMA
    low = jnp.bfloat16
    return pl.pallas_call(
        gather_tiles,
        out_shape=jax.ShapeDtypeStruct((TILES, 2, 2, 4 * SPAN, 2 * HALF), low),
        in_specs=[pl.BlockSpec(memory_space=pltpu.SMEM), any_space],
        out_specs=any_space,
        scratch_shapes=[
            pltpu.VMEM((2 * GROUP, SPAN, HALF), low),
            pltpu.VMEM((TILES, SPAN, HALF), low),
            dma,
            dma,
            dma((1 + PAIRS,)),
            dma((PAIRS, 3)),
            dma((PAIRS, 3)),
            dma((TILES,)),
            dma((TILES,)),
            dma((TILES,)),
            dma((TILES,)),
            dma((TILES, 2)),
            dma((TILES, 2)),
        ],
        compiler_params=pltpu.CompilerParams(collective_id=0, has_side_effects=True),
        name="gather_tiles",
    )(picks, tile_low.reshape(2, 2, 2, 4 * SPAN, 2 * HALF)).reshape(TILES, 2 * HALF, 2 * HALF)


def reduce_tiles(
    holds,
    keep_slot,
    part_ref,
    vec_ref,
    slot_grad,
    vec_out,
    mine,
    from_core,
    from_far,
    from_mid,
    from_z,
    outbox,
    vec_now,
    vec_in,
    own_sem,
    core_send,
    core_recv,
    far_send,
    far_recv,
    mid_send,
    mid_recv,
    z_send,
    z_recv,
    vec_send,
    vec_recv,
    swap_send,
    swap_recv,
):
    me = lax.axis_index("dp")
    z, y, x, core = place(me)
    sibling = me + 1 - 2 * core
    x_peer = me + 2 - 4 * x
    y_peer = me + 4 - 8 * y
    cols = lanes(core)
    rows = span(z)
    greet_all(me)

    own, to_core = [], []
    for pair in range(PAIRS):
        two = pl.ds(2 * pair, 2)
        own.append(pltpu.make_async_copy(part_ref.at[two, :, :, :, cols], mine.at[two], own_sem.at[pair]))
        to_core.append(
            remote(
                part_ref.at[two, :, :, :, lanes(1 - core)],
                from_core.at[two],
                core_send.at[pair],
                core_recv.at[pair],
                sibling,
            )
        )
        to_core[pair].start()
        own[pair].start()

    vec_copies = []

    def vec_step(number, device):
        copy = remote(vec_now.at[number], vec_in.at[number], vec_send.at[number], vec_recv.at[number], device)
        copy.start()
        vec_copies.append(copy)

    vec_now[0] = vec_ref[...]
    vec_step(0, sibling)

    def far(pair):
        a, b = 2 * pair, 2 * pair + 1
        return [
            remote(mine.at[a, 1 - x], from_far.at[a], far_send.at[a], far_recv.at[a], x_peer),
            remote(mine.at[b, :, 1 - y], from_far.at[b], far_send.at[b], far_recv.at[b], y_peer),
        ]

    def mid(pair):
        a, b = 2 * pair, 2 * pair + 1
        return [
            remote(mine.at[a, x, 1 - y], from_mid.at[a], mid_send.at[a], mid_recv.at[a], y_peer),
            remote(mine.at[b, 1 - x, y], from_mid.at[b], mid_send.at[b], mid_recv.at[b], x_peer),
        ]

    def along_z(pair):
        two = pl.ds(2 * pair, 2)
        copies = []
        for hop in range(1, 4):
            tz = lax.rem(z + hop, 4)
            copies.append(
                remote(
                    mine.at[two, x, y, span(tz)],
                    from_z.at[hop - 1, two],
                    z_send.at[pair, hop - 1],
                    z_recv.at[pair, hop - 1],
                    tz * 8 + lax.rem(me, 8),
                )
            )
        return copies

    fars, mids, zs = {}, {}, {}
    for step in range(PAIRS + 3):
        if step < PAIRS:
            pair = step
            own[pair].wait()
            to_core[pair].wait_recv()
            for tile in (2 * pair, 2 * pair + 1):
                mine[tile] = mine[tile] + from_core[tile]
            fars[pair] = far(pair)
            for copy in fars[pair]:
                copy.start()
        if 0 <= step - 1 < PAIRS:
            pair = step - 1
            a, b = 2 * pair, 2 * pair + 1
            for copy in fars[pair]:
                copy.wait_recv()
            mine[a, x] = mine[a, x] + from_far[a]
            mine[b, :, y] = mine[b, :, y] + from_far[b]
            mids[pair] = mid(pair)
            for copy in mids[pair]:
                copy.start()
        if 0 <= step - 2 < PAIRS:
            pair = step - 2
            a, b = 2 * pair, 2 * pair + 1
            for copy in mids[pair]:
                copy.wait_recv()
            mine[a, x, y] = mine[a, x, y] + from_mid[a]
            mine[b, x, y] = mine[b, x, y] + from_mid[b]
            zs[pair] = along_z(pair)
            for copy in zs[pair]:
                copy.start()
        if 0 <= step - 3 < PAIRS:
            pair = step - 3
            for copy in zs[pair]:
                copy.wait_recv()
            for tile in (2 * pair, 2 * pair + 1):
                total = mine[tile, x, y, rows].astype(jnp.float32)
                for hop in range(3):
                    total = total + from_z[hop, tile].astype(jnp.float32)
                from_z[0, tile] = total.astype(jnp.bfloat16)
        if step == 1:
            vec_copies[0].wait_recv()
            vec_now[1] = vec_now[0] + vec_in[0]
            vec_step(1, x_peer)
        if step == 2:
            vec_copies[1].wait_recv()
            vec_now[2] = vec_now[1] + vec_in[1]
            vec_step(2, y_peer)
        if step == 4:
            vec_copies[2].wait_recv()
            vec_now[3] = vec_now[2] + vec_in[2]
            for hop in range(1, 4):
                copy = remote(
                    vec_now.at[3],
                    vec_in.at[2 + hop],
                    vec_send.at[2 + hop],
                    vec_recv.at[2 + hop],
                    lax.rem(z + hop, 4) * 8 + lax.rem(me, 8),
                )
                copy.start()
                vec_copies.append(copy)

    for copy in vec_copies[3:]:
        copy.wait_recv()
    total = jnp.zeros_like(vec_out)
    for source in range(4):
        hop = lax.rem(z - source + 4, 4)
        total = total + jnp.where(hop == 0, vec_now[3], vec_in[2 + jnp.maximum(hop, 1)])
    vec_out[...] = total

    def fill(at, carry):
        tile = holds[at]
        value = from_z[0, tile]
        outbox[at] = jnp.where(keep_slot[at] > 0, value, jnp.zeros_like(value))
        return carry

    lax.fori_loop(0, 2 * GROUP, fill, 0)
    local = pltpu.make_async_copy(
        outbox.at[pl.ds(2 * me, 2)], slot_grad.at[:, x, y, rows, cols], own_sem.at[PAIRS]
    )
    local.start()

    def swap(step, carry):
        target = lax.rem(me + step, GROUP)
        remote(
            outbox.at[pl.ds(2 * target, 2)],
            slot_grad.at[:, x, y, rows, cols],
            swap_send,
            swap_recv,
            target,
        ).start()
        return carry

    lax.fori_loop(1, GROUP, swap, 0)
    local.wait()
    for group in [to_core] + list(fars.values()) + list(mids.values()) + list(zs.values()) + [vec_copies]:
        for copy in group:
            copy.wait_send()
    most = outbox.at[pl.ds(0, 2 * GROUP - 2)]
    pltpu.make_async_copy(most, most, swap_recv).wait()
    pltpu.make_async_copy(most, most, swap_send).wait()


def reduced_tiles(parts, vector_terms, holds, keep_slot):
    any_space = pl.BlockSpec(memory_space=pl.ANY)
    vmem = pl.BlockSpec(memory_space=pltpu.VMEM)
    smem = pl.BlockSpec(memory_space=pltpu.SMEM)
    dma = pltpu.SemaphoreType.DMA
    low = jnp.bfloat16
    vec_rows = vector_terms.shape[0]
    slot_grads, vector_sums = pl.pallas_call(
        reduce_tiles,
        out_shape=(
            jax.ShapeDtypeStruct((SLOTS, 2, 2, 4 * SPAN, 2 * HALF), low),
            jax.ShapeDtypeStruct(vector_terms.shape, jnp.float32),
        ),
        in_specs=[smem, smem, any_space, vmem],
        out_specs=(any_space, vmem),
        scratch_shapes=[
            pltpu.VMEM((TILES, 2, 2, 4 * SPAN, HALF), low),
            pltpu.VMEM((TILES, 2, 2, 4 * SPAN, HALF), low),
            pltpu.VMEM((TILES, 2, 4 * SPAN, HALF), low),
            pltpu.VMEM((TILES, 4 * SPAN, HALF), low),
            pltpu.VMEM((3, TILES, SPAN, HALF), low),
            pltpu.VMEM((2 * GROUP, SPAN, HALF), low),
            pltpu.VMEM((4, vec_rows, 2 * HALF), jnp.float32),
            pltpu.VMEM((6, vec_rows, 2 * HALF), jnp.float32),
            dma((PAIRS + 1,)),
            dma((PAIRS,)),
            dma((PAIRS,)),
            dma((TILES,)),
            dma((TILES,)),
            dma((TILES,)),
            dma((TILES,)),
            dma((PAIRS, 3)),
            dma((PAIRS, 3)),
            dma((6,)),
            dma((6,)),
            dma,
            dma,
        ],
        compiler_params=pltpu.CompilerParams(
            collective_id=1, has_side_effects=True, vmem_limit_bytes=56 * 2**20
        ),
        name="reduce_tiles",
    )(holds, keep_slot, parts.reshape(TILES, 2, 2, 4 * SPAN, 2 * HALF), vector_terms)
    return slot_grads.reshape(SLOTS, 2 * HALF, 2 * HALF), vector_sums


ROWS = 4 * BUCKET
SQRT_HALF = 0.7071067811865476
INV_SQRT_TAU = 0.3989422804014327
ALLOWED = 3.0e38
BARRED = -1000000000.0


def dot(left, right):
    return jnp.dot(left, right, preferred_element_type=jnp.float32)


def dot_back(left, right):
    return lax.dot_general(
        left, right, (((1,), (1,)), ((), ())), preferred_element_type=jnp.float32
    )


def outer(left, right):
    return lax.dot_general(
        left, right, (((0,), (0,)), ((), ())), preferred_element_type=jnp.float32
    )


def passage_facts(counts, lengths, position):
    places = lengths.shape[1]
    big_end = counts[0, 0]
    mid_end = big_end + counts[0, 1]
    all_end = mid_end + counts[0, 2]
    start = jnp.int32(0)
    member = jnp.zeros(position.shape, jnp.int32)
    usable = jnp.zeros(position.shape, jnp.int32)
    for number in range(places):
        size = jnp.where(
            number < big_end,
            4 * BUCKET,
            jnp.where(number < mid_end, 2 * BUCKET, jnp.where(number < all_end, BUCKET, 0)),
        )
        inside = (position >= start) & (position < start + size)
        live = inside & (position < start + lengths[0, number])
        member = jnp.where(inside, number + 1, member)
        usable = jnp.where(live, 1, usable)
        start = start + size
    passage = jnp.where(member > 0, member - 1, places + position // BUCKET)
    return usable, passage


def normalize(values):
    center = jnp.mean(values, -1, keepdims=True)
    centered = values - center
    spread = jnp.mean(centered * centered, -1, keepdims=True)
    inverse = lax.rsqrt(spread + norm_epsilon)
    return centered * inverse, inverse


def normalize_back(grad, hat, inverse):
    center = jnp.mean(grad, -1, keepdims=True)
    along = jnp.mean(grad * hat, -1, keepdims=True)
    return inverse * (grad - center - hat * along)


def columns_total(values):
    return jnp.sum(values, 0, keepdims=True)


def attend_forward(
    counts,
    lengths,
    x_ref,
    w_hbm,
    vec_ref,
    q_ref,
    k_ref,
    v_ref,
    p_ref,
    ctx_ref,
    hat_ref,
    inverse_ref,
    w_buf,
    cap_ref,
    w_sem,
):
    block, quad = pl.program_id(0), pl.program_id(1)
    width = 256
    first = (block == 0) & (quad == 0)
    loads = [pltpu.make_async_copy(w_hbm.at[at], w_buf.at[at], w_sem.at[at]) for at in range(4)]

    @pl.when(first)
    def _():
        for load in loads:
            load.start()

    @pl.when(quad == 0)
    def _():
        at_row = lax.broadcasted_iota(jnp.int32, (ROWS, 1), 0) + block * ROWS
        at_column = lax.broadcasted_iota(jnp.int32, (1, ROWS), 1) + block * ROWS
        _, passage_row = passage_facts(counts, lengths, at_row)
        usable_column, passage_column = passage_facts(counts, lengths, at_column)
        allowed = (passage_row == passage_column) & ((usable_column == 1) | (at_row == at_column))
        cap_ref[...] = jnp.where(allowed, ALLOWED, BARRED)

    @pl.when(first)
    def _():
        for load in loads[:3]:
            load.wait()

    cols = pl.ds(pl.multiple_of(quad * width, width), width)
    x = x_ref[...]
    query = (dot(x, w_buf[0, :, cols]) + vec_ref[0:1, cols]).astype(jnp.bfloat16)
    query = query * jnp.bfloat16(0.125)
    keyed = dot(x, w_buf[1, :, cols]).astype(jnp.bfloat16)
    valued = (dot(x, w_buf[2, :, cols]) + vec_ref[1:2, cols]).astype(jnp.bfloat16)
    q_ref[...] = query
    k_ref[...] = keyed
    v_ref[...] = valued
    low_half = lax.broadcasted_iota(jnp.int32, (1, 128), 1) < 64
    for pair in range(2):
        part = slice(128 * pair, 128 * pair + 128)
        contexts = []
        for head in range(2):
            here = low_half if head == 0 else ~low_half
            mine = jnp.where(here, query[:, part], jnp.zeros_like(query[:, part]))
            scores = jnp.minimum(dot_back(mine, keyed[:, part]), cap_ref[...])
            exponent = jnp.exp(scores - jnp.max(scores, -1, keepdims=True))
            inverse = 1.0 / jnp.sum(exponent, -1, keepdims=True)
            probability = (exponent * inverse).astype(jnp.bfloat16)
            p_ref[0, 2 * pair + head] = probability
            contexts.append(dot(probability, valued[:, part]))
        both = jnp.where(low_half, contexts[0], contexts[1]).astype(jnp.bfloat16)
        ctx_ref[:, pl.ds(pl.multiple_of(quad * width + 128 * pair, 128), 128)] = both

    @pl.when((block == 0) & (quad == 2))
    def _():
        loads[3].wait()

    @pl.when(quad == 2)
    def _():
        branch = dot(ctx_ref[...], w_buf[3]) + vec_ref[2:3, :]
        hat, inverse = normalize(x_ref[...].astype(jnp.float32) + branch)
        hat_ref[...] = hat
        inverse_ref[...] = inverse


def attended(counts, lengths, x, weights, vectors):
    tokens, width = x.shape
    blocks = tokens // ROWS
    low = jnp.bfloat16
    smem = pl.BlockSpec(memory_space=pltpu.SMEM)
    quad = pl.BlockSpec((ROWS, 256), lambda b, h: (b, h))
    rows = pl.BlockSpec((ROWS, width), lambda b, h: (b, 0))
    shaped = jax.ShapeDtypeStruct
    return pl.pallas_call(
        attend_forward,
        grid=(blocks, 3),
        out_shape=(
            shaped((tokens, width), low),
            shaped((tokens, width), low),
            shaped((tokens, width), low),
            shaped((blocks, HEADS, ROWS, ROWS), low),
            shaped((tokens, width), low),
            shaped((tokens, width), jnp.float32),
            shaped((tokens, 1), jnp.float32),
        ),
        in_specs=[
            smem,
            smem,
            rows,
            pl.BlockSpec(memory_space=pl.ANY),
            pl.BlockSpec((VROWS, width), lambda b, h: (0, 0)),
        ],
        out_specs=(
            quad,
            quad,
            quad,
            pl.BlockSpec((1, 4, ROWS, ROWS), lambda b, h: (b, h, 0, 0)),
            rows,
            rows,
            pl.BlockSpec((ROWS, 1), lambda b, h: (b, 0)),
        ),
        scratch_shapes=[
            pltpu.VMEM((4, width, width), low),
            pltpu.VMEM((ROWS, ROWS), jnp.float32),
            pltpu.SemaphoreType.DMA((4,)),
        ],
        compiler_params=pltpu.CompilerParams(vmem_limit_bytes=56 * 2**20),
        name="attend_forward",
    )(counts, lengths, x, weights, vectors)


def feed_forward_both(
    counts,
    lengths,
    hat_ref,
    inverse_ref,
    cot_ref,
    w_hbm,
    vec_ref,
    mixed_ref,
    first_ref,
    branch_ref,
    context_ref,
    up_grad_ref,
    down_grad_ref,
    sum_ref,
    w_buf,
    active_ref,
    up_ref,
    hidden_ref,
    down_ref,
    slope_ref,
    w_sem,
):
    step = pl.program_id(0)
    blocks = pl.num_programs(0) - 4
    loads = [
        pltpu.make_async_copy(w_hbm.at[3 + at], w_buf.at[at], w_sem.at[at]) for at in range(9)
    ]

    @pl.when(step == 0)
    def _():
        for load in loads[1:] + loads[:1]:
            load.start()
        sum_ref[...] = jnp.zeros_like(sum_ref)
        for load in loads[1:] + loads[:1]:
            load.wait()

    @pl.when(step < blocks)
    def _():
        here = pl.ds(pl.multiple_of(step * ROWS, ROWS), ROWS)
        at_row = lax.broadcasted_iota(jnp.int32, (ROWS, 1), 0) + step * ROWS
        live = passage_facts(counts, lengths, at_row)[0].astype(jnp.float32)
        hat = hat_ref[...]
        hidden = hat * vec_ref[10:11, :] + vec_ref[8:9, :]
        hidden_low = hidden.astype(jnp.bfloat16)
        hidden_ref[here, :] = hidden_low
        total = hidden + vec_ref[7:8, :]
        for tile in range(4):
            up = dot(hidden_low, w_buf[1 + tile]) + vec_ref[3 + tile : 4 + tile, :]
            share = 0.5 + 0.5 * lax.erf(up * SQRT_HALF)
            slope_ref[tile] = share + up * (jnp.exp(up * up * -0.5) * INV_SQRT_TAU)
            active = (up * share).astype(jnp.bfloat16)
            active_ref[tile, here, :] = active
            total = total + dot(active, w_buf[5 + tile])
        hat_two, inverse_two = normalize(total)
        mixed_ref[...] = ((hat_two * vec_ref[11:12, :] + vec_ref[9:10, :]) * live).astype(jnp.bfloat16)
        grad_out = cot_ref[...].astype(jnp.float32) * live
        sum_ref[11:12, :] += columns_total(grad_out * hat_two)
        sum_ref[9:10, :] += columns_total(grad_out)
        second = normalize_back(grad_out * vec_ref[11:12, :], hat_two, inverse_two)
        down_low = second.astype(jnp.bfloat16)
        down_ref[here, :] = down_low
        sum_ref[7:8, :] += columns_total(down_low.astype(jnp.float32))
        grad_hidden = second
        for tile in range(4):
            pulled = dot_back(down_low, w_buf[5 + tile])
            up_low = (pulled * slope_ref[tile]).astype(jnp.bfloat16)
            up_ref[tile, here, :] = up_low
            sum_ref[3 + tile : 4 + tile, :] += columns_total(up_low.astype(jnp.float32))
            grad_hidden = grad_hidden + dot_back(up_low, w_buf[1 + tile])
        sum_ref[10:11, :] += columns_total(grad_hidden * hat)
        sum_ref[8:9, :] += columns_total(grad_hidden)
        grad_first = normalize_back(grad_hidden * vec_ref[10:11, :], hat, inverse_ref[...])
        first_ref[...] = grad_first
        branch_low = grad_first.astype(jnp.bfloat16)
        branch_ref[...] = branch_low
        sum_ref[2:3, :] += columns_total(branch_low.astype(jnp.float32))
        context_ref[...] = dot_back(branch_low, w_buf[0]).astype(jnp.bfloat16)

    @pl.when(step >= blocks)
    def _():
        tile = step - blocks
        up_grad_ref[0] = outer(hidden_ref[...], up_ref[tile]).astype(jnp.bfloat16)
        down_grad_ref[0] = outer(active_ref[tile], down_ref[...]).astype(jnp.bfloat16)


def fed_forward_both(counts, lengths, hat, inverse, cotangent, weights, vectors):
    tokens, width = hat.shape
    blocks = tokens // ROWS
    low = jnp.bfloat16
    smem = pl.BlockSpec(memory_space=pltpu.SMEM)
    shaped = jax.ShapeDtypeStruct

    def block_of(step):
        return jnp.minimum(step, blocks - 1)

    def tile_of(step):
        return jnp.maximum(step - blocks, 0)

    rows = pl.BlockSpec((ROWS, width), lambda i: (block_of(i), 0))
    tile = pl.BlockSpec((1, width, width), lambda i: (tile_of(i), 0, 0))
    return pl.pallas_call(
        feed_forward_both,
        grid=(blocks + 4,),
        out_shape=(
            shaped((tokens, width), low),
            shaped((tokens, width), jnp.float32),
            shaped((tokens, width), low),
            shaped((tokens, width), low),
            shaped((4, width, width), low),
            shaped((4, width, width), low),
            shaped((16, width), jnp.float32),
        ),
        in_specs=[
            smem,
            smem,
            rows,
            pl.BlockSpec((ROWS, 1), lambda i: (block_of(i), 0)),
            rows,
            pl.BlockSpec(memory_space=pl.ANY),
            pl.BlockSpec((VROWS, width), lambda i: (0, 0)),
        ],
        out_specs=(
            rows,
            rows,
            rows,
            rows,
            tile,
            tile,
            pl.BlockSpec((16, width), lambda i: (0, 0)),
        ),
        scratch_shapes=[
            pltpu.VMEM((9, width, width), low),
            pltpu.VMEM((4, tokens, width), low),
            pltpu.VMEM((4, tokens, width), low),
            pltpu.VMEM((tokens, width), low),
            pltpu.VMEM((tokens, width), low),
            pltpu.VMEM((4, ROWS, width), jnp.float32),
            pltpu.SemaphoreType.DMA((9,)),
        ],
        compiler_params=pltpu.CompilerParams(vmem_limit_bytes=60 * 2**20),
        name="feed_forward_both",
    )(counts, lengths, hat, inverse, cotangent, weights, vectors)


def attend_backward(
    p_ref,
    q_ref,
    k_ref,
    v_ref,
    x_ref,
    ctx_ref,
    grad_ctx_ref,
    branch_ref,
    first_ref,
    w_hbm,
    input_ref,
    grad_ref,
    sum_ref,
    w_buf,
    pulled_ref,
    w_sem,
):
    step = pl.program_id(0)
    inner = pl.num_programs(0) - 4
    block, quad = step // 3, lax.rem(step, 3)
    width = 256
    loads = [pltpu.make_async_copy(w_hbm.at[at], w_buf.at[at], w_sem.at[at]) for at in range(3)]

    @pl.when(step == 0)
    def _():
        for load in loads:
            load.start()
        sum_ref[...] = jnp.zeros_like(sum_ref)

    @pl.when(step < inner)
    def _():
        low_half = lax.broadcasted_iota(jnp.int32, (1, 128), 1) < 64
        here = pl.ds(pl.multiple_of(block * ROWS, ROWS), ROWS)
        for pair in range(2):
            part = slice(128 * pair, 128 * pair + 128)
            cols = pl.ds(pl.multiple_of(quad * width + 128 * pair, 128), 128)
            query, keyed, valued = q_ref[:, part], k_ref[:, part], v_ref[:, part]
            pull = grad_ctx_ref[here, cols]
            along = pull.astype(jnp.float32) * ctx_ref[here, cols].astype(jnp.float32)
            by_query, by_key, by_value = [], [], []
            for head in range(2):
                mask = low_half if head == 0 else ~low_half
                mine = jnp.where(mask, pull, jnp.zeros_like(pull))
                level = jnp.sum(jnp.where(mask, along, 0.0), -1, keepdims=True)
                probability = p_ref[0, 2 * pair + head]
                grad_prob = dot_back(mine, valued)
                grad_scores = (probability.astype(jnp.float32) * (grad_prob - level)).astype(jnp.bfloat16)
                by_query.append(dot(grad_scores, keyed))
                by_key.append(outer(grad_scores, query))
                by_value.append(outer(probability, pull))
            grad_query = (jnp.where(low_half, by_query[0], by_query[1]) * 0.125).astype(jnp.bfloat16)
            grad_value = jnp.where(low_half, by_value[0], by_value[1]).astype(jnp.bfloat16)
            pulled_ref[0, here, cols] = grad_query
            pulled_ref[1, here, cols] = jnp.where(low_half, by_key[0], by_key[1]).astype(jnp.bfloat16)
            pulled_ref[2, here, cols] = grad_value
            sum_ref[0:1, cols] += columns_total(grad_query.astype(jnp.float32))
            sum_ref[1:2, cols] += columns_total(grad_value.astype(jnp.float32))

    @pl.when(step == 2)
    def _():
        for load in loads:
            load.wait()

    @pl.when((step < inner) & (quad == 2))
    def _():
        here = pl.ds(pl.multiple_of(block * ROWS, ROWS), ROWS)
        total = first_ref[...]
        for at in range(3):
            total = total + dot_back(pulled_ref[at, here, :], w_buf[at])
        input_ref[...] = total

    @pl.when((step >= inner) & (step < inner + 3))
    def _():
        grad_ref[0] = outer(x_ref[...], pulled_ref[step - inner]).astype(jnp.bfloat16)

    @pl.when(step == inner + 3)
    def _():
        grad_ref[0] = outer(ctx_ref[...], branch_ref[...]).astype(jnp.bfloat16)


def attended_back(probs, query, keyed, valued, x, context, grad_context, grad_branch, grad_first, weights):
    tokens, width = x.shape
    blocks = tokens // ROWS
    inner = 3 * blocks
    low = jnp.bfloat16
    shaped = jax.ShapeDtypeStruct

    def at(step):
        step = jnp.minimum(step, inner - 1)
        return step // 3, lax.rem(step, 3)

    quad = pl.BlockSpec((ROWS, 256), lambda i: at(i))
    whole = pl.BlockSpec((tokens, width), lambda i: (0, 0))
    rows = pl.BlockSpec((ROWS, width), lambda i: (at(i)[0], 0))
    return pl.pallas_call(
        attend_backward,
        grid=(inner + 4,),
        out_shape=(
            shaped((tokens, width), jnp.float32),
            shaped((4, width, width), low),
            shaped((16, width), jnp.float32),
        ),
        in_specs=[
            pl.BlockSpec((1, 4, ROWS, ROWS), lambda i: (*at(i), 0, 0)),
            quad,
            quad,
            quad,
            whole,
            whole,
            whole,
            whole,
            rows,
            pl.BlockSpec(memory_space=pl.ANY),
        ],
        out_specs=(
            rows,
            pl.BlockSpec((1, width, width), lambda i: (jnp.maximum(i - inner, 0), 0, 0)),
            pl.BlockSpec((16, width), lambda i: (0, 0)),
        ),
        scratch_shapes=[
            pltpu.VMEM((3, width, width), low),
            pltpu.VMEM((3, tokens, width), low),
            pltpu.SemaphoreType.DMA((3,)),
        ],
        compiler_params=pltpu.CompilerParams(vmem_limit_bytes=56 * 2**20),
        name="attend_backward",
    )(probs, query, keyed, valued, x, context, grad_context, grad_branch, grad_first, weights)


def moved(param, grad, first, second, average, rate):
    param_new, first_new, second_new = adam_update(param, grad, first, second, rate)
    return param_new, first_new, second_new, average_rate * average + (1.0 - average_rate) * param_new


def update_kernel(
    gain_scale,
    grad_ref,
    master_ref,
    first_ref,
    second_ref,
    ema_ref,
    vec_grad_ref,
    vec_ref,
    vec_first_ref,
    vec_second_ref,
    vec_ema_ref,
    master_out,
    first_out,
    second_out,
    ema_out,
    copy_out,
    vec_out,
    vec_first_out,
    vec_second_out,
    vec_ema_out,
):
    grad = grad_ref[...].astype(jnp.float32) * gain_scale
    result = moved(master_ref[0], grad, first_ref[0], second_ref[0], ema_ref[0], tile_rate)
    master_out[0], first_out[0], second_out[0], ema_out[0] = result
    copy_out[0] = result[0].astype(jnp.bfloat16)

    @pl.when((pl.program_id(0) == 0) & (pl.program_id(1) == 0))
    def _():
        vec_grad = vec_grad_ref[0:VROWS, :] * gain_scale
        vec_out[...], vec_first_out[...], vec_second_out[...], vec_ema_out[...] = moved(
            vec_ref[...], vec_grad, vec_first_ref[...], vec_second_ref[...], vec_ema_ref[...], vector_rate
        )


def updated(gain_scale, slot_grads, master, first, second, ema, vec_grad, vectors, vec_first, vec_second, vec_ema):
    width = master.shape[-1]
    chunk = 192
    tile = pl.BlockSpec((1, 1, chunk, width), lambda s, r: (0, s, r, 0))
    vec = pl.BlockSpec((VROWS, width), lambda s, r: (0, 0))
    shaped = jax.ShapeDtypeStruct
    tile_shape = shaped(master.shape, jnp.float32)
    vec_shape = shaped((VROWS, width), jnp.float32)
    return pl.pallas_call(
        functools.partial(update_kernel, gain_scale),
        grid=(SLOTS, width // chunk),
        out_shape=(tile_shape,) * 4 + (shaped(master.shape, jnp.bfloat16),) + (vec_shape,) * 4,
        in_specs=[pl.BlockSpec((1, chunk, width), lambda s, r: (s, r, 0))]
        + [tile] * 4
        + [pl.BlockSpec((16, width), lambda s, r: (0, 0))]
        + [vec] * 4,
        out_specs=(tile,) * 5 + (vec,) * 4,
        compiler_params=pltpu.CompilerParams(vmem_limit_bytes=40 * 2**20),
        name="update",
    )(slot_grads, master, first, second, ema, vec_grad, vectors, vec_first, vec_second, vec_ema)


def collected_tiles(tile_low, owners, slots):
    mine = owners == lax.axis_index("dp")
    local = jnp.where(mine[:, None, None], tile_low[slots], jnp.zeros((), tile_low.dtype))
    return lax.psum(local, "dp")


def summed_over_slice(parts, vector_terms, owners, slots):
    model_width = parts.shape[2]
    rows = parts.reshape(-1, model_width).astype(jnp.float32)
    summed_rows = lax.psum_scatter(rows, "dp", scatter_dimension=0, tiled=True)
    full_rows = lax.all_gather(summed_rows, "dp", axis=0, tiled=True)
    tile_grads = full_rows.reshape(parts.shape)
    myself = lax.axis_index("dp")
    slot_list = []
    for slot_number in range(SLOTS):
        select = (owners == myself) & (slots == slot_number)
        slot_list.append(jnp.sum(jnp.where(select[:, None, None], tile_grads, 0.0), 0))
    return jnp.stack(slot_list, 0), lax.psum(vector_terms, "dp")


def body(
    inputs,
    cotangent,
    counts,
    lengths,
    owners,
    tile_master,
    tile_first,
    tile_second,
    tile_ema,
    bias_vals,
    gain_vals,
    vector_first,
    vector_second,
    vector_ema,
):
    tokens = inputs.shape[0]
    small = lax.axis_size("dp") == GROUP
    slots = tile_slots(owners)
    vectors = jnp.concatenate([bias_vals, gain_vals], 0)
    tile_low = tile_master[0].astype(jnp.bfloat16)
    if small:
        weights = gathered_tiles(tile_low, owners * SLOTS + slots)
    else:
        weights = collected_tiles(tile_low, owners, slots)
    query, keyed, valued, probs, context, hat, inverse = attended(
        counts, lengths, inputs, weights, vectors
    )
    mixed, grad_first, grad_branch, grad_context, up_grads, down_grads, late_sums = fed_forward_both(
        counts, lengths, hat, inverse, cotangent, weights, vectors
    )
    input_grad, early_grads, early_sums = attended_back(
        probs, query, keyed, valued, inputs, context, grad_context, grad_branch, grad_first, weights
    )
    gain_scale = float(tokens * lax.axis_size("dp")) ** (-0.5)
    parts = jnp.concatenate([early_grads, up_grads, down_grads], 0)
    sums = late_sums + early_sums
    if small:
        places = jnp.arange(SLOTS * GROUP, dtype=jnp.int32)
        match = (owners * SLOTS + slots)[None, :] == places[:, None]
        holds = jnp.sum(jnp.where(match, jnp.arange(TILES, dtype=jnp.int32)[None, :], 0), 1)
        keep_slot = jnp.sum(match.astype(jnp.int32), 1)
        slot_grads, full_sums = reduced_tiles(parts, sums, holds, keep_slot)
    else:
        slot_grads, full_sums = summed_over_slice(parts, sums, owners, slots)
    return (mixed, input_grad) + tuple(
        updated(
            gain_scale,
            slot_grads,
            tile_master,
            tile_first,
            tile_second,
            tile_ema,
            full_sums,
            vectors,
            vector_first,
            vector_second,
            vector_ema,
        )
    )


def solution(mesh):
    placed = (
        P("dp", None),
        P("dp", None),
        P("dp", None),
        P("dp", None),
        P(),
        P("dp", None, None, None),
        P("dp", None, None, None),
        P("dp", None, None, None),
        P("dp", None, None, None),
        P(),
        P(),
        P(),
        P(),
        P(),
    )
    return jax.shard_map(
        body,
        mesh=mesh,
        in_specs=placed,
        out_specs=(
            P("dp", None),
            P("dp", None),
            P("dp", None, None, None),
            P("dp", None, None, None),
            P("dp", None, None, None),
            P("dp", None, None, None),
            P("dp", None, None, None),
            P(),
            P(),
            P(),
            P(),
        ),
        check_vma=False,
    )
```

```python
import functools

import jax
import jax.numpy as jnp
from jax import lax
from jax.experimental import pallas as pl
from jax.experimental.pallas import tpu as pltpu
from jax.sharding import PartitionSpec as P

HEADS = 12
BUCKET = 128
SLOTS = 2
TILES = 12
VROWS = 12
STEP = 5

norm_epsilon = 1e-12
tile_rate = 0.03
vector_rate = 0.2
first_decay = 0.5
second_decay = 0.5
adam_epsilon = 1e-08
weight_decay = 0.01
average_rate = 0.9


def tile_slots(owners):
    order = jnp.arange(owners.shape[0], dtype=jnp.int32)
    same = owners[:, None] == owners[None, :]
    earlier = order[None, :] < order[:, None]
    return jnp.sum((same & earlier).astype(jnp.int32), 1)


def adam_update(param, grad, first, second, rate):
    first_new = first_decay * first + (1.0 - first_decay) * grad
    second_new = second_decay * second + (1.0 - second_decay) * grad * grad
    first_hat = first_new / (1.0 - first_decay**STEP)
    second_hat = second_new / (1.0 - second_decay**STEP)
    param_new = param - rate * (
        first_hat / (jnp.sqrt(second_hat) + adam_epsilon) + weight_decay * param
    )
    return (param_new, first_new, second_new)


MESH = pl.DeviceIdType.MESH
GROUP = 32
CHIPS = 16
SPAN = 48
HALF = 384
PAIRS = TILES // 2
PLANE = 8
PIECE = 96


def remote(src, dst, send, recv, device):
    return pltpu.make_async_remote_copy(
        src_ref=src, dst_ref=dst, send_sem=send, recv_sem=recv, device_id=(device,), device_id_type=MESH
    )


def place(device):
    core = lax.rem(device, 2)
    x = lax.rem(device // 2, 2)
    y = lax.rem(device // 4, 2)
    z = device // 8
    return z, y, x, core


def greet_all(me):
    barrier = pltpu.get_barrier_semaphore()

    def greet(step, carry):
        pl.semaphore_signal(
            barrier, inc=1, device_id=(lax.rem(me + step, GROUP),), device_id_type=MESH
        )
        return carry

    lax.fori_loop(1, GROUP, greet, 0)
    pl.semaphore_wait(barrier, GROUP - 1)


def lanes(core):
    return pl.ds(pl.multiple_of(core * HALF, HALF), HALF)


def span(z):
    return pl.ds(pl.multiple_of(z * SPAN, 16), SPAN)


def gather_tiles(
    picks,
    slot_ref,
    w_ref,
    stage,
    chunk,
    swap_send,
    swap_recv,
    own_sem,
    z_send,
    z_recv,
    mid_send,
    mid_recv,
    far_send,
    far_recv,
    core_send,
    core_recv,
):
    me = lax.axis_index("dp")
    z, y, x, core = place(me)
    sibling = me + 1 - 2 * core
    x_peer = me + 2 - 4 * x
    y_peer = me + 4 - 8 * y
    cols = lanes(core)
    rows = span(z)
    greet_all(me)

    def swap(step, carry):
        target = lax.rem(me + step, GROUP)
        tz, ty, tx, tc = place(target)
        remote(
            slot_ref.at[:, tx, ty, span(tz), lanes(tc)],
            stage.at[pl.ds(2 * me, 2)],
            swap_send,
            swap_recv,
            target,
        ).start()
        return carry

    lax.fori_loop(1, GROUP, swap, 0)
    mine = pltpu.make_async_copy(
        slot_ref.at[:, x, y, rows, cols], stage.at[pl.ds(2 * me, 2)], own_sem.at[0]
    )
    mine.start()
    mine.wait()
    most = stage.at[pl.ds(0, 2 * GROUP - 2)]
    pltpu.make_async_copy(most, most, swap_recv).wait()
    for tile in range(TILES):
        chunk[tile] = stage[picks[tile]]

    keep = [
        pltpu.make_async_copy(
            chunk.at[pl.ds(2 * pair, 2)],
            w_ref.at[pl.ds(2 * pair, 2), x, y, rows, cols],
            own_sem.at[1 + pair],
        )
        for pair in range(PAIRS)
    ]
    z_copies = []
    for pair in range(PAIRS):
        keep[pair].start()
        group = []
        for hop in range(1, 4):
            target = lax.rem(z + hop, 4) * 8 + lax.rem(me, 8)
            copy = remote(
                chunk.at[pl.ds(2 * pair, 2)],
                w_ref.at[pl.ds(2 * pair, 2), x, y, rows, cols],
                z_send.at[pair, hop - 1],
                z_recv.at[pair, hop - 1],
                target,
            )
            copy.start()
            group.append(copy)
        z_copies.append(group)

    def mid(pair):
        a, b = 2 * pair, 2 * pair + 1
        block_a = w_ref.at[a, x, y, :, cols]
        block_b = w_ref.at[b, x, y, :, cols]
        return [
            remote(block_a, block_a, mid_send.at[a], mid_recv.at[a], y_peer),
            remote(block_b, block_b, mid_send.at[b], mid_recv.at[b], x_peer),
        ]

    def far(pair):
        a, b = 2 * pair, 2 * pair + 1
        block_a = w_ref.at[a, x, :, :, cols]
        block_b = w_ref.at[b, :, y, :, cols]
        return [
            remote(block_a, block_a, far_send.at[a], far_recv.at[a], x_peer),
            remote(block_b, block_b, far_send.at[b], far_recv.at[b], y_peer),
        ]

    def near(pair, last):
        a, b = 2 * pair, 2 * pair + 1
        if last:
            block_a = w_ref.at[a, 1 - x, :, :, cols]
            block_b = w_ref.at[b, :, 1 - y, :, cols]
        else:
            block_a = w_ref.at[a, x, :, :, cols]
            block_b = w_ref.at[b, :, y, :, cols]
        at = 1 if last else 0
        return [
            remote(block_a, block_a, core_send.at[a, at], core_recv.at[a, at], sibling),
            remote(block_b, block_b, core_send.at[b, at], core_recv.at[b, at], sibling),
        ]

    mids, fars, nears = {}, {}, {}
    for step in range(PAIRS + 2):
        if step < PAIRS:
            keep[step].wait()
            for copy in z_copies[step]:
                copy.wait_recv()
            mids[step] = mid(step)
            for copy in mids[step]:
                copy.start()
        if 0 <= step - 1 < PAIRS:
            for copy in mids[step - 1]:
                copy.wait_recv()
            fars[step - 1] = far(step - 1)
            nears[step - 1] = near(step - 1, False)
            for copy in fars[step - 1] + nears[step - 1]:
                copy.start()
        if 0 <= step - 2 < PAIRS:
            for copy in fars[step - 2]:
                copy.wait_recv()
            late = near(step - 2, True)
            for copy in late:
                copy.start()
            nears[step - 2] += late
    for pair in range(PAIRS):
        for copy in nears[pair]:
            copy.wait_recv()
    for pair in range(PAIRS):
        for copy in z_copies[pair] + mids[pair] + fars[pair] + nears[pair]:
            copy.wait_send()
    pltpu.make_async_copy(most, most, swap_send).wait()


def gathered_tiles(tile_low, picks):
    any_space = pl.BlockSpec(memory_space=pl.ANY)
    dma = pltpu.SemaphoreType.DMA
    low = jnp.bfloat16
    return pl.pallas_call(
        gather_tiles,
        out_shape=jax.ShapeDtypeStruct((TILES, 2, 2, 4 * SPAN, 2 * HALF), low),
        in_specs=[pl.BlockSpec(memory_space=pltpu.SMEM), any_space],
        out_specs=any_space,
        scratch_shapes=[
            pltpu.VMEM((2 * GROUP, SPAN, HALF), low),
            pltpu.VMEM((TILES, SPAN, HALF), low),
            dma,
            dma,
            dma((1 + PAIRS,)),
            dma((PAIRS, 3)),
            dma((PAIRS, 3)),
            dma((TILES,)),
            dma((TILES,)),
            dma((TILES,)),
            dma((TILES,)),
            dma((TILES, 2)),
            dma((TILES, 2)),
        ],
        compiler_params=pltpu.CompilerParams(collective_id=0, has_side_effects=True),
        name="gather_tiles",
    )(picks, tile_low.reshape(2, 2, 2, 4 * SPAN, 2 * HALF)).reshape(TILES, 2 * HALF, 2 * HALF)


ROWS = 4 * BUCKET
SQRT_HALF = 0.7071067811865476
INV_SQRT_TAU = 0.3989422804014327
ALLOWED = 3.0e38
BARRED = -1000000000.0


def dot(left, right):
    return jnp.dot(left, right, preferred_element_type=jnp.float32)


def dot_back(left, right):
    return lax.dot_general(
        left, right, (((1,), (1,)), ((), ())), preferred_element_type=jnp.float32
    )


def outer(left, right):
    return lax.dot_general(
        left, right, (((0,), (0,)), ((), ())), preferred_element_type=jnp.float32
    )


def passage_facts(counts, lengths, position):
    places = lengths.shape[1]
    big_end = counts[0, 0]
    mid_end = big_end + counts[0, 1]
    all_end = mid_end + counts[0, 2]
    start = jnp.int32(0)
    member = jnp.zeros(position.shape, jnp.int32)
    usable = jnp.zeros(position.shape, jnp.int32)
    for number in range(places):
        size = jnp.where(
            number < big_end,
            4 * BUCKET,
            jnp.where(number < mid_end, 2 * BUCKET, jnp.where(number < all_end, BUCKET, 0)),
        )
        inside = (position >= start) & (position < start + size)
        live = inside & (position < start + lengths[0, number])
        member = jnp.where(inside, number + 1, member)
        usable = jnp.where(live, 1, usable)
        start = start + size
    passage = jnp.where(member > 0, member - 1, places + position // BUCKET)
    return usable, passage


def normalize(values):
    center = jnp.mean(values, -1, keepdims=True)
    centered = values - center
    spread = jnp.mean(centered * centered, -1, keepdims=True)
    inverse = lax.rsqrt(spread + norm_epsilon)
    return centered * inverse, inverse


def normalize_back(grad, hat, inverse):
    center = jnp.mean(grad, -1, keepdims=True)
    along = jnp.mean(grad * hat, -1, keepdims=True)
    return inverse * (grad - center - hat * along)


def columns_total(values):
    return jnp.sum(values, 0, keepdims=True)


def attend_forward(
    counts,
    lengths,
    x_ref,
    w_hbm,
    vec_ref,
    q_ref,
    k_ref,
    v_ref,
    p_ref,
    ctx_ref,
    hat_ref,
    inverse_ref,
    w_buf,
    cap_ref,
    w_sem,
):
    block, quad = pl.program_id(0), pl.program_id(1)
    width = 256
    first = (block == 0) & (quad == 0)
    loads = [pltpu.make_async_copy(w_hbm.at[at], w_buf.at[at], w_sem.at[at]) for at in range(4)]

    @pl.when(first)
    def _():
        for load in loads:
            load.start()

    @pl.when(quad == 0)
    def _():
        at_row = lax.broadcasted_iota(jnp.int32, (ROWS, 1), 0) + block * ROWS
        at_column = lax.broadcasted_iota(jnp.int32, (1, ROWS), 1) + block * ROWS
        _, passage_row = passage_facts(counts, lengths, at_row)
        usable_column, passage_column = passage_facts(counts, lengths, at_column)
        allowed = (passage_row == passage_column) & ((usable_column == 1) | (at_row == at_column))
        cap_ref[...] = jnp.where(allowed, ALLOWED, BARRED)

    @pl.when(first)
    def _():
        for load in loads[:3]:
            load.wait()

    cols = pl.ds(pl.multiple_of(quad * width, width), width)
    x = x_ref[...]
    query = (dot(x, w_buf[0, :, cols]) + vec_ref[0:1, cols]).astype(jnp.bfloat16)
    query = query * jnp.bfloat16(0.125)
    keyed = dot(x, w_buf[1, :, cols]).astype(jnp.bfloat16)
    valued = (dot(x, w_buf[2, :, cols]) + vec_ref[1:2, cols]).astype(jnp.bfloat16)
    q_ref[...] = query
    k_ref[...] = keyed
    v_ref[...] = valued
    low_half = lax.broadcasted_iota(jnp.int32, (1, 128), 1) < 64
    for pair in range(2):
        part = slice(128 * pair, 128 * pair + 128)
        contexts = []
        for head in range(2):
            here = low_half if head == 0 else ~low_half
            mine = jnp.where(here, query[:, part], jnp.zeros_like(query[:, part]))
            scores = jnp.minimum(dot_back(mine, keyed[:, part]), cap_ref[...])
            exponent = jnp.exp(scores - jnp.max(scores, -1, keepdims=True))
            inverse = 1.0 / jnp.sum(exponent, -1, keepdims=True)
            probability = (exponent * inverse).astype(jnp.bfloat16)
            p_ref[0, 2 * pair + head] = probability
            contexts.append(dot(probability, valued[:, part]))
        both = jnp.where(low_half, contexts[0], contexts[1]).astype(jnp.bfloat16)
        ctx_ref[:, pl.ds(pl.multiple_of(quad * width + 128 * pair, 128), 128)] = both

    @pl.when((block == 0) & (quad == 2))
    def _():
        loads[3].wait()

    @pl.when(quad == 2)
    def _():
        branch = dot(ctx_ref[...], w_buf[3]) + vec_ref[2:3, :]
        hat, inverse = normalize(x_ref[...].astype(jnp.float32) + branch)
        hat_ref[...] = hat
        inverse_ref[...] = inverse


def attended(counts, lengths, x, weights, vectors):
    tokens, width = x.shape
    blocks = tokens // ROWS
    low = jnp.bfloat16
    smem = pl.BlockSpec(memory_space=pltpu.SMEM)
    quad = pl.BlockSpec((ROWS, 256), lambda b, h: (b, h))
    rows = pl.BlockSpec((ROWS, width), lambda b, h: (b, 0))
    shaped = jax.ShapeDtypeStruct
    return pl.pallas_call(
        attend_forward,
        grid=(blocks, 3),
        out_shape=(
            shaped((tokens, width), low),
            shaped((tokens, width), low),
            shaped((tokens, width), low),
            shaped((blocks, HEADS, ROWS, ROWS), low),
            shaped((tokens, width), low),
            shaped((tokens, width), jnp.float32),
            shaped((tokens, 1), jnp.float32),
        ),
        in_specs=[
            smem,
            smem,
            rows,
            pl.BlockSpec(memory_space=pl.ANY),
            pl.BlockSpec((VROWS, width), lambda b, h: (0, 0)),
        ],
        out_specs=(
            quad,
            quad,
            quad,
            pl.BlockSpec((1, 4, ROWS, ROWS), lambda b, h: (b, h, 0, 0)),
            rows,
            rows,
            pl.BlockSpec((ROWS, 1), lambda b, h: (b, 0)),
        ),
        scratch_shapes=[
            pltpu.VMEM((4, width, width), low),
            pltpu.VMEM((ROWS, ROWS), jnp.float32),
            pltpu.SemaphoreType.DMA((4,)),
        ],
        compiler_params=pltpu.CompilerParams(vmem_limit_bytes=56 * 2**20),
        name="attend_forward",
    )(counts, lengths, x, weights, vectors)


def feed_forward_both(
    counts,
    lengths,
    hat_ref,
    inverse_ref,
    cot_ref,
    w_hbm,
    vec_ref,
    mixed_ref,
    first_ref,
    branch_ref,
    context_ref,
    up_grad_ref,
    down_grad_ref,
    sum_ref,
    w_buf,
    active_ref,
    up_ref,
    hidden_ref,
    down_ref,
    slope_ref,
    w_sem,
):
    step = pl.program_id(0)
    blocks = pl.num_programs(0) - 4
    loads = [
        pltpu.make_async_copy(w_hbm.at[3 + at], w_buf.at[at], w_sem.at[at]) for at in range(9)
    ]

    @pl.when(step == 0)
    def _():
        for load in loads[1:] + loads[:1]:
            load.start()
        sum_ref[...] = jnp.zeros_like(sum_ref)
        for load in loads[1:] + loads[:1]:
            load.wait()

    @pl.when(step < blocks)
    def _():
        here = pl.ds(pl.multiple_of(step * ROWS, ROWS), ROWS)
        at_row = lax.broadcasted_iota(jnp.int32, (ROWS, 1), 0) + step * ROWS
        live = passage_facts(counts, lengths, at_row)[0].astype(jnp.float32)
        hat = hat_ref[...]
        hidden = hat * vec_ref[10:11, :] + vec_ref[8:9, :]
        hidden_low = hidden.astype(jnp.bfloat16)
        hidden_ref[here, :] = hidden_low
        total = hidden + vec_ref[7:8, :]
        for tile in range(4):
            up = dot(hidden_low, w_buf[1 + tile]) + vec_ref[3 + tile : 4 + tile, :]
            share = 0.5 + 0.5 * lax.erf(up * SQRT_HALF)
            slope_ref[tile] = share + up * (jnp.exp(up * up * -0.5) * INV_SQRT_TAU)
            active = (up * share).astype(jnp.bfloat16)
            active_ref[tile, here, :] = active
            total = total + dot(active, w_buf[5 + tile])
        hat_two, inverse_two = normalize(total)
        mixed_ref[...] = ((hat_two * vec_ref[11:12, :] + vec_ref[9:10, :]) * live).astype(jnp.bfloat16)
        grad_out = cot_ref[...].astype(jnp.float32) * live
        sum_ref[11:12, :] += columns_total(grad_out * hat_two)
        sum_ref[9:10, :] += columns_total(grad_out)
        second = normalize_back(grad_out * vec_ref[11:12, :], hat_two, inverse_two)
        down_low = second.astype(jnp.bfloat16)
        down_ref[here, :] = down_low
        sum_ref[7:8, :] += columns_total(down_low.astype(jnp.float32))
        grad_hidden = second
        for tile in range(4):
            pulled = dot_back(down_low, w_buf[5 + tile])
            up_low = (pulled * slope_ref[tile]).astype(jnp.bfloat16)
            up_ref[tile, here, :] = up_low
            sum_ref[3 + tile : 4 + tile, :] += columns_total(up_low.astype(jnp.float32))
            grad_hidden = grad_hidden + dot_back(up_low, w_buf[1 + tile])
        sum_ref[10:11, :] += columns_total(grad_hidden * hat)
        sum_ref[8:9, :] += columns_total(grad_hidden)
        grad_first = normalize_back(grad_hidden * vec_ref[10:11, :], hat, inverse_ref[...])
        first_ref[...] = grad_first
        branch_low = grad_first.astype(jnp.bfloat16)
        branch_ref[...] = branch_low
        sum_ref[2:3, :] += columns_total(branch_low.astype(jnp.float32))
        context_ref[...] = dot_back(branch_low, w_buf[0]).astype(jnp.bfloat16)

    @pl.when(step >= blocks)
    def _():
        tile = step - blocks
        up_grad_ref[0] = outer(hidden_ref[...], up_ref[tile]).astype(jnp.bfloat16)
        down_grad_ref[0] = outer(active_ref[tile], down_ref[...]).astype(jnp.bfloat16)


def fed_forward_both(counts, lengths, hat, inverse, cotangent, weights, vectors):
    tokens, width = hat.shape
    blocks = tokens // ROWS
    low = jnp.bfloat16
    smem = pl.BlockSpec(memory_space=pltpu.SMEM)
    shaped = jax.ShapeDtypeStruct

    def block_of(step):
        return jnp.minimum(step, blocks - 1)

    def tile_of(step):
        return jnp.maximum(step - blocks, 0)

    rows = pl.BlockSpec((ROWS, width), lambda i: (block_of(i), 0))
    tile = pl.BlockSpec((1, width, width), lambda i: (tile_of(i), 0, 0))
    return pl.pallas_call(
        feed_forward_both,
        grid=(blocks + 4,),
        out_shape=(
            shaped((tokens, width), low),
            shaped((tokens, width), jnp.float32),
            shaped((tokens, width), low),
            shaped((tokens, width), low),
            shaped((4, width, width), low),
            shaped((4, width, width), low),
            shaped((16, width), jnp.float32),
        ),
        in_specs=[
            smem,
            smem,
            rows,
            pl.BlockSpec((ROWS, 1), lambda i: (block_of(i), 0)),
            rows,
            pl.BlockSpec(memory_space=pl.ANY),
            pl.BlockSpec((VROWS, width), lambda i: (0, 0)),
        ],
        out_specs=(
            rows,
            rows,
            rows,
            rows,
            tile,
            tile,
            pl.BlockSpec((16, width), lambda i: (0, 0)),
        ),
        scratch_shapes=[
            pltpu.VMEM((9, width, width), low),
            pltpu.VMEM((4, tokens, width), low),
            pltpu.VMEM((4, tokens, width), low),
            pltpu.VMEM((tokens, width), low),
            pltpu.VMEM((tokens, width), low),
            pltpu.VMEM((4, ROWS, width), jnp.float32),
            pltpu.SemaphoreType.DMA((9,)),
        ],
        compiler_params=pltpu.CompilerParams(vmem_limit_bytes=60 * 2**20),
        name="feed_forward_both",
    )(counts, lengths, hat, inverse, cotangent, weights, vectors)


def attend_backward(
    p_ref,
    q_ref,
    k_ref,
    v_ref,
    x_ref,
    ctx_ref,
    grad_ctx_ref,
    branch_ref,
    first_ref,
    w_hbm,
    input_ref,
    grad_ref,
    sum_ref,
    w_buf,
    pulled_ref,
    w_sem,
):
    step = pl.program_id(0)
    inner = pl.num_programs(0) - 4
    block, quad = step // 3, lax.rem(step, 3)
    width = 256
    loads = [pltpu.make_async_copy(w_hbm.at[at], w_buf.at[at], w_sem.at[at]) for at in range(3)]

    @pl.when(step == 0)
    def _():
        for load in loads:
            load.start()
        sum_ref[...] = jnp.zeros_like(sum_ref)

    @pl.when(step < inner)
    def _():
        low_half = lax.broadcasted_iota(jnp.int32, (1, 128), 1) < 64
        here = pl.ds(pl.multiple_of(block * ROWS, ROWS), ROWS)
        for pair in range(2):
            part = slice(128 * pair, 128 * pair + 128)
            cols = pl.ds(pl.multiple_of(quad * width + 128 * pair, 128), 128)
            query, keyed, valued = q_ref[:, part], k_ref[:, part], v_ref[:, part]
            pull = grad_ctx_ref[here, cols]
            along = pull.astype(jnp.float32) * ctx_ref[here, cols].astype(jnp.float32)
            by_query, by_key, by_value = [], [], []
            for head in range(2):
                mask = low_half if head == 0 else ~low_half
                mine = jnp.where(mask, pull, jnp.zeros_like(pull))
                level = jnp.sum(jnp.where(mask, along, 0.0), -1, keepdims=True)
                probability = p_ref[0, 2 * pair + head]
                grad_prob = dot_back(mine, valued)
                grad_scores = (probability.astype(jnp.float32) * (grad_prob - level)).astype(jnp.bfloat16)
                by_query.append(dot(grad_scores, keyed))
                by_key.append(outer(grad_scores, query))
                by_value.append(outer(probability, pull))
            grad_query = (jnp.where(low_half, by_query[0], by_query[1]) * 0.125).astype(jnp.bfloat16)
            grad_value = jnp.where(low_half, by_value[0], by_value[1]).astype(jnp.bfloat16)
            pulled_ref[0, here, cols] = grad_query
            pulled_ref[1, here, cols] = jnp.where(low_half, by_key[0], by_key[1]).astype(jnp.bfloat16)
            pulled_ref[2, here, cols] = grad_value
            sum_ref[0:1, cols] += columns_total(grad_query.astype(jnp.float32))
            sum_ref[1:2, cols] += columns_total(grad_value.astype(jnp.float32))

    @pl.when(step == 2)
    def _():
        for load in loads:
            load.wait()

    @pl.when((step < inner) & (quad == 2))
    def _():
        here = pl.ds(pl.multiple_of(block * ROWS, ROWS), ROWS)
        total = first_ref[...]
        for at in range(3):
            total = total + dot_back(pulled_ref[at, here, :], w_buf[at])
        input_ref[...] = total

    @pl.when((step >= inner) & (step < inner + 3))
    def _():
        grad_ref[0] = outer(x_ref[...], pulled_ref[step - inner]).astype(jnp.bfloat16)

    @pl.when(step == inner + 3)
    def _():
        grad_ref[0] = outer(ctx_ref[...], branch_ref[...]).astype(jnp.bfloat16)


def attended_back(probs, query, keyed, valued, x, context, grad_context, grad_branch, grad_first, weights):
    tokens, width = x.shape
    blocks = tokens // ROWS
    inner = 3 * blocks
    low = jnp.bfloat16
    shaped = jax.ShapeDtypeStruct

    def at(step):
        step = jnp.minimum(step, inner - 1)
        return step // 3, lax.rem(step, 3)

    quad = pl.BlockSpec((ROWS, 256), lambda i: at(i))
    whole = pl.BlockSpec((tokens, width), lambda i: (0, 0))
    rows = pl.BlockSpec((ROWS, width), lambda i: (at(i)[0], 0))
    return pl.pallas_call(
        attend_backward,
        grid=(inner + 4,),
        out_shape=(
            shaped((tokens, width), jnp.float32),
            shaped((4, width, width), low),
            shaped((16, width), jnp.float32),
        ),
        in_specs=[
            pl.BlockSpec((1, 4, ROWS, ROWS), lambda i: (*at(i), 0, 0)),
            quad,
            quad,
            quad,
            whole,
            whole,
            whole,
            whole,
            rows,
            pl.BlockSpec(memory_space=pl.ANY),
        ],
        out_specs=(
            rows,
            pl.BlockSpec((1, width, width), lambda i: (jnp.maximum(i - inner, 0), 0, 0)),
            pl.BlockSpec((16, width), lambda i: (0, 0)),
        ),
        scratch_shapes=[
            pltpu.VMEM((3, width, width), low),
            pltpu.VMEM((3, tokens, width), low),
            pltpu.SemaphoreType.DMA((3,)),
        ],
        compiler_params=pltpu.CompilerParams(vmem_limit_bytes=56 * 2**20),
        name="attend_backward",
    )(probs, query, keyed, valued, x, context, grad_context, grad_branch, grad_first, weights)


def moved(param, grad, first, second, average, rate):
    param_new, first_new, second_new = adam_update(param, grad, first, second, rate)
    return param_new, first_new, second_new, average_rate * average + (1.0 - average_rate) * param_new


def update_kernel(
    gain_scale,
    grad_ref,
    master_ref,
    first_ref,
    second_ref,
    ema_ref,
    vec_grad_ref,
    vec_ref,
    vec_first_ref,
    vec_second_ref,
    vec_ema_ref,
    master_out,
    first_out,
    second_out,
    ema_out,
    copy_out,
    vec_out,
    vec_first_out,
    vec_second_out,
    vec_ema_out,
):
    grad = grad_ref[...].astype(jnp.float32) * gain_scale
    result = moved(master_ref[0], grad, first_ref[0], second_ref[0], ema_ref[0], tile_rate)
    master_out[0], first_out[0], second_out[0], ema_out[0] = result
    copy_out[0] = result[0].astype(jnp.bfloat16)

    @pl.when((pl.program_id(0) == 0) & (pl.program_id(1) == 0))
    def _():
        vec_grad = vec_grad_ref[0:VROWS, :] * gain_scale
        vec_out[...], vec_first_out[...], vec_second_out[...], vec_ema_out[...] = moved(
            vec_ref[...], vec_grad, vec_first_ref[...], vec_second_ref[...], vec_ema_ref[...], vector_rate
        )


def updated(gain_scale, slot_grads, master, first, second, ema, vec_grad, vectors, vec_first, vec_second, vec_ema):
    width = master.shape[-1]
    chunk = 192
    tile = pl.BlockSpec((1, 1, chunk, width), lambda s, r: (0, s, r, 0))
    vec = pl.BlockSpec((VROWS, width), lambda s, r: (0, 0))
    shaped = jax.ShapeDtypeStruct
    tile_shape = shaped(master.shape, jnp.float32)
    vec_shape = shaped((VROWS, width), jnp.float32)
    return pl.pallas_call(
        functools.partial(update_kernel, gain_scale),
        grid=(SLOTS, width // chunk),
        out_shape=(tile_shape,) * 4 + (shaped(master.shape, jnp.bfloat16),) + (vec_shape,) * 4,
        in_specs=[pl.BlockSpec((1, chunk, width), lambda s, r: (s, r, 0))]
        + [tile] * 4
        + [pl.BlockSpec((16, width), lambda s, r: (0, 0))]
        + [vec] * 4,
        out_specs=(tile,) * 5 + (vec,) * 4,
        compiler_params=pltpu.CompilerParams(vmem_limit_bytes=40 * 2**20),
        name="update",
    )(slot_grads, master, first, second, ema, vec_grad, vectors, vec_first, vec_second, vec_ema)


def attend_reduce(
    holds,
    keep_slot,
    p_ref,
    q_ref,
    k_ref,
    v_ref,
    x_ref,
    ctx_ref,
    grad_ctx_ref,
    branch_ref,
    first_hbm,
    w_hbm,
    up_hbm,
    down_hbm,
    late_ref,
    input_hbm,
    slot_grad,
    vec_out,
    w_buf,
    acc,
    pulled,
    part,
    own,
    from_core,
    from_far,
    from_mid,
    from_end,
    from_middle,
    total,
    snap,
    outbox,
    vec_now,
    vec_in,
    load_sem,
    own_sem,
    core_send,
    core_recv,
    far_send,
    far_recv,
    mid_send,
    mid_recv,
    z_send,
    z_recv,
    vec_send,
    vec_recv,
    out_send,
    out_recv,
):
    step = pl.program_id(0)
    quad, block = step // 2, lax.rem(step, 2)
    me = lax.axis_index("dp")
    z, y, x, core = place(me)
    in_plane = lax.rem(me, PLANE)
    sibling = me + 1 - 2 * core
    x_peer = me + 2 - 4 * x
    y_peer = me + 4 - 8 * y
    inner = (1 + z // 2) * PLANE + in_plane
    outer_end = lax.rem(lax.rem(z + 3, 4) * 3, 4) * PLANE + in_plane
    other_middle = (3 - z) * PLANE + in_plane
    is_end = (z == 0) | (z == 3)
    is_middle = (z == 1) | (z == 2)

    def items(batch):
        if batch < 4:
            return [(0, 4 + batch, slice(None)), (1, 8 + batch, slice(None))]
        cols = pl.ds(256 * (batch - 4), 256)
        return [(0, 0, cols), (1, 1, cols), (0, 2, cols), (1, 3, cols)]

    def held(tile):
        return part.at[tile, core] if tile < 4 else own.at[tile - 4]

    def source(tile, side):
        if tile < 4:
            return part.at[tile, side]
        return up_hbm.at[tile - 4, side] if tile < 8 else down_hbm.at[tile - 8, side]

    def own_loads(batch):
        return [
            pltpu.make_async_copy(source(tile, core), own.at[tile - 4], own_sem.at[batch, n])
            for n, (_, tile, _) in enumerate(items(batch))
        ]

    def core_copies(batch):
        return [
            remote(
                source(tile, 1 - core).at[:, :, :, cols],
                from_core.at[tile, :, :, :, cols],
                core_send.at[batch, n],
                core_recv.at[batch, n],
                sibling,
            )
            for n, (_, tile, cols) in enumerate(items(batch))
        ]

    def far_copies(batch):
        copies = []
        for n, (kind, tile, cols) in enumerate(items(batch)):
            mine = held(tile)
            copies.append(
                remote(
                    mine.at[:, 1 - y, :, cols] if kind else mine.at[1 - x, :, :, cols],
                    from_far.at[tile, :, :, cols],
                    far_send.at[batch, n],
                    far_recv.at[batch, n],
                    y_peer if kind else x_peer,
                )
            )
        return copies

    def mid_copies(batch):
        copies = []
        for n, (kind, tile, cols) in enumerate(items(batch)):
            mine = held(tile)
            copies.append(
                remote(
                    mine.at[1 - x, y, :, cols] if kind else mine.at[x, 1 - y, :, cols],
                    from_mid.at[tile, :, cols],
                    mid_send.at[batch, n],
                    mid_recv.at[batch, n],
                    x_peer if kind else y_peer,
                )
            )
        return copies

    def z_copies(batch, stage):
        copies = []
        for n, (_, tile, cols) in enumerate(items(batch)):
            if stage == 2:
                src, dst = total.at[tile, :, cols], total.at[tile, :, cols]
            else:
                src = held(tile).at[x, y, :, cols]
                dst = (from_middle if stage else from_end).at[tile, :, cols]
            copies.append(
                remote(
                    src,
                    dst,
                    z_send.at[stage, batch, n],
                    z_recv.at[stage, batch, n],
                    (inner, other_middle, outer_end)[stage],
                )
            )
        return copies

    def start(copies):
        for copy in copies:
            copy.start()

    def arrive(copies):
        for copy in copies:
            copy.wait_recv()

    def give_core(batch):
        if batch < 4:
            start(own_loads(batch))
        start(core_copies(batch))

    def give_far(batch):
        if batch < 4:
            for load in own_loads(batch):
                load.wait()
        arrive(core_copies(batch))
        for _, tile, cols in items(batch):
            mine = held(tile)
            mine[:, :, :, cols] = mine[:, :, :, cols] + from_core[tile, :, :, :, cols]
        start(far_copies(batch))

    def give_mid(batch):
        arrive(far_copies(batch))
        for kind, tile, cols in items(batch):
            mine = held(tile)
            if kind:
                mine[:, y, :, cols] = mine[:, y, :, cols] + from_far[tile, :, :, cols]
            else:
                mine[x, :, :, cols] = mine[x, :, :, cols] + from_far[tile, :, :, cols]
        start(mid_copies(batch))

    def give_end(batch):
        arrive(mid_copies(batch))
        for _, tile, cols in items(batch):
            mine = held(tile)
            mine[x, y, :, cols] = mine[x, y, :, cols] + from_mid[tile, :, cols]

        @pl.when(is_end)
        def _():
            start(z_copies(batch, 0))

    def give_middle(batch):
        @pl.when(is_middle)
        def _():
            arrive(z_copies(batch, 0))
            for _, tile, cols in items(batch):
                mine = held(tile)
                mine[x, y, :, cols] = mine[x, y, :, cols] + from_end[tile, :, cols]
            start(z_copies(batch, 1))

    def give_total(batch):
        @pl.when(is_middle)
        def _():
            arrive(z_copies(batch, 1))
            for _, tile, cols in items(batch):
                mine = held(tile)
                total[tile, :, cols] = mine[x, y, :, cols] + from_middle[tile, :, cols]
            start(z_copies(batch, 2))

    def take_total(batch):
        @pl.when(is_end)
        def _():
            arrive(z_copies(batch, 2))

    def deliver(third):
        cols = pl.ds(256 * third, 256)
        snap[...] = total[:, :, cols]

        def fill(at, carry):
            value = snap[holds[z * 2 * PLANE + at]]
            wanted = keep_slot[z * 2 * PLANE + at] > 0
            outbox[third, at] = jnp.where(wanted, value, jnp.zeros_like(value))
            return carry

        lax.fori_loop(0, 2 * PLANE, fill, 0)

        def send(hop, carry):
            target = lax.rem(in_plane + hop, PLANE)
            remote(
                outbox.at[third, pl.ds(2 * target, 2)],
                slot_grad.at[:, core, x, y, :, cols],
                out_send.at[third],
                out_recv.at[third],
                z * PLANE + target,
            ).start()
            return carry

        lax.fori_loop(1, PLANE, send, 0)
        keep_copy(third).start()

    def keep_copy(third):
        return pltpu.make_async_copy(
            outbox.at[third, pl.ds(2 * in_plane, 2)],
            slot_grad.at[:, core, x, y, :, pl.ds(256 * third, 256)],
            load_sem.at[5 + third],
        )

    def vec_copies(stage):
        if stage < 3:
            hops = [(stage, (sibling, x_peer, y_peer)[stage])]
        else:
            hops = [
                (2 + hop, lax.rem(z + hop, 4) * PLANE + in_plane) for hop in range(1, 4)
            ]
        return [
            remote(vec_now.at[stage], vec_in.at[at], vec_send.at[at], vec_recv.at[at], device)
            for at, device in hops
        ]

    def vec_next(stage):
        arrive(vec_copies(stage))
        vec_now[stage + 1] = vec_now[stage] + vec_in[stage]
        start(vec_copies(stage + 1))

    def first_load():
        return pltpu.make_async_copy(first_hbm, acc, load_sem.at[3])

    def input_store():
        return pltpu.make_async_copy(acc, input_hbm, load_sem.at[4])

    def w_loads():
        return [pltpu.make_async_copy(w_hbm.at[at], w_buf.at[at], load_sem.at[at]) for at in range(3)]

    def at_point(at, work):
        @pl.when(step == at)
        def _():
            for action, batch in work:
                action(batch)

    @pl.when(step == 0)
    def _():
        barrier = pltpu.get_barrier_semaphore()
        for hop in range(1, PLANE):
            other = z * PLANE + lax.rem(in_plane + hop, PLANE)
            pl.semaphore_signal(barrier, inc=1, device_id=(other,), device_id_type=MESH)
        for hop in range(1, 4):
            other = lax.rem(z + hop, 4) * PLANE + in_plane
            pl.semaphore_signal(barrier, inc=1, device_id=(other,), device_id_type=MESH)
        pl.semaphore_wait(barrier, PLANE + 2)
        give_core(0)
        give_core(1)
        start(w_loads() + [first_load()])
        vec_now[0] = late_ref[...]
        give_far(0)
        give_core(2)
        give_core(3)
        give_far(1)

    at_point(1, [(give_mid, 0), (give_far, 2)])
    at_point(2, [(give_mid, 1), (give_far, 3), (give_end, 0)])
    at_point(3, [(give_mid, 2), (give_far, 4), (give_end, 1), (give_middle, 0)])
    at_point(
        4, [(give_mid, 3), (give_far, 5), (give_end, 2), (give_middle, 1), (give_total, 0), (give_mid, 4)]
    )
    at_point(
        5, [(give_mid, 5), (give_end, 3), (give_middle, 2), (give_total, 1), (take_total, 0), (give_end, 4)]
    )

    low_half = lax.broadcasted_iota(jnp.int32, (1, 128), 1) < 64
    here = pl.ds(pl.multiple_of(block * ROWS, ROWS), ROWS)
    for pair in range(2):
        half = slice(128 * pair, 128 * pair + 128)
        cols = pl.ds(pl.multiple_of(quad * 256 + 128 * pair, 128), 128)
        query, keyed, valued = q_ref[:, half], k_ref[:, half], v_ref[:, half]
        pull = grad_ctx_ref[here, cols]
        along = pull.astype(jnp.float32) * ctx_ref[here, cols].astype(jnp.float32)
        by_query, by_key, by_value = [], [], []
        for head in range(2):
            mask = low_half if head == 0 else ~low_half
            mine = jnp.where(mask, pull, jnp.zeros_like(pull))
            level = jnp.sum(jnp.where(mask, along, 0.0), -1, keepdims=True)
            probability = p_ref[0, 2 * pair + head]
            grad_prob = dot_back(mine, valued)
            grad_scores = (probability.astype(jnp.float32) * (grad_prob - level)).astype(jnp.bfloat16)
            by_query.append(dot(grad_scores, keyed))
            by_key.append(outer(grad_scores, query))
            by_value.append(outer(probability, pull))
        grad_query = (jnp.where(low_half, by_query[0], by_query[1]) * 0.125).astype(jnp.bfloat16)
        grad_value = jnp.where(low_half, by_value[0], by_value[1]).astype(jnp.bfloat16)
        pulled[0, here, half] = grad_query
        pulled[1, here, half] = jnp.where(low_half, by_key[0], by_key[1]).astype(jnp.bfloat16)
        pulled[2, here, half] = grad_value
        vec_now[0, 0:1, cols] += columns_total(grad_query.astype(jnp.float32))
        vec_now[0, 1:2, cols] += columns_total(grad_value.astype(jnp.float32))

    @pl.when(step == 0)
    def _():
        for load in w_loads() + [first_load()]:
            load.wait()

    cols = pl.ds(pl.multiple_of(quad * 256, 256), 256)
    more = acc[here, :]
    for at in range(3):
        more = more + dot_back(pulled[at, here, :], w_buf[at, :, cols])
    acc[here, :] = more

    @pl.when(block == 1)
    def _():
        for tile in range(4):
            if tile < 3:
                value = outer(x_ref[...], pulled[tile])
            else:
                value = outer(ctx_ref[...], branch_ref[:, cols])
            part[tile, :, :, :, :, cols] = value.astype(jnp.bfloat16).reshape(2, 2, 2, PIECE, 256)

    at_point(1, [(give_core, 4)])
    at_point(3, [(give_core, 5)])

    @pl.when(step == 5)
    def _():
        input_store().start()
        give_core(6)
        start(vec_copies(0))
        give_middle(3)
        give_total(2)
        take_total(1)
        give_end(5)
        give_far(6)
        give_middle(4)
        give_total(3)
        take_total(2)
        vec_next(0)
        give_total(4)
        take_total(3)
        give_mid(6)
        give_middle(5)
        take_total(4)
        deliver(0)
        vec_next(1)
        give_end(6)
        give_total(5)
        give_middle(6)
        vec_next(2)
        take_total(5)
        deliver(1)
        give_total(6)
        take_total(6)
        deliver(2)
        arrive(vec_copies(3))
        summed = jnp.zeros(vec_out.shape, jnp.float32)
        for origin in range(4):
            hop = lax.rem(z - origin + 4, 4)
            summed = summed + jnp.where(hop == 0, vec_now[3], vec_in[2 + jnp.maximum(hop, 1)])
        vec_out[...] = summed
        for batch in range(7):
            for copy in core_copies(batch) + far_copies(batch) + mid_copies(batch):
                copy.wait_send()

            @pl.when(is_end)
            def _():
                for copy in z_copies(batch, 0):
                    copy.wait_send()

            @pl.when(is_middle)
            def _():
                for copy in z_copies(batch, 1) + z_copies(batch, 2):
                    copy.wait_send()

        for stage in range(4):
            for copy in vec_copies(stage):
                copy.wait_send()
        input_store().wait()
        for third in range(3):
            keep_copy(third).wait()
            most = outbox.at[third, pl.ds(0, 2 * PLANE - 2)]
            pltpu.make_async_copy(most, most, out_recv.at[third]).wait()
            pltpu.make_async_copy(most, most, out_send.at[third]).wait()


def attended_and_reduced(
    holds,
    keep_slot,
    probs,
    query,
    keyed,
    valued,
    x,
    context,
    grad_context,
    grad_branch,
    grad_first,
    weights,
    up_grads,
    down_grads,
    late_sums,
):
    tokens, width = x.shape
    low = jnp.bfloat16
    shaped = jax.ShapeDtypeStruct
    smem = pl.BlockSpec(memory_space=pltpu.SMEM)
    any_space = pl.BlockSpec(memory_space=pl.ANY)
    dma = pltpu.SemaphoreType.DMA
    once = pl.Buffered(1)
    quad = pl.BlockSpec((ROWS, 256), lambda i: (lax.rem(i, 2), i // 2))
    whole = pl.BlockSpec((tokens, width), lambda i: (0, 0), pipeline_mode=once)
    sums = pl.BlockSpec((16, width), lambda i: (0, 0))
    cut = (2, 2, 2, PIECE, width)
    input_grad, slot_grads, vector_sums = pl.pallas_call(
        attend_reduce,
        grid=(6,),
        out_shape=(
            shaped((tokens, width), jnp.float32),
            shaped((SLOTS,) + cut, low),
            shaped((16, width), jnp.float32),
        ),
        in_specs=[
            smem,
            smem,
            pl.BlockSpec((1, 4, ROWS, ROWS), lambda i: (lax.rem(i, 2), i // 2, 0, 0)),
            quad,
            quad,
            quad,
            whole,
            whole,
            whole,
            whole,
            any_space,
            any_space,
            any_space,
            any_space,
            sums,
        ],
        out_specs=(any_space, any_space, sums),
        scratch_shapes=[
            pltpu.VMEM((3, width, width), low),
            pltpu.VMEM((tokens, width), jnp.float32),
            pltpu.VMEM((3, tokens, 256), low),
            pltpu.VMEM((4,) + cut, low),
            pltpu.VMEM((8,) + cut[1:], low),
            pltpu.VMEM((TILES,) + cut[1:], low),
            pltpu.VMEM((TILES,) + cut[2:], low),
            pltpu.VMEM((TILES,) + cut[3:], low),
            pltpu.VMEM((TILES,) + cut[3:], low),
            pltpu.VMEM((TILES,) + cut[3:], low),
            pltpu.VMEM((TILES,) + cut[3:], low),
            pltpu.VMEM((TILES, PIECE, 256), low),
            pltpu.VMEM((3, 2 * PLANE, PIECE, 256), low),
            pltpu.VMEM((4, 16, width), jnp.float32),
            pltpu.VMEM((6, 16, width), jnp.float32),
            dma((8,)),
            dma((4, 2)),
            dma((7, 4)),
            dma((7, 4)),
            dma((7, 4)),
            dma((7, 4)),
            dma((7, 4)),
            dma((7, 4)),
            dma((3, 7, 4)),
            dma((3, 7, 4)),
            dma((6,)),
            dma((6,)),
            dma((3,)),
            dma((3,)),
        ],
        compiler_params=pltpu.CompilerParams(
            collective_id=1, has_side_effects=True, vmem_limit_bytes=62 * 2**20
        ),
        name="attend_reduce",
    )(
        holds,
        keep_slot,
        probs,
        query,
        keyed,
        valued,
        x,
        context,
        grad_context,
        grad_branch,
        grad_first,
        weights,
        up_grads.reshape((4,) + cut),
        down_grads.reshape((4,) + cut),
        late_sums,
    )
    return input_grad, slot_grads.reshape(SLOTS, width, width), vector_sums


def collected_tiles(tile_low, owners, slots):
    mine = owners == lax.axis_index("dp")
    local = jnp.where(mine[:, None, None], tile_low[slots], jnp.zeros((), tile_low.dtype))
    return lax.psum(local, "dp")


def summed_over_slice(parts, vector_terms, owners, slots):
    model_width = parts.shape[2]
    rows = parts.reshape(-1, model_width).astype(jnp.float32)
    summed_rows = lax.psum_scatter(rows, "dp", scatter_dimension=0, tiled=True)
    full_rows = lax.all_gather(summed_rows, "dp", axis=0, tiled=True)
    tile_grads = full_rows.reshape(parts.shape)
    myself = lax.axis_index("dp")
    slot_list = []
    for slot_number in range(SLOTS):
        select = (owners == myself) & (slots == slot_number)
        slot_list.append(jnp.sum(jnp.where(select[:, None, None], tile_grads, 0.0), 0))
    return jnp.stack(slot_list, 0), lax.psum(vector_terms, "dp")


def body(
    inputs,
    cotangent,
    counts,
    lengths,
    owners,
    tile_master,
    tile_first,
    tile_second,
    tile_ema,
    bias_vals,
    gain_vals,
    vector_first,
    vector_second,
    vector_ema,
):
    tokens = inputs.shape[0]
    small = lax.axis_size("dp") == GROUP
    slots = tile_slots(owners)
    vectors = jnp.concatenate([bias_vals, gain_vals], 0)
    tile_low = tile_master[0].astype(jnp.bfloat16)
    if small:
        weights = gathered_tiles(tile_low, owners * SLOTS + slots)
    else:
        weights = collected_tiles(tile_low, owners, slots)
    query, keyed, valued, probs, context, hat, inverse = attended(
        counts, lengths, inputs, weights, vectors
    )
    mixed, grad_first, grad_branch, grad_context, up_grads, down_grads, late_sums = fed_forward_both(
        counts, lengths, hat, inverse, cotangent, weights, vectors
    )
    gain_scale = float(tokens * lax.axis_size("dp")) ** (-0.5)
    if small:
        places = jnp.arange(SLOTS * GROUP, dtype=jnp.int32)
        match = (owners * SLOTS + slots)[None, :] == places[:, None]
        holds = jnp.sum(jnp.where(match, jnp.arange(TILES, dtype=jnp.int32)[None, :], 0), 1)
        keep_slot = jnp.sum(match.astype(jnp.int32), 1)
        input_grad, slot_grads, full_sums = attended_and_reduced(
            holds,
            keep_slot,
            probs,
            query,
            keyed,
            valued,
            inputs,
            context,
            grad_context,
            grad_branch,
            grad_first,
            weights,
            up_grads,
            down_grads,
            late_sums,
        )
    else:
        input_grad, early_grads, early_sums = attended_back(
            probs, query, keyed, valued, inputs, context, grad_context, grad_branch, grad_first, weights
        )
        parts = jnp.concatenate([early_grads, up_grads, down_grads], 0)
        slot_grads, full_sums = summed_over_slice(parts, late_sums + early_sums, owners, slots)
    return (mixed, input_grad) + tuple(
        updated(
            gain_scale,
            slot_grads,
            tile_master,
            tile_first,
            tile_second,
            tile_ema,
            full_sums,
            vectors,
            vector_first,
            vector_second,
            vector_ema,
        )
    )


def solution(mesh):
    placed = (
        P("dp", None),
        P("dp", None),
        P("dp", None),
        P("dp", None),
        P(),
        P("dp", None, None, None),
        P("dp", None, None, None),
        P("dp", None, None, None),
        P("dp", None, None, None),
        P(),
        P(),
        P(),
        P(),
        P(),
    )
    return jax.shard_map(
        body,
        mesh=mesh,
        in_specs=placed,
        out_specs=(
            P("dp", None),
            P("dp", None),
            P("dp", None, None, None),
            P("dp", None, None, None),
            P("dp", None, None, None),
            P("dp", None, None, None),
            P("dp", None, None, None),
            P(),
            P(),
            P(),
            P(),
        ),
        check_vma=False,
    )
```

```python
import functools

import jax
import jax.numpy as jnp
from jax import lax
from jax.experimental import pallas as pl
from jax.experimental.pallas import tpu as pltpu
from jax.sharding import PartitionSpec as P

HEADS = 12
BUCKET = 128
SLOTS = 2
TILES = 12
VROWS = 12
STEP = 5

norm_epsilon = 1e-12
tile_rate = 0.03
vector_rate = 0.2
first_decay = 0.5
second_decay = 0.5
adam_epsilon = 1e-08
weight_decay = 0.01
average_rate = 0.9


def tile_slots(owners):
    order = jnp.arange(owners.shape[0], dtype=jnp.int32)
    same = owners[:, None] == owners[None, :]
    earlier = order[None, :] < order[:, None]
    return jnp.sum((same & earlier).astype(jnp.int32), 1)


def adam_update(param, grad, first, second, rate):
    first_new = first_decay * first + (1.0 - first_decay) * grad
    second_new = second_decay * second + (1.0 - second_decay) * grad * grad
    first_hat = first_new / (1.0 - first_decay**STEP)
    second_hat = second_new / (1.0 - second_decay**STEP)
    param_new = param - rate * (
        first_hat / (jnp.sqrt(second_hat) + adam_epsilon) + weight_decay * param
    )
    return (param_new, first_new, second_new)


ROWS = 4 * BUCKET
SQRT_HALF = 0.7071067811865476
INV_SQRT_TAU = 0.3989422804014327
ALLOWED = 3.0e38
BARRED = -1000000000.0


def dot(left, right):
    return jnp.dot(left, right, preferred_element_type=jnp.float32)


def dot_back(left, right):
    return lax.dot_general(
        left, right, (((1,), (1,)), ((), ())), preferred_element_type=jnp.float32
    )


def outer(left, right):
    return lax.dot_general(
        left, right, (((0,), (0,)), ((), ())), preferred_element_type=jnp.float32
    )


def passage_facts(counts, lengths, position):
    places = lengths.shape[1]
    big_end = counts[0, 0]
    mid_end = big_end + counts[0, 1]
    all_end = mid_end + counts[0, 2]
    start = jnp.int32(0)
    member = jnp.zeros(position.shape, jnp.int32)
    usable = jnp.zeros(position.shape, jnp.int32)
    for number in range(places):
        size = jnp.where(
            number < big_end,
            4 * BUCKET,
            jnp.where(number < mid_end, 2 * BUCKET, jnp.where(number < all_end, BUCKET, 0)),
        )
        inside = (position >= start) & (position < start + size)
        live = inside & (position < start + lengths[0, number])
        member = jnp.where(inside, number + 1, member)
        usable = jnp.where(live, 1, usable)
        start = start + size
    passage = jnp.where(member > 0, member - 1, places + position // BUCKET)
    return usable, passage


def normalize(values):
    center = jnp.mean(values, -1, keepdims=True)
    centered = values - center
    spread = jnp.mean(centered * centered, -1, keepdims=True)
    inverse = lax.rsqrt(spread + norm_epsilon)
    return centered * inverse, inverse


def normalize_back(grad, hat, inverse):
    center = jnp.mean(grad, -1, keepdims=True)
    along = jnp.mean(grad * hat, -1, keepdims=True)
    return inverse * (grad - center - hat * along)


def columns_total(values):
    return jnp.sum(values, 0, keepdims=True)


def attention_caps(counts, lengths, block):
    at_row = lax.broadcasted_iota(jnp.int32, (ROWS, 1), 0) + block * ROWS
    at_column = lax.broadcasted_iota(jnp.int32, (1, ROWS), 1) + block * ROWS
    _, passage_row = passage_facts(counts, lengths, at_row)
    usable_column, passage_column = passage_facts(counts, lengths, at_column)
    allowed = (passage_row == passage_column) & ((usable_column == 1) | (at_row == at_column))
    return jnp.where(allowed, ALLOWED, BARRED)


def attend_quad(quad, weight, x_ref, vec_ref, cap_ref, q_ref, k_ref, v_ref, p_ref, ctx_ref):
    cols = pl.ds(pl.multiple_of(quad * 256, 256), 256)
    x = x_ref[...]
    query = (dot(x, weight(0, cols)) + vec_ref[0:1, cols]).astype(jnp.bfloat16)
    query = query * jnp.bfloat16(0.125)
    keyed = dot(x, weight(1, cols)).astype(jnp.bfloat16)
    valued = (dot(x, weight(2, cols)) + vec_ref[1:2, cols]).astype(jnp.bfloat16)
    q_ref[...] = query
    k_ref[...] = keyed
    v_ref[...] = valued
    low_half = lax.broadcasted_iota(jnp.int32, (1, 128), 1) < 64
    for pair in range(2):
        part = slice(128 * pair, 128 * pair + 128)
        contexts = []
        for head in range(2):
            here = low_half if head == 0 else ~low_half
            mine = jnp.where(here, query[:, part], jnp.zeros_like(query[:, part]))
            scores = jnp.minimum(dot_back(mine, keyed[:, part]), cap_ref[...])
            exponent = jnp.exp(scores - jnp.max(scores, -1, keepdims=True))
            inverse = 1.0 / jnp.sum(exponent, -1, keepdims=True)
            probability = (exponent * inverse).astype(jnp.bfloat16)
            p_ref[0, 2 * pair + head] = probability
            contexts.append(dot(probability, valued[:, part]))
        both = jnp.where(low_half, contexts[0], contexts[1]).astype(jnp.bfloat16)
        ctx_ref[:, pl.ds(pl.multiple_of(quad * 256 + 128 * pair, 128), 128)] = both


def close_block(w_out, x_ref, vec_ref, ctx_ref, hat_ref, inverse_ref):
    branch = dot(ctx_ref[...], w_out) + vec_ref[2:3, :]
    hat_ref[...], inverse_ref[...] = normalize(x_ref[...].astype(jnp.float32) + branch)


def attend_back_quad(quad, here, p_ref, q_ref, k_ref, v_ref, ctx_ref, grad_ctx_ref, pulled, add_sums):
    low_half = lax.broadcasted_iota(jnp.int32, (1, 128), 1) < 64
    for pair in range(2):
        half = slice(128 * pair, 128 * pair + 128)
        cols = pl.ds(pl.multiple_of(quad * 256 + 128 * pair, 128), 128)
        query, keyed, valued = q_ref[:, half], k_ref[:, half], v_ref[:, half]
        pull = grad_ctx_ref[here, cols]
        along = pull.astype(jnp.float32) * ctx_ref[here, cols].astype(jnp.float32)
        by_query, by_key, by_value = [], [], []
        for head in range(2):
            mask = low_half if head == 0 else ~low_half
            mine = jnp.where(mask, pull, jnp.zeros_like(pull))
            level = jnp.sum(jnp.where(mask, along, 0.0), -1, keepdims=True)
            probability = p_ref[0, 2 * pair + head]
            grad_prob = dot_back(mine, valued)
            grad_scores = (probability.astype(jnp.float32) * (grad_prob - level)).astype(jnp.bfloat16)
            by_query.append(dot(grad_scores, keyed))
            by_key.append(outer(grad_scores, query))
            by_value.append(outer(probability, pull))
        grad_query = (jnp.where(low_half, by_query[0], by_query[1]) * 0.125).astype(jnp.bfloat16)
        grad_value = jnp.where(low_half, by_value[0], by_value[1]).astype(jnp.bfloat16)
        pulled[0, here, half] = grad_query
        pulled[1, here, half] = jnp.where(low_half, by_key[0], by_key[1]).astype(jnp.bfloat16)
        pulled[2, here, half] = grad_value
        add_sums(cols, columns_total(grad_query.astype(jnp.float32)), columns_total(grad_value.astype(jnp.float32)))


def attend_forward(
    counts,
    lengths,
    x_ref,
    w_hbm,
    vec_ref,
    q_ref,
    k_ref,
    v_ref,
    p_ref,
    ctx_ref,
    hat_ref,
    inverse_ref,
    w_buf,
    cap_ref,
    w_sem,
):
    block, quad = pl.program_id(0), pl.program_id(1)
    loads = [pltpu.make_async_copy(w_hbm.at[at], w_buf.at[at], w_sem.at[at]) for at in range(4)]

    @pl.when((block == 0) & (quad == 0))
    def _():
        for load in loads:
            load.start()
        for load in loads:
            load.wait()

    @pl.when(quad == 0)
    def _():
        cap_ref[...] = attention_caps(counts, lengths, block)

    def weight(at, cols):
        return w_buf[at, :, cols]

    attend_quad(quad, weight, x_ref, vec_ref, cap_ref, q_ref, k_ref, v_ref, p_ref, ctx_ref)

    @pl.when(quad == 2)
    def _():
        close_block(w_buf[3], x_ref, vec_ref, ctx_ref, hat_ref, inverse_ref)


def attended(counts, lengths, x, weights, vectors):
    tokens, width = x.shape
    blocks = tokens // ROWS
    low = jnp.bfloat16
    smem = pl.BlockSpec(memory_space=pltpu.SMEM)
    quad = pl.BlockSpec((ROWS, 256), lambda b, h: (b, h))
    rows = pl.BlockSpec((ROWS, width), lambda b, h: (b, 0))
    shaped = jax.ShapeDtypeStruct
    return pl.pallas_call(
        attend_forward,
        grid=(blocks, 3),
        out_shape=(
            shaped((tokens, width), low),
            shaped((tokens, width), low),
            shaped((tokens, width), low),
            shaped((blocks, HEADS, ROWS, ROWS), low),
            shaped((tokens, width), low),
            shaped((tokens, width), jnp.float32),
            shaped((tokens, 1), jnp.float32),
        ),
        in_specs=[
            smem,
            smem,
            rows,
            pl.BlockSpec(memory_space=pl.ANY),
            pl.BlockSpec((VROWS, width), lambda b, h: (0, 0)),
        ],
        out_specs=(
            quad,
            quad,
            quad,
            pl.BlockSpec((1, 4, ROWS, ROWS), lambda b, h: (b, h, 0, 0)),
            rows,
            rows,
            pl.BlockSpec((ROWS, 1), lambda b, h: (b, 0)),
        ),
        scratch_shapes=[
            pltpu.VMEM((4, width, width), low),
            pltpu.VMEM((ROWS, ROWS), jnp.float32),
            pltpu.SemaphoreType.DMA((4,)),
        ],
        compiler_params=pltpu.CompilerParams(vmem_limit_bytes=56 * 2**20),
        name="attend_forward",
    )(counts, lengths, x, weights, vectors)


def feed_forward_both(
    counts,
    lengths,
    hat_ref,
    inverse_ref,
    cot_ref,
    w_hbm,
    vec_ref,
    mixed_ref,
    first_ref,
    branch_ref,
    context_ref,
    up_grad_ref,
    down_grad_ref,
    sum_ref,
    w_buf,
    active_ref,
    up_ref,
    hidden_ref,
    down_ref,
    slope_ref,
    w_sem,
):
    step = pl.program_id(0)
    blocks = pl.num_programs(0) - 4
    loads = [
        pltpu.make_async_copy(w_hbm.at[3 + at], w_buf.at[at], w_sem.at[at]) for at in range(9)
    ]

    @pl.when(step == 0)
    def _():
        for load in loads[1:] + loads[:1]:
            load.start()
        sum_ref[...] = jnp.zeros_like(sum_ref)
        for load in loads[1:] + loads[:1]:
            load.wait()

    @pl.when(step < blocks)
    def _():
        here = pl.ds(pl.multiple_of(step * ROWS, ROWS), ROWS)
        at_row = lax.broadcasted_iota(jnp.int32, (ROWS, 1), 0) + step * ROWS
        live = passage_facts(counts, lengths, at_row)[0].astype(jnp.float32)
        hat = hat_ref[...]
        hidden = hat * vec_ref[10:11, :] + vec_ref[8:9, :]
        hidden_low = hidden.astype(jnp.bfloat16)
        hidden_ref[here, :] = hidden_low
        total = hidden + vec_ref[7:8, :]
        for tile in range(4):
            up = dot(hidden_low, w_buf[1 + tile]) + vec_ref[3 + tile : 4 + tile, :]
            share = 0.5 + 0.5 * lax.erf(up * SQRT_HALF)
            slope_ref[tile] = share + up * (jnp.exp(up * up * -0.5) * INV_SQRT_TAU)
            active = (up * share).astype(jnp.bfloat16)
            active_ref[tile, here, :] = active
            total = total + dot(active, w_buf[5 + tile])
        hat_two, inverse_two = normalize(total)
        mixed_ref[...] = ((hat_two * vec_ref[11:12, :] + vec_ref[9:10, :]) * live).astype(jnp.bfloat16)
        grad_out = cot_ref[...].astype(jnp.float32) * live
        sum_ref[11:12, :] += columns_total(grad_out * hat_two)
        sum_ref[9:10, :] += columns_total(grad_out)
        second = normalize_back(grad_out * vec_ref[11:12, :], hat_two, inverse_two)
        down_low = second.astype(jnp.bfloat16)
        down_ref[here, :] = down_low
        sum_ref[7:8, :] += columns_total(down_low.astype(jnp.float32))
        grad_hidden = second
        for tile in range(4):
            pulled = dot_back(down_low, w_buf[5 + tile])
            up_low = (pulled * slope_ref[tile]).astype(jnp.bfloat16)
            up_ref[tile, here, :] = up_low
            sum_ref[3 + tile : 4 + tile, :] += columns_total(up_low.astype(jnp.float32))
            grad_hidden = grad_hidden + dot_back(up_low, w_buf[1 + tile])
        sum_ref[10:11, :] += columns_total(grad_hidden * hat)
        sum_ref[8:9, :] += columns_total(grad_hidden)
        grad_first = normalize_back(grad_hidden * vec_ref[10:11, :], hat, inverse_ref[...])
        first_ref[...] = grad_first
        branch_low = grad_first.astype(jnp.bfloat16)
        branch_ref[...] = branch_low
        sum_ref[2:3, :] += columns_total(branch_low.astype(jnp.float32))
        context_ref[...] = dot_back(branch_low, w_buf[0]).astype(jnp.bfloat16)

    @pl.when(step >= blocks)
    def _():
        tile = step - blocks
        up_grad_ref[0] = outer(hidden_ref[...], up_ref[tile]).astype(jnp.bfloat16)
        down_grad_ref[0] = outer(active_ref[tile], down_ref[...]).astype(jnp.bfloat16)


def fed_forward_both(counts, lengths, hat, inverse, cotangent, weights, vectors):
    tokens, width = hat.shape
    blocks = tokens // ROWS
    low = jnp.bfloat16
    smem = pl.BlockSpec(memory_space=pltpu.SMEM)
    shaped = jax.ShapeDtypeStruct

    def block_of(step):
        return jnp.minimum(step, blocks - 1)

    def tile_of(step):
        return jnp.maximum(step - blocks, 0)

    rows = pl.BlockSpec((ROWS, width), lambda i: (block_of(i), 0))
    tile = pl.BlockSpec((1, width, width), lambda i: (tile_of(i), 0, 0))
    return pl.pallas_call(
        feed_forward_both,
        grid=(blocks + 4,),
        out_shape=(
            shaped((tokens, width), low),
            shaped((tokens, width), jnp.float32),
            shaped((tokens, width), low),
            shaped((tokens, width), low),
            shaped((4, width, width), low),
            shaped((4, width, width), low),
            shaped((16, width), jnp.float32),
        ),
        in_specs=[
            smem,
            smem,
            rows,
            pl.BlockSpec((ROWS, 1), lambda i: (block_of(i), 0)),
            rows,
            pl.BlockSpec(memory_space=pl.ANY),
            pl.BlockSpec((VROWS, width), lambda i: (0, 0)),
        ],
        out_specs=(
            rows,
            rows,
            rows,
            rows,
            tile,
            tile,
            pl.BlockSpec((16, width), lambda i: (0, 0)),
        ),
        scratch_shapes=[
            pltpu.VMEM((9, width, width), low),
            pltpu.VMEM((4, tokens, width), low),
            pltpu.VMEM((4, tokens, width), low),
            pltpu.VMEM((tokens, width), low),
            pltpu.VMEM((tokens, width), low),
            pltpu.VMEM((4, ROWS, width), jnp.float32),
            pltpu.SemaphoreType.DMA((9,)),
        ],
        compiler_params=pltpu.CompilerParams(vmem_limit_bytes=60 * 2**20),
        name="feed_forward_both",
    )(counts, lengths, hat, inverse, cotangent, weights, vectors)


def attend_backward(
    p_ref,
    q_ref,
    k_ref,
    v_ref,
    x_ref,
    ctx_ref,
    grad_ctx_ref,
    branch_ref,
    first_ref,
    w_ref,
    input_ref,
    grad_ref,
    sum_ref,
    pulled,
):
    step = pl.program_id(0)
    quad, block = step // 2, lax.rem(step, 2)
    here = pl.ds(pl.multiple_of(block * ROWS, ROWS), ROWS)
    cols = pl.ds(pl.multiple_of(quad * 256, 256), 256)

    @pl.when(step == 0)
    def _():
        sum_ref[...] = jnp.zeros_like(sum_ref)
        input_ref[...] = first_ref[...]

    def add_sums(at, by_query, by_value):
        sum_ref[0:1, at] += by_query
        sum_ref[1:2, at] += by_value

    attend_back_quad(quad, here, p_ref, q_ref, k_ref, v_ref, ctx_ref, grad_ctx_ref, pulled, add_sums)
    more = input_ref[here, :]
    for at in range(3):
        more = more + dot_back(pulled[at, here, :], w_ref[at, :, cols])
    input_ref[here, :] = more

    @pl.when(block == 1)
    def _():
        for tile in range(3):
            grad_ref[tile, :, cols] = outer(x_ref[...], pulled[tile]).astype(jnp.bfloat16)
        grad_ref[3, :, cols] = outer(ctx_ref[...], branch_ref[:, cols]).astype(jnp.bfloat16)


def attended_back(probs, query, keyed, valued, x, context, grad_context, grad_branch, grad_first, weights):
    tokens, width = x.shape
    low = jnp.bfloat16
    shaped = jax.ShapeDtypeStruct
    once = pl.Buffered(1)
    quad = pl.BlockSpec((ROWS, 256), lambda i: (lax.rem(i, 2), i // 2))
    whole = pl.BlockSpec((tokens, width), lambda i: (0, 0), pipeline_mode=once)
    return pl.pallas_call(
        attend_backward,
        grid=(6,),
        out_shape=(
            shaped((tokens, width), jnp.float32),
            shaped((4, width, width), low),
            shaped((16, width), jnp.float32),
        ),
        in_specs=[
            pl.BlockSpec((1, 4, ROWS, ROWS), lambda i: (lax.rem(i, 2), i // 2, 0, 0)),
            quad,
            quad,
            quad,
            whole,
            whole,
            whole,
            whole,
            whole,
            pl.BlockSpec((3, width, width), lambda i: (0, 0, 0), pipeline_mode=once),
        ],
        out_specs=(
            whole,
            pl.BlockSpec((4, width, width), lambda i: (0, 0, 0), pipeline_mode=once),
            pl.BlockSpec((16, width), lambda i: (0, 0)),
        ),
        scratch_shapes=[pltpu.VMEM((3, tokens, 256), low)],
        compiler_params=pltpu.CompilerParams(vmem_limit_bytes=56 * 2**20),
        name="attend_backward",
    )(probs, query, keyed, valued, x, context, grad_context, grad_branch, grad_first, weights)


def moved(param, grad, first, second, average, rate):
    param_new, first_new, second_new = adam_update(param, grad, first, second, rate)
    return param_new, first_new, second_new, average_rate * average + (1.0 - average_rate) * param_new


def update_kernel(
    gain_scale,
    grad_ref,
    master_ref,
    first_ref,
    second_ref,
    ema_ref,
    vec_grad_ref,
    vec_ref,
    vec_first_ref,
    vec_second_ref,
    vec_ema_ref,
    master_out,
    first_out,
    second_out,
    ema_out,
    copy_out,
    vec_out,
    vec_first_out,
    vec_second_out,
    vec_ema_out,
):
    grad = grad_ref[...].astype(jnp.float32) * gain_scale
    result = moved(master_ref[0], grad, first_ref[0], second_ref[0], ema_ref[0], tile_rate)
    master_out[0], first_out[0], second_out[0], ema_out[0] = result
    copy_out[0] = result[0].astype(jnp.bfloat16)

    @pl.when((pl.program_id(0) == 0) & (pl.program_id(1) == 0))
    def _():
        vec_grad = vec_grad_ref[0:VROWS, :] * gain_scale
        vec_out[...], vec_first_out[...], vec_second_out[...], vec_ema_out[...] = moved(
            vec_ref[...], vec_grad, vec_first_ref[...], vec_second_ref[...], vec_ema_ref[...], vector_rate
        )


def updated(gain_scale, slot_grads, master, first, second, ema, vec_grad, vectors, vec_first, vec_second, vec_ema):
    width = master.shape[-1]
    chunk = 192
    tile = pl.BlockSpec((1, 1, chunk, width), lambda s, r: (0, s, r, 0))
    vec = pl.BlockSpec((VROWS, width), lambda s, r: (0, 0))
    shaped = jax.ShapeDtypeStruct
    tile_shape = shaped(master.shape, jnp.float32)
    vec_shape = shaped((VROWS, width), jnp.float32)
    return pl.pallas_call(
        functools.partial(update_kernel, gain_scale),
        grid=(SLOTS, width // chunk),
        out_shape=(tile_shape,) * 4 + (shaped(master.shape, jnp.bfloat16),) + (vec_shape,) * 4,
        in_specs=[pl.BlockSpec((1, chunk, width), lambda s, r: (s, r, 0))]
        + [tile] * 4
        + [pl.BlockSpec((16, width), lambda s, r: (0, 0))]
        + [vec] * 4,
        out_specs=(tile,) * 5 + (vec,) * 4,
        compiler_params=pltpu.CompilerParams(vmem_limit_bytes=40 * 2**20),
        name="update",
    )(slot_grads, master, first, second, ema, vec_grad, vectors, vec_first, vec_second, vec_ema)


MESH = pl.DeviceIdType.MESH
GROUP = 32
PAIRS = TILES // 2
PLANE = 8
PIECE = 96
PAIR_TILES = ((0, 1), (2, 3), (4, 8), (5, 9), (6, 10), (7, 11))
PARTS = ((0, 512), (512, 256))


def remote(src, dst, send, recv, device):
    return pltpu.make_async_remote_copy(
        src_ref=src, dst_ref=dst, send_sem=send, recv_sem=recv, device_id=(device,), device_id_type=MESH
    )


def place(device):
    core = lax.rem(device, 2)
    x = lax.rem(device // 2, 2)
    y = lax.rem(device // 4, 2)
    z = device // 8
    return z, y, x, core


def start(copies):
    for copy in copies:
        copy.start()


def arrive(copies):
    for copy in copies:
        copy.wait_recv()


def greet(z, in_plane):
    barrier = pltpu.get_barrier_semaphore()
    for hop in range(1, PLANE):
        other = z * PLANE + lax.rem(in_plane + hop, PLANE)
        pl.semaphore_signal(barrier, inc=1, device_id=(other,), device_id_type=MESH)
    for hop in range(1, 4):
        other = lax.rem(z + hop, 4) * PLANE + in_plane
        pl.semaphore_signal(barrier, inc=1, device_id=(other,), device_id_type=MESH)
    pl.semaphore_wait(barrier, PLANE + 2)


def along_z(z, in_plane):
    inner = (1 + z // 2) * PLANE + in_plane
    other_middle = (3 - z) * PLANE + in_plane
    outer_end = lax.rem(lax.rem(z + 3, 4) * 3, 4) * PLANE + in_plane
    return inner, other_middle, outer_end


def gather_attend(
    counts,
    lengths,
    spots,
    planes,
    x_ref,
    master_hbm,
    vec_ref,
    q_ref,
    k_ref,
    v_ref,
    p_ref,
    ctx_ref,
    hat_ref,
    inverse_ref,
    w_out,
    cap_ref,
    wide,
    low,
    stage_wide,
    stage_slim,
    chosen,
    from_end,
    from_middle,
    w_buf,
    wide_sem,
    out_sem,
    swap_send,
    swap_recv,
    z_send,
    z_recv,
    mid_send,
    mid_recv,
    far_send,
    far_recv,
    near_send,
    near_recv,
):
    step = pl.program_id(0)
    block, quad = step // 3, lax.rem(step, 3)
    me = lax.axis_index("dp")
    z, y, x, core = place(me)
    in_plane = lax.rem(me, PLANE)
    sibling = me + 1 - 2 * core
    x_peer = me + 2 - 4 * x
    y_peer = me + 4 - 8 * y
    z_targets = along_z(z, in_plane)
    stages = (stage_wide, stage_slim)
    is_end = (z == 0) | (z == 3)
    is_middle = (z == 1) | (z == 2)

    def lanes(part):
        return pl.ds(*PARTS[part])

    def swap(part):
        def send(hop, carry):
            target = lax.rem(in_plane + hop, PLANE)
            _, ty, tx, tc = place(target)
            remote(
                low.at[:, tc, tx, ty, :, lanes(part)],
                stages[part].at[pl.ds(2 * in_plane, 2)],
                swap_send.at[part],
                swap_recv.at[part],
                z * PLANE + target,
            ).start()
            return carry

        lax.fori_loop(1, PLANE, send, 0)

    def swap_wait(part, sem):
        most = stages[part].at[pl.ds(0, 2 * PLANE - 2)]
        pltpu.make_async_copy(most, most, sem.at[part]).wait()

    def choose(part):
        swap_wait(part, swap_recv)
        for pair in range(PAIRS):
            for n, tile in enumerate(PAIR_TILES[pair]):
                value = stages[part][spots[tile]]
                chosen[2 * pair + n, :, lanes(part)] = jnp.where(
                    planes[tile] == z, value, jnp.zeros_like(value)
                )

    def z_copy(pair, part, level):
        two = pl.ds(2 * pair, 2)
        cols = lanes(part)
        src = w_buf.at[two, core, x, y, :, cols] if level == 2 else chosen.at[two, :, cols]
        dst = (from_end.at[two, :, cols], from_middle.at[two, :, cols], src)[level]
        return remote(
            src, dst, z_send.at[level, pair, part], z_recv.at[level, pair, part], z_targets[level]
        )

    def z_end(pair, part):
        @pl.when(is_end)
        def _():
            z_copy(pair, part, 0).start()

    def z_middle(pair, part):
        @pl.when(is_middle)
        def _():
            z_copy(pair, part, 0).wait_recv()
            two, cols = pl.ds(2 * pair, 2), lanes(part)
            chosen[two, :, cols] = chosen[two, :, cols] + from_end[two, :, cols]
            z_copy(pair, part, 1).start()

    def z_total(pair, part):
        @pl.when(is_middle)
        def _():
            z_copy(pair, part, 1).wait_recv()
            two, cols = pl.ds(2 * pair, 2), lanes(part)
            w_buf[two, core, x, y, :, cols] = chosen[two, :, cols] + from_middle[two, :, cols]
            z_copy(pair, part, 2).start()

    def both(action, pair):
        action(pair, 0)
        action(pair, 1)

    def mid_copies(pair):
        copies = []
        for n, peer in enumerate((y_peer, x_peer)):
            at = 2 * pair + n
            spot = w_buf.at[at, core, x, y]
            copies.append(remote(spot, spot, mid_send.at[at], mid_recv.at[at], peer))
        return copies

    def halves(pair, late):
        row = 1 - x if late else x
        column = 1 - y if late else y
        return w_buf.at[2 * pair, core, row], w_buf.at[2 * pair + 1, core, :, column]

    def far_copies(pair):
        copies = []
        for n, peer in enumerate((x_peer, y_peer)):
            at = 2 * pair + n
            spot = halves(pair, False)[n]
            copies.append(remote(spot, spot, far_send.at[at], far_recv.at[at], peer))
        return copies

    def near_copies(pair, late):
        copies = []
        for n in range(2):
            at = 2 * pair + n
            spot = halves(pair, late)[n]
            sems = near_send.at[at, late], near_recv.at[at, late]
            copies.append(remote(spot, spot, *sems, sibling))
        return copies

    def give_mid(pair):
        @pl.when(is_end)
        def _():
            arrive([z_copy(pair, 0, 2), z_copy(pair, 1, 2)])

        start(mid_copies(pair))

    def give_far(pair):
        arrive(mid_copies(pair))
        start(far_copies(pair) + near_copies(pair, 0))

    def give_near(pair):
        arrive(far_copies(pair))
        start(near_copies(pair, 1))

    def out_copies(pair):
        return [
            pltpu.make_async_copy(w_buf.at[2 * pair + n], w_out.at[tile], out_sem.at[tile])
            for n, tile in enumerate(PAIR_TILES[pair])
        ]

    def finish(pair):
        arrive(near_copies(pair, 0) + near_copies(pair, 1))
        start(out_copies(pair))

    @pl.when(step == 0)
    def _():
        wide_load = pltpu.make_async_copy(master_hbm, wide, wide_sem)
        wide_load.start()
        greet(z, in_plane)
        wide_load.wait()
        low[...] = wide[...].astype(jnp.bfloat16)
        swap(0)
        for part in range(2):
            stages[part][pl.ds(2 * in_plane, 2)] = low[:, core, x, y, :, lanes(part)]
        swap_wait(0, swap_send)
        swap(1)
        choose(0)
        z_end(0, 0)
        z_end(1, 0)
        z_end(2, 0)
        z_middle(0, 0)
        z_middle(1, 0)
        z_total(0, 0)
        choose(1)
        z_end(0, 1)
        z_end(1, 1)
        z_middle(2, 0)
        z_total(1, 0)
        z_middle(0, 1)
        z_end(2, 1)
        z_middle(1, 1)
        z_total(0, 1)
        give_mid(0)
        z_total(1, 1)
        give_mid(1)
        z_total(2, 0)
        z_middle(2, 1)
        both(z_end, 3)
        give_far(0)
        z_total(2, 1)
        both(z_middle, 3)
        both(z_end, 4)
        give_far(1)
        give_mid(2)
        give_near(0)
        both(z_total, 3)
        both(z_middle, 4)
        both(z_end, 5)
        give_near(1)
        finish(0)
        give_far(2)
        finish(1)

    @pl.when(step == 1)
    def _():
        give_mid(3)
        both(z_total, 4)
        both(z_middle, 5)

    @pl.when(step == 2)
    def _():
        give_far(3)
        give_near(2)
        give_mid(4)
        both(z_total, 5)

    @pl.when(step == 3)
    def _():
        give_far(4)
        give_mid(5)
        give_near(3)
        finish(2)

    @pl.when(step == 4)
    def _():
        give_far(5)
        give_near(4)
        finish(3)

    @pl.when(quad == 0)
    def _():
        cap_ref[...] = attention_caps(counts, lengths, block)

    def weight(at, cols):
        return w_buf[at, :, :, :, :, cols].reshape(8 * PIECE, 256)

    attend_quad(quad, weight, x_ref, vec_ref, cap_ref, q_ref, k_ref, v_ref, p_ref, ctx_ref)

    @pl.when(quad == 2)
    def _():
        w_last = w_buf[3].reshape(8 * PIECE, 8 * PIECE)
        close_block(w_last, x_ref, vec_ref, ctx_ref, hat_ref, inverse_ref)

    @pl.when(step == 5)
    def _():
        give_near(5)
        finish(4)
        finish(5)
        swap_wait(1, swap_send)
        for pair in range(PAIRS):
            for copy in mid_copies(pair) + far_copies(pair) + near_copies(pair, 0) + near_copies(pair, 1):
                copy.wait_send()
            for copy in out_copies(pair):
                copy.wait()

            @pl.when(is_end)
            def _():
                for part in range(2):
                    z_copy(pair, part, 0).wait_send()

            @pl.when(is_middle)
            def _():
                for part in range(2):
                    z_copy(pair, part, 1).wait_send()
                    z_copy(pair, part, 2).wait_send()


def gathered_and_attended(counts, lengths, spots, planes, x, master, vectors):
    tokens, width = x.shape
    blocks = tokens // ROWS
    low = jnp.bfloat16
    smem = pl.BlockSpec(memory_space=pltpu.SMEM)
    any_space = pl.BlockSpec(memory_space=pl.ANY)
    dma = pltpu.SemaphoreType.DMA
    quad = pl.BlockSpec((ROWS, 256), lambda i: (i // 3, lax.rem(i, 3)))
    rows = pl.BlockSpec((ROWS, width), lambda i: (i // 3, 0))
    shaped = jax.ShapeDtypeStruct
    cut = (2, 2, 2, PIECE, width)
    results = pl.pallas_call(
        gather_attend,
        grid=(3 * blocks,),
        out_shape=(
            shaped((tokens, width), low),
            shaped((tokens, width), low),
            shaped((tokens, width), low),
            shaped((blocks, HEADS, ROWS, ROWS), low),
            shaped((tokens, width), low),
            shaped((tokens, width), jnp.float32),
            shaped((tokens, 1), jnp.float32),
            shaped((TILES,) + cut, low),
        ),
        in_specs=[
            smem,
            smem,
            smem,
            smem,
            rows,
            any_space,
            pl.BlockSpec((VROWS, width), lambda i: (0, 0)),
        ],
        out_specs=(
            quad,
            quad,
            quad,
            pl.BlockSpec((1, 4, ROWS, ROWS), lambda i: (i // 3, lax.rem(i, 3), 0, 0)),
            rows,
            rows,
            pl.BlockSpec((ROWS, 1), lambda i: (i // 3, 0)),
            any_space,
        ),
        scratch_shapes=[
            pltpu.VMEM((ROWS, ROWS), jnp.float32),
            pltpu.VMEM((SLOTS,) + cut, jnp.float32),
            pltpu.VMEM((SLOTS,) + cut, low),
            pltpu.VMEM((2 * PLANE, PIECE, PARTS[0][1]), low),
            pltpu.VMEM((2 * PLANE, PIECE, PARTS[1][1]), low),
            pltpu.VMEM((TILES, PIECE, width), low),
            pltpu.VMEM((TILES, PIECE, width), low),
            pltpu.VMEM((TILES, PIECE, width), low),
            pltpu.VMEM((TILES,) + cut, low),
            dma,
            dma((TILES,)),
            dma((2,)),
            dma((2,)),
            dma((3, PAIRS, 2)),
            dma((3, PAIRS, 2)),
            dma((TILES,)),
            dma((TILES,)),
            dma((TILES,)),
            dma((TILES,)),
            dma((TILES, 2)),
            dma((TILES, 2)),
        ],
        compiler_params=pltpu.CompilerParams(
            collective_id=0, has_side_effects=True, vmem_limit_bytes=60 * 2**20
        ),
        name="gather_attend",
    )(counts, lengths, spots, planes, x, master.reshape((SLOTS,) + cut), vectors)
    return results[:-1] + (results[-1].reshape(TILES, width, width),)


def attend_reduce(
    holds,
    keep_slot,
    p_ref,
    q_ref,
    k_ref,
    v_ref,
    x_ref,
    ctx_ref,
    grad_ctx_ref,
    branch_ref,
    first_hbm,
    w_hbm,
    up_hbm,
    down_hbm,
    late_ref,
    input_hbm,
    slot_grad,
    vec_out,
    w_buf,
    acc,
    pulled,
    part,
    own,
    from_core,
    from_far,
    from_mid,
    from_end,
    from_middle,
    total,
    snap,
    outbox,
    vec_now,
    vec_in,
    load_sem,
    own_sem,
    core_send,
    core_recv,
    far_send,
    far_recv,
    mid_send,
    mid_recv,
    z_send,
    z_recv,
    vec_send,
    vec_recv,
    out_send,
    out_recv,
):
    step = pl.program_id(0)
    quad, block = step // 2, lax.rem(step, 2)
    me = lax.axis_index("dp")
    z, y, x, core = place(me)
    in_plane = lax.rem(me, PLANE)
    sibling = me + 1 - 2 * core
    x_peer = me + 2 - 4 * x
    y_peer = me + 4 - 8 * y
    z_targets = along_z(z, in_plane)
    is_end = (z == 0) | (z == 3)
    is_middle = (z == 1) | (z == 2)

    def items(batch):
        if batch < 4:
            return [(0, 4 + batch, slice(None)), (1, 8 + batch, slice(None))]
        cols = pl.ds(256 * (batch - 4), 256)
        return [(0, 0, cols), (1, 1, cols), (0, 2, cols), (1, 3, cols)]

    def held(tile):
        return part.at[tile, core] if tile < 4 else own.at[tile - 4]

    def source(tile, side):
        if tile < 4:
            return part.at[tile, side]
        return up_hbm.at[tile - 4, side] if tile < 8 else down_hbm.at[tile - 8, side]

    def own_loads(batch):
        return [
            pltpu.make_async_copy(source(tile, core), own.at[tile - 4], own_sem.at[batch, n])
            for n, (_, tile, _) in enumerate(items(batch))
        ]

    def core_copies(batch):
        return [
            remote(
                source(tile, 1 - core).at[:, :, :, cols],
                from_core.at[tile, :, :, :, cols],
                core_send.at[batch, n],
                core_recv.at[batch, n],
                sibling,
            )
            for n, (_, tile, cols) in enumerate(items(batch))
        ]

    def far_copies(batch):
        copies = []
        for n, (kind, tile, cols) in enumerate(items(batch)):
            mine = held(tile)
            copies.append(
                remote(
                    mine.at[:, 1 - y, :, cols] if kind else mine.at[1 - x, :, :, cols],
                    from_far.at[tile, :, :, cols],
                    far_send.at[batch, n],
                    far_recv.at[batch, n],
                    y_peer if kind else x_peer,
                )
            )
        return copies

    def mid_copies(batch):
        copies = []
        for n, (kind, tile, cols) in enumerate(items(batch)):
            mine = held(tile)
            copies.append(
                remote(
                    mine.at[1 - x, y, :, cols] if kind else mine.at[x, 1 - y, :, cols],
                    from_mid.at[tile, :, cols],
                    mid_send.at[batch, n],
                    mid_recv.at[batch, n],
                    x_peer if kind else y_peer,
                )
            )
        return copies

    def z_copies(batch, stage):
        copies = []
        for n, (_, tile, cols) in enumerate(items(batch)):
            if stage == 2:
                src, dst = total.at[tile, :, cols], total.at[tile, :, cols]
            else:
                src = held(tile).at[x, y, :, cols]
                dst = (from_middle if stage else from_end).at[tile, :, cols]
            copies.append(
                remote(
                    src,
                    dst,
                    z_send.at[stage, batch, n],
                    z_recv.at[stage, batch, n],
                    z_targets[stage],
                )
            )
        return copies

    def give_core(batch):
        if batch < 4:
            start(own_loads(batch))
        start(core_copies(batch))

    def give_far(batch):
        if batch < 4:
            for load in own_loads(batch):
                load.wait()
        arrive(core_copies(batch))
        for _, tile, cols in items(batch):
            mine = held(tile)
            mine[:, :, :, cols] = mine[:, :, :, cols] + from_core[tile, :, :, :, cols]
        start(far_copies(batch))

    def give_mid(batch):
        arrive(far_copies(batch))
        for kind, tile, cols in items(batch):
            mine = held(tile)
            if kind:
                mine[:, y, :, cols] = mine[:, y, :, cols] + from_far[tile, :, :, cols]
            else:
                mine[x, :, :, cols] = mine[x, :, :, cols] + from_far[tile, :, :, cols]
        start(mid_copies(batch))

    def give_end(batch):
        arrive(mid_copies(batch))
        for _, tile, cols in items(batch):
            mine = held(tile)
            mine[x, y, :, cols] = mine[x, y, :, cols] + from_mid[tile, :, cols]

        @pl.when(is_end)
        def _():
            start(z_copies(batch, 0))

    def give_middle(batch):
        @pl.when(is_middle)
        def _():
            arrive(z_copies(batch, 0))
            for _, tile, cols in items(batch):
                mine = held(tile)
                mine[x, y, :, cols] = mine[x, y, :, cols] + from_end[tile, :, cols]
            start(z_copies(batch, 1))

    def give_total(batch):
        @pl.when(is_middle)
        def _():
            arrive(z_copies(batch, 1))
            for _, tile, cols in items(batch):
                mine = held(tile)
                total[tile, :, cols] = mine[x, y, :, cols] + from_middle[tile, :, cols]
            start(z_copies(batch, 2))

    def take_total(batch):
        @pl.when(is_end)
        def _():
            arrive(z_copies(batch, 2))

    def deliver(third):
        cols = pl.ds(256 * third, 256)
        snap[...] = total[:, :, cols]

        def fill(at, carry):
            value = snap[holds[z * 2 * PLANE + at]]
            wanted = keep_slot[z * 2 * PLANE + at] > 0
            outbox[third, at] = jnp.where(wanted, value, jnp.zeros_like(value))
            return carry

        lax.fori_loop(0, 2 * PLANE, fill, 0)

        def send(hop, carry):
            target = lax.rem(in_plane + hop, PLANE)
            remote(
                outbox.at[third, pl.ds(2 * target, 2)],
                slot_grad.at[:, core, x, y, :, cols],
                out_send.at[third],
                out_recv.at[third],
                z * PLANE + target,
            ).start()
            return carry

        lax.fori_loop(1, PLANE, send, 0)
        keep_copy(third).start()

    def keep_copy(third):
        return pltpu.make_async_copy(
            outbox.at[third, pl.ds(2 * in_plane, 2)],
            slot_grad.at[:, core, x, y, :, pl.ds(256 * third, 256)],
            load_sem.at[5 + third],
        )

    def vec_copies(stage):
        if stage < 3:
            hops = [(stage, (sibling, x_peer, y_peer)[stage])]
        else:
            hops = [
                (2 + hop, lax.rem(z + hop, 4) * PLANE + in_plane) for hop in range(1, 4)
            ]
        return [
            remote(vec_now.at[stage], vec_in.at[at], vec_send.at[at], vec_recv.at[at], device)
            for at, device in hops
        ]

    def vec_next(stage):
        arrive(vec_copies(stage))
        vec_now[stage + 1] = vec_now[stage] + vec_in[stage]
        start(vec_copies(stage + 1))

    def first_load():
        return pltpu.make_async_copy(first_hbm, acc, load_sem.at[3])

    def input_store():
        return pltpu.make_async_copy(acc, input_hbm, load_sem.at[4])

    def w_loads():
        return [pltpu.make_async_copy(w_hbm.at[at], w_buf.at[at], load_sem.at[at]) for at in range(3)]

    def at_point(at, work):
        @pl.when(step == at)
        def _():
            for action, batch in work:
                action(batch)

    @pl.when(step == 0)
    def _():
        greet(z, in_plane)
        give_core(0)
        give_core(1)
        start(w_loads() + [first_load()])
        vec_now[0] = late_ref[...]
        give_far(0)
        give_core(2)
        give_core(3)
        give_far(1)

    at_point(1, [(give_mid, 0), (give_far, 2)])
    at_point(2, [(give_mid, 1), (give_far, 3), (give_end, 0)])
    at_point(3, [(give_mid, 2), (give_far, 4), (give_end, 1), (give_middle, 0)])
    at_point(
        4, [(give_mid, 3), (give_far, 5), (give_end, 2), (give_middle, 1), (give_total, 0), (give_mid, 4)]
    )
    at_point(
        5, [(give_mid, 5), (give_end, 3), (give_middle, 2), (give_total, 1), (take_total, 0), (give_end, 4)]
    )

    here = pl.ds(pl.multiple_of(block * ROWS, ROWS), ROWS)

    def add_sums(at, by_query, by_value):
        vec_now[0, 0:1, at] += by_query
        vec_now[0, 1:2, at] += by_value

    attend_back_quad(quad, here, p_ref, q_ref, k_ref, v_ref, ctx_ref, grad_ctx_ref, pulled, add_sums)

    @pl.when(step == 0)
    def _():
        for load in w_loads() + [first_load()]:
            load.wait()

    cols = pl.ds(pl.multiple_of(quad * 256, 256), 256)
    more = acc[here, :]
    for at in range(3):
        more = more + dot_back(pulled[at, here, :], w_buf[at, :, cols])
    acc[here, :] = more

    @pl.when(block == 1)
    def _():
        for tile in range(4):
            if tile < 3:
                value = outer(x_ref[...], pulled[tile])
            else:
                value = outer(ctx_ref[...], branch_ref[:, cols])
            part[tile, :, :, :, :, cols] = value.astype(jnp.bfloat16).reshape(2, 2, 2, PIECE, 256)

    at_point(1, [(give_core, 4)])
    at_point(3, [(give_core, 5)])

    @pl.when(step == 5)
    def _():
        input_store().start()
        give_core(6)
        start(vec_copies(0))
        give_middle(3)
        give_total(2)
        take_total(1)
        give_end(5)
        give_far(6)
        give_middle(4)
        give_total(3)
        take_total(2)
        vec_next(0)
        give_total(4)
        take_total(3)
        give_mid(6)
        give_middle(5)
        take_total(4)
        deliver(0)
        vec_next(1)
        give_end(6)
        give_total(5)
        give_middle(6)
        vec_next(2)
        take_total(5)
        deliver(1)
        give_total(6)
        take_total(6)
        deliver(2)
        arrive(vec_copies(3))
        summed = jnp.zeros(vec_out.shape, jnp.float32)
        for origin in range(4):
            hop = lax.rem(z - origin + 4, 4)
            summed = summed + jnp.where(hop == 0, vec_now[3], vec_in[2 + jnp.maximum(hop, 1)])
        vec_out[...] = summed
        for batch in range(7):
            for copy in core_copies(batch) + far_copies(batch) + mid_copies(batch):
                copy.wait_send()

            @pl.when(is_end)
            def _():
                for copy in z_copies(batch, 0):
                    copy.wait_send()

            @pl.when(is_middle)
            def _():
                for copy in z_copies(batch, 1) + z_copies(batch, 2):
                    copy.wait_send()

        for stage in range(4):
            for copy in vec_copies(stage):
                copy.wait_send()
        input_store().wait()
        for third in range(3):
            keep_copy(third).wait()
            most = outbox.at[third, pl.ds(0, 2 * PLANE - 2)]
            pltpu.make_async_copy(most, most, out_recv.at[third]).wait()
            pltpu.make_async_copy(most, most, out_send.at[third]).wait()


def attended_and_reduced(
    holds,
    keep_slot,
    probs,
    query,
    keyed,
    valued,
    x,
    context,
    grad_context,
    grad_branch,
    grad_first,
    weights,
    up_grads,
    down_grads,
    late_sums,
):
    tokens, width = x.shape
    low = jnp.bfloat16
    shaped = jax.ShapeDtypeStruct
    smem = pl.BlockSpec(memory_space=pltpu.SMEM)
    any_space = pl.BlockSpec(memory_space=pl.ANY)
    dma = pltpu.SemaphoreType.DMA
    once = pl.Buffered(1)
    quad = pl.BlockSpec((ROWS, 256), lambda i: (lax.rem(i, 2), i // 2))
    whole = pl.BlockSpec((tokens, width), lambda i: (0, 0), pipeline_mode=once)
    sums = pl.BlockSpec((16, width), lambda i: (0, 0))
    cut = (2, 2, 2, PIECE, width)
    input_grad, slot_grads, vector_sums = pl.pallas_call(
        attend_reduce,
        grid=(6,),
        out_shape=(
            shaped((tokens, width), jnp.float32),
            shaped((SLOTS,) + cut, low),
            shaped((16, width), jnp.float32),
        ),
        in_specs=[
            smem,
            smem,
            pl.BlockSpec((1, 4, ROWS, ROWS), lambda i: (lax.rem(i, 2), i // 2, 0, 0)),
            quad,
            quad,
            quad,
            whole,
            whole,
            whole,
            whole,
            any_space,
            any_space,
            any_space,
            any_space,
            sums,
        ],
        out_specs=(any_space, any_space, sums),
        scratch_shapes=[
            pltpu.VMEM((3, width, width), low),
            pltpu.VMEM((tokens, width), jnp.float32),
            pltpu.VMEM((3, tokens, 256), low),
            pltpu.VMEM((4,) + cut, low),
            pltpu.VMEM((8,) + cut[1:], low),
            pltpu.VMEM((TILES,) + cut[1:], low),
            pltpu.VMEM((TILES,) + cut[2:], low),
            pltpu.VMEM((TILES,) + cut[3:], low),
            pltpu.VMEM((TILES,) + cut[3:], low),
            pltpu.VMEM((TILES,) + cut[3:], low),
            pltpu.VMEM((TILES,) + cut[3:], low),
            pltpu.VMEM((TILES, PIECE, 256), low),
            pltpu.VMEM((3, 2 * PLANE, PIECE, 256), low),
            pltpu.VMEM((4, 16, width), jnp.float32),
            pltpu.VMEM((6, 16, width), jnp.float32),
            dma((8,)),
            dma((4, 2)),
            dma((7, 4)),
            dma((7, 4)),
            dma((7, 4)),
            dma((7, 4)),
            dma((7, 4)),
            dma((7, 4)),
            dma((3, 7, 4)),
            dma((3, 7, 4)),
            dma((6,)),
            dma((6,)),
            dma((3,)),
            dma((3,)),
        ],
        compiler_params=pltpu.CompilerParams(
            collective_id=1, has_side_effects=True, vmem_limit_bytes=62 * 2**20
        ),
        name="attend_reduce",
    )(
        holds,
        keep_slot,
        probs,
        query,
        keyed,
        valued,
        x,
        context,
        grad_context,
        grad_branch,
        grad_first,
        weights,
        up_grads.reshape((4,) + cut),
        down_grads.reshape((4,) + cut),
        late_sums,
    )
    return input_grad, slot_grads.reshape(SLOTS, width, width), vector_sums


def collected_tiles(tile_low, owners, slots):
    mine = owners == lax.axis_index("dp")
    local = jnp.where(mine[:, None, None], tile_low[slots], jnp.zeros((), tile_low.dtype))
    return lax.psum(local, "dp")


def summed_over_slice(parts, vector_terms, owners, slots):
    model_width = parts.shape[2]
    rows = parts.reshape(-1, model_width).astype(jnp.float32)
    summed_rows = lax.psum_scatter(rows, "dp", scatter_dimension=0, tiled=True)
    full_rows = lax.all_gather(summed_rows, "dp", axis=0, tiled=True)
    tile_grads = full_rows.reshape(parts.shape)
    myself = lax.axis_index("dp")
    slot_list = []
    for slot_number in range(SLOTS):
        select = (owners == myself) & (slots == slot_number)
        slot_list.append(jnp.sum(jnp.where(select[:, None, None], tile_grads, 0.0), 0))
    return jnp.stack(slot_list, 0), lax.psum(vector_terms, "dp")


def body(
    inputs,
    cotangent,
    counts,
    lengths,
    owners,
    tile_master,
    tile_first,
    tile_second,
    tile_ema,
    bias_vals,
    gain_vals,
    vector_first,
    vector_second,
    vector_ema,
):
    tokens = inputs.shape[0]
    small = lax.axis_size("dp") == GROUP
    slots = tile_slots(owners)
    vectors = jnp.concatenate([bias_vals, gain_vals], 0)
    if small:
        picks = owners * SLOTS + slots
        per_plane = SLOTS * PLANE
        query, keyed, valued, probs, context, hat, inverse, weights = gathered_and_attended(
            counts, lengths, picks % per_plane, picks // per_plane, inputs, tile_master, vectors
        )
    else:
        weights = collected_tiles(tile_master[0].astype(jnp.bfloat16), owners, slots)
        query, keyed, valued, probs, context, hat, inverse = attended(
            counts, lengths, inputs, weights, vectors
        )
    mixed, grad_first, grad_branch, grad_context, up_grads, down_grads, late_sums = fed_forward_both(
        counts, lengths, hat, inverse, cotangent, weights, vectors
    )
    gain_scale = float(tokens * lax.axis_size("dp")) ** (-0.5)
    if small:
        places = jnp.arange(SLOTS * GROUP, dtype=jnp.int32)
        match = (owners * SLOTS + slots)[None, :] == places[:, None]
        holds = jnp.sum(jnp.where(match, jnp.arange(TILES, dtype=jnp.int32)[None, :], 0), 1)
        keep_slot = jnp.sum(match.astype(jnp.int32), 1)
        input_grad, slot_grads, full_sums = attended_and_reduced(
            holds,
            keep_slot,
            probs,
            query,
            keyed,
            valued,
            inputs,
            context,
            grad_context,
            grad_branch,
            grad_first,
            weights,
            up_grads,
            down_grads,
            late_sums,
        )
    else:
        input_grad, early_grads, early_sums = attended_back(
            probs, query, keyed, valued, inputs, context, grad_context, grad_branch, grad_first, weights
        )
        parts = jnp.concatenate([early_grads, up_grads, down_grads], 0)
        slot_grads, full_sums = summed_over_slice(parts, late_sums + early_sums, owners, slots)
    return (mixed, input_grad) + tuple(
        updated(
            gain_scale,
            slot_grads,
            tile_master,
            tile_first,
            tile_second,
            tile_ema,
            full_sums,
            vectors,
            vector_first,
            vector_second,
            vector_ema,
        )
    )


def solution(mesh):
    placed = (
        P("dp", None),
        P("dp", None),
        P("dp", None),
        P("dp", None),
        P(),
        P("dp", None, None, None),
        P("dp", None, None, None),
        P("dp", None, None, None),
        P("dp", None, None, None),
        P(),
        P(),
        P(),
        P(),
        P(),
    )
    return jax.shard_map(
        body,
        mesh=mesh,
        in_specs=placed,
        out_specs=(
            P("dp", None),
            P("dp", None),
            P("dp", None, None, None),
            P("dp", None, None, None),
            P("dp", None, None, None),
            P("dp", None, None, None),
            P("dp", None, None, None),
            P(),
            P(),
            P(),
            P(),
        ),
        check_vma=False,
    )
```

```python
import functools

import jax
import jax.numpy as jnp
from jax import lax
from jax.experimental import pallas as pl
from jax.experimental.pallas import tpu as pltpu
from jax.sharding import PartitionSpec as P

HEADS = 12
BUCKET = 128
SLOTS = 2
TILES = 12
VROWS = 12
STEP = 5

norm_epsilon = 1e-12
tile_rate = 0.03
vector_rate = 0.2
first_decay = 0.5
second_decay = 0.5
adam_epsilon = 1e-08
weight_decay = 0.01
average_rate = 0.9


def tile_slots(owners):
    order = jnp.arange(owners.shape[0], dtype=jnp.int32)
    same = owners[:, None] == owners[None, :]
    earlier = order[None, :] < order[:, None]
    return jnp.sum((same & earlier).astype(jnp.int32), 1)


def adam_update(param, grad, first, second, rate):
    first_new = first_decay * first + (1.0 - first_decay) * grad
    second_new = second_decay * second + (1.0 - second_decay) * grad * grad
    first_hat = first_new / (1.0 - first_decay**STEP)
    second_hat = second_new / (1.0 - second_decay**STEP)
    param_new = param - rate * (
        first_hat / (jnp.sqrt(second_hat) + adam_epsilon) + weight_decay * param
    )
    return (param_new, first_new, second_new)


ROWS = 4 * BUCKET
SQRT_HALF = 0.7071067811865476
INV_SQRT_TAU = 0.3989422804014327
ALLOWED = 3.0e38
BARRED = -1000000000.0


def dot(left, right):
    return jnp.dot(left, right, preferred_element_type=jnp.float32)


def dot_back(left, right):
    return lax.dot_general(
        left, right, (((1,), (1,)), ((), ())), preferred_element_type=jnp.float32
    )


def outer(left, right):
    return lax.dot_general(
        left, right, (((0,), (0,)), ((), ())), preferred_element_type=jnp.float32
    )


def passage_facts(counts, lengths, position):
    places = lengths.shape[1]
    big_end = counts[0, 0]
    mid_end = big_end + counts[0, 1]
    all_end = mid_end + counts[0, 2]
    start = jnp.int32(0)
    member = jnp.zeros(position.shape, jnp.int32)
    usable = jnp.zeros(position.shape, jnp.int32)
    for number in range(places):
        size = jnp.where(
            number < big_end,
            4 * BUCKET,
            jnp.where(number < mid_end, 2 * BUCKET, jnp.where(number < all_end, BUCKET, 0)),
        )
        inside = (position >= start) & (position < start + size)
        live = inside & (position < start + lengths[0, number])
        member = jnp.where(inside, number + 1, member)
        usable = jnp.where(live, 1, usable)
        start = start + size
    passage = jnp.where(member > 0, member - 1, places + position // BUCKET)
    return usable, passage


def normalize(values):
    center = jnp.mean(values, -1, keepdims=True)
    centered = values - center
    spread = jnp.mean(centered * centered, -1, keepdims=True)
    inverse = lax.rsqrt(spread + norm_epsilon)
    return centered * inverse, inverse


def normalize_back(grad, hat, inverse):
    center = jnp.mean(grad, -1, keepdims=True)
    along = jnp.mean(grad * hat, -1, keepdims=True)
    return inverse * (grad - center - hat * along)


def columns_total(values):
    return jnp.sum(values, 0, keepdims=True)


def attention_caps(counts, lengths, block):
    at_row = lax.broadcasted_iota(jnp.int32, (ROWS, 1), 0) + block * ROWS
    at_column = lax.broadcasted_iota(jnp.int32, (1, ROWS), 1) + block * ROWS
    _, passage_row = passage_facts(counts, lengths, at_row)
    usable_column, passage_column = passage_facts(counts, lengths, at_column)
    allowed = (passage_row == passage_column) & ((usable_column == 1) | (at_row == at_column))
    return jnp.where(allowed, ALLOWED, BARRED)


def attend_quad(quad, weight, x_ref, vec_ref, cap_ref, q_ref, k_ref, v_ref, p_ref, ctx_ref):
    cols = pl.ds(pl.multiple_of(quad * 256, 256), 256)
    x = x_ref[...]
    query = (dot(x, weight(0, cols)) + vec_ref[0:1, cols]).astype(jnp.bfloat16)
    query = query * jnp.bfloat16(0.125)
    keyed = dot(x, weight(1, cols)).astype(jnp.bfloat16)
    valued = (dot(x, weight(2, cols)) + vec_ref[1:2, cols]).astype(jnp.bfloat16)
    q_ref[...] = query
    k_ref[...] = keyed
    v_ref[...] = valued
    low_half = lax.broadcasted_iota(jnp.int32, (1, 128), 1) < 64
    for pair in range(2):
        part = slice(128 * pair, 128 * pair + 128)
        contexts = []
        for head in range(2):
            here = low_half if head == 0 else ~low_half
            mine = jnp.where(here, query[:, part], jnp.zeros_like(query[:, part]))
            scores = jnp.minimum(dot_back(mine, keyed[:, part]), cap_ref[...])
            exponent = jnp.exp(scores - jnp.max(scores, -1, keepdims=True))
            inverse = 1.0 / jnp.sum(exponent, -1, keepdims=True)
            probability = (exponent * inverse).astype(jnp.bfloat16)
            p_ref[0, 2 * pair + head] = probability
            contexts.append(dot(probability, valued[:, part]))
        both = jnp.where(low_half, contexts[0], contexts[1]).astype(jnp.bfloat16)
        ctx_ref[:, pl.ds(pl.multiple_of(quad * 256 + 128 * pair, 128), 128)] = both


def close_block(w_out, x_ref, vec_ref, ctx_ref, hat_ref, inverse_ref):
    branch = dot(ctx_ref[...], w_out) + vec_ref[2:3, :]
    hat_ref[...], inverse_ref[...] = normalize(x_ref[...].astype(jnp.float32) + branch)


def attend_back_pair(pair, here, p_ref, qkv, ctx_ref, grad_ctx_ref, pulled, half, add_sums):
    low_half = lax.broadcasted_iota(jnp.int32, (1, 128), 1) < 64
    cols = pl.ds(pl.multiple_of(pair * 128, 128), 128)
    query, keyed, valued = qkv
    pull = grad_ctx_ref[here, cols]
    along = pull.astype(jnp.float32) * ctx_ref[here, cols].astype(jnp.float32)
    by_query, by_key, by_value = [], [], []
    for head in range(2):
        mask = low_half if head == 0 else ~low_half
        mine = jnp.where(mask, pull, jnp.zeros_like(pull))
        level = jnp.sum(jnp.where(mask, along, 0.0), -1, keepdims=True)
        probability = p_ref[head]
        grad_prob = dot_back(mine, valued)
        grad_scores = (probability.astype(jnp.float32) * (grad_prob - level)).astype(jnp.bfloat16)
        by_query.append(dot(grad_scores, keyed))
        by_key.append(outer(grad_scores, query))
        by_value.append(outer(probability, pull))
    grad_query = (jnp.where(low_half, by_query[0], by_query[1]) * 0.125).astype(jnp.bfloat16)
    grad_value = jnp.where(low_half, by_value[0], by_value[1]).astype(jnp.bfloat16)
    pulled[0, here, half] = grad_query
    pulled[1, here, half] = jnp.where(low_half, by_key[0], by_key[1]).astype(jnp.bfloat16)
    pulled[2, here, half] = grad_value
    add_sums(cols, columns_total(grad_query.astype(jnp.float32)), columns_total(grad_value.astype(jnp.float32)))


def gelu_parts(up):
    share = 0.5 + 0.5 * lax.erf(up * SQRT_HALF)
    slope = share + up * (jnp.exp(up * up * -0.5) * INV_SQRT_TAU)
    return (up * share).astype(jnp.bfloat16), slope


def attend_forward(
    counts,
    lengths,
    x_ref,
    w_hbm,
    vec_ref,
    q_ref,
    k_ref,
    v_ref,
    p_ref,
    ctx_ref,
    hat_ref,
    inverse_ref,
    w_buf,
    cap_ref,
    w_sem,
):
    block, quad = pl.program_id(0), pl.program_id(1)
    loads = [pltpu.make_async_copy(w_hbm.at[at], w_buf.at[at], w_sem.at[at]) for at in range(4)]

    @pl.when((block == 0) & (quad == 0))
    def _():
        for load in loads:
            load.start()
        for load in loads:
            load.wait()

    @pl.when(quad == 0)
    def _():
        cap_ref[...] = attention_caps(counts, lengths, block)

    def weight(at, cols):
        return w_buf[at, :, cols]

    attend_quad(quad, weight, x_ref, vec_ref, cap_ref, q_ref, k_ref, v_ref, p_ref, ctx_ref)

    @pl.when(quad == 2)
    def _():
        close_block(w_buf[3], x_ref, vec_ref, ctx_ref, hat_ref, inverse_ref)


def attended(counts, lengths, x, weights, vectors):
    tokens, width = x.shape
    blocks = tokens // ROWS
    low = jnp.bfloat16
    smem = pl.BlockSpec(memory_space=pltpu.SMEM)
    quad = pl.BlockSpec((ROWS, 256), lambda b, h: (b, h))
    rows = pl.BlockSpec((ROWS, width), lambda b, h: (b, 0))
    shaped = jax.ShapeDtypeStruct
    return pl.pallas_call(
        attend_forward,
        grid=(blocks, 3),
        out_shape=(
            shaped((tokens, width), low),
            shaped((tokens, width), low),
            shaped((tokens, width), low),
            shaped((blocks, HEADS, ROWS, ROWS), low),
            shaped((tokens, width), low),
            shaped((tokens, width), jnp.float32),
            shaped((tokens, 1), jnp.float32),
        ),
        in_specs=[
            smem,
            smem,
            rows,
            pl.BlockSpec(memory_space=pl.ANY),
            pl.BlockSpec((VROWS, width), lambda b, h: (0, 0)),
        ],
        out_specs=(
            quad,
            quad,
            quad,
            pl.BlockSpec((1, 4, ROWS, ROWS), lambda b, h: (b, h, 0, 0)),
            rows,
            rows,
            pl.BlockSpec((ROWS, 1), lambda b, h: (b, 0)),
        ),
        scratch_shapes=[
            pltpu.VMEM((4, width, width), low),
            pltpu.VMEM((ROWS, ROWS), jnp.float32),
            pltpu.SemaphoreType.DMA((4,)),
        ],
        compiler_params=pltpu.CompilerParams(vmem_limit_bytes=56 * 2**20),
        name="attend_forward",
    )(counts, lengths, x, weights, vectors)


def feed_forward_both(
    counts,
    lengths,
    hat_ref,
    inverse_ref,
    cot_ref,
    w_hbm,
    vec_ref,
    mixed_ref,
    first_ref,
    branch_ref,
    context_ref,
    up_grad_ref,
    down_grad_ref,
    sum_ref,
    w_buf,
    active_ref,
    up_ref,
    hidden_ref,
    down_ref,
    slope_ref,
    w_sem,
):
    step = pl.program_id(0)
    blocks = pl.num_programs(0) - 4
    loads = [
        pltpu.make_async_copy(w_hbm.at[3 + at], w_buf.at[at], w_sem.at[at]) for at in range(9)
    ]

    @pl.when(step == 0)
    def _():
        for load in loads[1:] + loads[:1]:
            load.start()
        sum_ref[...] = jnp.zeros_like(sum_ref)
        for load in loads[1:] + loads[:1]:
            load.wait()

    @pl.when(step < blocks)
    def _():
        here = pl.ds(pl.multiple_of(step * ROWS, ROWS), ROWS)
        at_row = lax.broadcasted_iota(jnp.int32, (ROWS, 1), 0) + step * ROWS
        live = passage_facts(counts, lengths, at_row)[0].astype(jnp.float32)
        hat = hat_ref[...]
        hidden = hat * vec_ref[10:11, :] + vec_ref[8:9, :]
        hidden_low = hidden.astype(jnp.bfloat16)
        hidden_ref[here, :] = hidden_low
        total = hidden + vec_ref[7:8, :]
        for tile in range(4):
            up = dot(hidden_low, w_buf[1 + tile]) + vec_ref[3 + tile : 4 + tile, :]
            active, slope_ref[tile] = gelu_parts(up)
            active_ref[tile, here, :] = active
            total = total + dot(active, w_buf[5 + tile])
        hat_two, inverse_two = normalize(total)
        mixed_ref[...] = ((hat_two * vec_ref[11:12, :] + vec_ref[9:10, :]) * live).astype(jnp.bfloat16)
        grad_out = cot_ref[...].astype(jnp.float32) * live
        sum_ref[11:12, :] += columns_total(grad_out * hat_two)
        sum_ref[9:10, :] += columns_total(grad_out)
        second = normalize_back(grad_out * vec_ref[11:12, :], hat_two, inverse_two)
        down_low = second.astype(jnp.bfloat16)
        down_ref[here, :] = down_low
        sum_ref[7:8, :] += columns_total(down_low.astype(jnp.float32))
        grad_hidden = second
        for tile in range(4):
            pulled = dot_back(down_low, w_buf[5 + tile])
            up_low = (pulled * slope_ref[tile]).astype(jnp.bfloat16)
            up_ref[tile, here, :] = up_low
            sum_ref[3 + tile : 4 + tile, :] += columns_total(up_low.astype(jnp.float32))
            grad_hidden = grad_hidden + dot_back(up_low, w_buf[1 + tile])
        sum_ref[10:11, :] += columns_total(grad_hidden * hat)
        sum_ref[8:9, :] += columns_total(grad_hidden)
        grad_first = normalize_back(grad_hidden * vec_ref[10:11, :], hat, inverse_ref[...])
        first_ref[...] = grad_first
        branch_low = grad_first.astype(jnp.bfloat16)
        branch_ref[...] = branch_low
        sum_ref[2:3, :] += columns_total(branch_low.astype(jnp.float32))
        context_ref[...] = dot_back(branch_low, w_buf[0]).astype(jnp.bfloat16)

    @pl.when(step >= blocks)
    def _():
        tile = step - blocks
        up_grad_ref[0] = outer(hidden_ref[...], up_ref[tile]).astype(jnp.bfloat16)
        down_grad_ref[0] = outer(active_ref[tile], down_ref[...]).astype(jnp.bfloat16)


def fed_forward_both(counts, lengths, hat, inverse, cotangent, weights, vectors):
    tokens, width = hat.shape
    blocks = tokens // ROWS
    low = jnp.bfloat16
    smem = pl.BlockSpec(memory_space=pltpu.SMEM)
    shaped = jax.ShapeDtypeStruct

    def block_of(step):
        return jnp.minimum(step, blocks - 1)

    def tile_of(step):
        return jnp.maximum(step - blocks, 0)

    rows = pl.BlockSpec((ROWS, width), lambda i: (block_of(i), 0))
    tile = pl.BlockSpec((1, width, width), lambda i: (tile_of(i), 0, 0))
    return pl.pallas_call(
        feed_forward_both,
        grid=(blocks + 4,),
        out_shape=(
            shaped((tokens, width), low),
            shaped((tokens, width), jnp.float32),
            shaped((tokens, width), low),
            shaped((tokens, width), low),
            shaped((4, width, width), low),
            shaped((4, width, width), low),
            shaped((16, width), jnp.float32),
        ),
        in_specs=[
            smem,
            smem,
            rows,
            pl.BlockSpec((ROWS, 1), lambda i: (block_of(i), 0)),
            rows,
            pl.BlockSpec(memory_space=pl.ANY),
            pl.BlockSpec((VROWS, width), lambda i: (0, 0)),
        ],
        out_specs=(
            rows,
            rows,
            rows,
            rows,
            tile,
            tile,
            pl.BlockSpec((16, width), lambda i: (0, 0)),
        ),
        scratch_shapes=[
            pltpu.VMEM((9, width, width), low),
            pltpu.VMEM((4, tokens, width), low),
            pltpu.VMEM((4, tokens, width), low),
            pltpu.VMEM((tokens, width), low),
            pltpu.VMEM((tokens, width), low),
            pltpu.VMEM((4, ROWS, width), jnp.float32),
            pltpu.SemaphoreType.DMA((9,)),
        ],
        compiler_params=pltpu.CompilerParams(vmem_limit_bytes=60 * 2**20),
        name="feed_forward_both",
    )(counts, lengths, hat, inverse, cotangent, weights, vectors)


def attend_backward(
    p_ref,
    q_ref,
    k_ref,
    v_ref,
    x_ref,
    ctx_ref,
    grad_ctx_ref,
    branch_ref,
    first_ref,
    w_ref,
    input_ref,
    grad_ref,
    sum_ref,
    pulled,
):
    step = pl.program_id(0)
    quad, block = step // 2, lax.rem(step, 2)
    here = pl.ds(pl.multiple_of(block * ROWS, ROWS), ROWS)
    cols = pl.ds(pl.multiple_of(quad * 256, 256), 256)

    @pl.when(step == 0)
    def _():
        sum_ref[...] = jnp.zeros_like(sum_ref)
        input_ref[...] = first_ref[...]

    def add_sums(at, by_query, by_value):
        sum_ref[0:1, at] += by_query
        sum_ref[1:2, at] += by_value

    for pair in range(2):
        half = slice(128 * pair, 128 * pair + 128)
        qkv = q_ref[:, half], k_ref[:, half], v_ref[:, half]
        heads = p_ref.at[0, pl.ds(2 * pair, 2)]
        attend_back_pair(2 * quad + pair, here, heads, qkv, ctx_ref, grad_ctx_ref, pulled, half, add_sums)
    more = input_ref[here, :]
    for at in range(3):
        more = more + dot_back(pulled[at, here, :], w_ref[at, :, cols])
    input_ref[here, :] = more

    @pl.when(block == 1)
    def _():
        for tile in range(3):
            grad_ref[tile, :, cols] = outer(x_ref[...], pulled[tile]).astype(jnp.bfloat16)
        grad_ref[3, :, cols] = outer(ctx_ref[...], branch_ref[:, cols]).astype(jnp.bfloat16)


def attended_back(probs, query, keyed, valued, x, context, grad_context, grad_branch, grad_first, weights):
    tokens, width = x.shape
    low = jnp.bfloat16
    shaped = jax.ShapeDtypeStruct
    once = pl.Buffered(1)
    quad = pl.BlockSpec((ROWS, 256), lambda i: (lax.rem(i, 2), i // 2))
    whole = pl.BlockSpec((tokens, width), lambda i: (0, 0), pipeline_mode=once)
    return pl.pallas_call(
        attend_backward,
        grid=(6,),
        out_shape=(
            shaped((tokens, width), jnp.float32),
            shaped((4, width, width), low),
            shaped((16, width), jnp.float32),
        ),
        in_specs=[
            pl.BlockSpec((1, 4, ROWS, ROWS), lambda i: (lax.rem(i, 2), i // 2, 0, 0)),
            quad,
            quad,
            quad,
            whole,
            whole,
            whole,
            whole,
            whole,
            pl.BlockSpec((3, width, width), lambda i: (0, 0, 0), pipeline_mode=once),
        ],
        out_specs=(
            whole,
            pl.BlockSpec((4, width, width), lambda i: (0, 0, 0), pipeline_mode=once),
            pl.BlockSpec((16, width), lambda i: (0, 0)),
        ),
        scratch_shapes=[pltpu.VMEM((3, tokens, 256), low)],
        compiler_params=pltpu.CompilerParams(vmem_limit_bytes=56 * 2**20),
        name="attend_backward",
    )(probs, query, keyed, valued, x, context, grad_context, grad_branch, grad_first, weights)


def moved(param, grad, first, second, average, rate):
    param_new, first_new, second_new = adam_update(param, grad, first, second, rate)
    return param_new, first_new, second_new, average_rate * average + (1.0 - average_rate) * param_new


def update_kernel(
    gain_scale,
    grad_ref,
    master_ref,
    first_ref,
    second_ref,
    ema_ref,
    vec_grad_ref,
    vec_ref,
    vec_first_ref,
    vec_second_ref,
    vec_ema_ref,
    master_out,
    first_out,
    second_out,
    ema_out,
    copy_out,
    vec_out,
    vec_first_out,
    vec_second_out,
    vec_ema_out,
):
    grad = grad_ref[...].astype(jnp.float32) * gain_scale
    result = moved(master_ref[0], grad, first_ref[0], second_ref[0], ema_ref[0], tile_rate)
    master_out[0], first_out[0], second_out[0], ema_out[0] = result
    copy_out[0] = result[0].astype(jnp.bfloat16)

    @pl.when((pl.program_id(0) == 0) & (pl.program_id(1) == 0))
    def _():
        vec_grad = vec_grad_ref[0:VROWS, :] * gain_scale
        vec_out[...], vec_first_out[...], vec_second_out[...], vec_ema_out[...] = moved(
            vec_ref[...], vec_grad, vec_first_ref[...], vec_second_ref[...], vec_ema_ref[...], vector_rate
        )


def updated(gain_scale, slot_grads, master, first, second, ema, vec_grad, vectors, vec_first, vec_second, vec_ema):
    width = master.shape[-1]
    chunk = 192
    tile = pl.BlockSpec((1, 1, chunk, width), lambda s, r: (0, s, r, 0))
    vec = pl.BlockSpec((VROWS, width), lambda s, r: (0, 0))
    shaped = jax.ShapeDtypeStruct
    tile_shape = shaped(master.shape, jnp.float32)
    vec_shape = shaped((VROWS, width), jnp.float32)
    return pl.pallas_call(
        functools.partial(update_kernel, gain_scale),
        grid=(SLOTS, width // chunk),
        out_shape=(tile_shape,) * 4 + (shaped(master.shape, jnp.bfloat16),) + (vec_shape,) * 4,
        in_specs=[pl.BlockSpec((1, chunk, width), lambda s, r: (s, r, 0))]
        + [tile] * 4
        + [pl.BlockSpec((16, width), lambda s, r: (0, 0))]
        + [vec] * 4,
        out_specs=(tile,) * 5 + (vec,) * 4,
        compiler_params=pltpu.CompilerParams(vmem_limit_bytes=40 * 2**20),
        name="update",
    )(slot_grads, master, first, second, ema, vec_grad, vectors, vec_first, vec_second, vec_ema)


MESH = pl.DeviceIdType.MESH
GROUP = 32
PAIRS = TILES // 2
PLANE = 8
PIECE = 96
PAIR_TILES = ((0, 1), (2, 3), (4, 8), (5, 9), (6, 10), (7, 11))
EARLY = 2
WHOLE = 3


def remote(src, dst, send, recv, device):
    return pltpu.make_async_remote_copy(
        src_ref=src, dst_ref=dst, send_sem=send, recv_sem=recv, device_id=(device,), device_id_type=MESH
    )


def place(device):
    core = lax.rem(device, 2)
    x = lax.rem(device // 2, 2)
    y = lax.rem(device // 4, 2)
    z = device // 8
    return z, y, x, core


def start(copies):
    for copy in copies:
        copy.start()


def arrive(copies):
    for copy in copies:
        copy.wait_recv()


def greet(z, in_plane):
    barrier = pltpu.get_barrier_semaphore()
    for hop in range(1, PLANE):
        other = z * PLANE + lax.rem(in_plane + hop, PLANE)
        pl.semaphore_signal(barrier, inc=1, device_id=(other,), device_id_type=MESH)
    for hop in range(1, 4):
        other = lax.rem(z + hop, 4) * PLANE + in_plane
        pl.semaphore_signal(barrier, inc=1, device_id=(other,), device_id_type=MESH)
    pl.semaphore_wait(barrier, PLANE + 2)


def along_z(z, in_plane):
    inner = (1 + z // 2) * PLANE + in_plane
    other_middle = (3 - z) * PLANE + in_plane
    outer_end = lax.rem(lax.rem(z + 3, 4) * 3, 4) * PLANE + in_plane
    return inner, other_middle, outer_end


def third(part):
    return slice(None) if part == WHOLE else pl.ds(256 * part, 256)


def unit(pair, part):
    return 3 * pair + part if pair < EARLY else 2 * EARLY + pair


UNITS = [(pair, part) for pair in range(EARLY) for part in range(3)]
UNITS += [(pair, WHOLE) for pair in range(EARLY, PAIRS)]


def forward_and_pull(
    counts,
    lengths,
    spots,
    planes,
    x_hbm,
    cot_hbm,
    master_hbm,
    vec_ref,
    q_ref,
    k_ref,
    v_ref,
    p_ref,
    ctx_hbm,
    hidden_hbm,
    active_hbm,
    up_hbm,
    down_hbm,
    mixed_hbm,
    first_hbm,
    branch_hbm,
    grad_ctx_hbm,
    w_out,
    sum_ref,
    cap_ref,
    wide,
    low,
    stage_a,
    stage_b,
    stage_c,
    chosen,
    from_end,
    from_middle,
    w_buf,
    x_then_hidden,
    ctx_then_grad,
    cot_then_down,
    mixed_then_branch,
    hat_ref,
    inverse_ref,
    slope_ref,
    tile_buf,
    load_sem,
    store_sem,
    tile_sem,
    out_sem,
    swap_send,
    swap_recv,
    z_send,
    z_recv,
    mid_send,
    mid_recv,
    far_send,
    far_recv,
    near_send,
    near_recv,
):
    step = pl.program_id(0)
    width = 8 * PIECE
    me = lax.axis_index("dp")
    z, y, x, core = place(me)
    in_plane = lax.rem(me, PLANE)
    sibling = me + 1 - 2 * core
    x_peer = me + 2 - 4 * x
    y_peer = me + 4 - 8 * y
    z_targets = along_z(z, in_plane)
    stages = (stage_a, stage_b, stage_c)
    is_end = (z == 0) | (z == 3)
    is_middle = (z == 1) | (z == 2)

    def piece_rows(cell_core, cell_x, cell_y):
        return pl.ds(pl.multiple_of(((cell_core * 2 + cell_x) * 2 + cell_y) * PIECE, 16), PIECE)

    def swap(part):
        def send(hop, carry):
            target = lax.rem(in_plane + hop, PLANE)
            _, ty, tx, tc = place(target)
            remote(
                low.at[:, piece_rows(tc, tx, ty), third(part)],
                stages[part].at[pl.ds(2 * in_plane, 2)],
                swap_send.at[part],
                swap_recv.at[part],
                z * PLANE + target,
            ).start()
            return carry

        lax.fori_loop(1, PLANE, send, 0)

    def swap_wait(part, sem):
        most = stages[part].at[pl.ds(0, 2 * PLANE - 2)]
        pltpu.make_async_copy(most, most, sem.at[part]).wait()

    def z_copy(pair, part, level):
        two = pl.ds(2 * pair, 2)
        cols = third(part)
        src = w_buf.at[two, core, x, y, :, cols] if level == 2 else chosen.at[two, :, cols]
        dst = (from_end.at[two, :, cols], from_middle.at[two, :, cols], src)[level]
        at = unit(pair, part)
        return remote(src, dst, z_send.at[level, at], z_recv.at[level, at], z_targets[level])

    def z_end(pair, part=WHOLE):
        @pl.when(is_end)
        def _():
            z_copy(pair, part, 0).start()

    def z_middle(pair, part=WHOLE):
        @pl.when(is_middle)
        def _():
            z_copy(pair, part, 0).wait_recv()
            two, cols = pl.ds(2 * pair, 2), third(part)
            chosen[two, :, cols] = chosen[two, :, cols] + from_end[two, :, cols]
            z_copy(pair, part, 1).start()

    def z_total(pair, part=WHOLE):
        @pl.when(is_middle)
        def _():
            z_copy(pair, part, 1).wait_recv()
            two, cols = pl.ds(2 * pair, 2), third(part)
            w_buf[two, core, x, y, :, cols] = chosen[two, :, cols] + from_middle[two, :, cols]
            z_copy(pair, part, 2).start()

    def mid_copies(pair, part):
        copies = []
        for n, peer in enumerate((y_peer, x_peer)):
            spot = w_buf.at[2 * pair + n, core, x, y, :, third(part)]
            at = unit(pair, part), n
            copies.append(remote(spot, spot, mid_send.at[at], mid_recv.at[at], peer))
        return copies

    def halves(pair, part, late):
        row = 1 - x if late else x
        column = 1 - y if late else y
        cols = third(part)
        return w_buf.at[2 * pair, core, row, :, :, cols], w_buf.at[2 * pair + 1, core, :, column, :, cols]

    def far_copies(pair, part):
        copies = []
        for n, peer in enumerate((x_peer, y_peer)):
            spot = halves(pair, part, False)[n]
            at = unit(pair, part), n
            copies.append(remote(spot, spot, far_send.at[at], far_recv.at[at], peer))
        return copies

    def near_copies(pair, part, late):
        copies = []
        for n in range(2):
            spot = halves(pair, part, late)[n]
            at = unit(pair, part), n, late
            copies.append(remote(spot, spot, near_send.at[at], near_recv.at[at], sibling))
        return copies

    def give_mid(pair, part=WHOLE):
        @pl.when(is_end)
        def _():
            z_copy(pair, part, 2).wait_recv()

        start(mid_copies(pair, part))

    def give_far(pair, part=WHOLE):
        arrive(mid_copies(pair, part))
        start(far_copies(pair, part) + near_copies(pair, part, 0))

    def give_near(pair, part=WHOLE):
        arrive(far_copies(pair, part))
        start(near_copies(pair, part, 1))

    def finish(pair, part=WHOLE):
        arrive(near_copies(pair, part, 0) + near_copies(pair, part, 1))

    def choose(part):
        swap_wait(part, swap_recv)
        for pair in range(PAIRS):
            for n, tile in enumerate(PAIR_TILES[pair]):
                value = stages[part][spots[tile]]
                chosen[2 * pair + n, :, third(part)] = jnp.where(
                    planes[tile] == z, value, jnp.zeros_like(value)
                )

    def load(at):
        src = (x_hbm, cot_hbm, master_hbm)[at]
        dst = (x_then_hidden, cot_then_down, wide)[at]
        return pltpu.make_async_copy(src, dst, load_sem.at[at])

    def store(at):
        src, dst = (
            (x_then_hidden, hidden_hbm),
            (ctx_then_grad, ctx_hbm),
            (cot_then_down, down_hbm),
            (mixed_then_branch, mixed_hbm),
            (ctx_then_grad, grad_ctx_hbm),
            (mixed_then_branch, branch_hbm),
            (wide, first_hbm),
        )[at]
        src = src.at[pl.ds(0, 2 * ROWS)] if src is wide else src
        return pltpu.make_async_copy(src, dst, store_sem.at[at])

    def w_stores():
        return [
            pltpu.make_async_copy(w_buf.at[tile], w_out.at[tile], out_sem.at[tile]) for tile in range(3)
        ]

    def weight(at, cols=slice(None)):
        value = w_buf[at, :, :, :, :, cols]
        return value.reshape(width, value.shape[-1])

    @pl.when(step == 0)
    def _():
        for at in range(3):
            load(at).start()
        sum_ref[...] = jnp.zeros_like(sum_ref)
        greet(z, in_plane)
        load(2).wait()
        for slot in range(SLOTS):
            low[slot] = wide[width * slot : width * (slot + 1), :].astype(jnp.bfloat16)
        swap(0)
        for part in range(3):
            stages[part][pl.ds(2 * in_plane, 2)] = low[:, piece_rows(core, x, y), third(part)]
        swap_wait(0, swap_send)
        swap(1)
        for block in range(2):
            cap_ref[block] = attention_caps(counts, lengths, block)
        choose(0)
        z_end(0, 0)
        z_end(1, 0)
        z_middle(0, 0)
        z_middle(1, 0)
        swap_wait(1, swap_send)
        swap(2)
        choose(1)
        z_end(0, 1)
        z_end(1, 1)
        z_total(0, 0)
        z_total(1, 0)
        z_middle(0, 1)
        z_middle(1, 1)
        give_mid(0, 0)
        give_mid(1, 0)
        choose(2)
        z_end(0, 2)
        z_end(1, 2)
        z_total(0, 1)
        z_total(1, 1)
        give_far(0, 0)
        give_far(1, 0)
        z_middle(0, 2)
        z_middle(1, 2)
        give_mid(0, 1)
        give_mid(1, 1)
        z_total(0, 2)
        z_total(1, 2)
        z_end(2)
        give_near(0, 0)
        give_near(1, 0)
        give_far(0, 1)
        give_far(1, 1)
        load(0).wait()
        load(1).wait()
        finish(0, 0)
        finish(1, 0)

    @pl.when(step == 1)
    def _():
        z_middle(2)
        give_mid(0, 2)
        give_mid(1, 2)
        give_near(0, 1)
        give_near(1, 1)

    @pl.when(step == 2)
    def _():
        z_total(2)
        z_end(3)
        give_far(0, 2)
        give_far(1, 2)
        finish(0, 1)
        finish(1, 1)
        z_middle(3)

    @pl.when(step == 3)
    def _():
        give_mid(2)
        z_total(3)
        z_end(4)
        give_near(0, 2)
        give_near(1, 2)

    @pl.when(step == 4)
    def _():
        give_far(2)
        give_mid(3)
        z_middle(4)
        z_end(5)
        finish(0, 2)
        finish(1, 2)
        start(w_stores())

    @pl.when(step == 5)
    def _():
        give_far(3)
        z_total(4)
        z_middle(5)
        give_mid(4)
        give_near(2)

    @pl.when(step == 6)
    def _():
        give_far(4)
        z_total(5)
        give_mid(5)
        give_near(3)
        finish(2)

    @pl.when(step == 7)
    def _():
        give_far(5)
        give_near(4)
        finish(3)

    @pl.when(step == 8)
    def _():
        give_near(5)
        finish(4)

    @pl.when(step == 9)
    def _():
        finish(5)

    quad, block = step // 2, lax.rem(step, 2)
    here = pl.ds(pl.multiple_of(block * ROWS, ROWS), ROWS)

    @pl.when(step < 6)
    def _():
        attend_quad(
            quad,
            weight,
            x_then_hidden.at[here],
            vec_ref,
            cap_ref.at[block],
            q_ref,
            k_ref,
            v_ref,
            p_ref,
            ctx_then_grad.at[here],
        )

    @pl.when((step >= 4) & (step < 6))
    def _():
        branch = dot(ctx_then_grad[here, :], weight(3)) + vec_ref[2:3, :]
        hat, inverse = normalize(x_then_hidden[here, :].astype(jnp.float32) + branch)
        hat_ref[here, :] = hat
        inverse_ref[here, :] = inverse
        hidden = hat * vec_ref[10:11, :] + vec_ref[8:9, :]
        x_then_hidden[here, :] = hidden.astype(jnp.bfloat16)
        wide[here, :] = hidden + vec_ref[7:8, :]

    @pl.when(step == 5)
    def _():
        start([store(0), store(1)])

    turn = step - 6
    slot = lax.rem(turn, 2)

    def tile_store(source_slot, target):
        return pltpu.make_async_copy(tile_buf.at[source_slot], target, tile_sem.at[source_slot])

    @pl.when(turn >= 2)
    def _():
        tile_store(slot, active_hbm.at[0]).wait()

    @pl.when((step >= 6) & (step < 10))
    def _():
        for half in range(2):
            rows = slice(ROWS * half, ROWS * half + ROWS)
            up = dot(x_then_hidden[rows, :], weight(4 + 2 * turn)) + vec_ref[pl.ds(3 + turn, 1), :]
            active, slope = gelu_parts(up)
            slope_ref[turn, rows, :] = slope.astype(jnp.bfloat16)
            tile_buf[slot, rows, :] = active
            wide[rows, :] = wide[rows, :] + dot(active, weight(5 + 2 * turn))
        tile_store(slot, active_hbm.at[turn]).start()

    @pl.when(step == 10)
    def _():
        for half in range(2):
            rows = slice(ROWS * half, ROWS * half + ROWS)
            at_row = lax.broadcasted_iota(jnp.int32, (ROWS, 1), 0) + half * ROWS
            live = passage_facts(counts, lengths, at_row)[0].astype(jnp.float32)
            hat, inverse = normalize(wide[rows, :])
            mixed = (hat * vec_ref[11:12, :] + vec_ref[9:10, :]) * live
            mixed_then_branch[rows, :] = mixed.astype(jnp.bfloat16)
            grad_out = cot_then_down[rows, :].astype(jnp.float32) * live
            sum_ref[11:12, :] += columns_total(grad_out * hat)
            sum_ref[9:10, :] += columns_total(grad_out)
            second = normalize_back(grad_out * vec_ref[11:12, :], hat, inverse)
            wide[rows, :] = second
            down_low = second.astype(jnp.bfloat16)
            cot_then_down[rows, :] = down_low
            sum_ref[7:8, :] += columns_total(down_low.astype(jnp.float32))
        start([store(2), store(3)])

    @pl.when(step >= 10)
    def _():
        tile = step - 10
        for half in range(2):
            rows = slice(ROWS * half, ROWS * half + ROWS)
            pulled = dot_back(cot_then_down[rows, :], weight(5 + 2 * tile))
            up_low = (pulled * slope_ref[tile, rows, :].astype(jnp.float32)).astype(jnp.bfloat16)
            tile_buf[slot, rows, :] = up_low
            sum_ref[pl.ds(3 + tile, 1), :] += columns_total(up_low.astype(jnp.float32))
            wide[rows, :] = wide[rows, :] + dot_back(up_low, weight(4 + 2 * tile))
        tile_store(slot, up_hbm.at[tile]).start()

    @pl.when(step == 13)
    def _():
        store(1).wait()
        store(3).wait()
        for half in range(2):
            rows = slice(ROWS * half, ROWS * half + ROWS)
            grad_hidden, hat = wide[rows, :], hat_ref[rows, :]
            sum_ref[10:11, :] += columns_total(grad_hidden * hat)
            sum_ref[8:9, :] += columns_total(grad_hidden)
            first = normalize_back(grad_hidden * vec_ref[10:11, :], hat, inverse_ref[rows, :])
            wide[rows, :] = first
            branch_low = first.astype(jnp.bfloat16)
            mixed_then_branch[rows, :] = branch_low
            sum_ref[2:3, :] += columns_total(branch_low.astype(jnp.float32))
            ctx_then_grad[rows, :] = dot_back(branch_low, weight(3)).astype(jnp.bfloat16)
        start([store(4), store(5), store(6)])
        store(0).wait()
        store(2).wait()
        for at in range(2):
            tile_store(at, up_hbm.at[0]).wait()
        for copy in w_stores():
            copy.wait()
        swap_wait(2, swap_send)
        for pair, part in UNITS:
            for copy in mid_copies(pair, part) + far_copies(pair, part):
                copy.wait_send()
            for copy in near_copies(pair, part, 0) + near_copies(pair, part, 1):
                copy.wait_send()

            @pl.when(is_end)
            def _():
                z_copy(pair, part, 0).wait_send()

            @pl.when(is_middle)
            def _():
                z_copy(pair, part, 1).wait_send()
                z_copy(pair, part, 2).wait_send()

        for at in range(4, 7):
            store(at).wait()


def forwarded_and_pulled(counts, lengths, spots, planes, x, cotangent, master, vectors):
    tokens, width = x.shape
    blocks = tokens // ROWS
    low, high = jnp.bfloat16, jnp.float32
    smem = pl.BlockSpec(memory_space=pltpu.SMEM)
    any_space = pl.BlockSpec(memory_space=pl.ANY)
    dma = pltpu.SemaphoreType.DMA
    shaped = jax.ShapeDtypeStruct

    def at(step):
        step = jnp.minimum(step, 5)
        return lax.rem(step, 2), step // 2

    quad = pl.BlockSpec((ROWS, 256), at)
    rows = shaped((tokens, width), low)
    cut = (2, 2, 2, PIECE, width)
    units = len(UNITS)
    results = pl.pallas_call(
        forward_and_pull,
        grid=(14,),
        out_shape=(
            rows,
            rows,
            rows,
            shaped((blocks, HEADS, ROWS, ROWS), low),
            rows,
            rows,
            shaped((4, tokens, width), low),
            shaped((4, tokens, width), low),
            rows,
            rows,
            shaped((tokens, width), high),
            rows,
            rows,
            shaped((3,) + cut, low),
            shaped((16, width), high),
        ),
        in_specs=[smem] * 4 + [any_space] * 3 + [pl.BlockSpec((VROWS, width), lambda i: (0, 0))],
        out_specs=(quad, quad, quad, pl.BlockSpec((1, 4, ROWS, ROWS), lambda i: (*at(i), 0, 0)))
        + (any_space,) * 10
        + (pl.BlockSpec((16, width), lambda i: (0, 0)),),
        scratch_shapes=[
            pltpu.VMEM((2, ROWS, ROWS), high),
            pltpu.VMEM((SLOTS * width, width), high),
            pltpu.VMEM((SLOTS, width, width), low),
            pltpu.VMEM((2 * PLANE, PIECE, 256), low),
            pltpu.VMEM((2 * PLANE, PIECE, 256), low),
            pltpu.VMEM((2 * PLANE, PIECE, 256), low),
            pltpu.VMEM((TILES, PIECE, width), low),
            pltpu.VMEM((TILES, PIECE, width), low),
            pltpu.VMEM((TILES, PIECE, width), low),
            pltpu.VMEM((TILES,) + cut, low),
            pltpu.VMEM((tokens, width), low),
            pltpu.VMEM((tokens, width), low),
            pltpu.VMEM((tokens, width), low),
            pltpu.VMEM((tokens, width), low),
            pltpu.VMEM((tokens, width), high),
            pltpu.VMEM((tokens, 1), high),
            pltpu.VMEM((4, tokens, width), low),
            pltpu.VMEM((2, tokens, width), low),
            dma((3,)),
            dma((7,)),
            dma((2,)),
            dma((3,)),
            dma((3,)),
            dma((3,)),
            dma((3, units)),
            dma((3, units)),
            dma((units, 2)),
            dma((units, 2)),
            dma((units, 2)),
            dma((units, 2)),
            dma((units, 2, 2)),
            dma((units, 2, 2)),
        ],
        compiler_params=pltpu.CompilerParams(
            collective_id=0, has_side_effects=True, vmem_limit_bytes=63 * 2**20
        ),
        name="forward_and_pull",
    )(counts, lengths, spots, planes, x, cotangent, master.reshape(SLOTS * width, width), vectors)
    w_early = results[13].reshape(3, width, width)
    return results[:13] + (w_early,) + results[14:]


def pull_and_reduce(
    holds,
    keep_slot,
    p_ref,
    q_ref,
    k_ref,
    v_ref,
    ctx_ref,
    grad_ctx_ref,
    active_ref,
    up_ref,
    x_hbm,
    hidden_hbm,
    branch_hbm,
    down_hbm,
    first_hbm,
    w_hbm,
    late_ref,
    input_hbm,
    slot_grad,
    vec_out,
    w_buf,
    acc,
    pulled,
    hidden_then_x,
    down_then_branch,
    part,
    from_core,
    from_far,
    from_mid,
    from_end,
    from_middle,
    total,
    snap,
    outbox,
    vec_now,
    vec_in,
    load_sem,
    core_send,
    core_recv,
    far_send,
    far_recv,
    mid_send,
    mid_recv,
    z_send,
    z_recv,
    vec_send,
    vec_recv,
    out_send,
    out_recv,
):
    step = pl.program_id(0)
    inner = jnp.maximum(step - 4, 0)
    quad, block, pair = inner // 4, lax.rem(inner, 4) // 2, lax.rem(inner, 2)
    me = lax.axis_index("dp")
    z, y, x, core = place(me)
    in_plane = lax.rem(me, PLANE)
    sibling = me + 1 - 2 * core
    x_peer = me + 2 - 4 * x
    y_peer = me + 4 - 8 * y
    z_targets = along_z(z, in_plane)
    is_end = (z == 0) | (z == 3)
    is_middle = (z == 1) | (z == 2)

    def items(batch):
        if batch < 4:
            return [(0, 4 + batch, slice(None)), (1, 8 + batch, slice(None))]
        cols = pl.ds(256 * (batch - 4), 256)
        return [(0, 0, cols), (1, 1, cols), (0, 2, cols), (1, 3, cols)]

    def held(tile):
        return part.at[tile, core]

    def core_copies(batch):
        return [
            remote(
                part.at[tile, 1 - core, :, :, :, cols],
                from_core.at[tile, :, :, :, cols],
                core_send.at[batch, n],
                core_recv.at[batch, n],
                sibling,
            )
            for n, (_, tile, cols) in enumerate(items(batch))
        ]

    def far_copies(batch):
        copies = []
        for n, (kind, tile, cols) in enumerate(items(batch)):
            mine = held(tile)
            copies.append(
                remote(
                    mine.at[:, 1 - y, :, cols] if kind else mine.at[1 - x, :, :, cols],
                    from_far.at[tile, :, :, cols],
                    far_send.at[batch, n],
                    far_recv.at[batch, n],
                    y_peer if kind else x_peer,
                )
            )
        return copies

    def mid_copies(batch):
        copies = []
        for n, (kind, tile, cols) in enumerate(items(batch)):
            mine = held(tile)
            copies.append(
                remote(
                    mine.at[1 - x, y, :, cols] if kind else mine.at[x, 1 - y, :, cols],
                    from_mid.at[tile, :, cols],
                    mid_send.at[batch, n],
                    mid_recv.at[batch, n],
                    x_peer if kind else y_peer,
                )
            )
        return copies

    def z_copies(batch, stage):
        copies = []
        for n, (_, tile, cols) in enumerate(items(batch)):
            if stage == 2:
                src, dst = total.at[tile, :, cols], total.at[tile, :, cols]
            else:
                src = held(tile).at[x, y, :, cols]
                dst = (from_middle if stage else from_end).at[tile, :, cols]
            copies.append(
                remote(
                    src,
                    dst,
                    z_send.at[stage, batch, n],
                    z_recv.at[stage, batch, n],
                    z_targets[stage],
                )
            )
        return copies

    def give_core(batch):
        start(core_copies(batch))

    def give_far(batch):
        arrive(core_copies(batch))
        for _, tile, cols in items(batch):
            mine = held(tile)
            mine[:, :, :, cols] = mine[:, :, :, cols] + from_core[tile, :, :, :, cols]
        start(far_copies(batch))

    def give_mid(batch):
        arrive(far_copies(batch))
        for kind, tile, cols in items(batch):
            mine = held(tile)
            if kind:
                mine[:, y, :, cols] = mine[:, y, :, cols] + from_far[tile, :, :, cols]
            else:
                mine[x, :, :, cols] = mine[x, :, :, cols] + from_far[tile, :, :, cols]
        start(mid_copies(batch))

    def give_end(batch):
        arrive(mid_copies(batch))
        for _, tile, cols in items(batch):
            mine = held(tile)
            mine[x, y, :, cols] = mine[x, y, :, cols] + from_mid[tile, :, cols]

        @pl.when(is_end)
        def _():
            start(z_copies(batch, 0))

    def give_middle(batch):
        @pl.when(is_middle)
        def _():
            arrive(z_copies(batch, 0))
            for _, tile, cols in items(batch):
                mine = held(tile)
                mine[x, y, :, cols] = mine[x, y, :, cols] + from_end[tile, :, cols]
            start(z_copies(batch, 1))

    def give_total(batch):
        @pl.when(is_middle)
        def _():
            arrive(z_copies(batch, 1))
            for _, tile, cols in items(batch):
                mine = held(tile)
                total[tile, :, cols] = mine[x, y, :, cols] + from_middle[tile, :, cols]
            start(z_copies(batch, 2))

    def take_total(batch):
        @pl.when(is_end)
        def _():
            arrive(z_copies(batch, 2))

    def deliver(third):
        cols = pl.ds(256 * third, 256)
        snap[...] = total[:, :, cols]

        def fill(at, carry):
            value = snap[holds[z * 2 * PLANE + at]]
            wanted = keep_slot[z * 2 * PLANE + at] > 0
            outbox[third, at] = jnp.where(wanted, value, jnp.zeros_like(value))
            return carry

        lax.fori_loop(0, 2 * PLANE, fill, 0)

        def send(hop, carry):
            target = lax.rem(in_plane + hop, PLANE)
            remote(
                outbox.at[third, pl.ds(2 * target, 2)],
                slot_grad.at[:, core, x, y, :, cols],
                out_send.at[third],
                out_recv.at[third],
                z * PLANE + target,
            ).start()
            return carry

        lax.fori_loop(1, PLANE, send, 0)
        keep_copy(third).start()

    def keep_copy(third):
        return pltpu.make_async_copy(
            outbox.at[third, pl.ds(2 * in_plane, 2)],
            slot_grad.at[:, core, x, y, :, pl.ds(256 * third, 256)],
            load_sem.at[5 + third],
        )

    def vec_copies(stage):
        if stage < 3:
            hops = [(stage, (sibling, x_peer, y_peer)[stage])]
        else:
            hops = [
                (2 + hop, lax.rem(z + hop, 4) * PLANE + in_plane) for hop in range(1, 4)
            ]
        return [
            remote(vec_now.at[stage], vec_in.at[at], vec_send.at[at], vec_recv.at[at], device)
            for at, device in hops
        ]

    def vec_next(stage):
        arrive(vec_copies(stage))
        vec_now[stage + 1] = vec_now[stage] + vec_in[stage]
        start(vec_copies(stage + 1))

    def first_load():
        return pltpu.make_async_copy(first_hbm, acc, load_sem.at[3])

    def input_store():
        return pltpu.make_async_copy(acc, input_hbm, load_sem.at[4])

    def w_loads():
        return [pltpu.make_async_copy(w_hbm.at[at], w_buf.at[at], load_sem.at[at]) for at in range(3)]

    def early_loads():
        return [
            pltpu.make_async_copy(hidden_hbm, hidden_then_x, load_sem.at[8]),
            pltpu.make_async_copy(down_hbm, down_then_branch, load_sem.at[9]),
        ]

    def late_loads():
        return [
            pltpu.make_async_copy(x_hbm, hidden_then_x, load_sem.at[8]),
            pltpu.make_async_copy(branch_hbm, down_then_branch, load_sem.at[9]),
        ]

    def at_point(at, *work):
        @pl.when(step == at)
        def _():
            for action, batch in work:
                action(batch)

    @pl.when(step == 0)
    def _():
        start(early_loads() + w_loads() + [first_load()])
        greet(z, in_plane)
        vec_now[0] = late_ref[...]
        for load in early_loads():
            load.wait()

    at_point(5, (give_mid, 0))
    at_point(6, (give_far, 2))
    at_point(7, (give_mid, 1), (give_end, 0))
    at_point(8, (give_far, 3))
    at_point(9, (give_mid, 2), (give_middle, 0))
    at_point(10, (give_far, 4), (give_end, 1))
    at_point(11, (give_mid, 3), (give_total, 0), (give_middle, 1))
    at_point(12, (give_end, 2), (give_mid, 4))
    at_point(13, (give_far, 5), (take_total, 0), (give_total, 1), (give_middle, 2))
    at_point(14, (give_end, 3), (give_end, 4))
    at_point(
        15, (give_mid, 5), (take_total, 1), (give_total, 2), (give_middle, 3), (give_middle, 4)
    )

    @pl.when(step < 4)
    def _():
        by_up = outer(hidden_then_x[...], up_ref[0]).astype(jnp.bfloat16)
        part[4 + step] = by_up.reshape(2, 2, 2, PIECE, 8 * PIECE)
        by_down = outer(active_ref[0], down_then_branch[...]).astype(jnp.bfloat16)
        part[8 + step] = by_down.reshape(2, 2, 2, PIECE, 8 * PIECE)

    at_point(0, (give_core, 0))
    at_point(1, (give_core, 1), (give_far, 0))
    at_point(2, (give_core, 2), (give_far, 1))
    at_point(3, (give_core, 3))

    @pl.when(step == 3)
    def _():
        start(late_loads())

    here = pl.ds(pl.multiple_of(block * ROWS, ROWS), ROWS)
    quad_cols = pl.ds(pl.multiple_of(quad * 256, 256), 256)

    def add_sums(at, by_query, by_value):
        vec_now[0, 0:1, at] += by_query
        vec_now[0, 1:2, at] += by_value

    @pl.when(step >= 4)
    def _():
        attend_back_pair(
            2 * quad + pair,
            here,
            p_ref.at[0],
            (q_ref[...], k_ref[...], v_ref[...]),
            ctx_ref,
            grad_ctx_ref,
            pulled,
            pl.ds(pl.multiple_of(pair * 128, 128), 128),
            add_sums,
        )

    @pl.when(step == 4)
    def _():
        for load in w_loads() + [first_load()]:
            load.wait()

    @pl.when((step >= 4) & (pair == 1))
    def _():
        more = acc[here, :]
        for at in range(3):
            more = more + dot_back(pulled[at, here, :], w_buf[at, :, quad_cols])
        acc[here, :] = more

    @pl.when(step == 7)
    def _():
        for load in late_loads():
            load.wait()

    @pl.when((step >= 4) & (block == 1) & (pair == 1))
    def _():
        for tile in range(4):
            if tile < 3:
                value = outer(hidden_then_x[...], pulled[tile])
            else:
                value = outer(ctx_ref[...], down_then_branch[:, quad_cols])
            value = value.astype(jnp.bfloat16).reshape(2, 2, 2, PIECE, 256)
            part[tile, :, :, :, :, quad_cols] = value

    at_point(7, (give_core, 4))
    at_point(11, (give_core, 5))

    @pl.when(step == 15)
    def _():
        input_store().start()
        give_core(6)
        start(vec_copies(0))
        give_end(5)
        take_total(2)
        give_total(3)
        give_far(6)
        give_total(4)
        give_middle(5)
        vec_next(0)
        take_total(3)
        take_total(4)
        deliver(0)
        give_mid(6)
        give_total(5)
        vec_next(1)
        take_total(5)
        deliver(1)
        give_end(6)
        vec_next(2)
        give_middle(6)
        give_total(6)
        take_total(6)
        deliver(2)
        arrive(vec_copies(3))
        summed = jnp.zeros(vec_out.shape, jnp.float32)
        for origin in range(4):
            hop = lax.rem(z - origin + 4, 4)
            summed = summed + jnp.where(hop == 0, vec_now[3], vec_in[2 + jnp.maximum(hop, 1)])
        vec_out[...] = summed
        for batch in range(7):
            for copy in core_copies(batch) + far_copies(batch) + mid_copies(batch):
                copy.wait_send()

            @pl.when(is_end)
            def _():
                for copy in z_copies(batch, 0):
                    copy.wait_send()

            @pl.when(is_middle)
            def _():
                for copy in z_copies(batch, 1) + z_copies(batch, 2):
                    copy.wait_send()

        for stage in range(4):
            for copy in vec_copies(stage):
                copy.wait_send()
        input_store().wait()
        for third in range(3):
            keep_copy(third).wait()
            most = outbox.at[third, pl.ds(0, 2 * PLANE - 2)]
            pltpu.make_async_copy(most, most, out_recv.at[third]).wait()
            pltpu.make_async_copy(most, most, out_send.at[third]).wait()


def pulled_and_reduced(
    holds,
    keep_slot,
    probs,
    query,
    keyed,
    valued,
    context,
    grad_context,
    active,
    grad_up,
    x,
    hidden,
    grad_branch,
    grad_down,
    grad_first,
    weights,
    late_sums,
):
    tokens, width = x.shape
    low, high = jnp.bfloat16, jnp.float32
    shaped = jax.ShapeDtypeStruct
    smem = pl.BlockSpec(memory_space=pltpu.SMEM)
    any_space = pl.BlockSpec(memory_space=pl.ANY)
    dma = pltpu.SemaphoreType.DMA

    def at(step):
        inner = jnp.maximum(step - 4, 0)
        return lax.rem(inner, 4) // 2, inner // 4 * 2 + lax.rem(inner, 2)

    pair = pl.BlockSpec((ROWS, 128), at)
    whole = pl.BlockSpec((tokens, width), lambda i: (0, 0), pipeline_mode=pl.Buffered(1))
    tile = pl.BlockSpec((1, tokens, width), lambda i: (jnp.minimum(i, 3), 0, 0))
    sums = pl.BlockSpec((16, width), lambda i: (0, 0))
    cut = (2, 2, 2, PIECE, width)
    input_grad, slot_grads, vector_sums = pl.pallas_call(
        pull_and_reduce,
        grid=(16,),
        out_shape=(
            shaped((tokens, width), high),
            shaped((SLOTS,) + cut, low),
            shaped((16, width), high),
        ),
        in_specs=[smem, smem, pl.BlockSpec((1, 2, ROWS, ROWS), lambda i: (*at(i), 0, 0))]
        + [pair] * 3
        + [whole] * 2
        + [tile] * 2
        + [any_space] * 6
        + [sums],
        out_specs=(any_space, any_space, sums),
        scratch_shapes=[
            pltpu.VMEM((3, width, width), low),
            pltpu.VMEM((tokens, width), high),
            pltpu.VMEM((3, tokens, 256), low),
            pltpu.VMEM((tokens, width), low),
            pltpu.VMEM((tokens, width), low),
            pltpu.VMEM((TILES,) + cut, low),
            pltpu.VMEM((TILES,) + cut[1:], low),
            pltpu.VMEM((TILES,) + cut[2:], low),
            pltpu.VMEM((TILES,) + cut[3:], low),
            pltpu.VMEM((TILES,) + cut[3:], low),
            pltpu.VMEM((TILES,) + cut[3:], low),
            pltpu.VMEM((TILES,) + cut[3:], low),
            pltpu.VMEM((TILES, PIECE, 256), low),
            pltpu.VMEM((3, 2 * PLANE, PIECE, 256), low),
            pltpu.VMEM((4, 16, width), high),
            pltpu.VMEM((6, 16, width), high),
            dma((10,)),
            dma((7, 4)),
            dma((7, 4)),
            dma((7, 4)),
            dma((7, 4)),
            dma((7, 4)),
            dma((7, 4)),
            dma((3, 7, 4)),
            dma((3, 7, 4)),
            dma((6,)),
            dma((6,)),
            dma((3,)),
            dma((3,)),
        ],
        compiler_params=pltpu.CompilerParams(
            collective_id=1, has_side_effects=True, vmem_limit_bytes=63 * 2**20
        ),
        name="pull_and_reduce",
    )(
        holds,
        keep_slot,
        probs,
        query,
        keyed,
        valued,
        context,
        grad_context,
        active,
        grad_up,
        x,
        hidden,
        grad_branch,
        grad_down,
        grad_first,
        weights,
        late_sums,
    )
    return input_grad, slot_grads.reshape(SLOTS, width, width), vector_sums


def collected_tiles(tile_low, owners, slots):
    mine = owners == lax.axis_index("dp")
    local = jnp.where(mine[:, None, None], tile_low[slots], jnp.zeros((), tile_low.dtype))
    return lax.psum(local, "dp")


def summed_over_slice(parts, vector_terms, owners, slots):
    model_width = parts.shape[2]
    rows = parts.reshape(-1, model_width).astype(jnp.float32)
    summed_rows = lax.psum_scatter(rows, "dp", scatter_dimension=0, tiled=True)
    full_rows = lax.all_gather(summed_rows, "dp", axis=0, tiled=True)
    tile_grads = full_rows.reshape(parts.shape)
    myself = lax.axis_index("dp")
    slot_list = []
    for slot_number in range(SLOTS):
        select = (owners == myself) & (slots == slot_number)
        slot_list.append(jnp.sum(jnp.where(select[:, None, None], tile_grads, 0.0), 0))
    return jnp.stack(slot_list, 0), lax.psum(vector_terms, "dp")


def body(
    inputs,
    cotangent,
    counts,
    lengths,
    owners,
    tile_master,
    tile_first,
    tile_second,
    tile_ema,
    bias_vals,
    gain_vals,
    vector_first,
    vector_second,
    vector_ema,
):
    tokens = inputs.shape[0]
    small = lax.axis_size("dp") == GROUP
    slots = tile_slots(owners)
    vectors = jnp.concatenate([bias_vals, gain_vals], 0)
    gain_scale = float(tokens * lax.axis_size("dp")) ** (-0.5)
    if small:
        picks = owners * SLOTS + slots
        per_plane = SLOTS * PLANE
        (
            query,
            keyed,
            valued,
            probs,
            context,
            hidden,
            active,
            grad_up,
            grad_down,
            mixed,
            grad_first,
            grad_branch,
            grad_context,
            weights,
            late_sums,
        ) = forwarded_and_pulled(
            counts,
            lengths,
            picks % per_plane,
            picks // per_plane,
            inputs,
            cotangent,
            tile_master,
            vectors,
        )
        places = jnp.arange(SLOTS * GROUP, dtype=jnp.int32)
        match = picks[None, :] == places[:, None]
        holds = jnp.sum(jnp.where(match, jnp.arange(TILES, dtype=jnp.int32)[None, :], 0), 1)
        keep_slot = jnp.sum(match.astype(jnp.int32), 1)
        input_grad, slot_grads, full_sums = pulled_and_reduced(
            holds,
            keep_slot,
            probs,
            query,
            keyed,
            valued,
            context,
            grad_context,
            active,
            grad_up,
            inputs,
            hidden,
            grad_branch,
            grad_down,
            grad_first,
            weights,
            late_sums,
        )
    else:
        weights = collected_tiles(tile_master[0].astype(jnp.bfloat16), owners, slots)
        query, keyed, valued, probs, context, hat, inverse = attended(
            counts, lengths, inputs, weights, vectors
        )
        mixed, grad_first, grad_branch, grad_context, up_grads, down_grads, late_sums = fed_forward_both(
            counts, lengths, hat, inverse, cotangent, weights, vectors
        )
        input_grad, early_grads, early_sums = attended_back(
            probs, query, keyed, valued, inputs, context, grad_context, grad_branch, grad_first, weights
        )
        parts = jnp.concatenate([early_grads, up_grads, down_grads], 0)
        slot_grads, full_sums = summed_over_slice(parts, late_sums + early_sums, owners, slots)
    return (mixed, input_grad) + tuple(
        updated(
            gain_scale,
            slot_grads,
            tile_master,
            tile_first,
            tile_second,
            tile_ema,
            full_sums,
            vectors,
            vector_first,
            vector_second,
            vector_ema,
        )
    )


def solution(mesh):
    placed = (
        P("dp", None),
        P("dp", None),
        P("dp", None),
        P("dp", None),
        P(),
        P("dp", None, None, None),
        P("dp", None, None, None),
        P("dp", None, None, None),
        P("dp", None, None, None),
        P(),
        P(),
        P(),
        P(),
        P(),
    )
    return jax.shard_map(
        body,
        mesh=mesh,
        in_specs=placed,
        out_specs=(
            P("dp", None),
            P("dp", None),
            P("dp", None, None, None),
            P("dp", None, None, None),
            P("dp", None, None, None),
            P("dp", None, None, None),
            P("dp", None, None, None),
            P(),
            P(),
            P(),
            P(),
        ),
        check_vma=False,
    )
```

```python
import functools

import jax
import jax.numpy as jnp
from jax import lax
from jax.experimental import pallas as pl
from jax.experimental.pallas import tpu as pltpu
from jax.sharding import PartitionSpec as P

HEADS = 12
BUCKET = 128
SLOTS = 2
TILES = 12
VROWS = 12
STEP = 5

norm_epsilon = 1e-12
tile_rate = 0.03
vector_rate = 0.2
first_decay = 0.5
second_decay = 0.5
adam_epsilon = 1e-08
weight_decay = 0.01
average_rate = 0.9


def tile_slots(owners):
    order = jnp.arange(owners.shape[0], dtype=jnp.int32)
    same = owners[:, None] == owners[None, :]
    earlier = order[None, :] < order[:, None]
    return jnp.sum((same & earlier).astype(jnp.int32), 1)


def adam_update(param, grad, first, second, rate):
    first_new = first_decay * first + (1.0 - first_decay) * grad
    second_new = second_decay * second + (1.0 - second_decay) * grad * grad
    first_hat = first_new / (1.0 - first_decay**STEP)
    second_hat = second_new / (1.0 - second_decay**STEP)
    param_new = param - rate * (
        first_hat / (jnp.sqrt(second_hat) + adam_epsilon) + weight_decay * param
    )
    return (param_new, first_new, second_new)


ROWS = 4 * BUCKET
SQRT_HALF = 0.7071067811865476
INV_SQRT_TAU = 0.3989422804014327
ALLOWED = 3.0e38
BARRED = -1000000000.0


def dot(left, right):
    return jnp.dot(left, right, preferred_element_type=jnp.float32)


def dot_back(left, right):
    return lax.dot_general(
        left, right, (((1,), (1,)), ((), ())), preferred_element_type=jnp.float32
    )


def outer(left, right):
    return lax.dot_general(
        left, right, (((0,), (0,)), ((), ())), preferred_element_type=jnp.float32
    )


def passage_facts(counts, lengths, position):
    places = lengths.shape[1]
    big_end = counts[0, 0]
    mid_end = big_end + counts[0, 1]
    all_end = mid_end + counts[0, 2]
    start = jnp.int32(0)
    member = jnp.zeros(position.shape, jnp.int32)
    usable = jnp.zeros(position.shape, jnp.int32)
    for number in range(places):
        size = jnp.where(
            number < big_end,
            4 * BUCKET,
            jnp.where(number < mid_end, 2 * BUCKET, jnp.where(number < all_end, BUCKET, 0)),
        )
        inside = (position >= start) & (position < start + size)
        live = inside & (position < start + lengths[0, number])
        member = jnp.where(inside, number + 1, member)
        usable = jnp.where(live, 1, usable)
        start = start + size
    passage = jnp.where(member > 0, member - 1, places + position // BUCKET)
    return usable, passage


def normalize(values):
    center = jnp.mean(values, -1, keepdims=True)
    centered = values - center
    spread = jnp.mean(centered * centered, -1, keepdims=True)
    inverse = lax.rsqrt(spread + norm_epsilon)
    return centered * inverse, inverse


def normalize_back(grad, hat, inverse):
    center = jnp.mean(grad, -1, keepdims=True)
    along = jnp.mean(grad * hat, -1, keepdims=True)
    return inverse * (grad - center - hat * along)


def columns_total(values):
    return jnp.sum(values, 0, keepdims=True)


def attention_caps(counts, lengths, block):
    at_row = lax.broadcasted_iota(jnp.int32, (ROWS, 1), 0) + block * ROWS
    at_column = lax.broadcasted_iota(jnp.int32, (1, ROWS), 1) + block * ROWS
    _, passage_row = passage_facts(counts, lengths, at_row)
    usable_column, passage_column = passage_facts(counts, lengths, at_column)
    allowed = (passage_row == passage_column) & ((usable_column == 1) | (at_row == at_column))
    return jnp.where(allowed, ALLOWED, BARRED)


def attend_quad(
    quad, weight, x_ref, vec_ref, cap_ref, q_ref, k_ref, v_ref, p_ref, ctx_ref, between=lambda: None
):
    cols = pl.ds(pl.multiple_of(quad * 256, 256), 256)
    x = x_ref[...]
    query = (dot(x, weight(0, cols)) + vec_ref[0:1, cols]).astype(jnp.bfloat16)
    query = query * jnp.bfloat16(0.125)
    keyed = dot(x, weight(1, cols)).astype(jnp.bfloat16)
    valued = (dot(x, weight(2, cols)) + vec_ref[1:2, cols]).astype(jnp.bfloat16)
    q_ref[...] = query
    k_ref[...] = keyed
    v_ref[...] = valued
    low_half = lax.broadcasted_iota(jnp.int32, (1, 128), 1) < 64
    for pair in range(2):
        part = slice(128 * pair, 128 * pair + 128)
        contexts = []
        for head in range(2):
            here = low_half if head == 0 else ~low_half
            mine = jnp.where(here, query[:, part], jnp.zeros_like(query[:, part]))
            scores = jnp.minimum(dot_back(mine, keyed[:, part]), cap_ref[...])
            exponent = jnp.exp(scores - jnp.max(scores, -1, keepdims=True))
            inverse = 1.0 / jnp.sum(exponent, -1, keepdims=True)
            probability = (exponent * inverse).astype(jnp.bfloat16)
            p_ref[0, 2 * pair + head] = probability
            contexts.append(dot(probability, valued[:, part]))
        both = jnp.where(low_half, contexts[0], contexts[1]).astype(jnp.bfloat16)
        ctx_ref[:, pl.ds(pl.multiple_of(quad * 256 + 128 * pair, 128), 128)] = both
        if pair == 0:
            between()


def close_block(w_out, x_ref, vec_ref, ctx_ref, hat_ref, inverse_ref):
    branch = dot(ctx_ref[...], w_out) + vec_ref[2:3, :]
    hat_ref[...], inverse_ref[...] = normalize(x_ref[...].astype(jnp.float32) + branch)


def attend_back_pair(pair, here, p_ref, qkv, ctx_ref, grad_ctx_ref, pulled, half, add_sums):
    low_half = lax.broadcasted_iota(jnp.int32, (1, 128), 1) < 64
    cols = pl.ds(pl.multiple_of(pair * 128, 128), 128)
    query, keyed, valued = qkv
    pull = grad_ctx_ref[here, cols]
    along = pull.astype(jnp.float32) * ctx_ref[here, cols].astype(jnp.float32)
    by_query, by_key, by_value = [], [], []
    for head in range(2):
        mask = low_half if head == 0 else ~low_half
        mine = jnp.where(mask, pull, jnp.zeros_like(pull))
        level = jnp.sum(jnp.where(mask, along, 0.0), -1, keepdims=True)
        probability = p_ref[head]
        grad_prob = dot_back(mine, valued)
        grad_scores = (probability.astype(jnp.float32) * (grad_prob - level)).astype(jnp.bfloat16)
        by_query.append(dot(grad_scores, keyed))
        by_key.append(outer(grad_scores, query))
        by_value.append(outer(probability, pull))
    grad_query = (jnp.where(low_half, by_query[0], by_query[1]) * 0.125).astype(jnp.bfloat16)
    grad_value = jnp.where(low_half, by_value[0], by_value[1]).astype(jnp.bfloat16)
    pulled[0, here, half] = grad_query
    pulled[1, here, half] = jnp.where(low_half, by_key[0], by_key[1]).astype(jnp.bfloat16)
    pulled[2, here, half] = grad_value
    add_sums(cols, columns_total(grad_query.astype(jnp.float32)), columns_total(grad_value.astype(jnp.float32)))


def gelu_parts(up):
    share = 0.5 + 0.5 * lax.erf(up * SQRT_HALF)
    slope = share + up * (jnp.exp(up * up * -0.5) * INV_SQRT_TAU)
    return (up * share).astype(jnp.bfloat16), slope


def attend_forward(
    counts,
    lengths,
    x_ref,
    w_hbm,
    vec_ref,
    q_ref,
    k_ref,
    v_ref,
    p_ref,
    ctx_ref,
    hat_ref,
    inverse_ref,
    w_buf,
    cap_ref,
    w_sem,
):
    block, quad = pl.program_id(0), pl.program_id(1)
    loads = [pltpu.make_async_copy(w_hbm.at[at], w_buf.at[at], w_sem.at[at]) for at in range(4)]

    @pl.when((block == 0) & (quad == 0))
    def _():
        for load in loads:
            load.start()
        for load in loads:
            load.wait()

    @pl.when(quad == 0)
    def _():
        cap_ref[...] = attention_caps(counts, lengths, block)

    def weight(at, cols):
        return w_buf[at, :, cols]

    attend_quad(quad, weight, x_ref, vec_ref, cap_ref, q_ref, k_ref, v_ref, p_ref, ctx_ref)

    @pl.when(quad == 2)
    def _():
        close_block(w_buf[3], x_ref, vec_ref, ctx_ref, hat_ref, inverse_ref)


def attended(counts, lengths, x, weights, vectors):
    tokens, width = x.shape
    blocks = tokens // ROWS
    low = jnp.bfloat16
    smem = pl.BlockSpec(memory_space=pltpu.SMEM)
    quad = pl.BlockSpec((ROWS, 256), lambda b, h: (b, h))
    rows = pl.BlockSpec((ROWS, width), lambda b, h: (b, 0))
    shaped = jax.ShapeDtypeStruct
    return pl.pallas_call(
        attend_forward,
        grid=(blocks, 3),
        out_shape=(
            shaped((tokens, width), low),
            shaped((tokens, width), low),
            shaped((tokens, width), low),
            shaped((blocks, HEADS, ROWS, ROWS), low),
            shaped((tokens, width), low),
            shaped((tokens, width), jnp.float32),
            shaped((tokens, 1), jnp.float32),
        ),
        in_specs=[
            smem,
            smem,
            rows,
            pl.BlockSpec(memory_space=pl.ANY),
            pl.BlockSpec((VROWS, width), lambda b, h: (0, 0)),
        ],
        out_specs=(
            quad,
            quad,
            quad,
            pl.BlockSpec((1, 4, ROWS, ROWS), lambda b, h: (b, h, 0, 0)),
            rows,
            rows,
            pl.BlockSpec((ROWS, 1), lambda b, h: (b, 0)),
        ),
        scratch_shapes=[
            pltpu.VMEM((4, width, width), low),
            pltpu.VMEM((ROWS, ROWS), jnp.float32),
            pltpu.SemaphoreType.DMA((4,)),
        ],
        compiler_params=pltpu.CompilerParams(vmem_limit_bytes=56 * 2**20),
        name="attend_forward",
    )(counts, lengths, x, weights, vectors)


def feed_forward_both(
    counts,
    lengths,
    hat_ref,
    inverse_ref,
    cot_ref,
    w_hbm,
    vec_ref,
    mixed_ref,
    first_ref,
    branch_ref,
    context_ref,
    up_grad_ref,
    down_grad_ref,
    sum_ref,
    w_buf,
    active_ref,
    up_ref,
    hidden_ref,
    down_ref,
    slope_ref,
    w_sem,
):
    step = pl.program_id(0)
    blocks = pl.num_programs(0) - 4
    loads = [
        pltpu.make_async_copy(w_hbm.at[3 + at], w_buf.at[at], w_sem.at[at]) for at in range(9)
    ]

    @pl.when(step == 0)
    def _():
        for load in loads[1:] + loads[:1]:
            load.start()
        sum_ref[...] = jnp.zeros_like(sum_ref)
        for load in loads[1:] + loads[:1]:
            load.wait()

    @pl.when(step < blocks)
    def _():
        here = pl.ds(pl.multiple_of(step * ROWS, ROWS), ROWS)
        at_row = lax.broadcasted_iota(jnp.int32, (ROWS, 1), 0) + step * ROWS
        live = passage_facts(counts, lengths, at_row)[0].astype(jnp.float32)
        hat = hat_ref[...]
        hidden = hat * vec_ref[10:11, :] + vec_ref[8:9, :]
        hidden_low = hidden.astype(jnp.bfloat16)
        hidden_ref[here, :] = hidden_low
        total = hidden + vec_ref[7:8, :]
        for tile in range(4):
            up = dot(hidden_low, w_buf[1 + tile]) + vec_ref[3 + tile : 4 + tile, :]
            active, slope_ref[tile] = gelu_parts(up)
            active_ref[tile, here, :] = active
            total = total + dot(active, w_buf[5 + tile])
        hat_two, inverse_two = normalize(total)
        mixed_ref[...] = ((hat_two * vec_ref[11:12, :] + vec_ref[9:10, :]) * live).astype(jnp.bfloat16)
        grad_out = cot_ref[...].astype(jnp.float32) * live
        sum_ref[11:12, :] += columns_total(grad_out * hat_two)
        sum_ref[9:10, :] += columns_total(grad_out)
        second = normalize_back(grad_out * vec_ref[11:12, :], hat_two, inverse_two)
        down_low = second.astype(jnp.bfloat16)
        down_ref[here, :] = down_low
        sum_ref[7:8, :] += columns_total(down_low.astype(jnp.float32))
        grad_hidden = second
        for tile in range(4):
            pulled = dot_back(down_low, w_buf[5 + tile])
            up_low = (pulled * slope_ref[tile]).astype(jnp.bfloat16)
            up_ref[tile, here, :] = up_low
            sum_ref[3 + tile : 4 + tile, :] += columns_total(up_low.astype(jnp.float32))
            grad_hidden = grad_hidden + dot_back(up_low, w_buf[1 + tile])
        sum_ref[10:11, :] += columns_total(grad_hidden * hat)
        sum_ref[8:9, :] += columns_total(grad_hidden)
        grad_first = normalize_back(grad_hidden * vec_ref[10:11, :], hat, inverse_ref[...])
        first_ref[...] = grad_first
        branch_low = grad_first.astype(jnp.bfloat16)
        branch_ref[...] = branch_low
        sum_ref[2:3, :] += columns_total(branch_low.astype(jnp.float32))
        context_ref[...] = dot_back(branch_low, w_buf[0]).astype(jnp.bfloat16)

    @pl.when(step >= blocks)
    def _():
        tile = step - blocks
        up_grad_ref[0] = outer(hidden_ref[...], up_ref[tile]).astype(jnp.bfloat16)
        down_grad_ref[0] = outer(active_ref[tile], down_ref[...]).astype(jnp.bfloat16)


def fed_forward_both(counts, lengths, hat, inverse, cotangent, weights, vectors):
    tokens, width = hat.shape
    blocks = tokens // ROWS
    low = jnp.bfloat16
    smem = pl.BlockSpec(memory_space=pltpu.SMEM)
    shaped = jax.ShapeDtypeStruct

    def block_of(step):
        return jnp.minimum(step, blocks - 1)

    def tile_of(step):
        return jnp.maximum(step - blocks, 0)

    rows = pl.BlockSpec((ROWS, width), lambda i: (block_of(i), 0))
    tile = pl.BlockSpec((1, width, width), lambda i: (tile_of(i), 0, 0))
    return pl.pallas_call(
        feed_forward_both,
        grid=(blocks + 4,),
        out_shape=(
            shaped((tokens, width), low),
            shaped((tokens, width), jnp.float32),
            shaped((tokens, width), low),
            shaped((tokens, width), low),
            shaped((4, width, width), low),
            shaped((4, width, width), low),
            shaped((16, width), jnp.float32),
        ),
        in_specs=[
            smem,
            smem,
            rows,
            pl.BlockSpec((ROWS, 1), lambda i: (block_of(i), 0)),
            rows,
            pl.BlockSpec(memory_space=pl.ANY),
            pl.BlockSpec((VROWS, width), lambda i: (0, 0)),
        ],
        out_specs=(
            rows,
            rows,
            rows,
            rows,
            tile,
            tile,
            pl.BlockSpec((16, width), lambda i: (0, 0)),
        ),
        scratch_shapes=[
            pltpu.VMEM((9, width, width), low),
            pltpu.VMEM((4, tokens, width), low),
            pltpu.VMEM((4, tokens, width), low),
            pltpu.VMEM((tokens, width), low),
            pltpu.VMEM((tokens, width), low),
            pltpu.VMEM((4, ROWS, width), jnp.float32),
            pltpu.SemaphoreType.DMA((9,)),
        ],
        compiler_params=pltpu.CompilerParams(vmem_limit_bytes=60 * 2**20),
        name="feed_forward_both",
    )(counts, lengths, hat, inverse, cotangent, weights, vectors)


def attend_backward(
    p_ref,
    q_ref,
    k_ref,
    v_ref,
    x_ref,
    ctx_ref,
    grad_ctx_ref,
    branch_ref,
    first_ref,
    w_ref,
    input_ref,
    grad_ref,
    sum_ref,
    pulled,
):
    step = pl.program_id(0)
    quad, block = step // 2, lax.rem(step, 2)
    here = pl.ds(pl.multiple_of(block * ROWS, ROWS), ROWS)
    cols = pl.ds(pl.multiple_of(quad * 256, 256), 256)

    @pl.when(step == 0)
    def _():
        sum_ref[...] = jnp.zeros_like(sum_ref)
        input_ref[...] = first_ref[...]

    def add_sums(at, by_query, by_value):
        sum_ref[0:1, at] += by_query
        sum_ref[1:2, at] += by_value

    for pair in range(2):
        half = slice(128 * pair, 128 * pair + 128)
        qkv = q_ref[:, half], k_ref[:, half], v_ref[:, half]
        heads = p_ref.at[0, pl.ds(2 * pair, 2)]
        attend_back_pair(2 * quad + pair, here, heads, qkv, ctx_ref, grad_ctx_ref, pulled, half, add_sums)
    more = input_ref[here, :]
    for at in range(3):
        more = more + dot_back(pulled[at, here, :], w_ref[at, :, cols])
    input_ref[here, :] = more

    @pl.when(block == 1)
    def _():
        for tile in range(3):
            grad_ref[tile, :, cols] = outer(x_ref[...], pulled[tile]).astype(jnp.bfloat16)
        grad_ref[3, :, cols] = outer(ctx_ref[...], branch_ref[:, cols]).astype(jnp.bfloat16)


def attended_back(probs, query, keyed, valued, x, context, grad_context, grad_branch, grad_first, weights):
    tokens, width = x.shape
    low = jnp.bfloat16
    shaped = jax.ShapeDtypeStruct
    once = pl.Buffered(1)
    quad = pl.BlockSpec((ROWS, 256), lambda i: (lax.rem(i, 2), i // 2))
    whole = pl.BlockSpec((tokens, width), lambda i: (0, 0), pipeline_mode=once)
    return pl.pallas_call(
        attend_backward,
        grid=(6,),
        out_shape=(
            shaped((tokens, width), jnp.float32),
            shaped((4, width, width), low),
            shaped((16, width), jnp.float32),
        ),
        in_specs=[
            pl.BlockSpec((1, 4, ROWS, ROWS), lambda i: (lax.rem(i, 2), i // 2, 0, 0)),
            quad,
            quad,
            quad,
            whole,
            whole,
            whole,
            whole,
            whole,
            pl.BlockSpec((3, width, width), lambda i: (0, 0, 0), pipeline_mode=once),
        ],
        out_specs=(
            whole,
            pl.BlockSpec((4, width, width), lambda i: (0, 0, 0), pipeline_mode=once),
            pl.BlockSpec((16, width), lambda i: (0, 0)),
        ),
        scratch_shapes=[pltpu.VMEM((3, tokens, 256), low)],
        compiler_params=pltpu.CompilerParams(vmem_limit_bytes=56 * 2**20),
        name="attend_backward",
    )(probs, query, keyed, valued, x, context, grad_context, grad_branch, grad_first, weights)


def moved(param, grad, first, second, average, rate):
    param_new, first_new, second_new = adam_update(param, grad, first, second, rate)
    return param_new, first_new, second_new, average_rate * average + (1.0 - average_rate) * param_new


def update_kernel(
    gain_scale,
    grad_ref,
    master_ref,
    first_ref,
    second_ref,
    ema_ref,
    vec_grad_ref,
    bias_ref,
    gain_ref,
    vec_first_ref,
    vec_second_ref,
    vec_ema_ref,
    mixed_in,
    input_in,
    master_out,
    first_out,
    second_out,
    ema_out,
    copy_out,
    vec_out,
    vec_first_out,
    vec_second_out,
    vec_ema_out,
    mixed_out,
    input_out,
    vec_ref,
    pass_sem,
):
    slot, row = pl.program_id(0), pl.program_id(1)

    def passes():
        return [
            pltpu.make_async_copy(mixed_in, mixed_out, pass_sem.at[0]),
            pltpu.make_async_copy(input_in, input_out, pass_sem.at[1]),
        ]

    @pl.when((slot == 0) & (row == 0))
    def _():
        for copy in passes():
            copy.start()
        vec_ref[0:10, :] = bias_ref[...]
        vec_ref[10:12, :] = gain_ref[...]
        vec_grad = vec_grad_ref[0:VROWS, :] * gain_scale
        vec_out[...], vec_first_out[...], vec_second_out[...], vec_ema_out[...] = moved(
            vec_ref[...], vec_grad, vec_first_ref[...], vec_second_ref[...], vec_ema_ref[...], vector_rate
        )

    grad = grad_ref[...].astype(jnp.float32) * gain_scale
    result = moved(master_ref[0], grad, first_ref[0], second_ref[0], ema_ref[0], tile_rate)
    master_out[0], first_out[0], second_out[0], ema_out[0] = result
    copy_out[0] = result[0].astype(jnp.bfloat16)

    @pl.when((slot == SLOTS - 1) & (row == pl.num_programs(1) - 1))
    def _():
        for copy in passes():
            copy.wait()


def updated(
    gain_scale,
    slot_grads,
    master,
    first,
    second,
    ema,
    vec_grad,
    bias,
    gain,
    vec_first,
    vec_second,
    vec_ema,
    mixed,
    input_grad,
):
    width = master.shape[-1]
    chunk = 192
    tile = pl.BlockSpec((1, 1, chunk, width), lambda s, r: (0, s, r, 0))
    any_space = pl.BlockSpec(memory_space=pl.ANY)

    def whole(value):
        return pl.BlockSpec(value.shape, lambda s, r: (0, 0))

    shaped = jax.ShapeDtypeStruct
    tile_shape = shaped(master.shape, jnp.float32)
    vec_shape = shaped((VROWS, width), jnp.float32)
    results = pl.pallas_call(
        functools.partial(update_kernel, gain_scale),
        grid=(SLOTS, width // chunk),
        out_shape=(tile_shape,) * 4
        + (shaped(master.shape, jnp.bfloat16),)
        + (vec_shape,) * 4
        + (shaped(mixed.shape, mixed.dtype), shaped(input_grad.shape, input_grad.dtype)),
        in_specs=[pl.BlockSpec((1, chunk, width), lambda s, r: (s, r, 0))]
        + [tile] * 4
        + [whole(value) for value in (vec_grad, bias, gain, vec_first, vec_second, vec_ema)]
        + [any_space] * 2,
        out_specs=(tile,) * 5 + (whole(vec_first),) * 4 + (any_space,) * 2,
        scratch_shapes=[pltpu.VMEM((VROWS, width), jnp.float32), pltpu.SemaphoreType.DMA((2,))],
        compiler_params=pltpu.CompilerParams(vmem_limit_bytes=62 * 2**20),
        name="update",
    )(
        slot_grads,
        master,
        first,
        second,
        ema,
        vec_grad,
        bias,
        gain,
        vec_first,
        vec_second,
        vec_ema,
        mixed,
        input_grad,
    )
    return results[-2:] + results[:-2]


MESH = pl.DeviceIdType.MESH
GROUP = 32
PAIRS = TILES // 2
PLANE = 8
PIECE = 96
PAIR_TILES = ((0, 1), (2, 3), (4, 8), (5, 9), (6, 10), (7, 11))
EARLY = 2
WHOLE = 3


def remote(src, dst, send, recv, device):
    return pltpu.make_async_remote_copy(
        src_ref=src, dst_ref=dst, send_sem=send, recv_sem=recv, device_id=(device,), device_id_type=MESH
    )


def place(device):
    core = lax.rem(device, 2)
    x = lax.rem(device // 2, 2)
    y = lax.rem(device // 4, 2)
    z = device // 8
    return z, y, x, core


def start(copies):
    for copy in copies:
        copy.start()


def arrive(copies):
    for copy in copies:
        copy.wait_recv()


def greet(z, in_plane):
    barrier = pltpu.get_barrier_semaphore()
    for hop in range(1, PLANE):
        other = z * PLANE + lax.rem(in_plane + hop, PLANE)
        pl.semaphore_signal(barrier, inc=1, device_id=(other,), device_id_type=MESH)
    for hop in range(1, 4):
        other = lax.rem(z + hop, 4) * PLANE + in_plane
        pl.semaphore_signal(barrier, inc=1, device_id=(other,), device_id_type=MESH)
    pl.semaphore_wait(barrier, PLANE + 2)


def along_z(z, in_plane):
    inner = (1 + z // 2) * PLANE + in_plane
    other_middle = (3 - z) * PLANE + in_plane
    outer_end = lax.rem(lax.rem(z + 3, 4) * 3, 4) * PLANE + in_plane
    return inner, other_middle, outer_end


def third(part):
    return slice(None) if part == WHOLE else pl.ds(256 * part, 256)


def slot_number(owners, tile):
    number = jnp.int32(0)
    for earlier in range(tile):
        number = number + jnp.where(owners[earlier] == owners[tile], 1, 0)
    return number


def unit(pair, part):
    return 3 * pair + part if pair < EARLY else 2 * EARLY + pair


UNITS = [(pair, part) for pair in range(EARLY) for part in range(3)]
UNITS += [(pair, WHOLE) for pair in range(EARLY, PAIRS)]

FRONT_PLAN = (
    (
        ("open",),
        ("swap", 0),
        ("sent", 0),
        ("swap", 1),
        ("choose", 0),
        ("sent", 1),
        ("end", 0, 0),
        ("swap", 2),
        ("end", 1, 0),
        ("middle", 1, 0),
        ("choose", 1),
        ("end", 1, 1),
        ("end", 0, 1),
        ("caps",),
        ("middle", 0, 0),
        ("total", 1, 0),
        ("choose", 2),
        ("middle", 0, 1),
        ("total", 0, 0),
        ("end", 2),
        ("middle", 1, 1),
        ("total", 0, 1),
        ("end", 0, 2),
        ("middle", 0, 2),
        ("total", 1, 1),
        ("mid", 0, 0),
        ("middle", 2),
        ("end", 1, 2),
        ("mid", 0, 1),
        ("far", 0, 0),
        ("middle", 1, 2),
        ("end", 3),
        ("mid", 1, 0),
        ("total", 0, 2),
        ("near", 0, 0),
        ("far", 1, 0),
        ("mid", 1, 1),
        ("total", 1, 2),
        ("middle", 3),
        ("finish", 0, 0),
        ("total", 2),
        ("end", 4),
        ("far", 1, 1),
        ("near", 1, 0),
        ("far", 0, 1),
        ("finish", 1, 0),
        ("mid", 0, 2),
    ),
    (
        ("near", 1, 1),
        ("middle", 4),
        ("end", 5),
        ("mid", 1, 2),
        ("total", 3),
        ("far", 0, 2),
        ("near", 0, 1),
    ),
    (
        ("finish", 1, 1),
        ("mid", 2),
        ("far", 1, 2),
    ),
    (
        ("middle", 5),
        ("total", 4),
        ("near", 0, 2),
        ("mid", 3),
    ),
    (
        ("finish", 0, 1),
        ("far", 2),
    ),
    (
        ("near", 1, 2),
    ),
    (),
    (
        ("finish", 0, 2),
        ("total", 5),
        ("far", 3),
        ("finish", 1, 2),
        ("keep",),
        ("mid", 4),
    ),
    (),
    (),
    (
        ("near", 2),
        ("far", 4),
    ),
    (
        ("mid", 5),
    ),
    (
        ("finish", 2),
        ("near", 3),
    ),
    (),
    (
        ("far", 5),
        ("finish", 3),
    ),
    (
        ("near", 4),
    ),
    (
        ("finish", 4),
    ),
    (
        ("near", 5),
    ),
    (
        ("finish", 5),
    ),
)


def forward_and_pull(
    counts,
    lengths,
    owners,
    bias_ref,
    gain_ref,
    x_hbm,
    cot_hbm,
    master_hbm,
    q_ref,
    k_ref,
    v_ref,
    p_ref,
    ctx_hbm,
    hidden_hbm,
    active_hbm,
    up_hbm,
    down_hbm,
    mixed_hbm,
    first_hbm,
    branch_hbm,
    grad_ctx_hbm,
    w_out,
    sum_ref,
    vec_ref,
    cap_ref,
    wide,
    low,
    stage_a,
    stage_b,
    stage_c,
    chosen,
    from_end,
    from_middle,
    w_buf,
    x_then_hidden,
    ctx_then_grad,
    cot_then_down,
    mixed_then_branch,
    hat_ref,
    inverse_ref,
    slope_ref,
    tile_buf,
    load_sem,
    store_sem,
    tile_sem,
    out_sem,
    swap_send,
    swap_recv,
    z_send,
    z_recv,
    mid_send,
    mid_recv,
    far_send,
    far_recv,
    near_send,
    near_recv,
):
    step = pl.program_id(0)
    width = 8 * PIECE
    me = lax.axis_index("dp")
    z, y, x, core = place(me)
    in_plane = lax.rem(me, PLANE)
    sibling = me + 1 - 2 * core
    x_peer = me + 2 - 4 * x
    y_peer = me + 4 - 8 * y
    z_targets = along_z(z, in_plane)
    stages = (stage_a, stage_b, stage_c)
    is_end = (z == 0) | (z == 3)
    is_middle = (z == 1) | (z == 2)

    def piece_rows(cell_core, cell_x, cell_y):
        return pl.ds(pl.multiple_of(((cell_core * 2 + cell_x) * 2 + cell_y) * PIECE, 16), PIECE)

    def swap(part):
        def send(hop, carry):
            target = lax.rem(in_plane + hop, PLANE)
            _, ty, tx, tc = place(target)
            remote(
                low.at[:, piece_rows(tc, tx, ty), third(part)],
                stages[part].at[pl.ds(2 * in_plane, 2)],
                swap_send.at[part],
                swap_recv.at[part],
                z * PLANE + target,
            ).start()
            return carry

        lax.fori_loop(1, PLANE, send, 0)

    def swap_wait(part, sem):
        most = stages[part].at[pl.ds(0, 2 * PLANE - 2)]
        pltpu.make_async_copy(most, most, sem.at[part]).wait()

    def z_copy(pair, part, level):
        two = pl.ds(2 * pair, 2)
        cols = third(part)
        src = w_buf.at[two, core, x, y, :, cols] if level == 2 else chosen.at[two, :, cols]
        dst = (from_end.at[two, :, cols], from_middle.at[two, :, cols], src)[level]
        at = unit(pair, part)
        return remote(src, dst, z_send.at[level, at], z_recv.at[level, at], z_targets[level])

    def z_end(pair, part=WHOLE):
        @pl.when(is_end)
        def _():
            z_copy(pair, part, 0).start()

    def z_middle(pair, part=WHOLE):
        @pl.when(is_middle)
        def _():
            z_copy(pair, part, 0).wait_recv()
            two, cols = pl.ds(2 * pair, 2), third(part)
            chosen[two, :, cols] = chosen[two, :, cols] + from_end[two, :, cols]
            z_copy(pair, part, 1).start()

    def z_total(pair, part=WHOLE):
        @pl.when(is_middle)
        def _():
            z_copy(pair, part, 1).wait_recv()
            two, cols = pl.ds(2 * pair, 2), third(part)
            w_buf[two, core, x, y, :, cols] = chosen[two, :, cols] + from_middle[two, :, cols]
            z_copy(pair, part, 2).start()

    def mid_copies(pair, part):
        copies = []
        for n, peer in enumerate((y_peer, x_peer)):
            spot = w_buf.at[2 * pair + n, core, x, y, :, third(part)]
            at = unit(pair, part), n
            copies.append(remote(spot, spot, mid_send.at[at], mid_recv.at[at], peer))
        return copies

    def halves(pair, part, late):
        row = 1 - x if late else x
        column = 1 - y if late else y
        cols = third(part)
        return w_buf.at[2 * pair, core, row, :, :, cols], w_buf.at[2 * pair + 1, core, :, column, :, cols]

    def far_copies(pair, part):
        copies = []
        for n, peer in enumerate((x_peer, y_peer)):
            spot = halves(pair, part, False)[n]
            at = unit(pair, part), n
            copies.append(remote(spot, spot, far_send.at[at], far_recv.at[at], peer))
        return copies

    def near_copies(pair, part, late):
        copies = []
        for n in range(2):
            spot = halves(pair, part, late)[n]
            at = unit(pair, part), n, late
            copies.append(remote(spot, spot, near_send.at[at], near_recv.at[at], sibling))
        return copies

    def give_mid(pair, part=WHOLE):
        @pl.when(is_end)
        def _():
            z_copy(pair, part, 2).wait_recv()

        start(mid_copies(pair, part))

    def give_far(pair, part=WHOLE):
        arrive(mid_copies(pair, part))
        start(far_copies(pair, part) + near_copies(pair, part, 0))

    def give_near(pair, part=WHOLE):
        arrive(far_copies(pair, part))
        start(near_copies(pair, part, 1))

    def finish(pair, part=WHOLE):
        arrive(near_copies(pair, part, 0) + near_copies(pair, part, 1))

    def choose(part):
        swap_wait(part, swap_recv)
        for pair in range(PAIRS):
            for n, tile in enumerate(PAIR_TILES[pair]):
                owner = owners[tile]
                value = stages[part][SLOTS * lax.rem(owner, PLANE) + slot_number(owners, tile)]
                chosen[2 * pair + n, :, third(part)] = jnp.where(
                    owner // PLANE == z, value, jnp.zeros_like(value)
                )

    def load(at):
        src = (x_hbm, cot_hbm, master_hbm)[at]
        dst = (x_then_hidden, cot_then_down, wide)[at]
        return pltpu.make_async_copy(src, dst, load_sem.at[at])

    def store(at):
        src, dst = (
            (x_then_hidden, hidden_hbm),
            (ctx_then_grad, ctx_hbm),
            (cot_then_down, down_hbm),
            (mixed_then_branch, mixed_hbm),
            (ctx_then_grad, grad_ctx_hbm),
            (mixed_then_branch, branch_hbm),
            (wide, first_hbm),
        )[at]
        src = src.at[pl.ds(0, 2 * ROWS)] if src is wide else src
        return pltpu.make_async_copy(src, dst, store_sem.at[at])

    def w_stores():
        return [
            pltpu.make_async_copy(w_buf.at[tile], w_out.at[tile], out_sem.at[tile]) for tile in range(3)
        ]

    def weight(at, cols=slice(None)):
        value = w_buf[at, :, :, :, :, cols]
        return value.reshape(width, value.shape[-1])

    def open_all():
        for at in range(3):
            load(at).start()
        sum_ref[...] = jnp.zeros_like(sum_ref)
        vec_ref[0:10, :] = bias_ref[...]
        vec_ref[10:12, :] = gain_ref[...]
        greet(z, in_plane)
        load(2).wait()
        for slot in range(SLOTS):
            low[slot] = wide[width * slot : width * (slot + 1), :].astype(jnp.bfloat16)
        for part in range(3):
            stages[part][pl.ds(2 * in_plane, 2)] = low[:, piece_rows(core, x, y), third(part)]

    def make_caps():
        for block in range(2):
            cap_ref[block] = attention_caps(counts, lengths, block)
        load(0).wait()
        load(1).wait()

    actions = {
        "open": open_all,
        "caps": make_caps,
        "swap": swap,
        "sent": lambda part: swap_wait(part, swap_send),
        "choose": choose,
        "end": z_end,
        "middle": z_middle,
        "total": z_total,
        "mid": give_mid,
        "far": give_far,
        "near": give_near,
        "finish": finish,
        "keep": lambda: start(w_stores()),
    }

    def serve(half):
        for at in range(half, len(FRONT_PLAN), 2):
            if FRONT_PLAN[at]:

                @pl.when(step == at // 2)
                def _():
                    for name, *rest in FRONT_PLAN[at]:
                        actions[name](*rest)

    serve(0)
    quad, block = step // 2, lax.rem(step, 2)
    here = pl.ds(pl.multiple_of(block * ROWS, ROWS), ROWS)

    @pl.when(step < 6)
    def _():
        attend_quad(
            quad,
            weight,
            x_then_hidden.at[here],
            vec_ref,
            cap_ref.at[block],
            q_ref,
            k_ref,
            v_ref,
            p_ref,
            ctx_then_grad.at[here],
            lambda: serve(1),
        )

    @pl.when((step >= 4) & (step < 6))
    def _():
        branch = dot(ctx_then_grad[here, :], weight(3)) + vec_ref[2:3, :]
        hat, inverse = normalize(x_then_hidden[here, :].astype(jnp.float32) + branch)
        hat_ref[here, :] = hat
        inverse_ref[here, :] = inverse
        hidden = hat * vec_ref[10:11, :] + vec_ref[8:9, :]
        x_then_hidden[here, :] = hidden.astype(jnp.bfloat16)
        wide[here, :] = hidden + vec_ref[7:8, :]

    @pl.when(step == 5)
    def _():
        start([store(0), store(1)])

    turn = step - 6
    slot = lax.rem(turn, 2)

    def tile_store(source_slot, target):
        return pltpu.make_async_copy(tile_buf.at[source_slot], target, tile_sem.at[source_slot])

    @pl.when(turn >= 2)
    def _():
        tile_store(slot, active_hbm.at[0]).wait()

    @pl.when((step >= 6) & (step < 10))
    def _():
        for half in range(2):
            rows = slice(ROWS * half, ROWS * half + ROWS)
            up = dot(x_then_hidden[rows, :], weight(4 + 2 * turn)) + vec_ref[pl.ds(3 + turn, 1), :]
            active, slope = gelu_parts(up)
            slope_ref[turn, rows, :] = slope.astype(jnp.bfloat16)
            tile_buf[slot, rows, :] = active
            wide[rows, :] = wide[rows, :] + dot(active, weight(5 + 2 * turn))
            if half == 0:
                serve(1)
        tile_store(slot, active_hbm.at[turn]).start()

    @pl.when(step == 10)
    def _():
        for half in range(2):
            rows = slice(ROWS * half, ROWS * half + ROWS)
            at_row = lax.broadcasted_iota(jnp.int32, (ROWS, 1), 0) + half * ROWS
            live = passage_facts(counts, lengths, at_row)[0].astype(jnp.float32)
            hat, inverse = normalize(wide[rows, :])
            mixed = (hat * vec_ref[11:12, :] + vec_ref[9:10, :]) * live
            mixed_then_branch[rows, :] = mixed.astype(jnp.bfloat16)
            grad_out = cot_then_down[rows, :].astype(jnp.float32) * live
            sum_ref[11:12, :] += columns_total(grad_out * hat)
            sum_ref[9:10, :] += columns_total(grad_out)
            second = normalize_back(grad_out * vec_ref[11:12, :], hat, inverse)
            wide[rows, :] = second
            down_low = second.astype(jnp.bfloat16)
            cot_then_down[rows, :] = down_low
            sum_ref[7:8, :] += columns_total(down_low.astype(jnp.float32))
        start([store(2), store(3)])

    @pl.when(step >= 10)
    def _():
        tile = step - 10
        for half in range(2):
            rows = slice(ROWS * half, ROWS * half + ROWS)
            pulled = dot_back(cot_then_down[rows, :], weight(5 + 2 * tile))
            up_low = (pulled * slope_ref[tile, rows, :].astype(jnp.float32)).astype(jnp.bfloat16)
            tile_buf[slot, rows, :] = up_low
            sum_ref[pl.ds(3 + tile, 1), :] += columns_total(up_low.astype(jnp.float32))
            wide[rows, :] = wide[rows, :] + dot_back(up_low, weight(4 + 2 * tile))
        tile_store(slot, up_hbm.at[tile]).start()

    @pl.when(step == 13)
    def _():
        store(1).wait()
        store(3).wait()
        for half in range(2):
            rows = slice(ROWS * half, ROWS * half + ROWS)
            grad_hidden, hat = wide[rows, :], hat_ref[rows, :]
            sum_ref[10:11, :] += columns_total(grad_hidden * hat)
            sum_ref[8:9, :] += columns_total(grad_hidden)
            first = normalize_back(grad_hidden * vec_ref[10:11, :], hat, inverse_ref[rows, :])
            wide[rows, :] = first
            branch_low = first.astype(jnp.bfloat16)
            mixed_then_branch[rows, :] = branch_low
            sum_ref[2:3, :] += columns_total(branch_low.astype(jnp.float32))
            ctx_then_grad[rows, :] = dot_back(branch_low, weight(3)).astype(jnp.bfloat16)
        start([store(4), store(5), store(6)])
        store(0).wait()
        store(2).wait()
        for at in range(2):
            tile_store(at, up_hbm.at[0]).wait()
        for copy in w_stores():
            copy.wait()
        swap_wait(2, swap_send)
        for pair, part in UNITS:
            for copy in mid_copies(pair, part) + far_copies(pair, part):
                copy.wait_send()
            for copy in near_copies(pair, part, 0) + near_copies(pair, part, 1):
                copy.wait_send()

            @pl.when(is_end)
            def _():
                z_copy(pair, part, 0).wait_send()

            @pl.when(is_middle)
            def _():
                z_copy(pair, part, 1).wait_send()
                z_copy(pair, part, 2).wait_send()

        for at in range(4, 7):
            store(at).wait()


def forwarded_and_pulled(counts, lengths, owners, bias, gain, x, cotangent, master):
    tokens, width = x.shape
    blocks = tokens // ROWS
    low, high = jnp.bfloat16, jnp.float32
    smem = pl.BlockSpec(memory_space=pltpu.SMEM)
    any_space = pl.BlockSpec(memory_space=pl.ANY)
    dma = pltpu.SemaphoreType.DMA
    shaped = jax.ShapeDtypeStruct

    def at(step):
        step = jnp.minimum(step, 5)
        return lax.rem(step, 2), step // 2

    quad = pl.BlockSpec((ROWS, 256), at)
    rows = shaped((tokens, width), low)
    cut = (2, 2, 2, PIECE, width)
    units = len(UNITS)
    results = pl.pallas_call(
        forward_and_pull,
        grid=(14,),
        out_shape=(
            rows,
            rows,
            rows,
            shaped((blocks, HEADS, ROWS, ROWS), low),
            rows,
            rows,
            shaped((4, tokens, width), low),
            shaped((4, tokens, width), low),
            rows,
            rows,
            shaped((tokens, width), high),
            rows,
            rows,
            shaped((3,) + cut, low),
            shaped((16, width), high),
        ),
        in_specs=[smem] * 3
        + [pl.BlockSpec(bias.shape, lambda i: (0, 0)), pl.BlockSpec(gain.shape, lambda i: (0, 0))]
        + [any_space] * 3,
        out_specs=(quad, quad, quad, pl.BlockSpec((1, 4, ROWS, ROWS), lambda i: (*at(i), 0, 0)))
        + (any_space,) * 10
        + (pl.BlockSpec((16, width), lambda i: (0, 0)),),
        scratch_shapes=[
            pltpu.VMEM((VROWS, width), high),
            pltpu.VMEM((2, ROWS, ROWS), high),
            pltpu.VMEM((SLOTS * width, width), high),
            pltpu.VMEM((SLOTS, width, width), low),
            pltpu.VMEM((2 * PLANE, PIECE, 256), low),
            pltpu.VMEM((2 * PLANE, PIECE, 256), low),
            pltpu.VMEM((2 * PLANE, PIECE, 256), low),
            pltpu.VMEM((TILES, PIECE, width), low),
            pltpu.VMEM((TILES, PIECE, width), low),
            pltpu.VMEM((TILES, PIECE, width), low),
            pltpu.VMEM((TILES,) + cut, low),
            pltpu.VMEM((tokens, width), low),
            pltpu.VMEM((tokens, width), low),
            pltpu.VMEM((tokens, width), low),
            pltpu.VMEM((tokens, width), low),
            pltpu.VMEM((tokens, width), high),
            pltpu.VMEM((tokens, 1), high),
            pltpu.VMEM((4, tokens, width), low),
            pltpu.VMEM((2, tokens, width), low),
            dma((3,)),
            dma((7,)),
            dma((2,)),
            dma((3,)),
            dma((3,)),
            dma((3,)),
            dma((3, units)),
            dma((3, units)),
            dma((units, 2)),
            dma((units, 2)),
            dma((units, 2)),
            dma((units, 2)),
            dma((units, 2, 2)),
            dma((units, 2, 2)),
        ],
        compiler_params=pltpu.CompilerParams(
            collective_id=0, has_side_effects=True, vmem_limit_bytes=63 * 2**20
        ),
        name="forward_and_pull",
    )(counts, lengths, owners, bias, gain, x, cotangent, master.reshape(SLOTS * width, width))
    w_early = results[13].reshape(3, width, width)
    return results[:13] + (w_early,) + results[14:]


BACK_PLAN = (
    (),
    (
        ("core", 0),
    ),
    (
        ("core", 1),
        ("far", 0),
    ),
    (
        ("core", 2),
        ("far", 1),
    ),
    (),
    (
        ("far", 2),
        ("mid", 0),
    ),
    (
        ("core", 3),
    ),
    (),
    (
        ("mid", 1),
        ("end", 0),
    ),
    (
        ("mid", 2),
        ("core", 4),
        ("far", 3),
        ("middle", 0),
    ),
    (
        ("end", 1),
    ),
    (
        ("middle", 1),
    ),
    (
        ("end", 2),
        ("total", 0),
        ("core", 5),
        ("far", 4),
        ("mid", 3),
    ),
    (
        ("middle", 2),
        ("total", 1),
    ),
    (),
    (
        ("end", 3),
        ("mid", 4),
        ("middle", 3),
        ("far", 5),
        ("total", 2),
    ),
    (
        ("core", 6),
        ("mid", 5),
        ("end", 4),
        ("middle", 4),
        ("total", 3),
        ("take", 0),
        ("sum", 0),
        ("far", 6),
        ("total", 4),
        ("end", 5),
        ("middle", 5),
        ("mid", 6),
        ("take", 1),
        ("sum", 1),
        ("end", 6),
        ("take", 4),
        ("total", 5),
        ("take", 2),
        ("take", 3),
        ("deliver", 0),
        ("sum", 2),
        ("take", 5),
        ("middle", 6),
        ("total", 6),
        ("deliver", 1),
        ("take", 6),
        ("deliver", 2),
    ),
)


def pull_and_reduce(
    owners,
    p_ref,
    q_ref,
    k_ref,
    v_ref,
    ctx_ref,
    grad_ctx_ref,
    active_ref,
    up_ref,
    x_hbm,
    hidden_hbm,
    branch_hbm,
    down_hbm,
    first_hbm,
    w_hbm,
    late_ref,
    input_hbm,
    slot_grad,
    vec_out,
    w_buf,
    acc,
    pulled,
    hidden_then_x,
    down_then_branch,
    part,
    from_core,
    from_far,
    from_mid,
    from_end,
    from_middle,
    total,
    snap,
    outbox,
    vec_now,
    vec_in,
    holds,
    keeps,
    load_sem,
    core_send,
    core_recv,
    far_send,
    far_recv,
    mid_send,
    mid_recv,
    z_send,
    z_recv,
    vec_send,
    vec_recv,
    out_send,
    out_recv,
):
    step = pl.program_id(0)
    inner = jnp.maximum(step - 4, 0)
    quad, block, pair = inner // 4, lax.rem(inner, 4) // 2, lax.rem(inner, 2)
    me = lax.axis_index("dp")
    z, y, x, core = place(me)
    in_plane = lax.rem(me, PLANE)
    sibling = me + 1 - 2 * core
    x_peer = me + 2 - 4 * x
    y_peer = me + 4 - 8 * y
    z_targets = along_z(z, in_plane)
    is_end = (z == 0) | (z == 3)
    is_middle = (z == 1) | (z == 2)

    def items(batch):
        if batch < 4:
            return [(0, 4 + batch, slice(None)), (1, 8 + batch, slice(None))]
        cols = pl.ds(256 * (batch - 4), 256)
        return [(0, 0, cols), (1, 1, cols), (0, 2, cols), (1, 3, cols)]

    def held(tile):
        return part.at[tile, core]

    def core_copies(batch):
        return [
            remote(
                part.at[tile, 1 - core, :, :, :, cols],
                from_core.at[tile, :, :, :, cols],
                core_send.at[batch, n],
                core_recv.at[batch, n],
                sibling,
            )
            for n, (_, tile, cols) in enumerate(items(batch))
        ]

    def far_copies(batch):
        copies = []
        for n, (kind, tile, cols) in enumerate(items(batch)):
            mine = held(tile)
            copies.append(
                remote(
                    mine.at[:, 1 - y, :, cols] if kind else mine.at[1 - x, :, :, cols],
                    from_far.at[tile, :, :, cols],
                    far_send.at[batch, n],
                    far_recv.at[batch, n],
                    y_peer if kind else x_peer,
                )
            )
        return copies

    def mid_copies(batch):
        copies = []
        for n, (kind, tile, cols) in enumerate(items(batch)):
            mine = held(tile)
            copies.append(
                remote(
                    mine.at[1 - x, y, :, cols] if kind else mine.at[x, 1 - y, :, cols],
                    from_mid.at[tile, :, cols],
                    mid_send.at[batch, n],
                    mid_recv.at[batch, n],
                    x_peer if kind else y_peer,
                )
            )
        return copies

    def z_copies(batch, stage):
        copies = []
        for n, (_, tile, cols) in enumerate(items(batch)):
            if stage == 2:
                src, dst = total.at[tile, :, cols], total.at[tile, :, cols]
            else:
                src = held(tile).at[x, y, :, cols]
                dst = (from_middle if stage else from_end).at[tile, :, cols]
            copies.append(
                remote(
                    src,
                    dst,
                    z_send.at[stage, batch, n],
                    z_recv.at[stage, batch, n],
                    z_targets[stage],
                )
            )
        return copies

    def give_core(batch):
        start(core_copies(batch))

    def give_far(batch):
        arrive(core_copies(batch))
        for _, tile, cols in items(batch):
            mine = held(tile)
            mine[:, :, :, cols] = mine[:, :, :, cols] + from_core[tile, :, :, :, cols]
        start(far_copies(batch))

    def give_mid(batch):
        arrive(far_copies(batch))
        for kind, tile, cols in items(batch):
            mine = held(tile)
            if kind:
                mine[:, y, :, cols] = mine[:, y, :, cols] + from_far[tile, :, :, cols]
            else:
                mine[x, :, :, cols] = mine[x, :, :, cols] + from_far[tile, :, :, cols]
        start(mid_copies(batch))

    def give_end(batch):
        arrive(mid_copies(batch))
        for _, tile, cols in items(batch):
            mine = held(tile)
            mine[x, y, :, cols] = mine[x, y, :, cols] + from_mid[tile, :, cols]

        @pl.when(is_end)
        def _():
            start(z_copies(batch, 0))

    def give_middle(batch):
        @pl.when(is_middle)
        def _():
            arrive(z_copies(batch, 0))
            for _, tile, cols in items(batch):
                mine = held(tile)
                mine[x, y, :, cols] = mine[x, y, :, cols] + from_end[tile, :, cols]
            start(z_copies(batch, 1))

    def give_total(batch):
        @pl.when(is_middle)
        def _():
            arrive(z_copies(batch, 1))
            for _, tile, cols in items(batch):
                mine = held(tile)
                total[tile, :, cols] = mine[x, y, :, cols] + from_middle[tile, :, cols]
            start(z_copies(batch, 2))

    def take_total(batch):
        @pl.when(is_end)
        def _():
            arrive(z_copies(batch, 2))

    def deliver(third):
        cols = pl.ds(256 * third, 256)
        snap[...] = total[:, :, cols]

        def fill(at, carry):
            value = snap[holds[at]]
            outbox[third, at] = jnp.where(keeps[at] > 0, value, jnp.zeros_like(value))
            return carry

        lax.fori_loop(0, 2 * PLANE, fill, 0)

        def send(hop, carry):
            target = lax.rem(in_plane + hop, PLANE)
            remote(
                outbox.at[third, pl.ds(2 * target, 2)],
                slot_grad.at[:, core, x, y, :, cols],
                out_send.at[third],
                out_recv.at[third],
                z * PLANE + target,
            ).start()
            return carry

        lax.fori_loop(1, PLANE, send, 0)
        keep_copy(third).start()

    def keep_copy(third):
        return pltpu.make_async_copy(
            outbox.at[third, pl.ds(2 * in_plane, 2)],
            slot_grad.at[:, core, x, y, :, pl.ds(256 * third, 256)],
            load_sem.at[5 + third],
        )

    def vec_copies(stage):
        if stage < 3:
            hops = [(stage, (sibling, x_peer, y_peer)[stage])]
        else:
            hops = [
                (2 + hop, lax.rem(z + hop, 4) * PLANE + in_plane) for hop in range(1, 4)
            ]
        return [
            remote(vec_now.at[stage], vec_in.at[at], vec_send.at[at], vec_recv.at[at], device)
            for at, device in hops
        ]

    def vec_next(stage):
        arrive(vec_copies(stage))
        vec_now[stage + 1] = vec_now[stage] + vec_in[stage]
        start(vec_copies(stage + 1))

    def first_load():
        return pltpu.make_async_copy(first_hbm, acc, load_sem.at[3])

    def input_store():
        return pltpu.make_async_copy(acc, input_hbm, load_sem.at[4])

    def w_loads():
        return [pltpu.make_async_copy(w_hbm.at[at], w_buf.at[at], load_sem.at[at]) for at in range(3)]

    def early_loads():
        return [
            pltpu.make_async_copy(hidden_hbm, hidden_then_x, load_sem.at[8]),
            pltpu.make_async_copy(down_hbm, down_then_branch, load_sem.at[9]),
        ]

    def late_loads():
        return [
            pltpu.make_async_copy(x_hbm, hidden_then_x, load_sem.at[8]),
            pltpu.make_async_copy(branch_hbm, down_then_branch, load_sem.at[9]),
        ]

    actions = {
        "core": give_core,
        "far": give_far,
        "mid": give_mid,
        "end": give_end,
        "middle": give_middle,
        "total": give_total,
        "take": take_total,
        "deliver": deliver,
        "sum": vec_next,
    }

    @pl.when(step == 0)
    def _():
        start(early_loads() + w_loads() + [first_load()])
        for at in range(2 * PLANE):
            tile_here, kept = jnp.int32(0), jnp.int32(0)
            for tile in range(TILES):
                place_of = SLOTS * owners[tile] + slot_number(owners, tile)
                match = place_of == z * 2 * PLANE + at
                tile_here = tile_here + jnp.where(match, tile, 0)
                kept = kept + jnp.where(match, 1, 0)
            holds[at] = tile_here
            keeps[at] = kept
        greet(z, in_plane)
        vec_now[0] = late_ref[...]
        for load in early_loads():
            load.wait()

    for at in range(len(BACK_PLAN) - 1):
        if BACK_PLAN[at]:

            @pl.when(step == at)
            def _():
                for name, number in BACK_PLAN[at]:
                    actions[name](number)

    @pl.when(step < 4)
    def _():
        by_up = outer(hidden_then_x[...], up_ref[0]).astype(jnp.bfloat16)
        part[4 + step] = by_up.reshape(2, 2, 2, PIECE, 8 * PIECE)
        by_down = outer(active_ref[0], down_then_branch[...]).astype(jnp.bfloat16)
        part[8 + step] = by_down.reshape(2, 2, 2, PIECE, 8 * PIECE)


    @pl.when(step == 3)
    def _():
        start(late_loads())

    here = pl.ds(pl.multiple_of(block * ROWS, ROWS), ROWS)
    quad_cols = pl.ds(pl.multiple_of(quad * 256, 256), 256)

    def add_sums(at, by_query, by_value):
        vec_now[0, 0:1, at] += by_query
        vec_now[0, 1:2, at] += by_value

    @pl.when(step >= 4)
    def _():
        attend_back_pair(
            2 * quad + pair,
            here,
            p_ref.at[0],
            (q_ref[...], k_ref[...], v_ref[...]),
            ctx_ref,
            grad_ctx_ref,
            pulled,
            pl.ds(pl.multiple_of(pair * 128, 128), 128),
            add_sums,
        )

    @pl.when(step == 4)
    def _():
        for load in w_loads() + [first_load()]:
            load.wait()

    @pl.when((step >= 4) & (pair == 1))
    def _():
        more = acc[here, :]
        for at in range(3):
            more = more + dot_back(pulled[at, here, :], w_buf[at, :, quad_cols])
        acc[here, :] = more

    @pl.when(step == 7)
    def _():
        for load in late_loads():
            load.wait()

    @pl.when((step >= 4) & (block == 1) & (pair == 1))
    def _():
        for tile in range(4):
            if tile < 3:
                value = outer(hidden_then_x[...], pulled[tile])
            else:
                value = outer(ctx_ref[...], down_then_branch[:, quad_cols])
            value = value.astype(jnp.bfloat16).reshape(2, 2, 2, PIECE, 256)
            part[tile, :, :, :, :, quad_cols] = value


    @pl.when(step == 15)
    def _():
        input_store().start()
        start(vec_copies(0))
        for name, number in BACK_PLAN[-1]:
            actions[name](number)
        arrive(vec_copies(3))
        summed = jnp.zeros(vec_out.shape, jnp.float32)
        for origin in range(4):
            hop = lax.rem(z - origin + 4, 4)
            summed = summed + jnp.where(hop == 0, vec_now[3], vec_in[2 + jnp.maximum(hop, 1)])
        vec_out[...] = summed
        for batch in range(7):
            for copy in core_copies(batch) + far_copies(batch) + mid_copies(batch):
                copy.wait_send()

            @pl.when(is_end)
            def _():
                for copy in z_copies(batch, 0):
                    copy.wait_send()

            @pl.when(is_middle)
            def _():
                for copy in z_copies(batch, 1) + z_copies(batch, 2):
                    copy.wait_send()

        for stage in range(4):
            for copy in vec_copies(stage):
                copy.wait_send()
        input_store().wait()
        for third in range(3):
            keep_copy(third).wait()
            most = outbox.at[third, pl.ds(0, 2 * PLANE - 2)]
            pltpu.make_async_copy(most, most, out_recv.at[third]).wait()
            pltpu.make_async_copy(most, most, out_send.at[third]).wait()


def pulled_and_reduced(
    owners,
    probs,
    query,
    keyed,
    valued,
    context,
    grad_context,
    active,
    grad_up,
    x,
    hidden,
    grad_branch,
    grad_down,
    grad_first,
    weights,
    late_sums,
):
    tokens, width = x.shape
    low, high = jnp.bfloat16, jnp.float32
    shaped = jax.ShapeDtypeStruct
    smem = pl.BlockSpec(memory_space=pltpu.SMEM)
    any_space = pl.BlockSpec(memory_space=pl.ANY)
    dma = pltpu.SemaphoreType.DMA

    def at(step):
        inner = jnp.maximum(step - 4, 0)
        return lax.rem(inner, 4) // 2, inner // 4 * 2 + lax.rem(inner, 2)

    pair = pl.BlockSpec((ROWS, 128), at)
    whole = pl.BlockSpec((tokens, width), lambda i: (0, 0), pipeline_mode=pl.Buffered(1))
    tile = pl.BlockSpec((1, tokens, width), lambda i: (jnp.minimum(i, 3), 0, 0))
    sums = pl.BlockSpec((16, width), lambda i: (0, 0))
    cut = (2, 2, 2, PIECE, width)
    input_grad, slot_grads, vector_sums = pl.pallas_call(
        pull_and_reduce,
        grid=(16,),
        out_shape=(
            shaped((tokens, width), high),
            shaped((SLOTS,) + cut, low),
            shaped((16, width), high),
        ),
        in_specs=[smem, pl.BlockSpec((1, 2, ROWS, ROWS), lambda i: (*at(i), 0, 0))]
        + [pair] * 3
        + [whole] * 2
        + [tile] * 2
        + [any_space] * 6
        + [sums],
        out_specs=(any_space, any_space, sums),
        scratch_shapes=[
            pltpu.VMEM((3, width, width), low),
            pltpu.VMEM((tokens, width), high),
            pltpu.VMEM((3, tokens, 256), low),
            pltpu.VMEM((tokens, width), low),
            pltpu.VMEM((tokens, width), low),
            pltpu.VMEM((TILES,) + cut, low),
            pltpu.VMEM((TILES,) + cut[1:], low),
            pltpu.VMEM((TILES,) + cut[2:], low),
            pltpu.VMEM((TILES,) + cut[3:], low),
            pltpu.VMEM((TILES,) + cut[3:], low),
            pltpu.VMEM((TILES,) + cut[3:], low),
            pltpu.VMEM((TILES,) + cut[3:], low),
            pltpu.VMEM((TILES, PIECE, 256), low),
            pltpu.VMEM((3, 2 * PLANE, PIECE, 256), low),
            pltpu.VMEM((4, 16, width), high),
            pltpu.VMEM((6, 16, width), high),
            pltpu.SMEM((2 * PLANE,), jnp.int32),
            pltpu.SMEM((2 * PLANE,), jnp.int32),
            dma((10,)),
            dma((7, 4)),
            dma((7, 4)),
            dma((7, 4)),
            dma((7, 4)),
            dma((7, 4)),
            dma((7, 4)),
            dma((3, 7, 4)),
            dma((3, 7, 4)),
            dma((6,)),
            dma((6,)),
            dma((3,)),
            dma((3,)),
        ],
        compiler_params=pltpu.CompilerParams(
            collective_id=1, has_side_effects=True, vmem_limit_bytes=63 * 2**20
        ),
        name="pull_and_reduce",
    )(
        owners,
        probs,
        query,
        keyed,
        valued,
        context,
        grad_context,
        active,
        grad_up,
        x,
        hidden,
        grad_branch,
        grad_down,
        grad_first,
        weights,
        late_sums,
    )
    return input_grad, slot_grads.reshape(SLOTS, width, width), vector_sums


def collected_tiles(tile_low, owners, slots):
    mine = owners == lax.axis_index("dp")
    local = jnp.where(mine[:, None, None], tile_low[slots], jnp.zeros((), tile_low.dtype))
    return lax.psum(local, "dp")


def summed_over_slice(parts, vector_terms, owners, slots):
    myself = lax.axis_index("dp")

    def add(held, items):
        part, owner, slot = items
        total = lax.psum(part.astype(jnp.float32), "dp")
        here = (owner == myself) & (slot == jnp.arange(SLOTS, dtype=jnp.int32))
        return held + jnp.where(here[:, None, None], total[None], 0.0), None

    empty = jnp.zeros((SLOTS,) + parts.shape[1:], jnp.float32)
    return lax.scan(add, empty, (parts, owners, slots))[0], lax.psum(vector_terms, "dp")


def body(
    inputs,
    cotangent,
    counts,
    lengths,
    owners,
    tile_master,
    tile_first,
    tile_second,
    tile_ema,
    bias_vals,
    gain_vals,
    vector_first,
    vector_second,
    vector_ema,
):
    tokens = inputs.shape[0]
    small = lax.axis_size("dp") == GROUP
    gain_scale = float(tokens * lax.axis_size("dp")) ** (-0.5)
    if small:
        (
            query,
            keyed,
            valued,
            probs,
            context,
            hidden,
            active,
            grad_up,
            grad_down,
            mixed,
            grad_first,
            grad_branch,
            grad_context,
            weights,
            late_sums,
        ) = forwarded_and_pulled(
            counts,
            lengths,
            owners,
            bias_vals,
            gain_vals,
            inputs,
            cotangent,
            tile_master,
        )
        input_grad, slot_grads, full_sums = pulled_and_reduced(
            owners,
            probs,
            query,
            keyed,
            valued,
            context,
            grad_context,
            active,
            grad_up,
            inputs,
            hidden,
            grad_branch,
            grad_down,
            grad_first,
            weights,
            late_sums,
        )
    else:
        slots = tile_slots(owners)
        vectors = jnp.concatenate([bias_vals, gain_vals], 0)
        weights = collected_tiles(tile_master[0].astype(jnp.bfloat16), owners, slots)
        query, keyed, valued, probs, context, hat, inverse = attended(
            counts, lengths, inputs, weights, vectors
        )
        mixed, grad_first, grad_branch, grad_context, up_grads, down_grads, late_sums = fed_forward_both(
            counts, lengths, hat, inverse, cotangent, weights, vectors
        )
        input_grad, early_grads, early_sums = attended_back(
            probs, query, keyed, valued, inputs, context, grad_context, grad_branch, grad_first, weights
        )
        parts = jnp.concatenate([early_grads, up_grads, down_grads], 0)
        slot_grads, full_sums = summed_over_slice(parts, late_sums + early_sums, owners, slots)
    return updated(
        gain_scale,
        slot_grads,
        tile_master,
        tile_first,
        tile_second,
        tile_ema,
        full_sums,
        bias_vals,
        gain_vals,
        vector_first,
        vector_second,
        vector_ema,
        mixed,
        input_grad,
    )


def solution(mesh):
    placed = (
        P("dp", None),
        P("dp", None),
        P("dp", None),
        P("dp", None),
        P(),
        P("dp", None, None, None),
        P("dp", None, None, None),
        P("dp", None, None, None),
        P("dp", None, None, None),
        P(),
        P(),
        P(),
        P(),
        P(),
    )
    return jax.shard_map(
        body,
        mesh=mesh,
        in_specs=placed,
        out_specs=(
            P("dp", None),
            P("dp", None),
            P("dp", None, None, None),
            P("dp", None, None, None),
            P("dp", None, None, None),
            P("dp", None, None, None),
            P("dp", None, None, None),
            P(),
            P(),
            P(),
            P(),
        ),
        check_vma=False,
    )
```

```python
import functools

import jax
import jax.numpy as jnp
from jax import lax
from jax.experimental import pallas as pl
from jax.experimental.pallas import tpu as pltpu
from jax.sharding import PartitionSpec as P

HEADS = 12
BUCKET = 128
SLOTS = 2
TILES = 12
VROWS = 12
STEP = 5

norm_epsilon = 1e-12
tile_rate = 0.03
vector_rate = 0.2
first_decay = 0.5
second_decay = 0.5
adam_epsilon = 1e-08
weight_decay = 0.01
average_rate = 0.9


def tile_slots(owners):
    order = jnp.arange(owners.shape[0], dtype=jnp.int32)
    same = owners[:, None] == owners[None, :]
    earlier = order[None, :] < order[:, None]
    return jnp.sum((same & earlier).astype(jnp.int32), 1)


def adam_update(param, grad, first, second, rate):
    first_new = first_decay * first + (1.0 - first_decay) * grad
    second_new = second_decay * second + (1.0 - second_decay) * grad * grad
    first_hat = first_new / (1.0 - first_decay**STEP)
    second_hat = second_new / (1.0 - second_decay**STEP)
    param_new = param - rate * (
        first_hat / (jnp.sqrt(second_hat) + adam_epsilon) + weight_decay * param
    )
    return (param_new, first_new, second_new)


ROWS = 4 * BUCKET
TAIL_RATE = 0.28
TAIL_SERIES = (
    0.11615256574707405,
    0.06981038475559553,
    0.2631359597579608,
    -0.22983675561378278,
    0.38546775012288165,
    -0.10472989053809521,
)
INV_SQRT_TAU = 0.3989422804014327
ALLOWED = 3.0e38
BARRED = -1000000000.0


def dot(left, right):
    return jnp.dot(left, right, preferred_element_type=jnp.float32)


def dot_back(left, right):
    return lax.dot_general(
        left, right, (((1,), (1,)), ((), ())), preferred_element_type=jnp.float32
    )


def outer(left, right):
    return lax.dot_general(
        left, right, (((0,), (0,)), ((), ())), preferred_element_type=jnp.float32
    )


def passage_facts(counts, lengths, position):
    places = lengths.shape[1]
    big_end = counts[0, 0]
    mid_end = big_end + counts[0, 1]
    all_end = mid_end + counts[0, 2]
    start = jnp.int32(0)
    member = jnp.zeros(position.shape, jnp.int32)
    usable = jnp.zeros(position.shape, jnp.int32)
    for number in range(places):
        size = jnp.where(
            number < big_end,
            4 * BUCKET,
            jnp.where(number < mid_end, 2 * BUCKET, jnp.where(number < all_end, BUCKET, 0)),
        )
        inside = (position >= start) & (position < start + size)
        live = inside & (position < start + lengths[0, number])
        member = jnp.where(inside, number + 1, member)
        usable = jnp.where(live, 1, usable)
        start = start + size
    passage = jnp.where(member > 0, member - 1, places + position // BUCKET)
    return usable, passage


def normalize(values):
    center = jnp.mean(values, -1, keepdims=True)
    centered = values - center
    spread = jnp.mean(centered * centered, -1, keepdims=True)
    inverse = lax.rsqrt(spread + norm_epsilon)
    return centered * inverse, inverse


def normalize_back(grad, hat, inverse):
    center = jnp.mean(grad, -1, keepdims=True)
    along = jnp.mean(grad * hat, -1, keepdims=True)
    return inverse * (grad - center - hat * along)


def columns_total(values):
    return jnp.sum(values, 0, keepdims=True)


def attention_caps(counts, lengths, block):
    at_row = lax.broadcasted_iota(jnp.int32, (ROWS, 1), 0) + block * ROWS
    at_column = lax.broadcasted_iota(jnp.int32, (1, ROWS), 1) + block * ROWS
    _, passage_row = passage_facts(counts, lengths, at_row)
    usable_column, passage_column = passage_facts(counts, lengths, at_column)
    allowed = (passage_row == passage_column) & ((usable_column == 1) | (at_row == at_column))
    return jnp.where(allowed, ALLOWED, BARRED)


def attend_quad(quad, weight, x_ref, vec_ref, cap_ref, q_ref, k_ref, v_ref, p_ref, ctx_ref):
    cols = pl.ds(pl.multiple_of(quad * 256, 256), 256)
    x = x_ref[...]
    query = (dot(x, weight(0, cols)) + vec_ref[0:1, cols]).astype(jnp.bfloat16)
    query = query * jnp.bfloat16(0.125)
    keyed = dot(x, weight(1, cols)).astype(jnp.bfloat16)
    valued = (dot(x, weight(2, cols)) + vec_ref[1:2, cols]).astype(jnp.bfloat16)
    q_ref[...] = query
    k_ref[...] = keyed
    v_ref[...] = valued
    low_half = lax.broadcasted_iota(jnp.int32, (1, 128), 1) < 64
    for pair in range(2):
        part = slice(128 * pair, 128 * pair + 128)
        contexts = []
        for head in range(2):
            here = low_half if head == 0 else ~low_half
            mine = jnp.where(here, query[:, part], jnp.zeros_like(query[:, part]))
            scores = jnp.minimum(dot_back(mine, keyed[:, part]), cap_ref[...])
            exponent = jnp.exp(scores - jnp.max(scores, -1, keepdims=True))
            inverse = 1.0 / jnp.sum(exponent, -1, keepdims=True)
            probability = (exponent * inverse).astype(jnp.bfloat16)
            p_ref[0, 2 * pair + head] = probability
            contexts.append(dot(probability, valued[:, part]))
        both = jnp.where(low_half, contexts[0], contexts[1]).astype(jnp.bfloat16)
        ctx_ref[:, pl.ds(pl.multiple_of(quad * 256 + 128 * pair, 128), 128)] = both


def close_block(w_out, x_ref, vec_ref, ctx_ref, hat_ref, inverse_ref):
    branch = dot(ctx_ref[...], w_out) + vec_ref[2:3, :]
    hat_ref[...], inverse_ref[...] = normalize(x_ref[...].astype(jnp.float32) + branch)


def attend_back_pair(pair, here, p_ref, qkv, ctx_ref, grad_ctx_ref, pulled, half, add_sums):
    low_half = lax.broadcasted_iota(jnp.int32, (1, 128), 1) < 64
    cols = pl.ds(pl.multiple_of(pair * 128, 128), 128)
    query, keyed, valued = qkv
    pull = grad_ctx_ref[here, cols]
    along = pull.astype(jnp.float32) * ctx_ref[here, cols].astype(jnp.float32)
    by_query, by_key, by_value = [], [], []
    for head in range(2):
        mask = low_half if head == 0 else ~low_half
        mine = jnp.where(mask, pull, jnp.zeros_like(pull))
        level = jnp.sum(jnp.where(mask, along, 0.0), -1, keepdims=True)
        probability = p_ref[head]
        grad_prob = dot_back(mine, valued)
        grad_scores = (probability.astype(jnp.float32) * (grad_prob - level)).astype(jnp.bfloat16)
        by_query.append(dot(grad_scores, keyed))
        by_key.append(outer(grad_scores, query))
        by_value.append(outer(probability, pull))
    grad_query = (jnp.where(low_half, by_query[0], by_query[1]) * 0.125).astype(jnp.bfloat16)
    grad_value = jnp.where(low_half, by_value[0], by_value[1]).astype(jnp.bfloat16)
    pulled[0, here, half] = grad_query
    pulled[1, here, half] = jnp.where(low_half, by_key[0], by_key[1]).astype(jnp.bfloat16)
    pulled[2, here, half] = grad_value
    add_sums(cols, columns_total(grad_query.astype(jnp.float32)), columns_total(grad_value.astype(jnp.float32)))


def gelu_parts(up):
    near = 1.0 / (1.0 + TAIL_RATE * jnp.abs(up))
    decay = jnp.exp(up * up * -0.5)
    series = jnp.full_like(near, TAIL_SERIES[-1])
    for term in TAIL_SERIES[-2::-1]:
        series = series * near + term
    tail = series * near * decay
    share = jnp.where(up < 0.0, tail, 1.0 - tail)
    slope = share + up * (decay * INV_SQRT_TAU)
    return (up * share).astype(jnp.bfloat16), slope


def attend_forward(
    counts,
    lengths,
    x_ref,
    w_hbm,
    vec_ref,
    q_ref,
    k_ref,
    v_ref,
    p_ref,
    ctx_ref,
    hat_ref,
    inverse_ref,
    w_buf,
    cap_ref,
    w_sem,
):
    block, quad = pl.program_id(0), pl.program_id(1)
    loads = [pltpu.make_async_copy(w_hbm.at[at], w_buf.at[at], w_sem.at[at]) for at in range(4)]

    @pl.when((block == 0) & (quad == 0))
    def _():
        for load in loads:
            load.start()
        for load in loads:
            load.wait()

    @pl.when(quad == 0)
    def _():
        cap_ref[...] = attention_caps(counts, lengths, block)

    def weight(at, cols):
        return w_buf[at, :, cols]

    attend_quad(quad, weight, x_ref, vec_ref, cap_ref, q_ref, k_ref, v_ref, p_ref, ctx_ref)

    @pl.when(quad == 2)
    def _():
        close_block(w_buf[3], x_ref, vec_ref, ctx_ref, hat_ref, inverse_ref)


def attended(counts, lengths, x, weights, vectors):
    tokens, width = x.shape
    blocks = tokens // ROWS
    low = jnp.bfloat16
    smem = pl.BlockSpec(memory_space=pltpu.SMEM)
    quad = pl.BlockSpec((ROWS, 256), lambda b, h: (b, h))
    rows = pl.BlockSpec((ROWS, width), lambda b, h: (b, 0))
    shaped = jax.ShapeDtypeStruct
    return pl.pallas_call(
        attend_forward,
        grid=(blocks, 3),
        out_shape=(
            shaped((tokens, width), low),
            shaped((tokens, width), low),
            shaped((tokens, width), low),
            shaped((blocks, HEADS, ROWS, ROWS), low),
            shaped((tokens, width), low),
            shaped((tokens, width), jnp.float32),
            shaped((tokens, 1), jnp.float32),
        ),
        in_specs=[
            smem,
            smem,
            rows,
            pl.BlockSpec(memory_space=pl.ANY),
            pl.BlockSpec((VROWS, width), lambda b, h: (0, 0)),
        ],
        out_specs=(
            quad,
            quad,
            quad,
            pl.BlockSpec((1, 4, ROWS, ROWS), lambda b, h: (b, h, 0, 0)),
            rows,
            rows,
            pl.BlockSpec((ROWS, 1), lambda b, h: (b, 0)),
        ),
        scratch_shapes=[
            pltpu.VMEM((4, width, width), low),
            pltpu.VMEM((ROWS, ROWS), jnp.float32),
            pltpu.SemaphoreType.DMA((4,)),
        ],
        compiler_params=pltpu.CompilerParams(vmem_limit_bytes=56 * 2**20),
        name="attend_forward",
    )(counts, lengths, x, weights, vectors)


def feed_forward_both(
    counts,
    lengths,
    hat_ref,
    inverse_ref,
    cot_ref,
    w_hbm,
    vec_ref,
    mixed_ref,
    first_ref,
    branch_ref,
    context_ref,
    up_grad_ref,
    down_grad_ref,
    sum_ref,
    w_buf,
    active_ref,
    up_ref,
    hidden_ref,
    down_ref,
    slope_ref,
    w_sem,
):
    step = pl.program_id(0)
    blocks = pl.num_programs(0) - 4
    loads = [
        pltpu.make_async_copy(w_hbm.at[3 + at], w_buf.at[at], w_sem.at[at]) for at in range(9)
    ]

    @pl.when(step == 0)
    def _():
        for load in loads[1:] + loads[:1]:
            load.start()
        sum_ref[...] = jnp.zeros_like(sum_ref)
        for load in loads[1:] + loads[:1]:
            load.wait()

    @pl.when(step < blocks)
    def _():
        here = pl.ds(pl.multiple_of(step * ROWS, ROWS), ROWS)
        at_row = lax.broadcasted_iota(jnp.int32, (ROWS, 1), 0) + step * ROWS
        live = passage_facts(counts, lengths, at_row)[0].astype(jnp.float32)
        hat = hat_ref[...]
        hidden = hat * vec_ref[10:11, :] + vec_ref[8:9, :]
        hidden_low = hidden.astype(jnp.bfloat16)
        hidden_ref[here, :] = hidden_low
        total = hidden + vec_ref[7:8, :]
        for tile in range(4):
            up = dot(hidden_low, w_buf[1 + tile]) + vec_ref[3 + tile : 4 + tile, :]
            active, slope = gelu_parts(up)
            slope_ref[tile] = slope.astype(jnp.bfloat16)
            active_ref[tile, here, :] = active
            total = total + dot(active, w_buf[5 + tile])
        hat_two, inverse_two = normalize(total)
        mixed_ref[...] = ((hat_two * vec_ref[11:12, :] + vec_ref[9:10, :]) * live).astype(jnp.bfloat16)
        grad_out = cot_ref[...].astype(jnp.float32) * live
        sum_ref[11:12, :] += columns_total(grad_out * hat_two)
        sum_ref[9:10, :] += columns_total(grad_out)
        second = normalize_back(grad_out * vec_ref[11:12, :], hat_two, inverse_two)
        down_low = second.astype(jnp.bfloat16)
        down_ref[here, :] = down_low
        sum_ref[7:8, :] += columns_total(down_low.astype(jnp.float32))
        grad_hidden = second
        for tile in range(4):
            pulled = dot_back(down_low, w_buf[5 + tile])
            up_low = (pulled * slope_ref[tile].astype(jnp.float32)).astype(jnp.bfloat16)
            up_ref[tile, here, :] = up_low
            sum_ref[3 + tile : 4 + tile, :] += columns_total(up_low.astype(jnp.float32))
            grad_hidden = grad_hidden + dot_back(up_low, w_buf[1 + tile])
        sum_ref[10:11, :] += columns_total(grad_hidden * hat)
        sum_ref[8:9, :] += columns_total(grad_hidden)
        grad_first = normalize_back(grad_hidden * vec_ref[10:11, :], hat, inverse_ref[...])
        first_ref[...] = grad_first
        branch_low = grad_first.astype(jnp.bfloat16)
        branch_ref[...] = branch_low
        sum_ref[2:3, :] += columns_total(branch_low.astype(jnp.float32))
        context_ref[...] = dot_back(branch_low, w_buf[0]).astype(jnp.bfloat16)

    @pl.when(step >= blocks)
    def _():
        tile = step - blocks
        up_grad_ref[0] = outer(hidden_ref[...], up_ref[tile]).astype(jnp.bfloat16)
        down_grad_ref[0] = outer(active_ref[tile], down_ref[...]).astype(jnp.bfloat16)


def fed_forward_both(counts, lengths, hat, inverse, cotangent, weights, vectors):
    tokens, width = hat.shape
    blocks = tokens // ROWS
    low = jnp.bfloat16
    smem = pl.BlockSpec(memory_space=pltpu.SMEM)
    shaped = jax.ShapeDtypeStruct

    def block_of(step):
        return jnp.minimum(step, blocks - 1)

    def tile_of(step):
        return jnp.maximum(step - blocks, 0)

    rows = pl.BlockSpec((ROWS, width), lambda i: (block_of(i), 0))
    tile = pl.BlockSpec((1, width, width), lambda i: (tile_of(i), 0, 0))
    return pl.pallas_call(
        feed_forward_both,
        grid=(blocks + 4,),
        out_shape=(
            shaped((tokens, width), low),
            shaped((tokens, width), jnp.float32),
            shaped((tokens, width), low),
            shaped((tokens, width), low),
            shaped((4, width, width), low),
            shaped((4, width, width), low),
            shaped((16, width), jnp.float32),
        ),
        in_specs=[
            smem,
            smem,
            rows,
            pl.BlockSpec((ROWS, 1), lambda i: (block_of(i), 0)),
            rows,
            pl.BlockSpec(memory_space=pl.ANY),
            pl.BlockSpec((VROWS, width), lambda i: (0, 0)),
        ],
        out_specs=(
            rows,
            rows,
            rows,
            rows,
            tile,
            tile,
            pl.BlockSpec((16, width), lambda i: (0, 0)),
        ),
        scratch_shapes=[
            pltpu.VMEM((9, width, width), low),
            pltpu.VMEM((4, tokens, width), low),
            pltpu.VMEM((4, tokens, width), low),
            pltpu.VMEM((tokens, width), low),
            pltpu.VMEM((tokens, width), low),
            pltpu.VMEM((4, ROWS, width), low),
            pltpu.SemaphoreType.DMA((9,)),
        ],
        compiler_params=pltpu.CompilerParams(vmem_limit_bytes=60 * 2**20),
        name="feed_forward_both",
    )(counts, lengths, hat, inverse, cotangent, weights, vectors)


def attend_backward(
    p_ref,
    q_ref,
    k_ref,
    v_ref,
    x_ref,
    ctx_ref,
    grad_ctx_ref,
    branch_ref,
    first_ref,
    w_ref,
    input_ref,
    grad_ref,
    sum_ref,
    pulled,
):
    step = pl.program_id(0)
    quad, block = step // 2, lax.rem(step, 2)
    here = pl.ds(pl.multiple_of(block * ROWS, ROWS), ROWS)
    cols = pl.ds(pl.multiple_of(quad * 256, 256), 256)

    @pl.when(step == 0)
    def _():
        sum_ref[...] = jnp.zeros_like(sum_ref)
        input_ref[...] = first_ref[...]

    def add_sums(at, by_query, by_value):
        sum_ref[0:1, at] += by_query
        sum_ref[1:2, at] += by_value

    for pair in range(2):
        half = slice(128 * pair, 128 * pair + 128)
        qkv = q_ref[:, half], k_ref[:, half], v_ref[:, half]
        heads = p_ref.at[0, pl.ds(2 * pair, 2)]
        attend_back_pair(2 * quad + pair, here, heads, qkv, ctx_ref, grad_ctx_ref, pulled, half, add_sums)
    more = input_ref[here, :]
    for at in range(3):
        more = more + dot_back(pulled[at, here, :], w_ref[at, :, cols])
    input_ref[here, :] = more

    @pl.when(block == 1)
    def _():
        for tile in range(3):
            grad_ref[tile, :, cols] = outer(x_ref[...], pulled[tile]).astype(jnp.bfloat16)
        grad_ref[3, :, cols] = outer(ctx_ref[...], branch_ref[:, cols]).astype(jnp.bfloat16)


def attended_back(probs, query, keyed, valued, x, context, grad_context, grad_branch, grad_first, weights):
    tokens, width = x.shape
    low = jnp.bfloat16
    shaped = jax.ShapeDtypeStruct
    once = pl.Buffered(1)
    quad = pl.BlockSpec((ROWS, 256), lambda i: (lax.rem(i, 2), i // 2))
    whole = pl.BlockSpec((tokens, width), lambda i: (0, 0), pipeline_mode=once)
    return pl.pallas_call(
        attend_backward,
        grid=(6,),
        out_shape=(
            shaped((tokens, width), jnp.float32),
            shaped((4, width, width), low),
            shaped((16, width), jnp.float32),
        ),
        in_specs=[
            pl.BlockSpec((1, 4, ROWS, ROWS), lambda i: (lax.rem(i, 2), i // 2, 0, 0)),
            quad,
            quad,
            quad,
            whole,
            whole,
            whole,
            whole,
            whole,
            pl.BlockSpec((3, width, width), lambda i: (0, 0, 0), pipeline_mode=once),
        ],
        out_specs=(
            whole,
            pl.BlockSpec((4, width, width), lambda i: (0, 0, 0), pipeline_mode=once),
            pl.BlockSpec((16, width), lambda i: (0, 0)),
        ),
        scratch_shapes=[pltpu.VMEM((3, tokens, 256), low)],
        compiler_params=pltpu.CompilerParams(vmem_limit_bytes=56 * 2**20),
        name="attend_backward",
    )(probs, query, keyed, valued, x, context, grad_context, grad_branch, grad_first, weights)


def moved(param, grad, first, second, average, rate):
    param_new, first_new, second_new = adam_update(param, grad, first, second, rate)
    return param_new, first_new, second_new, average_rate * average + (1.0 - average_rate) * param_new


def update_kernel(
    gain_scale,
    grad_ref,
    master_ref,
    first_ref,
    second_ref,
    ema_ref,
    vec_grad_ref,
    bias_ref,
    gain_ref,
    vec_first_ref,
    vec_second_ref,
    vec_ema_ref,
    mixed_in,
    input_in,
    master_out,
    first_out,
    second_out,
    ema_out,
    copy_out,
    vec_out,
    vec_first_out,
    vec_second_out,
    vec_ema_out,
    mixed_out,
    input_out,
    vec_ref,
):
    mixed_out[...] = mixed_in[...]
    input_out[...] = input_in[...]

    @pl.when((pl.program_id(0) == 0) & (pl.program_id(1) == 0))
    def _():
        vec_ref[0:10, :] = bias_ref[...]
        vec_ref[10:12, :] = gain_ref[...]
        vec_grad = vec_grad_ref[0:VROWS, :] * gain_scale
        vec_out[...], vec_first_out[...], vec_second_out[...], vec_ema_out[...] = moved(
            vec_ref[...], vec_grad, vec_first_ref[...], vec_second_ref[...], vec_ema_ref[...], vector_rate
        )

    grad = grad_ref[...].astype(jnp.float32) * gain_scale
    result = moved(master_ref[0], grad, first_ref[0], second_ref[0], ema_ref[0], tile_rate)
    master_out[0], first_out[0], second_out[0], ema_out[0] = result
    copy_out[0] = result[0].astype(jnp.bfloat16)


def updated(
    gain_scale,
    slot_grads,
    master,
    first,
    second,
    ema,
    vec_grad,
    bias,
    gain,
    vec_first,
    vec_second,
    vec_ema,
    mixed,
    input_grad,
):
    width = master.shape[-1]
    chunk = 192
    tile = pl.BlockSpec((1, 1, chunk, width), lambda s, r: (0, s, r, 0))
    steps = width // chunk
    rows = pl.BlockSpec((mixed.shape[0] // (SLOTS * steps), width), lambda s, r: (s * steps + r, 0))

    def whole(value):
        return pl.BlockSpec(value.shape, lambda s, r: (0, 0))

    shaped = jax.ShapeDtypeStruct
    tile_shape = shaped(master.shape, jnp.float32)
    vec_shape = shaped((VROWS, width), jnp.float32)
    results = pl.pallas_call(
        functools.partial(update_kernel, gain_scale),
        grid=(SLOTS, steps),
        out_shape=(tile_shape,) * 4
        + (shaped(master.shape, jnp.bfloat16),)
        + (vec_shape,) * 4
        + (shaped(mixed.shape, mixed.dtype), shaped(input_grad.shape, input_grad.dtype)),
        in_specs=[pl.BlockSpec((1, chunk, width), lambda s, r: (s, r, 0))]
        + [tile] * 4
        + [whole(value) for value in (vec_grad, bias, gain, vec_first, vec_second, vec_ema)]
        + [rows] * 2,
        out_specs=(tile,) * 5 + (whole(vec_first),) * 4 + (rows,) * 2,
        scratch_shapes=[pltpu.VMEM((VROWS, width), jnp.float32)],
        compiler_params=pltpu.CompilerParams(vmem_limit_bytes=62 * 2**20),
        name="update",
    )(
        slot_grads,
        master,
        first,
        second,
        ema,
        vec_grad,
        bias,
        gain,
        vec_first,
        vec_second,
        vec_ema,
        mixed,
        input_grad,
    )
    return results[-2:] + results[:-2]


MESH = pl.DeviceIdType.MESH
GROUP = 32
PAIRS = TILES // 2
PLANE = 8
PIECE = 96
PAIR_TILES = ((0, 1), (2, 3), (4, 8), (5, 9), (6, 10), (7, 11))
EARLY = 2
WHOLE = 3


def remote(src, dst, send, recv, device):
    return pltpu.make_async_remote_copy(
        src_ref=src, dst_ref=dst, send_sem=send, recv_sem=recv, device_id=(device,), device_id_type=MESH
    )


def place(device):
    core = lax.rem(device, 2)
    x = lax.rem(device // 2, 2)
    y = lax.rem(device // 4, 2)
    z = device // 8
    return z, y, x, core


def start(copies):
    for copy in copies:
        copy.start()


def arrive(copies):
    for copy in copies:
        copy.wait_recv()


def greet(z, in_plane):
    barrier = pltpu.get_barrier_semaphore()
    for hop in range(1, PLANE):
        other = z * PLANE + lax.rem(in_plane + hop, PLANE)
        pl.semaphore_signal(barrier, inc=1, device_id=(other,), device_id_type=MESH)
    for hop in range(1, 4):
        other = lax.rem(z + hop, 4) * PLANE + in_plane
        pl.semaphore_signal(barrier, inc=1, device_id=(other,), device_id_type=MESH)
    pl.semaphore_wait(barrier, PLANE + 2)


def along_z(z, in_plane):
    inner = (1 + z // 2) * PLANE + in_plane
    other_middle = (3 - z) * PLANE + in_plane
    outer_end = lax.rem(lax.rem(z + 3, 4) * 3, 4) * PLANE + in_plane
    return inner, other_middle, outer_end


def third(part):
    return slice(None) if part == WHOLE else pl.ds(256 * part, 256)


def slot_number(owners, tile):
    number = jnp.int32(0)
    for earlier in range(tile):
        number = number + jnp.where(owners[earlier] == owners[tile], 1, 0)
    return number


def unit(pair, part):
    return 3 * pair + part if pair < EARLY else 2 * EARLY + pair


UNITS = [(pair, part) for pair in range(EARLY) for part in range(3)]
UNITS += [(pair, WHOLE) for pair in range(EARLY, PAIRS)]

FRONT_PLAN = (
    (
        ("open",),
        ("swap", 0),
        ("sent", 0),
        ("swap", 1),
        ("choose", 0),
        ("end", 0, 0),
        ("caps",),
        ("end", 1, 0),
        ("middle", 0, 0),
        ("sent", 1),
        ("swap", 2),
        ("choose", 1),
        ("end", 0, 1),
        ("middle", 1, 0),
        ("end", 1, 1),
        ("total", 0, 0),
        ("total", 1, 0),
        ("mid", 0, 0),
        ("middle", 0, 1),
        ("choose", 2),
        ("end", 1, 2),
        ("far", 0, 0),
        ("middle", 1, 1),
        ("total", 0, 1),
        ("mid", 1, 0),
        ("end", 4),
        ("mid", 0, 1),
        ("total", 1, 1),
        ("middle", 1, 2),
        ("far", 1, 0),
        ("mid", 1, 1),
        ("middle", 4),
        ("end", 0, 2),
        ("end", 2),
        ("far", 0, 1),
        ("total", 1, 2),
        ("near", 0, 0),
        ("far", 1, 1),
        ("near", 0, 1),
        ("near", 1, 0),
        ("middle", 0, 2),
        ("finish", 0, 1),
        ("total", 4),
        ("near", 1, 1),
        ("finish", 1, 0),
        ("end", 3),
        ("middle", 2),
        ("total", 0, 2),
        ("finish", 0, 0),
    ),
    (
        ("mid", 1, 2),
        ("end", 5),
        ("mid", 0, 2),
        ("middle", 3),
        ("mid", 4),
        ("total", 2),
        ("far", 0, 2),
    ),
    (
        ("finish", 1, 1),
        ("far", 1, 2),
        ("middle", 5),
        ("far", 4),
        ("near", 0, 2),
        ("total", 3),
    ),
    (
        ("mid", 2),
    ),
    (
        ("mid", 3),
        ("far", 2),
        ("finish", 0, 2),
        ("near", 1, 2),
        ("near", 4),
        ("finish", 1, 2),
        ("keep",),
        ("total", 5),
        ("far", 3),
    ),
    (
        ("near", 2),
        ("finish", 4),
        ("mid", 5),
    ),
    (
        ("near", 3),
        ("finish", 2),
        ("far", 5),
    ),
    (
        ("finish", 3),
    ),
    (
        ("near", 5),
    ),
    (
        ("finish", 5),
    ),
)


def forward_and_pull(
    counts,
    lengths,
    owners,
    bias_ref,
    gain_ref,
    x_hbm,
    cot_hbm,
    master_hbm,
    q_ref,
    k_ref,
    v_ref,
    p_ref,
    ctx_hbm,
    hidden_hbm,
    active_hbm,
    up_hbm,
    down_hbm,
    mixed_hbm,
    first_hbm,
    branch_hbm,
    grad_ctx_hbm,
    w_out,
    sum_ref,
    vec_ref,
    cap_ref,
    wide,
    low,
    stage_a,
    stage_b,
    stage_c,
    chosen,
    from_end,
    from_middle,
    w_buf,
    x_then_hidden,
    ctx_then_grad,
    cot_then_down,
    mixed_then_branch,
    hat_ref,
    inverse_ref,
    slope_ref,
    tile_buf,
    load_sem,
    store_sem,
    tile_sem,
    out_sem,
    swap_send,
    swap_recv,
    z_send,
    z_recv,
    mid_send,
    mid_recv,
    far_send,
    far_recv,
    near_send,
    near_recv,
):
    step = pl.program_id(0)
    width = 8 * PIECE
    me = lax.axis_index("dp")
    z, y, x, core = place(me)
    in_plane = lax.rem(me, PLANE)
    sibling = me + 1 - 2 * core
    x_peer = me + 2 - 4 * x
    y_peer = me + 4 - 8 * y
    z_targets = along_z(z, in_plane)
    stages = (stage_a, stage_b, stage_c)
    is_end = (z == 0) | (z == 3)
    is_middle = (z == 1) | (z == 2)

    def piece_rows(cell_core, cell_x, cell_y):
        return pl.ds(pl.multiple_of(((cell_core * 2 + cell_x) * 2 + cell_y) * PIECE, 16), PIECE)

    def swap(part):
        def send(hop, carry):
            target = lax.rem(in_plane + hop, PLANE)
            _, ty, tx, tc = place(target)
            remote(
                low.at[:, piece_rows(tc, tx, ty), third(part)],
                stages[part].at[pl.ds(2 * in_plane, 2)],
                swap_send.at[part],
                swap_recv.at[part],
                z * PLANE + target,
            ).start()
            return carry

        lax.fori_loop(1, PLANE, send, 0)

    def swap_wait(part, sem):
        most = stages[part].at[pl.ds(0, 2 * PLANE - 2)]
        pltpu.make_async_copy(most, most, sem.at[part]).wait()

    def z_copy(pair, part, level):
        two = pl.ds(2 * pair, 2)
        cols = third(part)
        src = w_buf.at[two, core, x, y, :, cols] if level == 2 else chosen.at[two, :, cols]
        dst = (from_end.at[two, :, cols], from_middle.at[two, :, cols], src)[level]
        at = unit(pair, part)
        return remote(src, dst, z_send.at[level, at], z_recv.at[level, at], z_targets[level])

    def z_end(pair, part=WHOLE):
        @pl.when(is_end)
        def _():
            z_copy(pair, part, 0).start()

    def z_middle(pair, part=WHOLE):
        @pl.when(is_middle)
        def _():
            z_copy(pair, part, 0).wait_recv()
            two, cols = pl.ds(2 * pair, 2), third(part)
            chosen[two, :, cols] = chosen[two, :, cols] + from_end[two, :, cols]
            z_copy(pair, part, 1).start()

    def z_total(pair, part=WHOLE):
        @pl.when(is_middle)
        def _():
            z_copy(pair, part, 1).wait_recv()
            two, cols = pl.ds(2 * pair, 2), third(part)
            w_buf[two, core, x, y, :, cols] = chosen[two, :, cols] + from_middle[two, :, cols]
            z_copy(pair, part, 2).start()

    def mid_copies(pair, part):
        copies = []
        for n, peer in enumerate((y_peer, x_peer)):
            spot = w_buf.at[2 * pair + n, core, x, y, :, third(part)]
            at = unit(pair, part), n
            copies.append(remote(spot, spot, mid_send.at[at], mid_recv.at[at], peer))
        return copies

    def halves(pair, part, late):
        row = 1 - x if late else x
        column = 1 - y if late else y
        cols = third(part)
        return w_buf.at[2 * pair, core, row, :, :, cols], w_buf.at[2 * pair + 1, core, :, column, :, cols]

    def far_copies(pair, part):
        copies = []
        for n, peer in enumerate((x_peer, y_peer)):
            spot = halves(pair, part, False)[n]
            at = unit(pair, part), n
            copies.append(remote(spot, spot, far_send.at[at], far_recv.at[at], peer))
        return copies

    def near_copies(pair, part, late):
        copies = []
        for n in range(2):
            spot = halves(pair, part, late)[n]
            at = unit(pair, part), n, late
            copies.append(remote(spot, spot, near_send.at[at], near_recv.at[at], sibling))
        return copies

    def give_mid(pair, part=WHOLE):
        @pl.when(is_end)
        def _():
            z_copy(pair, part, 2).wait_recv()

        start(mid_copies(pair, part))

    def give_far(pair, part=WHOLE):
        arrive(mid_copies(pair, part))
        start(far_copies(pair, part) + near_copies(pair, part, 0))

    def give_near(pair, part=WHOLE):
        arrive(far_copies(pair, part))
        start(near_copies(pair, part, 1))

    def finish(pair, part=WHOLE):
        arrive(near_copies(pair, part, 0) + near_copies(pair, part, 1))

    def choose(part):
        swap_wait(part, swap_recv)
        for pair in range(PAIRS):
            for n, tile in enumerate(PAIR_TILES[pair]):
                owner = owners[tile]
                value = stages[part][SLOTS * lax.rem(owner, PLANE) + slot_number(owners, tile)]
                chosen[2 * pair + n, :, third(part)] = jnp.where(
                    owner // PLANE == z, value, jnp.zeros_like(value)
                )

    def load(at):
        src = (x_hbm, cot_hbm, master_hbm)[at]
        dst = (x_then_hidden, cot_then_down, wide)[at]
        return pltpu.make_async_copy(src, dst, load_sem.at[at])

    def store(at):
        src, dst = (
            (x_then_hidden, hidden_hbm),
            (ctx_then_grad, ctx_hbm),
            (cot_then_down, down_hbm),
            (mixed_then_branch, mixed_hbm),
            (ctx_then_grad, grad_ctx_hbm),
            (mixed_then_branch, branch_hbm),
            (wide, first_hbm),
        )[at]
        src = src.at[pl.ds(0, 2 * ROWS)] if src is wide else src
        return pltpu.make_async_copy(src, dst, store_sem.at[at])

    def w_stores():
        return [
            pltpu.make_async_copy(w_buf.at[tile], w_out.at[tile], out_sem.at[tile]) for tile in range(3)
        ]

    def weight(at, cols=slice(None)):
        value = w_buf[at, :, :, :, :, cols]
        return value.reshape(width, value.shape[-1])

    def open_all():
        for at in range(3):
            load(at).start()
        sum_ref[...] = jnp.zeros_like(sum_ref)
        vec_ref[0:10, :] = bias_ref[...]
        vec_ref[10:12, :] = gain_ref[...]
        greet(z, in_plane)
        load(2).wait()
        for slot in range(SLOTS):
            low[slot] = wide[width * slot : width * (slot + 1), :].astype(jnp.bfloat16)
        for part in range(3):
            stages[part][pl.ds(2 * in_plane, 2)] = low[:, piece_rows(core, x, y), third(part)]

    def make_caps():
        for block in range(2):
            cap_ref[block] = attention_caps(counts, lengths, block)
        load(0).wait()
        load(1).wait()

    actions = {
        "open": open_all,
        "caps": make_caps,
        "swap": swap,
        "sent": lambda part: swap_wait(part, swap_send),
        "choose": choose,
        "end": z_end,
        "middle": z_middle,
        "total": z_total,
        "mid": give_mid,
        "far": give_far,
        "near": give_near,
        "finish": finish,
        "keep": lambda: start(w_stores()),
    }

    for at, work in enumerate(FRONT_PLAN):

        @pl.when(step == at)
        def _():
            for name, *rest in work:
                actions[name](*rest)

    quad, block = step // 2, lax.rem(step, 2)
    here = pl.ds(pl.multiple_of(block * ROWS, ROWS), ROWS)

    @pl.when(step < 6)
    def _():
        attend_quad(
            quad,
            weight,
            x_then_hidden.at[here],
            vec_ref,
            cap_ref.at[block],
            q_ref,
            k_ref,
            v_ref,
            p_ref,
            ctx_then_grad.at[here],
        )

    @pl.when((step >= 4) & (step < 6))
    def _():
        branch = dot(ctx_then_grad[here, :], weight(3)) + vec_ref[2:3, :]
        hat, inverse = normalize(x_then_hidden[here, :].astype(jnp.float32) + branch)
        hat_ref[here, :] = hat
        inverse_ref[here, :] = inverse
        hidden = hat * vec_ref[10:11, :] + vec_ref[8:9, :]
        x_then_hidden[here, :] = hidden.astype(jnp.bfloat16)
        wide[here, :] = hidden + vec_ref[7:8, :]

    @pl.when(step == 5)
    def _():
        start([store(0), store(1)])

    turn = step - 6
    slot = lax.rem(turn, 2)

    def tile_store(source_slot, target):
        return pltpu.make_async_copy(tile_buf.at[source_slot], target, tile_sem.at[source_slot])

    @pl.when(turn >= 2)
    def _():
        tile_store(slot, active_hbm.at[0]).wait()

    @pl.when((step >= 6) & (step < 10))
    def _():
        for half in range(2):
            rows = slice(ROWS * half, ROWS * half + ROWS)
            up = dot(x_then_hidden[rows, :], weight(4 + 2 * turn)) + vec_ref[pl.ds(3 + turn, 1), :]
            active, slope = gelu_parts(up)
            slope_ref[turn, rows, :] = slope.astype(jnp.bfloat16)
            tile_buf[slot, rows, :] = active
            wide[rows, :] = wide[rows, :] + dot(active, weight(5 + 2 * turn))
        tile_store(slot, active_hbm.at[turn]).start()

    @pl.when(step == 10)
    def _():
        for half in range(2):
            rows = slice(ROWS * half, ROWS * half + ROWS)
            at_row = lax.broadcasted_iota(jnp.int32, (ROWS, 1), 0) + half * ROWS
            live = passage_facts(counts, lengths, at_row)[0].astype(jnp.float32)
            hat, inverse = normalize(wide[rows, :])
            mixed = (hat * vec_ref[11:12, :] + vec_ref[9:10, :]) * live
            mixed_then_branch[rows, :] = mixed.astype(jnp.bfloat16)
            grad_out = cot_then_down[rows, :].astype(jnp.float32) * live
            sum_ref[11:12, :] += columns_total(grad_out * hat)
            sum_ref[9:10, :] += columns_total(grad_out)
            second = normalize_back(grad_out * vec_ref[11:12, :], hat, inverse)
            wide[rows, :] = second
            down_low = second.astype(jnp.bfloat16)
            cot_then_down[rows, :] = down_low
            sum_ref[7:8, :] += columns_total(down_low.astype(jnp.float32))
        start([store(2), store(3)])

    @pl.when(step >= 10)
    def _():
        tile = step - 10
        for half in range(2):
            rows = slice(ROWS * half, ROWS * half + ROWS)
            pulled = dot_back(cot_then_down[rows, :], weight(5 + 2 * tile))
            up_low = (pulled * slope_ref[tile, rows, :].astype(jnp.float32)).astype(jnp.bfloat16)
            tile_buf[slot, rows, :] = up_low
            sum_ref[pl.ds(3 + tile, 1), :] += columns_total(up_low.astype(jnp.float32))
            wide[rows, :] = wide[rows, :] + dot_back(up_low, weight(4 + 2 * tile))
        tile_store(slot, up_hbm.at[tile]).start()

    @pl.when(step == 13)
    def _():
        store(1).wait()
        store(3).wait()
        for half in range(2):
            rows = slice(ROWS * half, ROWS * half + ROWS)
            grad_hidden, hat = wide[rows, :], hat_ref[rows, :]
            sum_ref[10:11, :] += columns_total(grad_hidden * hat)
            sum_ref[8:9, :] += columns_total(grad_hidden)
            first = normalize_back(grad_hidden * vec_ref[10:11, :], hat, inverse_ref[rows, :])
            wide[rows, :] = first
            branch_low = first.astype(jnp.bfloat16)
            mixed_then_branch[rows, :] = branch_low
            sum_ref[2:3, :] += columns_total(branch_low.astype(jnp.float32))
            ctx_then_grad[rows, :] = dot_back(branch_low, weight(3)).astype(jnp.bfloat16)
        start([store(4), store(5), store(6)])
        store(0).wait()
        store(2).wait()
        for at in range(2):
            tile_store(at, up_hbm.at[0]).wait()
        for copy in w_stores():
            copy.wait()
        swap_wait(2, swap_send)
        for pair, part in UNITS:
            for copy in mid_copies(pair, part) + far_copies(pair, part):
                copy.wait_send()
            for copy in near_copies(pair, part, 0) + near_copies(pair, part, 1):
                copy.wait_send()

            @pl.when(is_end)
            def _():
                z_copy(pair, part, 0).wait_send()

            @pl.when(is_middle)
            def _():
                z_copy(pair, part, 1).wait_send()
                z_copy(pair, part, 2).wait_send()

        for at in range(4, 7):
            store(at).wait()


def forwarded_and_pulled(counts, lengths, owners, bias, gain, x, cotangent, master):
    tokens, width = x.shape
    blocks = tokens // ROWS
    low, high = jnp.bfloat16, jnp.float32
    smem = pl.BlockSpec(memory_space=pltpu.SMEM)
    any_space = pl.BlockSpec(memory_space=pl.ANY)
    dma = pltpu.SemaphoreType.DMA
    shaped = jax.ShapeDtypeStruct

    def at(step):
        step = jnp.minimum(step, 5)
        return lax.rem(step, 2), step // 2

    quad = pl.BlockSpec((ROWS, 256), at)
    rows = shaped((tokens, width), low)
    cut = (2, 2, 2, PIECE, width)
    units = len(UNITS)
    results = pl.pallas_call(
        forward_and_pull,
        grid=(14,),
        out_shape=(
            rows,
            rows,
            rows,
            shaped((blocks, HEADS, ROWS, ROWS), low),
            rows,
            rows,
            shaped((4, tokens, width), low),
            shaped((4, tokens, width), low),
            rows,
            rows,
            shaped((tokens, width), high),
            rows,
            rows,
            shaped((3,) + cut, low),
            shaped((16, width), high),
        ),
        in_specs=[smem] * 3
        + [pl.BlockSpec(bias.shape, lambda i: (0, 0)), pl.BlockSpec(gain.shape, lambda i: (0, 0))]
        + [any_space] * 3,
        out_specs=(quad, quad, quad, pl.BlockSpec((1, 4, ROWS, ROWS), lambda i: (*at(i), 0, 0)))
        + (any_space,) * 10
        + (pl.BlockSpec((16, width), lambda i: (0, 0)),),
        scratch_shapes=[
            pltpu.VMEM((VROWS, width), high),
            pltpu.VMEM((2, ROWS, ROWS), high),
            pltpu.VMEM((SLOTS * width, width), high),
            pltpu.VMEM((SLOTS, width, width), low),
            pltpu.VMEM((2 * PLANE, PIECE, 256), low),
            pltpu.VMEM((2 * PLANE, PIECE, 256), low),
            pltpu.VMEM((2 * PLANE, PIECE, 256), low),
            pltpu.VMEM((TILES, PIECE, width), low),
            pltpu.VMEM((TILES, PIECE, width), low),
            pltpu.VMEM((TILES, PIECE, width), low),
            pltpu.VMEM((TILES,) + cut, low),
            pltpu.VMEM((tokens, width), low),
            pltpu.VMEM((tokens, width), low),
            pltpu.VMEM((tokens, width), low),
            pltpu.VMEM((tokens, width), low),
            pltpu.VMEM((tokens, width), high),
            pltpu.VMEM((tokens, 1), high),
            pltpu.VMEM((4, tokens, width), low),
            pltpu.VMEM((2, tokens, width), low),
            dma((3,)),
            dma((7,)),
            dma((2,)),
            dma((3,)),
            dma((3,)),
            dma((3,)),
            dma((3, units)),
            dma((3, units)),
            dma((units, 2)),
            dma((units, 2)),
            dma((units, 2)),
            dma((units, 2)),
            dma((units, 2, 2)),
            dma((units, 2, 2)),
        ],
        compiler_params=pltpu.CompilerParams(
            collective_id=0, has_side_effects=True, vmem_limit_bytes=63 * 2**20
        ),
        name="forward_and_pull",
    )(counts, lengths, owners, bias, gain, x, cotangent, master.reshape(SLOTS * width, width))
    w_early = results[13].reshape(3, width, width)
    return results[:13] + (w_early,) + results[14:]


BACK_PLAN = (
    (),
    (
        ("core", 0),
    ),
    (
        ("core", 1),
        ("far", 0),
    ),
    (
        ("core", 2),
        ("far", 1),
    ),
    (),
    (
        ("far", 2),
        ("mid", 0),
    ),
    (
        ("core", 3),
    ),
    (),
    (
        ("mid", 1),
        ("end", 0),
    ),
    (
        ("mid", 2),
        ("core", 4),
        ("far", 3),
        ("middle", 0),
    ),
    (
        ("end", 1),
    ),
    (
        ("middle", 1),
    ),
    (
        ("end", 2),
        ("total", 0),
        ("core", 5),
        ("far", 4),
        ("mid", 3),
    ),
    (
        ("middle", 2),
        ("total", 1),
    ),
    (),
    (
        ("end", 3),
        ("mid", 4),
        ("middle", 3),
        ("far", 5),
        ("total", 2),
    ),
    (
        ("core", 6),
        ("mid", 5),
        ("end", 4),
        ("middle", 4),
        ("total", 3),
        ("take", 0),
        ("sum", 0),
        ("far", 6),
        ("total", 4),
        ("end", 5),
        ("middle", 5),
        ("mid", 6),
        ("take", 1),
        ("sum", 1),
        ("end", 6),
        ("take", 4),
        ("total", 5),
        ("take", 2),
        ("take", 3),
        ("deliver", 0),
        ("sum", 2),
        ("take", 5),
        ("middle", 6),
        ("total", 6),
        ("deliver", 1),
        ("take", 6),
        ("deliver", 2),
    ),
)


def pull_and_reduce(
    owners,
    p_ref,
    q_ref,
    k_ref,
    v_ref,
    ctx_ref,
    grad_ctx_ref,
    active_ref,
    up_ref,
    x_hbm,
    hidden_hbm,
    branch_hbm,
    down_hbm,
    first_hbm,
    w_hbm,
    late_ref,
    input_hbm,
    slot_grad,
    vec_out,
    w_buf,
    acc,
    pulled,
    hidden_then_x,
    down_then_branch,
    part,
    from_core,
    from_far,
    from_mid,
    from_end,
    from_middle,
    total,
    snap,
    outbox,
    vec_now,
    vec_in,
    holds,
    keeps,
    load_sem,
    core_send,
    core_recv,
    far_send,
    far_recv,
    mid_send,
    mid_recv,
    z_send,
    z_recv,
    vec_send,
    vec_recv,
    out_send,
    out_recv,
):
    step = pl.program_id(0)
    inner = jnp.maximum(step - 4, 0)
    quad, block, pair = inner // 4, lax.rem(inner, 4) // 2, lax.rem(inner, 2)
    me = lax.axis_index("dp")
    z, y, x, core = place(me)
    in_plane = lax.rem(me, PLANE)
    sibling = me + 1 - 2 * core
    x_peer = me + 2 - 4 * x
    y_peer = me + 4 - 8 * y
    z_targets = along_z(z, in_plane)
    is_end = (z == 0) | (z == 3)
    is_middle = (z == 1) | (z == 2)

    def items(batch):
        if batch < 4:
            return [(0, 4 + batch, slice(None)), (1, 8 + batch, slice(None))]
        cols = pl.ds(256 * (batch - 4), 256)
        return [(0, 0, cols), (1, 1, cols), (0, 2, cols), (1, 3, cols)]

    def held(tile):
        return part.at[tile, core]

    def core_copies(batch):
        return [
            remote(
                part.at[tile, 1 - core, :, :, :, cols],
                from_core.at[tile, :, :, :, cols],
                core_send.at[batch, n],
                core_recv.at[batch, n],
                sibling,
            )
            for n, (_, tile, cols) in enumerate(items(batch))
        ]

    def far_copies(batch):
        copies = []
        for n, (kind, tile, cols) in enumerate(items(batch)):
            mine = held(tile)
            copies.append(
                remote(
                    mine.at[:, 1 - y, :, cols] if kind else mine.at[1 - x, :, :, cols],
                    from_far.at[tile, :, :, cols],
                    far_send.at[batch, n],
                    far_recv.at[batch, n],
                    y_peer if kind else x_peer,
                )
            )
        return copies

    def mid_copies(batch):
        copies = []
        for n, (kind, tile, cols) in enumerate(items(batch)):
            mine = held(tile)
            copies.append(
                remote(
                    mine.at[1 - x, y, :, cols] if kind else mine.at[x, 1 - y, :, cols],
                    from_mid.at[tile, :, cols],
                    mid_send.at[batch, n],
                    mid_recv.at[batch, n],
                    x_peer if kind else y_peer,
                )
            )
        return copies

    def z_copies(batch, stage):
        copies = []
        for n, (_, tile, cols) in enumerate(items(batch)):
            if stage == 2:
                src, dst = total.at[tile, :, cols], total.at[tile, :, cols]
            else:
                src = held(tile).at[x, y, :, cols]
                dst = (from_middle if stage else from_end).at[tile, :, cols]
            copies.append(
                remote(
                    src,
                    dst,
                    z_send.at[stage, batch, n],
                    z_recv.at[stage, batch, n],
                    z_targets[stage],
                )
            )
        return copies

    def give_core(batch):
        start(core_copies(batch))

    def give_far(batch):
        arrive(core_copies(batch))
        for _, tile, cols in items(batch):
            mine = held(tile)
            mine[:, :, :, cols] = mine[:, :, :, cols] + from_core[tile, :, :, :, cols]
        start(far_copies(batch))

    def give_mid(batch):
        arrive(far_copies(batch))
        for kind, tile, cols in items(batch):
            mine = held(tile)
            if kind:
                mine[:, y, :, cols] = mine[:, y, :, cols] + from_far[tile, :, :, cols]
            else:
                mine[x, :, :, cols] = mine[x, :, :, cols] + from_far[tile, :, :, cols]
        start(mid_copies(batch))

    def give_end(batch):
        arrive(mid_copies(batch))
        for _, tile, cols in items(batch):
            mine = held(tile)
            mine[x, y, :, cols] = mine[x, y, :, cols] + from_mid[tile, :, cols]

        @pl.when(is_end)
        def _():
            start(z_copies(batch, 0))

    def give_middle(batch):
        @pl.when(is_middle)
        def _():
            arrive(z_copies(batch, 0))
            for _, tile, cols in items(batch):
                mine = held(tile)
                mine[x, y, :, cols] = mine[x, y, :, cols] + from_end[tile, :, cols]
            start(z_copies(batch, 1))

    def give_total(batch):
        @pl.when(is_middle)
        def _():
            arrive(z_copies(batch, 1))
            for _, tile, cols in items(batch):
                mine = held(tile)
                total[tile, :, cols] = mine[x, y, :, cols] + from_middle[tile, :, cols]
            start(z_copies(batch, 2))

    def take_total(batch):
        @pl.when(is_end)
        def _():
            arrive(z_copies(batch, 2))

    def deliver(third):
        cols = pl.ds(256 * third, 256)
        snap[...] = total[:, :, cols]

        def fill(at, carry):
            value = snap[holds[at]]
            outbox[third, at] = jnp.where(keeps[at] > 0, value, jnp.zeros_like(value))
            return carry

        lax.fori_loop(0, 2 * PLANE, fill, 0)

        def send(hop, carry):
            target = lax.rem(in_plane + hop, PLANE)
            remote(
                outbox.at[third, pl.ds(2 * target, 2)],
                slot_grad.at[:, core, x, y, :, cols],
                out_send.at[third],
                out_recv.at[third],
                z * PLANE + target,
            ).start()
            return carry

        lax.fori_loop(1, PLANE, send, 0)
        keep_copy(third).start()

    def keep_copy(third):
        return pltpu.make_async_copy(
            outbox.at[third, pl.ds(2 * in_plane, 2)],
            slot_grad.at[:, core, x, y, :, pl.ds(256 * third, 256)],
            load_sem.at[5 + third],
        )

    def vec_copies(stage):
        if stage < 3:
            hops = [(stage, (sibling, x_peer, y_peer)[stage])]
        else:
            hops = [
                (2 + hop, lax.rem(z + hop, 4) * PLANE + in_plane) for hop in range(1, 4)
            ]
        return [
            remote(vec_now.at[stage], vec_in.at[at], vec_send.at[at], vec_recv.at[at], device)
            for at, device in hops
        ]

    def vec_next(stage):
        arrive(vec_copies(stage))
        vec_now[stage + 1] = vec_now[stage] + vec_in[stage]
        start(vec_copies(stage + 1))

    def first_load():
        return pltpu.make_async_copy(first_hbm, acc, load_sem.at[3])

    def input_store():
        return pltpu.make_async_copy(acc, input_hbm, load_sem.at[4])

    def w_loads():
        return [pltpu.make_async_copy(w_hbm.at[at], w_buf.at[at], load_sem.at[at]) for at in range(3)]

    def early_loads():
        return [
            pltpu.make_async_copy(hidden_hbm, hidden_then_x, load_sem.at[8]),
            pltpu.make_async_copy(down_hbm, down_then_branch, load_sem.at[9]),
        ]

    def late_loads():
        return [
            pltpu.make_async_copy(x_hbm, hidden_then_x, load_sem.at[8]),
            pltpu.make_async_copy(branch_hbm, down_then_branch, load_sem.at[9]),
        ]

    actions = {
        "core": give_core,
        "far": give_far,
        "mid": give_mid,
        "end": give_end,
        "middle": give_middle,
        "total": give_total,
        "take": take_total,
        "deliver": deliver,
        "sum": vec_next,
    }

    @pl.when(step == 0)
    def _():
        start(early_loads() + w_loads() + [first_load()])
        for at in range(2 * PLANE):
            tile_here, kept = jnp.int32(0), jnp.int32(0)
            for tile in range(TILES):
                place_of = SLOTS * owners[tile] + slot_number(owners, tile)
                match = place_of == z * 2 * PLANE + at
                tile_here = tile_here + jnp.where(match, tile, 0)
                kept = kept + jnp.where(match, 1, 0)
            holds[at] = tile_here
            keeps[at] = kept
        greet(z, in_plane)
        vec_now[0] = late_ref[...]
        for load in early_loads():
            load.wait()

    for at in range(len(BACK_PLAN) - 1):
        if BACK_PLAN[at]:

            @pl.when(step == at)
            def _():
                for name, number in BACK_PLAN[at]:
                    actions[name](number)

    @pl.when(step < 4)
    def _():
        by_up = outer(hidden_then_x[...], up_ref[0]).astype(jnp.bfloat16)
        part[4 + step] = by_up.reshape(2, 2, 2, PIECE, 8 * PIECE)
        by_down = outer(active_ref[0], down_then_branch[...]).astype(jnp.bfloat16)
        part[8 + step] = by_down.reshape(2, 2, 2, PIECE, 8 * PIECE)


    @pl.when(step == 3)
    def _():
        start(late_loads())

    here = pl.ds(pl.multiple_of(block * ROWS, ROWS), ROWS)
    quad_cols = pl.ds(pl.multiple_of(quad * 256, 256), 256)

    def add_sums(at, by_query, by_value):
        vec_now[0, 0:1, at] += by_query
        vec_now[0, 1:2, at] += by_value

    @pl.when(step >= 4)
    def _():
        attend_back_pair(
            2 * quad + pair,
            here,
            p_ref.at[0],
            (q_ref[...], k_ref[...], v_ref[...]),
            ctx_ref,
            grad_ctx_ref,
            pulled,
            pl.ds(pl.multiple_of(pair * 128, 128), 128),
            add_sums,
        )

    @pl.when(step == 4)
    def _():
        for load in w_loads() + [first_load()]:
            load.wait()

    @pl.when((step >= 4) & (pair == 1))
    def _():
        more = acc[here, :]
        for at in range(3):
            more = more + dot_back(pulled[at, here, :], w_buf[at, :, quad_cols])
        acc[here, :] = more

    @pl.when(step == 7)
    def _():
        for load in late_loads():
            load.wait()

    @pl.when((step >= 4) & (block == 1) & (pair == 1))
    def _():
        for tile in range(4):
            if tile < 3:
                value = outer(hidden_then_x[...], pulled[tile])
            else:
                value = outer(ctx_ref[...], down_then_branch[:, quad_cols])
            value = value.astype(jnp.bfloat16).reshape(2, 2, 2, PIECE, 256)
            part[tile, :, :, :, :, quad_cols] = value


    @pl.when(step == 15)
    def _():
        input_store().start()
        start(vec_copies(0))
        for name, number in BACK_PLAN[-1]:
            actions[name](number)
        arrive(vec_copies(3))
        summed = jnp.zeros(vec_out.shape, jnp.float32)
        for origin in range(4):
            hop = lax.rem(z - origin + 4, 4)
            summed = summed + jnp.where(hop == 0, vec_now[3], vec_in[2 + jnp.maximum(hop, 1)])
        vec_out[...] = summed
        for batch in range(7):
            for copy in core_copies(batch) + far_copies(batch) + mid_copies(batch):
                copy.wait_send()

            @pl.when(is_end)
            def _():
                for copy in z_copies(batch, 0):
                    copy.wait_send()

            @pl.when(is_middle)
            def _():
                for copy in z_copies(batch, 1) + z_copies(batch, 2):
                    copy.wait_send()

        for stage in range(4):
            for copy in vec_copies(stage):
                copy.wait_send()
        input_store().wait()
        for third in range(3):
            keep_copy(third).wait()
            most = outbox.at[third, pl.ds(0, 2 * PLANE - 2)]
            pltpu.make_async_copy(most, most, out_recv.at[third]).wait()
            pltpu.make_async_copy(most, most, out_send.at[third]).wait()


def pulled_and_reduced(
    owners,
    probs,
    query,
    keyed,
    valued,
    context,
    grad_context,
    active,
    grad_up,
    x,
    hidden,
    grad_branch,
    grad_down,
    grad_first,
    weights,
    late_sums,
):
    tokens, width = x.shape
    low, high = jnp.bfloat16, jnp.float32
    shaped = jax.ShapeDtypeStruct
    smem = pl.BlockSpec(memory_space=pltpu.SMEM)
    any_space = pl.BlockSpec(memory_space=pl.ANY)
    dma = pltpu.SemaphoreType.DMA

    def at(step):
        inner = jnp.maximum(step - 4, 0)
        return lax.rem(inner, 4) // 2, inner // 4 * 2 + lax.rem(inner, 2)

    pair = pl.BlockSpec((ROWS, 128), at)
    whole = pl.BlockSpec((tokens, width), lambda i: (0, 0), pipeline_mode=pl.Buffered(1))
    tile = pl.BlockSpec((1, tokens, width), lambda i: (jnp.minimum(i, 3), 0, 0))
    sums = pl.BlockSpec((16, width), lambda i: (0, 0))
    cut = (2, 2, 2, PIECE, width)
    input_grad, slot_grads, vector_sums = pl.pallas_call(
        pull_and_reduce,
        grid=(16,),
        out_shape=(
            shaped((tokens, width), high),
            shaped((SLOTS,) + cut, low),
            shaped((16, width), high),
        ),
        in_specs=[smem, pl.BlockSpec((1, 2, ROWS, ROWS), lambda i: (*at(i), 0, 0))]
        + [pair] * 3
        + [whole] * 2
        + [tile] * 2
        + [any_space] * 6
        + [sums],
        out_specs=(any_space, any_space, sums),
        scratch_shapes=[
            pltpu.VMEM((3, width, width), low),
            pltpu.VMEM((tokens, width), high),
            pltpu.VMEM((3, tokens, 256), low),
            pltpu.VMEM((tokens, width), low),
            pltpu.VMEM((tokens, width), low),
            pltpu.VMEM((TILES,) + cut, low),
            pltpu.VMEM((TILES,) + cut[1:], low),
            pltpu.VMEM((TILES,) + cut[2:], low),
            pltpu.VMEM((TILES,) + cut[3:], low),
            pltpu.VMEM((TILES,) + cut[3:], low),
            pltpu.VMEM((TILES,) + cut[3:], low),
            pltpu.VMEM((TILES,) + cut[3:], low),
            pltpu.VMEM((TILES, PIECE, 256), low),
            pltpu.VMEM((3, 2 * PLANE, PIECE, 256), low),
            pltpu.VMEM((4, 16, width), high),
            pltpu.VMEM((6, 16, width), high),
            pltpu.SMEM((2 * PLANE,), jnp.int32),
            pltpu.SMEM((2 * PLANE,), jnp.int32),
            dma((10,)),
            dma((7, 4)),
            dma((7, 4)),
            dma((7, 4)),
            dma((7, 4)),
            dma((7, 4)),
            dma((7, 4)),
            dma((3, 7, 4)),
            dma((3, 7, 4)),
            dma((6,)),
            dma((6,)),
            dma((3,)),
            dma((3,)),
        ],
        compiler_params=pltpu.CompilerParams(
            collective_id=1, has_side_effects=True, vmem_limit_bytes=63 * 2**20
        ),
        name="pull_and_reduce",
    )(
        owners,
        probs,
        query,
        keyed,
        valued,
        context,
        grad_context,
        active,
        grad_up,
        x,
        hidden,
        grad_branch,
        grad_down,
        grad_first,
        weights,
        late_sums,
    )
    return input_grad, slot_grads.reshape(SLOTS, width, width), vector_sums


def collected_tiles(tile_low, owners, slots):
    mine = owners == lax.axis_index("dp")
    local = jnp.where(mine[:, None, None], tile_low[slots], jnp.zeros((), tile_low.dtype))
    return lax.psum(local, "dp")


def summed_over_slice(parts, vector_terms, owners, slots):
    myself = lax.axis_index("dp")

    def add(held, items):
        part, owner, slot = items
        total = lax.psum(part.astype(jnp.float32), "dp")
        here = (owner == myself) & (slot == jnp.arange(SLOTS, dtype=jnp.int32))
        return held + jnp.where(here[:, None, None], total[None], 0.0), None

    empty = jnp.zeros((SLOTS,) + parts.shape[1:], jnp.float32)
    return lax.scan(add, empty, (parts, owners, slots))[0], lax.psum(vector_terms, "dp")


def body(
    inputs,
    cotangent,
    counts,
    lengths,
    owners,
    tile_master,
    tile_first,
    tile_second,
    tile_ema,
    bias_vals,
    gain_vals,
    vector_first,
    vector_second,
    vector_ema,
):
    tokens = inputs.shape[0]
    small = lax.axis_size("dp") == GROUP
    gain_scale = float(tokens * lax.axis_size("dp")) ** (-0.5)
    if small:
        (
            query,
            keyed,
            valued,
            probs,
            context,
            hidden,
            active,
            grad_up,
            grad_down,
            mixed,
            grad_first,
            grad_branch,
            grad_context,
            weights,
            late_sums,
        ) = forwarded_and_pulled(
            counts,
            lengths,
            owners,
            bias_vals,
            gain_vals,
            inputs,
            cotangent,
            tile_master,
        )
        input_grad, slot_grads, full_sums = pulled_and_reduced(
            owners,
            probs,
            query,
            keyed,
            valued,
            context,
            grad_context,
            active,
            grad_up,
            inputs,
            hidden,
            grad_branch,
            grad_down,
            grad_first,
            weights,
            late_sums,
        )
    else:
        slots = tile_slots(owners)
        vectors = jnp.concatenate([bias_vals, gain_vals], 0)
        weights = collected_tiles(tile_master[0].astype(jnp.bfloat16), owners, slots)
        query, keyed, valued, probs, context, hat, inverse = attended(
            counts, lengths, inputs, weights, vectors
        )
        mixed, grad_first, grad_branch, grad_context, up_grads, down_grads, late_sums = fed_forward_both(
            counts, lengths, hat, inverse, cotangent, weights, vectors
        )
        input_grad, early_grads, early_sums = attended_back(
            probs, query, keyed, valued, inputs, context, grad_context, grad_branch, grad_first, weights
        )
        parts = jnp.concatenate([early_grads, up_grads, down_grads], 0)
        slot_grads, full_sums = summed_over_slice(parts, late_sums + early_sums, owners, slots)
    return updated(
        gain_scale,
        slot_grads,
        tile_master,
        tile_first,
        tile_second,
        tile_ema,
        full_sums,
        bias_vals,
        gain_vals,
        vector_first,
        vector_second,
        vector_ema,
        mixed,
        input_grad,
    )


def solution(mesh):
    placed = (
        P("dp", None),
        P("dp", None),
        P("dp", None),
        P("dp", None),
        P(),
        P("dp", None, None, None),
        P("dp", None, None, None),
        P("dp", None, None, None),
        P("dp", None, None, None),
        P(),
        P(),
        P(),
        P(),
        P(),
    )
    return jax.shard_map(
        body,
        mesh=mesh,
        in_specs=placed,
        out_specs=(
            P("dp", None),
            P("dp", None),
            P("dp", None, None, None),
            P("dp", None, None, None),
            P("dp", None, None, None),
            P("dp", None, None, None),
            P("dp", None, None, None),
            P(),
            P(),
            P(),
            P(),
        ),
        check_vma=False,
    )
```

```python
import functools

import jax
import jax.numpy as jnp
from jax import lax
from jax.experimental import pallas as pl
from jax.experimental.pallas import tpu as pltpu
from jax.sharding import PartitionSpec as P

HEADS = 12
BUCKET = 128
SLOTS = 2
TILES = 12
VROWS = 12
STEP = 5

norm_epsilon = 1e-12
tile_rate = 0.03
vector_rate = 0.2
first_decay = 0.5
second_decay = 0.5
adam_epsilon = 1e-08
weight_decay = 0.01
average_rate = 0.9


def tile_slots(owners):
    order = jnp.arange(owners.shape[0], dtype=jnp.int32)
    same = owners[:, None] == owners[None, :]
    earlier = order[None, :] < order[:, None]
    return jnp.sum((same & earlier).astype(jnp.int32), 1)


def adam_update(param, grad, first, second, rate):
    first_new = first_decay * first + (1.0 - first_decay) * grad
    second_new = second_decay * second + (1.0 - second_decay) * grad * grad
    first_hat = first_new / (1.0 - first_decay**STEP)
    second_hat = second_new / (1.0 - second_decay**STEP)
    param_new = param - rate * (
        first_hat / (jnp.sqrt(second_hat) + adam_epsilon) + weight_decay * param
    )
    return (param_new, first_new, second_new)


ROWS = 4 * BUCKET
TAIL_RATE = 0.28
TAIL_SERIES = (
    0.11615256574707405,
    0.06981038475559553,
    0.2631359597579608,
    -0.22983675561378278,
    0.38546775012288165,
    -0.10472989053809521,
)
INV_SQRT_TAU = 0.3989422804014327
ALLOWED = 3.0e38
BARRED = -1000000000.0


def dot(left, right):
    return jnp.dot(left, right, preferred_element_type=jnp.float32)


def dot_back(left, right):
    return lax.dot_general(
        left, right, (((1,), (1,)), ((), ())), preferred_element_type=jnp.float32
    )


def outer(left, right):
    return lax.dot_general(
        left, right, (((0,), (0,)), ((), ())), preferred_element_type=jnp.float32
    )


def strips(total, count):
    return [slice(at, at + count) for at in range(0, total, count)]


def passage_facts(counts, lengths, position):
    places = lengths.shape[1]
    big_end = counts[0, 0]
    mid_end = big_end + counts[0, 1]
    all_end = mid_end + counts[0, 2]
    start = jnp.int32(0)
    member = jnp.zeros(position.shape, jnp.int32)
    usable = jnp.zeros(position.shape, jnp.int32)
    for number in range(places):
        size = jnp.where(
            number < big_end,
            4 * BUCKET,
            jnp.where(number < mid_end, 2 * BUCKET, jnp.where(number < all_end, BUCKET, 0)),
        )
        inside = (position >= start) & (position < start + size)
        live = inside & (position < start + lengths[0, number])
        member = jnp.where(inside, number + 1, member)
        usable = jnp.where(live, 1, usable)
        start = start + size
    passage = jnp.where(member > 0, member - 1, places + position // BUCKET)
    return usable, passage


def normalize(values):
    center = jnp.mean(values, -1, keepdims=True)
    centered = values - center
    spread = jnp.mean(centered * centered, -1, keepdims=True)
    inverse = lax.rsqrt(spread + norm_epsilon)
    return centered * inverse, inverse


def normalize_back(grad, hat, inverse):
    center = jnp.mean(grad, -1, keepdims=True)
    along = jnp.mean(grad * hat, -1, keepdims=True)
    return inverse * (grad - center - hat * along)


def columns_total(values):
    return jnp.sum(values, 0, keepdims=True)


def attention_caps(counts, lengths, block):
    at_row = lax.broadcasted_iota(jnp.int32, (ROWS, 1), 0) + block * ROWS
    at_column = lax.broadcasted_iota(jnp.int32, (1, ROWS), 1) + block * ROWS
    _, passage_row = passage_facts(counts, lengths, at_row)
    usable_column, passage_column = passage_facts(counts, lengths, at_column)
    allowed = (passage_row == passage_column) & ((usable_column == 1) | (at_row == at_column))
    return jnp.where(allowed, ALLOWED, BARRED)


def attend_quad(quad, weight, x_ref, vec_ref, cap_ref, q_ref, k_ref, v_ref, p_ref, ctx_ref):
    cols = pl.ds(pl.multiple_of(quad * 256, 256), 256)
    x = x_ref[...]
    query = (dot(x, weight(0, cols)) + vec_ref[0:1, cols]).astype(jnp.bfloat16)
    query = query * jnp.bfloat16(0.125)
    keyed = dot(x, weight(1, cols)).astype(jnp.bfloat16)
    valued = (dot(x, weight(2, cols)) + vec_ref[1:2, cols]).astype(jnp.bfloat16)
    q_ref[...] = query
    k_ref[...] = keyed
    v_ref[...] = valued
    low_half = lax.broadcasted_iota(jnp.int32, (1, 128), 1) < 64
    for pair in range(2):
        part = slice(128 * pair, 128 * pair + 128)
        contexts = []
        for head in range(2):
            here = low_half if head == 0 else ~low_half
            mine = jnp.where(here, query[:, part], jnp.zeros_like(query[:, part]))
            scores = dot_back(mine, keyed[:, part])
            for rows in strips(ROWS, 64):
                capped = jnp.minimum(scores[rows], cap_ref[rows, :])
                exponent = jnp.exp(capped - jnp.max(capped, -1, keepdims=True))
                inverse = 1.0 / jnp.sum(exponent, -1, keepdims=True)
                p_ref[0, 2 * pair + head, rows, :] = (exponent * inverse).astype(jnp.bfloat16)
            contexts.append(dot(p_ref[0, 2 * pair + head], valued[:, part]))
        both = jnp.where(low_half, contexts[0], contexts[1]).astype(jnp.bfloat16)
        ctx_ref[:, pl.ds(pl.multiple_of(quad * 256 + 128 * pair, 128), 128)] = both


def close_block(w_out, x_ref, vec_ref, ctx_ref, hat_ref, inverse_ref):
    branch = dot(ctx_ref[...], w_out) + vec_ref[2:3, :]
    hat_ref[...], inverse_ref[...] = normalize(x_ref[...].astype(jnp.float32) + branch)


def attend_back_pair(pair, here, p_ref, qkv, ctx_ref, grad_ctx_ref, scores_ref, pulled, half, add_sums):
    low_half = lax.broadcasted_iota(jnp.int32, (1, 128), 1) < 64
    cols = pl.ds(pl.multiple_of(pair * 128, 128), 128)
    query, keyed, valued = qkv
    pull = grad_ctx_ref[here, cols]
    along = pull.astype(jnp.float32) * ctx_ref[here, cols].astype(jnp.float32)
    by_query, by_key, by_value = [], [], []
    for head in range(2):
        mask = low_half if head == 0 else ~low_half
        mine = jnp.where(mask, pull, jnp.zeros_like(pull))
        level = jnp.sum(jnp.where(mask, along, 0.0), -1, keepdims=True)
        grad_prob = dot_back(mine, valued)
        for rows in strips(ROWS, 64):
            weighted = p_ref[head, rows, :].astype(jnp.float32) * (grad_prob[rows] - level[rows])
            scores_ref[head, rows, :] = weighted.astype(jnp.bfloat16)
        by_query.append(dot(scores_ref[head], keyed))
        by_key.append(outer(scores_ref[head], query))
        by_value.append(outer(p_ref[head], pull))
    grad_query = (jnp.where(low_half, by_query[0], by_query[1]) * 0.125).astype(jnp.bfloat16)
    grad_value = jnp.where(low_half, by_value[0], by_value[1]).astype(jnp.bfloat16)
    pulled[0, here, half] = grad_query
    pulled[1, here, half] = jnp.where(low_half, by_key[0], by_key[1]).astype(jnp.bfloat16)
    pulled[2, here, half] = grad_value
    add_sums(cols, columns_total(grad_query.astype(jnp.float32)), columns_total(grad_value.astype(jnp.float32)))


def gelu_parts(up):
    near = 1.0 / (1.0 + TAIL_RATE * jnp.abs(up))
    decay = jnp.exp(up * up * -0.5)
    series = jnp.full_like(near, TAIL_SERIES[-1])
    for term in TAIL_SERIES[-2::-1]:
        series = series * near + term
    tail = series * near * decay
    share = jnp.where(up < 0.0, tail, 1.0 - tail)
    slope = share + up * (decay * INV_SQRT_TAU)
    return (up * share).astype(jnp.bfloat16), slope


def attend_forward(
    counts,
    lengths,
    x_ref,
    w_hbm,
    vec_ref,
    q_ref,
    k_ref,
    v_ref,
    p_ref,
    ctx_ref,
    hat_ref,
    inverse_ref,
    w_buf,
    cap_ref,
    w_sem,
):
    block, quad = pl.program_id(0), pl.program_id(1)
    loads = [pltpu.make_async_copy(w_hbm.at[at], w_buf.at[at], w_sem.at[at]) for at in range(4)]

    @pl.when((block == 0) & (quad == 0))
    def _():
        for load in loads:
            load.start()
        for load in loads:
            load.wait()

    @pl.when(quad == 0)
    def _():
        cap_ref[...] = attention_caps(counts, lengths, block)

    def weight(at, cols):
        return w_buf[at, :, cols]

    attend_quad(quad, weight, x_ref, vec_ref, cap_ref, q_ref, k_ref, v_ref, p_ref, ctx_ref)

    @pl.when(quad == 2)
    def _():
        close_block(w_buf[3], x_ref, vec_ref, ctx_ref, hat_ref, inverse_ref)


def attended(counts, lengths, x, weights, vectors):
    tokens, width = x.shape
    blocks = tokens // ROWS
    low = jnp.bfloat16
    smem = pl.BlockSpec(memory_space=pltpu.SMEM)
    quad = pl.BlockSpec((ROWS, 256), lambda b, h: (b, h))
    rows = pl.BlockSpec((ROWS, width), lambda b, h: (b, 0))
    shaped = jax.ShapeDtypeStruct
    return pl.pallas_call(
        attend_forward,
        grid=(blocks, 3),
        out_shape=(
            shaped((tokens, width), low),
            shaped((tokens, width), low),
            shaped((tokens, width), low),
            shaped((blocks, HEADS, ROWS, ROWS), low),
            shaped((tokens, width), low),
            shaped((tokens, width), jnp.float32),
            shaped((tokens, 1), jnp.float32),
        ),
        in_specs=[
            smem,
            smem,
            rows,
            pl.BlockSpec(memory_space=pl.ANY),
            pl.BlockSpec((VROWS, width), lambda b, h: (0, 0)),
        ],
        out_specs=(
            quad,
            quad,
            quad,
            pl.BlockSpec((1, 4, ROWS, ROWS), lambda b, h: (b, h, 0, 0)),
            rows,
            rows,
            pl.BlockSpec((ROWS, 1), lambda b, h: (b, 0)),
        ),
        scratch_shapes=[
            pltpu.VMEM((4, width, width), low),
            pltpu.VMEM((ROWS, ROWS), jnp.float32),
            pltpu.SemaphoreType.DMA((4,)),
        ],
        compiler_params=pltpu.CompilerParams(vmem_limit_bytes=56 * 2**20),
        name="attend_forward",
    )(counts, lengths, x, weights, vectors)


def feed_forward_both(
    counts,
    lengths,
    hat_ref,
    inverse_ref,
    cot_ref,
    w_hbm,
    vec_ref,
    mixed_ref,
    first_ref,
    branch_ref,
    context_ref,
    up_grad_ref,
    down_grad_ref,
    sum_ref,
    w_buf,
    active_ref,
    up_ref,
    hidden_ref,
    down_ref,
    slope_ref,
    w_sem,
):
    step = pl.program_id(0)
    blocks = pl.num_programs(0) - 4
    loads = [
        pltpu.make_async_copy(w_hbm.at[3 + at], w_buf.at[at], w_sem.at[at]) for at in range(9)
    ]

    @pl.when(step == 0)
    def _():
        for load in loads[1:] + loads[:1]:
            load.start()
        sum_ref[...] = jnp.zeros_like(sum_ref)
        for load in loads[1:] + loads[:1]:
            load.wait()

    @pl.when(step < blocks)
    def _():
        here = pl.ds(pl.multiple_of(step * ROWS, ROWS), ROWS)
        at_row = lax.broadcasted_iota(jnp.int32, (ROWS, 1), 0) + step * ROWS
        live = passage_facts(counts, lengths, at_row)[0].astype(jnp.float32)
        hat = hat_ref[...]
        hidden = hat * vec_ref[10:11, :] + vec_ref[8:9, :]
        hidden_low = hidden.astype(jnp.bfloat16)
        hidden_ref[here, :] = hidden_low
        total = hidden + vec_ref[7:8, :]
        for tile in range(4):
            up = dot(hidden_low, w_buf[1 + tile]) + vec_ref[3 + tile : 4 + tile, :]
            active, slope = gelu_parts(up)
            slope_ref[tile] = slope.astype(jnp.bfloat16)
            active_ref[tile, here, :] = active
            total = total + dot(active, w_buf[5 + tile])
        hat_two, inverse_two = normalize(total)
        mixed_ref[...] = ((hat_two * vec_ref[11:12, :] + vec_ref[9:10, :]) * live).astype(jnp.bfloat16)
        grad_out = cot_ref[...].astype(jnp.float32) * live
        sum_ref[11:12, :] += columns_total(grad_out * hat_two)
        sum_ref[9:10, :] += columns_total(grad_out)
        second = normalize_back(grad_out * vec_ref[11:12, :], hat_two, inverse_two)
        down_low = second.astype(jnp.bfloat16)
        down_ref[here, :] = down_low
        sum_ref[7:8, :] += columns_total(down_low.astype(jnp.float32))
        grad_hidden = second
        for tile in range(4):
            pulled = dot_back(down_low, w_buf[5 + tile])
            up_low = (pulled * slope_ref[tile].astype(jnp.float32)).astype(jnp.bfloat16)
            up_ref[tile, here, :] = up_low
            sum_ref[3 + tile : 4 + tile, :] += columns_total(up_low.astype(jnp.float32))
            grad_hidden = grad_hidden + dot_back(up_low, w_buf[1 + tile])
        sum_ref[10:11, :] += columns_total(grad_hidden * hat)
        sum_ref[8:9, :] += columns_total(grad_hidden)
        grad_first = normalize_back(grad_hidden * vec_ref[10:11, :], hat, inverse_ref[...])
        first_ref[...] = grad_first
        branch_low = grad_first.astype(jnp.bfloat16)
        branch_ref[...] = branch_low
        sum_ref[2:3, :] += columns_total(branch_low.astype(jnp.float32))
        context_ref[...] = dot_back(branch_low, w_buf[0]).astype(jnp.bfloat16)

    @pl.when(step >= blocks)
    def _():
        tile = step - blocks
        up_grad_ref[0] = outer(hidden_ref[...], up_ref[tile]).astype(jnp.bfloat16)
        down_grad_ref[0] = outer(active_ref[tile], down_ref[...]).astype(jnp.bfloat16)


def fed_forward_both(counts, lengths, hat, inverse, cotangent, weights, vectors):
    tokens, width = hat.shape
    blocks = tokens // ROWS
    low = jnp.bfloat16
    smem = pl.BlockSpec(memory_space=pltpu.SMEM)
    shaped = jax.ShapeDtypeStruct

    def block_of(step):
        return jnp.minimum(step, blocks - 1)

    def tile_of(step):
        return jnp.maximum(step - blocks, 0)

    rows = pl.BlockSpec((ROWS, width), lambda i: (block_of(i), 0))
    tile = pl.BlockSpec((1, width, width), lambda i: (tile_of(i), 0, 0))
    return pl.pallas_call(
        feed_forward_both,
        grid=(blocks + 4,),
        out_shape=(
            shaped((tokens, width), low),
            shaped((tokens, width), jnp.float32),
            shaped((tokens, width), low),
            shaped((tokens, width), low),
            shaped((4, width, width), low),
            shaped((4, width, width), low),
            shaped((16, width), jnp.float32),
        ),
        in_specs=[
            smem,
            smem,
            rows,
            pl.BlockSpec((ROWS, 1), lambda i: (block_of(i), 0)),
            rows,
            pl.BlockSpec(memory_space=pl.ANY),
            pl.BlockSpec((VROWS, width), lambda i: (0, 0)),
        ],
        out_specs=(
            rows,
            rows,
            rows,
            rows,
            tile,
            tile,
            pl.BlockSpec((16, width), lambda i: (0, 0)),
        ),
        scratch_shapes=[
            pltpu.VMEM((9, width, width), low),
            pltpu.VMEM((4, tokens, width), low),
            pltpu.VMEM((4, tokens, width), low),
            pltpu.VMEM((tokens, width), low),
            pltpu.VMEM((tokens, width), low),
            pltpu.VMEM((4, ROWS, width), low),
            pltpu.SemaphoreType.DMA((9,)),
        ],
        compiler_params=pltpu.CompilerParams(vmem_limit_bytes=60 * 2**20),
        name="feed_forward_both",
    )(counts, lengths, hat, inverse, cotangent, weights, vectors)


def attend_backward(
    p_ref,
    q_ref,
    k_ref,
    v_ref,
    x_ref,
    ctx_ref,
    grad_ctx_ref,
    branch_ref,
    first_ref,
    w_ref,
    input_ref,
    grad_ref,
    sum_ref,
    scores_ref,
    pulled,
):
    step = pl.program_id(0)
    quad, block = step // 2, lax.rem(step, 2)
    here = pl.ds(pl.multiple_of(block * ROWS, ROWS), ROWS)
    cols = pl.ds(pl.multiple_of(quad * 256, 256), 256)

    @pl.when(step == 0)
    def _():
        sum_ref[...] = jnp.zeros_like(sum_ref)
        input_ref[...] = first_ref[...]

    def add_sums(at, by_query, by_value):
        sum_ref[0:1, at] += by_query
        sum_ref[1:2, at] += by_value

    for pair in range(2):
        half = slice(128 * pair, 128 * pair + 128)
        qkv = q_ref[:, half], k_ref[:, half], v_ref[:, half]
        heads = p_ref.at[0, pl.ds(2 * pair, 2)]
        attend_back_pair(
            2 * quad + pair, here, heads, qkv, ctx_ref, grad_ctx_ref, scores_ref, pulled, half, add_sums
        )
    more = input_ref[here, :]
    for at in range(3):
        more = more + dot_back(pulled[at, here, :], w_ref[at, :, cols])
    input_ref[here, :] = more

    @pl.when(block == 1)
    def _():
        for tile in range(3):
            grad_ref[tile, :, cols] = outer(x_ref[...], pulled[tile]).astype(jnp.bfloat16)
        grad_ref[3, :, cols] = outer(ctx_ref[...], branch_ref[:, cols]).astype(jnp.bfloat16)


def attended_back(probs, query, keyed, valued, x, context, grad_context, grad_branch, grad_first, weights):
    tokens, width = x.shape
    low = jnp.bfloat16
    shaped = jax.ShapeDtypeStruct
    once = pl.Buffered(1)
    quad = pl.BlockSpec((ROWS, 256), lambda i: (lax.rem(i, 2), i // 2))
    whole = pl.BlockSpec((tokens, width), lambda i: (0, 0), pipeline_mode=once)
    return pl.pallas_call(
        attend_backward,
        grid=(6,),
        out_shape=(
            shaped((tokens, width), jnp.float32),
            shaped((4, width, width), low),
            shaped((16, width), jnp.float32),
        ),
        in_specs=[
            pl.BlockSpec((1, 4, ROWS, ROWS), lambda i: (lax.rem(i, 2), i // 2, 0, 0)),
            quad,
            quad,
            quad,
            whole,
            whole,
            whole,
            whole,
            whole,
            pl.BlockSpec((3, width, width), lambda i: (0, 0, 0), pipeline_mode=once),
        ],
        out_specs=(
            whole,
            pl.BlockSpec((4, width, width), lambda i: (0, 0, 0), pipeline_mode=once),
            pl.BlockSpec((16, width), lambda i: (0, 0)),
        ),
        scratch_shapes=[pltpu.VMEM((2, ROWS, ROWS), low), pltpu.VMEM((3, tokens, 256), low)],
        compiler_params=pltpu.CompilerParams(vmem_limit_bytes=56 * 2**20),
        name="attend_backward",
    )(probs, query, keyed, valued, x, context, grad_context, grad_branch, grad_first, weights)


def moved(param, grad, first, second, average, rate):
    param_new, first_new, second_new = adam_update(param, grad, first, second, rate)
    return param_new, first_new, second_new, average_rate * average + (1.0 - average_rate) * param_new


def update_kernel(
    gain_scale,
    grad_ref,
    master_ref,
    first_ref,
    second_ref,
    ema_ref,
    vec_grad_ref,
    bias_ref,
    gain_ref,
    vec_first_ref,
    vec_second_ref,
    vec_ema_ref,
    mixed_in,
    input_in,
    master_out,
    first_out,
    second_out,
    ema_out,
    copy_out,
    vec_out,
    vec_first_out,
    vec_second_out,
    vec_ema_out,
    mixed_out,
    input_out,
    vec_ref,
):
    mixed_out[...] = mixed_in[...]
    input_out[...] = input_in[...]

    @pl.when((pl.program_id(0) == 0) & (pl.program_id(1) == 0))
    def _():
        vec_ref[0:10, :] = bias_ref[...]
        vec_ref[10:12, :] = gain_ref[...]
        vec_grad = vec_grad_ref[0:VROWS, :] * gain_scale
        vec_out[...], vec_first_out[...], vec_second_out[...], vec_ema_out[...] = moved(
            vec_ref[...], vec_grad, vec_first_ref[...], vec_second_ref[...], vec_ema_ref[...], vector_rate
        )

    grad = grad_ref[...].astype(jnp.float32) * gain_scale
    result = moved(master_ref[0], grad, first_ref[0], second_ref[0], ema_ref[0], tile_rate)
    master_out[0], first_out[0], second_out[0], ema_out[0] = result
    copy_out[0] = result[0].astype(jnp.bfloat16)


def updated(
    gain_scale,
    slot_grads,
    master,
    first,
    second,
    ema,
    vec_grad,
    bias,
    gain,
    vec_first,
    vec_second,
    vec_ema,
    mixed,
    input_grad,
):
    width = master.shape[-1]
    chunk = 192
    tile = pl.BlockSpec((1, 1, chunk, width), lambda s, r: (0, s, r, 0))
    steps = width // chunk
    rows = pl.BlockSpec((mixed.shape[0] // (SLOTS * steps), width), lambda s, r: (s * steps + r, 0))

    def whole(value):
        return pl.BlockSpec(value.shape, lambda s, r: (0, 0))

    shaped = jax.ShapeDtypeStruct
    tile_shape = shaped(master.shape, jnp.float32)
    vec_shape = shaped((VROWS, width), jnp.float32)
    results = pl.pallas_call(
        functools.partial(update_kernel, gain_scale),
        grid=(SLOTS, steps),
        out_shape=(tile_shape,) * 4
        + (shaped(master.shape, jnp.bfloat16),)
        + (vec_shape,) * 4
        + (shaped(mixed.shape, mixed.dtype), shaped(input_grad.shape, input_grad.dtype)),
        in_specs=[pl.BlockSpec((1, chunk, width), lambda s, r: (s, r, 0))]
        + [tile] * 4
        + [whole(value) for value in (vec_grad, bias, gain, vec_first, vec_second, vec_ema)]
        + [rows] * 2,
        out_specs=(tile,) * 5 + (whole(vec_first),) * 4 + (rows,) * 2,
        scratch_shapes=[pltpu.VMEM((VROWS, width), jnp.float32)],
        compiler_params=pltpu.CompilerParams(vmem_limit_bytes=62 * 2**20),
        name="update",
    )(
        slot_grads,
        master,
        first,
        second,
        ema,
        vec_grad,
        bias,
        gain,
        vec_first,
        vec_second,
        vec_ema,
        mixed,
        input_grad,
    )
    return results[-2:] + results[:-2]


MESH = pl.DeviceIdType.MESH
GROUP = 32
PAIRS = TILES // 2
PLANE = 8
PIECE = 96
PAIR_TILES = ((0, 1), (2, 3), (4, 8), (5, 9), (6, 10), (7, 11))
EARLY = 2
WHOLE = 3


def remote(src, dst, send, recv, device):
    return pltpu.make_async_remote_copy(
        src_ref=src, dst_ref=dst, send_sem=send, recv_sem=recv, device_id=(device,), device_id_type=MESH
    )


def place(device):
    core = lax.rem(device, 2)
    x = lax.rem(device // 2, 2)
    y = lax.rem(device // 4, 2)
    z = device // 8
    return z, y, x, core


def start(copies):
    for copy in copies:
        copy.start()


def arrive(copies):
    for copy in copies:
        copy.wait_recv()


def greet(z, in_plane):
    barrier = pltpu.get_barrier_semaphore()
    for hop in range(1, PLANE):
        other = z * PLANE + lax.rem(in_plane + hop, PLANE)
        pl.semaphore_signal(barrier, inc=1, device_id=(other,), device_id_type=MESH)
    for hop in range(1, 4):
        other = lax.rem(z + hop, 4) * PLANE + in_plane
        pl.semaphore_signal(barrier, inc=1, device_id=(other,), device_id_type=MESH)
    pl.semaphore_wait(barrier, PLANE + 2)


def along_z(z, in_plane):
    inner = (1 + z // 2) * PLANE + in_plane
    other_middle = (3 - z) * PLANE + in_plane
    outer_end = lax.rem(lax.rem(z + 3, 4) * 3, 4) * PLANE + in_plane
    return inner, other_middle, outer_end


def third(part):
    return slice(None) if part == WHOLE else pl.ds(256 * part, 256)


def slot_number(owners, tile):
    number = jnp.int32(0)
    for earlier in range(tile):
        number = number + jnp.where(owners[earlier] == owners[tile], 1, 0)
    return number


def unit(pair, part):
    return 3 * pair + part if pair < EARLY else 2 * EARLY + pair


UNITS = [(pair, part) for pair in range(EARLY) for part in range(3)]
UNITS += [(pair, WHOLE) for pair in range(EARLY, PAIRS)]

FRONT_PLAN = (
    (
        ("open",),
        ("swap", 0),
        ("sent", 0),
        ("swap", 1),
        ("choose", 0),
        ("end", 0, 0),
        ("caps",),
        ("end", 1, 0),
        ("middle", 0, 0),
        ("sent", 1),
        ("swap", 2),
        ("choose", 1),
        ("end", 0, 1),
        ("middle", 1, 0),
        ("end", 1, 1),
        ("total", 0, 0),
        ("total", 1, 0),
        ("mid", 0, 0),
        ("middle", 0, 1),
        ("choose", 2),
        ("end", 1, 2),
        ("far", 0, 0),
        ("middle", 1, 1),
        ("total", 0, 1),
        ("mid", 1, 0),
        ("end", 4),
        ("mid", 0, 1),
        ("total", 1, 1),
        ("middle", 1, 2),
        ("far", 1, 0),
        ("mid", 1, 1),
        ("middle", 4),
        ("end", 0, 2),
        ("end", 2),
        ("far", 0, 1),
        ("total", 1, 2),
        ("near", 0, 0),
        ("far", 1, 1),
        ("near", 0, 1),
        ("near", 1, 0),
        ("middle", 0, 2),
        ("finish", 0, 1),
        ("total", 4),
        ("near", 1, 1),
        ("finish", 1, 0),
        ("end", 3),
        ("middle", 2),
        ("total", 0, 2),
        ("finish", 0, 0),
    ),
    (
        ("mid", 1, 2),
        ("end", 5),
        ("mid", 0, 2),
        ("middle", 3),
        ("mid", 4),
        ("total", 2),
        ("far", 0, 2),
    ),
    (
        ("finish", 1, 1),
        ("far", 1, 2),
        ("middle", 5),
        ("far", 4),
        ("near", 0, 2),
        ("total", 3),
    ),
    (
        ("mid", 2),
    ),
    (
        ("mid", 3),
        ("far", 2),
        ("finish", 0, 2),
        ("near", 1, 2),
        ("near", 4),
        ("finish", 1, 2),
        ("keep",),
        ("total", 5),
        ("far", 3),
    ),
    (
        ("near", 2),
        ("finish", 4),
        ("mid", 5),
    ),
    (
        ("near", 3),
        ("finish", 2),
        ("far", 5),
    ),
    (
        ("finish", 3),
    ),
    (
        ("near", 5),
    ),
    (
        ("finish", 5),
    ),
)


def forward_and_pull(
    counts,
    lengths,
    owners,
    bias_ref,
    gain_ref,
    x_hbm,
    cot_hbm,
    master_hbm,
    q_ref,
    k_ref,
    v_ref,
    p_ref,
    ctx_hbm,
    hidden_hbm,
    active_hbm,
    up_hbm,
    down_hbm,
    mixed_hbm,
    first_hbm,
    branch_hbm,
    grad_ctx_hbm,
    w_out,
    sum_ref,
    vec_ref,
    cap_ref,
    wide,
    low,
    stage_a,
    stage_b,
    stage_c,
    chosen,
    from_end,
    from_middle,
    w_buf,
    x_then_hidden,
    ctx_then_grad,
    cot_then_down,
    mixed_then_branch,
    hat_ref,
    inverse_ref,
    slope_ref,
    tile_buf,
    load_sem,
    store_sem,
    tile_sem,
    out_sem,
    swap_send,
    swap_recv,
    z_send,
    z_recv,
    mid_send,
    mid_recv,
    far_send,
    far_recv,
    near_send,
    near_recv,
):
    step = pl.program_id(0)
    width = 8 * PIECE
    me = lax.axis_index("dp")
    z, y, x, core = place(me)
    in_plane = lax.rem(me, PLANE)
    sibling = me + 1 - 2 * core
    x_peer = me + 2 - 4 * x
    y_peer = me + 4 - 8 * y
    z_targets = along_z(z, in_plane)
    stages = (stage_a, stage_b, stage_c)
    is_end = (z == 0) | (z == 3)
    is_middle = (z == 1) | (z == 2)

    def piece_rows(cell_core, cell_x, cell_y):
        return pl.ds(pl.multiple_of(((cell_core * 2 + cell_x) * 2 + cell_y) * PIECE, 16), PIECE)

    def swap(part):
        def send(hop, carry):
            target = lax.rem(in_plane + hop, PLANE)
            _, ty, tx, tc = place(target)
            remote(
                low.at[:, piece_rows(tc, tx, ty), third(part)],
                stages[part].at[pl.ds(2 * in_plane, 2)],
                swap_send.at[part],
                swap_recv.at[part],
                z * PLANE + target,
            ).start()
            return carry

        lax.fori_loop(1, PLANE, send, 0)

    def swap_wait(part, sem):
        most = stages[part].at[pl.ds(0, 2 * PLANE - 2)]
        pltpu.make_async_copy(most, most, sem.at[part]).wait()

    def z_copy(pair, part, level):
        two = pl.ds(2 * pair, 2)
        cols = third(part)
        src = w_buf.at[two, core, x, y, :, cols] if level == 2 else chosen.at[two, :, cols]
        dst = (from_end.at[two, :, cols], from_middle.at[two, :, cols], src)[level]
        at = unit(pair, part)
        return remote(src, dst, z_send.at[level, at], z_recv.at[level, at], z_targets[level])

    def z_end(pair, part=WHOLE):
        @pl.when(is_end)
        def _():
            z_copy(pair, part, 0).start()

    def z_middle(pair, part=WHOLE):
        @pl.when(is_middle)
        def _():
            z_copy(pair, part, 0).wait_recv()
            two, cols = pl.ds(2 * pair, 2), third(part)
            chosen[two, :, cols] = chosen[two, :, cols] + from_end[two, :, cols]
            z_copy(pair, part, 1).start()

    def z_total(pair, part=WHOLE):
        @pl.when(is_middle)
        def _():
            z_copy(pair, part, 1).wait_recv()
            two, cols = pl.ds(2 * pair, 2), third(part)
            w_buf[two, core, x, y, :, cols] = chosen[two, :, cols] + from_middle[two, :, cols]
            z_copy(pair, part, 2).start()

    def mid_copies(pair, part):
        copies = []
        for n, peer in enumerate((y_peer, x_peer)):
            spot = w_buf.at[2 * pair + n, core, x, y, :, third(part)]
            at = unit(pair, part), n
            copies.append(remote(spot, spot, mid_send.at[at], mid_recv.at[at], peer))
        return copies

    def halves(pair, part, late):
        row = 1 - x if late else x
        column = 1 - y if late else y
        cols = third(part)
        return w_buf.at[2 * pair, core, row, :, :, cols], w_buf.at[2 * pair + 1, core, :, column, :, cols]

    def far_copies(pair, part):
        copies = []
        for n, peer in enumerate((x_peer, y_peer)):
            spot = halves(pair, part, False)[n]
            at = unit(pair, part), n
            copies.append(remote(spot, spot, far_send.at[at], far_recv.at[at], peer))
        return copies

    def near_copies(pair, part, late):
        copies = []
        for n in range(2):
            spot = halves(pair, part, late)[n]
            at = unit(pair, part), n, late
            copies.append(remote(spot, spot, near_send.at[at], near_recv.at[at], sibling))
        return copies

    def give_mid(pair, part=WHOLE):
        @pl.when(is_end)
        def _():
            z_copy(pair, part, 2).wait_recv()

        start(mid_copies(pair, part))

    def give_far(pair, part=WHOLE):
        arrive(mid_copies(pair, part))
        start(far_copies(pair, part) + near_copies(pair, part, 0))

    def give_near(pair, part=WHOLE):
        arrive(far_copies(pair, part))
        start(near_copies(pair, part, 1))

    def finish(pair, part=WHOLE):
        arrive(near_copies(pair, part, 0) + near_copies(pair, part, 1))

    def choose(part):
        swap_wait(part, swap_recv)
        for pair in range(PAIRS):
            for n, tile in enumerate(PAIR_TILES[pair]):
                owner = owners[tile]
                value = stages[part][SLOTS * lax.rem(owner, PLANE) + slot_number(owners, tile)]
                chosen[2 * pair + n, :, third(part)] = jnp.where(
                    owner // PLANE == z, value, jnp.zeros_like(value)
                )

    def load(at):
        src = (x_hbm, cot_hbm, master_hbm)[at]
        dst = (x_then_hidden, cot_then_down, wide)[at]
        return pltpu.make_async_copy(src, dst, load_sem.at[at])

    def store(at):
        src, dst = (
            (x_then_hidden, hidden_hbm),
            (ctx_then_grad, ctx_hbm),
            (cot_then_down, down_hbm),
            (mixed_then_branch, mixed_hbm),
            (ctx_then_grad, grad_ctx_hbm),
            (mixed_then_branch, branch_hbm),
            (wide, first_hbm),
        )[at]
        src = src.at[pl.ds(0, 2 * ROWS)] if src is wide else src
        return pltpu.make_async_copy(src, dst, store_sem.at[at])

    def w_stores():
        return [
            pltpu.make_async_copy(w_buf.at[tile], w_out.at[tile], out_sem.at[tile]) for tile in range(3)
        ]

    def weight(at, cols=slice(None)):
        value = w_buf[at, :, :, :, :, cols]
        return value.reshape(width, value.shape[-1])

    def open_all():
        for at in range(3):
            load(at).start()
        sum_ref[...] = jnp.zeros_like(sum_ref)
        vec_ref[0:10, :] = bias_ref[...]
        vec_ref[10:12, :] = gain_ref[...]
        greet(z, in_plane)
        load(2).wait()
        for slot in range(SLOTS):
            low[slot] = wide[width * slot : width * (slot + 1), :].astype(jnp.bfloat16)
        for part in range(3):
            stages[part][pl.ds(2 * in_plane, 2)] = low[:, piece_rows(core, x, y), third(part)]

    def make_caps():
        for block in range(2):
            cap_ref[block] = attention_caps(counts, lengths, block)
        load(0).wait()
        load(1).wait()

    actions = {
        "open": open_all,
        "caps": make_caps,
        "swap": swap,
        "sent": lambda part: swap_wait(part, swap_send),
        "choose": choose,
        "end": z_end,
        "middle": z_middle,
        "total": z_total,
        "mid": give_mid,
        "far": give_far,
        "near": give_near,
        "finish": finish,
        "keep": lambda: start(w_stores()),
    }

    for at, work in enumerate(FRONT_PLAN):

        @pl.when(step == at)
        def _():
            for name, *rest in work:
                actions[name](*rest)

    quad, block = step // 2, lax.rem(step, 2)
    here = pl.ds(pl.multiple_of(block * ROWS, ROWS), ROWS)

    @pl.when(step < 6)
    def _():
        attend_quad(
            quad,
            weight,
            x_then_hidden.at[here],
            vec_ref,
            cap_ref.at[block],
            q_ref,
            k_ref,
            v_ref,
            p_ref,
            ctx_then_grad.at[here],
        )

    @pl.when((step >= 4) & (step < 6))
    def _():
        branch = dot(ctx_then_grad[here, :], weight(3)) + vec_ref[2:3, :]
        for rows in strips(ROWS, 32):
            there = pl.ds(pl.multiple_of(block * ROWS + rows.start, 32), 32)
            hat, inverse = normalize(x_then_hidden[there, :].astype(jnp.float32) + branch[rows])
            hat_ref[there, :] = hat
            inverse_ref[there, :] = inverse
            hidden = hat * vec_ref[10:11, :] + vec_ref[8:9, :]
            x_then_hidden[there, :] = hidden.astype(jnp.bfloat16)
            wide[there, :] = hidden + vec_ref[7:8, :]

    @pl.when(step == 5)
    def _():
        start([store(0), store(1)])

    turn = step - 6
    slot = lax.rem(turn, 2)

    def tile_store(source_slot, target):
        return pltpu.make_async_copy(tile_buf.at[source_slot], target, tile_sem.at[source_slot])

    @pl.when(turn >= 2)
    def _():
        tile_store(slot, active_hbm.at[0]).wait()

    @pl.when((step >= 6) & (step < 10))
    def _():
        for half in range(2):
            rows = slice(ROWS * half, ROWS * half + ROWS)
            up = dot(x_then_hidden[rows, :], weight(4 + 2 * turn)) + vec_ref[pl.ds(3 + turn, 1), :]
            for part in strips(ROWS, 32):
                there = slice(rows.start + part.start, rows.start + part.stop)
                active, slope = gelu_parts(up[part])
                slope_ref[turn, there, :] = slope.astype(jnp.bfloat16)
                tile_buf[slot, there, :] = active
            wide[rows, :] = wide[rows, :] + dot(tile_buf[slot, rows, :], weight(5 + 2 * turn))
        tile_store(slot, active_hbm.at[turn]).start()

    @pl.when(step == 10)
    def _():
        for rows in strips(2 * ROWS, 32):
            at_row = lax.broadcasted_iota(jnp.int32, (32, 1), 0) + rows.start
            live = passage_facts(counts, lengths, at_row)[0].astype(jnp.float32)
            hat, inverse = normalize(wide[rows, :])
            mixed = (hat * vec_ref[11:12, :] + vec_ref[9:10, :]) * live
            mixed_then_branch[rows, :] = mixed.astype(jnp.bfloat16)
            grad_out = cot_then_down[rows, :].astype(jnp.float32) * live
            sum_ref[11:12, :] += columns_total(grad_out * hat)
            sum_ref[9:10, :] += columns_total(grad_out)
            second = normalize_back(grad_out * vec_ref[11:12, :], hat, inverse)
            wide[rows, :] = second
            down_low = second.astype(jnp.bfloat16)
            cot_then_down[rows, :] = down_low
            sum_ref[7:8, :] += columns_total(down_low.astype(jnp.float32))
        start([store(2), store(3)])

    @pl.when(step >= 10)
    def _():
        tile = step - 10
        for half in range(2):
            rows = slice(ROWS * half, ROWS * half + ROWS)
            pulled = dot_back(cot_then_down[rows, :], weight(5 + 2 * tile))
            total = jnp.zeros((1, width), jnp.float32)
            for part in strips(ROWS, 32):
                there = slice(rows.start + part.start, rows.start + part.stop)
                up_low = (pulled[part] * slope_ref[tile, there, :].astype(jnp.float32)).astype(jnp.bfloat16)
                tile_buf[slot, there, :] = up_low
                total = total + columns_total(up_low.astype(jnp.float32))
            sum_ref[pl.ds(3 + tile, 1), :] += total
            wide[rows, :] = wide[rows, :] + dot_back(tile_buf[slot, rows, :], weight(4 + 2 * tile))
        tile_store(slot, up_hbm.at[tile]).start()

    @pl.when(step == 13)
    def _():
        store(1).wait()
        store(3).wait()
        for rows in strips(2 * ROWS, 32):
            grad_hidden, hat = wide[rows, :], hat_ref[rows, :]
            sum_ref[10:11, :] += columns_total(grad_hidden * hat)
            sum_ref[8:9, :] += columns_total(grad_hidden)
            first = normalize_back(grad_hidden * vec_ref[10:11, :], hat, inverse_ref[rows, :])
            wide[rows, :] = first
            branch_low = first.astype(jnp.bfloat16)
            mixed_then_branch[rows, :] = branch_low
            sum_ref[2:3, :] += columns_total(branch_low.astype(jnp.float32))
        for rows in strips(2 * ROWS, ROWS):
            pulled = dot_back(mixed_then_branch[rows, :], weight(3))
            ctx_then_grad[rows, :] = pulled.astype(jnp.bfloat16)
        start([store(4), store(5), store(6)])
        store(0).wait()
        store(2).wait()
        for at in range(2):
            tile_store(at, up_hbm.at[0]).wait()
        for copy in w_stores():
            copy.wait()
        swap_wait(2, swap_send)
        for pair, part in UNITS:
            for copy in mid_copies(pair, part) + far_copies(pair, part):
                copy.wait_send()
            for copy in near_copies(pair, part, 0) + near_copies(pair, part, 1):
                copy.wait_send()

            @pl.when(is_end)
            def _():
                z_copy(pair, part, 0).wait_send()

            @pl.when(is_middle)
            def _():
                z_copy(pair, part, 1).wait_send()
                z_copy(pair, part, 2).wait_send()

        for at in range(4, 7):
            store(at).wait()


def forwarded_and_pulled(counts, lengths, owners, bias, gain, x, cotangent, master):
    tokens, width = x.shape
    blocks = tokens // ROWS
    low, high = jnp.bfloat16, jnp.float32
    smem = pl.BlockSpec(memory_space=pltpu.SMEM)
    any_space = pl.BlockSpec(memory_space=pl.ANY)
    dma = pltpu.SemaphoreType.DMA
    shaped = jax.ShapeDtypeStruct

    def at(step):
        step = jnp.minimum(step, 5)
        return lax.rem(step, 2), step // 2

    quad = pl.BlockSpec((ROWS, 256), at)
    rows = shaped((tokens, width), low)
    cut = (2, 2, 2, PIECE, width)
    units = len(UNITS)
    results = pl.pallas_call(
        forward_and_pull,
        grid=(14,),
        out_shape=(
            rows,
            rows,
            rows,
            shaped((blocks, HEADS, ROWS, ROWS), low),
            rows,
            rows,
            shaped((4, tokens, width), low),
            shaped((4, tokens, width), low),
            rows,
            rows,
            shaped((tokens, width), high),
            rows,
            rows,
            shaped((3,) + cut, low),
            shaped((16, width), high),
        ),
        in_specs=[smem] * 3
        + [pl.BlockSpec(bias.shape, lambda i: (0, 0)), pl.BlockSpec(gain.shape, lambda i: (0, 0))]
        + [any_space] * 3,
        out_specs=(quad, quad, quad, pl.BlockSpec((1, 4, ROWS, ROWS), lambda i: (*at(i), 0, 0)))
        + (any_space,) * 10
        + (pl.BlockSpec((16, width), lambda i: (0, 0)),),
        scratch_shapes=[
            pltpu.VMEM((VROWS, width), high),
            pltpu.VMEM((2, ROWS, ROWS), high),
            pltpu.VMEM((SLOTS * width, width), high),
            pltpu.VMEM((SLOTS, width, width), low),
            pltpu.VMEM((2 * PLANE, PIECE, 256), low),
            pltpu.VMEM((2 * PLANE, PIECE, 256), low),
            pltpu.VMEM((2 * PLANE, PIECE, 256), low),
            pltpu.VMEM((TILES, PIECE, width), low),
            pltpu.VMEM((TILES, PIECE, width), low),
            pltpu.VMEM((TILES, PIECE, width), low),
            pltpu.VMEM((TILES,) + cut, low),
            pltpu.VMEM((tokens, width), low),
            pltpu.VMEM((tokens, width), low),
            pltpu.VMEM((tokens, width), low),
            pltpu.VMEM((tokens, width), low),
            pltpu.VMEM((tokens, width), high),
            pltpu.VMEM((tokens, 1), high),
            pltpu.VMEM((4, tokens, width), low),
            pltpu.VMEM((2, tokens, width), low),
            dma((3,)),
            dma((7,)),
            dma((2,)),
            dma((3,)),
            dma((3,)),
            dma((3,)),
            dma((3, units)),
            dma((3, units)),
            dma((units, 2)),
            dma((units, 2)),
            dma((units, 2)),
            dma((units, 2)),
            dma((units, 2, 2)),
            dma((units, 2, 2)),
        ],
        compiler_params=pltpu.CompilerParams(
            collective_id=0, has_side_effects=True, vmem_limit_bytes=63 * 2**20
        ),
        name="forward_and_pull",
    )(counts, lengths, owners, bias, gain, x, cotangent, master.reshape(SLOTS * width, width))
    w_early = results[13].reshape(3, width, width)
    return results[:13] + (w_early,) + results[14:]


BACK_PLAN = (
    (),
    (
        ("core", 0),
    ),
    (
        ("core", 1),
        ("far", 0),
    ),
    (
        ("core", 2),
        ("far", 1),
    ),
    (),
    (
        ("far", 2),
        ("mid", 0),
    ),
    (
        ("core", 3),
    ),
    (),
    (
        ("mid", 1),
        ("end", 0),
    ),
    (
        ("mid", 2),
        ("core", 4),
        ("far", 3),
        ("middle", 0),
    ),
    (
        ("end", 1),
    ),
    (
        ("middle", 1),
    ),
    (
        ("end", 2),
        ("total", 0),
        ("core", 5),
        ("far", 4),
        ("mid", 3),
    ),
    (
        ("middle", 2),
        ("total", 1),
    ),
    (),
    (
        ("end", 3),
        ("mid", 4),
        ("middle", 3),
        ("far", 5),
        ("total", 2),
    ),
    (
        ("core", 6),
        ("mid", 5),
        ("end", 4),
        ("middle", 4),
        ("total", 3),
        ("take", 0),
        ("sum", 0),
        ("far", 6),
        ("total", 4),
        ("end", 5),
        ("middle", 5),
        ("mid", 6),
        ("take", 1),
        ("sum", 1),
        ("end", 6),
        ("take", 4),
        ("total", 5),
        ("take", 2),
        ("take", 3),
        ("deliver", 0),
        ("sum", 2),
        ("take", 5),
        ("middle", 6),
        ("total", 6),
        ("deliver", 1),
        ("take", 6),
        ("deliver", 2),
    ),
)


def pull_and_reduce(
    owners,
    p_ref,
    q_ref,
    k_ref,
    v_ref,
    ctx_ref,
    grad_ctx_ref,
    active_ref,
    up_ref,
    x_hbm,
    hidden_hbm,
    branch_hbm,
    down_hbm,
    first_hbm,
    w_hbm,
    late_ref,
    input_hbm,
    slot_grad,
    vec_out,
    w_buf,
    acc,
    scores_ref,
    pulled,
    hidden_then_x,
    down_then_branch,
    part,
    from_core,
    from_far,
    from_mid,
    from_end,
    from_middle,
    total,
    snap,
    outbox,
    vec_now,
    vec_in,
    holds,
    keeps,
    load_sem,
    core_send,
    core_recv,
    far_send,
    far_recv,
    mid_send,
    mid_recv,
    z_send,
    z_recv,
    vec_send,
    vec_recv,
    out_send,
    out_recv,
):
    step = pl.program_id(0)
    inner = jnp.maximum(step - 4, 0)
    quad, block, pair = inner // 4, lax.rem(inner, 4) // 2, lax.rem(inner, 2)
    me = lax.axis_index("dp")
    z, y, x, core = place(me)
    in_plane = lax.rem(me, PLANE)
    sibling = me + 1 - 2 * core
    x_peer = me + 2 - 4 * x
    y_peer = me + 4 - 8 * y
    z_targets = along_z(z, in_plane)
    is_end = (z == 0) | (z == 3)
    is_middle = (z == 1) | (z == 2)

    def items(batch):
        if batch < 4:
            return [(0, 4 + batch, slice(None)), (1, 8 + batch, slice(None))]
        cols = pl.ds(256 * (batch - 4), 256)
        return [(0, 0, cols), (1, 1, cols), (0, 2, cols), (1, 3, cols)]

    def held(tile):
        return part.at[tile, core]

    def core_copies(batch):
        return [
            remote(
                part.at[tile, 1 - core, :, :, :, cols],
                from_core.at[tile, :, :, :, cols],
                core_send.at[batch, n],
                core_recv.at[batch, n],
                sibling,
            )
            for n, (_, tile, cols) in enumerate(items(batch))
        ]

    def far_copies(batch):
        copies = []
        for n, (kind, tile, cols) in enumerate(items(batch)):
            mine = held(tile)
            copies.append(
                remote(
                    mine.at[:, 1 - y, :, cols] if kind else mine.at[1 - x, :, :, cols],
                    from_far.at[tile, :, :, cols],
                    far_send.at[batch, n],
                    far_recv.at[batch, n],
                    y_peer if kind else x_peer,
                )
            )
        return copies

    def mid_copies(batch):
        copies = []
        for n, (kind, tile, cols) in enumerate(items(batch)):
            mine = held(tile)
            copies.append(
                remote(
                    mine.at[1 - x, y, :, cols] if kind else mine.at[x, 1 - y, :, cols],
                    from_mid.at[tile, :, cols],
                    mid_send.at[batch, n],
                    mid_recv.at[batch, n],
                    x_peer if kind else y_peer,
                )
            )
        return copies

    def z_copies(batch, stage):
        copies = []
        for n, (_, tile, cols) in enumerate(items(batch)):
            if stage == 2:
                src, dst = total.at[tile, :, cols], total.at[tile, :, cols]
            else:
                src = held(tile).at[x, y, :, cols]
                dst = (from_middle if stage else from_end).at[tile, :, cols]
            copies.append(
                remote(
                    src,
                    dst,
                    z_send.at[stage, batch, n],
                    z_recv.at[stage, batch, n],
                    z_targets[stage],
                )
            )
        return copies

    def give_core(batch):
        start(core_copies(batch))

    def give_far(batch):
        arrive(core_copies(batch))
        for _, tile, cols in items(batch):
            mine = held(tile)
            mine[:, :, :, cols] = mine[:, :, :, cols] + from_core[tile, :, :, :, cols]
        start(far_copies(batch))

    def give_mid(batch):
        arrive(far_copies(batch))
        for kind, tile, cols in items(batch):
            mine = held(tile)
            if kind:
                mine[:, y, :, cols] = mine[:, y, :, cols] + from_far[tile, :, :, cols]
            else:
                mine[x, :, :, cols] = mine[x, :, :, cols] + from_far[tile, :, :, cols]
        start(mid_copies(batch))

    def give_end(batch):
        arrive(mid_copies(batch))
        for _, tile, cols in items(batch):
            mine = held(tile)
            mine[x, y, :, cols] = mine[x, y, :, cols] + from_mid[tile, :, cols]

        @pl.when(is_end)
        def _():
            start(z_copies(batch, 0))

    def give_middle(batch):
        @pl.when(is_middle)
        def _():
            arrive(z_copies(batch, 0))
            for _, tile, cols in items(batch):
                mine = held(tile)
                mine[x, y, :, cols] = mine[x, y, :, cols] + from_end[tile, :, cols]
            start(z_copies(batch, 1))

    def give_total(batch):
        @pl.when(is_middle)
        def _():
            arrive(z_copies(batch, 1))
            for _, tile, cols in items(batch):
                mine = held(tile)
                total[tile, :, cols] = mine[x, y, :, cols] + from_middle[tile, :, cols]
            start(z_copies(batch, 2))

    def take_total(batch):
        @pl.when(is_end)
        def _():
            arrive(z_copies(batch, 2))

    def deliver(third):
        cols = pl.ds(256 * third, 256)
        snap[...] = total[:, :, cols]

        def fill(at, carry):
            value = snap[holds[at]]
            outbox[third, at] = jnp.where(keeps[at] > 0, value, jnp.zeros_like(value))
            return carry

        lax.fori_loop(0, 2 * PLANE, fill, 0)

        def send(hop, carry):
            target = lax.rem(in_plane + hop, PLANE)
            remote(
                outbox.at[third, pl.ds(2 * target, 2)],
                slot_grad.at[:, core, x, y, :, cols],
                out_send.at[third],
                out_recv.at[third],
                z * PLANE + target,
            ).start()
            return carry

        lax.fori_loop(1, PLANE, send, 0)
        keep_copy(third).start()

    def keep_copy(third):
        return pltpu.make_async_copy(
            outbox.at[third, pl.ds(2 * in_plane, 2)],
            slot_grad.at[:, core, x, y, :, pl.ds(256 * third, 256)],
            load_sem.at[5 + third],
        )

    def vec_copies(stage):
        if stage < 3:
            hops = [(stage, (sibling, x_peer, y_peer)[stage])]
        else:
            hops = [
                (2 + hop, lax.rem(z + hop, 4) * PLANE + in_plane) for hop in range(1, 4)
            ]
        return [
            remote(vec_now.at[stage], vec_in.at[at], vec_send.at[at], vec_recv.at[at], device)
            for at, device in hops
        ]

    def vec_next(stage):
        arrive(vec_copies(stage))
        vec_now[stage + 1] = vec_now[stage] + vec_in[stage]
        start(vec_copies(stage + 1))

    def first_load():
        return pltpu.make_async_copy(first_hbm, acc, load_sem.at[3])

    def input_store():
        return pltpu.make_async_copy(acc, input_hbm, load_sem.at[4])

    def w_loads():
        return [pltpu.make_async_copy(w_hbm.at[at], w_buf.at[at], load_sem.at[at]) for at in range(3)]

    def early_loads():
        return [
            pltpu.make_async_copy(hidden_hbm, hidden_then_x, load_sem.at[8]),
            pltpu.make_async_copy(down_hbm, down_then_branch, load_sem.at[9]),
        ]

    def late_loads():
        return [
            pltpu.make_async_copy(x_hbm, hidden_then_x, load_sem.at[8]),
            pltpu.make_async_copy(branch_hbm, down_then_branch, load_sem.at[9]),
        ]

    actions = {
        "core": give_core,
        "far": give_far,
        "mid": give_mid,
        "end": give_end,
        "middle": give_middle,
        "total": give_total,
        "take": take_total,
        "deliver": deliver,
        "sum": vec_next,
    }

    @pl.when(step == 0)
    def _():
        start(early_loads() + w_loads() + [first_load()])
        for at in range(2 * PLANE):
            tile_here, kept = jnp.int32(0), jnp.int32(0)
            for tile in range(TILES):
                place_of = SLOTS * owners[tile] + slot_number(owners, tile)
                match = place_of == z * 2 * PLANE + at
                tile_here = tile_here + jnp.where(match, tile, 0)
                kept = kept + jnp.where(match, 1, 0)
            holds[at] = tile_here
            keeps[at] = kept
        greet(z, in_plane)
        vec_now[0] = late_ref[...]
        for load in early_loads():
            load.wait()

    for at in range(len(BACK_PLAN) - 1):
        if BACK_PLAN[at]:

            @pl.when(step == at)
            def _():
                for name, number in BACK_PLAN[at]:
                    actions[name](number)

    @pl.when(step < 4)
    def _():
        by_up = outer(hidden_then_x[...], up_ref[0]).astype(jnp.bfloat16)
        part[4 + step] = by_up.reshape(2, 2, 2, PIECE, 8 * PIECE)
        by_down = outer(active_ref[0], down_then_branch[...]).astype(jnp.bfloat16)
        part[8 + step] = by_down.reshape(2, 2, 2, PIECE, 8 * PIECE)


    @pl.when(step == 3)
    def _():
        start(late_loads())

    here = pl.ds(pl.multiple_of(block * ROWS, ROWS), ROWS)
    quad_cols = pl.ds(pl.multiple_of(quad * 256, 256), 256)

    def add_sums(at, by_query, by_value):
        vec_now[0, 0:1, at] += by_query
        vec_now[0, 1:2, at] += by_value

    @pl.when(step >= 4)
    def _():
        attend_back_pair(
            2 * quad + pair,
            here,
            p_ref.at[0],
            (q_ref[...], k_ref[...], v_ref[...]),
            ctx_ref,
            grad_ctx_ref,
            scores_ref,
            pulled,
            pl.ds(pl.multiple_of(pair * 128, 128), 128),
            add_sums,
        )

    @pl.when(step == 4)
    def _():
        for load in w_loads() + [first_load()]:
            load.wait()

    @pl.when((step >= 4) & (pair == 1))
    def _():
        more = acc[here, :]
        for at in range(3):
            more = more + dot_back(pulled[at, here, :], w_buf[at, :, quad_cols])
        acc[here, :] = more

    @pl.when(step == 7)
    def _():
        for load in late_loads():
            load.wait()

    @pl.when((step >= 4) & (block == 1) & (pair == 1))
    def _():
        for tile in range(4):
            if tile < 3:
                value = outer(hidden_then_x[...], pulled[tile])
            else:
                value = outer(ctx_ref[...], down_then_branch[:, quad_cols])
            value = value.astype(jnp.bfloat16).reshape(2, 2, 2, PIECE, 256)
            part[tile, :, :, :, :, quad_cols] = value


    @pl.when(step == 15)
    def _():
        input_store().start()
        start(vec_copies(0))
        for name, number in BACK_PLAN[-1]:
            actions[name](number)
        arrive(vec_copies(3))
        summed = jnp.zeros(vec_out.shape, jnp.float32)
        for origin in range(4):
            hop = lax.rem(z - origin + 4, 4)
            summed = summed + jnp.where(hop == 0, vec_now[3], vec_in[2 + jnp.maximum(hop, 1)])
        vec_out[...] = summed
        for batch in range(7):
            for copy in core_copies(batch) + far_copies(batch) + mid_copies(batch):
                copy.wait_send()

            @pl.when(is_end)
            def _():
                for copy in z_copies(batch, 0):
                    copy.wait_send()

            @pl.when(is_middle)
            def _():
                for copy in z_copies(batch, 1) + z_copies(batch, 2):
                    copy.wait_send()

        for stage in range(4):
            for copy in vec_copies(stage):
                copy.wait_send()
        input_store().wait()
        for third in range(3):
            keep_copy(third).wait()
            most = outbox.at[third, pl.ds(0, 2 * PLANE - 2)]
            pltpu.make_async_copy(most, most, out_recv.at[third]).wait()
            pltpu.make_async_copy(most, most, out_send.at[third]).wait()


def pulled_and_reduced(
    owners,
    probs,
    query,
    keyed,
    valued,
    context,
    grad_context,
    active,
    grad_up,
    x,
    hidden,
    grad_branch,
    grad_down,
    grad_first,
    weights,
    late_sums,
):
    tokens, width = x.shape
    low, high = jnp.bfloat16, jnp.float32
    shaped = jax.ShapeDtypeStruct
    smem = pl.BlockSpec(memory_space=pltpu.SMEM)
    any_space = pl.BlockSpec(memory_space=pl.ANY)
    dma = pltpu.SemaphoreType.DMA

    def at(step):
        inner = jnp.maximum(step - 4, 0)
        return lax.rem(inner, 4) // 2, inner // 4 * 2 + lax.rem(inner, 2)

    pair = pl.BlockSpec((ROWS, 128), at)
    whole = pl.BlockSpec((tokens, width), lambda i: (0, 0), pipeline_mode=pl.Buffered(1))
    tile = pl.BlockSpec((1, tokens, width), lambda i: (jnp.minimum(i, 3), 0, 0))
    sums = pl.BlockSpec((16, width), lambda i: (0, 0))
    cut = (2, 2, 2, PIECE, width)
    input_grad, slot_grads, vector_sums = pl.pallas_call(
        pull_and_reduce,
        grid=(16,),
        out_shape=(
            shaped((tokens, width), high),
            shaped((SLOTS,) + cut, low),
            shaped((16, width), high),
        ),
        in_specs=[smem, pl.BlockSpec((1, 2, ROWS, ROWS), lambda i: (*at(i), 0, 0))]
        + [pair] * 3
        + [whole] * 2
        + [tile] * 2
        + [any_space] * 6
        + [sums],
        out_specs=(any_space, any_space, sums),
        scratch_shapes=[
            pltpu.VMEM((3, width, width), low),
            pltpu.VMEM((tokens, width), high),
            pltpu.VMEM((2, ROWS, ROWS), low),
            pltpu.VMEM((3, tokens, 256), low),
            pltpu.VMEM((tokens, width), low),
            pltpu.VMEM((tokens, width), low),
            pltpu.VMEM((TILES,) + cut, low),
            pltpu.VMEM((TILES,) + cut[1:], low),
            pltpu.VMEM((TILES,) + cut[2:], low),
            pltpu.VMEM((TILES,) + cut[3:], low),
            pltpu.VMEM((TILES,) + cut[3:], low),
            pltpu.VMEM((TILES,) + cut[3:], low),
            pltpu.VMEM((TILES,) + cut[3:], low),
            pltpu.VMEM((TILES, PIECE, 256), low),
            pltpu.VMEM((3, 2 * PLANE, PIECE, 256), low),
            pltpu.VMEM((4, 16, width), high),
            pltpu.VMEM((6, 16, width), high),
            pltpu.SMEM((2 * PLANE,), jnp.int32),
            pltpu.SMEM((2 * PLANE,), jnp.int32),
            dma((10,)),
            dma((7, 4)),
            dma((7, 4)),
            dma((7, 4)),
            dma((7, 4)),
            dma((7, 4)),
            dma((7, 4)),
            dma((3, 7, 4)),
            dma((3, 7, 4)),
            dma((6,)),
            dma((6,)),
            dma((3,)),
            dma((3,)),
        ],
        compiler_params=pltpu.CompilerParams(
            collective_id=1, has_side_effects=True, vmem_limit_bytes=63 * 2**20
        ),
        name="pull_and_reduce",
    )(
        owners,
        probs,
        query,
        keyed,
        valued,
        context,
        grad_context,
        active,
        grad_up,
        x,
        hidden,
        grad_branch,
        grad_down,
        grad_first,
        weights,
        late_sums,
    )
    return input_grad, slot_grads.reshape(SLOTS, width, width), vector_sums


def collected_tiles(tile_low, owners, slots):
    mine = owners == lax.axis_index("dp")
    local = jnp.where(mine[:, None, None], tile_low[slots], jnp.zeros((), tile_low.dtype))
    return lax.psum(local, "dp")


def summed_over_slice(parts, vector_terms, owners, slots):
    myself = lax.axis_index("dp")

    def add(held, items):
        part, owner, slot = items
        total = lax.psum(part.astype(jnp.float32), "dp")
        here = (owner == myself) & (slot == jnp.arange(SLOTS, dtype=jnp.int32))
        return held + jnp.where(here[:, None, None], total[None], 0.0), None

    empty = jnp.zeros((SLOTS,) + parts.shape[1:], jnp.float32)
    return lax.scan(add, empty, (parts, owners, slots))[0], lax.psum(vector_terms, "dp")


def body(
    inputs,
    cotangent,
    counts,
    lengths,
    owners,
    tile_master,
    tile_first,
    tile_second,
    tile_ema,
    bias_vals,
    gain_vals,
    vector_first,
    vector_second,
    vector_ema,
):
    tokens = inputs.shape[0]
    small = lax.axis_size("dp") == GROUP
    gain_scale = float(tokens * lax.axis_size("dp")) ** (-0.5)
    if small:
        (
            query,
            keyed,
            valued,
            probs,
            context,
            hidden,
            active,
            grad_up,
            grad_down,
            mixed,
            grad_first,
            grad_branch,
            grad_context,
            weights,
            late_sums,
        ) = forwarded_and_pulled(
            counts,
            lengths,
            owners,
            bias_vals,
            gain_vals,
            inputs,
            cotangent,
            tile_master,
        )
        input_grad, slot_grads, full_sums = pulled_and_reduced(
            owners,
            probs,
            query,
            keyed,
            valued,
            context,
            grad_context,
            active,
            grad_up,
            inputs,
            hidden,
            grad_branch,
            grad_down,
            grad_first,
            weights,
            late_sums,
        )
    else:
        slots = tile_slots(owners)
        vectors = jnp.concatenate([bias_vals, gain_vals], 0)
        weights = collected_tiles(tile_master[0].astype(jnp.bfloat16), owners, slots)
        query, keyed, valued, probs, context, hat, inverse = attended(
            counts, lengths, inputs, weights, vectors
        )
        mixed, grad_first, grad_branch, grad_context, up_grads, down_grads, late_sums = fed_forward_both(
            counts, lengths, hat, inverse, cotangent, weights, vectors
        )
        input_grad, early_grads, early_sums = attended_back(
            probs, query, keyed, valued, inputs, context, grad_context, grad_branch, grad_first, weights
        )
        parts = jnp.concatenate([early_grads, up_grads, down_grads], 0)
        slot_grads, full_sums = summed_over_slice(parts, late_sums + early_sums, owners, slots)
    return updated(
        gain_scale,
        slot_grads,
        tile_master,
        tile_first,
        tile_second,
        tile_ema,
        full_sums,
        bias_vals,
        gain_vals,
        vector_first,
        vector_second,
        vector_ema,
        mixed,
        input_grad,
    )


def solution(mesh):
    placed = (
        P("dp", None),
        P("dp", None),
        P("dp", None),
        P("dp", None),
        P(),
        P("dp", None, None, None),
        P("dp", None, None, None),
        P("dp", None, None, None),
        P("dp", None, None, None),
        P(),
        P(),
        P(),
        P(),
        P(),
    )
    return jax.shard_map(
        body,
        mesh=mesh,
        in_specs=placed,
        out_specs=(
            P("dp", None),
            P("dp", None),
            P("dp", None, None, None),
            P("dp", None, None, None),
            P("dp", None, None, None),
            P("dp", None, None, None),
            P("dp", None, None, None),
            P(),
            P(),
            P(),
            P(),
        ),
        check_vma=False,
    )
```

```python
import functools

import jax
import jax.numpy as jnp
from jax import lax
from jax.experimental import pallas as pl
from jax.experimental.pallas import tpu as pltpu
from jax.sharding import PartitionSpec as P

HEADS = 12
BUCKET = 128
SLOTS = 2
TILES = 12
VROWS = 12
STEP = 5

norm_epsilon = 1e-12
tile_rate = 0.03
vector_rate = 0.2
first_decay = 0.5
second_decay = 0.5
adam_epsilon = 1e-08
weight_decay = 0.01
average_rate = 0.9


def tile_slots(owners):
    order = jnp.arange(owners.shape[0], dtype=jnp.int32)
    same = owners[:, None] == owners[None, :]
    earlier = order[None, :] < order[:, None]
    return jnp.sum((same & earlier).astype(jnp.int32), 1)


def adam_update(param, grad, first, second, rate):
    first_new = first_decay * first + (1.0 - first_decay) * grad
    second_new = second_decay * second + (1.0 - second_decay) * grad * grad
    first_hat = first_new / (1.0 - first_decay**STEP)
    second_hat = second_new / (1.0 - second_decay**STEP)
    param_new = param - rate * (
        first_hat / (jnp.sqrt(second_hat) + adam_epsilon) + weight_decay * param
    )
    return (param_new, first_new, second_new)


ROWS = 4 * BUCKET
TAIL_RATE = 0.28
TAIL_SERIES = (
    0.11615256574707405,
    0.06981038475559553,
    0.2631359597579608,
    -0.22983675561378278,
    0.38546775012288165,
    -0.10472989053809521,
)
INV_SQRT_TAU = 0.3989422804014327
ALLOWED = 3.0e38
BARRED = -1000000000.0


def dot(left, right):
    return jnp.dot(left, right, preferred_element_type=jnp.float32)


def dot_back(left, right):
    return lax.dot_general(
        left, right, (((1,), (1,)), ((), ())), preferred_element_type=jnp.float32
    )


def outer(left, right):
    return lax.dot_general(
        left, right, (((0,), (0,)), ((), ())), preferred_element_type=jnp.float32
    )


def passage_facts(counts, lengths, position):
    places = lengths.shape[1]
    big_end = counts[0, 0]
    mid_end = big_end + counts[0, 1]
    all_end = mid_end + counts[0, 2]
    start = jnp.int32(0)
    member = jnp.zeros(position.shape, jnp.int32)
    usable = jnp.zeros(position.shape, jnp.int32)
    for number in range(places):
        size = jnp.where(
            number < big_end,
            4 * BUCKET,
            jnp.where(number < mid_end, 2 * BUCKET, jnp.where(number < all_end, BUCKET, 0)),
        )
        inside = (position >= start) & (position < start + size)
        live = inside & (position < start + lengths[0, number])
        member = jnp.where(inside, number + 1, member)
        usable = jnp.where(live, 1, usable)
        start = start + size
    passage = jnp.where(member > 0, member - 1, places + position // BUCKET)
    return usable, passage


def normalize(values):
    center = jnp.mean(values, -1, keepdims=True)
    centered = values - center
    spread = jnp.mean(centered * centered, -1, keepdims=True)
    inverse = lax.rsqrt(spread + norm_epsilon)
    return centered * inverse, inverse


def normalize_back(grad, hat, inverse):
    center = jnp.mean(grad, -1, keepdims=True)
    along = jnp.mean(grad * hat, -1, keepdims=True)
    return inverse * (grad - center - hat * along)


def columns_total(values):
    return jnp.sum(values, 0, keepdims=True)


def attention_caps(counts, lengths, block):
    at_row = lax.broadcasted_iota(jnp.int32, (ROWS, 1), 0) + block * ROWS
    at_column = lax.broadcasted_iota(jnp.int32, (1, ROWS), 1) + block * ROWS
    _, passage_row = passage_facts(counts, lengths, at_row)
    usable_column, passage_column = passage_facts(counts, lengths, at_column)
    allowed = (passage_row == passage_column) & ((usable_column == 1) | (at_row == at_column))
    return jnp.where(allowed, ALLOWED, BARRED)


def attend_quad(quad, weight, x_ref, vec_ref, cap_ref, q_ref, k_ref, v_ref, p_ref, ctx_ref):
    cols = pl.ds(pl.multiple_of(quad * 256, 256), 256)
    x = x_ref[...]
    query = (dot(x, weight(0, cols)) + vec_ref[0:1, cols]).astype(jnp.bfloat16)
    query = query * jnp.bfloat16(0.125)
    keyed = dot(x, weight(1, cols)).astype(jnp.bfloat16)
    valued = (dot(x, weight(2, cols)) + vec_ref[1:2, cols]).astype(jnp.bfloat16)
    q_ref[...] = query
    k_ref[...] = keyed
    v_ref[...] = valued
    low_half = lax.broadcasted_iota(jnp.int32, (1, 128), 1) < 64
    for pair in range(2):
        part = slice(128 * pair, 128 * pair + 128)
        contexts = []
        for head in range(2):
            here = low_half if head == 0 else ~low_half
            mine = jnp.where(here, query[:, part], jnp.zeros_like(query[:, part]))
            scores = jnp.minimum(dot_back(mine, keyed[:, part]), cap_ref[...])
            exponent = jnp.exp(scores - jnp.max(scores, -1, keepdims=True))
            inverse = 1.0 / jnp.sum(exponent, -1, keepdims=True)
            probability = (exponent * inverse).astype(jnp.bfloat16)
            p_ref[0, 2 * pair + head] = probability
            contexts.append(dot(probability, valued[:, part]))
        both = jnp.where(low_half, contexts[0], contexts[1]).astype(jnp.bfloat16)
        ctx_ref[:, pl.ds(pl.multiple_of(quad * 256 + 128 * pair, 128), 128)] = both


def close_block(w_out, x_ref, vec_ref, ctx_ref, hat_ref, inverse_ref):
    branch = dot(ctx_ref[...], w_out) + vec_ref[2:3, :]
    hat_ref[...], inverse_ref[...] = normalize(x_ref[...].astype(jnp.float32) + branch)


def attend_back_pair(pair, here, p_ref, qkv, ctx_ref, grad_ctx_ref, pulled, half, add_sums):
    low_half = lax.broadcasted_iota(jnp.int32, (1, 128), 1) < 64
    cols = pl.ds(pl.multiple_of(pair * 128, 128), 128)
    query, keyed, valued = qkv
    pull = grad_ctx_ref[here, cols]
    along = pull.astype(jnp.float32) * ctx_ref[here, cols].astype(jnp.float32)
    by_query, by_key, by_value = [], [], []
    for head in range(2):
        mask = low_half if head == 0 else ~low_half
        mine = jnp.where(mask, pull, jnp.zeros_like(pull))
        level = jnp.sum(jnp.where(mask, along, 0.0), -1, keepdims=True)
        probability = p_ref[head]
        grad_prob = dot_back(mine, valued)
        grad_scores = (probability.astype(jnp.float32) * (grad_prob - level)).astype(jnp.bfloat16)
        by_query.append(dot(grad_scores, keyed))
        by_key.append(outer(grad_scores, query))
        by_value.append(outer(probability, pull))
    grad_query = (jnp.where(low_half, by_query[0], by_query[1]) * 0.125).astype(jnp.bfloat16)
    grad_value = jnp.where(low_half, by_value[0], by_value[1]).astype(jnp.bfloat16)
    pulled[0, here, half] = grad_query
    pulled[1, here, half] = jnp.where(low_half, by_key[0], by_key[1]).astype(jnp.bfloat16)
    pulled[2, here, half] = grad_value
    add_sums(cols, columns_total(grad_query.astype(jnp.float32)), columns_total(grad_value.astype(jnp.float32)))


def gelu_parts(up):
    near = 1.0 / (1.0 + TAIL_RATE * jnp.abs(up))
    decay = jnp.exp(up * up * -0.5)
    series = jnp.full_like(near, TAIL_SERIES[-1])
    for term in TAIL_SERIES[-2::-1]:
        series = series * near + term
    tail = series * near * decay
    share = jnp.where(up < 0.0, tail, 1.0 - tail)
    slope = share + up * (decay * INV_SQRT_TAU)
    return (up * share).astype(jnp.bfloat16), slope


def attend_forward(
    counts,
    lengths,
    x_ref,
    w_hbm,
    vec_ref,
    q_ref,
    k_ref,
    v_ref,
    p_ref,
    ctx_ref,
    hat_ref,
    inverse_ref,
    w_buf,
    cap_ref,
    w_sem,
):
    block, quad = pl.program_id(0), pl.program_id(1)
    loads = [pltpu.make_async_copy(w_hbm.at[at], w_buf.at[at], w_sem.at[at]) for at in range(4)]

    @pl.when((block == 0) & (quad == 0))
    def _():
        for load in loads:
            load.start()
        for load in loads:
            load.wait()

    @pl.when(quad == 0)
    def _():
        cap_ref[...] = attention_caps(counts, lengths, block)

    def weight(at, cols):
        return w_buf[at, :, cols]

    attend_quad(quad, weight, x_ref, vec_ref, cap_ref, q_ref, k_ref, v_ref, p_ref, ctx_ref)

    @pl.when(quad == 2)
    def _():
        close_block(w_buf[3], x_ref, vec_ref, ctx_ref, hat_ref, inverse_ref)


def attended(counts, lengths, x, weights, vectors):
    tokens, width = x.shape
    blocks = tokens // ROWS
    low = jnp.bfloat16
    smem = pl.BlockSpec(memory_space=pltpu.SMEM)
    quad = pl.BlockSpec((ROWS, 256), lambda b, h: (b, h))
    rows = pl.BlockSpec((ROWS, width), lambda b, h: (b, 0))
    shaped = jax.ShapeDtypeStruct
    return pl.pallas_call(
        attend_forward,
        grid=(blocks, 3),
        out_shape=(
            shaped((tokens, width), low),
            shaped((tokens, width), low),
            shaped((tokens, width), low),
            shaped((blocks, HEADS, ROWS, ROWS), low),
            shaped((tokens, width), low),
            shaped((tokens, width), jnp.float32),
            shaped((tokens, 1), jnp.float32),
        ),
        in_specs=[
            smem,
            smem,
            rows,
            pl.BlockSpec(memory_space=pl.ANY),
            pl.BlockSpec((VROWS, width), lambda b, h: (0, 0)),
        ],
        out_specs=(
            quad,
            quad,
            quad,
            pl.BlockSpec((1, 4, ROWS, ROWS), lambda b, h: (b, h, 0, 0)),
            rows,
            rows,
            pl.BlockSpec((ROWS, 1), lambda b, h: (b, 0)),
        ),
        scratch_shapes=[
            pltpu.VMEM((4, width, width), low),
            pltpu.VMEM((ROWS, ROWS), jnp.float32),
            pltpu.SemaphoreType.DMA((4,)),
        ],
        compiler_params=pltpu.CompilerParams(vmem_limit_bytes=56 * 2**20),
        name="attend_forward",
    )(counts, lengths, x, weights, vectors)


def feed_forward_both(
    counts,
    lengths,
    hat_ref,
    inverse_ref,
    cot_ref,
    w_hbm,
    vec_ref,
    mixed_ref,
    first_ref,
    branch_ref,
    context_ref,
    up_grad_ref,
    down_grad_ref,
    sum_ref,
    w_buf,
    active_ref,
    up_ref,
    hidden_ref,
    down_ref,
    slope_ref,
    w_sem,
):
    step = pl.program_id(0)
    blocks = pl.num_programs(0) - 4
    loads = [
        pltpu.make_async_copy(w_hbm.at[3 + at], w_buf.at[at], w_sem.at[at]) for at in range(9)
    ]

    @pl.when(step == 0)
    def _():
        for load in loads[1:] + loads[:1]:
            load.start()
        sum_ref[...] = jnp.zeros_like(sum_ref)
        for load in loads[1:] + loads[:1]:
            load.wait()

    @pl.when(step < blocks)
    def _():
        here = pl.ds(pl.multiple_of(step * ROWS, ROWS), ROWS)
        at_row = lax.broadcasted_iota(jnp.int32, (ROWS, 1), 0) + step * ROWS
        live = passage_facts(counts, lengths, at_row)[0].astype(jnp.float32)
        hat = hat_ref[...]
        hidden = hat * vec_ref[10:11, :] + vec_ref[8:9, :]
        hidden_low = hidden.astype(jnp.bfloat16)
        hidden_ref[here, :] = hidden_low
        total = hidden + vec_ref[7:8, :]
        for tile in range(4):
            up = dot(hidden_low, w_buf[1 + tile]) + vec_ref[3 + tile : 4 + tile, :]
            active, slope = gelu_parts(up)
            slope_ref[tile] = slope.astype(jnp.bfloat16)
            active_ref[tile, here, :] = active
            total = total + dot(active, w_buf[5 + tile])
        hat_two, inverse_two = normalize(total)
        mixed_ref[...] = ((hat_two * vec_ref[11:12, :] + vec_ref[9:10, :]) * live).astype(jnp.bfloat16)
        grad_out = cot_ref[...].astype(jnp.float32) * live
        sum_ref[11:12, :] += columns_total(grad_out * hat_two)
        sum_ref[9:10, :] += columns_total(grad_out)
        second = normalize_back(grad_out * vec_ref[11:12, :], hat_two, inverse_two)
        down_low = second.astype(jnp.bfloat16)
        down_ref[here, :] = down_low
        sum_ref[7:8, :] += columns_total(down_low.astype(jnp.float32))
        grad_hidden = second
        for tile in range(4):
            pulled = dot_back(down_low, w_buf[5 + tile])
            up_low = (pulled * slope_ref[tile].astype(jnp.float32)).astype(jnp.bfloat16)
            up_ref[tile, here, :] = up_low
            sum_ref[3 + tile : 4 + tile, :] += columns_total(up_low.astype(jnp.float32))
            grad_hidden = grad_hidden + dot_back(up_low, w_buf[1 + tile])
        sum_ref[10:11, :] += columns_total(grad_hidden * hat)
        sum_ref[8:9, :] += columns_total(grad_hidden)
        grad_first = normalize_back(grad_hidden * vec_ref[10:11, :], hat, inverse_ref[...])
        first_ref[...] = grad_first
        branch_low = grad_first.astype(jnp.bfloat16)
        branch_ref[...] = branch_low
        sum_ref[2:3, :] += columns_total(branch_low.astype(jnp.float32))
        context_ref[...] = dot_back(branch_low, w_buf[0]).astype(jnp.bfloat16)

    @pl.when(step >= blocks)
    def _():
        tile = step - blocks
        up_grad_ref[0] = outer(hidden_ref[...], up_ref[tile]).astype(jnp.bfloat16)
        down_grad_ref[0] = outer(active_ref[tile], down_ref[...]).astype(jnp.bfloat16)


def fed_forward_both(counts, lengths, hat, inverse, cotangent, weights, vectors):
    tokens, width = hat.shape
    blocks = tokens // ROWS
    low = jnp.bfloat16
    smem = pl.BlockSpec(memory_space=pltpu.SMEM)
    shaped = jax.ShapeDtypeStruct

    def block_of(step):
        return jnp.minimum(step, blocks - 1)

    def tile_of(step):
        return jnp.maximum(step - blocks, 0)

    rows = pl.BlockSpec((ROWS, width), lambda i: (block_of(i), 0))
    tile = pl.BlockSpec((1, width, width), lambda i: (tile_of(i), 0, 0))
    return pl.pallas_call(
        feed_forward_both,
        grid=(blocks + 4,),
        out_shape=(
            shaped((tokens, width), low),
            shaped((tokens, width), jnp.float32),
            shaped((tokens, width), low),
            shaped((tokens, width), low),
            shaped((4, width, width), low),
            shaped((4, width, width), low),
            shaped((16, width), jnp.float32),
        ),
        in_specs=[
            smem,
            smem,
            rows,
            pl.BlockSpec((ROWS, 1), lambda i: (block_of(i), 0)),
            rows,
            pl.BlockSpec(memory_space=pl.ANY),
            pl.BlockSpec((VROWS, width), lambda i: (0, 0)),
        ],
        out_specs=(
            rows,
            rows,
            rows,
            rows,
            tile,
            tile,
            pl.BlockSpec((16, width), lambda i: (0, 0)),
        ),
        scratch_shapes=[
            pltpu.VMEM((9, width, width), low),
            pltpu.VMEM((4, tokens, width), low),
            pltpu.VMEM((4, tokens, width), low),
            pltpu.VMEM((tokens, width), low),
            pltpu.VMEM((tokens, width), low),
            pltpu.VMEM((4, ROWS, width), low),
            pltpu.SemaphoreType.DMA((9,)),
        ],
        compiler_params=pltpu.CompilerParams(vmem_limit_bytes=60 * 2**20),
        name="feed_forward_both",
    )(counts, lengths, hat, inverse, cotangent, weights, vectors)


def attend_backward(
    p_ref,
    q_ref,
    k_ref,
    v_ref,
    x_ref,
    ctx_ref,
    grad_ctx_ref,
    branch_ref,
    first_ref,
    w_ref,
    input_ref,
    grad_ref,
    sum_ref,
    pulled,
):
    step = pl.program_id(0)
    quad, block = step // 2, lax.rem(step, 2)
    here = pl.ds(pl.multiple_of(block * ROWS, ROWS), ROWS)
    cols = pl.ds(pl.multiple_of(quad * 256, 256), 256)

    @pl.when(step == 0)
    def _():
        sum_ref[...] = jnp.zeros_like(sum_ref)
        input_ref[...] = first_ref[...]

    def add_sums(at, by_query, by_value):
        sum_ref[0:1, at] += by_query
        sum_ref[1:2, at] += by_value

    for pair in range(2):
        half = slice(128 * pair, 128 * pair + 128)
        qkv = q_ref[:, half], k_ref[:, half], v_ref[:, half]
        heads = p_ref.at[0, pl.ds(2 * pair, 2)]
        attend_back_pair(2 * quad + pair, here, heads, qkv, ctx_ref, grad_ctx_ref, pulled, half, add_sums)
    more = input_ref[here, :]
    for at in range(3):
        more = more + dot_back(pulled[at, here, :], w_ref[at, :, cols])
    input_ref[here, :] = more

    @pl.when(block == 1)
    def _():
        for tile in range(3):
            grad_ref[tile, :, cols] = outer(x_ref[...], pulled[tile]).astype(jnp.bfloat16)
        grad_ref[3, :, cols] = outer(ctx_ref[...], branch_ref[:, cols]).astype(jnp.bfloat16)


def attended_back(probs, query, keyed, valued, x, context, grad_context, grad_branch, grad_first, weights):
    tokens, width = x.shape
    low = jnp.bfloat16
    shaped = jax.ShapeDtypeStruct
    once = pl.Buffered(1)
    quad = pl.BlockSpec((ROWS, 256), lambda i: (lax.rem(i, 2), i // 2))
    whole = pl.BlockSpec((tokens, width), lambda i: (0, 0), pipeline_mode=once)
    return pl.pallas_call(
        attend_backward,
        grid=(6,),
        out_shape=(
            shaped((tokens, width), jnp.float32),
            shaped((4, width, width), low),
            shaped((16, width), jnp.float32),
        ),
        in_specs=[
            pl.BlockSpec((1, 4, ROWS, ROWS), lambda i: (lax.rem(i, 2), i // 2, 0, 0)),
            quad,
            quad,
            quad,
            whole,
            whole,
            whole,
            whole,
            whole,
            pl.BlockSpec((3, width, width), lambda i: (0, 0, 0), pipeline_mode=once),
        ],
        out_specs=(
            whole,
            pl.BlockSpec((4, width, width), lambda i: (0, 0, 0), pipeline_mode=once),
            pl.BlockSpec((16, width), lambda i: (0, 0)),
        ),
        scratch_shapes=[pltpu.VMEM((3, tokens, 256), low)],
        compiler_params=pltpu.CompilerParams(vmem_limit_bytes=56 * 2**20),
        name="attend_backward",
    )(probs, query, keyed, valued, x, context, grad_context, grad_branch, grad_first, weights)


def moved(param, grad, first, second, average, rate):
    param_new, first_new, second_new = adam_update(param, grad, first, second, rate)
    return param_new, first_new, second_new, average_rate * average + (1.0 - average_rate) * param_new


def update_kernel(
    gain_scale,
    grad_ref,
    master_ref,
    first_ref,
    second_ref,
    ema_ref,
    vec_grad_ref,
    bias_ref,
    gain_ref,
    vec_first_ref,
    vec_second_ref,
    vec_ema_ref,
    mixed_in,
    input_in,
    master_out,
    first_out,
    second_out,
    ema_out,
    copy_out,
    vec_out,
    vec_first_out,
    vec_second_out,
    vec_ema_out,
    mixed_out,
    input_out,
    vec_ref,
):
    mixed_out[...] = mixed_in[...]
    input_out[...] = input_in[...]

    @pl.when((pl.program_id(0) == 0) & (pl.program_id(1) == 0))
    def _():
        vec_ref[0:10, :] = bias_ref[...]
        vec_ref[10:12, :] = gain_ref[...]
        vec_grad = vec_grad_ref[0:VROWS, :] * gain_scale
        vec_out[...], vec_first_out[...], vec_second_out[...], vec_ema_out[...] = moved(
            vec_ref[...], vec_grad, vec_first_ref[...], vec_second_ref[...], vec_ema_ref[...], vector_rate
        )

    grad = grad_ref[...].astype(jnp.float32) * gain_scale
    result = moved(master_ref[0], grad, first_ref[0], second_ref[0], ema_ref[0], tile_rate)
    master_out[0], first_out[0], second_out[0], ema_out[0] = result
    copy_out[0] = result[0].astype(jnp.bfloat16)


def updated(
    gain_scale,
    slot_grads,
    master,
    first,
    second,
    ema,
    vec_grad,
    bias,
    gain,
    vec_first,
    vec_second,
    vec_ema,
    mixed,
    input_grad,
):
    width = master.shape[-1]
    chunk = 192
    tile = pl.BlockSpec((1, 1, chunk, width), lambda s, r: (0, s, r, 0))
    steps = width // chunk
    rows = pl.BlockSpec((mixed.shape[0] // (SLOTS * steps), width), lambda s, r: (s * steps + r, 0))

    def whole(value):
        return pl.BlockSpec(value.shape, lambda s, r: (0, 0))

    shaped = jax.ShapeDtypeStruct
    tile_shape = shaped(master.shape, jnp.float32)
    vec_shape = shaped((VROWS, width), jnp.float32)
    results = pl.pallas_call(
        functools.partial(update_kernel, gain_scale),
        grid=(SLOTS, steps),
        out_shape=(tile_shape,) * 4
        + (shaped(master.shape, jnp.bfloat16),)
        + (vec_shape,) * 4
        + (shaped(mixed.shape, mixed.dtype), shaped(input_grad.shape, input_grad.dtype)),
        in_specs=[pl.BlockSpec((1, chunk, width), lambda s, r: (s, r, 0))]
        + [tile] * 4
        + [whole(value) for value in (vec_grad, bias, gain, vec_first, vec_second, vec_ema)]
        + [rows] * 2,
        out_specs=(tile,) * 5 + (whole(vec_first),) * 4 + (rows,) * 2,
        scratch_shapes=[pltpu.VMEM((VROWS, width), jnp.float32)],
        compiler_params=pltpu.CompilerParams(vmem_limit_bytes=62 * 2**20),
        name="update",
    )(
        slot_grads,
        master,
        first,
        second,
        ema,
        vec_grad,
        bias,
        gain,
        vec_first,
        vec_second,
        vec_ema,
        mixed,
        input_grad,
    )
    return results[-2:] + results[:-2]


MESH = pl.DeviceIdType.MESH
GROUP = 32
PAIRS = TILES // 2
PLANE = 8
PIECE = 96
PAIR_TILES = ((0, 1), (2, 3), (4, 8), (5, 9), (6, 10), (7, 11))
EARLY = 2
WHOLE = 3


def remote(src, dst, send, recv, device):
    return pltpu.make_async_remote_copy(
        src_ref=src, dst_ref=dst, send_sem=send, recv_sem=recv, device_id=(device,), device_id_type=MESH
    )


def place(device):
    core = lax.rem(device, 2)
    x = lax.rem(device // 2, 2)
    y = lax.rem(device // 4, 2)
    z = device // 8
    return z, y, x, core


def start(copies):
    for copy in copies:
        copy.start()


def arrive(copies):
    for copy in copies:
        copy.wait_recv()


def greet(z, in_plane):
    barrier = pltpu.get_barrier_semaphore()
    for hop in range(1, PLANE):
        other = z * PLANE + lax.rem(in_plane + hop, PLANE)
        pl.semaphore_signal(barrier, inc=1, device_id=(other,), device_id_type=MESH)
    for hop in range(1, 4):
        other = lax.rem(z + hop, 4) * PLANE + in_plane
        pl.semaphore_signal(barrier, inc=1, device_id=(other,), device_id_type=MESH)
    pl.semaphore_wait(barrier, PLANE + 2)


def along_z(z, in_plane):
    inner = (1 + z // 2) * PLANE + in_plane
    other_middle = (3 - z) * PLANE + in_plane
    outer_end = lax.rem(lax.rem(z + 3, 4) * 3, 4) * PLANE + in_plane
    return inner, other_middle, outer_end


def third(part):
    return slice(None) if part == WHOLE else pl.ds(256 * part, 256)


POSITIONS = [tile for pair in PAIR_TILES for tile in pair]


def slot_number(owners, tile):
    number = jnp.int32(0)
    for earlier in range(tile):
        number = number + jnp.where(owners[earlier] == owners[tile], 1, 0)
    return number


def unit(pair, part):
    return 3 * pair + part if pair < EARLY else 2 * EARLY + pair


UNITS = [(pair, part) for pair in range(EARLY) for part in range(3)]
UNITS += [(pair, WHOLE) for pair in range(EARLY, PAIRS)]

FRONT_PLAN = (
    (
        ("open",),
        ("swap", 0),
        ("caps",),
        ("sent", 0),
        ("swap", 1),
        ("choose", 0),
        ("end", 1, 0),
        ("middle", 1, 0),
        ("sent", 1),
        ("swap", 2),
        ("choose", 1),
        ("end", 0, 0),
        ("total", 1, 0),
        ("middle", 0, 0),
        ("end", 0, 1),
        ("end", 1, 1),
        ("choose", 2),
        ("end", 1, 2),
        ("mid", 1, 0),
        ("middle", 1, 1),
        ("total", 1, 1),
        ("middle", 0, 1),
        ("end", 2),
        ("total", 0, 0),
        ("end", 0, 2),
        ("mid", 0, 0),
        ("mid", 1, 1),
        ("far", 1, 0),
        ("middle", 0, 2),
        ("total", 0, 1),
        ("end", 4),
        ("middle", 1, 2),
        ("mid", 0, 1),
        ("far", 0, 0),
        ("middle", 2),
        ("total", 0, 2),
        ("far", 0, 1),
        ("total", 1, 2),
        ("end", 3),
        ("near", 0, 0),
        ("near", 1, 0),
        ("mid", 1, 2),
        ("middle", 4),
        ("near", 0, 1),
        ("finish", 0, 0),
        ("far", 1, 2),
        ("total", 2),
        ("mid", 0, 2),
        ("far", 0, 2),
        ("mid", 2),
        ("finish", 0, 1),
        ("far", 1, 1),
        ("end", 5),
        ("middle", 3),
        ("near", 1, 2),
        ("total", 4),
        ("finish", 1, 0),
    ),
    (
        ("near", 1, 1),
        ("near", 0, 2),
        ("mid", 4),
        ("total", 3),
        ("far", 2),
        ("middle", 5),
    ),
    (
        ("mid", 3),
        ("total", 5),
        ("finish", 1, 1),
    ),
    (
        ("finish", 1, 2),
        ("keep", 1),
        ("far", 3),
    ),
    (
        ("finish", 0, 2),
        ("keep", 0),
        ("near", 2),
        ("mid", 5),
    ),
    (
        ("far", 4),
        ("finish", 2),
        ("keep", 2),
    ),
    (
        ("near", 3),
        ("far", 5),
    ),
    (
        ("finish", 3),
        ("keep", 3),
        ("near", 4),
    ),
    (
        ("near", 5),
        ("finish", 4),
        ("keep", 4),
    ),
    (
        ("finish", 5),
        ("keep", 5),
    ),
)


def gather_and_forward(
    counts,
    lengths,
    owners,
    bias_ref,
    gain_ref,
    x_hbm,
    cot_hbm,
    master_hbm,
    q_ref,
    k_ref,
    v_ref,
    p_ref,
    ctx_hbm,
    hidden_hbm,
    active_hbm,
    slope_hbm,
    down_hbm,
    mixed_hbm,
    second_hbm,
    hat_hbm,
    w_out,
    inverse_ref,
    sum_ref,
    vec_ref,
    cap_ref,
    wide,
    low,
    stage_a,
    stage_b,
    stage_c,
    chosen,
    from_end,
    from_middle,
    w_buf,
    x_then_hidden,
    ctx_ref,
    cot_then_down,
    mixed_ref,
    hat_ref,
    slope_buf,
    active_buf,
    load_sem,
    store_sem,
    tile_sem,
    out_sem,
    swap_send,
    swap_recv,
    z_send,
    z_recv,
    mid_send,
    mid_recv,
    far_send,
    far_recv,
    near_send,
    near_recv,
):
    step = pl.program_id(0)
    width = 8 * PIECE
    me = lax.axis_index("dp")
    z, y, x, core = place(me)
    in_plane = lax.rem(me, PLANE)
    sibling = me + 1 - 2 * core
    x_peer = me + 2 - 4 * x
    y_peer = me + 4 - 8 * y
    z_targets = along_z(z, in_plane)
    stages = (stage_a, stage_b, stage_c)
    is_end = (z == 0) | (z == 3)
    is_middle = (z == 1) | (z == 2)

    def piece_rows(cell_core, cell_x, cell_y):
        return pl.ds(pl.multiple_of(((cell_core * 2 + cell_x) * 2 + cell_y) * PIECE, 16), PIECE)

    def swap(part):
        def send(hop, carry):
            target = lax.rem(in_plane + hop, PLANE)
            _, ty, tx, tc = place(target)
            remote(
                low.at[:, piece_rows(tc, tx, ty), third(part)],
                stages[part].at[pl.ds(2 * in_plane, 2)],
                swap_send.at[part],
                swap_recv.at[part],
                z * PLANE + target,
            ).start()
            return carry

        lax.fori_loop(1, PLANE, send, 0)

    def swap_wait(part, sem):
        most = stages[part].at[pl.ds(0, 2 * PLANE - 2)]
        pltpu.make_async_copy(most, most, sem.at[part]).wait()

    def z_copy(pair, part, level):
        two = pl.ds(2 * pair, 2)
        cols = third(part)
        src = w_buf.at[two, core, x, y, :, cols] if level == 2 else chosen.at[two, :, cols]
        dst = (from_end.at[two, :, cols], from_middle.at[two, :, cols], src)[level]
        at = unit(pair, part)
        return remote(src, dst, z_send.at[level, at], z_recv.at[level, at], z_targets[level])

    def z_end(pair, part=WHOLE):
        @pl.when(is_end)
        def _():
            z_copy(pair, part, 0).start()

    def z_middle(pair, part=WHOLE):
        @pl.when(is_middle)
        def _():
            z_copy(pair, part, 0).wait_recv()
            two, cols = pl.ds(2 * pair, 2), third(part)
            chosen[two, :, cols] = chosen[two, :, cols] + from_end[two, :, cols]
            z_copy(pair, part, 1).start()

    def z_total(pair, part=WHOLE):
        @pl.when(is_middle)
        def _():
            z_copy(pair, part, 1).wait_recv()
            two, cols = pl.ds(2 * pair, 2), third(part)
            w_buf[two, core, x, y, :, cols] = chosen[two, :, cols] + from_middle[two, :, cols]
            z_copy(pair, part, 2).start()

    def mid_copies(pair, part):
        copies = []
        for n, peer in enumerate((y_peer, x_peer)):
            spot = w_buf.at[2 * pair + n, core, x, y, :, third(part)]
            at = unit(pair, part), n
            copies.append(remote(spot, spot, mid_send.at[at], mid_recv.at[at], peer))
        return copies

    def halves(pair, part, late):
        row = 1 - x if late else x
        column = 1 - y if late else y
        cols = third(part)
        return w_buf.at[2 * pair, core, row, :, :, cols], w_buf.at[2 * pair + 1, core, :, column, :, cols]

    def far_copies(pair, part):
        copies = []
        for n, peer in enumerate((x_peer, y_peer)):
            spot = halves(pair, part, False)[n]
            at = unit(pair, part), n
            copies.append(remote(spot, spot, far_send.at[at], far_recv.at[at], peer))
        return copies

    def near_copies(pair, part, late):
        copies = []
        for n in range(2):
            spot = halves(pair, part, late)[n]
            at = unit(pair, part), n, late
            copies.append(remote(spot, spot, near_send.at[at], near_recv.at[at], sibling))
        return copies

    def give_mid(pair, part=WHOLE):
        @pl.when(is_end)
        def _():
            z_copy(pair, part, 2).wait_recv()

        start(mid_copies(pair, part))

    def give_far(pair, part=WHOLE):
        arrive(mid_copies(pair, part))
        start(far_copies(pair, part) + near_copies(pair, part, 0))

    def give_near(pair, part=WHOLE):
        arrive(far_copies(pair, part))
        start(near_copies(pair, part, 1))

    def finish(pair, part=WHOLE):
        arrive(near_copies(pair, part, 0) + near_copies(pair, part, 1))

    def choose(part):
        swap_wait(part, swap_recv)
        for pair in range(PAIRS):
            for n, tile in enumerate(PAIR_TILES[pair]):
                owner = owners[tile]
                value = stages[part][SLOTS * lax.rem(owner, PLANE) + slot_number(owners, tile)]
                chosen[2 * pair + n, :, third(part)] = jnp.where(
                    owner // PLANE == z, value, jnp.zeros_like(value)
                )

    def load(at):
        src = (x_hbm, cot_hbm, master_hbm)[at]
        dst = (x_then_hidden, cot_then_down, wide)[at]
        return pltpu.make_async_copy(src, dst, load_sem.at[at])

    def store(at):
        src, dst = (
            (x_then_hidden, hidden_hbm),
            (ctx_ref, ctx_hbm),
            (hat_ref, hat_hbm),
            (cot_then_down, down_hbm),
            (mixed_ref, mixed_hbm),
            (wide, second_hbm),
        )[at]
        src = src.at[pl.ds(0, 2 * ROWS)] if src is wide else src
        return pltpu.make_async_copy(src, dst, store_sem.at[at])

    def w_store(pair):
        two = pl.ds(2 * pair, 2)
        return pltpu.make_async_copy(w_buf.at[two], w_out.at[two], out_sem.at[pair])

    def weight(at, cols=slice(None)):
        value = w_buf[at, :, :, :, :, cols]
        return value.reshape(width, value.shape[-1])

    def open_all():
        for at in range(3):
            load(at).start()
        sum_ref[...] = jnp.zeros_like(sum_ref)
        vec_ref[0:10, :] = bias_ref[...]
        vec_ref[10:12, :] = gain_ref[...]
        greet(z, in_plane)
        load(2).wait()
        for slot in range(SLOTS):
            low[slot] = wide[width * slot : width * (slot + 1), :].astype(jnp.bfloat16)
        for part in range(3):
            stages[part][pl.ds(2 * in_plane, 2)] = low[:, piece_rows(core, x, y), third(part)]

    def make_caps():
        for block in range(2):
            cap_ref[block] = attention_caps(counts, lengths, block)
        load(0).wait()
        load(1).wait()

    actions = {
        "open": open_all,
        "caps": make_caps,
        "swap": swap,
        "sent": lambda part: swap_wait(part, swap_send),
        "choose": choose,
        "end": z_end,
        "middle": z_middle,
        "total": z_total,
        "mid": give_mid,
        "far": give_far,
        "near": give_near,
        "finish": finish,
        "keep": lambda pair: w_store(pair).start(),
    }

    for at, work in enumerate(FRONT_PLAN):

        @pl.when(step == at)
        def _():
            for name, *rest in work:
                actions[name](*rest)

    quad, block = step // 2, lax.rem(step, 2)
    here = pl.ds(pl.multiple_of(block * ROWS, ROWS), ROWS)

    @pl.when(step < 6)
    def _():
        attend_quad(
            quad,
            weight,
            x_then_hidden.at[here],
            vec_ref,
            cap_ref.at[block],
            q_ref,
            k_ref,
            v_ref,
            p_ref,
            ctx_ref.at[here],
        )

    @pl.when((step >= 4) & (step < 6))
    def _():
        branch = dot(ctx_ref[here, :], weight(3)) + vec_ref[2:3, :]
        hat, inverse = normalize(x_then_hidden[here, :].astype(jnp.float32) + branch)
        hat_ref[here, :] = hat.astype(jnp.bfloat16)
        inverse_ref[here, :] = inverse
        hidden = hat * vec_ref[10:11, :] + vec_ref[8:9, :]
        x_then_hidden[here, :] = hidden.astype(jnp.bfloat16)
        wide[here, :] = hidden + vec_ref[7:8, :]

    @pl.when(step == 5)
    def _():
        start([store(0), store(1), store(2)])

    turn = step - 6
    slot = lax.rem(turn, 2)

    def tile_stores(source_slot, tile):
        return [
            pltpu.make_async_copy(src.at[source_slot], dst.at[tile], tile_sem.at[source_slot, at])
            for at, (src, dst) in enumerate(((active_buf, active_hbm), (slope_buf, slope_hbm)))
        ]

    @pl.when(turn >= 2)
    def _():
        for copy in tile_stores(slot, 0):
            copy.wait()

    @pl.when(turn >= 0)
    def _():
        for half in range(2):
            rows = slice(ROWS * half, ROWS * half + ROWS)
            up = dot(x_then_hidden[rows, :], weight(4 + 2 * turn)) + vec_ref[pl.ds(3 + turn, 1), :]
            active, slope = gelu_parts(up)
            slope_buf[slot, rows, :] = slope.astype(jnp.bfloat16)
            active_buf[slot, rows, :] = active
            wide[rows, :] = wide[rows, :] + dot(active, weight(5 + 2 * turn))
        start(tile_stores(slot, turn))

    @pl.when(step == 9)
    def _():
        for half in range(2):
            rows = slice(ROWS * half, ROWS * half + ROWS)
            at_row = lax.broadcasted_iota(jnp.int32, (ROWS, 1), 0) + half * ROWS
            live = passage_facts(counts, lengths, at_row)[0].astype(jnp.float32)
            hat, inverse = normalize(wide[rows, :])
            mixed = (hat * vec_ref[11:12, :] + vec_ref[9:10, :]) * live
            mixed_ref[rows, :] = mixed.astype(jnp.bfloat16)
            grad_out = cot_then_down[rows, :].astype(jnp.float32) * live
            sum_ref[11:12, :] += columns_total(grad_out * hat)
            sum_ref[9:10, :] += columns_total(grad_out)
            second = normalize_back(grad_out * vec_ref[11:12, :], hat, inverse)
            wide[rows, :] = second
            down_low = second.astype(jnp.bfloat16)
            cot_then_down[rows, :] = down_low
            sum_ref[7:8, :] += columns_total(down_low.astype(jnp.float32))
        start([store(3), store(4), store(5)])
        for at in range(2):
            for copy in tile_stores(at, 0):
                copy.wait()
        for pair in range(PAIRS):
            w_store(pair).wait()
        swap_wait(2, swap_send)
        for pair, part in UNITS:
            for copy in mid_copies(pair, part) + far_copies(pair, part):
                copy.wait_send()
            for copy in near_copies(pair, part, 0) + near_copies(pair, part, 1):
                copy.wait_send()

            @pl.when(is_end)
            def _():
                z_copy(pair, part, 0).wait_send()

            @pl.when(is_middle)
            def _():
                z_copy(pair, part, 1).wait_send()
                z_copy(pair, part, 2).wait_send()

        for at in range(6):
            store(at).wait()


def gathered_and_forwarded(counts, lengths, owners, bias, gain, x, cotangent, master):
    tokens, width = x.shape
    blocks = tokens // ROWS
    low, high = jnp.bfloat16, jnp.float32
    smem = pl.BlockSpec(memory_space=pltpu.SMEM)
    any_space = pl.BlockSpec(memory_space=pl.ANY)
    dma = pltpu.SemaphoreType.DMA
    shaped = jax.ShapeDtypeStruct

    def at(step):
        step = jnp.minimum(step, 5)
        return lax.rem(step, 2), step // 2

    quad = pl.BlockSpec((ROWS, 256), at)
    rows = shaped((tokens, width), low)
    cut = (2, 2, 2, PIECE, width)
    units = len(UNITS)
    return pl.pallas_call(
        gather_and_forward,
        grid=(10,),
        out_shape=(
            rows,
            rows,
            rows,
            shaped((blocks, HEADS, ROWS, ROWS), low),
            rows,
            rows,
            shaped((4, tokens, width), low),
            shaped((4, tokens, width), low),
            rows,
            rows,
            shaped((tokens, width), high),
            rows,
            shaped((TILES,) + cut, low),
            shaped((tokens, 1), high),
            shaped((16, width), high),
        ),
        in_specs=[smem] * 3
        + [pl.BlockSpec(bias.shape, lambda i: (0, 0)), pl.BlockSpec(gain.shape, lambda i: (0, 0))]
        + [any_space] * 3,
        out_specs=(quad, quad, quad, pl.BlockSpec((1, 4, ROWS, ROWS), lambda i: (*at(i), 0, 0)))
        + (any_space,) * 9
        + (
            pl.BlockSpec((tokens, 1), lambda i: (0, 0), pipeline_mode=pl.Buffered(1)),
            pl.BlockSpec((16, width), lambda i: (0, 0)),
        ),
        scratch_shapes=[
            pltpu.VMEM((VROWS, width), high),
            pltpu.VMEM((2, ROWS, ROWS), high),
            pltpu.VMEM((SLOTS * width, width), high),
            pltpu.VMEM((SLOTS, width, width), low),
            pltpu.VMEM((2 * PLANE, PIECE, 256), low),
            pltpu.VMEM((2 * PLANE, PIECE, 256), low),
            pltpu.VMEM((2 * PLANE, PIECE, 256), low),
            pltpu.VMEM((TILES, PIECE, width), low),
            pltpu.VMEM((TILES, PIECE, width), low),
            pltpu.VMEM((TILES, PIECE, width), low),
            pltpu.VMEM((TILES,) + cut, low),
            pltpu.VMEM((tokens, width), low),
            pltpu.VMEM((tokens, width), low),
            pltpu.VMEM((tokens, width), low),
            pltpu.VMEM((tokens, width), low),
            pltpu.VMEM((tokens, width), low),
            pltpu.VMEM((2, tokens, width), low),
            pltpu.VMEM((2, tokens, width), low),
            dma((3,)),
            dma((6,)),
            dma((2, 2)),
            dma((PAIRS,)),
            dma((3,)),
            dma((3,)),
            dma((3, units)),
            dma((3, units)),
            dma((units, 2)),
            dma((units, 2)),
            dma((units, 2)),
            dma((units, 2)),
            dma((units, 2, 2)),
            dma((units, 2, 2)),
        ],
        compiler_params=pltpu.CompilerParams(
            collective_id=0, has_side_effects=True, vmem_limit_bytes=63 * 2**20
        ),
        name="gather_and_forward",
    )(counts, lengths, owners, bias, gain, x, cotangent, master.reshape(SLOTS * width, width))


BACK_PLAN = (
    (),
    (),
    (
        ("core", 0),
    ),
    (),
    (
        ("far", 0),
    ),
    (),
    (
        ("core", 1),
    ),
    (
        ("mid", 0),
    ),
    (
        ("core", 3),
        ("core", 2),
        ("far", 1),
        ("end", 0),
    ),
    (),
    (
        ("far", 3),
    ),
    (),
    (
        ("mid", 1),
    ),
    (
        ("middle", 0),
        ("mid", 3),
        ("far", 2),
    ),
    (
        ("end", 1),
    ),
    (
        ("core", 4),
        ("total", 0),
        ("far", 4),
        ("middle", 1),
        ("end", 3),
    ),
    (
        ("middle", 3),
        ("mid", 4),
        ("total", 1),
    ),
    (
        ("mid", 2),
        ("end", 4),
    ),
    (
        ("middle", 4),
        ("core", 5),
        ("end", 2),
        ("total", 3),
    ),
    (
        ("far", 5),
        ("take", 0),
        ("middle", 2),
        ("total", 4),
    ),
    (
        ("take", 1),
        ("core", 6),
        ("mid", 5),
        ("total", 2),
        ("far", 6),
        ("sum", 0),
        ("end", 5),
        ("take", 4),
        ("middle", 5),
        ("mid", 6),
        ("take", 3),
        ("sum", 1),
        ("take", 2),
        ("deliver", 0),
        ("end", 6),
        ("total", 5),
        ("middle", 6),
        ("sum", 2),
        ("take", 5),
        ("deliver", 1),
        ("total", 6),
        ("take", 6),
        ("deliver", 2),
    ),
)


def backward_and_reduce(
    owners,
    p_ref,
    q_ref,
    k_ref,
    v_ref,
    ctx_ref,
    inverse_ref,
    gain_ref,
    late_ref,
    x_hbm,
    hidden_hbm,
    active_hbm,
    slope_hbm,
    down_hbm,
    second_hbm,
    hat_hbm,
    w_hbm,
    input_hbm,
    slot_grad,
    vec_out,
    w_part,
    acc,
    pulled,
    hidden_then_x,
    down_then_branch,
    grad_ctx_ref,
    hat_ref,
    tile_buf,
    up_buf,
    part,
    from_core,
    from_far,
    from_mid,
    from_end,
    from_middle,
    total,
    snap,
    outbox,
    vec_now,
    vec_in,
    holds,
    keeps,
    load_sem,
    w_sem,
    core_send,
    core_recv,
    far_send,
    far_recv,
    mid_send,
    mid_recv,
    z_send,
    z_recv,
    vec_send,
    vec_recv,
    out_send,
    out_recv,
):
    step = pl.program_id(0)
    inner = jnp.maximum(step - 4, 0)
    quad, block, pair = inner // 4, lax.rem(inner, 4) // 2, lax.rem(inner, 2)
    me = lax.axis_index("dp")
    z, y, x, core = place(me)
    in_plane = lax.rem(me, PLANE)
    sibling = me + 1 - 2 * core
    x_peer = me + 2 - 4 * x
    y_peer = me + 4 - 8 * y
    z_targets = along_z(z, in_plane)
    is_end = (z == 0) | (z == 3)
    is_middle = (z == 1) | (z == 2)

    def items(batch):
        if batch < 4:
            return [(0, 4 + 2 * batch, slice(None)), (1, 5 + 2 * batch, slice(None))]
        cols = pl.ds(256 * (batch - 4), 256)
        return [(0, 0, cols), (1, 1, cols), (0, 2, cols), (1, 3, cols)]

    def half_of(tile, side):
        return part.at[tile, side] if tile < 4 else w_part.at[tile, side]

    def held(tile):
        return half_of(tile, core)

    def core_copies(batch):
        return [
            remote(
                half_of(tile, 1 - core).at[:, :, :, cols],
                from_core.at[tile, :, :, :, cols],
                core_send.at[batch, n],
                core_recv.at[batch, n],
                sibling,
            )
            for n, (_, tile, cols) in enumerate(items(batch))
        ]

    def far_copies(batch):
        copies = []
        for n, (kind, tile, cols) in enumerate(items(batch)):
            mine = held(tile)
            copies.append(
                remote(
                    mine.at[:, 1 - y, :, cols] if kind else mine.at[1 - x, :, :, cols],
                    from_far.at[tile, :, :, cols],
                    far_send.at[batch, n],
                    far_recv.at[batch, n],
                    y_peer if kind else x_peer,
                )
            )
        return copies

    def mid_copies(batch):
        copies = []
        for n, (kind, tile, cols) in enumerate(items(batch)):
            mine = held(tile)
            copies.append(
                remote(
                    mine.at[1 - x, y, :, cols] if kind else mine.at[x, 1 - y, :, cols],
                    from_mid.at[tile, :, cols],
                    mid_send.at[batch, n],
                    mid_recv.at[batch, n],
                    x_peer if kind else y_peer,
                )
            )
        return copies

    def z_copies(batch, stage):
        copies = []
        for n, (_, tile, cols) in enumerate(items(batch)):
            if stage == 2:
                src, dst = total.at[tile, :, cols], total.at[tile, :, cols]
            else:
                src = held(tile).at[x, y, :, cols]
                dst = (from_middle if stage else from_end).at[tile, :, cols]
            copies.append(
                remote(
                    src,
                    dst,
                    z_send.at[stage, batch, n],
                    z_recv.at[stage, batch, n],
                    z_targets[stage],
                )
            )
        return copies

    def give_core(batch):
        start(core_copies(batch))

    def give_far(batch):
        arrive(core_copies(batch))
        for _, tile, cols in items(batch):
            mine = held(tile)
            mine[:, :, :, cols] = mine[:, :, :, cols] + from_core[tile, :, :, :, cols]
        start(far_copies(batch))

    def give_mid(batch):
        arrive(far_copies(batch))
        for kind, tile, cols in items(batch):
            mine = held(tile)
            if kind:
                mine[:, y, :, cols] = mine[:, y, :, cols] + from_far[tile, :, :, cols]
            else:
                mine[x, :, :, cols] = mine[x, :, :, cols] + from_far[tile, :, :, cols]
        start(mid_copies(batch))

    def give_end(batch):
        arrive(mid_copies(batch))
        for _, tile, cols in items(batch):
            mine = held(tile)
            mine[x, y, :, cols] = mine[x, y, :, cols] + from_mid[tile, :, cols]

        @pl.when(is_end)
        def _():
            start(z_copies(batch, 0))

    def give_middle(batch):
        @pl.when(is_middle)
        def _():
            arrive(z_copies(batch, 0))
            for _, tile, cols in items(batch):
                mine = held(tile)
                mine[x, y, :, cols] = mine[x, y, :, cols] + from_end[tile, :, cols]
            start(z_copies(batch, 1))

    def give_total(batch):
        @pl.when(is_middle)
        def _():
            arrive(z_copies(batch, 1))
            for _, tile, cols in items(batch):
                mine = held(tile)
                total[tile, :, cols] = mine[x, y, :, cols] + from_middle[tile, :, cols]
            start(z_copies(batch, 2))

    def take_total(batch):
        @pl.when(is_end)
        def _():
            arrive(z_copies(batch, 2))

    def deliver(third):
        cols = pl.ds(256 * third, 256)
        snap[...] = total[:, :, cols]

        def fill(at, carry):
            value = snap[holds[at]]
            outbox[third, at] = jnp.where(keeps[at] > 0, value, jnp.zeros_like(value))
            return carry

        lax.fori_loop(0, 2 * PLANE, fill, 0)

        def send(hop, carry):
            target = lax.rem(in_plane + hop, PLANE)
            remote(
                outbox.at[third, pl.ds(2 * target, 2)],
                slot_grad.at[:, core, x, y, :, cols],
                out_send.at[third],
                out_recv.at[third],
                z * PLANE + target,
            ).start()
            return carry

        lax.fori_loop(1, PLANE, send, 0)
        keep_copy(third).start()

    def keep_copy(third):
        return pltpu.make_async_copy(
            outbox.at[third, pl.ds(2 * in_plane, 2)],
            slot_grad.at[:, core, x, y, :, pl.ds(256 * third, 256)],
            load_sem.at[5 + third],
        )

    def vec_copies(stage):
        if stage < 3:
            hops = [(stage, (sibling, x_peer, y_peer)[stage])]
        else:
            hops = [
                (2 + hop, lax.rem(z + hop, 4) * PLANE + in_plane) for hop in range(1, 4)
            ]
        return [
            remote(vec_now.at[stage], vec_in.at[at], vec_send.at[at], vec_recv.at[at], device)
            for at, device in hops
        ]

    def vec_next(stage):
        arrive(vec_copies(stage))
        vec_now[stage + 1] = vec_now[stage] + vec_in[stage]
        start(vec_copies(stage + 1))

    def input_store():
        return pltpu.make_async_copy(acc, input_hbm, load_sem.at[4])

    def load(at):
        src, dst = (
            (hidden_hbm, hidden_then_x),
            (down_hbm, down_then_branch),
            (second_hbm, acc),
            (hat_hbm, hat_ref),
            None,
            None,
            None,
            None,
            (x_hbm, hidden_then_x),
        )[at]
        return pltpu.make_async_copy(src, dst, load_sem.at[at])

    def tile_load(tile, side):
        source = (slope_hbm, active_hbm)[side]
        return pltpu.make_async_copy(source.at[tile], tile_buf.at[side], load_sem.at[9 + side])

    def w_load(at):
        return pltpu.make_async_copy(w_hbm.at[at], w_part.at[at], w_sem.at[at])

    def weight(at, cols=slice(None)):
        value = w_part[at, :, :, :, :, cols]
        return value.reshape(8 * PIECE, value.shape[-1])

    actions = {
        "core": give_core,
        "far": give_far,
        "mid": give_mid,
        "end": give_end,
        "middle": give_middle,
        "total": give_total,
        "take": take_total,
        "deliver": deliver,
        "sum": vec_next,
    }

    @pl.when(step == 0)
    def _():
        start([load(1), tile_load(0, 0), w_load(5), w_load(4), load(2), tile_load(0, 1), load(0)])
        start([w_load(at) for at in range(6, TILES)] + [load(3)] + [w_load(3 - at) for at in range(4)])
        for at in range(2 * PLANE):
            tile_here, kept = jnp.int32(0), jnp.int32(0)
            for tile in range(TILES):
                place_of = SLOTS * owners[tile] + slot_number(owners, tile)
                match = place_of == z * 2 * PLANE + at
                tile_here = tile_here + jnp.where(match, POSITIONS.index(tile), 0)
                kept = kept + jnp.where(match, 1, 0)
            holds[at] = tile_here
            keeps[at] = kept
        vec_now[0] = late_ref[...]
        greet(z, in_plane)

    def serve(points):
        for at in points:
            if BACK_PLAN[at]:

                @pl.when(step == (at // 2 if at < 8 else at - 4))
                def _():
                    for name, number in BACK_PLAN[at]:
                        actions[name](number)

    serve(range(0, 8, 2))

    @pl.when(step < 4)
    def _():
        tile_load(step, 0).wait()
        w_load(5 + 2 * step).wait()

        @pl.when(step == 0)
        def _():
            load(1).wait()

        for half in range(2):
            rows = slice(ROWS * half, ROWS * half + ROWS)
            back = dot_back(down_then_branch[rows, :], weight(5 + 2 * step))
            up_low = (back * tile_buf[0, rows, :].astype(jnp.float32)).astype(jnp.bfloat16)
            up_buf[rows, :] = up_low
            vec_now[0, pl.ds(3 + step, 1), :] += columns_total(up_low.astype(jnp.float32))

        @pl.when(step < 3)
        def _():
            tile_load(step + 1, 0).start()

        w_load(4 + 2 * step).wait()

        @pl.when(step == 0)
        def _():
            load(2).wait()
            load(0).wait()

        for half in range(2):
            rows = slice(ROWS * half, ROWS * half + ROWS)
            acc[rows, :] = acc[rows, :] + dot_back(up_buf[rows, :], weight(4 + 2 * step))

    serve(range(1, 8, 2))

    @pl.when(step < 4)
    def _():
        tile_load(step, 1).wait()
        by_down = outer(tile_buf[1], down_then_branch[...]).astype(jnp.bfloat16)
        w_part[5 + 2 * step] = by_down.reshape(2, 2, 2, PIECE, 8 * PIECE)

        @pl.when(step < 3)
        def _():
            tile_load(step + 1, 1).start()

        by_up = outer(hidden_then_x[...], up_buf[...]).astype(jnp.bfloat16)
        w_part[4 + 2 * step] = by_up.reshape(2, 2, 2, PIECE, 8 * PIECE)

    @pl.when(step == 3)
    def _():
        load(8).start()
        load(3).wait()
        for at in range(4):
            w_load(at).wait()
        for half in range(2):
            rows = slice(ROWS * half, ROWS * half + ROWS)
            grad_hidden, hat = acc[rows, :], hat_ref[rows, :].astype(jnp.float32)
            vec_now[0, 10:11, :] += columns_total(grad_hidden * hat)
            vec_now[0, 8:9, :] += columns_total(grad_hidden)
            first = normalize_back(grad_hidden * gain_ref[0:1, :], hat, inverse_ref[rows, :])
            acc[rows, :] = first
            branch_low = first.astype(jnp.bfloat16)
            down_then_branch[rows, :] = branch_low
            vec_now[0, 2:3, :] += columns_total(branch_low.astype(jnp.float32))
            grad_ctx_ref[rows, :] = dot_back(branch_low, weight(3)).astype(jnp.bfloat16)

    serve(range(8, 20))

    here = pl.ds(pl.multiple_of(block * ROWS, ROWS), ROWS)
    quad_cols = pl.ds(pl.multiple_of(quad * 256, 256), 256)

    def add_sums(at, by_query, by_value):
        vec_now[0, 0:1, at] += by_query
        vec_now[0, 1:2, at] += by_value

    @pl.when(step >= 4)
    def _():
        attend_back_pair(
            2 * quad + pair,
            here,
            p_ref.at[0],
            (q_ref[...], k_ref[...], v_ref[...]),
            ctx_ref,
            grad_ctx_ref,
            pulled,
            pl.ds(pl.multiple_of(pair * 128, 128), 128),
            add_sums,
        )

    @pl.when((step >= 4) & (pair == 1))
    def _():
        more = acc[here, :]
        for at in range(3):
            more = more + dot_back(pulled[at, here, :], weight(at, quad_cols))
        acc[here, :] = more

    @pl.when(step == 7)
    def _():
        load(8).wait()

    @pl.when((step >= 4) & (block == 1) & (pair == 1))
    def _():
        for tile in range(4):
            if tile < 3:
                value = outer(hidden_then_x[...], pulled[tile])
            else:
                value = outer(ctx_ref[...], down_then_branch[:, quad_cols])
            value = value.astype(jnp.bfloat16).reshape(2, 2, 2, PIECE, 256)
            part[tile, :, :, :, :, quad_cols] = value


    @pl.when(step == 15)
    def _():
        input_store().start()
        start(vec_copies(0))
        for name, number in BACK_PLAN[-1]:
            actions[name](number)
        arrive(vec_copies(3))
        summed = jnp.zeros(vec_out.shape, jnp.float32)
        for origin in range(4):
            hop = lax.rem(z - origin + 4, 4)
            summed = summed + jnp.where(hop == 0, vec_now[3], vec_in[2 + jnp.maximum(hop, 1)])
        vec_out[...] = summed
        for batch in range(7):
            for copy in core_copies(batch) + far_copies(batch) + mid_copies(batch):
                copy.wait_send()

            @pl.when(is_end)
            def _():
                for copy in z_copies(batch, 0):
                    copy.wait_send()

            @pl.when(is_middle)
            def _():
                for copy in z_copies(batch, 1) + z_copies(batch, 2):
                    copy.wait_send()

        for stage in range(4):
            for copy in vec_copies(stage):
                copy.wait_send()
        input_store().wait()
        for third in range(3):
            keep_copy(third).wait()
            most = outbox.at[third, pl.ds(0, 2 * PLANE - 2)]
            pltpu.make_async_copy(most, most, out_recv.at[third]).wait()
            pltpu.make_async_copy(most, most, out_send.at[third]).wait()


def backward_and_reduced(
    owners,
    probs,
    query,
    keyed,
    valued,
    context,
    inverse,
    gain,
    late_sums,
    x,
    hidden,
    active,
    slope,
    grad_down,
    grad_second,
    hat,
    weights,
):
    tokens, width = x.shape
    low, high = jnp.bfloat16, jnp.float32
    shaped = jax.ShapeDtypeStruct
    smem = pl.BlockSpec(memory_space=pltpu.SMEM)
    any_space = pl.BlockSpec(memory_space=pl.ANY)
    dma = pltpu.SemaphoreType.DMA
    once = pl.Buffered(1)

    def at(step):
        inner = jnp.maximum(step - 4, 0)
        return lax.rem(inner, 4) // 2, inner // 4 * 2 + lax.rem(inner, 2)

    pair = pl.BlockSpec((ROWS, 128), at)
    sums = pl.BlockSpec((16, width), lambda i: (0, 0))
    cut = (2, 2, 2, PIECE, width)
    input_grad, slot_grads, vector_sums = pl.pallas_call(
        backward_and_reduce,
        grid=(16,),
        out_shape=(
            shaped((tokens, width), high),
            shaped((SLOTS,) + cut, low),
            shaped((16, width), high),
        ),
        in_specs=[smem, pl.BlockSpec((1, 2, ROWS, ROWS), lambda i: (*at(i), 0, 0))]
        + [pair] * 3
        + [
            pl.BlockSpec((tokens, width), lambda i: (0, 0), pipeline_mode=once),
            pl.BlockSpec((tokens, 1), lambda i: (0, 0), pipeline_mode=once),
            pl.BlockSpec(gain.shape, lambda i: (0, 0)),
            sums,
        ]
        + [any_space] * 8,
        out_specs=(any_space, any_space, sums),
        scratch_shapes=[
            pltpu.VMEM((TILES,) + cut, low),
            pltpu.VMEM((tokens, width), high),
            pltpu.VMEM((3, tokens, 256), low),
            pltpu.VMEM((tokens, width), low),
            pltpu.VMEM((tokens, width), low),
            pltpu.VMEM((tokens, width), low),
            pltpu.VMEM((tokens, width), low),
            pltpu.VMEM((2, tokens, width), low),
            pltpu.VMEM((tokens, width), low),
            pltpu.VMEM((4,) + cut, low),
            pltpu.VMEM((TILES,) + cut[1:], low),
            pltpu.VMEM((TILES,) + cut[2:], low),
            pltpu.VMEM((TILES,) + cut[3:], low),
            pltpu.VMEM((TILES,) + cut[3:], low),
            pltpu.VMEM((TILES,) + cut[3:], low),
            pltpu.VMEM((TILES,) + cut[3:], low),
            pltpu.VMEM((TILES, PIECE, 256), low),
            pltpu.VMEM((3, 2 * PLANE, PIECE, 256), low),
            pltpu.VMEM((4, 16, width), high),
            pltpu.VMEM((6, 16, width), high),
            pltpu.SMEM((2 * PLANE,), jnp.int32),
            pltpu.SMEM((2 * PLANE,), jnp.int32),
            dma((11,)),
            dma((TILES,)),
            dma((7, 4)),
            dma((7, 4)),
            dma((7, 4)),
            dma((7, 4)),
            dma((7, 4)),
            dma((7, 4)),
            dma((3, 7, 4)),
            dma((3, 7, 4)),
            dma((6,)),
            dma((6,)),
            dma((3,)),
            dma((3,)),
        ],
        compiler_params=pltpu.CompilerParams(
            collective_id=1, has_side_effects=True, vmem_limit_bytes=63 * 2**20
        ),
        name="backward_and_reduce",
    )(
        owners,
        probs,
        query,
        keyed,
        valued,
        context,
        inverse,
        gain,
        late_sums,
        x,
        hidden,
        active,
        slope,
        grad_down,
        grad_second,
        hat,
        weights,
    )
    return input_grad, slot_grads.reshape(SLOTS, width, width), vector_sums


def collected_tiles(tile_low, owners, slots):
    mine = owners == lax.axis_index("dp")
    local = jnp.where(mine[:, None, None], tile_low[slots], jnp.zeros((), tile_low.dtype))
    return lax.psum(local, "dp")


def summed_over_slice(parts, vector_terms, owners, slots):
    myself = lax.axis_index("dp")

    def add(held, items):
        part, owner, slot = items
        total = lax.psum(part.astype(jnp.float32), "dp")
        here = (owner == myself) & (slot == jnp.arange(SLOTS, dtype=jnp.int32))
        return held + jnp.where(here[:, None, None], total[None], 0.0), None

    empty = jnp.zeros((SLOTS,) + parts.shape[1:], jnp.float32)
    return lax.scan(add, empty, (parts, owners, slots))[0], lax.psum(vector_terms, "dp")


def body(
    inputs,
    cotangent,
    counts,
    lengths,
    owners,
    tile_master,
    tile_first,
    tile_second,
    tile_ema,
    bias_vals,
    gain_vals,
    vector_first,
    vector_second,
    vector_ema,
):
    tokens = inputs.shape[0]
    small = lax.axis_size("dp") == GROUP
    gain_scale = float(tokens * lax.axis_size("dp")) ** (-0.5)
    if small:
        (
            query,
            keyed,
            valued,
            probs,
            context,
            hidden,
            active,
            slope,
            grad_down,
            mixed,
            grad_second,
            hat,
            weights,
            inverse,
            late_sums,
        ) = gathered_and_forwarded(
            counts,
            lengths,
            owners,
            bias_vals,
            gain_vals,
            inputs,
            cotangent,
            tile_master,
        )
        input_grad, slot_grads, full_sums = backward_and_reduced(
            owners,
            probs,
            query,
            keyed,
            valued,
            context,
            inverse,
            gain_vals,
            late_sums,
            inputs,
            hidden,
            active,
            slope,
            grad_down,
            grad_second,
            hat,
            weights,
        )
    else:
        slots = tile_slots(owners)
        vectors = jnp.concatenate([bias_vals, gain_vals], 0)
        weights = collected_tiles(tile_master[0].astype(jnp.bfloat16), owners, slots)
        query, keyed, valued, probs, context, hat, inverse = attended(
            counts, lengths, inputs, weights, vectors
        )
        mixed, grad_first, grad_branch, grad_context, up_grads, down_grads, late_sums = fed_forward_both(
            counts, lengths, hat, inverse, cotangent, weights, vectors
        )
        input_grad, early_grads, early_sums = attended_back(
            probs, query, keyed, valued, inputs, context, grad_context, grad_branch, grad_first, weights
        )
        parts = jnp.concatenate([early_grads, up_grads, down_grads], 0)
        slot_grads, full_sums = summed_over_slice(parts, late_sums + early_sums, owners, slots)
    return updated(
        gain_scale,
        slot_grads,
        tile_master,
        tile_first,
        tile_second,
        tile_ema,
        full_sums,
        bias_vals,
        gain_vals,
        vector_first,
        vector_second,
        vector_ema,
        mixed,
        input_grad,
    )


def solution(mesh):
    placed = (
        P("dp", None),
        P("dp", None),
        P("dp", None),
        P("dp", None),
        P(),
        P("dp", None, None, None),
        P("dp", None, None, None),
        P("dp", None, None, None),
        P("dp", None, None, None),
        P(),
        P(),
        P(),
        P(),
        P(),
    )
    return jax.shard_map(
        body,
        mesh=mesh,
        in_specs=placed,
        out_specs=(
            P("dp", None),
            P("dp", None),
            P("dp", None, None, None),
            P("dp", None, None, None),
            P("dp", None, None, None),
            P("dp", None, None, None),
            P("dp", None, None, None),
            P(),
            P(),
            P(),
            P(),
        ),
        check_vma=False,
    )
```

```python
import functools

import jax
import jax.numpy as jnp
from jax import lax
from jax.experimental import pallas as pl
from jax.experimental.pallas import tpu as pltpu
from jax.sharding import PartitionSpec as P

HEADS = 12
BUCKET = 128
SLOTS = 2
TILES = 12
VROWS = 12
STEP = 5

norm_epsilon = 1e-12
tile_rate = 0.03
vector_rate = 0.2
first_decay = 0.5
second_decay = 0.5
adam_epsilon = 1e-08
weight_decay = 0.01
average_rate = 0.9


def tile_slots(owners):
    order = jnp.arange(owners.shape[0], dtype=jnp.int32)
    same = owners[:, None] == owners[None, :]
    earlier = order[None, :] < order[:, None]
    return jnp.sum((same & earlier).astype(jnp.int32), 1)


def adam_update(param, grad, first, second, rate):
    first_new = first_decay * first + (1.0 - first_decay) * grad
    second_new = second_decay * second + (1.0 - second_decay) * grad * grad
    first_hat = first_new / (1.0 - first_decay**STEP)
    second_hat = second_new / (1.0 - second_decay**STEP)
    param_new = param - rate * (
        first_hat / (jnp.sqrt(second_hat) + adam_epsilon) + weight_decay * param
    )
    return (param_new, first_new, second_new)


ROWS = 4 * BUCKET
TAIL_RATE = 0.28
TAIL_SERIES = (
    0.11615256574707405,
    0.06981038475559553,
    0.2631359597579608,
    -0.22983675561378278,
    0.38546775012288165,
    -0.10472989053809521,
)
INV_SQRT_TAU = 0.3989422804014327
ALLOWED = 3.0e38
BARRED = -1000000000.0


def dot(left, right):
    return jnp.dot(left, right, preferred_element_type=jnp.float32)


def dot_back(left, right):
    return lax.dot_general(
        left, right, (((1,), (1,)), ((), ())), preferred_element_type=jnp.float32
    )


def outer(left, right):
    return lax.dot_general(
        left, right, (((0,), (0,)), ((), ())), preferred_element_type=jnp.float32
    )


def passage_facts(counts, lengths, position):
    places = lengths.shape[1]
    big_end = counts[0, 0]
    mid_end = big_end + counts[0, 1]
    all_end = mid_end + counts[0, 2]
    start = jnp.int32(0)
    member = jnp.zeros(position.shape, jnp.int32)
    usable = jnp.zeros(position.shape, jnp.int32)
    for number in range(places):
        size = jnp.where(
            number < big_end,
            4 * BUCKET,
            jnp.where(number < mid_end, 2 * BUCKET, jnp.where(number < all_end, BUCKET, 0)),
        )
        inside = (position >= start) & (position < start + size)
        live = inside & (position < start + lengths[0, number])
        member = jnp.where(inside, number + 1, member)
        usable = jnp.where(live, 1, usable)
        start = start + size
    passage = jnp.where(member > 0, member - 1, places + position // BUCKET)
    return usable, passage


def normalize(values):
    center = jnp.mean(values, -1, keepdims=True)
    centered = values - center
    spread = jnp.mean(centered * centered, -1, keepdims=True)
    inverse = lax.rsqrt(spread + norm_epsilon)
    return centered * inverse, inverse


def normalize_back(grad, hat, inverse):
    center = jnp.mean(grad, -1, keepdims=True)
    along = jnp.mean(grad * hat, -1, keepdims=True)
    return inverse * (grad - center - hat * along)


def columns_total(values):
    return jnp.sum(values, 0, keepdims=True)


def attention_caps(counts, lengths, block):
    at_row = lax.broadcasted_iota(jnp.int32, (ROWS, 1), 0) + block * ROWS
    at_column = lax.broadcasted_iota(jnp.int32, (1, ROWS), 1) + block * ROWS
    _, passage_row = passage_facts(counts, lengths, at_row)
    usable_column, passage_column = passage_facts(counts, lengths, at_column)
    allowed = (passage_row == passage_column) & ((usable_column == 1) | (at_row == at_column))
    return jnp.where(allowed, ALLOWED, BARRED)


def attend_quad(quad, weight, x_ref, vec_ref, cap_ref, q_ref, k_ref, v_ref, p_ref, ctx_ref):
    cols = pl.ds(pl.multiple_of(quad * 256, 256), 256)
    x = x_ref[...]
    query = (dot(x, weight(0, cols)) + vec_ref[0:1, cols]).astype(jnp.bfloat16)
    query = query * jnp.bfloat16(0.125)
    keyed = dot(x, weight(1, cols)).astype(jnp.bfloat16)
    valued = (dot(x, weight(2, cols)) + vec_ref[1:2, cols]).astype(jnp.bfloat16)
    q_ref[...] = query
    k_ref[...] = keyed
    v_ref[...] = valued
    low_half = lax.broadcasted_iota(jnp.int32, (1, 128), 1) < 64
    for pair in range(2):
        part = slice(128 * pair, 128 * pair + 128)
        contexts = []
        for head in range(2):
            here = low_half if head == 0 else ~low_half
            mine = jnp.where(here, query[:, part], jnp.zeros_like(query[:, part]))
            scores = jnp.minimum(dot_back(mine, keyed[:, part]), cap_ref[...])
            exponent = jnp.exp(scores - jnp.max(scores, -1, keepdims=True))
            inverse = 1.0 / jnp.sum(exponent, -1, keepdims=True)
            probability = (exponent * inverse).astype(jnp.bfloat16)
            p_ref[0, 2 * pair + head] = probability
            contexts.append(dot(probability, valued[:, part]))
        both = jnp.where(low_half, contexts[0], contexts[1]).astype(jnp.bfloat16)
        ctx_ref[:, pl.ds(pl.multiple_of(quad * 256 + 128 * pair, 128), 128)] = both


def close_block(w_out, x_ref, vec_ref, ctx_ref, hat_ref, inverse_ref):
    branch = dot(ctx_ref[...], w_out) + vec_ref[2:3, :]
    hat_ref[...], inverse_ref[...] = normalize(x_ref[...].astype(jnp.float32) + branch)


def attend_back_pair(pull, level_from, p_ref, query, keyed, valued):
    low_half = lax.broadcasted_iota(jnp.int32, (1, 128), 1) < 64
    along = pull.astype(jnp.float32) * level_from.astype(jnp.float32)
    pull_turned, query_turned = pull.T, query.T
    by_query, by_key, by_value = [], [], []
    for head in range(2):
        mask = low_half if head == 0 else ~low_half
        mine = jnp.where(mask, pull, jnp.zeros_like(pull))
        level = jnp.sum(jnp.where(mask, along, 0.0), -1, keepdims=True)
        probability = p_ref[head]
        grad_prob = dot_back(mine, valued)
        grad_scores = (probability.astype(jnp.float32) * (grad_prob - level)).astype(jnp.bfloat16)
        rows = slice(64 * head, 64 * head + 64)
        by_query.append(dot(grad_scores, keyed))
        by_key.append(dot(query_turned[rows], grad_scores))
        by_value.append(dot(pull_turned[rows], probability))
    grad_query = jnp.where(low_half, by_query[0], by_query[1]) * 0.125
    grad_key = jnp.concatenate(by_key, 0).T
    grad_value = jnp.concatenate(by_value, 0).T
    return [value.astype(jnp.bfloat16) for value in (grad_query, grad_key, grad_value)]


def gelu_parts(up):
    near = 1.0 / (1.0 + TAIL_RATE * jnp.abs(up))
    decay = jnp.exp(up * up * -0.5)
    series = jnp.full_like(near, TAIL_SERIES[-1])
    for term in TAIL_SERIES[-2::-1]:
        series = series * near + term
    tail = series * near * decay
    share = jnp.where(up < 0.0, tail, 1.0 - tail)
    slope = share + up * (decay * INV_SQRT_TAU)
    return (up * share).astype(jnp.bfloat16), slope


def attend_forward(
    counts,
    lengths,
    x_ref,
    w_hbm,
    vec_ref,
    q_ref,
    k_ref,
    v_ref,
    p_ref,
    ctx_ref,
    hat_ref,
    inverse_ref,
    w_buf,
    cap_ref,
    w_sem,
):
    block, quad = pl.program_id(0), pl.program_id(1)
    loads = [pltpu.make_async_copy(w_hbm.at[at], w_buf.at[at], w_sem.at[at]) for at in range(4)]

    @pl.when((block == 0) & (quad == 0))
    def _():
        for load in loads:
            load.start()
        for load in loads:
            load.wait()

    @pl.when(quad == 0)
    def _():
        cap_ref[...] = attention_caps(counts, lengths, block)

    def weight(at, cols):
        return w_buf[at, :, cols]

    attend_quad(quad, weight, x_ref, vec_ref, cap_ref, q_ref, k_ref, v_ref, p_ref, ctx_ref)

    @pl.when(quad == 2)
    def _():
        close_block(w_buf[3], x_ref, vec_ref, ctx_ref, hat_ref, inverse_ref)


def attended(counts, lengths, x, weights, vectors):
    tokens, width = x.shape
    blocks = tokens // ROWS
    low = jnp.bfloat16
    smem = pl.BlockSpec(memory_space=pltpu.SMEM)
    quad = pl.BlockSpec((ROWS, 256), lambda b, h: (b, h))
    rows = pl.BlockSpec((ROWS, width), lambda b, h: (b, 0))
    shaped = jax.ShapeDtypeStruct
    return pl.pallas_call(
        attend_forward,
        grid=(blocks, 3),
        out_shape=(
            shaped((tokens, width), low),
            shaped((tokens, width), low),
            shaped((tokens, width), low),
            shaped((blocks, HEADS, ROWS, ROWS), low),
            shaped((tokens, width), low),
            shaped((tokens, width), jnp.float32),
            shaped((tokens, 1), jnp.float32),
        ),
        in_specs=[
            smem,
            smem,
            rows,
            pl.BlockSpec(memory_space=pl.ANY),
            pl.BlockSpec((VROWS, width), lambda b, h: (0, 0)),
        ],
        out_specs=(
            quad,
            quad,
            quad,
            pl.BlockSpec((1, 4, ROWS, ROWS), lambda b, h: (b, h, 0, 0)),
            rows,
            rows,
            pl.BlockSpec((ROWS, 1), lambda b, h: (b, 0)),
        ),
        scratch_shapes=[
            pltpu.VMEM((4, width, width), low),
            pltpu.VMEM((ROWS, ROWS), jnp.float32),
            pltpu.SemaphoreType.DMA((4,)),
        ],
        compiler_params=pltpu.CompilerParams(vmem_limit_bytes=56 * 2**20),
        name="attend_forward",
    )(counts, lengths, x, weights, vectors)


def feed_forward_both(
    counts,
    lengths,
    hat_ref,
    inverse_ref,
    cot_ref,
    w_hbm,
    vec_ref,
    mixed_ref,
    first_ref,
    branch_ref,
    context_ref,
    up_grad_ref,
    down_grad_ref,
    sum_ref,
    w_buf,
    active_ref,
    up_ref,
    hidden_ref,
    down_ref,
    slope_ref,
    w_sem,
):
    step = pl.program_id(0)
    blocks = pl.num_programs(0) - 4
    loads = [
        pltpu.make_async_copy(w_hbm.at[3 + at], w_buf.at[at], w_sem.at[at]) for at in range(9)
    ]

    @pl.when(step == 0)
    def _():
        for load in loads[1:] + loads[:1]:
            load.start()
        sum_ref[...] = jnp.zeros_like(sum_ref)
        for load in loads[1:] + loads[:1]:
            load.wait()

    @pl.when(step < blocks)
    def _():
        here = pl.ds(pl.multiple_of(step * ROWS, ROWS), ROWS)
        at_row = lax.broadcasted_iota(jnp.int32, (ROWS, 1), 0) + step * ROWS
        live = passage_facts(counts, lengths, at_row)[0].astype(jnp.float32)
        hat = hat_ref[...]
        hidden = hat * vec_ref[10:11, :] + vec_ref[8:9, :]
        hidden_low = hidden.astype(jnp.bfloat16)
        hidden_ref[here, :] = hidden_low
        total = hidden + vec_ref[7:8, :]
        for tile in range(4):
            up = dot(hidden_low, w_buf[1 + tile]) + vec_ref[3 + tile : 4 + tile, :]
            active, slope = gelu_parts(up)
            slope_ref[tile] = slope.astype(jnp.bfloat16)
            active_ref[tile, here, :] = active
            total = total + dot(active, w_buf[5 + tile])
        hat_two, inverse_two = normalize(total)
        mixed_ref[...] = ((hat_two * vec_ref[11:12, :] + vec_ref[9:10, :]) * live).astype(jnp.bfloat16)
        grad_out = cot_ref[...].astype(jnp.float32) * live
        sum_ref[11:12, :] += columns_total(grad_out * hat_two)
        sum_ref[9:10, :] += columns_total(grad_out)
        second = normalize_back(grad_out * vec_ref[11:12, :], hat_two, inverse_two)
        down_low = second.astype(jnp.bfloat16)
        down_ref[here, :] = down_low
        sum_ref[7:8, :] += columns_total(down_low.astype(jnp.float32))
        grad_hidden = second
        for tile in range(4):
            pulled = dot_back(down_low, w_buf[5 + tile])
            up_low = (pulled * slope_ref[tile].astype(jnp.float32)).astype(jnp.bfloat16)
            up_ref[tile, here, :] = up_low
            sum_ref[3 + tile : 4 + tile, :] += columns_total(up_low.astype(jnp.float32))
            grad_hidden = grad_hidden + dot_back(up_low, w_buf[1 + tile])
        sum_ref[10:11, :] += columns_total(grad_hidden * hat)
        sum_ref[8:9, :] += columns_total(grad_hidden)
        grad_first = normalize_back(grad_hidden * vec_ref[10:11, :], hat, inverse_ref[...])
        first_ref[...] = grad_first
        branch_low = grad_first.astype(jnp.bfloat16)
        branch_ref[...] = branch_low
        sum_ref[2:3, :] += columns_total(branch_low.astype(jnp.float32))
        context_ref[...] = dot_back(branch_low, w_buf[0]).astype(jnp.bfloat16)

    @pl.when(step >= blocks)
    def _():
        tile = step - blocks
        up_grad_ref[0] = outer(hidden_ref[...], up_ref[tile]).astype(jnp.bfloat16)
        down_grad_ref[0] = outer(active_ref[tile], down_ref[...]).astype(jnp.bfloat16)


def fed_forward_both(counts, lengths, hat, inverse, cotangent, weights, vectors):
    tokens, width = hat.shape
    blocks = tokens // ROWS
    low = jnp.bfloat16
    smem = pl.BlockSpec(memory_space=pltpu.SMEM)
    shaped = jax.ShapeDtypeStruct

    def block_of(step):
        return jnp.minimum(step, blocks - 1)

    def tile_of(step):
        return jnp.maximum(step - blocks, 0)

    rows = pl.BlockSpec((ROWS, width), lambda i: (block_of(i), 0))
    tile = pl.BlockSpec((1, width, width), lambda i: (tile_of(i), 0, 0))
    return pl.pallas_call(
        feed_forward_both,
        grid=(blocks + 4,),
        out_shape=(
            shaped((tokens, width), low),
            shaped((tokens, width), jnp.float32),
            shaped((tokens, width), low),
            shaped((tokens, width), low),
            shaped((4, width, width), low),
            shaped((4, width, width), low),
            shaped((16, width), jnp.float32),
        ),
        in_specs=[
            smem,
            smem,
            rows,
            pl.BlockSpec((ROWS, 1), lambda i: (block_of(i), 0)),
            rows,
            pl.BlockSpec(memory_space=pl.ANY),
            pl.BlockSpec((VROWS, width), lambda i: (0, 0)),
        ],
        out_specs=(
            rows,
            rows,
            rows,
            rows,
            tile,
            tile,
            pl.BlockSpec((16, width), lambda i: (0, 0)),
        ),
        scratch_shapes=[
            pltpu.VMEM((9, width, width), low),
            pltpu.VMEM((4, tokens, width), low),
            pltpu.VMEM((4, tokens, width), low),
            pltpu.VMEM((tokens, width), low),
            pltpu.VMEM((tokens, width), low),
            pltpu.VMEM((4, ROWS, width), low),
            pltpu.SemaphoreType.DMA((9,)),
        ],
        compiler_params=pltpu.CompilerParams(vmem_limit_bytes=60 * 2**20),
        name="feed_forward_both",
    )(counts, lengths, hat, inverse, cotangent, weights, vectors)


def attend_backward(
    p_ref,
    q_ref,
    k_ref,
    v_ref,
    x_ref,
    ctx_ref,
    grad_ctx_ref,
    branch_ref,
    first_ref,
    w_ref,
    input_ref,
    grad_ref,
    sum_ref,
    pulled,
):
    step = pl.program_id(0)
    quad, block = step // 2, lax.rem(step, 2)
    here = pl.ds(pl.multiple_of(block * ROWS, ROWS), ROWS)
    cols = pl.ds(pl.multiple_of(quad * 256, 256), 256)

    @pl.when(step == 0)
    def _():
        sum_ref[...] = jnp.zeros_like(sum_ref)
        input_ref[...] = first_ref[...]

    for pair in range(2):
        half = slice(128 * pair, 128 * pair + 128)
        at = pl.ds(pl.multiple_of(quad * 256 + 128 * pair, 128), 128)
        heads = p_ref.at[0, pl.ds(2 * pair, 2)]
        grads = attend_back_pair(
            grad_ctx_ref[here, at], ctx_ref[here, at], heads, q_ref[:, half], k_ref[:, half], v_ref[:, half]
        )
        for number, grad in enumerate(grads):
            pulled[number, here, half] = grad
        sum_ref[0:1, at] += columns_total(grads[0].astype(jnp.float32))
        sum_ref[1:2, at] += columns_total(grads[2].astype(jnp.float32))

    more = input_ref[here, :]
    for at in range(3):
        more = more + dot_back(pulled[at, here, :], w_ref[at, :, cols])
    input_ref[here, :] = more

    @pl.when(block == 1)
    def _():
        for tile in range(3):
            grad_ref[tile, :, cols] = outer(x_ref[...], pulled[tile]).astype(jnp.bfloat16)
        grad_ref[3, :, cols] = outer(ctx_ref[...], branch_ref[:, cols]).astype(jnp.bfloat16)


def attended_back(probs, query, keyed, valued, x, context, grad_context, grad_branch, grad_first, weights):
    tokens, width = x.shape
    low = jnp.bfloat16
    shaped = jax.ShapeDtypeStruct
    once = pl.Buffered(1)
    quad = pl.BlockSpec((ROWS, 256), lambda i: (lax.rem(i, 2), i // 2))
    whole = pl.BlockSpec((tokens, width), lambda i: (0, 0), pipeline_mode=once)
    return pl.pallas_call(
        attend_backward,
        grid=(6,),
        out_shape=(
            shaped((tokens, width), jnp.float32),
            shaped((4, width, width), low),
            shaped((16, width), jnp.float32),
        ),
        in_specs=[
            pl.BlockSpec((1, 4, ROWS, ROWS), lambda i: (lax.rem(i, 2), i // 2, 0, 0)),
            quad,
            quad,
            quad,
            whole,
            whole,
            whole,
            whole,
            whole,
            pl.BlockSpec((3, width, width), lambda i: (0, 0, 0), pipeline_mode=once),
        ],
        out_specs=(
            whole,
            pl.BlockSpec((4, width, width), lambda i: (0, 0, 0), pipeline_mode=once),
            pl.BlockSpec((16, width), lambda i: (0, 0)),
        ),
        scratch_shapes=[pltpu.VMEM((3, tokens, 256), low)],
        compiler_params=pltpu.CompilerParams(vmem_limit_bytes=56 * 2**20),
        name="attend_backward",
    )(probs, query, keyed, valued, x, context, grad_context, grad_branch, grad_first, weights)


def moved(param, grad, first, second, average, rate):
    param_new, first_new, second_new = adam_update(param, grad, first, second, rate)
    return param_new, first_new, second_new, average_rate * average + (1.0 - average_rate) * param_new


def update_kernel(
    gain_scale,
    grad_ref,
    master_ref,
    first_ref,
    second_ref,
    ema_ref,
    vec_grad_ref,
    bias_ref,
    gain_ref,
    vec_first_ref,
    vec_second_ref,
    vec_ema_ref,
    mixed_in,
    input_in,
    master_out,
    first_out,
    second_out,
    ema_out,
    copy_out,
    vec_out,
    vec_first_out,
    vec_second_out,
    vec_ema_out,
    mixed_out,
    input_out,
    vec_ref,
):
    mixed_out[...] = mixed_in[...]
    input_out[...] = input_in[...]

    @pl.when((pl.program_id(0) == 0) & (pl.program_id(1) == 0))
    def _():
        vec_ref[0:10, :] = bias_ref[...]
        vec_ref[10:12, :] = gain_ref[...]
        vec_grad = vec_grad_ref[0:VROWS, :] * gain_scale
        vec_out[...], vec_first_out[...], vec_second_out[...], vec_ema_out[...] = moved(
            vec_ref[...], vec_grad, vec_first_ref[...], vec_second_ref[...], vec_ema_ref[...], vector_rate
        )

    grad = grad_ref[...].astype(jnp.float32) * gain_scale
    result = moved(master_ref[0], grad, first_ref[0], second_ref[0], ema_ref[0], tile_rate)
    master_out[0], first_out[0], second_out[0], ema_out[0] = result
    copy_out[0] = result[0].astype(jnp.bfloat16)


def updated(
    gain_scale,
    slot_grads,
    master,
    first,
    second,
    ema,
    vec_grad,
    bias,
    gain,
    vec_first,
    vec_second,
    vec_ema,
    mixed,
    input_grad,
):
    width = master.shape[-1]
    chunk = 192
    tile = pl.BlockSpec((1, 1, chunk, width), lambda s, r: (0, s, r, 0))
    steps = width // chunk
    rows = pl.BlockSpec((mixed.shape[0] // (SLOTS * steps), width), lambda s, r: (s * steps + r, 0))

    def whole(value):
        return pl.BlockSpec(value.shape, lambda s, r: (0, 0))

    shaped = jax.ShapeDtypeStruct
    tile_shape = shaped(master.shape, jnp.float32)
    vec_shape = shaped((VROWS, width), jnp.float32)
    results = pl.pallas_call(
        functools.partial(update_kernel, gain_scale),
        grid=(SLOTS, steps),
        out_shape=(tile_shape,) * 4
        + (shaped(master.shape, jnp.bfloat16),)
        + (vec_shape,) * 4
        + (shaped(mixed.shape, mixed.dtype), shaped(input_grad.shape, input_grad.dtype)),
        in_specs=[pl.BlockSpec((1, chunk, width), lambda s, r: (s, r, 0))]
        + [tile] * 4
        + [whole(value) for value in (vec_grad, bias, gain, vec_first, vec_second, vec_ema)]
        + [rows] * 2,
        out_specs=(tile,) * 5 + (whole(vec_first),) * 4 + (rows,) * 2,
        scratch_shapes=[pltpu.VMEM((VROWS, width), jnp.float32)],
        compiler_params=pltpu.CompilerParams(vmem_limit_bytes=62 * 2**20),
        name="update",
    )(
        slot_grads,
        master,
        first,
        second,
        ema,
        vec_grad,
        bias,
        gain,
        vec_first,
        vec_second,
        vec_ema,
        mixed,
        input_grad,
    )
    return results[-2:] + results[:-2]


MESH = pl.DeviceIdType.MESH
GROUP = 32
PAIRS = TILES // 2
PLANE = 8
PIECE = 96
PAIR_TILES = ((0, 1), (2, 3), (4, 8), (5, 9), (6, 10), (7, 11))
EARLY = 2
WHOLE = 3


def remote(src, dst, send, recv, device):
    return pltpu.make_async_remote_copy(
        src_ref=src, dst_ref=dst, send_sem=send, recv_sem=recv, device_id=(device,), device_id_type=MESH
    )


def place(device):
    core = lax.rem(device, 2)
    x = lax.rem(device // 2, 2)
    y = lax.rem(device // 4, 2)
    z = device // 8
    return z, y, x, core


def start(copies):
    for copy in copies:
        copy.start()


def arrive(copies):
    for copy in copies:
        copy.wait_recv()


def greet(z, in_plane):
    barrier = pltpu.get_barrier_semaphore()
    for hop in range(1, PLANE):
        other = z * PLANE + lax.rem(in_plane + hop, PLANE)
        pl.semaphore_signal(barrier, inc=1, device_id=(other,), device_id_type=MESH)
    for hop in range(1, 4):
        other = lax.rem(z + hop, 4) * PLANE + in_plane
        pl.semaphore_signal(barrier, inc=1, device_id=(other,), device_id_type=MESH)
    pl.semaphore_wait(barrier, PLANE + 2)


def along_z(z, in_plane):
    inner = (1 + z // 2) * PLANE + in_plane
    other_middle = (3 - z) * PLANE + in_plane
    outer_end = lax.rem(lax.rem(z + 3, 4) * 3, 4) * PLANE + in_plane
    return inner, other_middle, outer_end


def third(part):
    return slice(None) if part == WHOLE else pl.ds(256 * part, 256)


POSITIONS = [tile for pair in PAIR_TILES for tile in pair]


def slot_number(owners, tile):
    number = jnp.int32(0)
    for earlier in range(tile):
        number = number + jnp.where(owners[earlier] == owners[tile], 1, 0)
    return number


def unit(pair, part):
    return 3 * pair + part if pair < EARLY else 2 * EARLY + pair


UNITS = [(pair, part) for pair in range(EARLY) for part in range(3)]
UNITS += [(pair, WHOLE) for pair in range(EARLY, PAIRS)]

FRONT_PLAN = (
    (
        ("open",),
        ("swap", 0),
        ("caps",),
        ("sent", 0),
        ("swap", 1),
        ("choose", 0),
        ("end", 1, 0),
        ("middle", 1, 0),
        ("sent", 1),
        ("swap", 2),
        ("choose", 1),
        ("end", 0, 0),
        ("total", 1, 0),
        ("middle", 0, 0),
        ("end", 0, 1),
        ("end", 1, 1),
        ("choose", 2),
        ("end", 1, 2),
        ("mid", 1, 0),
        ("middle", 1, 1),
        ("total", 1, 1),
        ("middle", 0, 1),
        ("end", 2),
        ("total", 0, 0),
        ("end", 0, 2),
        ("mid", 0, 0),
        ("mid", 1, 1),
        ("far", 1, 0),
        ("middle", 0, 2),
        ("total", 0, 1),
        ("end", 4),
        ("middle", 1, 2),
        ("mid", 0, 1),
        ("far", 0, 0),
        ("middle", 2),
        ("total", 0, 2),
        ("far", 0, 1),
        ("total", 1, 2),
        ("end", 3),
        ("near", 0, 0),
        ("near", 1, 0),
        ("mid", 1, 2),
        ("middle", 4),
        ("near", 0, 1),
        ("finish", 0, 0),
        ("far", 1, 2),
        ("total", 2),
        ("mid", 0, 2),
        ("far", 0, 2),
        ("mid", 2),
        ("finish", 0, 1),
        ("far", 1, 1),
        ("end", 5),
        ("middle", 3),
        ("near", 1, 2),
        ("total", 4),
        ("finish", 1, 0),
    ),
    (
        ("near", 1, 1),
        ("near", 0, 2),
        ("mid", 4),
        ("total", 3),
        ("far", 2),
        ("middle", 5),
    ),
    (
        ("mid", 3),
        ("total", 5),
        ("finish", 1, 1),
    ),
    (
        ("finish", 1, 2),
        ("keep", 1),
        ("far", 3),
    ),
    (
        ("finish", 0, 2),
        ("keep", 0),
        ("near", 2),
        ("mid", 5),
    ),
    (
        ("far", 4),
        ("finish", 2),
        ("keep", 2),
    ),
    (
        ("near", 3),
        ("far", 5),
    ),
    (
        ("finish", 3),
        ("keep", 3),
        ("near", 4),
    ),
    (
        ("near", 5),
        ("finish", 4),
        ("keep", 4),
    ),
    (
        ("finish", 5),
        ("keep", 5),
    ),
)


def gather_and_forward(
    counts,
    lengths,
    owners,
    bias_ref,
    gain_ref,
    x_hbm,
    cot_hbm,
    master_hbm,
    q_ref,
    k_ref,
    v_ref,
    p_ref,
    ctx_hbm,
    x_turned_hbm,
    ctx_turned_hbm,
    hidden_hbm,
    active_hbm,
    slope_hbm,
    down_hbm,
    mixed_hbm,
    second_hbm,
    hat_hbm,
    w_out,
    inverse_ref,
    sum_ref,
    vec_ref,
    cap_ref,
    wide,
    low,
    stage_a,
    stage_b,
    stage_c,
    chosen,
    from_end,
    from_middle,
    w_buf,
    x_then_hidden,
    x_turned,
    ctx_turned,
    hidden_turned,
    ctx_ref,
    cot_then_down,
    mixed_ref,
    hat_ref,
    slope_buf,
    active_buf,
    load_sem,
    store_sem,
    tile_sem,
    out_sem,
    swap_send,
    swap_recv,
    z_send,
    z_recv,
    mid_send,
    mid_recv,
    far_send,
    far_recv,
    near_send,
    near_recv,
):
    step = pl.program_id(0)
    width = 8 * PIECE
    me = lax.axis_index("dp")
    z, y, x, core = place(me)
    in_plane = lax.rem(me, PLANE)
    sibling = me + 1 - 2 * core
    x_peer = me + 2 - 4 * x
    y_peer = me + 4 - 8 * y
    z_targets = along_z(z, in_plane)
    stages = (stage_a, stage_b, stage_c)
    is_end = (z == 0) | (z == 3)
    is_middle = (z == 1) | (z == 2)

    def piece_rows(cell_core, cell_x, cell_y):
        return pl.ds(pl.multiple_of(((cell_core * 2 + cell_x) * 2 + cell_y) * PIECE, 16), PIECE)

    def swap(part):
        def send(hop, carry):
            target = lax.rem(in_plane + hop, PLANE)
            _, ty, tx, tc = place(target)
            remote(
                low.at[:, piece_rows(tc, tx, ty), third(part)],
                stages[part].at[pl.ds(2 * in_plane, 2)],
                swap_send.at[part],
                swap_recv.at[part],
                z * PLANE + target,
            ).start()
            return carry

        lax.fori_loop(1, PLANE, send, 0)

    def swap_wait(part, sem):
        most = stages[part].at[pl.ds(0, 2 * PLANE - 2)]
        pltpu.make_async_copy(most, most, sem.at[part]).wait()

    def z_copy(pair, part, level):
        two = pl.ds(2 * pair, 2)
        cols = third(part)
        src = w_buf.at[two, core, x, y, :, cols] if level == 2 else chosen.at[two, :, cols]
        dst = (from_end.at[two, :, cols], from_middle.at[two, :, cols], src)[level]
        at = unit(pair, part)
        return remote(src, dst, z_send.at[level, at], z_recv.at[level, at], z_targets[level])

    def z_end(pair, part=WHOLE):
        @pl.when(is_end)
        def _():
            z_copy(pair, part, 0).start()

    def z_middle(pair, part=WHOLE):
        @pl.when(is_middle)
        def _():
            z_copy(pair, part, 0).wait_recv()
            two, cols = pl.ds(2 * pair, 2), third(part)
            chosen[two, :, cols] = chosen[two, :, cols] + from_end[two, :, cols]
            z_copy(pair, part, 1).start()

    def z_total(pair, part=WHOLE):
        @pl.when(is_middle)
        def _():
            z_copy(pair, part, 1).wait_recv()
            two, cols = pl.ds(2 * pair, 2), third(part)
            w_buf[two, core, x, y, :, cols] = chosen[two, :, cols] + from_middle[two, :, cols]
            z_copy(pair, part, 2).start()

    def mid_copies(pair, part):
        copies = []
        for n, peer in enumerate((y_peer, x_peer)):
            spot = w_buf.at[2 * pair + n, core, x, y, :, third(part)]
            at = unit(pair, part), n
            copies.append(remote(spot, spot, mid_send.at[at], mid_recv.at[at], peer))
        return copies

    def halves(pair, part, late):
        row = 1 - x if late else x
        column = 1 - y if late else y
        cols = third(part)
        return w_buf.at[2 * pair, core, row, :, :, cols], w_buf.at[2 * pair + 1, core, :, column, :, cols]

    def far_copies(pair, part):
        copies = []
        for n, peer in enumerate((x_peer, y_peer)):
            spot = halves(pair, part, False)[n]
            at = unit(pair, part), n
            copies.append(remote(spot, spot, far_send.at[at], far_recv.at[at], peer))
        return copies

    def near_copies(pair, part, late):
        copies = []
        for n in range(2):
            spot = halves(pair, part, late)[n]
            at = unit(pair, part), n, late
            copies.append(remote(spot, spot, near_send.at[at], near_recv.at[at], sibling))
        return copies

    def give_mid(pair, part=WHOLE):
        @pl.when(is_end)
        def _():
            z_copy(pair, part, 2).wait_recv()

        start(mid_copies(pair, part))

    def give_far(pair, part=WHOLE):
        arrive(mid_copies(pair, part))
        start(far_copies(pair, part) + near_copies(pair, part, 0))

    def give_near(pair, part=WHOLE):
        arrive(far_copies(pair, part))
        start(near_copies(pair, part, 1))

    def finish(pair, part=WHOLE):
        arrive(near_copies(pair, part, 0) + near_copies(pair, part, 1))

    def choose(part):
        swap_wait(part, swap_recv)
        for pair in range(PAIRS):
            for n, tile in enumerate(PAIR_TILES[pair]):
                owner = owners[tile]
                value = stages[part][SLOTS * lax.rem(owner, PLANE) + slot_number(owners, tile)]
                chosen[2 * pair + n, :, third(part)] = jnp.where(
                    owner // PLANE == z, value, jnp.zeros_like(value)
                )

    def load(at):
        src = (x_hbm, cot_hbm, master_hbm)[at]
        dst = (x_then_hidden, cot_then_down, wide)[at]
        return pltpu.make_async_copy(src, dst, load_sem.at[at])

    def store(at):
        src, dst = (
            (hidden_turned, hidden_hbm),
            (ctx_ref, ctx_hbm),
            (hat_ref, hat_hbm),
            (cot_then_down, down_hbm),
            (mixed_ref, mixed_hbm),
            (wide, second_hbm),
            (x_turned, x_turned_hbm),
            (ctx_turned, ctx_turned_hbm),
        )[at]
        src = src.at[pl.ds(0, 2 * ROWS)] if src is wide else src
        return pltpu.make_async_copy(src, dst, store_sem.at[at])

    def w_store(pair):
        two = pl.ds(2 * pair, 2)
        return pltpu.make_async_copy(w_buf.at[two], w_out.at[two], out_sem.at[pair])

    def weight(at, cols=slice(None)):
        value = w_buf[at, :, :, :, :, cols]
        return value.reshape(width, value.shape[-1])

    def open_all():
        for at in range(3):
            load(at).start()
        sum_ref[...] = jnp.zeros_like(sum_ref)
        vec_ref[0:10, :] = bias_ref[...]
        vec_ref[10:12, :] = gain_ref[...]
        greet(z, in_plane)
        load(2).wait()
        for slot in range(SLOTS):
            low[slot] = wide[width * slot : width * (slot + 1), :].astype(jnp.bfloat16)
        for part in range(3):
            stages[part][pl.ds(2 * in_plane, 2)] = low[:, piece_rows(core, x, y), third(part)]

    def make_caps():
        for block in range(2):
            cap_ref[block] = attention_caps(counts, lengths, block)
        load(0).wait()
        x_turned[...] = x_then_hidden[...].T
        store(6).start()
        load(1).wait()

    actions = {
        "open": open_all,
        "caps": make_caps,
        "swap": swap,
        "sent": lambda part: swap_wait(part, swap_send),
        "choose": choose,
        "end": z_end,
        "middle": z_middle,
        "total": z_total,
        "mid": give_mid,
        "far": give_far,
        "near": give_near,
        "finish": finish,
        "keep": lambda pair: w_store(pair).start(),
    }

    for at, work in enumerate(FRONT_PLAN):

        @pl.when(step == at)
        def _():
            for name, *rest in work:
                actions[name](*rest)

    quad, block = step // 2, lax.rem(step, 2)
    here = pl.ds(pl.multiple_of(block * ROWS, ROWS), ROWS)

    @pl.when(step < 6)
    def _():
        attend_quad(
            quad,
            weight,
            x_then_hidden.at[here],
            vec_ref,
            cap_ref.at[block],
            q_ref,
            k_ref,
            v_ref,
            p_ref,
            ctx_ref.at[here],
        )

    @pl.when((step >= 4) & (step < 6))
    def _():
        branch = dot(ctx_ref[here, :], weight(3)) + vec_ref[2:3, :]
        hat, inverse = normalize(x_then_hidden[here, :].astype(jnp.float32) + branch)
        hat_ref[here, :] = hat.astype(jnp.bfloat16)
        inverse_ref[here, :] = inverse
        hidden = hat * vec_ref[10:11, :] + vec_ref[8:9, :]
        hidden_low = hidden.astype(jnp.bfloat16)
        x_then_hidden[here, :] = hidden_low
        hidden_turned[:, here] = hidden_low.T
        ctx_turned[:, here] = ctx_ref[here, :].T
        wide[here, :] = hidden + vec_ref[7:8, :]

    @pl.when(step == 5)
    def _():
        start([store(0), store(1), store(2), store(7)])

    turn = step - 6
    slot = lax.rem(turn, 2)

    def tile_stores(source_slot, tile):
        return [
            pltpu.make_async_copy(src.at[source_slot], dst.at[tile], tile_sem.at[source_slot, at])
            for at, (src, dst) in enumerate(((active_buf, active_hbm), (slope_buf, slope_hbm)))
        ]

    @pl.when(turn >= 2)
    def _():
        for copy in tile_stores(slot, 0):
            copy.wait()

    @pl.when(turn >= 0)
    def _():
        for half in range(2):
            rows = slice(ROWS * half, ROWS * half + ROWS)
            up = dot(x_then_hidden[rows, :], weight(4 + 2 * turn)) + vec_ref[pl.ds(3 + turn, 1), :]
            active, slope = gelu_parts(up)
            slope_buf[slot, rows, :] = slope.astype(jnp.bfloat16)
            active_buf[slot, :, rows] = active.T
            wide[rows, :] = wide[rows, :] + dot(active, weight(5 + 2 * turn))
        start(tile_stores(slot, turn))

    @pl.when(step == 9)
    def _():
        for half in range(2):
            rows = slice(ROWS * half, ROWS * half + ROWS)
            at_row = lax.broadcasted_iota(jnp.int32, (ROWS, 1), 0) + half * ROWS
            live = passage_facts(counts, lengths, at_row)[0].astype(jnp.float32)
            hat, inverse = normalize(wide[rows, :])
            mixed = (hat * vec_ref[11:12, :] + vec_ref[9:10, :]) * live
            mixed_ref[rows, :] = mixed.astype(jnp.bfloat16)
            grad_out = cot_then_down[rows, :].astype(jnp.float32) * live
            sum_ref[11:12, :] += columns_total(grad_out * hat)
            sum_ref[9:10, :] += columns_total(grad_out)
            second = normalize_back(grad_out * vec_ref[11:12, :], hat, inverse)
            wide[rows, :] = second
            down_low = second.astype(jnp.bfloat16)
            cot_then_down[rows, :] = down_low
            sum_ref[7:8, :] += columns_total(down_low.astype(jnp.float32))
        start([store(3), store(4), store(5)])
        for at in range(2):
            for copy in tile_stores(at, 0):
                copy.wait()
        for pair in range(PAIRS):
            w_store(pair).wait()
        swap_wait(2, swap_send)
        for pair, part in UNITS:
            for copy in mid_copies(pair, part) + far_copies(pair, part):
                copy.wait_send()
            for copy in near_copies(pair, part, 0) + near_copies(pair, part, 1):
                copy.wait_send()

            @pl.when(is_end)
            def _():
                z_copy(pair, part, 0).wait_send()

            @pl.when(is_middle)
            def _():
                z_copy(pair, part, 1).wait_send()
                z_copy(pair, part, 2).wait_send()

        for at in range(8):
            store(at).wait()


def gathered_and_forwarded(counts, lengths, owners, bias, gain, x, cotangent, master):
    tokens, width = x.shape
    blocks = tokens // ROWS
    low, high = jnp.bfloat16, jnp.float32
    smem = pl.BlockSpec(memory_space=pltpu.SMEM)
    any_space = pl.BlockSpec(memory_space=pl.ANY)
    dma = pltpu.SemaphoreType.DMA
    shaped = jax.ShapeDtypeStruct

    def at(step):
        step = jnp.minimum(step, 5)
        return lax.rem(step, 2), step // 2

    quad = pl.BlockSpec((ROWS, 256), at)
    rows = shaped((tokens, width), low)
    turned = shaped((width, tokens), low)
    cut = (2, 2, 2, PIECE, width)
    units = len(UNITS)
    return pl.pallas_call(
        gather_and_forward,
        grid=(10,),
        out_shape=(
            rows,
            rows,
            rows,
            shaped((blocks, HEADS, ROWS, ROWS), low),
            rows,
            turned,
            turned,
            turned,
            shaped((4, width, tokens), low),
            shaped((4, tokens, width), low),
            rows,
            rows,
            shaped((tokens, width), high),
            rows,
            shaped((TILES,) + cut, low),
            shaped((tokens, 1), high),
            shaped((16, width), high),
        ),
        in_specs=[smem] * 3
        + [pl.BlockSpec(bias.shape, lambda i: (0, 0)), pl.BlockSpec(gain.shape, lambda i: (0, 0))]
        + [any_space] * 3,
        out_specs=(quad, quad, quad, pl.BlockSpec((1, 4, ROWS, ROWS), lambda i: (*at(i), 0, 0)))
        + (any_space,) * 11
        + (
            pl.BlockSpec((tokens, 1), lambda i: (0, 0), pipeline_mode=pl.Buffered(1)),
            pl.BlockSpec((16, width), lambda i: (0, 0)),
        ),
        scratch_shapes=[
            pltpu.VMEM((VROWS, width), high),
            pltpu.VMEM((2, ROWS, ROWS), high),
            pltpu.VMEM((SLOTS * width, width), high),
            pltpu.VMEM((SLOTS, width, width), low),
            pltpu.VMEM((2 * PLANE, PIECE, 256), low),
            pltpu.VMEM((2 * PLANE, PIECE, 256), low),
            pltpu.VMEM((2 * PLANE, PIECE, 256), low),
            pltpu.VMEM((TILES, PIECE, width), low),
            pltpu.VMEM((TILES, PIECE, width), low),
            pltpu.VMEM((TILES, PIECE, width), low),
            pltpu.VMEM((TILES,) + cut, low),
            pltpu.VMEM((tokens, width), low),
            pltpu.VMEM((width, tokens), low),
            pltpu.VMEM((width, tokens), low),
            pltpu.VMEM((width, tokens), low),
            pltpu.VMEM((tokens, width), low),
            pltpu.VMEM((tokens, width), low),
            pltpu.VMEM((tokens, width), low),
            pltpu.VMEM((tokens, width), low),
            pltpu.VMEM((2, tokens, width), low),
            pltpu.VMEM((2, width, tokens), low),
            dma((3,)),
            dma((8,)),
            dma((2, 2)),
            dma((PAIRS,)),
            dma((3,)),
            dma((3,)),
            dma((3, units)),
            dma((3, units)),
            dma((units, 2)),
            dma((units, 2)),
            dma((units, 2)),
            dma((units, 2)),
            dma((units, 2, 2)),
            dma((units, 2, 2)),
        ],
        compiler_params=pltpu.CompilerParams(
            collective_id=0, has_side_effects=True, vmem_limit_bytes=63 * 2**20
        ),
        name="gather_and_forward",
    )(counts, lengths, owners, bias, gain, x, cotangent, master.reshape(SLOTS * width, width))


BACK_PLAN = (
    (),
    (),
    (
        ("core", 0),
    ),
    (),
    (
        ("far", 0),
    ),
    (),
    (
        ("core", 1),
    ),
    (
        ("mid", 0),
    ),
    (
        ("core", 3),
        ("core", 2),
        ("far", 1),
        ("end", 0),
    ),
    (),
    (
        ("far", 3),
    ),
    (),
    (
        ("mid", 1),
    ),
    (
        ("middle", 0),
        ("mid", 3),
        ("far", 2),
    ),
    (
        ("end", 1),
    ),
    (
        ("core", 4),
        ("total", 0),
        ("far", 4),
        ("middle", 1),
        ("end", 3),
    ),
    (
        ("middle", 3),
        ("mid", 4),
        ("total", 1),
    ),
    (
        ("mid", 2),
        ("end", 4),
    ),
    (
        ("middle", 4),
        ("core", 5),
        ("end", 2),
        ("total", 3),
    ),
    (
        ("far", 5),
        ("take", 0),
        ("middle", 2),
        ("total", 4),
    ),
    (
        ("take", 1),
        ("core", 6),
        ("mid", 5),
        ("total", 2),
        ("far", 6),
        ("input", 0),
        ("sum", 0),
        ("input", 1),
        ("end", 5),
        ("take", 4),
        ("middle", 5),
        ("mid", 6),
        ("take", 3),
        ("sum", 1),
        ("take", 2),
        ("deliver", 0),
        ("end", 6),
        ("total", 5),
        ("middle", 6),
        ("sum", 2),
        ("take", 5),
        ("deliver", 1),
        ("total", 6),
        ("take", 6),
        ("deliver", 2),
    ),
)


def backward_and_reduce(
    owners,
    p_ref,
    q_ref,
    k_ref,
    v_ref,
    ctx_ref,
    inverse_ref,
    gain_ref,
    late_ref,
    x_turned_hbm,
    ctx_turned_hbm,
    hidden_hbm,
    active_hbm,
    slope_hbm,
    down_hbm,
    second_hbm,
    hat_hbm,
    w_hbm,
    input_hbm,
    slot_grad,
    vec_out,
    w_part,
    acc,
    hidden_then_x,
    active_then_ctx,
    down_then_branch,
    grad_ctx_ref,
    hat_ref,
    slope_then_query,
    up_then_key,
    value_buf,
    part,
    from_core,
    from_far,
    from_mid,
    from_end,
    from_middle,
    total,
    snap,
    outbox,
    vec_now,
    vec_in,
    holds,
    keeps,
    load_sem,
    w_sem,
    core_send,
    core_recv,
    far_send,
    far_recv,
    mid_send,
    mid_recv,
    z_send,
    z_recv,
    vec_send,
    vec_recv,
    out_send,
    out_recv,
):
    step = pl.program_id(0)
    inner = jnp.maximum(step - 4, 0)
    quad, block, pair = inner // 4, lax.rem(inner, 4) // 2, lax.rem(inner, 2)
    me = lax.axis_index("dp")
    z, y, x, core = place(me)
    in_plane = lax.rem(me, PLANE)
    sibling = me + 1 - 2 * core
    x_peer = me + 2 - 4 * x
    y_peer = me + 4 - 8 * y
    z_targets = along_z(z, in_plane)
    is_end = (z == 0) | (z == 3)
    is_middle = (z == 1) | (z == 2)

    def items(batch):
        if batch < 4:
            return [(0, 4 + 2 * batch, slice(None)), (1, 5 + 2 * batch, slice(None))]
        cols = pl.ds(256 * (batch - 4), 256)
        return [(0, 0, cols), (1, 1, cols), (0, 2, cols), (1, 3, cols)]

    def half_of(tile, side):
        return part.at[tile, side] if tile < 4 else w_part.at[tile, side]

    def held(tile):
        return half_of(tile, core)

    def core_copies(batch):
        return [
            remote(
                half_of(tile, 1 - core).at[:, :, :, cols],
                from_core.at[tile, :, :, :, cols],
                core_send.at[batch, n],
                core_recv.at[batch, n],
                sibling,
            )
            for n, (_, tile, cols) in enumerate(items(batch))
        ]

    def far_copies(batch):
        copies = []
        for n, (kind, tile, cols) in enumerate(items(batch)):
            mine = held(tile)
            copies.append(
                remote(
                    mine.at[:, 1 - y, :, cols] if kind else mine.at[1 - x, :, :, cols],
                    from_far.at[tile, :, :, cols],
                    far_send.at[batch, n],
                    far_recv.at[batch, n],
                    y_peer if kind else x_peer,
                )
            )
        return copies

    def mid_copies(batch):
        copies = []
        for n, (kind, tile, cols) in enumerate(items(batch)):
            mine = held(tile)
            copies.append(
                remote(
                    mine.at[1 - x, y, :, cols] if kind else mine.at[x, 1 - y, :, cols],
                    from_mid.at[tile, :, cols],
                    mid_send.at[batch, n],
                    mid_recv.at[batch, n],
                    x_peer if kind else y_peer,
                )
            )
        return copies

    def z_copies(batch, stage):
        copies = []
        for n, (_, tile, cols) in enumerate(items(batch)):
            if stage == 2:
                src, dst = total.at[tile, :, cols], total.at[tile, :, cols]
            else:
                src = held(tile).at[x, y, :, cols]
                dst = (from_middle if stage else from_end).at[tile, :, cols]
            copies.append(
                remote(
                    src,
                    dst,
                    z_send.at[stage, batch, n],
                    z_recv.at[stage, batch, n],
                    z_targets[stage],
                )
            )
        return copies

    def give_core(batch):
        start(core_copies(batch))

    def give_far(batch):
        arrive(core_copies(batch))
        for _, tile, cols in items(batch):
            mine = held(tile)
            mine[:, :, :, cols] = mine[:, :, :, cols] + from_core[tile, :, :, :, cols]
        start(far_copies(batch))

    def give_mid(batch):
        arrive(far_copies(batch))
        for kind, tile, cols in items(batch):
            mine = held(tile)
            if kind:
                mine[:, y, :, cols] = mine[:, y, :, cols] + from_far[tile, :, :, cols]
            else:
                mine[x, :, :, cols] = mine[x, :, :, cols] + from_far[tile, :, :, cols]
        start(mid_copies(batch))

    def give_end(batch):
        arrive(mid_copies(batch))
        for _, tile, cols in items(batch):
            mine = held(tile)
            mine[x, y, :, cols] = mine[x, y, :, cols] + from_mid[tile, :, cols]

        @pl.when(is_end)
        def _():
            start(z_copies(batch, 0))

    def give_middle(batch):
        @pl.when(is_middle)
        def _():
            arrive(z_copies(batch, 0))
            for _, tile, cols in items(batch):
                mine = held(tile)
                mine[x, y, :, cols] = mine[x, y, :, cols] + from_end[tile, :, cols]
            start(z_copies(batch, 1))

    def give_total(batch):
        @pl.when(is_middle)
        def _():
            arrive(z_copies(batch, 1))
            for _, tile, cols in items(batch):
                mine = held(tile)
                total[tile, :, cols] = mine[x, y, :, cols] + from_middle[tile, :, cols]
            start(z_copies(batch, 2))

    def take_total(batch):
        @pl.when(is_end)
        def _():
            arrive(z_copies(batch, 2))

    def deliver(third):
        cols = pl.ds(256 * third, 256)
        snap[...] = total[:, :, cols]

        def fill(at, carry):
            value = snap[holds[at]]
            outbox[third, at] = jnp.where(keeps[at] > 0, value, jnp.zeros_like(value))
            return carry

        lax.fori_loop(0, 2 * PLANE, fill, 0)

        def send(hop, carry):
            target = lax.rem(in_plane + hop, PLANE)
            remote(
                outbox.at[third, pl.ds(2 * target, 2)],
                slot_grad.at[:, core, x, y, :, cols],
                out_send.at[third],
                out_recv.at[third],
                z * PLANE + target,
            ).start()
            return carry

        lax.fori_loop(1, PLANE, send, 0)
        keep_copy(third).start()

    def keep_copy(third):
        return pltpu.make_async_copy(
            outbox.at[third, pl.ds(2 * in_plane, 2)],
            slot_grad.at[:, core, x, y, :, pl.ds(256 * third, 256)],
            load_sem.at[5 + third],
        )

    def vec_copies(stage):
        if stage < 3:
            hops = [(stage, (sibling, x_peer, y_peer)[stage])]
        else:
            hops = [
                (2 + hop, lax.rem(z + hop, 4) * PLANE + in_plane) for hop in range(1, 4)
            ]
        return [
            remote(vec_now.at[stage], vec_in.at[at], vec_send.at[at], vec_recv.at[at], device)
            for at, device in hops
        ]

    def vec_next(stage):
        arrive(vec_copies(stage))
        vec_now[stage + 1] = vec_now[stage] + vec_in[stage]
        start(vec_copies(stage + 1))

    def input_store():
        return pltpu.make_async_copy(acc, input_hbm, load_sem.at[4])

    def load(at):
        src, dst = (
            (hidden_hbm, hidden_then_x),
            (down_hbm, down_then_branch),
            (second_hbm, acc),
            (hat_hbm, hat_ref),
            None,
            None,
            None,
            None,
            (x_turned_hbm, hidden_then_x),
            (ctx_turned_hbm, active_then_ctx),
        )[at]
        return pltpu.make_async_copy(src, dst, load_sem.at[at])

    def tile_load(tile, side):
        src, dst = ((slope_hbm, slope_then_query), (active_hbm, active_then_ctx))[side]
        return pltpu.make_async_copy(src.at[tile], dst, load_sem.at[10 + side])

    def w_load(at):
        return pltpu.make_async_copy(w_hbm.at[at], w_part.at[at], w_sem.at[at])

    def weight(at, cols=slice(None)):
        value = w_part[at, :, :, :, :, cols]
        return value.reshape(8 * PIECE, value.shape[-1])

    def input_rows(half):
        rows = slice(ROWS * half, ROWS * half + ROWS)
        more = acc[rows, :]
        for at, buf in enumerate((slope_then_query, up_then_key, value_buf)):
            more = more + dot_back(buf[rows, :], weight(at))
        acc[rows, :] = more
        if half == 1:
            input_store().start()

    actions = {
        "core": give_core,
        "far": give_far,
        "mid": give_mid,
        "end": give_end,
        "middle": give_middle,
        "total": give_total,
        "take": take_total,
        "deliver": deliver,
        "sum": vec_next,
        "input": input_rows,
    }

    @pl.when(step == 0)
    def _():
        start([load(1), tile_load(0, 0), w_load(5), w_load(4), load(2), tile_load(0, 1), load(0)])
        start([w_load(at) for at in range(6, TILES)] + [load(3)] + [w_load(3 - at) for at in range(4)])
        for at in range(2 * PLANE):
            tile_here, kept = jnp.int32(0), jnp.int32(0)
            for tile in range(TILES):
                place_of = SLOTS * owners[tile] + slot_number(owners, tile)
                match = place_of == z * 2 * PLANE + at
                tile_here = tile_here + jnp.where(match, POSITIONS.index(tile), 0)
                kept = kept + jnp.where(match, 1, 0)
            holds[at] = tile_here
            keeps[at] = kept
        vec_now[0] = late_ref[...]
        greet(z, in_plane)

    def serve(points):
        for at in points:
            if BACK_PLAN[at]:

                @pl.when(step == (at // 2 if at < 8 else at - 4))
                def _():
                    for name, number in BACK_PLAN[at]:
                        actions[name](number)

    serve(range(0, 8, 2))

    @pl.when(step < 4)
    def _():
        tile_load(step, 0).wait()
        w_load(5 + 2 * step).wait()

        @pl.when(step == 0)
        def _():
            load(1).wait()

        for half in range(2):
            rows = slice(ROWS * half, ROWS * half + ROWS)
            back = dot_back(down_then_branch[rows, :], weight(5 + 2 * step))
            up_low = (back * slope_then_query[rows, :].astype(jnp.float32)).astype(jnp.bfloat16)
            up_then_key[rows, :] = up_low
            vec_now[0, pl.ds(3 + step, 1), :] += columns_total(up_low.astype(jnp.float32))

        @pl.when(step < 3)
        def _():
            tile_load(step + 1, 0).start()

        w_load(4 + 2 * step).wait()

        @pl.when(step == 0)
        def _():
            load(2).wait()
            load(0).wait()

        for half in range(2):
            rows = slice(ROWS * half, ROWS * half + ROWS)
            acc[rows, :] = acc[rows, :] + dot_back(up_then_key[rows, :], weight(4 + 2 * step))

    serve(range(1, 8, 2))

    @pl.when(step < 4)
    def _():
        tile_load(step, 1).wait()
        by_down = dot(active_then_ctx[...], down_then_branch[...]).astype(jnp.bfloat16)
        w_part[5 + 2 * step] = by_down.reshape(2, 2, 2, PIECE, 8 * PIECE)

        @pl.when(step < 3)
        def _():
            tile_load(step + 1, 1).start()

        by_up = dot(hidden_then_x[...], up_then_key[...]).astype(jnp.bfloat16)
        w_part[4 + 2 * step] = by_up.reshape(2, 2, 2, PIECE, 8 * PIECE)

    @pl.when(step == 3)
    def _():
        start([load(8), load(9)])
        load(3).wait()
        for at in range(4):
            w_load(at).wait()
        for half in range(2):
            rows = slice(ROWS * half, ROWS * half + ROWS)
            grad_hidden, hat = acc[rows, :], hat_ref[rows, :].astype(jnp.float32)
            vec_now[0, 10:11, :] += columns_total(grad_hidden * hat)
            vec_now[0, 8:9, :] += columns_total(grad_hidden)
            first = normalize_back(grad_hidden * gain_ref[0:1, :], hat, inverse_ref[rows, :])
            acc[rows, :] = first
            branch_low = first.astype(jnp.bfloat16)
            down_then_branch[rows, :] = branch_low
            vec_now[0, 2:3, :] += columns_total(branch_low.astype(jnp.float32))
            grad_ctx_ref[rows, :] = dot_back(branch_low, weight(3)).astype(jnp.bfloat16)

    serve(range(8, 20))

    here = pl.ds(pl.multiple_of(block * ROWS, ROWS), ROWS)
    quad_cols = pl.ds(pl.multiple_of(quad * 256, 256), 256)

    pair_cols = pl.ds(pl.multiple_of(quad * 256 + pair * 128, 128), 128)
    grad_bufs = (slope_then_query, up_then_key, value_buf)

    @pl.when(step >= 4)
    def _():
        grads = attend_back_pair(
            grad_ctx_ref[here, pair_cols],
            ctx_ref[here, pair_cols],
            p_ref.at[0],
            q_ref[...],
            k_ref[...],
            v_ref[...],
        )
        for buf, grad in zip(grad_bufs, grads):
            buf[here, pair_cols] = grad
        vec_now[0, 0:1, pair_cols] += columns_total(grads[0].astype(jnp.float32))
        vec_now[0, 1:2, pair_cols] += columns_total(grads[2].astype(jnp.float32))

    @pl.when(step == 7)
    def _():
        load(8).wait()
        load(9).wait()

    @pl.when((step >= 4) & (block == 1) & (pair == 1))
    def _():
        for tile in range(4):
            if tile < 3:
                value = dot(hidden_then_x[...], grad_bufs[tile][:, quad_cols])
            else:
                value = dot(active_then_ctx[...], down_then_branch[:, quad_cols])
            value = value.astype(jnp.bfloat16).reshape(2, 2, 2, PIECE, 256)
            part[tile, :, :, :, :, quad_cols] = value


    @pl.when(step == 15)
    def _():
        start(vec_copies(0))
        for name, number in BACK_PLAN[-1]:
            actions[name](number)
        arrive(vec_copies(3))
        summed = jnp.zeros(vec_out.shape, jnp.float32)
        for origin in range(4):
            hop = lax.rem(z - origin + 4, 4)
            summed = summed + jnp.where(hop == 0, vec_now[3], vec_in[2 + jnp.maximum(hop, 1)])
        vec_out[...] = summed
        for batch in range(7):
            for copy in core_copies(batch) + far_copies(batch) + mid_copies(batch):
                copy.wait_send()

            @pl.when(is_end)
            def _():
                for copy in z_copies(batch, 0):
                    copy.wait_send()

            @pl.when(is_middle)
            def _():
                for copy in z_copies(batch, 1) + z_copies(batch, 2):
                    copy.wait_send()

        for stage in range(4):
            for copy in vec_copies(stage):
                copy.wait_send()
        input_store().wait()
        for third in range(3):
            keep_copy(third).wait()
            most = outbox.at[third, pl.ds(0, 2 * PLANE - 2)]
            pltpu.make_async_copy(most, most, out_recv.at[third]).wait()
            pltpu.make_async_copy(most, most, out_send.at[third]).wait()


def backward_and_reduced(
    owners,
    probs,
    query,
    keyed,
    valued,
    context,
    inverse,
    gain,
    late_sums,
    x_turned,
    ctx_turned,
    hidden,
    active,
    slope,
    grad_down,
    grad_second,
    hat,
    weights,
):
    tokens, width = grad_down.shape
    low, high = jnp.bfloat16, jnp.float32
    shaped = jax.ShapeDtypeStruct
    smem = pl.BlockSpec(memory_space=pltpu.SMEM)
    any_space = pl.BlockSpec(memory_space=pl.ANY)
    dma = pltpu.SemaphoreType.DMA
    once = pl.Buffered(1)

    def at(step):
        inner = jnp.maximum(step - 4, 0)
        return lax.rem(inner, 4) // 2, inner // 4 * 2 + lax.rem(inner, 2)

    pair = pl.BlockSpec((ROWS, 128), at)
    sums = pl.BlockSpec((16, width), lambda i: (0, 0))
    cut = (2, 2, 2, PIECE, width)
    input_grad, slot_grads, vector_sums = pl.pallas_call(
        backward_and_reduce,
        grid=(16,),
        out_shape=(
            shaped((tokens, width), high),
            shaped((SLOTS,) + cut, low),
            shaped((16, width), high),
        ),
        in_specs=[smem, pl.BlockSpec((1, 2, ROWS, ROWS), lambda i: (*at(i), 0, 0))]
        + [pair] * 3
        + [
            pl.BlockSpec((tokens, width), lambda i: (0, 0), pipeline_mode=once),
            pl.BlockSpec((tokens, 1), lambda i: (0, 0), pipeline_mode=once),
            pl.BlockSpec(gain.shape, lambda i: (0, 0)),
            sums,
        ]
        + [any_space] * 9,
        out_specs=(any_space, any_space, sums),
        scratch_shapes=[
            pltpu.VMEM((TILES,) + cut, low),
            pltpu.VMEM((tokens, width), high),
            pltpu.VMEM((width, tokens), low),
            pltpu.VMEM((width, tokens), low),
            pltpu.VMEM((tokens, width), low),
            pltpu.VMEM((tokens, width), low),
            pltpu.VMEM((tokens, width), low),
            pltpu.VMEM((tokens, width), low),
            pltpu.VMEM((tokens, width), low),
            pltpu.VMEM((tokens, width), low),
            pltpu.VMEM((4,) + cut, low),
            pltpu.VMEM((TILES,) + cut[1:], low),
            pltpu.VMEM((TILES,) + cut[2:], low),
            pltpu.VMEM((TILES,) + cut[3:], low),
            pltpu.VMEM((TILES,) + cut[3:], low),
            pltpu.VMEM((TILES,) + cut[3:], low),
            pltpu.VMEM((TILES,) + cut[3:], low),
            pltpu.VMEM((TILES, PIECE, 256), low),
            pltpu.VMEM((3, 2 * PLANE, PIECE, 256), low),
            pltpu.VMEM((4, 16, width), high),
            pltpu.VMEM((6, 16, width), high),
            pltpu.SMEM((2 * PLANE,), jnp.int32),
            pltpu.SMEM((2 * PLANE,), jnp.int32),
            dma((12,)),
            dma((TILES,)),
            dma((7, 4)),
            dma((7, 4)),
            dma((7, 4)),
            dma((7, 4)),
            dma((7, 4)),
            dma((7, 4)),
            dma((3, 7, 4)),
            dma((3, 7, 4)),
            dma((6,)),
            dma((6,)),
            dma((3,)),
            dma((3,)),
        ],
        compiler_params=pltpu.CompilerParams(
            collective_id=1, has_side_effects=True, vmem_limit_bytes=63 * 2**20
        ),
        name="backward_and_reduce",
    )(
        owners,
        probs,
        query,
        keyed,
        valued,
        context,
        inverse,
        gain,
        late_sums,
        x_turned,
        ctx_turned,
        hidden,
        active,
        slope,
        grad_down,
        grad_second,
        hat,
        weights,
    )
    return input_grad, slot_grads.reshape(SLOTS, width, width), vector_sums


def collected_tiles(tile_low, owners, slots):
    mine = owners == lax.axis_index("dp")
    local = jnp.where(mine[:, None, None], tile_low[slots], jnp.zeros((), tile_low.dtype))
    return lax.psum(local, "dp")


def summed_over_slice(parts, vector_terms, owners, slots):
    myself = lax.axis_index("dp")

    def add(held, items):
        part, owner, slot = items
        total = lax.psum(part.astype(jnp.float32), "dp")
        here = (owner == myself) & (slot == jnp.arange(SLOTS, dtype=jnp.int32))
        return held + jnp.where(here[:, None, None], total[None], 0.0), None

    empty = jnp.zeros((SLOTS,) + parts.shape[1:], jnp.float32)
    return lax.scan(add, empty, (parts, owners, slots))[0], lax.psum(vector_terms, "dp")


def body(
    inputs,
    cotangent,
    counts,
    lengths,
    owners,
    tile_master,
    tile_first,
    tile_second,
    tile_ema,
    bias_vals,
    gain_vals,
    vector_first,
    vector_second,
    vector_ema,
):
    tokens = inputs.shape[0]
    small = lax.axis_size("dp") == GROUP
    gain_scale = float(tokens * lax.axis_size("dp")) ** (-0.5)
    if small:
        (
            query,
            keyed,
            valued,
            probs,
            context,
            x_turned,
            ctx_turned,
            hidden,
            active,
            slope,
            grad_down,
            mixed,
            grad_second,
            hat,
            weights,
            inverse,
            late_sums,
        ) = gathered_and_forwarded(
            counts,
            lengths,
            owners,
            bias_vals,
            gain_vals,
            inputs,
            cotangent,
            tile_master,
        )
        input_grad, slot_grads, full_sums = backward_and_reduced(
            owners,
            probs,
            query,
            keyed,
            valued,
            context,
            inverse,
            gain_vals,
            late_sums,
            x_turned,
            ctx_turned,
            hidden,
            active,
            slope,
            grad_down,
            grad_second,
            hat,
            weights,
        )
    else:
        slots = tile_slots(owners)
        vectors = jnp.concatenate([bias_vals, gain_vals], 0)
        weights = collected_tiles(tile_master[0].astype(jnp.bfloat16), owners, slots)
        query, keyed, valued, probs, context, hat, inverse = attended(
            counts, lengths, inputs, weights, vectors
        )
        mixed, grad_first, grad_branch, grad_context, up_grads, down_grads, late_sums = fed_forward_both(
            counts, lengths, hat, inverse, cotangent, weights, vectors
        )
        input_grad, early_grads, early_sums = attended_back(
            probs, query, keyed, valued, inputs, context, grad_context, grad_branch, grad_first, weights
        )
        parts = jnp.concatenate([early_grads, up_grads, down_grads], 0)
        slot_grads, full_sums = summed_over_slice(parts, late_sums + early_sums, owners, slots)
    return updated(
        gain_scale,
        slot_grads,
        tile_master,
        tile_first,
        tile_second,
        tile_ema,
        full_sums,
        bias_vals,
        gain_vals,
        vector_first,
        vector_second,
        vector_ema,
        mixed,
        input_grad,
    )


def solution(mesh):
    placed = (
        P("dp", None),
        P("dp", None),
        P("dp", None),
        P("dp", None),
        P(),
        P("dp", None, None, None),
        P("dp", None, None, None),
        P("dp", None, None, None),
        P("dp", None, None, None),
        P(),
        P(),
        P(),
        P(),
        P(),
    )
    return jax.shard_map(
        body,
        mesh=mesh,
        in_specs=placed,
        out_specs=(
            P("dp", None),
            P("dp", None),
            P("dp", None, None, None),
            P("dp", None, None, None),
            P("dp", None, None, None),
            P("dp", None, None, None),
            P("dp", None, None, None),
            P(),
            P(),
            P(),
            P(),
        ),
        check_vma=False,
    )
```

```python
import functools

import jax
import jax.numpy as jnp
from jax import lax
from jax.experimental import pallas as pl
from jax.experimental.pallas import tpu as pltpu
from jax.sharding import PartitionSpec as P

HEADS = 12
BUCKET = 128
SLOTS = 2
TILES = 12
VROWS = 12
STEP = 5

norm_epsilon = 1e-12
tile_rate = 0.03
vector_rate = 0.2
first_decay = 0.5
second_decay = 0.5
adam_epsilon = 1e-08
weight_decay = 0.01
average_rate = 0.9


def tile_slots(owners):
    order = jnp.arange(owners.shape[0], dtype=jnp.int32)
    same = owners[:, None] == owners[None, :]
    earlier = order[None, :] < order[:, None]
    return jnp.sum((same & earlier).astype(jnp.int32), 1)


def adam_update(param, grad, first, second, rate):
    first_new = first_decay * first + (1.0 - first_decay) * grad
    second_new = second_decay * second + (1.0 - second_decay) * grad * grad
    first_hat = first_new / (1.0 - first_decay**STEP)
    second_hat = second_new / (1.0 - second_decay**STEP)
    param_new = param - rate * (
        first_hat / (jnp.sqrt(second_hat) + adam_epsilon) + weight_decay * param
    )
    return (param_new, first_new, second_new)


ROWS = 4 * BUCKET
TAIL_RATE = 0.28
TAIL_SERIES = (
    0.11615256574707405,
    0.06981038475559553,
    0.2631359597579608,
    -0.22983675561378278,
    0.38546775012288165,
    -0.10472989053809521,
)
INV_SQRT_TAU = 0.3989422804014327
ALLOWED = 3.0e38
BARRED = -1000000000.0


def dot(left, right):
    return jnp.dot(left, right, preferred_element_type=jnp.float32)


def dot_back(left, right):
    return lax.dot_general(
        left, right, (((1,), (1,)), ((), ())), preferred_element_type=jnp.float32
    )


def outer(left, right):
    return lax.dot_general(
        left, right, (((0,), (0,)), ((), ())), preferred_element_type=jnp.float32
    )


def passage_facts(counts, lengths, position):
    places = lengths.shape[1]
    big_end = counts[0, 0]
    mid_end = big_end + counts[0, 1]
    all_end = mid_end + counts[0, 2]
    start = jnp.int32(0)
    member = jnp.zeros(position.shape, jnp.int32)
    usable = jnp.zeros(position.shape, jnp.int32)
    for number in range(places):
        size = jnp.where(
            number < big_end,
            4 * BUCKET,
            jnp.where(number < mid_end, 2 * BUCKET, jnp.where(number < all_end, BUCKET, 0)),
        )
        inside = (position >= start) & (position < start + size)
        live = inside & (position < start + lengths[0, number])
        member = jnp.where(inside, number + 1, member)
        usable = jnp.where(live, 1, usable)
        start = start + size
    passage = jnp.where(member > 0, member - 1, places + position // BUCKET)
    return usable, passage


def normalize(values):
    center = jnp.mean(values, -1, keepdims=True)
    centered = values - center
    spread = jnp.mean(centered * centered, -1, keepdims=True)
    inverse = lax.rsqrt(spread + norm_epsilon)
    return centered * inverse, inverse


def normalize_back(grad, hat, inverse):
    center = jnp.mean(grad, -1, keepdims=True)
    along = jnp.mean(grad * hat, -1, keepdims=True)
    return inverse * (grad - center - hat * along)


def columns_total(values):
    return jnp.sum(values, 0, keepdims=True)


def attention_caps(counts, lengths, block):
    at_row = lax.broadcasted_iota(jnp.int32, (ROWS, 1), 0) + block * ROWS
    at_column = lax.broadcasted_iota(jnp.int32, (1, ROWS), 1) + block * ROWS
    _, passage_row = passage_facts(counts, lengths, at_row)
    usable_column, passage_column = passage_facts(counts, lengths, at_column)
    allowed = (passage_row == passage_column) & ((usable_column == 1) | (at_row == at_column))
    return jnp.where(allowed, ALLOWED, BARRED)


def attend_quad(quad, weight, x_ref, vec_ref, cap_ref, q_ref, k_ref, v_ref, p_ref, ctx_ref):
    cols = pl.ds(pl.multiple_of(quad * 256, 256), 256)
    x = x_ref[...]
    query = (dot(x, weight(0, cols)) + vec_ref[0:1, cols]).astype(jnp.bfloat16)
    query = query * jnp.bfloat16(0.125)
    keyed = dot(x, weight(1, cols)).astype(jnp.bfloat16)
    valued = (dot(x, weight(2, cols)) + vec_ref[1:2, cols]).astype(jnp.bfloat16)
    q_ref[...] = query
    k_ref[...] = keyed
    v_ref[...] = valued
    low_half = lax.broadcasted_iota(jnp.int32, (1, 128), 1) < 64
    for pair in range(2):
        part = slice(128 * pair, 128 * pair + 128)
        contexts = []
        for head in range(2):
            here = low_half if head == 0 else ~low_half
            mine = jnp.where(here, query[:, part], jnp.zeros_like(query[:, part]))
            scores = jnp.minimum(dot_back(mine, keyed[:, part]), cap_ref[...])
            exponent = jnp.exp(scores - jnp.max(scores, -1, keepdims=True))
            inverse = 1.0 / jnp.sum(exponent, -1, keepdims=True)
            probability = (exponent * inverse).astype(jnp.bfloat16)
            p_ref[0, 2 * pair + head] = probability
            contexts.append(dot(probability, valued[:, part]))
        both = jnp.where(low_half, contexts[0], contexts[1]).astype(jnp.bfloat16)
        ctx_ref[:, pl.ds(pl.multiple_of(quad * 256 + 128 * pair, 128), 128)] = both


def close_block(w_out, x_ref, vec_ref, ctx_ref, hat_ref, inverse_ref):
    branch = dot(ctx_ref[...], w_out) + vec_ref[2:3, :]
    hat_ref[...], inverse_ref[...] = normalize(x_ref[...].astype(jnp.float32) + branch)


def attend_back_pair(pull, level_from, p_ref, query, keyed, valued):
    low_half = lax.broadcasted_iota(jnp.int32, (1, 128), 1) < 64
    along = pull.astype(jnp.float32) * level_from.astype(jnp.float32)
    by_query, by_key, by_value = [], [], []
    for head in range(2):
        mask = low_half if head == 0 else ~low_half
        mine = jnp.where(mask, pull, jnp.zeros_like(pull))
        level = jnp.sum(jnp.where(mask, along, 0.0), -1, keepdims=True)
        probability = p_ref[head]
        grad_prob = dot_back(mine, valued)
        grad_scores = (probability.astype(jnp.float32) * (grad_prob - level)).astype(jnp.bfloat16)
        by_query.append(dot(grad_scores, keyed))
        by_key.append(outer(grad_scores, query))
        by_value.append(outer(probability, pull))
    grad_query = jnp.where(low_half, by_query[0], by_query[1]) * 0.125
    grad_key = jnp.where(low_half, by_key[0], by_key[1])
    grad_value = jnp.where(low_half, by_value[0], by_value[1])
    return [value.astype(jnp.bfloat16) for value in (grad_query, grad_key, grad_value)]


def gelu_parts(up):
    near = 1.0 / (1.0 + TAIL_RATE * jnp.abs(up))
    decay = jnp.exp(up * up * -0.5)
    series = jnp.full_like(near, TAIL_SERIES[-1])
    for term in TAIL_SERIES[-2::-1]:
        series = series * near + term
    tail = series * near * decay
    share = jnp.where(up < 0.0, tail, 1.0 - tail)
    slope = share + up * (decay * INV_SQRT_TAU)
    return (up * share).astype(jnp.bfloat16), slope


def attend_forward(
    counts,
    lengths,
    x_ref,
    w_hbm,
    vec_ref,
    q_ref,
    k_ref,
    v_ref,
    p_ref,
    ctx_ref,
    hat_ref,
    inverse_ref,
    w_buf,
    cap_ref,
    w_sem,
):
    block, quad = pl.program_id(0), pl.program_id(1)
    loads = [pltpu.make_async_copy(w_hbm.at[at], w_buf.at[at], w_sem.at[at]) for at in range(4)]

    @pl.when((block == 0) & (quad == 0))
    def _():
        for load in loads:
            load.start()
        for load in loads:
            load.wait()

    @pl.when(quad == 0)
    def _():
        cap_ref[...] = attention_caps(counts, lengths, block)

    def weight(at, cols):
        return w_buf[at, :, cols]

    attend_quad(quad, weight, x_ref, vec_ref, cap_ref, q_ref, k_ref, v_ref, p_ref, ctx_ref)

    @pl.when(quad == 2)
    def _():
        close_block(w_buf[3], x_ref, vec_ref, ctx_ref, hat_ref, inverse_ref)


def attended(counts, lengths, x, weights, vectors):
    tokens, width = x.shape
    blocks = tokens // ROWS
    low = jnp.bfloat16
    smem = pl.BlockSpec(memory_space=pltpu.SMEM)
    quad = pl.BlockSpec((ROWS, 256), lambda b, h: (b, h))
    rows = pl.BlockSpec((ROWS, width), lambda b, h: (b, 0))
    shaped = jax.ShapeDtypeStruct
    return pl.pallas_call(
        attend_forward,
        grid=(blocks, 3),
        out_shape=(
            shaped((tokens, width), low),
            shaped((tokens, width), low),
            shaped((tokens, width), low),
            shaped((blocks, HEADS, ROWS, ROWS), low),
            shaped((tokens, width), low),
            shaped((tokens, width), jnp.float32),
            shaped((tokens, 1), jnp.float32),
        ),
        in_specs=[
            smem,
            smem,
            rows,
            pl.BlockSpec(memory_space=pl.ANY),
            pl.BlockSpec((VROWS, width), lambda b, h: (0, 0)),
        ],
        out_specs=(
            quad,
            quad,
            quad,
            pl.BlockSpec((1, 4, ROWS, ROWS), lambda b, h: (b, h, 0, 0)),
            rows,
            rows,
            pl.BlockSpec((ROWS, 1), lambda b, h: (b, 0)),
        ),
        scratch_shapes=[
            pltpu.VMEM((4, width, width), low),
            pltpu.VMEM((ROWS, ROWS), jnp.float32),
            pltpu.SemaphoreType.DMA((4,)),
        ],
        compiler_params=pltpu.CompilerParams(vmem_limit_bytes=56 * 2**20),
        name="attend_forward",
    )(counts, lengths, x, weights, vectors)


def feed_forward_both(
    counts,
    lengths,
    hat_ref,
    inverse_ref,
    cot_ref,
    w_hbm,
    vec_ref,
    mixed_ref,
    first_ref,
    branch_ref,
    context_ref,
    up_grad_ref,
    down_grad_ref,
    sum_ref,
    w_buf,
    active_ref,
    up_ref,
    hidden_ref,
    down_ref,
    slope_ref,
    w_sem,
):
    step = pl.program_id(0)
    blocks = pl.num_programs(0) - 4
    loads = [
        pltpu.make_async_copy(w_hbm.at[3 + at], w_buf.at[at], w_sem.at[at]) for at in range(9)
    ]

    @pl.when(step == 0)
    def _():
        for load in loads[1:] + loads[:1]:
            load.start()
        sum_ref[...] = jnp.zeros_like(sum_ref)
        for load in loads[1:] + loads[:1]:
            load.wait()

    @pl.when(step < blocks)
    def _():
        here = pl.ds(pl.multiple_of(step * ROWS, ROWS), ROWS)
        at_row = lax.broadcasted_iota(jnp.int32, (ROWS, 1), 0) + step * ROWS
        live = passage_facts(counts, lengths, at_row)[0].astype(jnp.float32)
        hat = hat_ref[...]
        hidden = hat * vec_ref[10:11, :] + vec_ref[8:9, :]
        hidden_low = hidden.astype(jnp.bfloat16)
        hidden_ref[here, :] = hidden_low
        total = hidden + vec_ref[7:8, :]
        for tile in range(4):
            up = dot(hidden_low, w_buf[1 + tile]) + vec_ref[3 + tile : 4 + tile, :]
            active, slope = gelu_parts(up)
            slope_ref[tile] = slope.astype(jnp.bfloat16)
            active_ref[tile, here, :] = active
            total = total + dot(active, w_buf[5 + tile])
        hat_two, inverse_two = normalize(total)
        mixed_ref[...] = ((hat_two * vec_ref[11:12, :] + vec_ref[9:10, :]) * live).astype(jnp.bfloat16)
        grad_out = cot_ref[...].astype(jnp.float32) * live
        sum_ref[11:12, :] += columns_total(grad_out * hat_two)
        sum_ref[9:10, :] += columns_total(grad_out)
        second = normalize_back(grad_out * vec_ref[11:12, :], hat_two, inverse_two)
        down_low = second.astype(jnp.bfloat16)
        down_ref[here, :] = down_low
        sum_ref[7:8, :] += columns_total(down_low.astype(jnp.float32))
        grad_hidden = second
        for tile in range(4):
            pulled = dot_back(down_low, w_buf[5 + tile])
            up_low = (pulled * slope_ref[tile].astype(jnp.float32)).astype(jnp.bfloat16)
            up_ref[tile, here, :] = up_low
            sum_ref[3 + tile : 4 + tile, :] += columns_total(up_low.astype(jnp.float32))
            grad_hidden = grad_hidden + dot_back(up_low, w_buf[1 + tile])
        sum_ref[10:11, :] += columns_total(grad_hidden * hat)
        sum_ref[8:9, :] += columns_total(grad_hidden)
        grad_first = normalize_back(grad_hidden * vec_ref[10:11, :], hat, inverse_ref[...])
        first_ref[...] = grad_first
        branch_low = grad_first.astype(jnp.bfloat16)
        branch_ref[...] = branch_low
        sum_ref[2:3, :] += columns_total(branch_low.astype(jnp.float32))
        context_ref[...] = dot_back(branch_low, w_buf[0]).astype(jnp.bfloat16)

    @pl.when(step >= blocks)
    def _():
        tile = step - blocks
        up_grad_ref[0] = outer(hidden_ref[...], up_ref[tile]).astype(jnp.bfloat16)
        down_grad_ref[0] = outer(active_ref[tile], down_ref[...]).astype(jnp.bfloat16)


def fed_forward_both(counts, lengths, hat, inverse, cotangent, weights, vectors):
    tokens, width = hat.shape
    blocks = tokens // ROWS
    low = jnp.bfloat16
    smem = pl.BlockSpec(memory_space=pltpu.SMEM)
    shaped = jax.ShapeDtypeStruct

    def block_of(step):
        return jnp.minimum(step, blocks - 1)

    def tile_of(step):
        return jnp.maximum(step - blocks, 0)

    rows = pl.BlockSpec((ROWS, width), lambda i: (block_of(i), 0))
    tile = pl.BlockSpec((1, width, width), lambda i: (tile_of(i), 0, 0))
    return pl.pallas_call(
        feed_forward_both,
        grid=(blocks + 4,),
        out_shape=(
            shaped((tokens, width), low),
            shaped((tokens, width), jnp.float32),
            shaped((tokens, width), low),
            shaped((tokens, width), low),
            shaped((4, width, width), low),
            shaped((4, width, width), low),
            shaped((16, width), jnp.float32),
        ),
        in_specs=[
            smem,
            smem,
            rows,
            pl.BlockSpec((ROWS, 1), lambda i: (block_of(i), 0)),
            rows,
            pl.BlockSpec(memory_space=pl.ANY),
            pl.BlockSpec((VROWS, width), lambda i: (0, 0)),
        ],
        out_specs=(
            rows,
            rows,
            rows,
            rows,
            tile,
            tile,
            pl.BlockSpec((16, width), lambda i: (0, 0)),
        ),
        scratch_shapes=[
            pltpu.VMEM((9, width, width), low),
            pltpu.VMEM((4, tokens, width), low),
            pltpu.VMEM((4, tokens, width), low),
            pltpu.VMEM((tokens, width), low),
            pltpu.VMEM((tokens, width), low),
            pltpu.VMEM((4, ROWS, width), low),
            pltpu.SemaphoreType.DMA((9,)),
        ],
        compiler_params=pltpu.CompilerParams(vmem_limit_bytes=60 * 2**20),
        name="feed_forward_both",
    )(counts, lengths, hat, inverse, cotangent, weights, vectors)


def attend_backward(
    p_ref,
    q_ref,
    k_ref,
    v_ref,
    x_ref,
    ctx_ref,
    grad_ctx_ref,
    branch_ref,
    first_ref,
    w_ref,
    input_ref,
    grad_ref,
    sum_ref,
    pulled,
):
    step = pl.program_id(0)
    quad, block = step // 2, lax.rem(step, 2)
    here = pl.ds(pl.multiple_of(block * ROWS, ROWS), ROWS)
    cols = pl.ds(pl.multiple_of(quad * 256, 256), 256)

    @pl.when(step == 0)
    def _():
        sum_ref[...] = jnp.zeros_like(sum_ref)
        input_ref[...] = first_ref[...]

    for pair in range(2):
        half = slice(128 * pair, 128 * pair + 128)
        at = pl.ds(pl.multiple_of(quad * 256 + 128 * pair, 128), 128)
        heads = p_ref.at[0, pl.ds(2 * pair, 2)]
        grads = attend_back_pair(
            grad_ctx_ref[here, at], ctx_ref[here, at], heads, q_ref[:, half], k_ref[:, half], v_ref[:, half]
        )
        for number, grad in enumerate(grads):
            pulled[number, here, half] = grad
        sum_ref[0:1, at] += columns_total(grads[0].astype(jnp.float32))
        sum_ref[1:2, at] += columns_total(grads[2].astype(jnp.float32))

    more = input_ref[here, :]
    for at in range(3):
        more = more + dot_back(pulled[at, here, :], w_ref[at, :, cols])
    input_ref[here, :] = more

    @pl.when(block == 1)
    def _():
        for tile in range(3):
            grad_ref[tile, :, cols] = outer(x_ref[...], pulled[tile]).astype(jnp.bfloat16)
        grad_ref[3, :, cols] = outer(ctx_ref[...], branch_ref[:, cols]).astype(jnp.bfloat16)


def attended_back(probs, query, keyed, valued, x, context, grad_context, grad_branch, grad_first, weights):
    tokens, width = x.shape
    low = jnp.bfloat16
    shaped = jax.ShapeDtypeStruct
    once = pl.Buffered(1)
    quad = pl.BlockSpec((ROWS, 256), lambda i: (lax.rem(i, 2), i // 2))
    whole = pl.BlockSpec((tokens, width), lambda i: (0, 0), pipeline_mode=once)
    return pl.pallas_call(
        attend_backward,
        grid=(6,),
        out_shape=(
            shaped((tokens, width), jnp.float32),
            shaped((4, width, width), low),
            shaped((16, width), jnp.float32),
        ),
        in_specs=[
            pl.BlockSpec((1, 4, ROWS, ROWS), lambda i: (lax.rem(i, 2), i // 2, 0, 0)),
            quad,
            quad,
            quad,
            whole,
            whole,
            whole,
            whole,
            whole,
            pl.BlockSpec((3, width, width), lambda i: (0, 0, 0), pipeline_mode=once),
        ],
        out_specs=(
            whole,
            pl.BlockSpec((4, width, width), lambda i: (0, 0, 0), pipeline_mode=once),
            pl.BlockSpec((16, width), lambda i: (0, 0)),
        ),
        scratch_shapes=[pltpu.VMEM((3, tokens, 256), low)],
        compiler_params=pltpu.CompilerParams(vmem_limit_bytes=56 * 2**20),
        name="attend_backward",
    )(probs, query, keyed, valued, x, context, grad_context, grad_branch, grad_first, weights)


def moved(param, grad, first, second, average, rate):
    param_new, first_new, second_new = adam_update(param, grad, first, second, rate)
    return param_new, first_new, second_new, average_rate * average + (1.0 - average_rate) * param_new


def update_kernel(
    gain_scale,
    grad_ref,
    master_ref,
    first_ref,
    second_ref,
    ema_ref,
    vec_grad_ref,
    bias_ref,
    gain_ref,
    vec_first_ref,
    vec_second_ref,
    vec_ema_ref,
    mixed_in,
    input_in,
    master_out,
    first_out,
    second_out,
    ema_out,
    copy_out,
    vec_out,
    vec_first_out,
    vec_second_out,
    vec_ema_out,
    mixed_out,
    input_out,
    vec_ref,
):
    mixed_out[...] = mixed_in[...]
    input_out[...] = input_in[...]

    @pl.when((pl.program_id(0) == 0) & (pl.program_id(1) == 0))
    def _():
        vec_ref[0:10, :] = bias_ref[...]
        vec_ref[10:12, :] = gain_ref[...]
        vec_grad = vec_grad_ref[0:VROWS, :] * gain_scale
        vec_out[...], vec_first_out[...], vec_second_out[...], vec_ema_out[...] = moved(
            vec_ref[...], vec_grad, vec_first_ref[...], vec_second_ref[...], vec_ema_ref[...], vector_rate
        )

    grad = grad_ref[...].astype(jnp.float32) * gain_scale
    result = moved(master_ref[0], grad, first_ref[0], second_ref[0], ema_ref[0], tile_rate)
    master_out[0], first_out[0], second_out[0], ema_out[0] = result
    copy_out[0] = result[0].astype(jnp.bfloat16)


def updated(
    gain_scale,
    slot_grads,
    master,
    first,
    second,
    ema,
    vec_grad,
    bias,
    gain,
    vec_first,
    vec_second,
    vec_ema,
    mixed,
    input_grad,
):
    width = master.shape[-1]
    chunk = 192
    tile = pl.BlockSpec((1, 1, chunk, width), lambda s, r: (0, s, r, 0))
    steps = width // chunk
    rows = pl.BlockSpec((mixed.shape[0] // (SLOTS * steps), width), lambda s, r: (s * steps + r, 0))

    def whole(value):
        return pl.BlockSpec(value.shape, lambda s, r: (0, 0))

    shaped = jax.ShapeDtypeStruct
    tile_shape = shaped(master.shape, jnp.float32)
    vec_shape = shaped((VROWS, width), jnp.float32)
    results = pl.pallas_call(
        functools.partial(update_kernel, gain_scale),
        grid=(SLOTS, steps),
        out_shape=(tile_shape,) * 4
        + (shaped(master.shape, jnp.bfloat16),)
        + (vec_shape,) * 4
        + (shaped(mixed.shape, mixed.dtype), shaped(input_grad.shape, input_grad.dtype)),
        in_specs=[pl.BlockSpec((1, chunk, width), lambda s, r: (s, r, 0))]
        + [tile] * 4
        + [whole(value) for value in (vec_grad, bias, gain, vec_first, vec_second, vec_ema)]
        + [rows] * 2,
        out_specs=(tile,) * 5 + (whole(vec_first),) * 4 + (rows,) * 2,
        scratch_shapes=[pltpu.VMEM((VROWS, width), jnp.float32)],
        compiler_params=pltpu.CompilerParams(vmem_limit_bytes=62 * 2**20),
        name="update",
    )(
        slot_grads,
        master,
        first,
        second,
        ema,
        vec_grad,
        bias,
        gain,
        vec_first,
        vec_second,
        vec_ema,
        mixed,
        input_grad,
    )
    return results[-2:] + results[:-2]


MESH = pl.DeviceIdType.MESH
GROUP = 32
PAIRS = TILES // 2
PLANE = 8
PIECE = 96
PAIR_TILES = ((0, 1), (2, 3), (4, 8), (5, 9), (6, 10), (7, 11))


def remote(src, dst, send, recv, device):
    return pltpu.make_async_remote_copy(
        src_ref=src, dst_ref=dst, send_sem=send, recv_sem=recv, device_id=(device,), device_id_type=MESH
    )


def place(device):
    core = lax.rem(device, 2)
    x = lax.rem(device // 2, 2)
    y = lax.rem(device // 4, 2)
    z = device // 8
    return z, y, x, core


def start(copies):
    for copy in copies:
        copy.start()


def arrive(copies):
    for copy in copies:
        copy.wait_recv()


def greet(z, in_plane):
    barrier = pltpu.get_barrier_semaphore()
    for hop in range(1, PLANE):
        other = z * PLANE + lax.rem(in_plane + hop, PLANE)
        pl.semaphore_signal(barrier, inc=1, device_id=(other,), device_id_type=MESH)
    for hop in range(1, 4):
        other = lax.rem(z + hop, 4) * PLANE + in_plane
        pl.semaphore_signal(barrier, inc=1, device_id=(other,), device_id_type=MESH)
    pl.semaphore_wait(barrier, PLANE + 2)


def along_z(z, in_plane):
    inner = (1 + z // 2) * PLANE + in_plane
    other_middle = (3 - z) * PLANE + in_plane
    outer_end = lax.rem(lax.rem(z + 3, 4) * 3, 4) * PLANE + in_plane
    return inner, other_middle, outer_end


def third(part):
    return pl.ds(256 * part, 256)


UNITS = [(0, 4, pl.ds(256 * part, 256)) for part in range(3)]
UNITS += [(2 * pair, 2, pl.ds(0, 768)) for pair in range(2, PAIRS)]
Z_PARTS = (pl.ds(0, 512), pl.ds(512, 256))


POSITIONS = [tile for pair in PAIR_TILES for tile in pair]


def slot_number(owners, tile):
    number = jnp.int32(0)
    for earlier in range(tile):
        number = number + jnp.where(owners[earlier] == owners[tile], 1, 0)
    return number

FRONT_PLAN = (
    (
        ("open",),
        ("swap", 0),
        ("sent", 0),
        ("swap", 1),
        ("choose", 0),
        ("end", 0),
        ("sent", 1),
        ("swap", 2),
        ("middle", 0),
        ("choose", 1),
        ("end", 1),
        ("caps",),
        ("middle", 1),
        ("total", 0),
        ("end", 3, 0),
        ("choose", 2),
        ("end", 3, 1),
        ("end", 2),
        ("end", 4, 0),
        ("mid", 0),
        ("far", 0),
        ("end", 5, 0),
        ("middle", 3, 0),
        ("total", 1),
        ("near", 0),
        ("end", 4, 1),
        ("middle", 3, 1),
        ("total", 3, 0),
        ("mid", 1),
        ("total", 3, 1),
        ("middle", 2),
        ("end", 5, 1),
        ("mid", 3),
        ("finish", 0),
        ("end", 6, 0),
        ("far", 1),
    ),
    (
        ("middle", 4, 0),
        ("total", 2),
        ("far", 3),
        ("near", 1),
        ("middle", 4, 1),
        ("mid", 2),
        ("middle", 5, 0),
        ("total", 4, 0),
    ),
    (
        ("middle", 5, 1),
        ("total", 4, 1),
        ("end", 6, 1),
        ("mid", 4),
        ("finish", 1),
    ),
    (
        ("middle", 6, 0),
        ("total", 5, 1),
        ("far", 2),
        ("total", 5, 0),
        ("near", 3),
    ),
    (
        ("middle", 6, 1),
        ("far", 4),
        ("total", 6, 0),
        ("total", 6, 1),
        ("near", 2),
        ("mid", 5),
        ("finish", 3),
        ("keep", 2),
        ("finish", 2),
        ("keep", 0),
        ("keep", 1),
        ("mid", 6),
    ),
    (
        ("far", 5),
    ),
    (
        ("far", 6),
        ("near", 4),
    ),
    (
        ("finish", 4),
        ("keep", 3),
        ("near", 5),
    ),
    (
        ("near", 6),
        ("finish", 5),
        ("keep", 4),
    ),
    (
        ("finish", 6),
        ("keep", 5),
    ),
)


def gather_and_forward(
    counts,
    lengths,
    owners,
    bias_ref,
    gain_ref,
    x_hbm,
    cot_hbm,
    master_hbm,
    q_ref,
    k_ref,
    v_ref,
    p_ref,
    ctx_hbm,
    x_turned_hbm,
    ctx_turned_hbm,
    hidden_hbm,
    active_hbm,
    slope_hbm,
    down_hbm,
    mixed_hbm,
    second_hbm,
    hat_hbm,
    w_out,
    inverse_ref,
    sum_ref,
    vec_ref,
    cap_ref,
    wide,
    low,
    stage_a,
    stage_b,
    stage_c,
    chosen,
    from_end,
    from_middle,
    w_buf,
    x_then_hidden,
    x_turned,
    ctx_turned,
    hidden_turned,
    ctx_ref,
    cot_then_down,
    mixed_ref,
    hat_ref,
    slope_buf,
    active_buf,
    load_sem,
    store_sem,
    tile_sem,
    out_sem,
    swap_send,
    swap_recv,
    z_send,
    z_recv,
    mid_send,
    mid_recv,
    far_send,
    far_recv,
    near_send,
    near_recv,
):
    step = pl.program_id(0)
    width = 8 * PIECE
    me = lax.axis_index("dp")
    z, y, x, core = place(me)
    in_plane = lax.rem(me, PLANE)
    sibling = me + 1 - 2 * core
    x_peer = me + 2 - 4 * x
    y_peer = me + 4 - 8 * y
    z_targets = along_z(z, in_plane)
    stages = (stage_a, stage_b, stage_c)
    is_end = (z == 0) | (z == 3)
    is_middle = (z == 1) | (z == 2)

    def piece_rows(cell_core, cell_x, cell_y):
        return pl.ds(pl.multiple_of(((cell_core * 2 + cell_x) * 2 + cell_y) * PIECE, 16), PIECE)

    def swap(part):
        def send(hop, carry):
            target = lax.rem(in_plane + hop, PLANE)
            _, ty, tx, tc = place(target)
            remote(
                low.at[:, piece_rows(tc, tx, ty), third(part)],
                stages[part].at[pl.ds(2 * in_plane, 2)],
                swap_send.at[part],
                swap_recv.at[part],
                z * PLANE + target,
            ).start()
            return carry

        lax.fori_loop(1, PLANE, send, 0)

    def swap_wait(part, sem):
        most = stages[part].at[pl.ds(0, 2 * PLANE - 2)]
        pltpu.make_async_copy(most, most, sem.at[part]).wait()

    def z_copy(unit, part, level):
        first, count, cols = UNITS[unit]
        tiles = pl.ds(first, count)
        cols = cols if count == 4 else Z_PARTS[part]
        src = w_buf.at[tiles, core, x, y, :, cols] if level == 2 else chosen.at[tiles, :, cols]
        dst = (from_end.at[tiles, :, cols], from_middle.at[tiles, :, cols], src)[level]
        at = level, unit, part
        return remote(src, dst, z_send.at[at], z_recv.at[at], z_targets[level])

    def z_parts(unit):
        return range(1 if UNITS[unit][1] == 4 else 2)

    def z_end(unit, part=0):
        @pl.when(is_end)
        def _():
            z_copy(unit, part, 0).start()

    def z_rows(unit, part):
        first, count, cols = UNITS[unit]
        return pl.ds(first, count), cols if count == 4 else Z_PARTS[part]

    def z_middle(unit, part=0):
        @pl.when(is_middle)
        def _():
            z_copy(unit, part, 0).wait_recv()
            tiles, cols = z_rows(unit, part)
            chosen[tiles, :, cols] = chosen[tiles, :, cols] + from_end[tiles, :, cols]
            z_copy(unit, part, 1).start()

    def z_total(unit, part=0):
        @pl.when(is_middle)
        def _():
            z_copy(unit, part, 1).wait_recv()
            tiles, cols = z_rows(unit, part)
            w_buf[tiles, core, x, y, :, cols] = chosen[tiles, :, cols] + from_middle[tiles, :, cols]
            z_copy(unit, part, 2).start()

    def mid_copies(unit):
        first, count, cols = UNITS[unit]
        copies = []
        for n, peer in enumerate((y_peer, x_peer)):
            spot = w_buf.at[pl.ds(first + n * count // 2, count // 2), core, x, y, :, cols]
            copies.append(remote(spot, spot, mid_send.at[unit, n], mid_recv.at[unit, n], peer))
        return copies

    def far_copies(unit):
        first, count, cols = UNITS[unit]
        half = count // 2
        by_row = w_buf.at[pl.ds(first, half), core, x, :, :, cols]
        by_column = w_buf.at[pl.ds(first + half, half), core, :, y, :, cols]
        return [
            remote(spot, spot, far_send.at[unit, n], far_recv.at[unit, n], peer)
            for n, (spot, peer) in enumerate(((by_row, x_peer), (by_column, y_peer)))
        ]

    def near_copy(unit):
        first, count, cols = UNITS[unit]
        spot = w_buf.at[pl.ds(first, count), core, :, :, :, cols]
        return remote(spot, spot, near_send.at[unit], near_recv.at[unit], sibling)

    def give_mid(unit):
        @pl.when(is_end)
        def _():
            arrive([z_copy(unit, part, 2) for part in z_parts(unit)])

        start(mid_copies(unit))

    def give_far(unit):
        arrive(mid_copies(unit))
        start(far_copies(unit))

    def give_near(unit):
        arrive(far_copies(unit))
        near_copy(unit).start()

    def finish(unit):
        near_copy(unit).wait_recv()

    def choose(part):
        swap_wait(part, swap_recv)
        for pair in range(PAIRS):
            for n, tile in enumerate(PAIR_TILES[pair]):
                owner = owners[tile]
                value = stages[part][SLOTS * lax.rem(owner, PLANE) + slot_number(owners, tile)]
                chosen[2 * pair + n, :, third(part)] = jnp.where(
                    owner // PLANE == z, value, jnp.zeros_like(value)
                )

    def load(at):
        src = (x_hbm, cot_hbm, master_hbm)[at]
        dst = (x_then_hidden, cot_then_down, wide)[at]
        return pltpu.make_async_copy(src, dst, load_sem.at[at])

    def store(at):
        src, dst = (
            (hidden_turned, hidden_hbm),
            (ctx_ref, ctx_hbm),
            (hat_ref, hat_hbm),
            (cot_then_down, down_hbm),
            (mixed_ref, mixed_hbm),
            (wide, second_hbm),
            (x_turned, x_turned_hbm),
            (ctx_turned, ctx_turned_hbm),
        )[at]
        src = src.at[pl.ds(0, 2 * ROWS)] if src is wide else src
        return pltpu.make_async_copy(src, dst, store_sem.at[at])

    def w_store(pair):
        two = pl.ds(2 * pair, 2)
        return pltpu.make_async_copy(w_buf.at[two], w_out.at[two], out_sem.at[pair])

    def weight(at, cols=slice(None)):
        value = w_buf[at, :, :, :, :, cols]
        return value.reshape(width, value.shape[-1])

    def open_all():
        for at in range(3):
            load(at).start()
        sum_ref[...] = jnp.zeros_like(sum_ref)
        vec_ref[0:10, :] = bias_ref[...]
        vec_ref[10:12, :] = gain_ref[...]
        greet(z, in_plane)
        load(2).wait()
        for slot in range(SLOTS):
            low[slot] = wide[width * slot : width * (slot + 1), :].astype(jnp.bfloat16)
        for part in range(3):
            stages[part][pl.ds(2 * in_plane, 2)] = low[:, piece_rows(core, x, y), third(part)]

    def make_caps():
        for block in range(2):
            cap_ref[block] = attention_caps(counts, lengths, block)
        load(0).wait()
        x_turned[...] = x_then_hidden[...].T
        store(6).start()
        load(1).wait()

    actions = {
        "open": open_all,
        "caps": make_caps,
        "swap": swap,
        "sent": lambda part: swap_wait(part, swap_send),
        "choose": choose,
        "end": z_end,
        "middle": z_middle,
        "total": z_total,
        "mid": give_mid,
        "far": give_far,
        "near": give_near,
        "finish": finish,
        "keep": lambda pair: w_store(pair).start(),
    }

    for at, work in enumerate(FRONT_PLAN):

        @pl.when(step == at)
        def _():
            for name, *rest in work:
                actions[name](*rest)

    quad, block = step // 2, lax.rem(step, 2)
    here = pl.ds(pl.multiple_of(block * ROWS, ROWS), ROWS)

    @pl.when(step < 6)
    def _():
        attend_quad(
            quad,
            weight,
            x_then_hidden.at[here],
            vec_ref,
            cap_ref.at[block],
            q_ref,
            k_ref,
            v_ref,
            p_ref,
            ctx_ref.at[here],
        )

    @pl.when((step >= 4) & (step < 6))
    def _():
        branch = dot(ctx_ref[here, :], weight(3)) + vec_ref[2:3, :]
        hat, inverse = normalize(x_then_hidden[here, :].astype(jnp.float32) + branch)
        hat_ref[here, :] = hat.astype(jnp.bfloat16)
        inverse_ref[here, :] = inverse
        hidden = hat * vec_ref[10:11, :] + vec_ref[8:9, :]
        hidden_low = hidden.astype(jnp.bfloat16)
        x_then_hidden[here, :] = hidden_low
        hidden_turned[:, here] = hidden_low.T
        ctx_turned[:, here] = ctx_ref[here, :].T
        wide[here, :] = hidden + vec_ref[7:8, :]

    @pl.when(step == 5)
    def _():
        start([store(0), store(1), store(2), store(7)])

    turn = step - 6
    slot = lax.rem(turn, 2)

    def tile_stores(source_slot, tile):
        return [
            pltpu.make_async_copy(src.at[source_slot], dst.at[tile], tile_sem.at[source_slot, at])
            for at, (src, dst) in enumerate(((active_buf, active_hbm), (slope_buf, slope_hbm)))
        ]

    @pl.when(turn >= 2)
    def _():
        for copy in tile_stores(slot, 0):
            copy.wait()

    @pl.when(turn >= 0)
    def _():
        for half in range(2):
            rows = slice(ROWS * half, ROWS * half + ROWS)
            up = dot(x_then_hidden[rows, :], weight(4 + 2 * turn)) + vec_ref[pl.ds(3 + turn, 1), :]
            active, slope = gelu_parts(up)
            slope_buf[slot, rows, :] = slope.astype(jnp.bfloat16)
            active_buf[slot, :, rows] = active.T
            wide[rows, :] = wide[rows, :] + dot(active, weight(5 + 2 * turn))
        start(tile_stores(slot, turn))

    @pl.when(step == 9)
    def _():
        for half in range(2):
            rows = slice(ROWS * half, ROWS * half + ROWS)
            at_row = lax.broadcasted_iota(jnp.int32, (ROWS, 1), 0) + half * ROWS
            live = passage_facts(counts, lengths, at_row)[0].astype(jnp.float32)
            hat, inverse = normalize(wide[rows, :])
            mixed = (hat * vec_ref[11:12, :] + vec_ref[9:10, :]) * live
            mixed_ref[rows, :] = mixed.astype(jnp.bfloat16)
            grad_out = cot_then_down[rows, :].astype(jnp.float32) * live
            sum_ref[11:12, :] += columns_total(grad_out * hat)
            sum_ref[9:10, :] += columns_total(grad_out)
            second = normalize_back(grad_out * vec_ref[11:12, :], hat, inverse)
            wide[rows, :] = second
            down_low = second.astype(jnp.bfloat16)
            cot_then_down[rows, :] = down_low
            sum_ref[7:8, :] += columns_total(down_low.astype(jnp.float32))
        start([store(3), store(4), store(5)])
        for at in range(2):
            for copy in tile_stores(at, 0):
                copy.wait()
        for pair in range(PAIRS):
            w_store(pair).wait()
        swap_wait(2, swap_send)
        for unit in range(len(UNITS)):
            for copy in mid_copies(unit) + far_copies(unit) + [near_copy(unit)]:
                copy.wait_send()

            @pl.when(is_end)
            def _():
                for part in z_parts(unit):
                    z_copy(unit, part, 0).wait_send()

            @pl.when(is_middle)
            def _():
                for part in z_parts(unit):
                    z_copy(unit, part, 1).wait_send()
                    z_copy(unit, part, 2).wait_send()

        for at in range(8):
            store(at).wait()


def gathered_and_forwarded(counts, lengths, owners, bias, gain, x, cotangent, master):
    tokens, width = x.shape
    blocks = tokens // ROWS
    low, high = jnp.bfloat16, jnp.float32
    smem = pl.BlockSpec(memory_space=pltpu.SMEM)
    any_space = pl.BlockSpec(memory_space=pl.ANY)
    dma = pltpu.SemaphoreType.DMA
    shaped = jax.ShapeDtypeStruct

    def at(step):
        step = jnp.minimum(step, 5)
        return lax.rem(step, 2), step // 2

    quad = pl.BlockSpec((ROWS, 256), at)
    rows = shaped((tokens, width), low)
    turned = shaped((width, tokens), low)
    cut = (2, 2, 2, PIECE, width)
    units = len(UNITS)
    return pl.pallas_call(
        gather_and_forward,
        grid=(10,),
        out_shape=(
            rows,
            rows,
            rows,
            shaped((blocks, HEADS, ROWS, ROWS), low),
            rows,
            turned,
            turned,
            turned,
            shaped((4, width, tokens), low),
            shaped((4, tokens, width), low),
            rows,
            rows,
            shaped((tokens, width), high),
            rows,
            shaped((TILES,) + cut, low),
            shaped((tokens, 1), high),
            shaped((16, width), high),
        ),
        in_specs=[smem] * 3
        + [pl.BlockSpec(bias.shape, lambda i: (0, 0)), pl.BlockSpec(gain.shape, lambda i: (0, 0))]
        + [any_space] * 3,
        out_specs=(quad, quad, quad, pl.BlockSpec((1, 4, ROWS, ROWS), lambda i: (*at(i), 0, 0)))
        + (any_space,) * 11
        + (
            pl.BlockSpec((tokens, 1), lambda i: (0, 0), pipeline_mode=pl.Buffered(1)),
            pl.BlockSpec((16, width), lambda i: (0, 0)),
        ),
        scratch_shapes=[
            pltpu.VMEM((VROWS, width), high),
            pltpu.VMEM((2, ROWS, ROWS), high),
            pltpu.VMEM((SLOTS * width, width), high),
            pltpu.VMEM((SLOTS, width, width), low),
            pltpu.VMEM((2 * PLANE, PIECE, 256), low),
            pltpu.VMEM((2 * PLANE, PIECE, 256), low),
            pltpu.VMEM((2 * PLANE, PIECE, 256), low),
            pltpu.VMEM((TILES, PIECE, width), low),
            pltpu.VMEM((TILES, PIECE, width), low),
            pltpu.VMEM((TILES, PIECE, width), low),
            pltpu.VMEM((TILES,) + cut, low),
            pltpu.VMEM((tokens, width), low),
            pltpu.VMEM((width, tokens), low),
            pltpu.VMEM((width, tokens), low),
            pltpu.VMEM((width, tokens), low),
            pltpu.VMEM((tokens, width), low),
            pltpu.VMEM((tokens, width), low),
            pltpu.VMEM((tokens, width), low),
            pltpu.VMEM((tokens, width), low),
            pltpu.VMEM((2, tokens, width), low),
            pltpu.VMEM((2, width, tokens), low),
            dma((3,)),
            dma((8,)),
            dma((2, 2)),
            dma((PAIRS,)),
            dma((3,)),
            dma((3,)),
            dma((3, units, 2)),
            dma((3, units, 2)),
            dma((units, 2)),
            dma((units, 2)),
            dma((units, 2)),
            dma((units, 2)),
            dma((units,)),
            dma((units,)),
        ],
        compiler_params=pltpu.CompilerParams(
            collective_id=0, has_side_effects=True, vmem_limit_bytes=63 * 2**20
        ),
        name="gather_and_forward",
    )(counts, lengths, owners, bias, gain, x, cotangent, master.reshape(SLOTS * width, width))


BACK_PLAN = (
    (),
    (),
    (
        ("core", 0),
    ),
    (),
    (
        ("far", 0),
        ("core", 1),
    ),
    (),
    (
        ("far", 1),
        ("core", 2),
        ("mid", 0),
    ),
    (
        ("far", 2),
    ),
    (
        ("end", 0),
    ),
    (
        ("mid", 1),
        ("core", 3),
    ),
    (),
    (
        ("mid", 2),
        ("far", 3),
        ("end", 1),
        ("middle", 0),
    ),
    (),
    (),
    (
        ("middle", 1),
        ("core", 4),
        ("end", 2),
        ("total", 0),
        ("mid", 3),
    ),
    (
        ("far", 4),
    ),
    (
        ("middle", 2),
        ("end", 3),
        ("core", 5),
        ("total", 1),
    ),
    (
        ("mid", 4),
    ),
    (
        ("far", 5),
        ("end", 4),
        ("middle", 3),
        ("total", 2),
    ),
    (),
    (
        ("core", 6),
        ("total", 3),
        ("middle", 4),
        ("take", 0),
        ("mid", 5),
        ("take", 1),
        ("sum", 0),
        ("take", 2),
        ("far", 6),
        ("total", 4),
        ("end", 5),
        ("middle", 5),
        ("mid", 6),
        ("sum", 1),
        ("end", 6),
        ("take", 3),
        ("take", 4),
        ("deliver", 0),
        ("total", 5),
        ("middle", 6),
        ("sum", 2),
        ("take", 5),
        ("deliver", 1),
        ("total", 6),
        ("take", 6),
        ("deliver", 2),
        ("input", 0),
        ("input", 1),
    ),
)


def backward_and_reduce(
    owners,
    p_ref,
    q_ref,
    k_ref,
    v_ref,
    ctx_ref,
    inverse_ref,
    gain_ref,
    late_ref,
    x_turned_hbm,
    ctx_turned_hbm,
    hidden_hbm,
    active_hbm,
    slope_hbm,
    down_hbm,
    second_hbm,
    hat_hbm,
    w_hbm,
    input_hbm,
    slot_grad,
    vec_out,
    w_part,
    acc,
    hidden_then_x,
    active_then_ctx,
    down_then_branch,
    grad_ctx_ref,
    hat_ref,
    slope_then_query,
    up_then_key,
    value_buf,
    part,
    from_core,
    from_far,
    from_mid,
    from_end,
    from_middle,
    total,
    snap,
    outbox,
    vec_now,
    vec_in,
    holds,
    keeps,
    load_sem,
    w_sem,
    core_send,
    core_recv,
    far_send,
    far_recv,
    mid_send,
    mid_recv,
    z_send,
    z_recv,
    vec_send,
    vec_recv,
    out_send,
    out_recv,
):
    step = pl.program_id(0)
    inner = jnp.maximum(step - 4, 0)
    quad, block, pair = inner // 4, lax.rem(inner, 4) // 2, lax.rem(inner, 2)
    me = lax.axis_index("dp")
    z, y, x, core = place(me)
    in_plane = lax.rem(me, PLANE)
    sibling = me + 1 - 2 * core
    x_peer = me + 2 - 4 * x
    y_peer = me + 4 - 8 * y
    z_targets = along_z(z, in_plane)
    is_end = (z == 0) | (z == 3)
    is_middle = (z == 1) | (z == 2)

    def tiles_of(batch):
        if batch < 4:
            return w_part, 4 + 2 * batch, 2, slice(None)
        return part, 0, 4, pl.ds(256 * (batch - 4), 256)

    def halves(batch, turned):
        ref, first, count, cols = tiles_of(batch)
        return ref, pl.ds(first + turned * count // 2, count // 2), cols

    def core_copy(batch):
        ref, first, count, cols = tiles_of(batch)
        tiles = pl.ds(first, count)
        return remote(
            ref.at[tiles, 1 - core, :, :, :, cols],
            from_core.at[tiles, :, :, :, cols],
            core_send.at[batch],
            core_recv.at[batch],
            sibling,
        )

    def far_copies(batch):
        copies = []
        for turned in range(2):
            ref, tiles, cols = halves(batch, turned)
            src = ref.at[tiles, core, :, 1 - y, :, cols] if turned else ref.at[tiles, core, 1 - x, :, :, cols]
            copies.append(
                remote(
                    src,
                    from_far.at[tiles, :, :, cols],
                    far_send.at[batch, turned],
                    far_recv.at[batch, turned],
                    y_peer if turned else x_peer,
                )
            )
        return copies

    def mid_copies(batch):
        copies = []
        for turned in range(2):
            ref, tiles, cols = halves(batch, turned)
            src = ref.at[tiles, core, 1 - x, y, :, cols] if turned else ref.at[tiles, core, x, 1 - y, :, cols]
            copies.append(
                remote(
                    src,
                    from_mid.at[tiles, :, cols],
                    mid_send.at[batch, turned],
                    mid_recv.at[batch, turned],
                    x_peer if turned else y_peer,
                )
            )
        return copies

    def z_copy(batch, stage):
        ref, first, count, cols = tiles_of(batch)
        tiles = pl.ds(first, count)
        if stage == 2:
            src, dst = total.at[tiles, :, cols], total.at[tiles, :, cols]
        else:
            src = ref.at[tiles, core, x, y, :, cols]
            dst = (from_middle if stage else from_end).at[tiles, :, cols]
        return remote(src, dst, z_send.at[stage, batch], z_recv.at[stage, batch], z_targets[stage])

    def give_core(batch):
        core_copy(batch).start()

    def give_far(batch):
        core_copy(batch).wait_recv()
        ref, first, count, cols = tiles_of(batch)
        for tile in range(first, first + count):
            ref[tile, core, :, :, :, cols] = ref[tile, core, :, :, :, cols] + from_core[tile, :, :, :, cols]
        start(far_copies(batch))

    def give_mid(batch):
        arrive(far_copies(batch))
        for turned in range(2):
            ref, tiles, cols = halves(batch, turned)
            if turned:
                ref[tiles, core, :, y, :, cols] = ref[tiles, core, :, y, :, cols] + from_far[tiles, :, :, cols]
            else:
                ref[tiles, core, x, :, :, cols] = ref[tiles, core, x, :, :, cols] + from_far[tiles, :, :, cols]
        start(mid_copies(batch))

    def add_piece(batch, other):
        ref, first, count, cols = tiles_of(batch)
        tiles = pl.ds(first, count)
        return ref[tiles, core, x, y, :, cols] + other[tiles, :, cols]

    def give_end(batch):
        arrive(mid_copies(batch))
        ref, first, count, cols = tiles_of(batch)
        ref[pl.ds(first, count), core, x, y, :, cols] = add_piece(batch, from_mid)

        @pl.when(is_end)
        def _():
            z_copy(batch, 0).start()

    def give_middle(batch):
        @pl.when(is_middle)
        def _():
            z_copy(batch, 0).wait_recv()
            ref, first, count, cols = tiles_of(batch)
            ref[pl.ds(first, count), core, x, y, :, cols] = add_piece(batch, from_end)
            z_copy(batch, 1).start()

    def give_total(batch):
        @pl.when(is_middle)
        def _():
            z_copy(batch, 1).wait_recv()
            _, first, count, cols = tiles_of(batch)
            total[pl.ds(first, count), :, cols] = add_piece(batch, from_middle)
            z_copy(batch, 2).start()

    def take_total(batch):
        @pl.when(is_end)
        def _():
            z_copy(batch, 2).wait_recv()

    def deliver(third):
        cols = pl.ds(256 * third, 256)
        snap[...] = total[:, :, cols]

        def fill(at, carry):
            value = snap[holds[at]]
            outbox[third, at] = jnp.where(keeps[at] > 0, value, jnp.zeros_like(value))
            return carry

        lax.fori_loop(0, 2 * PLANE, fill, 0)

        def send(hop, carry):
            target = lax.rem(in_plane + hop, PLANE)
            remote(
                outbox.at[third, pl.ds(2 * target, 2)],
                slot_grad.at[:, core, x, y, :, cols],
                out_send.at[third],
                out_recv.at[third],
                z * PLANE + target,
            ).start()
            return carry

        lax.fori_loop(1, PLANE, send, 0)
        keep_copy(third).start()

    def keep_copy(third):
        return pltpu.make_async_copy(
            outbox.at[third, pl.ds(2 * in_plane, 2)],
            slot_grad.at[:, core, x, y, :, pl.ds(256 * third, 256)],
            load_sem.at[5 + third],
        )

    def vec_copies(stage):
        if stage < 3:
            hops = [(stage, (sibling, x_peer, y_peer)[stage])]
        else:
            hops = [
                (2 + hop, lax.rem(z + hop, 4) * PLANE + in_plane) for hop in range(1, 4)
            ]
        return [
            remote(vec_now.at[stage], vec_in.at[at], vec_send.at[at], vec_recv.at[at], device)
            for at, device in hops
        ]

    def vec_next(stage):
        arrive(vec_copies(stage))
        vec_now[stage + 1] = vec_now[stage] + vec_in[stage]
        start(vec_copies(stage + 1))

    def input_store():
        return pltpu.make_async_copy(acc, input_hbm, load_sem.at[4])

    def load(at):
        src, dst = (
            (hidden_hbm, hidden_then_x),
            (down_hbm, down_then_branch),
            (second_hbm, acc),
            (hat_hbm, hat_ref),
            None,
            None,
            None,
            None,
            (x_turned_hbm, hidden_then_x),
            (ctx_turned_hbm, active_then_ctx),
        )[at]
        return pltpu.make_async_copy(src, dst, load_sem.at[at])

    def tile_load(tile, side):
        src, dst = ((slope_hbm, slope_then_query), (active_hbm, active_then_ctx))[side]
        return pltpu.make_async_copy(src.at[tile], dst, load_sem.at[10 + side])

    def w_load(at):
        return pltpu.make_async_copy(w_hbm.at[at], w_part.at[at], w_sem.at[at])

    def weight(at, cols=slice(None)):
        value = w_part[at, :, :, :, :, cols]
        return value.reshape(8 * PIECE, value.shape[-1])

    def input_rows(half):
        rows = slice(ROWS * half, ROWS * half + ROWS)
        more = acc[rows, :]
        for at, buf in enumerate((slope_then_query, up_then_key, value_buf)):
            more = more + dot_back(buf[rows, :], weight(at))
        acc[rows, :] = more
        if half == 1:
            input_store().start()

    actions = {
        "core": give_core,
        "far": give_far,
        "mid": give_mid,
        "end": give_end,
        "middle": give_middle,
        "total": give_total,
        "take": take_total,
        "deliver": deliver,
        "sum": vec_next,
        "input": input_rows,
    }

    @pl.when(step == 0)
    def _():
        start([load(1), tile_load(0, 0), w_load(5), w_load(4), load(2), tile_load(0, 1), load(0)])
        start([w_load(at) for at in range(6, TILES)] + [load(3)] + [w_load(3 - at) for at in range(4)])
        for at in range(2 * PLANE):
            tile_here, kept = jnp.int32(0), jnp.int32(0)
            for tile in range(TILES):
                place_of = SLOTS * owners[tile] + slot_number(owners, tile)
                match = place_of == z * 2 * PLANE + at
                tile_here = tile_here + jnp.where(match, POSITIONS.index(tile), 0)
                kept = kept + jnp.where(match, 1, 0)
            holds[at] = tile_here
            keeps[at] = kept
        vec_now[0] = late_ref[...]
        greet(z, in_plane)

    def serve(points):
        for at in points:
            if BACK_PLAN[at]:

                @pl.when(step == (at // 2 if at < 8 else at - 4))
                def _():
                    for name, number in BACK_PLAN[at]:
                        actions[name](number)

    serve(range(0, 8, 2))

    @pl.when(step < 4)
    def _():
        tile_load(step, 0).wait()
        w_load(5 + 2 * step).wait()

        @pl.when(step == 0)
        def _():
            load(1).wait()

        for half in range(2):
            rows = slice(ROWS * half, ROWS * half + ROWS)
            back = dot_back(down_then_branch[rows, :], weight(5 + 2 * step))
            up_low = (back * slope_then_query[rows, :].astype(jnp.float32)).astype(jnp.bfloat16)
            up_then_key[rows, :] = up_low
            vec_now[0, pl.ds(3 + step, 1), :] += columns_total(up_low.astype(jnp.float32))

        @pl.when(step < 3)
        def _():
            tile_load(step + 1, 0).start()

        w_load(4 + 2 * step).wait()

        @pl.when(step == 0)
        def _():
            load(2).wait()
            load(0).wait()

        for half in range(2):
            rows = slice(ROWS * half, ROWS * half + ROWS)
            acc[rows, :] = acc[rows, :] + dot_back(up_then_key[rows, :], weight(4 + 2 * step))

    serve(range(1, 8, 2))

    @pl.when(step < 4)
    def _():
        tile_load(step, 1).wait()
        by_down = dot(active_then_ctx[...], down_then_branch[...]).astype(jnp.bfloat16)
        w_part[5 + 2 * step] = by_down.reshape(2, 2, 2, PIECE, 8 * PIECE)

        @pl.when(step < 3)
        def _():
            tile_load(step + 1, 1).start()

        by_up = dot(hidden_then_x[...], up_then_key[...]).astype(jnp.bfloat16)
        w_part[4 + 2 * step] = by_up.reshape(2, 2, 2, PIECE, 8 * PIECE)

    @pl.when(step == 3)
    def _():
        start([load(8), load(9)])
        load(3).wait()
        for at in range(4):
            w_load(at).wait()
        for half in range(2):
            rows = slice(ROWS * half, ROWS * half + ROWS)
            grad_hidden, hat = acc[rows, :], hat_ref[rows, :].astype(jnp.float32)
            vec_now[0, 10:11, :] += columns_total(grad_hidden * hat)
            vec_now[0, 8:9, :] += columns_total(grad_hidden)
            first = normalize_back(grad_hidden * gain_ref[0:1, :], hat, inverse_ref[rows, :])
            acc[rows, :] = first
            branch_low = first.astype(jnp.bfloat16)
            down_then_branch[rows, :] = branch_low
            vec_now[0, 2:3, :] += columns_total(branch_low.astype(jnp.float32))
            grad_ctx_ref[rows, :] = dot_back(branch_low, weight(3)).astype(jnp.bfloat16)

    serve(range(8, 20))

    here = pl.ds(pl.multiple_of(block * ROWS, ROWS), ROWS)
    quad_cols = pl.ds(pl.multiple_of(quad * 256, 256), 256)

    pair_cols = pl.ds(pl.multiple_of(quad * 256 + pair * 128, 128), 128)
    grad_bufs = (slope_then_query, up_then_key, value_buf)

    @pl.when(step >= 4)
    def _():
        grads = attend_back_pair(
            grad_ctx_ref[here, pair_cols],
            ctx_ref[here, pair_cols],
            p_ref.at[0],
            q_ref[...],
            k_ref[...],
            v_ref[...],
        )
        for buf, grad in zip(grad_bufs, grads):
            buf[here, pair_cols] = grad
        vec_now[0, 0:1, pair_cols] += columns_total(grads[0].astype(jnp.float32))
        vec_now[0, 1:2, pair_cols] += columns_total(grads[2].astype(jnp.float32))

    @pl.when(step == 7)
    def _():
        load(8).wait()
        load(9).wait()

    @pl.when((step >= 4) & (block == 1) & (pair == 1))
    def _():
        for tile in range(4):
            if tile < 3:
                value = dot(hidden_then_x[...], grad_bufs[tile][:, quad_cols])
            else:
                value = dot(active_then_ctx[...], down_then_branch[:, quad_cols])
            value = value.astype(jnp.bfloat16).reshape(2, 2, 2, PIECE, 256)
            part[tile, :, :, :, :, quad_cols] = value


    @pl.when(step == 15)
    def _():
        start(vec_copies(0))
        for name, number in BACK_PLAN[-1]:
            actions[name](number)
        arrive(vec_copies(3))
        summed = jnp.zeros(vec_out.shape, jnp.float32)
        for origin in range(4):
            hop = lax.rem(z - origin + 4, 4)
            summed = summed + jnp.where(hop == 0, vec_now[3], vec_in[2 + jnp.maximum(hop, 1)])
        vec_out[...] = summed
        for batch in range(7):
            for copy in [core_copy(batch)] + far_copies(batch) + mid_copies(batch):
                copy.wait_send()

            @pl.when(is_end)
            def _():
                z_copy(batch, 0).wait_send()

            @pl.when(is_middle)
            def _():
                z_copy(batch, 1).wait_send()
                z_copy(batch, 2).wait_send()

        for stage in range(4):
            for copy in vec_copies(stage):
                copy.wait_send()
        input_store().wait()
        for third in range(3):
            keep_copy(third).wait()
            most = outbox.at[third, pl.ds(0, 2 * PLANE - 2)]
            pltpu.make_async_copy(most, most, out_recv.at[third]).wait()
            pltpu.make_async_copy(most, most, out_send.at[third]).wait()


def backward_and_reduced(
    owners,
    probs,
    query,
    keyed,
    valued,
    context,
    inverse,
    gain,
    late_sums,
    x_turned,
    ctx_turned,
    hidden,
    active,
    slope,
    grad_down,
    grad_second,
    hat,
    weights,
):
    tokens, width = grad_down.shape
    low, high = jnp.bfloat16, jnp.float32
    shaped = jax.ShapeDtypeStruct
    smem = pl.BlockSpec(memory_space=pltpu.SMEM)
    any_space = pl.BlockSpec(memory_space=pl.ANY)
    dma = pltpu.SemaphoreType.DMA
    once = pl.Buffered(1)

    def at(step):
        inner = jnp.maximum(step - 4, 0)
        return lax.rem(inner, 4) // 2, inner // 4 * 2 + lax.rem(inner, 2)

    pair = pl.BlockSpec((ROWS, 128), at)
    sums = pl.BlockSpec((16, width), lambda i: (0, 0))
    cut = (2, 2, 2, PIECE, width)
    input_grad, slot_grads, vector_sums = pl.pallas_call(
        backward_and_reduce,
        grid=(16,),
        out_shape=(
            shaped((tokens, width), high),
            shaped((SLOTS,) + cut, low),
            shaped((16, width), high),
        ),
        in_specs=[smem, pl.BlockSpec((1, 2, ROWS, ROWS), lambda i: (*at(i), 0, 0))]
        + [pair] * 3
        + [
            pl.BlockSpec((tokens, width), lambda i: (0, 0), pipeline_mode=once),
            pl.BlockSpec((tokens, 1), lambda i: (0, 0), pipeline_mode=once),
            pl.BlockSpec(gain.shape, lambda i: (0, 0)),
            sums,
        ]
        + [any_space] * 9,
        out_specs=(any_space, any_space, sums),
        scratch_shapes=[
            pltpu.VMEM((TILES,) + cut, low),
            pltpu.VMEM((tokens, width), high),
            pltpu.VMEM((width, tokens), low),
            pltpu.VMEM((width, tokens), low),
            pltpu.VMEM((tokens, width), low),
            pltpu.VMEM((tokens, width), low),
            pltpu.VMEM((tokens, width), low),
            pltpu.VMEM((tokens, width), low),
            pltpu.VMEM((tokens, width), low),
            pltpu.VMEM((tokens, width), low),
            pltpu.VMEM((4,) + cut, low),
            pltpu.VMEM((TILES,) + cut[1:], low),
            pltpu.VMEM((TILES,) + cut[2:], low),
            pltpu.VMEM((TILES,) + cut[3:], low),
            pltpu.VMEM((TILES,) + cut[3:], low),
            pltpu.VMEM((TILES,) + cut[3:], low),
            pltpu.VMEM((TILES,) + cut[3:], low),
            pltpu.VMEM((TILES, PIECE, 256), low),
            pltpu.VMEM((3, 2 * PLANE, PIECE, 256), low),
            pltpu.VMEM((4, 16, width), high),
            pltpu.VMEM((6, 16, width), high),
            pltpu.SMEM((2 * PLANE,), jnp.int32),
            pltpu.SMEM((2 * PLANE,), jnp.int32),
            dma((12,)),
            dma((TILES,)),
            dma((7,)),
            dma((7,)),
            dma((7, 2)),
            dma((7, 2)),
            dma((7, 2)),
            dma((7, 2)),
            dma((3, 7)),
            dma((3, 7)),
            dma((6,)),
            dma((6,)),
            dma((3,)),
            dma((3,)),
        ],
        compiler_params=pltpu.CompilerParams(
            collective_id=1, has_side_effects=True, vmem_limit_bytes=63 * 2**20
        ),
        name="backward_and_reduce",
    )(
        owners,
        probs,
        query,
        keyed,
        valued,
        context,
        inverse,
        gain,
        late_sums,
        x_turned,
        ctx_turned,
        hidden,
        active,
        slope,
        grad_down,
        grad_second,
        hat,
        weights,
    )
    return input_grad, slot_grads.reshape(SLOTS, width, width), vector_sums


def collected_tiles(tile_low, owners, slots):
    mine = owners == lax.axis_index("dp")
    local = jnp.where(mine[:, None, None], tile_low[slots], jnp.zeros((), tile_low.dtype))
    return lax.psum(local, "dp")


def summed_over_slice(parts, vector_terms, owners, slots):
    myself = lax.axis_index("dp")

    def add(held, items):
        part, owner, slot = items
        total = lax.psum(part.astype(jnp.float32), "dp")
        here = (owner == myself) & (slot == jnp.arange(SLOTS, dtype=jnp.int32))
        return held + jnp.where(here[:, None, None], total[None], 0.0), None

    empty = jnp.zeros((SLOTS,) + parts.shape[1:], jnp.float32)
    return lax.scan(add, empty, (parts, owners, slots))[0], lax.psum(vector_terms, "dp")


def body(
    inputs,
    cotangent,
    counts,
    lengths,
    owners,
    tile_master,
    tile_first,
    tile_second,
    tile_ema,
    bias_vals,
    gain_vals,
    vector_first,
    vector_second,
    vector_ema,
):
    tokens = inputs.shape[0]
    small = lax.axis_size("dp") == GROUP
    gain_scale = float(tokens * lax.axis_size("dp")) ** (-0.5)
    if small:
        (
            query,
            keyed,
            valued,
            probs,
            context,
            x_turned,
            ctx_turned,
            hidden,
            active,
            slope,
            grad_down,
            mixed,
            grad_second,
            hat,
            weights,
            inverse,
            late_sums,
        ) = gathered_and_forwarded(
            counts,
            lengths,
            owners,
            bias_vals,
            gain_vals,
            inputs,
            cotangent,
            tile_master,
        )
        input_grad, slot_grads, full_sums = backward_and_reduced(
            owners,
            probs,
            query,
            keyed,
            valued,
            context,
            inverse,
            gain_vals,
            late_sums,
            x_turned,
            ctx_turned,
            hidden,
            active,
            slope,
            grad_down,
            grad_second,
            hat,
            weights,
        )
    else:
        slots = tile_slots(owners)
        vectors = jnp.concatenate([bias_vals, gain_vals], 0)
        weights = collected_tiles(tile_master[0].astype(jnp.bfloat16), owners, slots)
        query, keyed, valued, probs, context, hat, inverse = attended(
            counts, lengths, inputs, weights, vectors
        )
        mixed, grad_first, grad_branch, grad_context, up_grads, down_grads, late_sums = fed_forward_both(
            counts, lengths, hat, inverse, cotangent, weights, vectors
        )
        input_grad, early_grads, early_sums = attended_back(
            probs, query, keyed, valued, inputs, context, grad_context, grad_branch, grad_first, weights
        )
        parts = jnp.concatenate([early_grads, up_grads, down_grads], 0)
        slot_grads, full_sums = summed_over_slice(parts, late_sums + early_sums, owners, slots)
    return updated(
        gain_scale,
        slot_grads,
        tile_master,
        tile_first,
        tile_second,
        tile_ema,
        full_sums,
        bias_vals,
        gain_vals,
        vector_first,
        vector_second,
        vector_ema,
        mixed,
        input_grad,
    )


def solution(mesh):
    placed = (
        P("dp", None),
        P("dp", None),
        P("dp", None),
        P("dp", None),
        P(),
        P("dp", None, None, None),
        P("dp", None, None, None),
        P("dp", None, None, None),
        P("dp", None, None, None),
        P(),
        P(),
        P(),
        P(),
        P(),
    )
    return jax.shard_map(
        body,
        mesh=mesh,
        in_specs=placed,
        out_specs=(
            P("dp", None),
            P("dp", None),
            P("dp", None, None, None),
            P("dp", None, None, None),
            P("dp", None, None, None),
            P("dp", None, None, None),
            P("dp", None, None, None),
            P(),
            P(),
            P(),
            P(),
        ),
        check_vma=False,
    )
```

```python
import functools

import jax
import jax.numpy as jnp
from jax import lax
from jax.experimental import pallas as pl
from jax.experimental.pallas import tpu as pltpu
from jax.sharding import PartitionSpec as P

HEADS = 12
BUCKET = 128
SLOTS = 2
TILES = 12
VROWS = 12
STEP = 5

norm_epsilon = 1e-12
tile_rate = 0.03
vector_rate = 0.2
first_decay = 0.5
second_decay = 0.5
adam_epsilon = 1e-08
weight_decay = 0.01
average_rate = 0.9


def tile_slots(owners):
    order = jnp.arange(owners.shape[0], dtype=jnp.int32)
    same = owners[:, None] == owners[None, :]
    earlier = order[None, :] < order[:, None]
    return jnp.sum((same & earlier).astype(jnp.int32), 1)


def adam_update(param, grad, first, second, rate):
    first_new = first_decay * first + (1.0 - first_decay) * grad
    second_new = second_decay * second + (1.0 - second_decay) * grad * grad
    first_hat = first_new / (1.0 - first_decay**STEP)
    second_hat = second_new / (1.0 - second_decay**STEP)
    param_new = param - rate * (
        first_hat / (jnp.sqrt(second_hat) + adam_epsilon) + weight_decay * param
    )
    return (param_new, first_new, second_new)


ROWS = 4 * BUCKET
TAIL_RATE = 0.28
TAIL_SERIES = (
    0.11615256574707405,
    0.06981038475559553,
    0.2631359597579608,
    -0.22983675561378278,
    0.38546775012288165,
    -0.10472989053809521,
)
INV_SQRT_TAU = 0.3989422804014327
ALLOWED = 3.0e38
BARRED = -1000000000.0


def dot(left, right):
    return jnp.dot(left, right, preferred_element_type=jnp.float32)


def dot_back(left, right):
    return lax.dot_general(
        left, right, (((1,), (1,)), ((), ())), preferred_element_type=jnp.float32
    )


def outer(left, right):
    return lax.dot_general(
        left, right, (((0,), (0,)), ((), ())), preferred_element_type=jnp.float32
    )


def passage_facts(counts, lengths, position):
    places = lengths.shape[1]
    big_end = counts[0, 0]
    mid_end = big_end + counts[0, 1]
    all_end = mid_end + counts[0, 2]
    start = jnp.int32(0)
    member = jnp.zeros(position.shape, jnp.int32)
    usable = jnp.zeros(position.shape, jnp.int32)
    for number in range(places):
        size = jnp.where(
            number < big_end,
            4 * BUCKET,
            jnp.where(number < mid_end, 2 * BUCKET, jnp.where(number < all_end, BUCKET, 0)),
        )
        inside = (position >= start) & (position < start + size)
        live = inside & (position < start + lengths[0, number])
        member = jnp.where(inside, number + 1, member)
        usable = jnp.where(live, 1, usable)
        start = start + size
    passage = jnp.where(member > 0, member - 1, places + position // BUCKET)
    return usable, passage


def normalize(values):
    center = jnp.mean(values, -1, keepdims=True)
    centered = values - center
    spread = jnp.mean(centered * centered, -1, keepdims=True)
    inverse = lax.rsqrt(spread + norm_epsilon)
    return centered * inverse, inverse


def normalize_back(grad, hat, inverse):
    center = jnp.mean(grad, -1, keepdims=True)
    along = jnp.mean(grad * hat, -1, keepdims=True)
    return inverse * (grad - center - hat * along)


def columns_total(values):
    return jnp.sum(values, 0, keepdims=True)


def attention_caps(counts, lengths, block):
    at_row = lax.broadcasted_iota(jnp.int32, (ROWS, 1), 0) + block * ROWS
    at_column = lax.broadcasted_iota(jnp.int32, (1, ROWS), 1) + block * ROWS
    _, passage_row = passage_facts(counts, lengths, at_row)
    usable_column, passage_column = passage_facts(counts, lengths, at_column)
    allowed = (passage_row == passage_column) & ((usable_column == 1) | (at_row == at_column))
    return jnp.where(allowed, ALLOWED, BARRED)


def attend_quad(quad, weight, x_ref, vec_ref, cap_ref, q_ref, k_ref, v_ref, p_ref, ctx_ref):
    cols = pl.ds(pl.multiple_of(quad * 256, 256), 256)
    x = x_ref[...]
    query = (dot(x, weight(0, cols)) + vec_ref[0:1, cols]).astype(jnp.bfloat16)
    query = query * jnp.bfloat16(0.125)
    keyed = dot(x, weight(1, cols)).astype(jnp.bfloat16)
    valued = (dot(x, weight(2, cols)) + vec_ref[1:2, cols]).astype(jnp.bfloat16)
    q_ref[...] = query
    k_ref[...] = keyed
    v_ref[...] = valued
    low_half = lax.broadcasted_iota(jnp.int32, (1, 128), 1) < 64
    for pair in range(2):
        part = slice(128 * pair, 128 * pair + 128)
        contexts = []
        for head in range(2):
            here = low_half if head == 0 else ~low_half
            mine = jnp.where(here, query[:, part], jnp.zeros_like(query[:, part]))
            scores = jnp.minimum(dot_back(mine, keyed[:, part]), cap_ref[...])
            exponent = jnp.exp(scores - jnp.max(scores, -1, keepdims=True))
            inverse = 1.0 / jnp.sum(exponent, -1, keepdims=True)
            probability = (exponent * inverse).astype(jnp.bfloat16)
            p_ref[0, 2 * pair + head] = probability
            contexts.append(dot(probability, valued[:, part]))
        both = jnp.where(low_half, contexts[0], contexts[1]).astype(jnp.bfloat16)
        ctx_ref[:, pl.ds(pl.multiple_of(quad * 256 + 128 * pair, 128), 128)] = both


def close_block(w_out, x_ref, vec_ref, ctx_ref, hat_ref, inverse_ref):
    branch = dot(ctx_ref[...], w_out) + vec_ref[2:3, :]
    hat_ref[...], inverse_ref[...] = normalize(x_ref[...].astype(jnp.float32) + branch)


def attend_back_pair(pull, level_from, p_ref, query, keyed, valued):
    low_half = lax.broadcasted_iota(jnp.int32, (1, 128), 1) < 64
    along = pull.astype(jnp.float32) * level_from.astype(jnp.float32)
    by_query, by_key, by_value = [], [], []
    for head in range(2):
        mask = low_half if head == 0 else ~low_half
        mine = jnp.where(mask, pull, jnp.zeros_like(pull))
        level = jnp.sum(jnp.where(mask, along, 0.0), -1, keepdims=True)
        probability = p_ref[head]
        grad_prob = dot_back(mine, valued)
        grad_scores = (probability.astype(jnp.float32) * (grad_prob - level)).astype(jnp.bfloat16)
        by_query.append(dot(grad_scores, keyed))
        by_key.append(outer(grad_scores, query))
        by_value.append(outer(probability, pull))
    grad_query = jnp.where(low_half, by_query[0], by_query[1]) * 0.125
    grad_key = jnp.where(low_half, by_key[0], by_key[1])
    grad_value = jnp.where(low_half, by_value[0], by_value[1])
    return [value.astype(jnp.bfloat16) for value in (grad_query, grad_key, grad_value)]


def gelu_parts(up):
    near = 1.0 / (1.0 + TAIL_RATE * jnp.abs(up))
    decay = jnp.exp(up * up * -0.5)
    series = jnp.full_like(near, TAIL_SERIES[-1])
    for term in TAIL_SERIES[-2::-1]:
        series = series * near + term
    tail = series * near * decay
    share = jnp.where(up < 0.0, tail, 1.0 - tail)
    slope = share + up * (decay * INV_SQRT_TAU)
    return (up * share).astype(jnp.bfloat16), slope


def attend_forward(
    counts,
    lengths,
    x_ref,
    w_hbm,
    vec_ref,
    q_ref,
    k_ref,
    v_ref,
    p_ref,
    ctx_ref,
    hat_ref,
    inverse_ref,
    w_buf,
    cap_ref,
    w_sem,
):
    block, quad = pl.program_id(0), pl.program_id(1)
    loads = [pltpu.make_async_copy(w_hbm.at[at], w_buf.at[at], w_sem.at[at]) for at in range(4)]

    @pl.when((block == 0) & (quad == 0))
    def _():
        for load in loads:
            load.start()
        for load in loads:
            load.wait()

    @pl.when(quad == 0)
    def _():
        cap_ref[...] = attention_caps(counts, lengths, block)

    def weight(at, cols):
        return w_buf[at, :, cols]

    attend_quad(quad, weight, x_ref, vec_ref, cap_ref, q_ref, k_ref, v_ref, p_ref, ctx_ref)

    @pl.when(quad == 2)
    def _():
        close_block(w_buf[3], x_ref, vec_ref, ctx_ref, hat_ref, inverse_ref)


def attended(counts, lengths, x, weights, vectors):
    tokens, width = x.shape
    blocks = tokens // ROWS
    low = jnp.bfloat16
    smem = pl.BlockSpec(memory_space=pltpu.SMEM)
    quad = pl.BlockSpec((ROWS, 256), lambda b, h: (b, h))
    rows = pl.BlockSpec((ROWS, width), lambda b, h: (b, 0))
    shaped = jax.ShapeDtypeStruct
    return pl.pallas_call(
        attend_forward,
        grid=(blocks, 3),
        out_shape=(
            shaped((tokens, width), low),
            shaped((tokens, width), low),
            shaped((tokens, width), low),
            shaped((blocks, HEADS, ROWS, ROWS), low),
            shaped((tokens, width), low),
            shaped((tokens, width), jnp.float32),
            shaped((tokens, 1), jnp.float32),
        ),
        in_specs=[
            smem,
            smem,
            rows,
            pl.BlockSpec(memory_space=pl.ANY),
            pl.BlockSpec((VROWS, width), lambda b, h: (0, 0)),
        ],
        out_specs=(
            quad,
            quad,
            quad,
            pl.BlockSpec((1, 4, ROWS, ROWS), lambda b, h: (b, h, 0, 0)),
            rows,
            rows,
            pl.BlockSpec((ROWS, 1), lambda b, h: (b, 0)),
        ),
        scratch_shapes=[
            pltpu.VMEM((4, width, width), low),
            pltpu.VMEM((ROWS, ROWS), jnp.float32),
            pltpu.SemaphoreType.DMA((4,)),
        ],
        compiler_params=pltpu.CompilerParams(vmem_limit_bytes=56 * 2**20),
        name="attend_forward",
    )(counts, lengths, x, weights, vectors)


def feed_forward_both(
    counts,
    lengths,
    hat_ref,
    inverse_ref,
    cot_ref,
    w_hbm,
    vec_ref,
    mixed_ref,
    first_ref,
    branch_ref,
    context_ref,
    up_grad_ref,
    down_grad_ref,
    sum_ref,
    w_buf,
    active_ref,
    up_ref,
    hidden_ref,
    down_ref,
    slope_ref,
    w_sem,
):
    step = pl.program_id(0)
    blocks = pl.num_programs(0) - 4
    loads = [
        pltpu.make_async_copy(w_hbm.at[3 + at], w_buf.at[at], w_sem.at[at]) for at in range(9)
    ]

    @pl.when(step == 0)
    def _():
        for load in loads[1:] + loads[:1]:
            load.start()
        sum_ref[...] = jnp.zeros_like(sum_ref)
        for load in loads[1:] + loads[:1]:
            load.wait()

    @pl.when(step < blocks)
    def _():
        here = pl.ds(pl.multiple_of(step * ROWS, ROWS), ROWS)
        at_row = lax.broadcasted_iota(jnp.int32, (ROWS, 1), 0) + step * ROWS
        live = passage_facts(counts, lengths, at_row)[0].astype(jnp.float32)
        hat = hat_ref[...]
        hidden = hat * vec_ref[10:11, :] + vec_ref[8:9, :]
        hidden_low = hidden.astype(jnp.bfloat16)
        hidden_ref[here, :] = hidden_low
        total = hidden + vec_ref[7:8, :]
        for tile in range(4):
            up = dot(hidden_low, w_buf[1 + tile]) + vec_ref[3 + tile : 4 + tile, :]
            active, slope = gelu_parts(up)
            slope_ref[tile] = slope.astype(jnp.bfloat16)
            active_ref[tile, here, :] = active
            total = total + dot(active, w_buf[5 + tile])
        hat_two, inverse_two = normalize(total)
        mixed_ref[...] = ((hat_two * vec_ref[11:12, :] + vec_ref[9:10, :]) * live).astype(jnp.bfloat16)
        grad_out = cot_ref[...].astype(jnp.float32) * live
        sum_ref[11:12, :] += columns_total(grad_out * hat_two)
        sum_ref[9:10, :] += columns_total(grad_out)
        second = normalize_back(grad_out * vec_ref[11:12, :], hat_two, inverse_two)
        down_low = second.astype(jnp.bfloat16)
        down_ref[here, :] = down_low
        sum_ref[7:8, :] += columns_total(down_low.astype(jnp.float32))
        grad_hidden = second
        for tile in range(4):
            pulled = dot_back(down_low, w_buf[5 + tile])
            up_low = (pulled * slope_ref[tile].astype(jnp.float32)).astype(jnp.bfloat16)
            up_ref[tile, here, :] = up_low
            sum_ref[3 + tile : 4 + tile, :] += columns_total(up_low.astype(jnp.float32))
            grad_hidden = grad_hidden + dot_back(up_low, w_buf[1 + tile])
        sum_ref[10:11, :] += columns_total(grad_hidden * hat)
        sum_ref[8:9, :] += columns_total(grad_hidden)
        grad_first = normalize_back(grad_hidden * vec_ref[10:11, :], hat, inverse_ref[...])
        first_ref[...] = grad_first
        branch_low = grad_first.astype(jnp.bfloat16)
        branch_ref[...] = branch_low
        sum_ref[2:3, :] += columns_total(branch_low.astype(jnp.float32))
        context_ref[...] = dot_back(branch_low, w_buf[0]).astype(jnp.bfloat16)

    @pl.when(step >= blocks)
    def _():
        tile = step - blocks
        up_grad_ref[0] = outer(hidden_ref[...], up_ref[tile]).astype(jnp.bfloat16)
        down_grad_ref[0] = outer(active_ref[tile], down_ref[...]).astype(jnp.bfloat16)


def fed_forward_both(counts, lengths, hat, inverse, cotangent, weights, vectors):
    tokens, width = hat.shape
    blocks = tokens // ROWS
    low = jnp.bfloat16
    smem = pl.BlockSpec(memory_space=pltpu.SMEM)
    shaped = jax.ShapeDtypeStruct

    def block_of(step):
        return jnp.minimum(step, blocks - 1)

    def tile_of(step):
        return jnp.maximum(step - blocks, 0)

    rows = pl.BlockSpec((ROWS, width), lambda i: (block_of(i), 0))
    tile = pl.BlockSpec((1, width, width), lambda i: (tile_of(i), 0, 0))
    return pl.pallas_call(
        feed_forward_both,
        grid=(blocks + 4,),
        out_shape=(
            shaped((tokens, width), low),
            shaped((tokens, width), jnp.float32),
            shaped((tokens, width), low),
            shaped((tokens, width), low),
            shaped((4, width, width), low),
            shaped((4, width, width), low),
            shaped((16, width), jnp.float32),
        ),
        in_specs=[
            smem,
            smem,
            rows,
            pl.BlockSpec((ROWS, 1), lambda i: (block_of(i), 0)),
            rows,
            pl.BlockSpec(memory_space=pl.ANY),
            pl.BlockSpec((VROWS, width), lambda i: (0, 0)),
        ],
        out_specs=(
            rows,
            rows,
            rows,
            rows,
            tile,
            tile,
            pl.BlockSpec((16, width), lambda i: (0, 0)),
        ),
        scratch_shapes=[
            pltpu.VMEM((9, width, width), low),
            pltpu.VMEM((4, tokens, width), low),
            pltpu.VMEM((4, tokens, width), low),
            pltpu.VMEM((tokens, width), low),
            pltpu.VMEM((tokens, width), low),
            pltpu.VMEM((4, ROWS, width), low),
            pltpu.SemaphoreType.DMA((9,)),
        ],
        compiler_params=pltpu.CompilerParams(vmem_limit_bytes=60 * 2**20),
        name="feed_forward_both",
    )(counts, lengths, hat, inverse, cotangent, weights, vectors)


def attend_backward(
    p_ref,
    q_ref,
    k_ref,
    v_ref,
    x_ref,
    ctx_ref,
    grad_ctx_ref,
    branch_ref,
    first_ref,
    w_ref,
    input_ref,
    grad_ref,
    sum_ref,
    pulled,
):
    step = pl.program_id(0)
    quad, block = step // 2, lax.rem(step, 2)
    here = pl.ds(pl.multiple_of(block * ROWS, ROWS), ROWS)
    cols = pl.ds(pl.multiple_of(quad * 256, 256), 256)

    @pl.when(step == 0)
    def _():
        sum_ref[...] = jnp.zeros_like(sum_ref)
        input_ref[...] = first_ref[...]

    for pair in range(2):
        half = slice(128 * pair, 128 * pair + 128)
        at = pl.ds(pl.multiple_of(quad * 256 + 128 * pair, 128), 128)
        heads = p_ref.at[0, pl.ds(2 * pair, 2)]
        grads = attend_back_pair(
            grad_ctx_ref[here, at], ctx_ref[here, at], heads, q_ref[:, half], k_ref[:, half], v_ref[:, half]
        )
        for number, grad in enumerate(grads):
            pulled[number, here, half] = grad
        sum_ref[0:1, at] += columns_total(grads[0].astype(jnp.float32))
        sum_ref[1:2, at] += columns_total(grads[2].astype(jnp.float32))

    more = input_ref[here, :]
    for at in range(3):
        more = more + dot_back(pulled[at, here, :], w_ref[at, :, cols])
    input_ref[here, :] = more

    @pl.when(block == 1)
    def _():
        for tile in range(3):
            grad_ref[tile, :, cols] = outer(x_ref[...], pulled[tile]).astype(jnp.bfloat16)
        grad_ref[3, :, cols] = outer(ctx_ref[...], branch_ref[:, cols]).astype(jnp.bfloat16)


def attended_back(probs, query, keyed, valued, x, context, grad_context, grad_branch, grad_first, weights):
    tokens, width = x.shape
    low = jnp.bfloat16
    shaped = jax.ShapeDtypeStruct
    once = pl.Buffered(1)
    quad = pl.BlockSpec((ROWS, 256), lambda i: (lax.rem(i, 2), i // 2))
    whole = pl.BlockSpec((tokens, width), lambda i: (0, 0), pipeline_mode=once)
    return pl.pallas_call(
        attend_backward,
        grid=(6,),
        out_shape=(
            shaped((tokens, width), jnp.float32),
            shaped((4, width, width), low),
            shaped((16, width), jnp.float32),
        ),
        in_specs=[
            pl.BlockSpec((1, 4, ROWS, ROWS), lambda i: (lax.rem(i, 2), i // 2, 0, 0)),
            quad,
            quad,
            quad,
            whole,
            whole,
            whole,
            whole,
            whole,
            pl.BlockSpec((3, width, width), lambda i: (0, 0, 0), pipeline_mode=once),
        ],
        out_specs=(
            whole,
            pl.BlockSpec((4, width, width), lambda i: (0, 0, 0), pipeline_mode=once),
            pl.BlockSpec((16, width), lambda i: (0, 0)),
        ),
        scratch_shapes=[pltpu.VMEM((3, tokens, 256), low)],
        compiler_params=pltpu.CompilerParams(vmem_limit_bytes=56 * 2**20),
        name="attend_backward",
    )(probs, query, keyed, valued, x, context, grad_context, grad_branch, grad_first, weights)


def moved(param, grad, first, second, average, rate):
    param_new, first_new, second_new = adam_update(param, grad, first, second, rate)
    return param_new, first_new, second_new, average_rate * average + (1.0 - average_rate) * param_new


def update_kernel(
    gain_scale,
    grad_ref,
    master_ref,
    first_ref,
    second_ref,
    ema_ref,
    vec_grad_ref,
    bias_ref,
    gain_ref,
    vec_first_ref,
    vec_second_ref,
    vec_ema_ref,
    mixed_in,
    input_in,
    master_out,
    first_out,
    second_out,
    ema_out,
    copy_out,
    vec_out,
    vec_first_out,
    vec_second_out,
    vec_ema_out,
    mixed_out,
    input_out,
    vec_ref,
):
    mixed_out[...] = mixed_in[...]
    input_out[...] = input_in[...]

    @pl.when((pl.program_id(0) == 0) & (pl.program_id(1) == 0))
    def _():
        vec_ref[0:10, :] = bias_ref[...]
        vec_ref[10:12, :] = gain_ref[...]
        vec_grad = vec_grad_ref[0:VROWS, :] * gain_scale
        vec_out[...], vec_first_out[...], vec_second_out[...], vec_ema_out[...] = moved(
            vec_ref[...], vec_grad, vec_first_ref[...], vec_second_ref[...], vec_ema_ref[...], vector_rate
        )

    grad = grad_ref[...].astype(jnp.float32) * gain_scale
    result = moved(master_ref[0], grad, first_ref[0], second_ref[0], ema_ref[0], tile_rate)
    master_out[0], first_out[0], second_out[0], ema_out[0] = result
    copy_out[0] = result[0].astype(jnp.bfloat16)


def updated(
    gain_scale,
    slot_grads,
    master,
    first,
    second,
    ema,
    vec_grad,
    bias,
    gain,
    vec_first,
    vec_second,
    vec_ema,
    mixed,
    input_grad,
):
    width = master.shape[-1]
    chunk = 96
    tile = pl.BlockSpec((1, 1, chunk, width), lambda s, r: (0, s, r, 0))
    steps = width // chunk
    rows = pl.BlockSpec((mixed.shape[0] // (SLOTS * steps), width), lambda s, r: (s * steps + r, 0))

    def whole(value):
        return pl.BlockSpec(value.shape, lambda s, r: (0, 0))

    shaped = jax.ShapeDtypeStruct
    tile_shape = shaped(master.shape, jnp.float32)
    vec_shape = shaped((VROWS, width), jnp.float32)
    results = pl.pallas_call(
        functools.partial(update_kernel, gain_scale),
        grid=(SLOTS, steps),
        out_shape=(tile_shape,) * 4
        + (shaped(master.shape, jnp.bfloat16),)
        + (vec_shape,) * 4
        + (shaped(mixed.shape, mixed.dtype), shaped(input_grad.shape, input_grad.dtype)),
        in_specs=[pl.BlockSpec((1, chunk, width), lambda s, r: (s, r, 0))]
        + [tile] * 4
        + [whole(value) for value in (vec_grad, bias, gain, vec_first, vec_second, vec_ema)]
        + [rows] * 2,
        out_specs=(tile,) * 5 + (whole(vec_first),) * 4 + (rows,) * 2,
        scratch_shapes=[pltpu.VMEM((VROWS, width), jnp.float32)],
        compiler_params=pltpu.CompilerParams(vmem_limit_bytes=62 * 2**20),
        name="update",
    )(
        slot_grads,
        master,
        first,
        second,
        ema,
        vec_grad,
        bias,
        gain,
        vec_first,
        vec_second,
        vec_ema,
        mixed,
        input_grad,
    )
    return results[-2:] + results[:-2]


MESH = pl.DeviceIdType.MESH
GROUP = 32
PAIRS = TILES // 2
PLANE = 8
PIECE = 96
PAIR_TILES = ((0, 1), (2, 3), (4, 8), (5, 9), (6, 10), (7, 11))


def remote(src, dst, send, recv, device):
    return pltpu.make_async_remote_copy(
        src_ref=src, dst_ref=dst, send_sem=send, recv_sem=recv, device_id=(device,), device_id_type=MESH
    )


def place(device):
    core = lax.rem(device, 2)
    x = lax.rem(device // 2, 2)
    y = lax.rem(device // 4, 2)
    z = device // 8
    return z, y, x, core


def start(copies):
    for copy in copies:
        copy.start()


def arrive(copies):
    for copy in copies:
        copy.wait_recv()


def greet(z, in_plane):
    barrier = pltpu.get_barrier_semaphore()
    for hop in range(1, PLANE):
        other = z * PLANE + lax.rem(in_plane + hop, PLANE)
        pl.semaphore_signal(barrier, inc=1, device_id=(other,), device_id_type=MESH)
    for hop in range(1, 4):
        other = lax.rem(z + hop, 4) * PLANE + in_plane
        pl.semaphore_signal(barrier, inc=1, device_id=(other,), device_id_type=MESH)
    pl.semaphore_wait(barrier, PLANE + 2)


def along_z(z, in_plane):
    inner = (1 + z // 2) * PLANE + in_plane
    other_middle = (3 - z) * PLANE + in_plane
    outer_end = lax.rem(lax.rem(z + 3, 4) * 3, 4) * PLANE + in_plane
    return inner, other_middle, outer_end


def third(part):
    return pl.ds(256 * part, 256)


UNITS = [(0, 4, pl.ds(256 * part, 256)) for part in range(3)]
UNITS += [(2 * pair, 2, pl.ds(0, 768)) for pair in range(2, PAIRS)]
Z_PARTS = (pl.ds(0, 512), pl.ds(512, 256))


POSITIONS = [tile for pair in PAIR_TILES for tile in pair]


def slot_number(owners, tile):
    number = jnp.int32(0)
    for earlier in range(tile):
        number = number + jnp.where(owners[earlier] == owners[tile], 1, 0)
    return number

FRONT_PLAN = (
    (
        ("open",),
        ("swap", 0),
        ("sent", 0),
        ("swap", 1),
        ("choose", 0),
        ("end", 0),
        ("sent", 1),
        ("middle", 0),
        ("choose", 1),
        ("end", 1),
        ("swap", 2),
        ("total", 0),
        ("end", 3, 0),
        ("middle", 1),
        ("mid", 0),
        ("choose", 2),
        ("end", 2),
        ("end", 3, 1),
        ("far", 0),
        ("middle", 3, 0),
        ("total", 1),
        ("caps",),
        ("middle", 3, 1),
        ("end", 4, 0),
        ("mid", 1),
        ("near", 0),
        ("total", 3, 0),
        ("end", 5, 0),
        ("middle", 2),
        ("end", 4, 1),
        ("total", 3, 1),
        ("far", 1),
        ("finish", 0),
    ),
    (
        ("middle", 4, 0),
        ("total", 2),
        ("mid", 3),
        ("middle", 4, 1),
        ("end", 5, 1),
    ),
    (
        ("mid", 2),
        ("end", 6, 0),
        ("middle", 5, 0),
        ("near", 1),
        ("total", 4, 1),
        ("far", 3),
        ("finish", 1),
        ("far", 2),
        ("middle", 5, 1),
        ("end", 6, 1),
        ("total", 4, 0),
    ),
    (
        ("total", 5, 0),
        ("middle", 6, 0),
        ("mid", 4),
        ("total", 5, 1),
        ("middle", 6, 1),
    ),
    (
        ("total", 6, 1),
        ("mid", 5),
        ("near", 2),
        ("far", 4),
        ("total", 6, 0),
        ("finish", 2),
        ("keep", 0),
        ("keep", 1),
    ),
    (
        ("mid", 6),
        ("near", 3),
        ("near", 4),
        ("far", 5),
    ),
    (
        ("far", 6),
        ("finish", 4),
        ("keep", 3),
        ("finish", 3),
        ("keep", 2),
    ),
    (
        ("near", 5),
    ),
    (
        ("near", 6),
        ("finish", 5),
        ("keep", 4),
    ),
    (
        ("finish", 6),
        ("keep", 5),
    ),
)


def gather_and_forward(
    counts,
    lengths,
    owners,
    bias_ref,
    gain_ref,
    x_hbm,
    cot_hbm,
    master_hbm,
    q_ref,
    k_ref,
    v_ref,
    p_ref,
    ctx_hbm,
    x_turned_hbm,
    ctx_turned_hbm,
    hidden_hbm,
    active_hbm,
    slope_hbm,
    down_hbm,
    mixed_hbm,
    second_hbm,
    hat_hbm,
    w_out,
    inverse_ref,
    sum_ref,
    vec_ref,
    cap_ref,
    wide,
    low,
    stage_a,
    stage_b,
    stage_c,
    chosen,
    from_end,
    from_middle,
    w_buf,
    x_then_hidden,
    x_turned,
    ctx_turned,
    hidden_turned,
    ctx_ref,
    cot_then_down,
    mixed_ref,
    hat_ref,
    slope_buf,
    active_buf,
    wide_sem,
    load_sem,
    store_sem,
    half_sem,
    tile_sem,
    out_sem,
    swap_send,
    swap_recv,
    z_send,
    z_recv,
    mid_send,
    mid_recv,
    far_send,
    far_recv,
    near_send,
    near_recv,
):
    step = pl.program_id(0)
    width = 8 * PIECE
    me = lax.axis_index("dp")
    z, y, x, core = place(me)
    in_plane = lax.rem(me, PLANE)
    sibling = me + 1 - 2 * core
    x_peer = me + 2 - 4 * x
    y_peer = me + 4 - 8 * y
    z_targets = along_z(z, in_plane)
    stages = (stage_a, stage_b, stage_c)
    is_end = (z == 0) | (z == 3)
    is_middle = (z == 1) | (z == 2)

    def piece_rows(cell_core, cell_x, cell_y):
        return pl.ds(pl.multiple_of(((cell_core * 2 + cell_x) * 2 + cell_y) * PIECE, 16), PIECE)

    def wide_load(part):
        cols = third(part)
        return pltpu.make_async_copy(master_hbm.at[:, cols], wide.at[:, cols], wide_sem.at[part])

    def swap(part):
        wide_load(part).wait()
        for slot in range(SLOTS):
            master = wide[width * slot : width * (slot + 1), third(part)]
            low[slot, :, third(part)] = master.astype(jnp.bfloat16)

        def send(hop, carry):
            target = lax.rem(in_plane + hop, PLANE)
            _, ty, tx, tc = place(target)
            remote(
                low.at[:, piece_rows(tc, tx, ty), third(part)],
                stages[part].at[pl.ds(2 * in_plane, 2)],
                swap_send.at[part],
                swap_recv.at[part],
                z * PLANE + target,
            ).start()
            return carry

        lax.fori_loop(1, PLANE, send, 0)
        stages[part][pl.ds(2 * in_plane, 2)] = low[:, piece_rows(core, x, y), third(part)]
        if part == 0:
            start([load(0), load(1)])

    def swap_wait(part, sem):
        most = stages[part].at[pl.ds(0, 2 * PLANE - 2)]
        pltpu.make_async_copy(most, most, sem.at[part]).wait()

    def z_copy(unit, part, level):
        first, count, cols = UNITS[unit]
        tiles = pl.ds(first, count)
        cols = cols if count == 4 else Z_PARTS[part]
        src = w_buf.at[tiles, core, x, y, :, cols] if level == 2 else chosen.at[tiles, :, cols]
        dst = (from_end.at[tiles, :, cols], from_middle.at[tiles, :, cols], src)[level]
        at = level, unit, part
        return remote(src, dst, z_send.at[at], z_recv.at[at], z_targets[level])

    def z_parts(unit):
        return range(1 if UNITS[unit][1] == 4 else 2)

    def z_end(unit, part=0):
        @pl.when(is_end)
        def _():
            z_copy(unit, part, 0).start()

    def z_rows(unit, part):
        first, count, cols = UNITS[unit]
        return pl.ds(first, count), cols if count == 4 else Z_PARTS[part]

    def z_middle(unit, part=0):
        @pl.when(is_middle)
        def _():
            z_copy(unit, part, 0).wait_recv()
            tiles, cols = z_rows(unit, part)
            chosen[tiles, :, cols] = chosen[tiles, :, cols] + from_end[tiles, :, cols]
            z_copy(unit, part, 1).start()

    def z_total(unit, part=0):
        @pl.when(is_middle)
        def _():
            z_copy(unit, part, 1).wait_recv()
            tiles, cols = z_rows(unit, part)
            w_buf[tiles, core, x, y, :, cols] = chosen[tiles, :, cols] + from_middle[tiles, :, cols]
            z_copy(unit, part, 2).start()

    def mid_copies(unit):
        first, count, cols = UNITS[unit]
        copies = []
        for n, peer in enumerate((y_peer, x_peer)):
            spot = w_buf.at[pl.ds(first + n * count // 2, count // 2), core, x, y, :, cols]
            copies.append(remote(spot, spot, mid_send.at[unit, n], mid_recv.at[unit, n], peer))
        return copies

    def far_copies(unit):
        first, count, cols = UNITS[unit]
        half = count // 2
        by_row = w_buf.at[pl.ds(first, half), core, x, :, :, cols]
        by_column = w_buf.at[pl.ds(first + half, half), core, :, y, :, cols]
        return [
            remote(spot, spot, far_send.at[unit, n], far_recv.at[unit, n], peer)
            for n, (spot, peer) in enumerate(((by_row, x_peer), (by_column, y_peer)))
        ]

    def near_copy(unit):
        first, count, cols = UNITS[unit]
        spot = w_buf.at[pl.ds(first, count), core, :, :, :, cols]
        return remote(spot, spot, near_send.at[unit], near_recv.at[unit], sibling)

    def give_mid(unit):
        @pl.when(is_end)
        def _():
            arrive([z_copy(unit, part, 2) for part in z_parts(unit)])

        start(mid_copies(unit))

    def give_far(unit):
        arrive(mid_copies(unit))
        start(far_copies(unit))

    def give_near(unit):
        arrive(far_copies(unit))
        near_copy(unit).start()

    def finish(unit):
        near_copy(unit).wait_recv()

    def choose(part):
        swap_wait(part, swap_recv)
        for pair in range(PAIRS):
            for n, tile in enumerate(PAIR_TILES[pair]):
                owner = owners[tile]
                value = stages[part][SLOTS * lax.rem(owner, PLANE) + slot_number(owners, tile)]
                chosen[2 * pair + n, :, third(part)] = jnp.where(
                    owner // PLANE == z, value, jnp.zeros_like(value)
                )

    def load(at):
        src = (x_hbm, cot_hbm)[at]
        dst = (x_then_hidden, cot_then_down)[at]
        return pltpu.make_async_copy(src, dst, load_sem.at[at])

    def store(at):
        src, dst = (
            (hidden_turned, hidden_hbm),
            (ctx_ref, ctx_hbm),
            (hat_ref, hat_hbm),
            None,
            None,
            None,
            (x_turned, x_turned_hbm),
            (ctx_turned, ctx_turned_hbm),
        )[at]
        return pltpu.make_async_copy(src, dst, store_sem.at[at])

    def half_stores(half):
        rows = pl.ds(ROWS * half, ROWS)
        pairs = ((cot_then_down, down_hbm), (mixed_ref, mixed_hbm), (wide, second_hbm))
        return [
            pltpu.make_async_copy(src.at[rows], dst.at[rows], half_sem.at[half, at])
            for at, (src, dst) in enumerate(pairs)
        ]

    def w_store(pair):
        two = pl.ds(2 * pair, 2)
        return pltpu.make_async_copy(w_buf.at[two], w_out.at[two], out_sem.at[pair])

    def weight(at, cols=slice(None)):
        value = w_buf[at, :, :, :, :, cols]
        return value.reshape(width, value.shape[-1])

    def open_all():
        start([wide_load(part) for part in range(3)])
        sum_ref[...] = jnp.zeros_like(sum_ref)
        vec_ref[0:10, :] = bias_ref[...]
        vec_ref[10:12, :] = gain_ref[...]
        greet(z, in_plane)

    def make_caps():
        for block in range(2):
            cap_ref[block] = attention_caps(counts, lengths, block)
        load(0).wait()
        x_turned[...] = x_then_hidden[...].T
        store(6).start()

    actions = {
        "open": open_all,
        "caps": make_caps,
        "swap": swap,
        "sent": lambda part: swap_wait(part, swap_send),
        "choose": choose,
        "end": z_end,
        "middle": z_middle,
        "total": z_total,
        "mid": give_mid,
        "far": give_far,
        "near": give_near,
        "finish": finish,
        "keep": lambda pair: w_store(pair).start(),
    }

    for at, work in enumerate(FRONT_PLAN):

        @pl.when(step == at)
        def _():
            for name, *rest in work:
                actions[name](*rest)

    quad, block = step // 2, lax.rem(step, 2)
    here = pl.ds(pl.multiple_of(block * ROWS, ROWS), ROWS)

    @pl.when(step < 6)
    def _():
        attend_quad(
            quad,
            weight,
            x_then_hidden.at[here],
            vec_ref,
            cap_ref.at[block],
            q_ref,
            k_ref,
            v_ref,
            p_ref,
            ctx_ref.at[here],
        )

    @pl.when((step >= 4) & (step < 6))
    def _():
        branch = dot(ctx_ref[here, :], weight(3)) + vec_ref[2:3, :]
        hat, inverse = normalize(x_then_hidden[here, :].astype(jnp.float32) + branch)
        hat_ref[here, :] = hat.astype(jnp.bfloat16)
        inverse_ref[here, :] = inverse
        hidden = hat * vec_ref[10:11, :] + vec_ref[8:9, :]
        hidden_low = hidden.astype(jnp.bfloat16)
        x_then_hidden[here, :] = hidden_low
        hidden_turned[:, here] = hidden_low.T
        ctx_turned[:, here] = ctx_ref[here, :].T
        wide[here, :] = hidden + vec_ref[7:8, :]

    @pl.when(step == 5)
    def _():
        start([store(0), store(1), store(2), store(7)])

    turn = step - 6
    slot = lax.rem(turn, 2)

    def tile_stores(source_slot, tile):
        return [
            pltpu.make_async_copy(src.at[source_slot], dst.at[tile], tile_sem.at[source_slot, at])
            for at, (src, dst) in enumerate(((active_buf, active_hbm), (slope_buf, slope_hbm)))
        ]

    @pl.when(turn >= 2)
    def _():
        for copy in tile_stores(slot, 0):
            copy.wait()

    @pl.when(turn >= 0)
    def _():
        for half in range(2):
            rows = slice(ROWS * half, ROWS * half + ROWS)
            up = dot(x_then_hidden[rows, :], weight(4 + 2 * turn)) + vec_ref[pl.ds(3 + turn, 1), :]
            active, slope = gelu_parts(up)
            slope_buf[slot, rows, :] = slope.astype(jnp.bfloat16)
            active_buf[slot, :, rows] = active.T
            wide[rows, :] = wide[rows, :] + dot(active, weight(5 + 2 * turn))
        start(tile_stores(slot, turn))

    @pl.when(step == 9)
    def _():
        load(1).wait()
        for half in range(2):
            rows = slice(ROWS * half, ROWS * half + ROWS)
            at_row = lax.broadcasted_iota(jnp.int32, (ROWS, 1), 0) + half * ROWS
            live = passage_facts(counts, lengths, at_row)[0].astype(jnp.float32)
            hat, inverse = normalize(wide[rows, :])
            mixed = (hat * vec_ref[11:12, :] + vec_ref[9:10, :]) * live
            mixed_ref[rows, :] = mixed.astype(jnp.bfloat16)
            grad_out = cot_then_down[rows, :].astype(jnp.float32) * live
            sum_ref[11:12, :] += columns_total(grad_out * hat)
            sum_ref[9:10, :] += columns_total(grad_out)
            second = normalize_back(grad_out * vec_ref[11:12, :], hat, inverse)
            wide[rows, :] = second
            down_low = second.astype(jnp.bfloat16)
            cot_then_down[rows, :] = down_low
            sum_ref[7:8, :] += columns_total(down_low.astype(jnp.float32))
            start(half_stores(half))
        for at in range(2):
            for copy in tile_stores(at, 0):
                copy.wait()
        for pair in range(PAIRS):
            w_store(pair).wait()
        swap_wait(2, swap_send)
        for unit in range(len(UNITS)):
            for copy in mid_copies(unit) + far_copies(unit) + [near_copy(unit)]:
                copy.wait_send()

            @pl.when(is_end)
            def _():
                for part in z_parts(unit):
                    z_copy(unit, part, 0).wait_send()

            @pl.when(is_middle)
            def _():
                for part in z_parts(unit):
                    z_copy(unit, part, 1).wait_send()
                    z_copy(unit, part, 2).wait_send()

        for at in (0, 1, 2, 6, 7):
            store(at).wait()
        for copy in half_stores(0) + half_stores(1):
            copy.wait()


def gathered_and_forwarded(counts, lengths, owners, bias, gain, x, cotangent, master):
    tokens, width = x.shape
    blocks = tokens // ROWS
    low, high = jnp.bfloat16, jnp.float32
    smem = pl.BlockSpec(memory_space=pltpu.SMEM)
    any_space = pl.BlockSpec(memory_space=pl.ANY)
    dma = pltpu.SemaphoreType.DMA
    shaped = jax.ShapeDtypeStruct

    def at(step):
        step = jnp.minimum(step, 5)
        return lax.rem(step, 2), step // 2

    quad = pl.BlockSpec((ROWS, 256), at)
    rows = shaped((tokens, width), low)
    turned = shaped((width, tokens), low)
    cut = (2, 2, 2, PIECE, width)
    units = len(UNITS)
    return pl.pallas_call(
        gather_and_forward,
        grid=(10,),
        out_shape=(
            rows,
            rows,
            rows,
            shaped((blocks, HEADS, ROWS, ROWS), low),
            rows,
            turned,
            turned,
            turned,
            shaped((4, width, tokens), low),
            shaped((4, tokens, width), low),
            rows,
            rows,
            shaped((tokens, width), high),
            rows,
            shaped((TILES,) + cut, low),
            shaped((tokens, 1), high),
            shaped((16, width), high),
        ),
        in_specs=[smem] * 3
        + [pl.BlockSpec(bias.shape, lambda i: (0, 0)), pl.BlockSpec(gain.shape, lambda i: (0, 0))]
        + [any_space] * 3,
        out_specs=(quad, quad, quad, pl.BlockSpec((1, 4, ROWS, ROWS), lambda i: (*at(i), 0, 0)))
        + (any_space,) * 11
        + (
            pl.BlockSpec((tokens, 1), lambda i: (0, 0), pipeline_mode=pl.Buffered(1)),
            pl.BlockSpec((16, width), lambda i: (0, 0)),
        ),
        scratch_shapes=[
            pltpu.VMEM((VROWS, width), high),
            pltpu.VMEM((2, ROWS, ROWS), high),
            pltpu.VMEM((SLOTS * width, width), high),
            pltpu.VMEM((SLOTS, width, width), low),
            pltpu.VMEM((2 * PLANE, PIECE, 256), low),
            pltpu.VMEM((2 * PLANE, PIECE, 256), low),
            pltpu.VMEM((2 * PLANE, PIECE, 256), low),
            pltpu.VMEM((TILES, PIECE, width), low),
            pltpu.VMEM((TILES, PIECE, width), low),
            pltpu.VMEM((TILES, PIECE, width), low),
            pltpu.VMEM((TILES,) + cut, low),
            pltpu.VMEM((tokens, width), low),
            pltpu.VMEM((width, tokens), low),
            pltpu.VMEM((width, tokens), low),
            pltpu.VMEM((width, tokens), low),
            pltpu.VMEM((tokens, width), low),
            pltpu.VMEM((tokens, width), low),
            pltpu.VMEM((tokens, width), low),
            pltpu.VMEM((tokens, width), low),
            pltpu.VMEM((2, tokens, width), low),
            pltpu.VMEM((2, width, tokens), low),
            dma((3,)),
            dma((2,)),
            dma((8,)),
            dma((2, 3)),
            dma((2, 2)),
            dma((PAIRS,)),
            dma((3,)),
            dma((3,)),
            dma((3, units, 2)),
            dma((3, units, 2)),
            dma((units, 2)),
            dma((units, 2)),
            dma((units, 2)),
            dma((units, 2)),
            dma((units,)),
            dma((units,)),
        ],
        compiler_params=pltpu.CompilerParams(
            collective_id=0, has_side_effects=True, vmem_limit_bytes=63 * 2**20
        ),
        name="gather_and_forward",
    )(counts, lengths, owners, bias, gain, x, cotangent, master.reshape(SLOTS * width, width))


BACK_PLAN = (
    (),
    (),
    (
        ("core", 0),
    ),
    (),
    (
        ("core", 1),
        ("far", 0),
    ),
    (),
    (
        ("core", 2),
        ("far", 1),
    ),
    (
        ("mid", 0),
        ("far", 2),
    ),
    (),
    (
        ("core", 3),
        ("mid", 1),
        ("end", 0),
    ),
    (),
    (
        ("far", 3),
        ("end", 1),
        ("mid", 2),
    ),
    (
        ("core", 4),
        ("middle", 0),
    ),
    (),
    (
        ("middle", 1),
        ("end", 2),
        ("mid", 3),
        ("far", 4),
    ),
    (
        ("total", 0),
    ),
    (
        ("middle", 2),
        ("end", 3),
        ("total", 1),
        ("core", 5),
        ("mid", 4),
    ),
    (),
    (
        ("far", 5),
        ("end", 4),
        ("middle", 3),
        ("total", 2),
    ),
    (),
    (
        ("core", 6),
        ("total", 3),
        ("middle", 4),
        ("mid", 5),
        ("far", 6),
        ("total", 4),
        ("sum", 0),
        ("end", 5),
        ("mid", 6),
        ("middle", 5),
        ("end", 6),
        ("take", 4),
        ("take", 0),
        ("sum", 1),
        ("take", 2),
        ("take", 3),
        ("take", 1),
        ("deliver", 0),
        ("total", 5),
        ("middle", 6),
        ("sum", 2),
        ("take", 5),
        ("deliver", 1),
        ("total", 6),
        ("take", 6),
        ("deliver", 2),
        ("input", 0),
        ("input", 1),
    ),
)


def backward_and_reduce(
    owners,
    p_ref,
    q_ref,
    k_ref,
    v_ref,
    inverse_ref,
    gain_ref,
    late_ref,
    ctx_hbm,
    x_turned_hbm,
    ctx_turned_hbm,
    hidden_hbm,
    active_hbm,
    slope_hbm,
    down_hbm,
    second_hbm,
    hat_hbm,
    w_hbm,
    input_hbm,
    slot_grad,
    vec_out,
    w_part,
    acc,
    hidden_then_x,
    active_then_ctx,
    down_then_branch,
    ctx_ref,
    grad_ctx_ref,
    hat_ref,
    slope_then_query,
    up_then_key,
    value_buf,
    part,
    from_core,
    from_far,
    from_mid,
    from_end,
    from_middle,
    total,
    snap,
    outbox,
    vec_now,
    vec_in,
    holds,
    keeps,
    load_sem,
    w_sem,
    core_send,
    core_recv,
    far_send,
    far_recv,
    mid_send,
    mid_recv,
    z_send,
    z_recv,
    vec_send,
    vec_recv,
    out_send,
    out_recv,
):
    step = pl.program_id(0)
    inner = jnp.maximum(step - 4, 0)
    quad, block, pair = inner // 4, lax.rem(inner, 4) // 2, lax.rem(inner, 2)
    me = lax.axis_index("dp")
    z, y, x, core = place(me)
    in_plane = lax.rem(me, PLANE)
    sibling = me + 1 - 2 * core
    x_peer = me + 2 - 4 * x
    y_peer = me + 4 - 8 * y
    z_targets = along_z(z, in_plane)
    is_end = (z == 0) | (z == 3)
    is_middle = (z == 1) | (z == 2)

    def tiles_of(batch):
        if batch < 4:
            return w_part, 4 + 2 * batch, 2, slice(None)
        return part, 0, 4, pl.ds(256 * (batch - 4), 256)

    def halves(batch, turned):
        ref, first, count, cols = tiles_of(batch)
        return ref, pl.ds(first + turned * count // 2, count // 2), cols

    def core_copy(batch):
        ref, first, count, cols = tiles_of(batch)
        tiles = pl.ds(first, count)
        return remote(
            ref.at[tiles, 1 - core, :, :, :, cols],
            from_core.at[tiles, :, :, :, cols],
            core_send.at[batch],
            core_recv.at[batch],
            sibling,
        )

    def far_copies(batch):
        copies = []
        for turned in range(2):
            ref, tiles, cols = halves(batch, turned)
            src = ref.at[tiles, core, :, 1 - y, :, cols] if turned else ref.at[tiles, core, 1 - x, :, :, cols]
            copies.append(
                remote(
                    src,
                    from_far.at[tiles, :, :, cols],
                    far_send.at[batch, turned],
                    far_recv.at[batch, turned],
                    y_peer if turned else x_peer,
                )
            )
        return copies

    def mid_copies(batch):
        copies = []
        for turned in range(2):
            ref, tiles, cols = halves(batch, turned)
            src = ref.at[tiles, core, 1 - x, y, :, cols] if turned else ref.at[tiles, core, x, 1 - y, :, cols]
            copies.append(
                remote(
                    src,
                    from_mid.at[tiles, :, cols],
                    mid_send.at[batch, turned],
                    mid_recv.at[batch, turned],
                    x_peer if turned else y_peer,
                )
            )
        return copies

    def z_copy(batch, stage):
        ref, first, count, cols = tiles_of(batch)
        tiles = pl.ds(first, count)
        if stage == 2:
            src, dst = total.at[tiles, :, cols], total.at[tiles, :, cols]
        else:
            src = ref.at[tiles, core, x, y, :, cols]
            dst = (from_middle if stage else from_end).at[tiles, :, cols]
        return remote(src, dst, z_send.at[stage, batch], z_recv.at[stage, batch], z_targets[stage])

    def give_core(batch):
        core_copy(batch).start()

    def give_far(batch):
        core_copy(batch).wait_recv()
        ref, first, count, cols = tiles_of(batch)
        for tile in range(first, first + count):
            ref[tile, core, :, :, :, cols] = ref[tile, core, :, :, :, cols] + from_core[tile, :, :, :, cols]
        start(far_copies(batch))

    def give_mid(batch):
        arrive(far_copies(batch))
        for turned in range(2):
            ref, tiles, cols = halves(batch, turned)
            if turned:
                ref[tiles, core, :, y, :, cols] = ref[tiles, core, :, y, :, cols] + from_far[tiles, :, :, cols]
            else:
                ref[tiles, core, x, :, :, cols] = ref[tiles, core, x, :, :, cols] + from_far[tiles, :, :, cols]
        start(mid_copies(batch))

    def add_piece(batch, other):
        ref, first, count, cols = tiles_of(batch)
        tiles = pl.ds(first, count)
        return ref[tiles, core, x, y, :, cols] + other[tiles, :, cols]

    def give_end(batch):
        arrive(mid_copies(batch))
        ref, first, count, cols = tiles_of(batch)
        ref[pl.ds(first, count), core, x, y, :, cols] = add_piece(batch, from_mid)

        @pl.when(is_end)
        def _():
            z_copy(batch, 0).start()

    def give_middle(batch):
        @pl.when(is_middle)
        def _():
            z_copy(batch, 0).wait_recv()
            ref, first, count, cols = tiles_of(batch)
            ref[pl.ds(first, count), core, x, y, :, cols] = add_piece(batch, from_end)
            z_copy(batch, 1).start()

    def give_total(batch):
        @pl.when(is_middle)
        def _():
            z_copy(batch, 1).wait_recv()
            _, first, count, cols = tiles_of(batch)
            total[pl.ds(first, count), :, cols] = add_piece(batch, from_middle)
            z_copy(batch, 2).start()

    def take_total(batch):
        @pl.when(is_end)
        def _():
            z_copy(batch, 2).wait_recv()

    def deliver(third):
        cols = pl.ds(256 * third, 256)
        snap[...] = total[:, :, cols]

        def fill(at, carry):
            value = snap[holds[at]]
            outbox[third, at] = jnp.where(keeps[at] > 0, value, jnp.zeros_like(value))
            return carry

        lax.fori_loop(0, 2 * PLANE, fill, 0)

        def send(hop, carry):
            target = lax.rem(in_plane + hop, PLANE)
            remote(
                outbox.at[third, pl.ds(2 * target, 2)],
                slot_grad.at[:, core, x, y, :, cols],
                out_send.at[third],
                out_recv.at[third],
                z * PLANE + target,
            ).start()
            return carry

        lax.fori_loop(1, PLANE, send, 0)
        keep_copy(third).start()

    def keep_copy(third):
        return pltpu.make_async_copy(
            outbox.at[third, pl.ds(2 * in_plane, 2)],
            slot_grad.at[:, core, x, y, :, pl.ds(256 * third, 256)],
            load_sem.at[5 + third],
        )

    def vec_copies(stage):
        if stage < 3:
            hops = [(stage, (sibling, x_peer, y_peer)[stage])]
        else:
            hops = [
                (2 + hop, lax.rem(z + hop, 4) * PLANE + in_plane) for hop in range(1, 4)
            ]
        return [
            remote(vec_now.at[stage], vec_in.at[at], vec_send.at[at], vec_recv.at[at], device)
            for at, device in hops
        ]

    def vec_next(stage):
        arrive(vec_copies(stage))
        vec_now[stage + 1] = vec_now[stage] + vec_in[stage]
        start(vec_copies(stage + 1))

    def input_store():
        return pltpu.make_async_copy(acc, input_hbm, load_sem.at[4])

    def load(at):
        src, dst = (
            (hidden_hbm, hidden_then_x),
            (down_hbm, down_then_branch),
            (second_hbm, acc),
            (hat_hbm, hat_ref),
            None,
            None,
            None,
            None,
            (x_turned_hbm, hidden_then_x),
            (ctx_turned_hbm, active_then_ctx),
            None,
            None,
            (ctx_hbm, ctx_ref),
        )[at]
        return pltpu.make_async_copy(src, dst, load_sem.at[at])

    def tile_load(tile, side):
        src, dst = ((slope_hbm, slope_then_query), (active_hbm, active_then_ctx))[side]
        return pltpu.make_async_copy(src.at[tile], dst, load_sem.at[10 + side])

    def w_load(at):
        return pltpu.make_async_copy(w_hbm.at[at], w_part.at[at], w_sem.at[at])

    def weight(at, cols=slice(None)):
        value = w_part[at, :, :, :, :, cols]
        return value.reshape(8 * PIECE, value.shape[-1])

    def input_rows(half):
        rows = slice(ROWS * half, ROWS * half + ROWS)
        more = acc[rows, :]
        for at, buf in enumerate((slope_then_query, up_then_key, value_buf)):
            more = more + dot_back(buf[rows, :], weight(at))
        acc[rows, :] = more
        if half == 1:
            input_store().start()

    actions = {
        "core": give_core,
        "far": give_far,
        "mid": give_mid,
        "end": give_end,
        "middle": give_middle,
        "total": give_total,
        "take": take_total,
        "deliver": deliver,
        "sum": vec_next,
        "input": input_rows,
    }

    @pl.when(step == 0)
    def _():
        start([load(1), tile_load(0, 0), w_load(5), w_load(4)])
        for at in range(2 * PLANE):
            tile_here, kept = jnp.int32(0), jnp.int32(0)
            for tile in range(TILES):
                place_of = SLOTS * owners[tile] + slot_number(owners, tile)
                match = place_of == z * 2 * PLANE + at
                tile_here = tile_here + jnp.where(match, POSITIONS.index(tile), 0)
                kept = kept + jnp.where(match, 1, 0)
            holds[at] = tile_here
            keeps[at] = kept
        vec_now[0] = late_ref[...]
        greet(z, in_plane)

    def serve(points):
        for at in points:
            if BACK_PLAN[at]:

                @pl.when(step == (at // 2 if at < 8 else at - 4))
                def _():
                    for name, number in BACK_PLAN[at]:
                        actions[name](number)

    serve(range(0, 8, 2))

    @pl.when(step < 4)
    def _():
        tile_load(step, 0).wait()
        w_load(5 + 2 * step).wait()

        @pl.when(step == 0)
        def _():
            load(1).wait()
            start([load(2), tile_load(0, 1), load(0)])

        @pl.when(step < 3)
        def _():
            start([w_load(7 + 2 * step), w_load(6 + 2 * step)])

        @pl.when(step == 1)
        def _():
            load(3).start()

        @pl.when(step == 2)
        def _():
            w_load(3).start()

        @pl.when(step == 3)
        def _():
            start([load(12), w_load(0), w_load(1), w_load(2)])

        for half in range(2):
            rows = slice(ROWS * half, ROWS * half + ROWS)
            back = dot_back(down_then_branch[rows, :], weight(5 + 2 * step))
            up_low = (back * slope_then_query[rows, :].astype(jnp.float32)).astype(jnp.bfloat16)
            up_then_key[rows, :] = up_low
            vec_now[0, pl.ds(3 + step, 1), :] += columns_total(up_low.astype(jnp.float32))

        @pl.when(step < 3)
        def _():
            tile_load(step + 1, 0).start()

        w_load(4 + 2 * step).wait()

        @pl.when(step == 0)
        def _():
            load(2).wait()
            load(0).wait()

        for half in range(2):
            rows = slice(ROWS * half, ROWS * half + ROWS)
            acc[rows, :] = acc[rows, :] + dot_back(up_then_key[rows, :], weight(4 + 2 * step))

    serve(range(1, 8, 2))

    @pl.when(step < 4)
    def _():
        tile_load(step, 1).wait()
        by_down = dot(active_then_ctx[...], down_then_branch[...]).astype(jnp.bfloat16)
        w_part[5 + 2 * step] = by_down.reshape(2, 2, 2, PIECE, 8 * PIECE)

        @pl.when(step < 3)
        def _():
            tile_load(step + 1, 1).start()

        by_up = dot(hidden_then_x[...], up_then_key[...]).astype(jnp.bfloat16)
        w_part[4 + 2 * step] = by_up.reshape(2, 2, 2, PIECE, 8 * PIECE)

    @pl.when(step == 3)
    def _():
        start([load(8), load(9)])
        load(3).wait()
        w_load(3).wait()
        for half in range(2):
            rows = slice(ROWS * half, ROWS * half + ROWS)
            grad_hidden, hat = acc[rows, :], hat_ref[rows, :].astype(jnp.float32)
            vec_now[0, 10:11, :] += columns_total(grad_hidden * hat)
            vec_now[0, 8:9, :] += columns_total(grad_hidden)
            first = normalize_back(grad_hidden * gain_ref[0:1, :], hat, inverse_ref[rows, :])
            acc[rows, :] = first
            branch_low = first.astype(jnp.bfloat16)
            down_then_branch[rows, :] = branch_low
            vec_now[0, 2:3, :] += columns_total(branch_low.astype(jnp.float32))
            grad_ctx_ref[rows, :] = dot_back(branch_low, weight(3)).astype(jnp.bfloat16)

    serve(range(8, 20))

    here = pl.ds(pl.multiple_of(block * ROWS, ROWS), ROWS)
    quad_cols = pl.ds(pl.multiple_of(quad * 256, 256), 256)

    @pl.when(step == 4)
    def _():
        load(12).wait()
        for at in range(3):
            w_load(at).wait()

    pair_cols = pl.ds(pl.multiple_of(quad * 256 + pair * 128, 128), 128)
    grad_bufs = (slope_then_query, up_then_key, value_buf)

    @pl.when(step >= 4)
    def _():
        grads = attend_back_pair(
            grad_ctx_ref[here, pair_cols],
            ctx_ref[here, pair_cols],
            p_ref.at[0],
            q_ref[...],
            k_ref[...],
            v_ref[...],
        )
        for buf, grad in zip(grad_bufs, grads):
            buf[here, pair_cols] = grad
        vec_now[0, 0:1, pair_cols] += columns_total(grads[0].astype(jnp.float32))
        vec_now[0, 1:2, pair_cols] += columns_total(grads[2].astype(jnp.float32))

    @pl.when(step == 7)
    def _():
        load(8).wait()
        load(9).wait()

    @pl.when((step >= 4) & (block == 1) & (pair == 1))
    def _():
        for tile in range(4):
            if tile < 3:
                value = dot(hidden_then_x[...], grad_bufs[tile][:, quad_cols])
            else:
                value = dot(active_then_ctx[...], down_then_branch[:, quad_cols])
            value = value.astype(jnp.bfloat16).reshape(2, 2, 2, PIECE, 256)
            part[tile, :, :, :, :, quad_cols] = value


    @pl.when(step == 15)
    def _():
        start(vec_copies(0))
        for name, number in BACK_PLAN[-1]:
            actions[name](number)
        arrive(vec_copies(3))
        summed = jnp.zeros(vec_out.shape, jnp.float32)
        for origin in range(4):
            hop = lax.rem(z - origin + 4, 4)
            summed = summed + jnp.where(hop == 0, vec_now[3], vec_in[2 + jnp.maximum(hop, 1)])
        vec_out[...] = summed
        for batch in range(7):
            for copy in [core_copy(batch)] + far_copies(batch) + mid_copies(batch):
                copy.wait_send()

            @pl.when(is_end)
            def _():
                z_copy(batch, 0).wait_send()

            @pl.when(is_middle)
            def _():
                z_copy(batch, 1).wait_send()
                z_copy(batch, 2).wait_send()

        for stage in range(4):
            for copy in vec_copies(stage):
                copy.wait_send()
        input_store().wait()
        for third in range(3):
            keep_copy(third).wait()
            most = outbox.at[third, pl.ds(0, 2 * PLANE - 2)]
            pltpu.make_async_copy(most, most, out_recv.at[third]).wait()
            pltpu.make_async_copy(most, most, out_send.at[third]).wait()


def backward_and_reduced(
    owners,
    probs,
    query,
    keyed,
    valued,
    inverse,
    gain,
    late_sums,
    context,
    x_turned,
    ctx_turned,
    hidden,
    active,
    slope,
    grad_down,
    grad_second,
    hat,
    weights,
):
    tokens, width = grad_down.shape
    low, high = jnp.bfloat16, jnp.float32
    shaped = jax.ShapeDtypeStruct
    smem = pl.BlockSpec(memory_space=pltpu.SMEM)
    any_space = pl.BlockSpec(memory_space=pl.ANY)
    dma = pltpu.SemaphoreType.DMA
    once = pl.Buffered(1)

    def at(step):
        inner = jnp.maximum(step - 4, 0)
        return lax.rem(inner, 4) // 2, inner // 4 * 2 + lax.rem(inner, 2)

    pair = pl.BlockSpec((ROWS, 128), at)
    sums = pl.BlockSpec((16, width), lambda i: (0, 0))
    cut = (2, 2, 2, PIECE, width)
    input_grad, slot_grads, vector_sums = pl.pallas_call(
        backward_and_reduce,
        grid=(16,),
        out_shape=(
            shaped((tokens, width), high),
            shaped((SLOTS,) + cut, low),
            shaped((16, width), high),
        ),
        in_specs=[smem, pl.BlockSpec((1, 2, ROWS, ROWS), lambda i: (*at(i), 0, 0))]
        + [pair] * 3
        + [
            pl.BlockSpec((tokens, 1), lambda i: (0, 0), pipeline_mode=once),
            pl.BlockSpec(gain.shape, lambda i: (0, 0)),
            sums,
        ]
        + [any_space] * 10,
        out_specs=(any_space, any_space, sums),
        scratch_shapes=[
            pltpu.VMEM((TILES,) + cut, low),
            pltpu.VMEM((tokens, width), high),
            pltpu.VMEM((width, tokens), low),
            pltpu.VMEM((width, tokens), low),
            pltpu.VMEM((tokens, width), low),
            pltpu.VMEM((tokens, width), low),
            pltpu.VMEM((tokens, width), low),
            pltpu.VMEM((tokens, width), low),
            pltpu.VMEM((tokens, width), low),
            pltpu.VMEM((tokens, width), low),
            pltpu.VMEM((tokens, width), low),
            pltpu.VMEM((4,) + cut, low),
            pltpu.VMEM((TILES,) + cut[1:], low),
            pltpu.VMEM((TILES,) + cut[2:], low),
            pltpu.VMEM((TILES,) + cut[3:], low),
            pltpu.VMEM((TILES,) + cut[3:], low),
            pltpu.VMEM((TILES,) + cut[3:], low),
            pltpu.VMEM((TILES,) + cut[3:], low),
            pltpu.VMEM((TILES, PIECE, 256), low),
            pltpu.VMEM((3, 2 * PLANE, PIECE, 256), low),
            pltpu.VMEM((4, 16, width), high),
            pltpu.VMEM((6, 16, width), high),
            pltpu.SMEM((2 * PLANE,), jnp.int32),
            pltpu.SMEM((2 * PLANE,), jnp.int32),
            dma((13,)),
            dma((TILES,)),
            dma((7,)),
            dma((7,)),
            dma((7, 2)),
            dma((7, 2)),
            dma((7, 2)),
            dma((7, 2)),
            dma((3, 7)),
            dma((3, 7)),
            dma((6,)),
            dma((6,)),
            dma((3,)),
            dma((3,)),
        ],
        compiler_params=pltpu.CompilerParams(
            collective_id=1, has_side_effects=True, vmem_limit_bytes=63 * 2**20
        ),
        name="backward_and_reduce",
    )(
        owners,
        probs,
        query,
        keyed,
        valued,
        inverse,
        gain,
        late_sums,
        context,
        x_turned,
        ctx_turned,
        hidden,
        active,
        slope,
        grad_down,
        grad_second,
        hat,
        weights,
    )
    return input_grad, slot_grads.reshape(SLOTS, width, width), vector_sums


def collected_tiles(tile_low, owners, slots):
    mine = owners == lax.axis_index("dp")
    local = jnp.where(mine[:, None, None], tile_low[slots], jnp.zeros((), tile_low.dtype))
    return lax.psum(local, "dp")


def summed_over_slice(parts, vector_terms, owners, slots):
    myself = lax.axis_index("dp")

    def add(held, items):
        part, owner, slot = items
        total = lax.psum(part.astype(jnp.float32), "dp")
        here = (owner == myself) & (slot == jnp.arange(SLOTS, dtype=jnp.int32))
        return held + jnp.where(here[:, None, None], total[None], 0.0), None

    empty = jnp.zeros((SLOTS,) + parts.shape[1:], jnp.float32)
    return lax.scan(add, empty, (parts, owners, slots))[0], lax.psum(vector_terms, "dp")


def body(
    inputs,
    cotangent,
    counts,
    lengths,
    owners,
    tile_master,
    tile_first,
    tile_second,
    tile_ema,
    bias_vals,
    gain_vals,
    vector_first,
    vector_second,
    vector_ema,
):
    tokens = inputs.shape[0]
    small = lax.axis_size("dp") == GROUP
    gain_scale = float(tokens * lax.axis_size("dp")) ** (-0.5)
    if small:
        (
            query,
            keyed,
            valued,
            probs,
            context,
            x_turned,
            ctx_turned,
            hidden,
            active,
            slope,
            grad_down,
            mixed,
            grad_second,
            hat,
            weights,
            inverse,
            late_sums,
        ) = gathered_and_forwarded(
            counts,
            lengths,
            owners,
            bias_vals,
            gain_vals,
            inputs,
            cotangent,
            tile_master,
        )
        input_grad, slot_grads, full_sums = backward_and_reduced(
            owners,
            probs,
            query,
            keyed,
            valued,
            inverse,
            gain_vals,
            late_sums,
            context,
            x_turned,
            ctx_turned,
            hidden,
            active,
            slope,
            grad_down,
            grad_second,
            hat,
            weights,
        )
    else:
        slots = tile_slots(owners)
        vectors = jnp.concatenate([bias_vals, gain_vals], 0)
        weights = collected_tiles(tile_master[0].astype(jnp.bfloat16), owners, slots)
        query, keyed, valued, probs, context, hat, inverse = attended(
            counts, lengths, inputs, weights, vectors
        )
        mixed, grad_first, grad_branch, grad_context, up_grads, down_grads, late_sums = fed_forward_both(
            counts, lengths, hat, inverse, cotangent, weights, vectors
        )
        input_grad, early_grads, early_sums = attended_back(
            probs, query, keyed, valued, inputs, context, grad_context, grad_branch, grad_first, weights
        )
        parts = jnp.concatenate([early_grads, up_grads, down_grads], 0)
        slot_grads, full_sums = summed_over_slice(parts, late_sums + early_sums, owners, slots)
    return updated(
        gain_scale,
        slot_grads,
        tile_master,
        tile_first,
        tile_second,
        tile_ema,
        full_sums,
        bias_vals,
        gain_vals,
        vector_first,
        vector_second,
        vector_ema,
        mixed,
        input_grad,
    )


def solution(mesh):
    placed = (
        P("dp", None),
        P("dp", None),
        P("dp", None),
        P("dp", None),
        P(),
        P("dp", None, None, None),
        P("dp", None, None, None),
        P("dp", None, None, None),
        P("dp", None, None, None),
        P(),
        P(),
        P(),
        P(),
        P(),
    )
    return jax.shard_map(
        body,
        mesh=mesh,
        in_specs=placed,
        out_specs=(
            P("dp", None),
            P("dp", None),
            P("dp", None, None, None),
            P("dp", None, None, None),
            P("dp", None, None, None),
            P("dp", None, None, None),
            P("dp", None, None, None),
            P(),
            P(),
            P(),
            P(),
        ),
        check_vma=False,
    )
```

```python
import functools

import jax
import jax.numpy as jnp
from jax import lax
from jax.experimental import pallas as pl
from jax.experimental.pallas import tpu as pltpu
from jax.sharding import PartitionSpec as P

HEADS = 12
BUCKET = 128
SLOTS = 2
TILES = 12
VROWS = 12
STEP = 5

norm_epsilon = 1e-12
tile_rate = 0.03
vector_rate = 0.2
first_decay = 0.5
second_decay = 0.5
adam_epsilon = 1e-08
weight_decay = 0.01
average_rate = 0.9


def tile_slots(owners):
    order = jnp.arange(owners.shape[0], dtype=jnp.int32)
    same = owners[:, None] == owners[None, :]
    earlier = order[None, :] < order[:, None]
    return jnp.sum((same & earlier).astype(jnp.int32), 1)


def adam_update(param, grad, first, second, rate):
    first_new = first_decay * first + (1.0 - first_decay) * grad
    second_new = second_decay * second + (1.0 - second_decay) * grad * grad
    first_hat = first_new / (1.0 - first_decay**STEP)
    second_hat = second_new / (1.0 - second_decay**STEP)
    param_new = param - rate * (
        first_hat / (jnp.sqrt(second_hat) + adam_epsilon) + weight_decay * param
    )
    return (param_new, first_new, second_new)


ROWS = 4 * BUCKET
TAIL_RATE = 0.28
TAIL_SERIES = (
    0.11615256574707405,
    0.06981038475559553,
    0.2631359597579608,
    -0.22983675561378278,
    0.38546775012288165,
    -0.10472989053809521,
)
INV_SQRT_TAU = 0.3989422804014327
ALLOWED = 3.0e38
BARRED = -1000000000.0


def dot(left, right):
    return jnp.dot(left, right, preferred_element_type=jnp.float32)


def dot_back(left, right):
    return lax.dot_general(
        left, right, (((1,), (1,)), ((), ())), preferred_element_type=jnp.float32
    )


def outer(left, right):
    return lax.dot_general(
        left, right, (((0,), (0,)), ((), ())), preferred_element_type=jnp.float32
    )


def passage_facts(counts, lengths, position):
    places = lengths.shape[1]
    big_end = counts[0, 0]
    mid_end = big_end + counts[0, 1]
    all_end = mid_end + counts[0, 2]
    start = jnp.int32(0)
    member = jnp.zeros(position.shape, jnp.int32)
    usable = jnp.zeros(position.shape, jnp.int32)
    for number in range(places):
        size = jnp.where(
            number < big_end,
            4 * BUCKET,
            jnp.where(number < mid_end, 2 * BUCKET, jnp.where(number < all_end, BUCKET, 0)),
        )
        inside = (position >= start) & (position < start + size)
        live = inside & (position < start + lengths[0, number])
        member = jnp.where(inside, number + 1, member)
        usable = jnp.where(live, 1, usable)
        start = start + size
    passage = jnp.where(member > 0, member - 1, places + position // BUCKET)
    return usable, passage


def normalize(values):
    center = jnp.mean(values, -1, keepdims=True)
    centered = values - center
    spread = jnp.mean(centered * centered, -1, keepdims=True)
    inverse = lax.rsqrt(spread + norm_epsilon)
    return centered * inverse, inverse


def normalize_back(grad, hat, inverse):
    center = jnp.mean(grad, -1, keepdims=True)
    along = jnp.mean(grad * hat, -1, keepdims=True)
    return inverse * (grad - center - hat * along)


def columns_total(values):
    return jnp.sum(values, 0, keepdims=True)


def attention_caps(counts, lengths, block):
    at_row = lax.broadcasted_iota(jnp.int32, (ROWS, 1), 0) + block * ROWS
    at_column = lax.broadcasted_iota(jnp.int32, (1, ROWS), 1) + block * ROWS
    _, passage_row = passage_facts(counts, lengths, at_row)
    usable_column, passage_column = passage_facts(counts, lengths, at_column)
    allowed = (passage_row == passage_column) & ((usable_column == 1) | (at_row == at_column))
    return jnp.where(allowed, ALLOWED, BARRED)


def attend_quad(quad, weight, x_ref, vec_ref, cap_ref, q_ref, k_ref, v_ref, p_ref, ctx_ref):
    cols = pl.ds(pl.multiple_of(quad * 256, 256), 256)
    x = x_ref[...]
    query = (dot(x, weight(0, cols)) + vec_ref[0:1, cols]).astype(jnp.bfloat16)
    query = query * jnp.bfloat16(0.125)
    keyed = dot(x, weight(1, cols)).astype(jnp.bfloat16)
    valued = (dot(x, weight(2, cols)) + vec_ref[1:2, cols]).astype(jnp.bfloat16)
    q_ref[...] = query
    k_ref[...] = keyed
    v_ref[...] = valued
    low_half = lax.broadcasted_iota(jnp.int32, (1, 128), 1) < 64
    for pair in range(2):
        part = slice(128 * pair, 128 * pair + 128)
        contexts = []
        for head in range(2):
            here = low_half if head == 0 else ~low_half
            mine = jnp.where(here, query[:, part], jnp.zeros_like(query[:, part]))
            scores = jnp.minimum(dot_back(mine, keyed[:, part]), cap_ref[...])
            exponent = jnp.exp(scores - jnp.max(scores, -1, keepdims=True))
            inverse = 1.0 / jnp.sum(exponent, -1, keepdims=True)
            probability = (exponent * inverse).astype(jnp.bfloat16)
            p_ref[0, 2 * pair + head] = probability
            contexts.append(dot(probability, valued[:, part]))
        both = jnp.where(low_half, contexts[0], contexts[1]).astype(jnp.bfloat16)
        ctx_ref[:, pl.ds(pl.multiple_of(quad * 256 + 128 * pair, 128), 128)] = both


def close_block(w_out, x_ref, vec_ref, ctx_ref, hat_ref, inverse_ref):
    branch = dot(ctx_ref[...], w_out) + vec_ref[2:3, :]
    hat_ref[...], inverse_ref[...] = normalize(x_ref[...].astype(jnp.float32) + branch)


def attend_back_pair(pull, level_from, p_ref, query, keyed, valued):
    low_half = lax.broadcasted_iota(jnp.int32, (1, 128), 1) < 64
    along = pull.astype(jnp.float32) * level_from.astype(jnp.float32)
    by_query, by_key, by_value = [], [], []
    for head in range(2):
        mask = low_half if head == 0 else ~low_half
        mine = jnp.where(mask, pull, jnp.zeros_like(pull))
        level = jnp.sum(jnp.where(mask, along, 0.0), -1, keepdims=True)
        probability = p_ref[head]
        grad_prob = dot_back(mine, valued)
        grad_scores = (probability.astype(jnp.float32) * (grad_prob - level)).astype(jnp.bfloat16)
        by_query.append(dot(grad_scores, keyed))
        by_key.append(outer(grad_scores, query))
        by_value.append(outer(probability, pull))
    grad_query = jnp.where(low_half, by_query[0], by_query[1]) * 0.125
    grad_key = jnp.where(low_half, by_key[0], by_key[1])
    grad_value = jnp.where(low_half, by_value[0], by_value[1])
    return [value.astype(jnp.bfloat16) for value in (grad_query, grad_key, grad_value)]


def gelu_parts(up):
    near = 1.0 / (1.0 + TAIL_RATE * jnp.abs(up))
    decay = jnp.exp(up * up * -0.5)
    series = jnp.full_like(near, TAIL_SERIES[-1])
    for term in TAIL_SERIES[-2::-1]:
        series = series * near + term
    tail = series * near * decay
    share = jnp.where(up < 0.0, tail, 1.0 - tail)
    slope = share + up * (decay * INV_SQRT_TAU)
    return (up * share).astype(jnp.bfloat16), slope


def attend_forward(
    counts,
    lengths,
    x_ref,
    w_hbm,
    vec_ref,
    q_ref,
    k_ref,
    v_ref,
    p_ref,
    ctx_ref,
    hat_ref,
    inverse_ref,
    w_buf,
    cap_ref,
    w_sem,
):
    block, quad = pl.program_id(0), pl.program_id(1)
    loads = [pltpu.make_async_copy(w_hbm.at[at], w_buf.at[at], w_sem.at[at]) for at in range(4)]

    @pl.when((block == 0) & (quad == 0))
    def _():
        for load in loads:
            load.start()
        for load in loads:
            load.wait()

    @pl.when(quad == 0)
    def _():
        cap_ref[...] = attention_caps(counts, lengths, block)

    def weight(at, cols):
        return w_buf[at, :, cols]

    attend_quad(quad, weight, x_ref, vec_ref, cap_ref, q_ref, k_ref, v_ref, p_ref, ctx_ref)

    @pl.when(quad == 2)
    def _():
        close_block(w_buf[3], x_ref, vec_ref, ctx_ref, hat_ref, inverse_ref)


def attended(counts, lengths, x, weights, vectors):
    tokens, width = x.shape
    blocks = tokens // ROWS
    low = jnp.bfloat16
    smem = pl.BlockSpec(memory_space=pltpu.SMEM)
    quad = pl.BlockSpec((ROWS, 256), lambda b, h: (b, h))
    rows = pl.BlockSpec((ROWS, width), lambda b, h: (b, 0))
    shaped = jax.ShapeDtypeStruct
    return pl.pallas_call(
        attend_forward,
        grid=(blocks, 3),
        out_shape=(
            shaped((tokens, width), low),
            shaped((tokens, width), low),
            shaped((tokens, width), low),
            shaped((blocks, HEADS, ROWS, ROWS), low),
            shaped((tokens, width), low),
            shaped((tokens, width), jnp.float32),
            shaped((tokens, 1), jnp.float32),
        ),
        in_specs=[
            smem,
            smem,
            rows,
            pl.BlockSpec(memory_space=pl.ANY),
            pl.BlockSpec((VROWS, width), lambda b, h: (0, 0)),
        ],
        out_specs=(
            quad,
            quad,
            quad,
            pl.BlockSpec((1, 4, ROWS, ROWS), lambda b, h: (b, h, 0, 0)),
            rows,
            rows,
            pl.BlockSpec((ROWS, 1), lambda b, h: (b, 0)),
        ),
        scratch_shapes=[
            pltpu.VMEM((4, width, width), low),
            pltpu.VMEM((ROWS, ROWS), jnp.float32),
            pltpu.SemaphoreType.DMA((4,)),
        ],
        compiler_params=pltpu.CompilerParams(vmem_limit_bytes=56 * 2**20),
        name="attend_forward",
    )(counts, lengths, x, weights, vectors)


def feed_forward_both(
    counts,
    lengths,
    hat_ref,
    inverse_ref,
    cot_ref,
    w_hbm,
    vec_ref,
    mixed_ref,
    first_ref,
    branch_ref,
    context_ref,
    up_grad_ref,
    down_grad_ref,
    sum_ref,
    w_buf,
    active_ref,
    up_ref,
    hidden_ref,
    down_ref,
    slope_ref,
    w_sem,
):
    step = pl.program_id(0)
    blocks = pl.num_programs(0) - 4
    loads = [
        pltpu.make_async_copy(w_hbm.at[3 + at], w_buf.at[at], w_sem.at[at]) for at in range(9)
    ]

    @pl.when(step == 0)
    def _():
        for load in loads[1:] + loads[:1]:
            load.start()
        sum_ref[...] = jnp.zeros_like(sum_ref)
        for load in loads[1:] + loads[:1]:
            load.wait()

    @pl.when(step < blocks)
    def _():
        here = pl.ds(pl.multiple_of(step * ROWS, ROWS), ROWS)
        at_row = lax.broadcasted_iota(jnp.int32, (ROWS, 1), 0) + step * ROWS
        live = passage_facts(counts, lengths, at_row)[0].astype(jnp.float32)
        hat = hat_ref[...]
        hidden = hat * vec_ref[10:11, :] + vec_ref[8:9, :]
        hidden_low = hidden.astype(jnp.bfloat16)
        hidden_ref[here, :] = hidden_low
        total = hidden + vec_ref[7:8, :]
        for tile in range(4):
            up = dot(hidden_low, w_buf[1 + tile]) + vec_ref[3 + tile : 4 + tile, :]
            active, slope = gelu_parts(up)
            slope_ref[tile] = slope.astype(jnp.bfloat16)
            active_ref[tile, here, :] = active
            total = total + dot(active, w_buf[5 + tile])
        hat_two, inverse_two = normalize(total)
        mixed_ref[...] = ((hat_two * vec_ref[11:12, :] + vec_ref[9:10, :]) * live).astype(jnp.bfloat16)
        grad_out = cot_ref[...].astype(jnp.float32) * live
        sum_ref[11:12, :] += columns_total(grad_out * hat_two)
        sum_ref[9:10, :] += columns_total(grad_out)
        second = normalize_back(grad_out * vec_ref[11:12, :], hat_two, inverse_two)
        down_low = second.astype(jnp.bfloat16)
        down_ref[here, :] = down_low
        sum_ref[7:8, :] += columns_total(down_low.astype(jnp.float32))
        grad_hidden = second
        for tile in range(4):
            pulled = dot_back(down_low, w_buf[5 + tile])
            up_low = (pulled * slope_ref[tile].astype(jnp.float32)).astype(jnp.bfloat16)
            up_ref[tile, here, :] = up_low
            sum_ref[3 + tile : 4 + tile, :] += columns_total(up_low.astype(jnp.float32))
            grad_hidden = grad_hidden + dot_back(up_low, w_buf[1 + tile])
        sum_ref[10:11, :] += columns_total(grad_hidden * hat)
        sum_ref[8:9, :] += columns_total(grad_hidden)
        grad_first = normalize_back(grad_hidden * vec_ref[10:11, :], hat, inverse_ref[...])
        first_ref[...] = grad_first
        branch_low = grad_first.astype(jnp.bfloat16)
        branch_ref[...] = branch_low
        sum_ref[2:3, :] += columns_total(branch_low.astype(jnp.float32))
        context_ref[...] = dot_back(branch_low, w_buf[0]).astype(jnp.bfloat16)

    @pl.when(step >= blocks)
    def _():
        tile = step - blocks
        up_grad_ref[0] = outer(hidden_ref[...], up_ref[tile]).astype(jnp.bfloat16)
        down_grad_ref[0] = outer(active_ref[tile], down_ref[...]).astype(jnp.bfloat16)


def fed_forward_both(counts, lengths, hat, inverse, cotangent, weights, vectors):
    tokens, width = hat.shape
    blocks = tokens // ROWS
    low = jnp.bfloat16
    smem = pl.BlockSpec(memory_space=pltpu.SMEM)
    shaped = jax.ShapeDtypeStruct

    def block_of(step):
        return jnp.minimum(step, blocks - 1)

    def tile_of(step):
        return jnp.maximum(step - blocks, 0)

    rows = pl.BlockSpec((ROWS, width), lambda i: (block_of(i), 0))
    tile = pl.BlockSpec((1, width, width), lambda i: (tile_of(i), 0, 0))
    return pl.pallas_call(
        feed_forward_both,
        grid=(blocks + 4,),
        out_shape=(
            shaped((tokens, width), low),
            shaped((tokens, width), jnp.float32),
            shaped((tokens, width), low),
            shaped((tokens, width), low),
            shaped((4, width, width), low),
            shaped((4, width, width), low),
            shaped((16, width), jnp.float32),
        ),
        in_specs=[
            smem,
            smem,
            rows,
            pl.BlockSpec((ROWS, 1), lambda i: (block_of(i), 0)),
            rows,
            pl.BlockSpec(memory_space=pl.ANY),
            pl.BlockSpec((VROWS, width), lambda i: (0, 0)),
        ],
        out_specs=(
            rows,
            rows,
            rows,
            rows,
            tile,
            tile,
            pl.BlockSpec((16, width), lambda i: (0, 0)),
        ),
        scratch_shapes=[
            pltpu.VMEM((9, width, width), low),
            pltpu.VMEM((4, tokens, width), low),
            pltpu.VMEM((4, tokens, width), low),
            pltpu.VMEM((tokens, width), low),
            pltpu.VMEM((tokens, width), low),
            pltpu.VMEM((4, ROWS, width), low),
            pltpu.SemaphoreType.DMA((9,)),
        ],
        compiler_params=pltpu.CompilerParams(vmem_limit_bytes=60 * 2**20),
        name="feed_forward_both",
    )(counts, lengths, hat, inverse, cotangent, weights, vectors)


def attend_backward(
    p_ref,
    q_ref,
    k_ref,
    v_ref,
    x_ref,
    ctx_ref,
    grad_ctx_ref,
    branch_ref,
    first_ref,
    w_ref,
    input_ref,
    grad_ref,
    sum_ref,
    pulled,
):
    step = pl.program_id(0)
    quad, block = step // 2, lax.rem(step, 2)
    here = pl.ds(pl.multiple_of(block * ROWS, ROWS), ROWS)
    cols = pl.ds(pl.multiple_of(quad * 256, 256), 256)

    @pl.when(step == 0)
    def _():
        sum_ref[...] = jnp.zeros_like(sum_ref)
        input_ref[...] = first_ref[...]

    for pair in range(2):
        half = slice(128 * pair, 128 * pair + 128)
        at = pl.ds(pl.multiple_of(quad * 256 + 128 * pair, 128), 128)
        heads = p_ref.at[0, pl.ds(2 * pair, 2)]
        grads = attend_back_pair(
            grad_ctx_ref[here, at], ctx_ref[here, at], heads, q_ref[:, half], k_ref[:, half], v_ref[:, half]
        )
        for number, grad in enumerate(grads):
            pulled[number, here, half] = grad
        sum_ref[0:1, at] += columns_total(grads[0].astype(jnp.float32))
        sum_ref[1:2, at] += columns_total(grads[2].astype(jnp.float32))

    more = input_ref[here, :]
    for at in range(3):
        more = more + dot_back(pulled[at, here, :], w_ref[at, :, cols])
    input_ref[here, :] = more

    @pl.when(block == 1)
    def _():
        for tile in range(3):
            grad_ref[tile, :, cols] = outer(x_ref[...], pulled[tile]).astype(jnp.bfloat16)
        grad_ref[3, :, cols] = outer(ctx_ref[...], branch_ref[:, cols]).astype(jnp.bfloat16)


def attended_back(probs, query, keyed, valued, x, context, grad_context, grad_branch, grad_first, weights):
    tokens, width = x.shape
    low = jnp.bfloat16
    shaped = jax.ShapeDtypeStruct
    once = pl.Buffered(1)
    quad = pl.BlockSpec((ROWS, 256), lambda i: (lax.rem(i, 2), i // 2))
    whole = pl.BlockSpec((tokens, width), lambda i: (0, 0), pipeline_mode=once)
    return pl.pallas_call(
        attend_backward,
        grid=(6,),
        out_shape=(
            shaped((tokens, width), jnp.float32),
            shaped((4, width, width), low),
            shaped((16, width), jnp.float32),
        ),
        in_specs=[
            pl.BlockSpec((1, 4, ROWS, ROWS), lambda i: (lax.rem(i, 2), i // 2, 0, 0)),
            quad,
            quad,
            quad,
            whole,
            whole,
            whole,
            whole,
            whole,
            pl.BlockSpec((3, width, width), lambda i: (0, 0, 0), pipeline_mode=once),
        ],
        out_specs=(
            whole,
            pl.BlockSpec((4, width, width), lambda i: (0, 0, 0), pipeline_mode=once),
            pl.BlockSpec((16, width), lambda i: (0, 0)),
        ),
        scratch_shapes=[pltpu.VMEM((3, tokens, 256), low)],
        compiler_params=pltpu.CompilerParams(vmem_limit_bytes=56 * 2**20),
        name="attend_backward",
    )(probs, query, keyed, valued, x, context, grad_context, grad_branch, grad_first, weights)


def moved(param, grad, first, second, average, rate):
    param_new, first_new, second_new = adam_update(param, grad, first, second, rate)
    return param_new, first_new, second_new, average_rate * average + (1.0 - average_rate) * param_new


def update_kernel(
    gain_scale,
    vec_grad_ref,
    bias_ref,
    gain_ref,
    vec_first_ref,
    vec_second_ref,
    vec_ema_ref,
    grad_hbm,
    master_hbm,
    first_hbm,
    second_hbm,
    ema_hbm,
    mixed_hbm,
    input_hbm,
    vec_out,
    vec_first_out,
    vec_second_out,
    vec_ema_out,
    master_out,
    first_out,
    second_out,
    ema_out,
    copy_out,
    mixed_out,
    input_out,
    vec_ref,
    grad_buf,
    master_buf,
    first_buf,
    second_buf,
    ema_buf,
    mixed_buf,
    input_buf,
    load_sem,
    store_sem,
    pass_sem,
):
    rows = master_buf.shape[0]
    chunks = load_sem.shape[0]
    bufs = (grad_buf, master_buf, first_buf, second_buf, ema_buf)
    sources = (grad_hbm, master_hbm, first_hbm, second_hbm, ema_hbm)
    targets = (copy_out, master_out, first_out, second_out, ema_out)

    def part(at):
        return pl.ds(at * (rows // chunks), rows // chunks)

    def loads(at):
        return [
            pltpu.make_async_copy(src.at[part(at)], buf.at[part(at)], load_sem.at[at, n])
            for n, (src, buf) in enumerate(zip(sources, bufs))
        ]

    def stores(at):
        return [
            pltpu.make_async_copy(buf.at[part(at)], dst.at[part(at)], store_sem.at[at, n])
            for n, (dst, buf) in enumerate(zip(targets, bufs))
        ]

    def passing(at, way):
        stops = ((mixed_hbm, mixed_buf, mixed_out), (input_hbm, input_buf, input_out))[at]
        return pltpu.make_async_copy(stops[way], stops[way + 1], pass_sem.at[at, way])

    for at in range(2):
        for load in loads(at):
            load.start()
    vec_ref[0:10, :] = bias_ref[...]
    vec_ref[10:12, :] = gain_ref[...]
    vec_grad = vec_grad_ref[0:VROWS, :] * gain_scale
    vec_out[...], vec_first_out[...], vec_second_out[...], vec_ema_out[...] = moved(
        vec_ref[...], vec_grad, vec_first_ref[...], vec_second_ref[...], vec_ema_ref[...], vector_rate
    )
    for at in range(chunks):
        if at + 2 < chunks:
            for load in loads(at + 2):
                load.start()
        else:
            passing(at + 2 - chunks, 0).start()
        for load in loads(at):
            load.wait()
        here = part(at)
        grad = grad_buf[here, :].astype(jnp.float32) * gain_scale
        result = moved(
            master_buf[here, :], grad, first_buf[here, :], second_buf[here, :], ema_buf[here, :], tile_rate
        )
        master_buf[here, :], first_buf[here, :], second_buf[here, :], ema_buf[here, :] = result
        grad_buf[here, :] = result[0].astype(jnp.bfloat16)
        for store in stores(at):
            store.start()
    for at in range(2):
        passing(at, 0).wait()
        passing(at, 1).start()
    for at in range(chunks):
        for store in stores(at):
            store.wait()
    for at in range(2):
        passing(at, 1).wait()


def updated(
    gain_scale,
    slot_grads,
    master,
    first,
    second,
    ema,
    vec_grad,
    bias,
    gain,
    vec_first,
    vec_second,
    vec_ema,
    mixed,
    input_grad,
):
    width = master.shape[-1]
    rows, chunks = SLOTS * width, 8
    low, high = jnp.bfloat16, jnp.float32
    any_space = pl.BlockSpec(memory_space=pl.ANY)
    vmem = pl.BlockSpec(memory_space=pltpu.VMEM)
    shaped = jax.ShapeDtypeStruct
    dma = pltpu.SemaphoreType.DMA
    results = pl.pallas_call(
        functools.partial(update_kernel, gain_scale),
        out_shape=(shaped((VROWS, width), high),) * 4
        + (shaped((rows, width), high),) * 4
        + (shaped((rows, width), low),)
        + (shaped(mixed.shape, mixed.dtype), shaped(input_grad.shape, input_grad.dtype)),
        in_specs=[vmem] * 6 + [any_space] * 7,
        out_specs=(vmem,) * 4 + (any_space,) * 7,
        scratch_shapes=[
            pltpu.VMEM((VROWS, width), high),
            pltpu.VMEM((rows, width), low),
            pltpu.VMEM((rows, width), high),
            pltpu.VMEM((rows, width), high),
            pltpu.VMEM((rows, width), high),
            pltpu.VMEM((rows, width), high),
            pltpu.VMEM(mixed.shape, mixed.dtype),
            pltpu.VMEM(input_grad.shape, input_grad.dtype),
            dma((chunks, 5)),
            dma((chunks, 5)),
            dma((2, 2)),
        ],
        compiler_params=pltpu.CompilerParams(vmem_limit_bytes=62 * 2**20),
        name="update",
    )(
        vec_grad,
        bias,
        gain,
        vec_first,
        vec_second,
        vec_ema,
        slot_grads.reshape(rows, width),
        *(state.reshape(rows, width) for state in (master, first, second, ema)),
        mixed,
        input_grad,
    )
    tiles = tuple(result.reshape(master.shape) for result in results[4:9])
    return results[9:] + tiles + results[:4]


MESH = pl.DeviceIdType.MESH
GROUP = 32
PAIRS = TILES // 2
PLANE = 8
PIECE = 96
PAIR_TILES = ((0, 1), (2, 3), (4, 8), (5, 9), (6, 10), (7, 11))


def remote(src, dst, send, recv, device):
    return pltpu.make_async_remote_copy(
        src_ref=src, dst_ref=dst, send_sem=send, recv_sem=recv, device_id=(device,), device_id_type=MESH
    )


def place(device):
    core = lax.rem(device, 2)
    x = lax.rem(device // 2, 2)
    y = lax.rem(device // 4, 2)
    z = device // 8
    return z, y, x, core


def start(copies):
    for copy in copies:
        copy.start()


def arrive(copies):
    for copy in copies:
        copy.wait_recv()


def greet(z, in_plane):
    barrier = pltpu.get_barrier_semaphore()
    for hop in range(1, PLANE):
        other = z * PLANE + lax.rem(in_plane + hop, PLANE)
        pl.semaphore_signal(barrier, inc=1, device_id=(other,), device_id_type=MESH)
    for hop in range(1, 4):
        other = lax.rem(z + hop, 4) * PLANE + in_plane
        pl.semaphore_signal(barrier, inc=1, device_id=(other,), device_id_type=MESH)
    pl.semaphore_wait(barrier, PLANE + 2)


def along_z(z, in_plane):
    inner = (1 + z // 2) * PLANE + in_plane
    other_middle = (3 - z) * PLANE + in_plane
    outer_end = lax.rem(lax.rem(z + 3, 4) * 3, 4) * PLANE + in_plane
    return inner, other_middle, outer_end


def third(part):
    return pl.ds(256 * part, 256)


UNITS = [(0, 4, pl.ds(256 * part, 256)) for part in range(3)]
UNITS += [(2 * pair, 2, pl.ds(0, 768)) for pair in range(2, PAIRS)]
Z_PARTS = (pl.ds(0, 512), pl.ds(512, 256))


POSITIONS = [tile for pair in PAIR_TILES for tile in pair]


def slot_number(owners, tile):
    number = jnp.int32(0)
    for earlier in range(tile):
        number = number + jnp.where(owners[earlier] == owners[tile], 1, 0)
    return number

FRONT_PLAN = (
    (
        ("open",),
        ("swap", 0),
        ("sent", 0),
        ("swap", 1),
        ("choose", 0),
        ("end", 0),
        ("sent", 1),
        ("middle", 0),
        ("choose", 1),
        ("end", 1),
        ("swap", 2),
        ("total", 0),
        ("end", 3, 0),
        ("middle", 1),
        ("mid", 0),
        ("choose", 2),
        ("end", 2),
        ("end", 3, 1),
        ("far", 0),
        ("middle", 3, 0),
        ("total", 1),
        ("caps",),
        ("middle", 3, 1),
        ("end", 4, 0),
        ("mid", 1),
        ("near", 0),
        ("total", 3, 0),
        ("end", 5, 0),
        ("middle", 2),
        ("end", 4, 1),
        ("total", 3, 1),
        ("far", 1),
        ("finish", 0),
    ),
    (
        ("middle", 4, 0),
        ("total", 2),
        ("mid", 3),
        ("middle", 4, 1),
        ("end", 5, 1),
    ),
    (
        ("mid", 2),
        ("end", 6, 0),
        ("middle", 5, 0),
        ("near", 1),
        ("total", 4, 1),
        ("far", 3),
        ("finish", 1),
        ("far", 2),
        ("middle", 5, 1),
        ("end", 6, 1),
        ("total", 4, 0),
    ),
    (
        ("total", 5, 0),
        ("middle", 6, 0),
        ("mid", 4),
        ("total", 5, 1),
        ("middle", 6, 1),
    ),
    (
        ("total", 6, 1),
        ("mid", 5),
        ("near", 2),
        ("far", 4),
        ("total", 6, 0),
        ("finish", 2),
        ("keep", 0),
        ("keep", 1),
    ),
    (
        ("mid", 6),
        ("near", 3),
        ("near", 4),
        ("far", 5),
    ),
    (
        ("far", 6),
        ("finish", 4),
        ("keep", 3),
        ("finish", 3),
        ("keep", 2),
    ),
    (
        ("near", 5),
    ),
    (
        ("near", 6),
        ("finish", 5),
        ("keep", 4),
    ),
    (
        ("finish", 6),
        ("keep", 5),
    ),
)


def gather_and_forward(
    counts,
    lengths,
    owners,
    bias_ref,
    gain_ref,
    x_hbm,
    cot_hbm,
    master_hbm,
    q_ref,
    k_ref,
    v_ref,
    p_ref,
    ctx_hbm,
    x_turned_hbm,
    ctx_turned_hbm,
    hidden_hbm,
    active_hbm,
    slope_hbm,
    down_hbm,
    mixed_hbm,
    second_hbm,
    hat_hbm,
    w_out,
    inverse_ref,
    sum_ref,
    vec_ref,
    cap_ref,
    wide,
    low,
    stage_a,
    stage_b,
    stage_c,
    chosen,
    from_end,
    from_middle,
    w_buf,
    x_then_hidden,
    x_turned,
    ctx_turned,
    hidden_turned,
    ctx_ref,
    cot_then_down,
    mixed_ref,
    hat_ref,
    slope_buf,
    active_buf,
    wide_sem,
    load_sem,
    store_sem,
    half_sem,
    tile_sem,
    out_sem,
    swap_send,
    swap_recv,
    z_send,
    z_recv,
    mid_send,
    mid_recv,
    far_send,
    far_recv,
    near_send,
    near_recv,
):
    step = pl.program_id(0)
    width = 8 * PIECE
    me = lax.axis_index("dp")
    z, y, x, core = place(me)
    in_plane = lax.rem(me, PLANE)
    sibling = me + 1 - 2 * core
    x_peer = me + 2 - 4 * x
    y_peer = me + 4 - 8 * y
    z_targets = along_z(z, in_plane)
    stages = (stage_a, stage_b, stage_c)
    is_end = (z == 0) | (z == 3)
    is_middle = (z == 1) | (z == 2)

    def piece_rows(cell_core, cell_x, cell_y):
        return pl.ds(pl.multiple_of(((cell_core * 2 + cell_x) * 2 + cell_y) * PIECE, 16), PIECE)

    def wide_load(part):
        cols = third(part)
        return pltpu.make_async_copy(master_hbm.at[:, cols], wide.at[:, cols], wide_sem.at[part])

    def swap(part):
        wide_load(part).wait()
        for slot in range(SLOTS):
            master = wide[width * slot : width * (slot + 1), third(part)]
            low[slot, :, third(part)] = master.astype(jnp.bfloat16)

        def send(hop, carry):
            target = lax.rem(in_plane + hop, PLANE)
            _, ty, tx, tc = place(target)
            remote(
                low.at[:, piece_rows(tc, tx, ty), third(part)],
                stages[part].at[pl.ds(2 * in_plane, 2)],
                swap_send.at[part],
                swap_recv.at[part],
                z * PLANE + target,
            ).start()
            return carry

        lax.fori_loop(1, PLANE, send, 0)
        stages[part][pl.ds(2 * in_plane, 2)] = low[:, piece_rows(core, x, y), third(part)]
        if part == 0:
            start([load(0), load(1)])

    def swap_wait(part, sem):
        most = stages[part].at[pl.ds(0, 2 * PLANE - 2)]
        pltpu.make_async_copy(most, most, sem.at[part]).wait()

    def z_copy(unit, part, level):
        first, count, cols = UNITS[unit]
        tiles = pl.ds(first, count)
        cols = cols if count == 4 else Z_PARTS[part]
        src = w_buf.at[tiles, core, x, y, :, cols] if level == 2 else chosen.at[tiles, :, cols]
        dst = (from_end.at[tiles, :, cols], from_middle.at[tiles, :, cols], src)[level]
        at = level, unit, part
        return remote(src, dst, z_send.at[at], z_recv.at[at], z_targets[level])

    def z_parts(unit):
        return range(1 if UNITS[unit][1] == 4 else 2)

    def z_end(unit, part=0):
        @pl.when(is_end)
        def _():
            z_copy(unit, part, 0).start()

    def z_rows(unit, part):
        first, count, cols = UNITS[unit]
        return pl.ds(first, count), cols if count == 4 else Z_PARTS[part]

    def z_middle(unit, part=0):
        @pl.when(is_middle)
        def _():
            z_copy(unit, part, 0).wait_recv()
            tiles, cols = z_rows(unit, part)
            chosen[tiles, :, cols] = chosen[tiles, :, cols] + from_end[tiles, :, cols]
            z_copy(unit, part, 1).start()

    def z_total(unit, part=0):
        @pl.when(is_middle)
        def _():
            z_copy(unit, part, 1).wait_recv()
            tiles, cols = z_rows(unit, part)
            w_buf[tiles, core, x, y, :, cols] = chosen[tiles, :, cols] + from_middle[tiles, :, cols]
            z_copy(unit, part, 2).start()

    def mid_copies(unit):
        first, count, cols = UNITS[unit]
        copies = []
        for n, peer in enumerate((y_peer, x_peer)):
            spot = w_buf.at[pl.ds(first + n * count // 2, count // 2), core, x, y, :, cols]
            copies.append(remote(spot, spot, mid_send.at[unit, n], mid_recv.at[unit, n], peer))
        return copies

    def far_copies(unit):
        first, count, cols = UNITS[unit]
        half = count // 2
        by_row = w_buf.at[pl.ds(first, half), core, x, :, :, cols]
        by_column = w_buf.at[pl.ds(first + half, half), core, :, y, :, cols]
        return [
            remote(spot, spot, far_send.at[unit, n], far_recv.at[unit, n], peer)
            for n, (spot, peer) in enumerate(((by_row, x_peer), (by_column, y_peer)))
        ]

    def near_copy(unit):
        first, count, cols = UNITS[unit]
        spot = w_buf.at[pl.ds(first, count), core, :, :, :, cols]
        return remote(spot, spot, near_send.at[unit], near_recv.at[unit], sibling)

    def give_mid(unit):
        @pl.when(is_end)
        def _():
            arrive([z_copy(unit, part, 2) for part in z_parts(unit)])

        start(mid_copies(unit))

    def give_far(unit):
        arrive(mid_copies(unit))
        start(far_copies(unit))

    def give_near(unit):
        arrive(far_copies(unit))
        near_copy(unit).start()

    def finish(unit):
        near_copy(unit).wait_recv()

    def choose(part):
        swap_wait(part, swap_recv)
        for pair in range(PAIRS):
            for n, tile in enumerate(PAIR_TILES[pair]):
                owner = owners[tile]
                value = stages[part][SLOTS * lax.rem(owner, PLANE) + slot_number(owners, tile)]
                chosen[2 * pair + n, :, third(part)] = jnp.where(
                    owner // PLANE == z, value, jnp.zeros_like(value)
                )

    def load(at):
        src = (x_hbm, cot_hbm)[at]
        dst = (x_then_hidden, cot_then_down)[at]
        return pltpu.make_async_copy(src, dst, load_sem.at[at])

    def store(at):
        src, dst = (
            (hidden_turned, hidden_hbm),
            (ctx_ref, ctx_hbm),
            (hat_ref, hat_hbm),
            None,
            None,
            None,
            (x_turned, x_turned_hbm),
            (ctx_turned, ctx_turned_hbm),
        )[at]
        return pltpu.make_async_copy(src, dst, store_sem.at[at])

    def half_stores(half):
        rows = pl.ds(ROWS * half, ROWS)
        pairs = ((cot_then_down, down_hbm), (mixed_ref, mixed_hbm), (wide, second_hbm))
        return [
            pltpu.make_async_copy(src.at[rows], dst.at[rows], half_sem.at[half, at])
            for at, (src, dst) in enumerate(pairs)
        ]

    def w_store(pair):
        two = pl.ds(2 * pair, 2)
        return pltpu.make_async_copy(w_buf.at[two], w_out.at[two], out_sem.at[pair])

    def weight(at, cols=slice(None)):
        value = w_buf[at, :, :, :, :, cols]
        return value.reshape(width, value.shape[-1])

    def open_all():
        start([wide_load(part) for part in range(3)])
        sum_ref[...] = jnp.zeros_like(sum_ref)
        vec_ref[0:10, :] = bias_ref[...]
        vec_ref[10:12, :] = gain_ref[...]
        greet(z, in_plane)

    def make_caps():
        for block in range(2):
            cap_ref[block] = attention_caps(counts, lengths, block)
        load(0).wait()
        x_turned[...] = x_then_hidden[...].T
        store(6).start()

    actions = {
        "open": open_all,
        "caps": make_caps,
        "swap": swap,
        "sent": lambda part: swap_wait(part, swap_send),
        "choose": choose,
        "end": z_end,
        "middle": z_middle,
        "total": z_total,
        "mid": give_mid,
        "far": give_far,
        "near": give_near,
        "finish": finish,
        "keep": lambda pair: w_store(pair).start(),
    }

    for at, work in enumerate(FRONT_PLAN):

        @pl.when(step == at)
        def _():
            for name, *rest in work:
                actions[name](*rest)

    quad, block = step // 2, lax.rem(step, 2)
    here = pl.ds(pl.multiple_of(block * ROWS, ROWS), ROWS)

    @pl.when(step < 6)
    def _():
        attend_quad(
            quad,
            weight,
            x_then_hidden.at[here],
            vec_ref,
            cap_ref.at[block],
            q_ref,
            k_ref,
            v_ref,
            p_ref,
            ctx_ref.at[here],
        )

    @pl.when((step >= 4) & (step < 6))
    def _():
        branch = dot(ctx_ref[here, :], weight(3)) + vec_ref[2:3, :]
        hat, inverse = normalize(x_then_hidden[here, :].astype(jnp.float32) + branch)
        hat_ref[here, :] = hat.astype(jnp.bfloat16)
        inverse_ref[here, :] = inverse
        hidden = hat * vec_ref[10:11, :] + vec_ref[8:9, :]
        hidden_low = hidden.astype(jnp.bfloat16)
        x_then_hidden[here, :] = hidden_low
        hidden_turned[:, here] = hidden_low.T
        ctx_turned[:, here] = ctx_ref[here, :].T
        wide[here, :] = hidden + vec_ref[7:8, :]

    @pl.when(step == 5)
    def _():
        start([store(0), store(1), store(2), store(7)])

    turn = step - 6
    slot = lax.rem(turn, 2)

    def tile_stores(source_slot, tile):
        return [
            pltpu.make_async_copy(src.at[source_slot], dst.at[tile], tile_sem.at[source_slot, at])
            for at, (src, dst) in enumerate(((active_buf, active_hbm), (slope_buf, slope_hbm)))
        ]

    @pl.when(turn >= 2)
    def _():
        for copy in tile_stores(slot, 0):
            copy.wait()

    def feed(tile, half):
        rows = slice(ROWS * half, ROWS * half + ROWS)
        up = dot(x_then_hidden[rows, :], weight(4 + 2 * tile)) + vec_ref[pl.ds(3 + tile, 1), :]
        active, slope = gelu_parts(up)
        slope_buf[slot, rows, :] = slope.astype(jnp.bfloat16)
        active_buf[slot, :, rows] = active.T
        wide[rows, :] = wide[rows, :] + dot(active, weight(5 + 2 * tile))

    def close(half):
        rows = slice(ROWS * half, ROWS * half + ROWS)
        at_row = lax.broadcasted_iota(jnp.int32, (ROWS, 1), 0) + half * ROWS
        live = passage_facts(counts, lengths, at_row)[0].astype(jnp.float32)
        hat, inverse = normalize(wide[rows, :])
        mixed = (hat * vec_ref[11:12, :] + vec_ref[9:10, :]) * live
        mixed_ref[rows, :] = mixed.astype(jnp.bfloat16)
        grad_out = cot_then_down[rows, :].astype(jnp.float32) * live
        sum_ref[11:12, :] += columns_total(grad_out * hat)
        sum_ref[9:10, :] += columns_total(grad_out)
        second = normalize_back(grad_out * vec_ref[11:12, :], hat, inverse)
        wide[rows, :] = second
        down_low = second.astype(jnp.bfloat16)
        cot_then_down[rows, :] = down_low
        sum_ref[7:8, :] += columns_total(down_low.astype(jnp.float32))

    @pl.when((turn >= 0) & (turn < 3))
    def _():
        feed(turn, 0)
        feed(turn, 1)
        start(tile_stores(slot, turn))

    @pl.when(step == 9)
    def _():
        load(1).wait()
        feed(3, 0)
        close(0)
        feed(3, 1)
        start(half_stores(0) + tile_stores(slot, 3))
        close(1)
        start(half_stores(1))
        for at in range(2):
            for copy in tile_stores(at, 0):
                copy.wait()
        for pair in range(PAIRS):
            w_store(pair).wait()
        swap_wait(2, swap_send)
        for unit in range(len(UNITS)):
            for copy in mid_copies(unit) + far_copies(unit) + [near_copy(unit)]:
                copy.wait_send()

            @pl.when(is_end)
            def _():
                for part in z_parts(unit):
                    z_copy(unit, part, 0).wait_send()

            @pl.when(is_middle)
            def _():
                for part in z_parts(unit):
                    z_copy(unit, part, 1).wait_send()
                    z_copy(unit, part, 2).wait_send()

        for at in (0, 1, 2, 6, 7):
            store(at).wait()
        for copy in half_stores(0) + half_stores(1):
            copy.wait()


def gathered_and_forwarded(counts, lengths, owners, bias, gain, x, cotangent, master):
    tokens, width = x.shape
    blocks = tokens // ROWS
    low, high = jnp.bfloat16, jnp.float32
    smem = pl.BlockSpec(memory_space=pltpu.SMEM)
    any_space = pl.BlockSpec(memory_space=pl.ANY)
    dma = pltpu.SemaphoreType.DMA
    shaped = jax.ShapeDtypeStruct

    def at(step):
        step = jnp.minimum(step, 5)
        return lax.rem(step, 2), step // 2

    quad = pl.BlockSpec((ROWS, 256), at)
    rows = shaped((tokens, width), low)
    turned = shaped((width, tokens), low)
    cut = (2, 2, 2, PIECE, width)
    units = len(UNITS)
    return pl.pallas_call(
        gather_and_forward,
        grid=(10,),
        out_shape=(
            rows,
            rows,
            rows,
            shaped((blocks, HEADS, ROWS, ROWS), low),
            rows,
            turned,
            turned,
            turned,
            shaped((4, width, tokens), low),
            shaped((4, tokens, width), low),
            rows,
            rows,
            shaped((tokens, width), high),
            rows,
            shaped((TILES,) + cut, low),
            shaped((tokens, 1), high),
            shaped((16, width), high),
        ),
        in_specs=[smem] * 3
        + [pl.BlockSpec(bias.shape, lambda i: (0, 0)), pl.BlockSpec(gain.shape, lambda i: (0, 0))]
        + [any_space] * 3,
        out_specs=(quad, quad, quad, pl.BlockSpec((1, 4, ROWS, ROWS), lambda i: (*at(i), 0, 0)))
        + (any_space,) * 11
        + (
            pl.BlockSpec((tokens, 1), lambda i: (0, 0), pipeline_mode=pl.Buffered(1)),
            pl.BlockSpec((16, width), lambda i: (0, 0)),
        ),
        scratch_shapes=[
            pltpu.VMEM((VROWS, width), high),
            pltpu.VMEM((2, ROWS, ROWS), high),
            pltpu.VMEM((SLOTS * width, width), high),
            pltpu.VMEM((SLOTS, width, width), low),
            pltpu.VMEM((2 * PLANE, PIECE, 256), low),
            pltpu.VMEM((2 * PLANE, PIECE, 256), low),
            pltpu.VMEM((2 * PLANE, PIECE, 256), low),
            pltpu.VMEM((TILES, PIECE, width), low),
            pltpu.VMEM((TILES, PIECE, width), low),
            pltpu.VMEM((TILES, PIECE, width), low),
            pltpu.VMEM((TILES,) + cut, low),
            pltpu.VMEM((tokens, width), low),
            pltpu.VMEM((width, tokens), low),
            pltpu.VMEM((width, tokens), low),
            pltpu.VMEM((width, tokens), low),
            pltpu.VMEM((tokens, width), low),
            pltpu.VMEM((tokens, width), low),
            pltpu.VMEM((tokens, width), low),
            pltpu.VMEM((tokens, width), low),
            pltpu.VMEM((2, tokens, width), low),
            pltpu.VMEM((2, width, tokens), low),
            dma((3,)),
            dma((2,)),
            dma((8,)),
            dma((2, 3)),
            dma((2, 2)),
            dma((PAIRS,)),
            dma((3,)),
            dma((3,)),
            dma((3, units, 2)),
            dma((3, units, 2)),
            dma((units, 2)),
            dma((units, 2)),
            dma((units, 2)),
            dma((units, 2)),
            dma((units,)),
            dma((units,)),
        ],
        compiler_params=pltpu.CompilerParams(
            collective_id=0, has_side_effects=True, vmem_limit_bytes=63 * 2**20
        ),
        name="gather_and_forward",
    )(counts, lengths, owners, bias, gain, x, cotangent, master.reshape(SLOTS * width, width))


BACK_PLAN = (
    (),
    (),
    (
        ("core", 0),
    ),
    (),
    (
        ("core", 1),
        ("far", 0),
    ),
    (),
    (
        ("core", 2),
        ("far", 1),
    ),
    (
        ("mid", 0),
        ("far", 2),
    ),
    (),
    (
        ("core", 3),
        ("mid", 1),
        ("end", 0),
    ),
    (),
    (
        ("far", 3),
        ("end", 1),
        ("mid", 2),
    ),
    (
        ("core", 4),
        ("middle", 0),
    ),
    (),
    (
        ("middle", 1),
        ("end", 2),
        ("mid", 3),
        ("far", 4),
    ),
    (
        ("total", 0),
    ),
    (
        ("middle", 2),
        ("end", 3),
        ("total", 1),
        ("core", 5),
        ("mid", 4),
    ),
    (),
    (
        ("far", 5),
        ("end", 4),
        ("middle", 3),
        ("total", 2),
    ),
    (),
    (
        ("core", 6),
        ("total", 3),
        ("middle", 4),
        ("mid", 5),
        ("far", 6),
        ("total", 4),
        ("sum", 0),
        ("end", 5),
        ("mid", 6),
        ("middle", 5),
        ("end", 6),
        ("take", 4),
        ("take", 0),
        ("sum", 1),
        ("take", 2),
        ("take", 3),
        ("take", 1),
        ("deliver", 0),
        ("total", 5),
        ("middle", 6),
        ("sum", 2),
        ("take", 5),
        ("deliver", 1),
        ("total", 6),
        ("take", 6),
        ("deliver", 2),
        ("input", 0),
        ("input", 1),
    ),
)


def backward_and_reduce(
    owners,
    p_ref,
    q_ref,
    k_ref,
    v_ref,
    inverse_ref,
    gain_ref,
    late_ref,
    ctx_hbm,
    x_turned_hbm,
    ctx_turned_hbm,
    hidden_hbm,
    active_hbm,
    slope_hbm,
    down_hbm,
    second_hbm,
    hat_hbm,
    w_hbm,
    input_hbm,
    slot_grad,
    vec_out,
    w_part,
    acc,
    hidden_then_x,
    active_then_ctx,
    down_then_branch,
    ctx_ref,
    grad_ctx_ref,
    hat_ref,
    slope_then_query,
    up_then_key,
    value_buf,
    part,
    from_core,
    from_far,
    from_mid,
    from_end,
    from_middle,
    total,
    snap,
    outbox,
    vec_now,
    vec_in,
    holds,
    keeps,
    load_sem,
    w_sem,
    core_send,
    core_recv,
    far_send,
    far_recv,
    mid_send,
    mid_recv,
    z_send,
    z_recv,
    vec_send,
    vec_recv,
    out_send,
    out_recv,
):
    step = pl.program_id(0)
    inner = jnp.maximum(step - 4, 0)
    quad, block, pair = inner // 4, lax.rem(inner, 4) // 2, lax.rem(inner, 2)
    me = lax.axis_index("dp")
    z, y, x, core = place(me)
    in_plane = lax.rem(me, PLANE)
    sibling = me + 1 - 2 * core
    x_peer = me + 2 - 4 * x
    y_peer = me + 4 - 8 * y
    z_targets = along_z(z, in_plane)
    is_end = (z == 0) | (z == 3)
    is_middle = (z == 1) | (z == 2)

    def tiles_of(batch):
        if batch < 4:
            return w_part, 4 + 2 * batch, 2, slice(None)
        return part, 0, 4, pl.ds(256 * (batch - 4), 256)

    def halves(batch, turned):
        ref, first, count, cols = tiles_of(batch)
        return ref, pl.ds(first + turned * count // 2, count // 2), cols

    def core_copy(batch):
        ref, first, count, cols = tiles_of(batch)
        tiles = pl.ds(first, count)
        return remote(
            ref.at[tiles, 1 - core, :, :, :, cols],
            from_core.at[tiles, :, :, :, cols],
            core_send.at[batch],
            core_recv.at[batch],
            sibling,
        )

    def far_copies(batch):
        copies = []
        for turned in range(2):
            ref, tiles, cols = halves(batch, turned)
            src = ref.at[tiles, core, :, 1 - y, :, cols] if turned else ref.at[tiles, core, 1 - x, :, :, cols]
            copies.append(
                remote(
                    src,
                    from_far.at[tiles, :, :, cols],
                    far_send.at[batch, turned],
                    far_recv.at[batch, turned],
                    y_peer if turned else x_peer,
                )
            )
        return copies

    def mid_copies(batch):
        copies = []
        for turned in range(2):
            ref, tiles, cols = halves(batch, turned)
            src = ref.at[tiles, core, 1 - x, y, :, cols] if turned else ref.at[tiles, core, x, 1 - y, :, cols]
            copies.append(
                remote(
                    src,
                    from_mid.at[tiles, :, cols],
                    mid_send.at[batch, turned],
                    mid_recv.at[batch, turned],
                    x_peer if turned else y_peer,
                )
            )
        return copies

    def z_copy(batch, stage):
        ref, first, count, cols = tiles_of(batch)
        tiles = pl.ds(first, count)
        if stage == 2:
            src, dst = total.at[tiles, :, cols], total.at[tiles, :, cols]
        else:
            src = ref.at[tiles, core, x, y, :, cols]
            dst = (from_middle if stage else from_end).at[tiles, :, cols]
        return remote(src, dst, z_send.at[stage, batch], z_recv.at[stage, batch], z_targets[stage])

    def give_core(batch):
        core_copy(batch).start()

    def give_far(batch):
        core_copy(batch).wait_recv()
        ref, first, count, cols = tiles_of(batch)
        for tile in range(first, first + count):
            ref[tile, core, :, :, :, cols] = ref[tile, core, :, :, :, cols] + from_core[tile, :, :, :, cols]
        start(far_copies(batch))

    def give_mid(batch):
        arrive(far_copies(batch))
        for turned in range(2):
            ref, tiles, cols = halves(batch, turned)
            if turned:
                ref[tiles, core, :, y, :, cols] = ref[tiles, core, :, y, :, cols] + from_far[tiles, :, :, cols]
            else:
                ref[tiles, core, x, :, :, cols] = ref[tiles, core, x, :, :, cols] + from_far[tiles, :, :, cols]
        start(mid_copies(batch))

    def add_piece(batch, other):
        ref, first, count, cols = tiles_of(batch)
        tiles = pl.ds(first, count)
        return ref[tiles, core, x, y, :, cols] + other[tiles, :, cols]

    def give_end(batch):
        arrive(mid_copies(batch))
        ref, first, count, cols = tiles_of(batch)
        ref[pl.ds(first, count), core, x, y, :, cols] = add_piece(batch, from_mid)

        @pl.when(is_end)
        def _():
            z_copy(batch, 0).start()

    def give_middle(batch):
        @pl.when(is_middle)
        def _():
            z_copy(batch, 0).wait_recv()
            ref, first, count, cols = tiles_of(batch)
            ref[pl.ds(first, count), core, x, y, :, cols] = add_piece(batch, from_end)
            z_copy(batch, 1).start()

    def give_total(batch):
        @pl.when(is_middle)
        def _():
            z_copy(batch, 1).wait_recv()
            _, first, count, cols = tiles_of(batch)
            total[pl.ds(first, count), :, cols] = add_piece(batch, from_middle)
            z_copy(batch, 2).start()

    def take_total(batch):
        @pl.when(is_end)
        def _():
            z_copy(batch, 2).wait_recv()

    def deliver(third):
        cols = pl.ds(256 * third, 256)
        snap[...] = total[:, :, cols]

        def fill(at, carry):
            value = snap[holds[at]]
            outbox[third, at] = jnp.where(keeps[at] > 0, value, jnp.zeros_like(value))
            return carry

        lax.fori_loop(0, 2 * PLANE, fill, 0)

        def send(hop, carry):
            target = lax.rem(in_plane + hop, PLANE)
            remote(
                outbox.at[third, pl.ds(2 * target, 2)],
                slot_grad.at[:, core, x, y, :, cols],
                out_send.at[third],
                out_recv.at[third],
                z * PLANE + target,
            ).start()
            return carry

        lax.fori_loop(1, PLANE, send, 0)
        keep_copy(third).start()

    def keep_copy(third):
        return pltpu.make_async_copy(
            outbox.at[third, pl.ds(2 * in_plane, 2)],
            slot_grad.at[:, core, x, y, :, pl.ds(256 * third, 256)],
            load_sem.at[5 + third],
        )

    def vec_copies(stage):
        if stage < 3:
            hops = [(stage, (sibling, x_peer, y_peer)[stage])]
        else:
            hops = [
                (2 + hop, lax.rem(z + hop, 4) * PLANE + in_plane) for hop in range(1, 4)
            ]
        return [
            remote(vec_now.at[stage], vec_in.at[at], vec_send.at[at], vec_recv.at[at], device)
            for at, device in hops
        ]

    def vec_next(stage):
        arrive(vec_copies(stage))
        vec_now[stage + 1] = vec_now[stage] + vec_in[stage]
        start(vec_copies(stage + 1))

    def input_store():
        return pltpu.make_async_copy(acc, input_hbm, load_sem.at[4])

    def load(at):
        src, dst = (
            (hidden_hbm, hidden_then_x),
            (down_hbm, down_then_branch),
            (second_hbm, acc),
            (hat_hbm, hat_ref),
            None,
            None,
            None,
            None,
            (x_turned_hbm, hidden_then_x),
            (ctx_turned_hbm, active_then_ctx),
            None,
            None,
            (ctx_hbm, ctx_ref),
        )[at]
        return pltpu.make_async_copy(src, dst, load_sem.at[at])

    def tile_load(tile, side):
        src, dst = ((slope_hbm, slope_then_query), (active_hbm, active_then_ctx))[side]
        return pltpu.make_async_copy(src.at[tile], dst, load_sem.at[10 + side])

    def w_load(at):
        return pltpu.make_async_copy(w_hbm.at[at], w_part.at[at], w_sem.at[at])

    def weight(at, cols=slice(None)):
        value = w_part[at, :, :, :, :, cols]
        return value.reshape(8 * PIECE, value.shape[-1])

    def input_rows(half):
        rows = slice(ROWS * half, ROWS * half + ROWS)
        more = acc[rows, :]
        for at, buf in enumerate((slope_then_query, up_then_key, value_buf)):
            more = more + dot_back(buf[rows, :], weight(at))
        acc[rows, :] = more
        if half == 1:
            input_store().start()

    actions = {
        "core": give_core,
        "far": give_far,
        "mid": give_mid,
        "end": give_end,
        "middle": give_middle,
        "total": give_total,
        "take": take_total,
        "deliver": deliver,
        "sum": vec_next,
        "input": input_rows,
    }

    @pl.when(step == 0)
    def _():
        start([load(1), tile_load(0, 0), w_load(5), w_load(4)])
        for at in range(2 * PLANE):
            tile_here, kept = jnp.int32(0), jnp.int32(0)
            for tile in range(TILES):
                place_of = SLOTS * owners[tile] + slot_number(owners, tile)
                match = place_of == z * 2 * PLANE + at
                tile_here = tile_here + jnp.where(match, POSITIONS.index(tile), 0)
                kept = kept + jnp.where(match, 1, 0)
            holds[at] = tile_here
            keeps[at] = kept
        vec_now[0] = late_ref[...]
        greet(z, in_plane)

    def serve(points):
        for at in points:
            if BACK_PLAN[at]:

                @pl.when(step == (at // 2 if at < 8 else at - 4))
                def _():
                    for name, number in BACK_PLAN[at]:
                        actions[name](number)

    serve(range(0, 8, 2))

    @pl.when(step < 4)
    def _():
        tile_load(step, 0).wait()
        w_load(5 + 2 * step).wait()

        @pl.when(step == 0)
        def _():
            load(1).wait()
            start([load(2), tile_load(0, 1), load(0)])

        @pl.when(step < 3)
        def _():
            start([w_load(7 + 2 * step), w_load(6 + 2 * step)])

        @pl.when(step == 1)
        def _():
            load(3).start()

        @pl.when(step == 2)
        def _():
            w_load(3).start()

        @pl.when(step == 3)
        def _():
            start([load(12), w_load(0), w_load(1), w_load(2)])

        for half in range(2):
            rows = slice(ROWS * half, ROWS * half + ROWS)
            back = dot_back(down_then_branch[rows, :], weight(5 + 2 * step))
            up_low = (back * slope_then_query[rows, :].astype(jnp.float32)).astype(jnp.bfloat16)
            up_then_key[rows, :] = up_low
            vec_now[0, pl.ds(3 + step, 1), :] += columns_total(up_low.astype(jnp.float32))

        @pl.when(step < 3)
        def _():
            tile_load(step + 1, 0).start()

        w_load(4 + 2 * step).wait()

        @pl.when(step == 0)
        def _():
            load(2).wait()
            load(0).wait()

        for half in range(2):
            rows = slice(ROWS * half, ROWS * half + ROWS)
            acc[rows, :] = acc[rows, :] + dot_back(up_then_key[rows, :], weight(4 + 2 * step))

    serve(range(1, 8, 2))

    def weight_grads(tile):
        by_down = dot(active_then_ctx[...], down_then_branch[...]).astype(jnp.bfloat16)
        w_part[5 + 2 * tile] = by_down.reshape(2, 2, 2, PIECE, 8 * PIECE)
        by_up = dot(hidden_then_x[...], up_then_key[...]).astype(jnp.bfloat16)
        w_part[4 + 2 * tile] = by_up.reshape(2, 2, 2, PIECE, 8 * PIECE)

    @pl.when(step < 3)
    def _():
        tile_load(step, 1).wait()
        weight_grads(step)
        tile_load(step + 1, 1).start()

    @pl.when(step == 3)
    def _():
        tile_load(3, 1).wait()
        load(3).wait()
        w_load(3).wait()
        for half in range(2):
            rows = slice(ROWS * half, ROWS * half + ROWS)
            grad_hidden, hat = acc[rows, :], hat_ref[rows, :].astype(jnp.float32)
            vec_now[0, 10:11, :] += columns_total(grad_hidden * hat)
            vec_now[0, 8:9, :] += columns_total(grad_hidden)
            first = normalize_back(grad_hidden * gain_ref[0:1, :], hat, inverse_ref[rows, :])
            acc[rows, :] = first
        weight_grads(3)
        for half in range(2):
            rows = slice(ROWS * half, ROWS * half + ROWS)
            branch_low = acc[rows, :].astype(jnp.bfloat16)
            down_then_branch[rows, :] = branch_low
            vec_now[0, 2:3, :] += columns_total(branch_low.astype(jnp.float32))
            grad_ctx_ref[rows, :] = dot_back(branch_low, weight(3)).astype(jnp.bfloat16)
        start([load(8), load(9)])

    serve(range(8, 20))

    here = pl.ds(pl.multiple_of(block * ROWS, ROWS), ROWS)
    quad_cols = pl.ds(pl.multiple_of(quad * 256, 256), 256)

    @pl.when(step == 4)
    def _():
        load(12).wait()
        for at in range(3):
            w_load(at).wait()

    pair_cols = pl.ds(pl.multiple_of(quad * 256 + pair * 128, 128), 128)
    grad_bufs = (slope_then_query, up_then_key, value_buf)

    @pl.when(step >= 4)
    def _():
        grads = attend_back_pair(
            grad_ctx_ref[here, pair_cols],
            ctx_ref[here, pair_cols],
            p_ref.at[0],
            q_ref[...],
            k_ref[...],
            v_ref[...],
        )
        for buf, grad in zip(grad_bufs, grads):
            buf[here, pair_cols] = grad
        vec_now[0, 0:1, pair_cols] += columns_total(grads[0].astype(jnp.float32))
        vec_now[0, 1:2, pair_cols] += columns_total(grads[2].astype(jnp.float32))

    @pl.when(step == 7)
    def _():
        load(8).wait()
        load(9).wait()

    @pl.when((step >= 4) & (block == 1) & (pair == 1))
    def _():
        for tile in range(4):
            if tile < 3:
                value = dot(hidden_then_x[...], grad_bufs[tile][:, quad_cols])
            else:
                value = dot(active_then_ctx[...], down_then_branch[:, quad_cols])
            value = value.astype(jnp.bfloat16).reshape(2, 2, 2, PIECE, 256)
            part[tile, :, :, :, :, quad_cols] = value


    @pl.when(step == 15)
    def _():
        start(vec_copies(0))
        for name, number in BACK_PLAN[-1]:
            actions[name](number)
        arrive(vec_copies(3))
        summed = jnp.zeros(vec_out.shape, jnp.float32)
        for origin in range(4):
            hop = lax.rem(z - origin + 4, 4)
            summed = summed + jnp.where(hop == 0, vec_now[3], vec_in[2 + jnp.maximum(hop, 1)])
        vec_out[...] = summed
        for batch in range(7):
            for copy in [core_copy(batch)] + far_copies(batch) + mid_copies(batch):
                copy.wait_send()

            @pl.when(is_end)
            def _():
                z_copy(batch, 0).wait_send()

            @pl.when(is_middle)
            def _():
                z_copy(batch, 1).wait_send()
                z_copy(batch, 2).wait_send()

        for stage in range(4):
            for copy in vec_copies(stage):
                copy.wait_send()
        input_store().wait()
        for third in range(3):
            keep_copy(third).wait()
            most = outbox.at[third, pl.ds(0, 2 * PLANE - 2)]
            pltpu.make_async_copy(most, most, out_recv.at[third]).wait()
            pltpu.make_async_copy(most, most, out_send.at[third]).wait()


def backward_and_reduced(
    owners,
    probs,
    query,
    keyed,
    valued,
    inverse,
    gain,
    late_sums,
    context,
    x_turned,
    ctx_turned,
    hidden,
    active,
    slope,
    grad_down,
    grad_second,
    hat,
    weights,
):
    tokens, width = grad_down.shape
    low, high = jnp.bfloat16, jnp.float32
    shaped = jax.ShapeDtypeStruct
    smem = pl.BlockSpec(memory_space=pltpu.SMEM)
    any_space = pl.BlockSpec(memory_space=pl.ANY)
    dma = pltpu.SemaphoreType.DMA
    once = pl.Buffered(1)

    def at(step):
        inner = jnp.maximum(step - 4, 0)
        return lax.rem(inner, 4) // 2, inner // 4 * 2 + lax.rem(inner, 2)

    pair = pl.BlockSpec((ROWS, 128), at)
    sums = pl.BlockSpec((16, width), lambda i: (0, 0))
    cut = (2, 2, 2, PIECE, width)
    input_grad, slot_grads, vector_sums = pl.pallas_call(
        backward_and_reduce,
        grid=(16,),
        out_shape=(
            shaped((tokens, width), high),
            shaped((SLOTS,) + cut, low),
            shaped((16, width), high),
        ),
        in_specs=[smem, pl.BlockSpec((1, 2, ROWS, ROWS), lambda i: (*at(i), 0, 0))]
        + [pair] * 3
        + [
            pl.BlockSpec((tokens, 1), lambda i: (0, 0), pipeline_mode=once),
            pl.BlockSpec(gain.shape, lambda i: (0, 0)),
            sums,
        ]
        + [any_space] * 10,
        out_specs=(any_space, any_space, sums),
        scratch_shapes=[
            pltpu.VMEM((TILES,) + cut, low),
            pltpu.VMEM((tokens, width), high),
            pltpu.VMEM((width, tokens), low),
            pltpu.VMEM((width, tokens), low),
            pltpu.VMEM((tokens, width), low),
            pltpu.VMEM((tokens, width), low),
            pltpu.VMEM((tokens, width), low),
            pltpu.VMEM((tokens, width), low),
            pltpu.VMEM((tokens, width), low),
            pltpu.VMEM((tokens, width), low),
            pltpu.VMEM((tokens, width), low),
            pltpu.VMEM((4,) + cut, low),
            pltpu.VMEM((TILES,) + cut[1:], low),
            pltpu.VMEM((TILES,) + cut[2:], low),
            pltpu.VMEM((TILES,) + cut[3:], low),
            pltpu.VMEM((TILES,) + cut[3:], low),
            pltpu.VMEM((TILES,) + cut[3:], low),
            pltpu.VMEM((TILES,) + cut[3:], low),
            pltpu.VMEM((TILES, PIECE, 256), low),
            pltpu.VMEM((3, 2 * PLANE, PIECE, 256), low),
            pltpu.VMEM((4, 16, width), high),
            pltpu.VMEM((6, 16, width), high),
            pltpu.SMEM((2 * PLANE,), jnp.int32),
            pltpu.SMEM((2 * PLANE,), jnp.int32),
            dma((13,)),
            dma((TILES,)),
            dma((7,)),
            dma((7,)),
            dma((7, 2)),
            dma((7, 2)),
            dma((7, 2)),
            dma((7, 2)),
            dma((3, 7)),
            dma((3, 7)),
            dma((6,)),
            dma((6,)),
            dma((3,)),
            dma((3,)),
        ],
        compiler_params=pltpu.CompilerParams(
            collective_id=1, has_side_effects=True, vmem_limit_bytes=63 * 2**20
        ),
        name="backward_and_reduce",
    )(
        owners,
        probs,
        query,
        keyed,
        valued,
        inverse,
        gain,
        late_sums,
        context,
        x_turned,
        ctx_turned,
        hidden,
        active,
        slope,
        grad_down,
        grad_second,
        hat,
        weights,
    )
    return input_grad, slot_grads.reshape(SLOTS, width, width), vector_sums


def collected_tiles(tile_low, owners, slots):
    mine = owners == lax.axis_index("dp")
    local = jnp.where(mine[:, None, None], tile_low[slots], jnp.zeros((), tile_low.dtype))
    return lax.psum(local, "dp")


def summed_over_slice(parts, vector_terms, owners, slots):
    myself = lax.axis_index("dp")

    def add(held, items):
        part, owner, slot = items
        total = lax.psum(part.astype(jnp.float32), "dp")
        here = (owner == myself) & (slot == jnp.arange(SLOTS, dtype=jnp.int32))
        return held + jnp.where(here[:, None, None], total[None], 0.0), None

    empty = jnp.zeros((SLOTS,) + parts.shape[1:], jnp.float32)
    return lax.scan(add, empty, (parts, owners, slots))[0], lax.psum(vector_terms, "dp")


def body(
    inputs,
    cotangent,
    counts,
    lengths,
    owners,
    tile_master,
    tile_first,
    tile_second,
    tile_ema,
    bias_vals,
    gain_vals,
    vector_first,
    vector_second,
    vector_ema,
):
    tokens = inputs.shape[0]
    small = lax.axis_size("dp") == GROUP
    gain_scale = float(tokens * lax.axis_size("dp")) ** (-0.5)
    if small:
        (
            query,
            keyed,
            valued,
            probs,
            context,
            x_turned,
            ctx_turned,
            hidden,
            active,
            slope,
            grad_down,
            mixed,
            grad_second,
            hat,
            weights,
            inverse,
            late_sums,
        ) = gathered_and_forwarded(
            counts,
            lengths,
            owners,
            bias_vals,
            gain_vals,
            inputs,
            cotangent,
            tile_master,
        )
        input_grad, slot_grads, full_sums = backward_and_reduced(
            owners,
            probs,
            query,
            keyed,
            valued,
            inverse,
            gain_vals,
            late_sums,
            context,
            x_turned,
            ctx_turned,
            hidden,
            active,
            slope,
            grad_down,
            grad_second,
            hat,
            weights,
        )
    else:
        slots = tile_slots(owners)
        vectors = jnp.concatenate([bias_vals, gain_vals], 0)
        weights = collected_tiles(tile_master[0].astype(jnp.bfloat16), owners, slots)
        query, keyed, valued, probs, context, hat, inverse = attended(
            counts, lengths, inputs, weights, vectors
        )
        mixed, grad_first, grad_branch, grad_context, up_grads, down_grads, late_sums = fed_forward_both(
            counts, lengths, hat, inverse, cotangent, weights, vectors
        )
        input_grad, early_grads, early_sums = attended_back(
            probs, query, keyed, valued, inputs, context, grad_context, grad_branch, grad_first, weights
        )
        parts = jnp.concatenate([early_grads, up_grads, down_grads], 0)
        slot_grads, full_sums = summed_over_slice(parts, late_sums + early_sums, owners, slots)
        slot_grads = slot_grads.astype(jnp.bfloat16)
    return updated(
        gain_scale,
        slot_grads,
        tile_master,
        tile_first,
        tile_second,
        tile_ema,
        full_sums,
        bias_vals,
        gain_vals,
        vector_first,
        vector_second,
        vector_ema,
        mixed,
        input_grad,
    )


def solution(mesh):
    placed = (
        P("dp", None),
        P("dp", None),
        P("dp", None),
        P("dp", None),
        P(),
        P("dp", None, None, None),
        P("dp", None, None, None),
        P("dp", None, None, None),
        P("dp", None, None, None),
        P(),
        P(),
        P(),
        P(),
        P(),
    )
    return jax.shard_map(
        body,
        mesh=mesh,
        in_specs=placed,
        out_specs=(
            P("dp", None),
            P("dp", None),
            P("dp", None, None, None),
            P("dp", None, None, None),
            P("dp", None, None, None),
            P("dp", None, None, None),
            P("dp", None, None, None),
            P(),
            P(),
            P(),
            P(),
        ),
        check_vma=False,
    )
```

```python
import functools

import jax
import jax.numpy as jnp
from jax import lax
from jax.experimental import pallas as pl
from jax.experimental.pallas import tpu as pltpu
from jax.sharding import PartitionSpec as P

HEADS = 12
BUCKET = 128
SLOTS = 2
TILES = 12
VROWS = 12
STEP = 5

norm_epsilon = 1e-12
tile_rate = 0.03
vector_rate = 0.2
first_decay = 0.5
second_decay = 0.5
adam_epsilon = 1e-08
weight_decay = 0.01
average_rate = 0.9


def tile_slots(owners):
    order = jnp.arange(owners.shape[0], dtype=jnp.int32)
    same = owners[:, None] == owners[None, :]
    earlier = order[None, :] < order[:, None]
    return jnp.sum((same & earlier).astype(jnp.int32), 1)


def adam_update(param, grad, first, second, rate):
    first_new = first_decay * first + (1.0 - first_decay) * grad
    second_new = second_decay * second + (1.0 - second_decay) * grad * grad
    first_hat = first_new / (1.0 - first_decay**STEP)
    second_hat = second_new / (1.0 - second_decay**STEP)
    param_new = param - rate * (
        first_hat / (jnp.sqrt(second_hat) + adam_epsilon) + weight_decay * param
    )
    return (param_new, first_new, second_new)


ROWS = 4 * BUCKET
TAIL_RATE = 0.28
TAIL_SERIES = (
    0.11615256574707405,
    0.06981038475559553,
    0.2631359597579608,
    -0.22983675561378278,
    0.38546775012288165,
    -0.10472989053809521,
)
INV_SQRT_TAU = 0.3989422804014327
ALLOWED = 3.0e38
BARRED = -1000000000.0


def dot(left, right):
    return jnp.dot(left, right, preferred_element_type=jnp.float32)


def dot_back(left, right):
    return lax.dot_general(
        left, right, (((1,), (1,)), ((), ())), preferred_element_type=jnp.float32
    )


def outer(left, right):
    return lax.dot_general(
        left, right, (((0,), (0,)), ((), ())), preferred_element_type=jnp.float32
    )


def passage_facts(counts, lengths, position):
    places = lengths.shape[1]
    big_end = counts[0, 0]
    mid_end = big_end + counts[0, 1]
    all_end = mid_end + counts[0, 2]
    start = jnp.int32(0)
    member = jnp.zeros(position.shape, jnp.int32)
    usable = jnp.zeros(position.shape, jnp.int32)
    for number in range(places):
        size = jnp.where(
            number < big_end,
            4 * BUCKET,
            jnp.where(number < mid_end, 2 * BUCKET, jnp.where(number < all_end, BUCKET, 0)),
        )
        inside = (position >= start) & (position < start + size)
        live = inside & (position < start + lengths[0, number])
        member = jnp.where(inside, number + 1, member)
        usable = jnp.where(live, 1, usable)
        start = start + size
    passage = jnp.where(member > 0, member - 1, places + position // BUCKET)
    return usable, passage


def normalize(values):
    center = jnp.mean(values, -1, keepdims=True)
    centered = values - center
    spread = jnp.mean(centered * centered, -1, keepdims=True)
    inverse = lax.rsqrt(spread + norm_epsilon)
    return centered * inverse, inverse


def normalize_back(grad, hat, inverse):
    center = jnp.mean(grad, -1, keepdims=True)
    along = jnp.mean(grad * hat, -1, keepdims=True)
    return inverse * (grad - center - hat * along)


def columns_total(values):
    return jnp.sum(values, 0, keepdims=True)


def attention_caps(counts, lengths, block):
    at_row = lax.broadcasted_iota(jnp.int32, (ROWS, 1), 0) + block * ROWS
    at_column = lax.broadcasted_iota(jnp.int32, (1, ROWS), 1) + block * ROWS
    _, passage_row = passage_facts(counts, lengths, at_row)
    usable_column, passage_column = passage_facts(counts, lengths, at_column)
    allowed = (passage_row == passage_column) & ((usable_column == 1) | (at_row == at_column))
    return jnp.where(allowed, ALLOWED, BARRED)


def attend_quad(quad, weight, x_ref, vec_ref, cap_ref, q_ref, k_ref, v_ref, p_ref, ctx_ref):
    cols = pl.ds(pl.multiple_of(quad * 256, 256), 256)
    x = x_ref[...]
    query = (dot(x, weight(0, cols)) + vec_ref[0:1, cols]).astype(jnp.bfloat16)
    query = query * jnp.bfloat16(0.125)
    keyed = dot(x, weight(1, cols)).astype(jnp.bfloat16)
    valued = (dot(x, weight(2, cols)) + vec_ref[1:2, cols]).astype(jnp.bfloat16)
    q_ref[...] = query
    k_ref[...] = keyed
    v_ref[...] = valued
    low_half = lax.broadcasted_iota(jnp.int32, (1, 128), 1) < 64

    def attend_pair(pair, carry):
        part = pl.ds(pl.multiple_of(128 * pair, 128), 128)
        query, keyed, valued = q_ref[:, part], k_ref[:, part], v_ref[:, part]
        contexts = []
        for head in range(2):
            here = low_half if head == 0 else ~low_half
            mine = jnp.where(here, query, jnp.zeros_like(query))
            scores = jnp.minimum(dot_back(mine, keyed), cap_ref[...])
            exponent = jnp.exp(scores - jnp.max(scores, -1, keepdims=True))
            inverse = 1.0 / jnp.sum(exponent, -1, keepdims=True)
            probability = (exponent * inverse).astype(jnp.bfloat16)
            p_ref[0, 2 * pair + head] = probability
            contexts.append(dot(probability, valued))
        both = jnp.where(low_half, contexts[0], contexts[1]).astype(jnp.bfloat16)
        ctx_ref[:, pl.ds(pl.multiple_of(quad * 256 + 128 * pair, 128), 128)] = both
        return carry

    lax.fori_loop(0, 2, attend_pair, 0)


def close_block(w_out, x_ref, vec_ref, ctx_ref, hat_ref, inverse_ref):
    branch = dot(ctx_ref[...], w_out) + vec_ref[2:3, :]
    hat_ref[...], inverse_ref[...] = normalize(x_ref[...].astype(jnp.float32) + branch)


def attend_back_pair(pull, level_from, p_ref, query, keyed, valued):
    low_half = lax.broadcasted_iota(jnp.int32, (1, 128), 1) < 64
    along = pull.astype(jnp.float32) * level_from.astype(jnp.float32)
    by_query, by_key, by_value = [], [], []
    for head in range(2):
        mask = low_half if head == 0 else ~low_half
        mine = jnp.where(mask, pull, jnp.zeros_like(pull))
        level = jnp.sum(jnp.where(mask, along, 0.0), -1, keepdims=True)
        probability = p_ref[head]
        grad_prob = dot_back(mine, valued)
        grad_scores = (probability.astype(jnp.float32) * (grad_prob - level)).astype(jnp.bfloat16)
        by_query.append(dot(grad_scores, keyed))
        by_key.append(outer(grad_scores, query))
        by_value.append(outer(probability, pull))
    grad_query = jnp.where(low_half, by_query[0], by_query[1]) * 0.125
    grad_key = jnp.where(low_half, by_key[0], by_key[1])
    grad_value = jnp.where(low_half, by_value[0], by_value[1])
    return [value.astype(jnp.bfloat16) for value in (grad_query, grad_key, grad_value)]


def gelu_parts(up):
    near = 1.0 / (1.0 + TAIL_RATE * jnp.abs(up))
    decay = jnp.exp(up * up * -0.5)
    series = jnp.full_like(near, TAIL_SERIES[-1])
    for term in TAIL_SERIES[-2::-1]:
        series = series * near + term
    tail = series * near * decay
    share = jnp.where(up < 0.0, tail, 1.0 - tail)
    slope = share + up * (decay * INV_SQRT_TAU)
    return (up * share).astype(jnp.bfloat16), slope


def attend_forward(
    counts,
    lengths,
    x_ref,
    w_hbm,
    vec_ref,
    q_ref,
    k_ref,
    v_ref,
    p_ref,
    ctx_ref,
    hat_ref,
    inverse_ref,
    w_buf,
    cap_ref,
    w_sem,
):
    block, quad = pl.program_id(0), pl.program_id(1)
    loads = [pltpu.make_async_copy(w_hbm.at[at], w_buf.at[at], w_sem.at[at]) for at in range(4)]

    @pl.when((block == 0) & (quad == 0))
    def _():
        for load in loads:
            load.start()
        for load in loads:
            load.wait()

    @pl.when(quad == 0)
    def _():
        cap_ref[...] = attention_caps(counts, lengths, block)

    def weight(at, cols):
        return w_buf[at, :, cols]

    attend_quad(quad, weight, x_ref, vec_ref, cap_ref, q_ref, k_ref, v_ref, p_ref, ctx_ref)

    @pl.when(quad == 2)
    def _():
        close_block(w_buf[3], x_ref, vec_ref, ctx_ref, hat_ref, inverse_ref)


def attended(counts, lengths, x, weights, vectors):
    tokens, width = x.shape
    blocks = tokens // ROWS
    low = jnp.bfloat16
    smem = pl.BlockSpec(memory_space=pltpu.SMEM)
    quad = pl.BlockSpec((ROWS, 256), lambda b, h: (b, h))
    rows = pl.BlockSpec((ROWS, width), lambda b, h: (b, 0))
    shaped = jax.ShapeDtypeStruct
    return pl.pallas_call(
        attend_forward,
        grid=(blocks, 3),
        out_shape=(
            shaped((tokens, width), low),
            shaped((tokens, width), low),
            shaped((tokens, width), low),
            shaped((blocks, HEADS, ROWS, ROWS), low),
            shaped((tokens, width), low),
            shaped((tokens, width), jnp.float32),
            shaped((tokens, 1), jnp.float32),
        ),
        in_specs=[
            smem,
            smem,
            rows,
            pl.BlockSpec(memory_space=pl.ANY),
            pl.BlockSpec((VROWS, width), lambda b, h: (0, 0)),
        ],
        out_specs=(
            quad,
            quad,
            quad,
            pl.BlockSpec((1, 4, ROWS, ROWS), lambda b, h: (b, h, 0, 0)),
            rows,
            rows,
            pl.BlockSpec((ROWS, 1), lambda b, h: (b, 0)),
        ),
        scratch_shapes=[
            pltpu.VMEM((4, width, width), low),
            pltpu.VMEM((ROWS, ROWS), jnp.float32),
            pltpu.SemaphoreType.DMA((4,)),
        ],
        compiler_params=pltpu.CompilerParams(vmem_limit_bytes=56 * 2**20),
        name="attend_forward",
    )(counts, lengths, x, weights, vectors)


def feed_forward_both(
    counts,
    lengths,
    hat_ref,
    inverse_ref,
    cot_ref,
    w_hbm,
    vec_ref,
    mixed_ref,
    first_ref,
    branch_ref,
    context_ref,
    up_grad_ref,
    down_grad_ref,
    sum_ref,
    w_buf,
    active_ref,
    up_ref,
    hidden_ref,
    down_ref,
    slope_ref,
    w_sem,
):
    step = pl.program_id(0)
    blocks = pl.num_programs(0) - 4
    loads = [
        pltpu.make_async_copy(w_hbm.at[3 + at], w_buf.at[at], w_sem.at[at]) for at in range(9)
    ]

    @pl.when(step == 0)
    def _():
        for load in loads[1:] + loads[:1]:
            load.start()
        sum_ref[...] = jnp.zeros_like(sum_ref)
        for load in loads[1:] + loads[:1]:
            load.wait()

    @pl.when(step < blocks)
    def _():
        here = pl.ds(pl.multiple_of(step * ROWS, ROWS), ROWS)
        at_row = lax.broadcasted_iota(jnp.int32, (ROWS, 1), 0) + step * ROWS
        live = passage_facts(counts, lengths, at_row)[0].astype(jnp.float32)
        hat = hat_ref[...]
        hidden = hat * vec_ref[10:11, :] + vec_ref[8:9, :]
        hidden_low = hidden.astype(jnp.bfloat16)
        hidden_ref[here, :] = hidden_low
        total = hidden + vec_ref[7:8, :]
        for tile in range(4):
            up = dot(hidden_low, w_buf[1 + tile]) + vec_ref[3 + tile : 4 + tile, :]
            active, slope = gelu_parts(up)
            slope_ref[tile] = slope.astype(jnp.bfloat16)
            active_ref[tile, here, :] = active
            total = total + dot(active, w_buf[5 + tile])
        hat_two, inverse_two = normalize(total)
        mixed_ref[...] = ((hat_two * vec_ref[11:12, :] + vec_ref[9:10, :]) * live).astype(jnp.bfloat16)
        grad_out = cot_ref[...].astype(jnp.float32) * live
        sum_ref[11:12, :] += columns_total(grad_out * hat_two)
        sum_ref[9:10, :] += columns_total(grad_out)
        second = normalize_back(grad_out * vec_ref[11:12, :], hat_two, inverse_two)
        down_low = second.astype(jnp.bfloat16)
        down_ref[here, :] = down_low
        sum_ref[7:8, :] += columns_total(down_low.astype(jnp.float32))
        grad_hidden = second
        for tile in range(4):
            pulled = dot_back(down_low, w_buf[5 + tile])
            up_low = (pulled * slope_ref[tile].astype(jnp.float32)).astype(jnp.bfloat16)
            up_ref[tile, here, :] = up_low
            sum_ref[3 + tile : 4 + tile, :] += columns_total(up_low.astype(jnp.float32))
            grad_hidden = grad_hidden + dot_back(up_low, w_buf[1 + tile])
        sum_ref[10:11, :] += columns_total(grad_hidden * hat)
        sum_ref[8:9, :] += columns_total(grad_hidden)
        grad_first = normalize_back(grad_hidden * vec_ref[10:11, :], hat, inverse_ref[...])
        first_ref[...] = grad_first
        branch_low = grad_first.astype(jnp.bfloat16)
        branch_ref[...] = branch_low
        sum_ref[2:3, :] += columns_total(branch_low.astype(jnp.float32))
        context_ref[...] = dot_back(branch_low, w_buf[0]).astype(jnp.bfloat16)

    @pl.when(step >= blocks)
    def _():
        tile = step - blocks
        up_grad_ref[0] = outer(hidden_ref[...], up_ref[tile]).astype(jnp.bfloat16)
        down_grad_ref[0] = outer(active_ref[tile], down_ref[...]).astype(jnp.bfloat16)


def fed_forward_both(counts, lengths, hat, inverse, cotangent, weights, vectors):
    tokens, width = hat.shape
    blocks = tokens // ROWS
    low = jnp.bfloat16
    smem = pl.BlockSpec(memory_space=pltpu.SMEM)
    shaped = jax.ShapeDtypeStruct

    def block_of(step):
        return jnp.minimum(step, blocks - 1)

    def tile_of(step):
        return jnp.maximum(step - blocks, 0)

    rows = pl.BlockSpec((ROWS, width), lambda i: (block_of(i), 0))
    tile = pl.BlockSpec((1, width, width), lambda i: (tile_of(i), 0, 0))
    return pl.pallas_call(
        feed_forward_both,
        grid=(blocks + 4,),
        out_shape=(
            shaped((tokens, width), low),
            shaped((tokens, width), jnp.float32),
            shaped((tokens, width), low),
            shaped((tokens, width), low),
            shaped((4, width, width), low),
            shaped((4, width, width), low),
            shaped((16, width), jnp.float32),
        ),
        in_specs=[
            smem,
            smem,
            rows,
            pl.BlockSpec((ROWS, 1), lambda i: (block_of(i), 0)),
            rows,
            pl.BlockSpec(memory_space=pl.ANY),
            pl.BlockSpec((VROWS, width), lambda i: (0, 0)),
        ],
        out_specs=(
            rows,
            rows,
            rows,
            rows,
            tile,
            tile,
            pl.BlockSpec((16, width), lambda i: (0, 0)),
        ),
        scratch_shapes=[
            pltpu.VMEM((9, width, width), low),
            pltpu.VMEM((4, tokens, width), low),
            pltpu.VMEM((4, tokens, width), low),
            pltpu.VMEM((tokens, width), low),
            pltpu.VMEM((tokens, width), low),
            pltpu.VMEM((4, ROWS, width), low),
            pltpu.SemaphoreType.DMA((9,)),
        ],
        compiler_params=pltpu.CompilerParams(vmem_limit_bytes=60 * 2**20),
        name="feed_forward_both",
    )(counts, lengths, hat, inverse, cotangent, weights, vectors)


def attend_backward(
    p_ref,
    q_ref,
    k_ref,
    v_ref,
    x_ref,
    ctx_ref,
    grad_ctx_ref,
    branch_ref,
    first_ref,
    w_ref,
    input_ref,
    grad_ref,
    sum_ref,
    pulled,
):
    step = pl.program_id(0)
    quad, block = step // 2, lax.rem(step, 2)
    here = pl.ds(pl.multiple_of(block * ROWS, ROWS), ROWS)
    cols = pl.ds(pl.multiple_of(quad * 256, 256), 256)

    @pl.when(step == 0)
    def _():
        sum_ref[...] = jnp.zeros_like(sum_ref)
        input_ref[...] = first_ref[...]

    for pair in range(2):
        half = slice(128 * pair, 128 * pair + 128)
        at = pl.ds(pl.multiple_of(quad * 256 + 128 * pair, 128), 128)
        heads = p_ref.at[0, pl.ds(2 * pair, 2)]
        grads = attend_back_pair(
            grad_ctx_ref[here, at], ctx_ref[here, at], heads, q_ref[:, half], k_ref[:, half], v_ref[:, half]
        )
        for number, grad in enumerate(grads):
            pulled[number, here, half] = grad
        sum_ref[0:1, at] += columns_total(grads[0].astype(jnp.float32))
        sum_ref[1:2, at] += columns_total(grads[2].astype(jnp.float32))

    more = input_ref[here, :]
    for at in range(3):
        more = more + dot_back(pulled[at, here, :], w_ref[at, :, cols])
    input_ref[here, :] = more

    @pl.when(block == 1)
    def _():
        for tile in range(3):
            grad_ref[tile, :, cols] = outer(x_ref[...], pulled[tile]).astype(jnp.bfloat16)
        grad_ref[3, :, cols] = outer(ctx_ref[...], branch_ref[:, cols]).astype(jnp.bfloat16)


def attended_back(probs, query, keyed, valued, x, context, grad_context, grad_branch, grad_first, weights):
    tokens, width = x.shape
    low = jnp.bfloat16
    shaped = jax.ShapeDtypeStruct
    once = pl.Buffered(1)
    quad = pl.BlockSpec((ROWS, 256), lambda i: (lax.rem(i, 2), i // 2))
    whole = pl.BlockSpec((tokens, width), lambda i: (0, 0), pipeline_mode=once)
    return pl.pallas_call(
        attend_backward,
        grid=(6,),
        out_shape=(
            shaped((tokens, width), jnp.float32),
            shaped((4, width, width), low),
            shaped((16, width), jnp.float32),
        ),
        in_specs=[
            pl.BlockSpec((1, 4, ROWS, ROWS), lambda i: (lax.rem(i, 2), i // 2, 0, 0)),
            quad,
            quad,
            quad,
            whole,
            whole,
            whole,
            whole,
            whole,
            pl.BlockSpec((3, width, width), lambda i: (0, 0, 0), pipeline_mode=once),
        ],
        out_specs=(
            whole,
            pl.BlockSpec((4, width, width), lambda i: (0, 0, 0), pipeline_mode=once),
            pl.BlockSpec((16, width), lambda i: (0, 0)),
        ),
        scratch_shapes=[pltpu.VMEM((3, tokens, 256), low)],
        compiler_params=pltpu.CompilerParams(vmem_limit_bytes=56 * 2**20),
        name="attend_backward",
    )(probs, query, keyed, valued, x, context, grad_context, grad_branch, grad_first, weights)


def moved(param, grad, first, second, average, rate):
    param_new, first_new, second_new = adam_update(param, grad, first, second, rate)
    return param_new, first_new, second_new, average_rate * average + (1.0 - average_rate) * param_new


def update_kernel(
    gain_scale,
    grad_ref,
    master_ref,
    first_ref,
    second_ref,
    ema_ref,
    vec_grad_ref,
    bias_ref,
    gain_ref,
    vec_first_ref,
    vec_second_ref,
    vec_ema_ref,
    mixed_in,
    input_in,
    master_out,
    first_out,
    second_out,
    ema_out,
    copy_out,
    vec_out,
    vec_first_out,
    vec_second_out,
    vec_ema_out,
    mixed_out,
    input_out,
    vec_ref,
):
    mixed_out[...] = mixed_in[...]
    input_out[...] = input_in[...]

    @pl.when((pl.program_id(0) == 0) & (pl.program_id(1) == 0))
    def _():
        vec_ref[0:10, :] = bias_ref[...]
        vec_ref[10:12, :] = gain_ref[...]
        vec_grad = vec_grad_ref[0:VROWS, :] * gain_scale
        vec_out[...], vec_first_out[...], vec_second_out[...], vec_ema_out[...] = moved(
            vec_ref[...], vec_grad, vec_first_ref[...], vec_second_ref[...], vec_ema_ref[...], vector_rate
        )

    grad = grad_ref[...].astype(jnp.float32) * gain_scale
    result = moved(master_ref[0], grad, first_ref[0], second_ref[0], ema_ref[0], tile_rate)
    master_out[0], first_out[0], second_out[0], ema_out[0] = result
    copy_out[0] = result[0].astype(jnp.bfloat16)


def updated(
    gain_scale,
    slot_grads,
    master,
    first,
    second,
    ema,
    vec_grad,
    bias,
    gain,
    vec_first,
    vec_second,
    vec_ema,
    mixed,
    input_grad,
):
    width = master.shape[-1]
    chunk = 192
    tile = pl.BlockSpec((1, 1, chunk, width), lambda s, r: (0, s, r, 0))
    steps = width // chunk
    rows = pl.BlockSpec((mixed.shape[0] // (SLOTS * steps), width), lambda s, r: (s * steps + r, 0))

    def whole(value):
        return pl.BlockSpec(value.shape, lambda s, r: (0, 0))

    shaped = jax.ShapeDtypeStruct
    tile_shape = shaped(master.shape, jnp.float32)
    vec_shape = shaped((VROWS, width), jnp.float32)
    results = pl.pallas_call(
        functools.partial(update_kernel, gain_scale),
        grid=(SLOTS, steps),
        out_shape=(tile_shape,) * 4
        + (shaped(master.shape, jnp.bfloat16),)
        + (vec_shape,) * 4
        + (shaped(mixed.shape, mixed.dtype), shaped(input_grad.shape, input_grad.dtype)),
        in_specs=[pl.BlockSpec((1, chunk, width), lambda s, r: (s, r, 0))]
        + [tile] * 4
        + [whole(value) for value in (vec_grad, bias, gain, vec_first, vec_second, vec_ema)]
        + [rows] * 2,
        out_specs=(tile,) * 5 + (whole(vec_first),) * 4 + (rows,) * 2,
        scratch_shapes=[pltpu.VMEM((VROWS, width), jnp.float32)],
        compiler_params=pltpu.CompilerParams(vmem_limit_bytes=62 * 2**20),
        name="update",
    )(
        slot_grads,
        master,
        first,
        second,
        ema,
        vec_grad,
        bias,
        gain,
        vec_first,
        vec_second,
        vec_ema,
        mixed,
        input_grad,
    )
    return results[-2:] + results[:-2]


MESH = pl.DeviceIdType.MESH
GROUP = 32
PAIRS = TILES // 2
PLANE = 8
PIECE = 96
PAIR_TILES = ((0, 1), (2, 3), (4, 8), (5, 9), (6, 10), (7, 11))


def remote(src, dst, send, recv, device):
    return pltpu.make_async_remote_copy(
        src_ref=src, dst_ref=dst, send_sem=send, recv_sem=recv, device_id=(device,), device_id_type=MESH
    )


def place(device):
    core = lax.rem(device, 2)
    x = lax.rem(device // 2, 2)
    y = lax.rem(device // 4, 2)
    z = device // 8
    return z, y, x, core


def start(copies):
    for copy in copies:
        copy.start()


def arrive(copies):
    for copy in copies:
        copy.wait_recv()


def greet(z, in_plane):
    barrier = pltpu.get_barrier_semaphore()
    for hop in range(1, PLANE):
        other = z * PLANE + lax.rem(in_plane + hop, PLANE)
        pl.semaphore_signal(barrier, inc=1, device_id=(other,), device_id_type=MESH)
    for hop in range(1, 4):
        other = lax.rem(z + hop, 4) * PLANE + in_plane
        pl.semaphore_signal(barrier, inc=1, device_id=(other,), device_id_type=MESH)
    pl.semaphore_wait(barrier, PLANE + 2)


def along_z(z, in_plane):
    inner = (1 + z // 2) * PLANE + in_plane
    other_middle = (3 - z) * PLANE + in_plane
    outer_end = lax.rem(lax.rem(z + 3, 4) * 3, 4) * PLANE + in_plane
    return inner, other_middle, outer_end


def third(part):
    return pl.ds(256 * part, 256)


UNITS = [(0, 4, pl.ds(256 * part, 256)) for part in range(3)]
UNITS += [(2 * pair, 2, pl.ds(0, 768)) for pair in range(2, PAIRS)]
Z_PARTS = (pl.ds(0, 512), pl.ds(512, 256))


POSITIONS = [tile for pair in PAIR_TILES for tile in pair]


def slot_number(owners, tile):
    number = jnp.int32(0)
    for earlier in range(tile):
        number = number + jnp.where(owners[earlier] == owners[tile], 1, 0)
    return number

FRONT_PLAN = (
    (
        ("open",),
        ("swap", 0),
        ("sent", 0),
        ("swap", 1),
        ("choose", 0),
        ("end", 0),
        ("sent", 1),
        ("middle", 0),
        ("choose", 1),
        ("end", 1),
        ("swap", 2),
        ("total", 0),
        ("end", 3, 0),
        ("middle", 1),
        ("mid", 0),
        ("choose", 2),
        ("end", 2),
        ("end", 3, 1),
        ("far", 0),
        ("middle", 3, 0),
        ("total", 1),
        ("caps",),
        ("middle", 3, 1),
        ("end", 4, 0),
        ("mid", 1),
        ("near", 0),
        ("total", 3, 0),
        ("end", 5, 0),
        ("middle", 2),
        ("end", 4, 1),
        ("total", 3, 1),
        ("far", 1),
        ("finish", 0),
    ),
    (
        ("middle", 4, 0),
        ("total", 2),
        ("mid", 3),
        ("middle", 4, 1),
        ("end", 5, 1),
    ),
    (
        ("mid", 2),
        ("end", 6, 0),
        ("middle", 5, 0),
        ("near", 1),
        ("total", 4, 1),
        ("far", 3),
        ("finish", 1),
        ("far", 2),
        ("middle", 5, 1),
        ("end", 6, 1),
        ("total", 4, 0),
    ),
    (
        ("total", 5, 0),
        ("middle", 6, 0),
        ("mid", 4),
        ("total", 5, 1),
        ("middle", 6, 1),
    ),
    (
        ("total", 6, 1),
        ("mid", 5),
        ("near", 2),
        ("far", 4),
        ("total", 6, 0),
        ("finish", 2),
        ("keep", 0),
        ("keep", 1),
    ),
    (
        ("mid", 6),
        ("near", 3),
        ("near", 4),
        ("far", 5),
    ),
    (
        ("far", 6),
        ("finish", 4),
        ("keep", 3),
        ("finish", 3),
        ("keep", 2),
    ),
    (
        ("near", 5),
    ),
    (
        ("near", 6),
        ("finish", 5),
        ("keep", 4),
    ),
    (
        ("finish", 6),
        ("keep", 5),
    ),
)


def gather_and_forward(
    counts,
    lengths,
    owners,
    bias_ref,
    gain_ref,
    x_hbm,
    cot_hbm,
    master_hbm,
    q_ref,
    k_ref,
    v_ref,
    p_ref,
    ctx_hbm,
    x_turned_hbm,
    ctx_turned_hbm,
    hidden_hbm,
    active_hbm,
    slope_hbm,
    down_hbm,
    mixed_hbm,
    second_hbm,
    hat_hbm,
    w_out,
    inverse_ref,
    sum_ref,
    vec_ref,
    cap_ref,
    wide,
    low,
    stage_a,
    stage_b,
    stage_c,
    chosen,
    from_end,
    from_middle,
    w_buf,
    x_then_hidden,
    x_turned,
    ctx_turned,
    hidden_turned,
    ctx_ref,
    cot_then_down,
    mixed_ref,
    hat_ref,
    slope_buf,
    active_buf,
    wide_sem,
    load_sem,
    store_sem,
    half_sem,
    tile_sem,
    out_sem,
    swap_send,
    swap_recv,
    z_send,
    z_recv,
    mid_send,
    mid_recv,
    far_send,
    far_recv,
    near_send,
    near_recv,
):
    step = pl.program_id(0)
    width = 8 * PIECE
    me = lax.axis_index("dp")
    z, y, x, core = place(me)
    in_plane = lax.rem(me, PLANE)
    sibling = me + 1 - 2 * core
    x_peer = me + 2 - 4 * x
    y_peer = me + 4 - 8 * y
    z_targets = along_z(z, in_plane)
    stages = (stage_a, stage_b, stage_c)
    is_end = (z == 0) | (z == 3)
    is_middle = (z == 1) | (z == 2)

    def piece_rows(cell_core, cell_x, cell_y):
        return pl.ds(pl.multiple_of(((cell_core * 2 + cell_x) * 2 + cell_y) * PIECE, 16), PIECE)

    def wide_load(part):
        cols = third(part)
        return pltpu.make_async_copy(master_hbm.at[:, cols], wide.at[:, cols], wide_sem.at[part])

    def swap(part):
        wide_load(part).wait()
        for slot in range(SLOTS):
            master = wide[width * slot : width * (slot + 1), third(part)]
            low[slot, :, third(part)] = master.astype(jnp.bfloat16)

        def send(hop, carry):
            target = lax.rem(in_plane + hop, PLANE)
            _, ty, tx, tc = place(target)
            remote(
                low.at[:, piece_rows(tc, tx, ty), third(part)],
                stages[part].at[pl.ds(2 * in_plane, 2)],
                swap_send.at[part],
                swap_recv.at[part],
                z * PLANE + target,
            ).start()
            return carry

        lax.fori_loop(1, PLANE, send, 0)
        stages[part][pl.ds(2 * in_plane, 2)] = low[:, piece_rows(core, x, y), third(part)]
        if part == 0:
            start([load(0), load(1)])

    def swap_wait(part, sem):
        most = stages[part].at[pl.ds(0, 2 * PLANE - 2)]
        pltpu.make_async_copy(most, most, sem.at[part]).wait()

    def z_copy(unit, part, level):
        first, count, cols = UNITS[unit]
        tiles = pl.ds(first, count)
        cols = cols if count == 4 else Z_PARTS[part]
        src = w_buf.at[tiles, core, x, y, :, cols] if level == 2 else chosen.at[tiles, :, cols]
        dst = (from_end.at[tiles, :, cols], from_middle.at[tiles, :, cols], src)[level]
        at = level, unit, part
        return remote(src, dst, z_send.at[at], z_recv.at[at], z_targets[level])

    def z_parts(unit):
        return range(1 if UNITS[unit][1] == 4 else 2)

    def z_end(unit, part=0):
        @pl.when(is_end)
        def _():
            z_copy(unit, part, 0).start()

    def z_rows(unit, part):
        first, count, cols = UNITS[unit]
        return pl.ds(first, count), cols if count == 4 else Z_PARTS[part]

    def z_middle(unit, part=0):
        @pl.when(is_middle)
        def _():
            z_copy(unit, part, 0).wait_recv()
            tiles, cols = z_rows(unit, part)
            chosen[tiles, :, cols] = chosen[tiles, :, cols] + from_end[tiles, :, cols]
            z_copy(unit, part, 1).start()

    def z_total(unit, part=0):
        @pl.when(is_middle)
        def _():
            z_copy(unit, part, 1).wait_recv()
            tiles, cols = z_rows(unit, part)
            w_buf[tiles, core, x, y, :, cols] = chosen[tiles, :, cols] + from_middle[tiles, :, cols]
            z_copy(unit, part, 2).start()

    def mid_copies(unit):
        first, count, cols = UNITS[unit]
        copies = []
        for n, peer in enumerate((y_peer, x_peer)):
            spot = w_buf.at[pl.ds(first + n * count // 2, count // 2), core, x, y, :, cols]
            copies.append(remote(spot, spot, mid_send.at[unit, n], mid_recv.at[unit, n], peer))
        return copies

    def far_copies(unit):
        first, count, cols = UNITS[unit]
        half = count // 2
        by_row = w_buf.at[pl.ds(first, half), core, x, :, :, cols]
        by_column = w_buf.at[pl.ds(first + half, half), core, :, y, :, cols]
        return [
            remote(spot, spot, far_send.at[unit, n], far_recv.at[unit, n], peer)
            for n, (spot, peer) in enumerate(((by_row, x_peer), (by_column, y_peer)))
        ]

    def near_copy(unit):
        first, count, cols = UNITS[unit]
        spot = w_buf.at[pl.ds(first, count), core, :, :, :, cols]
        return remote(spot, spot, near_send.at[unit], near_recv.at[unit], sibling)

    def give_mid(unit):
        @pl.when(is_end)
        def _():
            arrive([z_copy(unit, part, 2) for part in z_parts(unit)])

        start(mid_copies(unit))

    def give_far(unit):
        arrive(mid_copies(unit))
        start(far_copies(unit))

    def give_near(unit):
        arrive(far_copies(unit))
        near_copy(unit).start()

    def finish(unit):
        near_copy(unit).wait_recv()

    def choose(part):
        swap_wait(part, swap_recv)
        for pair in range(PAIRS):
            for n, tile in enumerate(PAIR_TILES[pair]):
                owner = owners[tile]
                value = stages[part][SLOTS * lax.rem(owner, PLANE) + slot_number(owners, tile)]
                chosen[2 * pair + n, :, third(part)] = jnp.where(
                    owner // PLANE == z, value, jnp.zeros_like(value)
                )

    def load(at):
        src = (x_hbm, cot_hbm)[at]
        dst = (x_then_hidden, cot_then_down)[at]
        return pltpu.make_async_copy(src, dst, load_sem.at[at])

    def store(at):
        src, dst = (
            (hidden_turned, hidden_hbm),
            (ctx_ref, ctx_hbm),
            (hat_ref, hat_hbm),
            None,
            None,
            None,
            (x_turned, x_turned_hbm),
            (ctx_turned, ctx_turned_hbm),
        )[at]
        return pltpu.make_async_copy(src, dst, store_sem.at[at])

    def half_stores(half):
        rows = pl.ds(ROWS * half, ROWS)
        pairs = ((cot_then_down, down_hbm), (mixed_ref, mixed_hbm), (wide, second_hbm))
        return [
            pltpu.make_async_copy(src.at[rows], dst.at[rows], half_sem.at[half, at])
            for at, (src, dst) in enumerate(pairs)
        ]

    def w_store(pair):
        two = pl.ds(2 * pair, 2)
        return pltpu.make_async_copy(w_buf.at[two], w_out.at[two], out_sem.at[pair])

    def weight(at, cols=slice(None)):
        value = w_buf[at, :, :, :, :, cols]
        return value.reshape(width, value.shape[-1])

    def open_all():
        start([wide_load(part) for part in range(3)])
        sum_ref[...] = jnp.zeros_like(sum_ref)
        vec_ref[0:10, :] = bias_ref[...]
        vec_ref[10:12, :] = gain_ref[...]
        greet(z, in_plane)

    def make_caps():
        for block in range(2):
            cap_ref[block] = attention_caps(counts, lengths, block)
        load(0).wait()
        x_turned[...] = x_then_hidden[...].T
        store(6).start()

    actions = {
        "open": open_all,
        "caps": make_caps,
        "swap": swap,
        "sent": lambda part: swap_wait(part, swap_send),
        "choose": choose,
        "end": z_end,
        "middle": z_middle,
        "total": z_total,
        "mid": give_mid,
        "far": give_far,
        "near": give_near,
        "finish": finish,
        "keep": lambda pair: w_store(pair).start(),
    }

    for at, work in enumerate(FRONT_PLAN):

        @pl.when(step == at)
        def _():
            for name, *rest in work:
                actions[name](*rest)

    quad, block = step // 2, lax.rem(step, 2)
    here = pl.ds(pl.multiple_of(block * ROWS, ROWS), ROWS)

    @pl.when(step < 6)
    def _():
        attend_quad(
            quad,
            weight,
            x_then_hidden.at[here],
            vec_ref,
            cap_ref.at[block],
            q_ref,
            k_ref,
            v_ref,
            p_ref,
            ctx_ref.at[here],
        )

    @pl.when((step >= 4) & (step < 6))
    def _():
        branch = dot(ctx_ref[here, :], weight(3)) + vec_ref[2:3, :]
        hat, inverse = normalize(x_then_hidden[here, :].astype(jnp.float32) + branch)
        hat_ref[here, :] = hat.astype(jnp.bfloat16)
        inverse_ref[here, :] = inverse
        hidden = hat * vec_ref[10:11, :] + vec_ref[8:9, :]
        hidden_low = hidden.astype(jnp.bfloat16)
        x_then_hidden[here, :] = hidden_low
        hidden_turned[:, here] = hidden_low.T
        ctx_turned[:, here] = ctx_ref[here, :].T
        wide[here, :] = hidden + vec_ref[7:8, :]

    @pl.when(step == 5)
    def _():
        start([store(0), store(1), store(2), store(7)])

    turn = step - 6
    slot = lax.rem(turn, 2)

    def tile_stores(source_slot, tile):
        return [
            pltpu.make_async_copy(src.at[source_slot], dst.at[tile], tile_sem.at[source_slot, at])
            for at, (src, dst) in enumerate(((active_buf, active_hbm), (slope_buf, slope_hbm)))
        ]

    @pl.when(turn >= 2)
    def _():
        for copy in tile_stores(slot, 0):
            copy.wait()

    @pl.when(turn >= 0)
    def _():
        def feed(half, carry):
            rows = pl.ds(pl.multiple_of(half * ROWS, ROWS), ROWS)
            up = dot(x_then_hidden[rows, :], weight(4 + 2 * turn)) + vec_ref[pl.ds(3 + turn, 1), :]
            active, slope = gelu_parts(up)
            slope_buf[slot, rows, :] = slope.astype(jnp.bfloat16)
            active_buf[slot, :, rows] = active.T
            wide[rows, :] = wide[rows, :] + dot(active, weight(5 + 2 * turn))
            return carry

        lax.fori_loop(0, 2, feed, 0)
        start(tile_stores(slot, turn))

    @pl.when(step == 9)
    def _():
        load(1).wait()

        def close(quarter, carry):
            rows = pl.ds(pl.multiple_of(quarter * 256, 256), 256)
            at_row = lax.broadcasted_iota(jnp.int32, (256, 1), 0) + quarter * 256
            live = passage_facts(counts, lengths, at_row)[0].astype(jnp.float32)
            hat, inverse = normalize(wide[rows, :])
            mixed = (hat * vec_ref[11:12, :] + vec_ref[9:10, :]) * live
            mixed_ref[rows, :] = mixed.astype(jnp.bfloat16)
            grad_out = cot_then_down[rows, :].astype(jnp.float32) * live
            sum_ref[11:12, :] += columns_total(grad_out * hat)
            sum_ref[9:10, :] += columns_total(grad_out)
            second = normalize_back(grad_out * vec_ref[11:12, :], hat, inverse)
            wide[rows, :] = second
            down_low = second.astype(jnp.bfloat16)
            cot_then_down[rows, :] = down_low
            sum_ref[7:8, :] += columns_total(down_low.astype(jnp.float32))
            return carry

        lax.fori_loop(0, 2, close, 0)
        start(half_stores(0))
        lax.fori_loop(2, 4, close, 0)
        start(half_stores(1))
        for at in range(2):
            for copy in tile_stores(at, 0):
                copy.wait()
        for pair in range(PAIRS):
            w_store(pair).wait()
        swap_wait(2, swap_send)
        for unit in range(len(UNITS)):
            for copy in mid_copies(unit) + far_copies(unit) + [near_copy(unit)]:
                copy.wait_send()

            @pl.when(is_end)
            def _():
                for part in z_parts(unit):
                    z_copy(unit, part, 0).wait_send()

            @pl.when(is_middle)
            def _():
                for part in z_parts(unit):
                    z_copy(unit, part, 1).wait_send()
                    z_copy(unit, part, 2).wait_send()

        for at in (0, 1, 2, 6, 7):
            store(at).wait()
        for copy in half_stores(0) + half_stores(1):
            copy.wait()


def gathered_and_forwarded(counts, lengths, owners, bias, gain, x, cotangent, master):
    tokens, width = x.shape
    blocks = tokens // ROWS
    low, high = jnp.bfloat16, jnp.float32
    smem = pl.BlockSpec(memory_space=pltpu.SMEM)
    any_space = pl.BlockSpec(memory_space=pl.ANY)
    dma = pltpu.SemaphoreType.DMA
    shaped = jax.ShapeDtypeStruct

    def at(step):
        step = jnp.minimum(step, 5)
        return lax.rem(step, 2), step // 2

    quad = pl.BlockSpec((ROWS, 256), at)
    rows = shaped((tokens, width), low)
    turned = shaped((width, tokens), low)
    cut = (2, 2, 2, PIECE, width)
    units = len(UNITS)
    return pl.pallas_call(
        gather_and_forward,
        grid=(10,),
        out_shape=(
            rows,
            rows,
            rows,
            shaped((blocks, HEADS, ROWS, ROWS), low),
            rows,
            turned,
            turned,
            turned,
            shaped((4, width, tokens), low),
            shaped((4, tokens, width), low),
            rows,
            rows,
            shaped((tokens, width), high),
            rows,
            shaped((TILES,) + cut, low),
            shaped((tokens, 1), high),
            shaped((16, width), high),
        ),
        in_specs=[smem] * 3
        + [pl.BlockSpec(bias.shape, lambda i: (0, 0)), pl.BlockSpec(gain.shape, lambda i: (0, 0))]
        + [any_space] * 3,
        out_specs=(quad, quad, quad, pl.BlockSpec((1, 4, ROWS, ROWS), lambda i: (*at(i), 0, 0)))
        + (any_space,) * 11
        + (
            pl.BlockSpec((tokens, 1), lambda i: (0, 0), pipeline_mode=pl.Buffered(1)),
            pl.BlockSpec((16, width), lambda i: (0, 0)),
        ),
        scratch_shapes=[
            pltpu.VMEM((VROWS, width), high),
            pltpu.VMEM((2, ROWS, ROWS), high),
            pltpu.VMEM((SLOTS * width, width), high),
            pltpu.VMEM((SLOTS, width, width), low),
            pltpu.VMEM((2 * PLANE, PIECE, 256), low),
            pltpu.VMEM((2 * PLANE, PIECE, 256), low),
            pltpu.VMEM((2 * PLANE, PIECE, 256), low),
            pltpu.VMEM((TILES, PIECE, width), low),
            pltpu.VMEM((TILES, PIECE, width), low),
            pltpu.VMEM((TILES, PIECE, width), low),
            pltpu.VMEM((TILES,) + cut, low),
            pltpu.VMEM((tokens, width), low),
            pltpu.VMEM((width, tokens), low),
            pltpu.VMEM((width, tokens), low),
            pltpu.VMEM((width, tokens), low),
            pltpu.VMEM((tokens, width), low),
            pltpu.VMEM((tokens, width), low),
            pltpu.VMEM((tokens, width), low),
            pltpu.VMEM((tokens, width), low),
            pltpu.VMEM((2, tokens, width), low),
            pltpu.VMEM((2, width, tokens), low),
            dma((3,)),
            dma((2,)),
            dma((8,)),
            dma((2, 3)),
            dma((2, 2)),
            dma((PAIRS,)),
            dma((3,)),
            dma((3,)),
            dma((3, units, 2)),
            dma((3, units, 2)),
            dma((units, 2)),
            dma((units, 2)),
            dma((units, 2)),
            dma((units, 2)),
            dma((units,)),
            dma((units,)),
        ],
        compiler_params=pltpu.CompilerParams(
            collective_id=0, has_side_effects=True, vmem_limit_bytes=63 * 2**20
        ),
        name="gather_and_forward",
    )(counts, lengths, owners, bias, gain, x, cotangent, master.reshape(SLOTS * width, width))


BACK_PLAN = (
    (),
    (),
    (
        ("core", 0),
    ),
    (),
    (
        ("core", 1),
        ("far", 0),
    ),
    (),
    (
        ("core", 2),
        ("far", 1),
    ),
    (
        ("mid", 0),
        ("far", 2),
    ),
    (),
    (
        ("core", 3),
        ("mid", 1),
        ("end", 0),
    ),
    (),
    (
        ("far", 3),
        ("end", 1),
        ("mid", 2),
    ),
    (
        ("core", 4),
        ("middle", 0),
    ),
    (),
    (
        ("middle", 1),
        ("end", 2),
        ("mid", 3),
        ("far", 4),
    ),
    (
        ("total", 0),
    ),
    (
        ("middle", 2),
        ("end", 3),
        ("total", 1),
        ("core", 5),
        ("mid", 4),
    ),
    (),
    (
        ("far", 5),
        ("end", 4),
        ("middle", 3),
        ("total", 2),
    ),
    (),
    (
        ("core", 6),
        ("total", 3),
        ("middle", 4),
        ("mid", 5),
        ("far", 6),
        ("total", 4),
        ("sum", 0),
        ("end", 5),
        ("mid", 6),
        ("middle", 5),
        ("end", 6),
        ("take", 4),
        ("take", 0),
        ("sum", 1),
        ("take", 2),
        ("take", 3),
        ("take", 1),
        ("deliver", 0),
        ("total", 5),
        ("middle", 6),
        ("sum", 2),
        ("take", 5),
        ("deliver", 1),
        ("total", 6),
        ("take", 6),
        ("deliver", 2),
        ("input", 0),
        ("input", 1),
    ),
)


def backward_and_reduce(
    owners,
    p_ref,
    q_ref,
    k_ref,
    v_ref,
    inverse_ref,
    gain_ref,
    late_ref,
    ctx_hbm,
    x_turned_hbm,
    ctx_turned_hbm,
    hidden_hbm,
    active_hbm,
    slope_hbm,
    down_hbm,
    second_hbm,
    hat_hbm,
    w_hbm,
    input_hbm,
    slot_grad,
    vec_out,
    w_part,
    acc,
    hidden_then_x,
    active_then_ctx,
    down_then_branch,
    ctx_ref,
    grad_ctx_ref,
    hat_ref,
    slope_then_query,
    up_then_key,
    value_buf,
    part,
    from_core,
    from_far,
    from_mid,
    from_end,
    from_middle,
    total,
    snap,
    outbox,
    vec_now,
    vec_in,
    holds,
    keeps,
    load_sem,
    w_sem,
    core_send,
    core_recv,
    far_send,
    far_recv,
    mid_send,
    mid_recv,
    z_send,
    z_recv,
    vec_send,
    vec_recv,
    out_send,
    out_recv,
):
    step = pl.program_id(0)
    inner = jnp.maximum(step - 4, 0)
    quad, block, pair = inner // 4, lax.rem(inner, 4) // 2, lax.rem(inner, 2)
    me = lax.axis_index("dp")
    z, y, x, core = place(me)
    in_plane = lax.rem(me, PLANE)
    sibling = me + 1 - 2 * core
    x_peer = me + 2 - 4 * x
    y_peer = me + 4 - 8 * y
    z_targets = along_z(z, in_plane)
    is_end = (z == 0) | (z == 3)
    is_middle = (z == 1) | (z == 2)

    def tiles_of(batch):
        if batch < 4:
            return w_part, 4 + 2 * batch, 2, slice(None)
        return part, 0, 4, pl.ds(256 * (batch - 4), 256)

    def halves(batch, turned):
        ref, first, count, cols = tiles_of(batch)
        return ref, pl.ds(first + turned * count // 2, count // 2), cols

    def core_copy(batch):
        ref, first, count, cols = tiles_of(batch)
        tiles = pl.ds(first, count)
        return remote(
            ref.at[tiles, 1 - core, :, :, :, cols],
            from_core.at[tiles, :, :, :, cols],
            core_send.at[batch],
            core_recv.at[batch],
            sibling,
        )

    def far_copies(batch):
        copies = []
        for turned in range(2):
            ref, tiles, cols = halves(batch, turned)
            src = ref.at[tiles, core, :, 1 - y, :, cols] if turned else ref.at[tiles, core, 1 - x, :, :, cols]
            copies.append(
                remote(
                    src,
                    from_far.at[tiles, :, :, cols],
                    far_send.at[batch, turned],
                    far_recv.at[batch, turned],
                    y_peer if turned else x_peer,
                )
            )
        return copies

    def mid_copies(batch):
        copies = []
        for turned in range(2):
            ref, tiles, cols = halves(batch, turned)
            src = ref.at[tiles, core, 1 - x, y, :, cols] if turned else ref.at[tiles, core, x, 1 - y, :, cols]
            copies.append(
                remote(
                    src,
                    from_mid.at[tiles, :, cols],
                    mid_send.at[batch, turned],
                    mid_recv.at[batch, turned],
                    x_peer if turned else y_peer,
                )
            )
        return copies

    def z_copy(batch, stage):
        ref, first, count, cols = tiles_of(batch)
        tiles = pl.ds(first, count)
        if stage == 2:
            src, dst = total.at[tiles, :, cols], total.at[tiles, :, cols]
        else:
            src = ref.at[tiles, core, x, y, :, cols]
            dst = (from_middle if stage else from_end).at[tiles, :, cols]
        return remote(src, dst, z_send.at[stage, batch], z_recv.at[stage, batch], z_targets[stage])

    def give_core(batch):
        core_copy(batch).start()

    def give_far(batch):
        core_copy(batch).wait_recv()
        ref, first, count, cols = tiles_of(batch)
        for tile in range(first, first + count):
            ref[tile, core, :, :, :, cols] = ref[tile, core, :, :, :, cols] + from_core[tile, :, :, :, cols]
        start(far_copies(batch))

    def give_mid(batch):
        arrive(far_copies(batch))
        for turned in range(2):
            ref, tiles, cols = halves(batch, turned)
            if turned:
                ref[tiles, core, :, y, :, cols] = ref[tiles, core, :, y, :, cols] + from_far[tiles, :, :, cols]
            else:
                ref[tiles, core, x, :, :, cols] = ref[tiles, core, x, :, :, cols] + from_far[tiles, :, :, cols]
        start(mid_copies(batch))

    def add_piece(batch, other):
        ref, first, count, cols = tiles_of(batch)
        tiles = pl.ds(first, count)
        return ref[tiles, core, x, y, :, cols] + other[tiles, :, cols]

    def give_end(batch):
        arrive(mid_copies(batch))
        ref, first, count, cols = tiles_of(batch)
        ref[pl.ds(first, count), core, x, y, :, cols] = add_piece(batch, from_mid)

        @pl.when(is_end)
        def _():
            z_copy(batch, 0).start()

    def give_middle(batch):
        @pl.when(is_middle)
        def _():
            z_copy(batch, 0).wait_recv()
            ref, first, count, cols = tiles_of(batch)
            ref[pl.ds(first, count), core, x, y, :, cols] = add_piece(batch, from_end)
            z_copy(batch, 1).start()

    def give_total(batch):
        @pl.when(is_middle)
        def _():
            z_copy(batch, 1).wait_recv()
            _, first, count, cols = tiles_of(batch)
            total[pl.ds(first, count), :, cols] = add_piece(batch, from_middle)
            z_copy(batch, 2).start()

    def take_total(batch):
        @pl.when(is_end)
        def _():
            z_copy(batch, 2).wait_recv()

    def deliver(third):
        cols = pl.ds(256 * third, 256)
        snap[...] = total[:, :, cols]

        def fill(at, carry):
            value = snap[holds[at]]
            outbox[third, at] = jnp.where(keeps[at] > 0, value, jnp.zeros_like(value))
            return carry

        lax.fori_loop(0, 2 * PLANE, fill, 0)

        def send(hop, carry):
            target = lax.rem(in_plane + hop, PLANE)
            remote(
                outbox.at[third, pl.ds(2 * target, 2)],
                slot_grad.at[:, core, x, y, :, cols],
                out_send.at[third],
                out_recv.at[third],
                z * PLANE + target,
            ).start()
            return carry

        lax.fori_loop(1, PLANE, send, 0)
        keep_copy(third).start()

    def keep_copy(third):
        return pltpu.make_async_copy(
            outbox.at[third, pl.ds(2 * in_plane, 2)],
            slot_grad.at[:, core, x, y, :, pl.ds(256 * third, 256)],
            load_sem.at[5 + third],
        )

    def vec_copies(stage):
        if stage < 3:
            hops = [(stage, (sibling, x_peer, y_peer)[stage])]
        else:
            hops = [
                (2 + hop, lax.rem(z + hop, 4) * PLANE + in_plane) for hop in range(1, 4)
            ]
        return [
            remote(vec_now.at[stage], vec_in.at[at], vec_send.at[at], vec_recv.at[at], device)
            for at, device in hops
        ]

    def vec_next(stage):
        arrive(vec_copies(stage))
        vec_now[stage + 1] = vec_now[stage] + vec_in[stage]
        start(vec_copies(stage + 1))

    def input_store():
        return pltpu.make_async_copy(acc, input_hbm, load_sem.at[4])

    def load(at):
        src, dst = (
            (hidden_hbm, hidden_then_x),
            (down_hbm, down_then_branch),
            (second_hbm, acc),
            (hat_hbm, hat_ref),
            None,
            None,
            None,
            None,
            (x_turned_hbm, hidden_then_x),
            (ctx_turned_hbm, active_then_ctx),
            None,
            None,
            (ctx_hbm, ctx_ref),
        )[at]
        return pltpu.make_async_copy(src, dst, load_sem.at[at])

    def tile_load(tile, side):
        src, dst = ((slope_hbm, slope_then_query), (active_hbm, active_then_ctx))[side]
        return pltpu.make_async_copy(src.at[tile], dst, load_sem.at[10 + side])

    def w_load(at):
        return pltpu.make_async_copy(w_hbm.at[at], w_part.at[at], w_sem.at[at])

    def weight(at, cols=slice(None)):
        value = w_part[at, :, :, :, :, cols]
        return value.reshape(8 * PIECE, value.shape[-1])

    def input_rows(half):
        rows = slice(ROWS * half, ROWS * half + ROWS)
        more = acc[rows, :]
        for at, buf in enumerate((slope_then_query, up_then_key, value_buf)):
            more = more + dot_back(buf[rows, :], weight(at))
        acc[rows, :] = more
        if half == 1:
            input_store().start()

    actions = {
        "core": give_core,
        "far": give_far,
        "mid": give_mid,
        "end": give_end,
        "middle": give_middle,
        "total": give_total,
        "take": take_total,
        "deliver": deliver,
        "sum": vec_next,
        "input": input_rows,
    }

    @pl.when(step == 0)
    def _():
        start([load(1), tile_load(0, 0), w_load(5), w_load(4)])
        for at in range(2 * PLANE):
            tile_here, kept = jnp.int32(0), jnp.int32(0)
            for tile in range(TILES):
                place_of = SLOTS * owners[tile] + slot_number(owners, tile)
                match = place_of == z * 2 * PLANE + at
                tile_here = tile_here + jnp.where(match, POSITIONS.index(tile), 0)
                kept = kept + jnp.where(match, 1, 0)
            holds[at] = tile_here
            keeps[at] = kept
        vec_now[0] = late_ref[...]
        greet(z, in_plane)

    def serve(points):
        for at in points:
            if BACK_PLAN[at]:

                @pl.when(step == (at // 2 if at < 8 else at - 4))
                def _():
                    for name, number in BACK_PLAN[at]:
                        actions[name](number)

    serve(range(0, 8, 2))

    @pl.when(step < 4)
    def _():
        tile_load(step, 0).wait()
        w_load(5 + 2 * step).wait()

        @pl.when(step == 0)
        def _():
            load(1).wait()
            start([load(2), tile_load(0, 1), load(0)])

        @pl.when(step < 3)
        def _():
            start([w_load(7 + 2 * step), w_load(6 + 2 * step)])

        @pl.when(step == 1)
        def _():
            load(3).start()

        @pl.when(step == 2)
        def _():
            w_load(3).start()

        @pl.when(step == 3)
        def _():
            start([load(12), w_load(0), w_load(1), w_load(2)])

        def pull(half, carry):
            rows = pl.ds(pl.multiple_of(half * ROWS, ROWS), ROWS)
            back = dot_back(down_then_branch[rows, :], weight(5 + 2 * step))
            up_low = (back * slope_then_query[rows, :].astype(jnp.float32)).astype(jnp.bfloat16)
            up_then_key[rows, :] = up_low
            vec_now[0, pl.ds(3 + step, 1), :] += columns_total(up_low.astype(jnp.float32))
            return carry

        lax.fori_loop(0, 2, pull, 0)

        @pl.when(step < 3)
        def _():
            tile_load(step + 1, 0).start()

        w_load(4 + 2 * step).wait()

        @pl.when(step == 0)
        def _():
            load(2).wait()
            load(0).wait()

        for half in range(2):
            rows = slice(ROWS * half, ROWS * half + ROWS)
            acc[rows, :] = acc[rows, :] + dot_back(up_then_key[rows, :], weight(4 + 2 * step))

    serve(range(1, 8, 2))

    @pl.when(step < 4)
    def _():
        tile_load(step, 1).wait()
        by_down = dot(active_then_ctx[...], down_then_branch[...]).astype(jnp.bfloat16)
        w_part[5 + 2 * step] = by_down.reshape(2, 2, 2, PIECE, 8 * PIECE)

        @pl.when(step < 3)
        def _():
            tile_load(step + 1, 1).start()

        by_up = dot(hidden_then_x[...], up_then_key[...]).astype(jnp.bfloat16)
        w_part[4 + 2 * step] = by_up.reshape(2, 2, 2, PIECE, 8 * PIECE)

    @pl.when(step == 3)
    def _():
        start([load(8), load(9)])
        load(3).wait()
        w_load(3).wait()
        def open_first(quarter, carry):
            rows = pl.ds(pl.multiple_of(quarter * 256, 256), 256)
            grad_hidden, hat = acc[rows, :], hat_ref[rows, :].astype(jnp.float32)
            vec_now[0, 10:11, :] += columns_total(grad_hidden * hat)
            vec_now[0, 8:9, :] += columns_total(grad_hidden)
            first = normalize_back(grad_hidden * gain_ref[0:1, :], hat, inverse_ref[rows, :])
            acc[rows, :] = first
            branch_low = first.astype(jnp.bfloat16)
            down_then_branch[rows, :] = branch_low
            vec_now[0, 2:3, :] += columns_total(branch_low.astype(jnp.float32))
            grad_ctx_ref[rows, :] = dot_back(branch_low, weight(3)).astype(jnp.bfloat16)
            return carry

        lax.fori_loop(0, 4, open_first, 0)

    serve(range(8, 20))

    here = pl.ds(pl.multiple_of(block * ROWS, ROWS), ROWS)
    quad_cols = pl.ds(pl.multiple_of(quad * 256, 256), 256)

    @pl.when(step == 4)
    def _():
        load(12).wait()
        for at in range(3):
            w_load(at).wait()

    pair_cols = pl.ds(pl.multiple_of(quad * 256 + pair * 128, 128), 128)
    grad_bufs = (slope_then_query, up_then_key, value_buf)

    @pl.when(step >= 4)
    def _():
        grads = attend_back_pair(
            grad_ctx_ref[here, pair_cols],
            ctx_ref[here, pair_cols],
            p_ref.at[0],
            q_ref[...],
            k_ref[...],
            v_ref[...],
        )
        for buf, grad in zip(grad_bufs, grads):
            buf[here, pair_cols] = grad
        vec_now[0, 0:1, pair_cols] += columns_total(grads[0].astype(jnp.float32))
        vec_now[0, 1:2, pair_cols] += columns_total(grads[2].astype(jnp.float32))

    @pl.when(step == 7)
    def _():
        load(8).wait()
        load(9).wait()

    @pl.when((step >= 4) & (block == 1) & (pair == 1))
    def _():
        for tile in range(4):
            if tile < 3:
                value = dot(hidden_then_x[...], grad_bufs[tile][:, quad_cols])
            else:
                value = dot(active_then_ctx[...], down_then_branch[:, quad_cols])
            value = value.astype(jnp.bfloat16).reshape(2, 2, 2, PIECE, 256)
            part[tile, :, :, :, :, quad_cols] = value


    @pl.when(step == 15)
    def _():
        start(vec_copies(0))
        for name, number in BACK_PLAN[-1]:
            actions[name](number)
        arrive(vec_copies(3))
        summed = jnp.zeros(vec_out.shape, jnp.float32)
        for origin in range(4):
            hop = lax.rem(z - origin + 4, 4)
            summed = summed + jnp.where(hop == 0, vec_now[3], vec_in[2 + jnp.maximum(hop, 1)])
        vec_out[...] = summed
        for batch in range(7):
            for copy in [core_copy(batch)] + far_copies(batch) + mid_copies(batch):
                copy.wait_send()

            @pl.when(is_end)
            def _():
                z_copy(batch, 0).wait_send()

            @pl.when(is_middle)
            def _():
                z_copy(batch, 1).wait_send()
                z_copy(batch, 2).wait_send()

        for stage in range(4):
            for copy in vec_copies(stage):
                copy.wait_send()
        input_store().wait()
        for third in range(3):
            keep_copy(third).wait()
            most = outbox.at[third, pl.ds(0, 2 * PLANE - 2)]
            pltpu.make_async_copy(most, most, out_recv.at[third]).wait()
            pltpu.make_async_copy(most, most, out_send.at[third]).wait()


def backward_and_reduced(
    owners,
    probs,
    query,
    keyed,
    valued,
    inverse,
    gain,
    late_sums,
    context,
    x_turned,
    ctx_turned,
    hidden,
    active,
    slope,
    grad_down,
    grad_second,
    hat,
    weights,
):
    tokens, width = grad_down.shape
    low, high = jnp.bfloat16, jnp.float32
    shaped = jax.ShapeDtypeStruct
    smem = pl.BlockSpec(memory_space=pltpu.SMEM)
    any_space = pl.BlockSpec(memory_space=pl.ANY)
    dma = pltpu.SemaphoreType.DMA
    once = pl.Buffered(1)

    def at(step):
        inner = jnp.maximum(step - 4, 0)
        return lax.rem(inner, 4) // 2, inner // 4 * 2 + lax.rem(inner, 2)

    pair = pl.BlockSpec((ROWS, 128), at)
    sums = pl.BlockSpec((16, width), lambda i: (0, 0))
    cut = (2, 2, 2, PIECE, width)
    input_grad, slot_grads, vector_sums = pl.pallas_call(
        backward_and_reduce,
        grid=(16,),
        out_shape=(
            shaped((tokens, width), high),
            shaped((SLOTS,) + cut, low),
            shaped((16, width), high),
        ),
        in_specs=[smem, pl.BlockSpec((1, 2, ROWS, ROWS), lambda i: (*at(i), 0, 0))]
        + [pair] * 3
        + [
            pl.BlockSpec((tokens, 1), lambda i: (0, 0), pipeline_mode=once),
            pl.BlockSpec(gain.shape, lambda i: (0, 0)),
            sums,
        ]
        + [any_space] * 10,
        out_specs=(any_space, any_space, sums),
        scratch_shapes=[
            pltpu.VMEM((TILES,) + cut, low),
            pltpu.VMEM((tokens, width), high),
            pltpu.VMEM((width, tokens), low),
            pltpu.VMEM((width, tokens), low),
            pltpu.VMEM((tokens, width), low),
            pltpu.VMEM((tokens, width), low),
            pltpu.VMEM((tokens, width), low),
            pltpu.VMEM((tokens, width), low),
            pltpu.VMEM((tokens, width), low),
            pltpu.VMEM((tokens, width), low),
            pltpu.VMEM((tokens, width), low),
            pltpu.VMEM((4,) + cut, low),
            pltpu.VMEM((TILES,) + cut[1:], low),
            pltpu.VMEM((TILES,) + cut[2:], low),
            pltpu.VMEM((TILES,) + cut[3:], low),
            pltpu.VMEM((TILES,) + cut[3:], low),
            pltpu.VMEM((TILES,) + cut[3:], low),
            pltpu.VMEM((TILES,) + cut[3:], low),
            pltpu.VMEM((TILES, PIECE, 256), low),
            pltpu.VMEM((3, 2 * PLANE, PIECE, 256), low),
            pltpu.VMEM((4, 16, width), high),
            pltpu.VMEM((6, 16, width), high),
            pltpu.SMEM((2 * PLANE,), jnp.int32),
            pltpu.SMEM((2 * PLANE,), jnp.int32),
            dma((13,)),
            dma((TILES,)),
            dma((7,)),
            dma((7,)),
            dma((7, 2)),
            dma((7, 2)),
            dma((7, 2)),
            dma((7, 2)),
            dma((3, 7)),
            dma((3, 7)),
            dma((6,)),
            dma((6,)),
            dma((3,)),
            dma((3,)),
        ],
        compiler_params=pltpu.CompilerParams(
            collective_id=1, has_side_effects=True, vmem_limit_bytes=63 * 2**20
        ),
        name="backward_and_reduce",
    )(
        owners,
        probs,
        query,
        keyed,
        valued,
        inverse,
        gain,
        late_sums,
        context,
        x_turned,
        ctx_turned,
        hidden,
        active,
        slope,
        grad_down,
        grad_second,
        hat,
        weights,
    )
    return input_grad, slot_grads.reshape(SLOTS, width, width), vector_sums


def collected_tiles(tile_low, owners, slots):
    mine = owners == lax.axis_index("dp")
    local = jnp.where(mine[:, None, None], tile_low[slots], jnp.zeros((), tile_low.dtype))
    return lax.psum(local, "dp")


def summed_over_slice(parts, vector_terms, owners, slots):
    myself = lax.axis_index("dp")

    def add(held, items):
        part, owner, slot = items
        total = lax.psum(part.astype(jnp.float32), "dp")
        here = (owner == myself) & (slot == jnp.arange(SLOTS, dtype=jnp.int32))
        return held + jnp.where(here[:, None, None], total[None], 0.0), None

    empty = jnp.zeros((SLOTS,) + parts.shape[1:], jnp.float32)
    return lax.scan(add, empty, (parts, owners, slots))[0], lax.psum(vector_terms, "dp")


def body(
    inputs,
    cotangent,
    counts,
    lengths,
    owners,
    tile_master,
    tile_first,
    tile_second,
    tile_ema,
    bias_vals,
    gain_vals,
    vector_first,
    vector_second,
    vector_ema,
):
    tokens = inputs.shape[0]
    small = lax.axis_size("dp") == GROUP
    gain_scale = float(tokens * lax.axis_size("dp")) ** (-0.5)
    if small:
        (
            query,
            keyed,
            valued,
            probs,
            context,
            x_turned,
            ctx_turned,
            hidden,
            active,
            slope,
            grad_down,
            mixed,
            grad_second,
            hat,
            weights,
            inverse,
            late_sums,
        ) = gathered_and_forwarded(
            counts,
            lengths,
            owners,
            bias_vals,
            gain_vals,
            inputs,
            cotangent,
            tile_master,
        )
        input_grad, slot_grads, full_sums = backward_and_reduced(
            owners,
            probs,
            query,
            keyed,
            valued,
            inverse,
            gain_vals,
            late_sums,
            context,
            x_turned,
            ctx_turned,
            hidden,
            active,
            slope,
            grad_down,
            grad_second,
            hat,
            weights,
        )
    else:
        slots = tile_slots(owners)
        vectors = jnp.concatenate([bias_vals, gain_vals], 0)
        weights = collected_tiles(tile_master[0].astype(jnp.bfloat16), owners, slots)
        query, keyed, valued, probs, context, hat, inverse = attended(
            counts, lengths, inputs, weights, vectors
        )
        mixed, grad_first, grad_branch, grad_context, up_grads, down_grads, late_sums = fed_forward_both(
            counts, lengths, hat, inverse, cotangent, weights, vectors
        )
        input_grad, early_grads, early_sums = attended_back(
            probs, query, keyed, valued, inputs, context, grad_context, grad_branch, grad_first, weights
        )
        parts = jnp.concatenate([early_grads, up_grads, down_grads], 0)
        slot_grads, full_sums = summed_over_slice(parts, late_sums + early_sums, owners, slots)
    return updated(
        gain_scale,
        slot_grads,
        tile_master,
        tile_first,
        tile_second,
        tile_ema,
        full_sums,
        bias_vals,
        gain_vals,
        vector_first,
        vector_second,
        vector_ema,
        mixed,
        input_grad,
    )


def solution(mesh):
    placed = (
        P("dp", None),
        P("dp", None),
        P("dp", None),
        P("dp", None),
        P(),
        P("dp", None, None, None),
        P("dp", None, None, None),
        P("dp", None, None, None),
        P("dp", None, None, None),
        P(),
        P(),
        P(),
        P(),
        P(),
    )
    return jax.shard_map(
        body,
        mesh=mesh,
        in_specs=placed,
        out_specs=(
            P("dp", None),
            P("dp", None),
            P("dp", None, None, None),
            P("dp", None, None, None),
            P("dp", None, None, None),
            P("dp", None, None, None),
            P("dp", None, None, None),
            P(),
            P(),
            P(),
            P(),
        ),
        check_vma=False,
    )
```

```python
import functools

import jax
import jax.numpy as jnp
from jax import lax
from jax.experimental import pallas as pl
from jax.experimental.pallas import tpu as pltpu
from jax.sharding import PartitionSpec as P

HEADS = 12
BUCKET = 128
SLOTS = 2
TILES = 12
VROWS = 12
STEP = 5

norm_epsilon = 1e-12
tile_rate = 0.03
vector_rate = 0.2
first_decay = 0.5
second_decay = 0.5
adam_epsilon = 1e-08
weight_decay = 0.01
average_rate = 0.9


def tile_slots(owners):
    order = jnp.arange(owners.shape[0], dtype=jnp.int32)
    same = owners[:, None] == owners[None, :]
    earlier = order[None, :] < order[:, None]
    return jnp.sum((same & earlier).astype(jnp.int32), 1)


def adam_update(param, grad, first, second, rate):
    first_new = first_decay * first + (1.0 - first_decay) * grad
    second_new = second_decay * second + (1.0 - second_decay) * grad * grad
    first_hat = first_new / (1.0 - first_decay**STEP)
    second_hat = second_new / (1.0 - second_decay**STEP)
    param_new = param - rate * (
        first_hat / (jnp.sqrt(second_hat) + adam_epsilon) + weight_decay * param
    )
    return (param_new, first_new, second_new)


ROWS = 4 * BUCKET
TAIL_RATE = 0.28
TAIL_SERIES = (
    0.11615256574707405,
    0.06981038475559553,
    0.2631359597579608,
    -0.22983675561378278,
    0.38546775012288165,
    -0.10472989053809521,
)
INV_SQRT_TAU = 0.3989422804014327
ALLOWED = 3.0e38
BARRED = -1000000000.0


def dot(left, right):
    return jnp.dot(left, right, preferred_element_type=jnp.float32)


def dot_back(left, right):
    return lax.dot_general(
        left, right, (((1,), (1,)), ((), ())), preferred_element_type=jnp.float32
    )


def outer(left, right):
    return lax.dot_general(
        left, right, (((0,), (0,)), ((), ())), preferred_element_type=jnp.float32
    )


def passage_facts(counts, lengths, position):
    places = lengths.shape[1]
    big_end = counts[0, 0]
    mid_end = big_end + counts[0, 1]
    all_end = mid_end + counts[0, 2]
    start = jnp.int32(0)
    member = jnp.zeros(position.shape, jnp.int32)
    usable = jnp.zeros(position.shape, jnp.int32)
    for number in range(places):
        size = jnp.where(
            number < big_end,
            4 * BUCKET,
            jnp.where(number < mid_end, 2 * BUCKET, jnp.where(number < all_end, BUCKET, 0)),
        )
        inside = (position >= start) & (position < start + size)
        live = inside & (position < start + lengths[0, number])
        member = jnp.where(inside, number + 1, member)
        usable = jnp.where(live, 1, usable)
        start = start + size
    passage = jnp.where(member > 0, member - 1, places + position // BUCKET)
    return usable, passage


def normalize(values):
    center = jnp.mean(values, -1, keepdims=True)
    centered = values - center
    spread = jnp.mean(centered * centered, -1, keepdims=True)
    inverse = lax.rsqrt(spread + norm_epsilon)
    return centered * inverse, inverse


def normalize_back(grad, hat, inverse):
    center = jnp.mean(grad, -1, keepdims=True)
    along = jnp.mean(grad * hat, -1, keepdims=True)
    return inverse * (grad - center - hat * along)


def columns_total(values):
    return jnp.sum(values, 0, keepdims=True)


def attention_caps(counts, lengths, block):
    at_row = lax.broadcasted_iota(jnp.int32, (ROWS, 1), 0) + block * ROWS
    at_column = lax.broadcasted_iota(jnp.int32, (1, ROWS), 1) + block * ROWS
    _, passage_row = passage_facts(counts, lengths, at_row)
    usable_column, passage_column = passage_facts(counts, lengths, at_column)
    allowed = (passage_row == passage_column) & ((usable_column == 1) | (at_row == at_column))
    return jnp.where(allowed, ALLOWED, BARRED)


def attend_quad(quad, weight, x_ref, vec_ref, cap_ref, q_ref, k_ref, v_ref, p_ref, ctx_ref):
    cols = pl.ds(pl.multiple_of(quad * 256, 256), 256)
    x = x_ref[...]
    query = (dot(x, weight(0, cols)) + vec_ref[0:1, cols]).astype(jnp.bfloat16)
    query = query * jnp.bfloat16(0.125)
    keyed = dot(x, weight(1, cols)).astype(jnp.bfloat16)
    valued = (dot(x, weight(2, cols)) + vec_ref[1:2, cols]).astype(jnp.bfloat16)
    q_ref[...] = query
    k_ref[...] = keyed
    v_ref[...] = valued
    low_half = lax.broadcasted_iota(jnp.int32, (1, 128), 1) < 64
    for pair in range(2):
        part = slice(128 * pair, 128 * pair + 128)
        contexts = []
        for head in range(2):
            here = low_half if head == 0 else ~low_half
            mine = jnp.where(here, query[:, part], jnp.zeros_like(query[:, part]))
            scores = jnp.minimum(dot_back(mine, keyed[:, part]), cap_ref[...])
            exponent = jnp.exp(scores - jnp.max(scores, -1, keepdims=True))
            inverse = 1.0 / jnp.sum(exponent, -1, keepdims=True)
            probability = (exponent * inverse).astype(jnp.bfloat16)
            p_ref[0, 2 * pair + head] = probability
            contexts.append(dot(probability, valued[:, part]))
        both = jnp.where(low_half, contexts[0], contexts[1]).astype(jnp.bfloat16)
        ctx_ref[:, pl.ds(pl.multiple_of(quad * 256 + 128 * pair, 128), 128)] = both


def close_block(w_out, x_ref, vec_ref, ctx_ref, hat_ref, inverse_ref):
    branch = dot(ctx_ref[...], w_out) + vec_ref[2:3, :]
    hat_ref[...], inverse_ref[...] = normalize(x_ref[...].astype(jnp.float32) + branch)


def attend_back_pair(pull, level_from, p_ref, query, keyed, valued):
    low_half = lax.broadcasted_iota(jnp.int32, (1, 128), 1) < 64
    along = pull.astype(jnp.float32) * level_from.astype(jnp.float32)
    by_query, by_key, by_value = [], [], []
    for head in range(2):
        mask = low_half if head == 0 else ~low_half
        mine = jnp.where(mask, pull, jnp.zeros_like(pull))
        level = jnp.sum(jnp.where(mask, along, 0.0), -1, keepdims=True)
        probability = p_ref[head]
        grad_prob = dot_back(mine, valued)
        grad_scores = (probability.astype(jnp.float32) * (grad_prob - level)).astype(jnp.bfloat16)
        by_query.append(dot(grad_scores, keyed))
        by_key.append(outer(grad_scores, query))
        by_value.append(outer(probability, pull))
    grad_query = jnp.where(low_half, by_query[0], by_query[1]) * 0.125
    grad_key = jnp.where(low_half, by_key[0], by_key[1])
    grad_value = jnp.where(low_half, by_value[0], by_value[1])
    return [value.astype(jnp.bfloat16) for value in (grad_query, grad_key, grad_value)]


def gelu_parts(up):
    near = 1.0 / (1.0 + TAIL_RATE * jnp.abs(up))
    decay = jnp.exp(up * up * -0.5)
    series = jnp.full_like(near, TAIL_SERIES[-1])
    for term in TAIL_SERIES[-2::-1]:
        series = series * near + term
    tail = series * near * decay
    share = jnp.where(up < 0.0, tail, 1.0 - tail)
    slope = share + up * (decay * INV_SQRT_TAU)
    return (up * share).astype(jnp.bfloat16), slope


def attend_forward(
    counts,
    lengths,
    x_ref,
    w_hbm,
    vec_ref,
    q_ref,
    k_ref,
    v_ref,
    p_ref,
    ctx_ref,
    hat_ref,
    inverse_ref,
    w_buf,
    cap_ref,
    w_sem,
):
    block, quad = pl.program_id(0), pl.program_id(1)
    loads = [pltpu.make_async_copy(w_hbm.at[at], w_buf.at[at], w_sem.at[at]) for at in range(4)]

    @pl.when((block == 0) & (quad == 0))
    def _():
        for load in loads:
            load.start()
        for load in loads:
            load.wait()

    @pl.when(quad == 0)
    def _():
        cap_ref[...] = attention_caps(counts, lengths, block)

    def weight(at, cols):
        return w_buf[at, :, cols]

    attend_quad(quad, weight, x_ref, vec_ref, cap_ref, q_ref, k_ref, v_ref, p_ref, ctx_ref)

    @pl.when(quad == 2)
    def _():
        close_block(w_buf[3], x_ref, vec_ref, ctx_ref, hat_ref, inverse_ref)


def attended(counts, lengths, x, weights, vectors):
    tokens, width = x.shape
    blocks = tokens // ROWS
    low = jnp.bfloat16
    smem = pl.BlockSpec(memory_space=pltpu.SMEM)
    quad = pl.BlockSpec((ROWS, 256), lambda b, h: (b, h))
    rows = pl.BlockSpec((ROWS, width), lambda b, h: (b, 0))
    shaped = jax.ShapeDtypeStruct
    return pl.pallas_call(
        attend_forward,
        grid=(blocks, 3),
        out_shape=(
            shaped((tokens, width), low),
            shaped((tokens, width), low),
            shaped((tokens, width), low),
            shaped((blocks, HEADS, ROWS, ROWS), low),
            shaped((tokens, width), low),
            shaped((tokens, width), jnp.float32),
            shaped((tokens, 1), jnp.float32),
        ),
        in_specs=[
            smem,
            smem,
            rows,
            pl.BlockSpec(memory_space=pl.ANY),
            pl.BlockSpec((VROWS, width), lambda b, h: (0, 0)),
        ],
        out_specs=(
            quad,
            quad,
            quad,
            pl.BlockSpec((1, 4, ROWS, ROWS), lambda b, h: (b, h, 0, 0)),
            rows,
            rows,
            pl.BlockSpec((ROWS, 1), lambda b, h: (b, 0)),
        ),
        scratch_shapes=[
            pltpu.VMEM((4, width, width), low),
            pltpu.VMEM((ROWS, ROWS), jnp.float32),
            pltpu.SemaphoreType.DMA((4,)),
        ],
        compiler_params=pltpu.CompilerParams(vmem_limit_bytes=56 * 2**20),
        name="attend_forward",
    )(counts, lengths, x, weights, vectors)


def feed_forward_both(
    counts,
    lengths,
    hat_ref,
    inverse_ref,
    cot_ref,
    w_hbm,
    vec_ref,
    mixed_ref,
    first_ref,
    branch_ref,
    context_ref,
    up_grad_ref,
    down_grad_ref,
    sum_ref,
    w_buf,
    active_ref,
    up_ref,
    hidden_ref,
    down_ref,
    slope_ref,
    w_sem,
):
    step = pl.program_id(0)
    blocks = pl.num_programs(0) - 4
    loads = [
        pltpu.make_async_copy(w_hbm.at[3 + at], w_buf.at[at], w_sem.at[at]) for at in range(9)
    ]

    @pl.when(step == 0)
    def _():
        for load in loads[1:] + loads[:1]:
            load.start()
        sum_ref[...] = jnp.zeros_like(sum_ref)
        for load in loads[1:] + loads[:1]:
            load.wait()

    @pl.when(step < blocks)
    def _():
        here = pl.ds(pl.multiple_of(step * ROWS, ROWS), ROWS)
        at_row = lax.broadcasted_iota(jnp.int32, (ROWS, 1), 0) + step * ROWS
        live = passage_facts(counts, lengths, at_row)[0].astype(jnp.float32)
        hat = hat_ref[...]
        hidden = hat * vec_ref[10:11, :] + vec_ref[8:9, :]
        hidden_low = hidden.astype(jnp.bfloat16)
        hidden_ref[here, :] = hidden_low
        total = hidden + vec_ref[7:8, :]
        for tile in range(4):
            up = dot(hidden_low, w_buf[1 + tile]) + vec_ref[3 + tile : 4 + tile, :]
            active, slope = gelu_parts(up)
            slope_ref[tile] = slope.astype(jnp.bfloat16)
            active_ref[tile, here, :] = active
            total = total + dot(active, w_buf[5 + tile])
        hat_two, inverse_two = normalize(total)
        mixed_ref[...] = ((hat_two * vec_ref[11:12, :] + vec_ref[9:10, :]) * live).astype(jnp.bfloat16)
        grad_out = cot_ref[...].astype(jnp.float32) * live
        sum_ref[11:12, :] += columns_total(grad_out * hat_two)
        sum_ref[9:10, :] += columns_total(grad_out)
        second = normalize_back(grad_out * vec_ref[11:12, :], hat_two, inverse_two)
        down_low = second.astype(jnp.bfloat16)
        down_ref[here, :] = down_low
        sum_ref[7:8, :] += columns_total(down_low.astype(jnp.float32))
        grad_hidden = second
        for tile in range(4):
            pulled = dot_back(down_low, w_buf[5 + tile])
            up_low = (pulled * slope_ref[tile].astype(jnp.float32)).astype(jnp.bfloat16)
            up_ref[tile, here, :] = up_low
            sum_ref[3 + tile : 4 + tile, :] += columns_total(up_low.astype(jnp.float32))
            grad_hidden = grad_hidden + dot_back(up_low, w_buf[1 + tile])
        sum_ref[10:11, :] += columns_total(grad_hidden * hat)
        sum_ref[8:9, :] += columns_total(grad_hidden)
        grad_first = normalize_back(grad_hidden * vec_ref[10:11, :], hat, inverse_ref[...])
        first_ref[...] = grad_first
        branch_low = grad_first.astype(jnp.bfloat16)
        branch_ref[...] = branch_low
        sum_ref[2:3, :] += columns_total(branch_low.astype(jnp.float32))
        context_ref[...] = dot_back(branch_low, w_buf[0]).astype(jnp.bfloat16)

    @pl.when(step >= blocks)
    def _():
        tile = step - blocks
        up_grad_ref[0] = outer(hidden_ref[...], up_ref[tile]).astype(jnp.bfloat16)
        down_grad_ref[0] = outer(active_ref[tile], down_ref[...]).astype(jnp.bfloat16)


def fed_forward_both(counts, lengths, hat, inverse, cotangent, weights, vectors):
    tokens, width = hat.shape
    blocks = tokens // ROWS
    low = jnp.bfloat16
    smem = pl.BlockSpec(memory_space=pltpu.SMEM)
    shaped = jax.ShapeDtypeStruct

    def block_of(step):
        return jnp.minimum(step, blocks - 1)

    def tile_of(step):
        return jnp.maximum(step - blocks, 0)

    rows = pl.BlockSpec((ROWS, width), lambda i: (block_of(i), 0))
    tile = pl.BlockSpec((1, width, width), lambda i: (tile_of(i), 0, 0))
    return pl.pallas_call(
        feed_forward_both,
        grid=(blocks + 4,),
        out_shape=(
            shaped((tokens, width), low),
            shaped((tokens, width), jnp.float32),
            shaped((tokens, width), low),
            shaped((tokens, width), low),
            shaped((4, width, width), low),
            shaped((4, width, width), low),
            shaped((16, width), jnp.float32),
        ),
        in_specs=[
            smem,
            smem,
            rows,
            pl.BlockSpec((ROWS, 1), lambda i: (block_of(i), 0)),
            rows,
            pl.BlockSpec(memory_space=pl.ANY),
            pl.BlockSpec((VROWS, width), lambda i: (0, 0)),
        ],
        out_specs=(
            rows,
            rows,
            rows,
            rows,
            tile,
            tile,
            pl.BlockSpec((16, width), lambda i: (0, 0)),
        ),
        scratch_shapes=[
            pltpu.VMEM((9, width, width), low),
            pltpu.VMEM((4, tokens, width), low),
            pltpu.VMEM((4, tokens, width), low),
            pltpu.VMEM((tokens, width), low),
            pltpu.VMEM((tokens, width), low),
            pltpu.VMEM((4, ROWS, width), low),
            pltpu.SemaphoreType.DMA((9,)),
        ],
        compiler_params=pltpu.CompilerParams(vmem_limit_bytes=60 * 2**20),
        name="feed_forward_both",
    )(counts, lengths, hat, inverse, cotangent, weights, vectors)


def attend_backward(
    p_ref,
    q_ref,
    k_ref,
    v_ref,
    x_ref,
    ctx_ref,
    grad_ctx_ref,
    branch_ref,
    first_ref,
    w_ref,
    input_ref,
    grad_ref,
    sum_ref,
    pulled,
):
    step = pl.program_id(0)
    quad, block = step // 2, lax.rem(step, 2)
    here = pl.ds(pl.multiple_of(block * ROWS, ROWS), ROWS)
    cols = pl.ds(pl.multiple_of(quad * 256, 256), 256)

    @pl.when(step == 0)
    def _():
        sum_ref[...] = jnp.zeros_like(sum_ref)
        input_ref[...] = first_ref[...]

    for pair in range(2):
        half = slice(128 * pair, 128 * pair + 128)
        at = pl.ds(pl.multiple_of(quad * 256 + 128 * pair, 128), 128)
        heads = p_ref.at[0, pl.ds(2 * pair, 2)]
        grads = attend_back_pair(
            grad_ctx_ref[here, at], ctx_ref[here, at], heads, q_ref[:, half], k_ref[:, half], v_ref[:, half]
        )
        for number, grad in enumerate(grads):
            pulled[number, here, half] = grad
        sum_ref[0:1, at] += columns_total(grads[0].astype(jnp.float32))
        sum_ref[1:2, at] += columns_total(grads[2].astype(jnp.float32))

    more = input_ref[here, :]
    for at in range(3):
        more = more + dot_back(pulled[at, here, :], w_ref[at, :, cols])
    input_ref[here, :] = more

    @pl.when(block == 1)
    def _():
        for tile in range(3):
            grad_ref[tile, :, cols] = outer(x_ref[...], pulled[tile]).astype(jnp.bfloat16)
        grad_ref[3, :, cols] = outer(ctx_ref[...], branch_ref[:, cols]).astype(jnp.bfloat16)


def attended_back(probs, query, keyed, valued, x, context, grad_context, grad_branch, grad_first, weights):
    tokens, width = x.shape
    low = jnp.bfloat16
    shaped = jax.ShapeDtypeStruct
    once = pl.Buffered(1)
    quad = pl.BlockSpec((ROWS, 256), lambda i: (lax.rem(i, 2), i // 2))
    whole = pl.BlockSpec((tokens, width), lambda i: (0, 0), pipeline_mode=once)
    return pl.pallas_call(
        attend_backward,
        grid=(6,),
        out_shape=(
            shaped((tokens, width), jnp.float32),
            shaped((4, width, width), low),
            shaped((16, width), jnp.float32),
        ),
        in_specs=[
            pl.BlockSpec((1, 4, ROWS, ROWS), lambda i: (lax.rem(i, 2), i // 2, 0, 0)),
            quad,
            quad,
            quad,
            whole,
            whole,
            whole,
            whole,
            whole,
            pl.BlockSpec((3, width, width), lambda i: (0, 0, 0), pipeline_mode=once),
        ],
        out_specs=(
            whole,
            pl.BlockSpec((4, width, width), lambda i: (0, 0, 0), pipeline_mode=once),
            pl.BlockSpec((16, width), lambda i: (0, 0)),
        ),
        scratch_shapes=[pltpu.VMEM((3, tokens, 256), low)],
        compiler_params=pltpu.CompilerParams(vmem_limit_bytes=56 * 2**20),
        name="attend_backward",
    )(probs, query, keyed, valued, x, context, grad_context, grad_branch, grad_first, weights)


def moved(param, grad, first, second, average, rate):
    param_new, first_new, second_new = adam_update(param, grad, first, second, rate)
    return param_new, first_new, second_new, average_rate * average + (1.0 - average_rate) * param_new


def update_kernel(
    gain_scale,
    grad_ref,
    master_ref,
    first_ref,
    second_ref,
    ema_ref,
    vec_grad_ref,
    bias_ref,
    gain_ref,
    vec_first_ref,
    vec_second_ref,
    vec_ema_ref,
    mixed_in,
    input_in,
    master_out,
    first_out,
    second_out,
    ema_out,
    copy_out,
    vec_out,
    vec_first_out,
    vec_second_out,
    vec_ema_out,
    mixed_out,
    input_out,
    vec_ref,
):
    mixed_out[...] = mixed_in[...]
    input_out[...] = input_in[...]

    @pl.when((pl.program_id(0) == 0) & (pl.program_id(1) == 0))
    def _():
        vec_ref[0:10, :] = bias_ref[...]
        vec_ref[10:12, :] = gain_ref[...]
        vec_grad = vec_grad_ref[0:VROWS, :] * gain_scale
        vec_out[...], vec_first_out[...], vec_second_out[...], vec_ema_out[...] = moved(
            vec_ref[...], vec_grad, vec_first_ref[...], vec_second_ref[...], vec_ema_ref[...], vector_rate
        )

    grad = grad_ref[...].astype(jnp.float32) * gain_scale
    result = moved(master_ref[0], grad, first_ref[0], second_ref[0], ema_ref[0], tile_rate)
    master_out[0], first_out[0], second_out[0], ema_out[0] = result
    copy_out[0] = result[0].astype(jnp.bfloat16)


def updated(
    gain_scale,
    slot_grads,
    master,
    first,
    second,
    ema,
    vec_grad,
    bias,
    gain,
    vec_first,
    vec_second,
    vec_ema,
    mixed,
    input_grad,
):
    width = master.shape[-1]
    chunk = 192
    tile = pl.BlockSpec((1, 1, chunk, width), lambda s, r: (0, s, r, 0))
    steps = width // chunk
    rows = pl.BlockSpec((mixed.shape[0] // (SLOTS * steps), width), lambda s, r: (s * steps + r, 0))

    def whole(value):
        return pl.BlockSpec(value.shape, lambda s, r: (0, 0))

    shaped = jax.ShapeDtypeStruct
    tile_shape = shaped(master.shape, jnp.float32)
    vec_shape = shaped((VROWS, width), jnp.float32)
    results = pl.pallas_call(
        functools.partial(update_kernel, gain_scale),
        grid=(SLOTS, steps),
        out_shape=(tile_shape,) * 4
        + (shaped(master.shape, jnp.bfloat16),)
        + (vec_shape,) * 4
        + (shaped(mixed.shape, mixed.dtype), shaped(input_grad.shape, input_grad.dtype)),
        in_specs=[pl.BlockSpec((1, chunk, width), lambda s, r: (s, r, 0))]
        + [tile] * 4
        + [whole(value) for value in (vec_grad, bias, gain, vec_first, vec_second, vec_ema)]
        + [rows] * 2,
        out_specs=(tile,) * 5 + (whole(vec_first),) * 4 + (rows,) * 2,
        scratch_shapes=[pltpu.VMEM((VROWS, width), jnp.float32)],
        compiler_params=pltpu.CompilerParams(vmem_limit_bytes=62 * 2**20),
        name="update",
    )(
        slot_grads,
        master,
        first,
        second,
        ema,
        vec_grad,
        bias,
        gain,
        vec_first,
        vec_second,
        vec_ema,
        mixed,
        input_grad,
    )
    return results[-2:] + results[:-2]


MESH = pl.DeviceIdType.MESH
GROUP = 32
PAIRS = TILES // 2
PLANE = 8
PIECE = 96
PAIR_TILES = ((0, 1), (2, 3), (4, 8), (5, 9), (6, 10), (7, 11))


def remote(src, dst, send, recv, device):
    return pltpu.make_async_remote_copy(
        src_ref=src, dst_ref=dst, send_sem=send, recv_sem=recv, device_id=(device,), device_id_type=MESH
    )


def place(device):
    core = lax.rem(device, 2)
    x = lax.rem(device // 2, 2)
    y = lax.rem(device // 4, 2)
    z = device // 8
    return z, y, x, core


def start(copies):
    for copy in copies:
        copy.start()


def arrive(copies):
    for copy in copies:
        copy.wait_recv()


def greet(z, in_plane):
    barrier = pltpu.get_barrier_semaphore()
    for hop in range(1, PLANE):
        other = z * PLANE + lax.rem(in_plane + hop, PLANE)
        pl.semaphore_signal(barrier, inc=1, device_id=(other,), device_id_type=MESH)
    for hop in range(1, 4):
        other = lax.rem(z + hop, 4) * PLANE + in_plane
        pl.semaphore_signal(barrier, inc=1, device_id=(other,), device_id_type=MESH)
    pl.semaphore_wait(barrier, PLANE + 2)


def along_z(z, in_plane):
    inner = (1 + z // 2) * PLANE + in_plane
    other_middle = (3 - z) * PLANE + in_plane
    outer_end = lax.rem(lax.rem(z + 3, 4) * 3, 4) * PLANE + in_plane
    return inner, other_middle, outer_end


def third(part):
    return pl.ds(256 * part, 256)


UNITS = [(0, 4, pl.ds(256 * part, 256)) for part in range(3)]
UNITS += [(2 * pair, 2, pl.ds(0, 768)) for pair in range(2, PAIRS)]
Z_PARTS = (pl.ds(0, 512), pl.ds(512, 256))


POSITIONS = [tile for pair in PAIR_TILES for tile in pair]


def slot_number(owners, tile):
    number = jnp.int32(0)
    for earlier in range(tile):
        number = number + jnp.where(owners[earlier] == owners[tile], 1, 0)
    return number

FRONT_PLAN = (
    (
        ("open",),
        ("swap", 0),
        ("sent", 0),
        ("swap", 1),
        ("choose", 0),
        ("end", 0),
        ("sent", 1),
        ("middle", 0),
        ("choose", 1),
        ("end", 1),
        ("swap", 2),
        ("total", 0),
        ("end", 3, 0),
        ("middle", 1),
        ("mid", 0),
        ("choose", 2),
        ("end", 2),
        ("end", 3, 1),
        ("far", 0),
        ("middle", 3, 0),
        ("total", 1),
        ("caps",),
        ("middle", 3, 1),
        ("end", 4, 0),
        ("mid", 1),
        ("near", 0),
        ("total", 3, 0),
        ("end", 5, 0),
        ("middle", 2),
        ("end", 4, 1),
        ("total", 3, 1),
        ("far", 1),
        ("finish", 0),
    ),
    (
        ("middle", 4, 0),
        ("total", 2),
        ("mid", 3),
        ("middle", 4, 1),
        ("end", 5, 1),
    ),
    (
        ("mid", 2),
        ("end", 6, 0),
        ("middle", 5, 0),
        ("near", 1),
        ("total", 4, 1),
        ("far", 3),
        ("finish", 1),
        ("far", 2),
        ("middle", 5, 1),
        ("end", 6, 1),
        ("total", 4, 0),
    ),
    (
        ("total", 5, 0),
        ("middle", 6, 0),
        ("mid", 4),
        ("total", 5, 1),
        ("middle", 6, 1),
    ),
    (
        ("total", 6, 1),
        ("mid", 5),
        ("near", 2),
        ("far", 4),
        ("total", 6, 0),
        ("finish", 2),
        ("keep", 0),
        ("keep", 1),
    ),
    (
        ("mid", 6),
        ("near", 3),
        ("near", 4),
        ("far", 5),
    ),
    (
        ("far", 6),
        ("finish", 4),
        ("keep", 3),
        ("finish", 3),
        ("keep", 2),
    ),
    (
        ("near", 5),
    ),
    (
        ("near", 6),
        ("finish", 5),
        ("keep", 4),
    ),
    (
        ("finish", 6),
        ("keep", 5),
    ),
)


def gather_and_forward(
    counts,
    lengths,
    owners,
    bias_ref,
    gain_ref,
    x_hbm,
    cot_hbm,
    master_hbm,
    q_ref,
    k_ref,
    v_ref,
    p_ref,
    ctx_hbm,
    x_turned_hbm,
    ctx_turned_hbm,
    hidden_hbm,
    active_hbm,
    slope_hbm,
    down_hbm,
    mixed_hbm,
    second_hbm,
    hat_hbm,
    w_out,
    inverse_ref,
    sum_ref,
    vec_ref,
    cap_ref,
    wide,
    low,
    stage_a,
    stage_b,
    stage_c,
    chosen,
    from_end,
    from_middle,
    w_buf,
    x_then_hidden,
    x_turned,
    ctx_turned,
    hidden_turned,
    ctx_ref,
    cot_then_down,
    mixed_ref,
    hat_ref,
    slope_buf,
    active_buf,
    wide_sem,
    load_sem,
    store_sem,
    half_sem,
    tile_sem,
    out_sem,
    swap_send,
    swap_recv,
    z_send,
    z_recv,
    mid_send,
    mid_recv,
    far_send,
    far_recv,
    near_send,
    near_recv,
):
    step = pl.program_id(0)
    width = 8 * PIECE
    me = lax.axis_index("dp")
    z, y, x, core = place(me)
    in_plane = lax.rem(me, PLANE)
    sibling = me + 1 - 2 * core
    x_peer = me + 2 - 4 * x
    y_peer = me + 4 - 8 * y
    z_targets = along_z(z, in_plane)
    stages = (stage_a, stage_b, stage_c)
    is_end = (z == 0) | (z == 3)
    is_middle = (z == 1) | (z == 2)

    def piece_rows(cell_core, cell_x, cell_y):
        return pl.ds(pl.multiple_of(((cell_core * 2 + cell_x) * 2 + cell_y) * PIECE, 16), PIECE)

    def wide_load(part):
        cols = third(part)
        return pltpu.make_async_copy(master_hbm.at[:, cols], wide.at[:, cols], wide_sem.at[part])

    def swap(part):
        wide_load(part).wait()
        for slot in range(SLOTS):
            master = wide[width * slot : width * (slot + 1), third(part)]
            low[slot, :, third(part)] = master.astype(jnp.bfloat16)

        def send(hop, carry):
            target = lax.rem(in_plane + hop, PLANE)
            _, ty, tx, tc = place(target)
            remote(
                low.at[:, piece_rows(tc, tx, ty), third(part)],
                stages[part].at[pl.ds(2 * in_plane, 2)],
                swap_send.at[part],
                swap_recv.at[part],
                z * PLANE + target,
            ).start()
            return carry

        lax.fori_loop(1, PLANE, send, 0)
        stages[part][pl.ds(2 * in_plane, 2)] = low[:, piece_rows(core, x, y), third(part)]
        if part == 0:
            start([load(0), load(1)])

    def swap_wait(part, sem):
        most = stages[part].at[pl.ds(0, 2 * PLANE - 2)]
        pltpu.make_async_copy(most, most, sem.at[part]).wait()

    def z_copy(unit, part, level):
        first, count, cols = UNITS[unit]
        tiles = pl.ds(first, count)
        cols = cols if count == 4 else Z_PARTS[part]
        src = w_buf.at[tiles, core, x, y, :, cols] if level == 2 else chosen.at[tiles, :, cols]
        dst = (from_end.at[tiles, :, cols], from_middle.at[tiles, :, cols], src)[level]
        at = level, unit, part
        return remote(src, dst, z_send.at[at], z_recv.at[at], z_targets[level])

    def z_parts(unit):
        return range(1 if UNITS[unit][1] == 4 else 2)

    def z_end(unit, part=0):
        @pl.when(is_end)
        def _():
            z_copy(unit, part, 0).start()

    def z_rows(unit, part):
        first, count, cols = UNITS[unit]
        return pl.ds(first, count), cols if count == 4 else Z_PARTS[part]

    def z_middle(unit, part=0):
        @pl.when(is_middle)
        def _():
            z_copy(unit, part, 0).wait_recv()
            tiles, cols = z_rows(unit, part)
            chosen[tiles, :, cols] = chosen[tiles, :, cols] + from_end[tiles, :, cols]
            z_copy(unit, part, 1).start()

    def z_total(unit, part=0):
        @pl.when(is_middle)
        def _():
            z_copy(unit, part, 1).wait_recv()
            tiles, cols = z_rows(unit, part)
            w_buf[tiles, core, x, y, :, cols] = chosen[tiles, :, cols] + from_middle[tiles, :, cols]
            z_copy(unit, part, 2).start()

    def mid_copies(unit):
        first, count, cols = UNITS[unit]
        copies = []
        for n, peer in enumerate((y_peer, x_peer)):
            spot = w_buf.at[pl.ds(first + n * count // 2, count // 2), core, x, y, :, cols]
            copies.append(remote(spot, spot, mid_send.at[unit, n], mid_recv.at[unit, n], peer))
        return copies

    def far_copies(unit):
        first, count, cols = UNITS[unit]
        half = count // 2
        by_row = w_buf.at[pl.ds(first, half), core, x, :, :, cols]
        by_column = w_buf.at[pl.ds(first + half, half), core, :, y, :, cols]
        return [
            remote(spot, spot, far_send.at[unit, n], far_recv.at[unit, n], peer)
            for n, (spot, peer) in enumerate(((by_row, x_peer), (by_column, y_peer)))
        ]

    def near_copy(unit):
        first, count, cols = UNITS[unit]
        spot = w_buf.at[pl.ds(first, count), core, :, :, :, cols]
        return remote(spot, spot, near_send.at[unit], near_recv.at[unit], sibling)

    def give_mid(unit):
        @pl.when(is_end)
        def _():
            arrive([z_copy(unit, part, 2) for part in z_parts(unit)])

        start(mid_copies(unit))

    def give_far(unit):
        arrive(mid_copies(unit))
        start(far_copies(unit))

    def give_near(unit):
        arrive(far_copies(unit))
        near_copy(unit).start()

    def finish(unit):
        near_copy(unit).wait_recv()

    def choose(part):
        swap_wait(part, swap_recv)
        for pair in range(PAIRS):
            for n, tile in enumerate(PAIR_TILES[pair]):
                owner = owners[tile]
                value = stages[part][SLOTS * lax.rem(owner, PLANE) + slot_number(owners, tile)]
                chosen[2 * pair + n, :, third(part)] = jnp.where(
                    owner // PLANE == z, value, jnp.zeros_like(value)
                )

    def load(at):
        src = (x_hbm, cot_hbm)[at]
        dst = (x_then_hidden, cot_then_down)[at]
        return pltpu.make_async_copy(src, dst, load_sem.at[at])

    def store(at):
        src, dst = (
            (hidden_turned, hidden_hbm),
            (ctx_ref, ctx_hbm),
            (hat_ref, hat_hbm),
            None,
            None,
            None,
            (x_turned, x_turned_hbm),
            (ctx_turned, ctx_turned_hbm),
        )[at]
        return pltpu.make_async_copy(src, dst, store_sem.at[at])

    def half_stores(half):
        rows = pl.ds(ROWS * half, ROWS)
        pairs = ((cot_then_down, down_hbm), (mixed_ref, mixed_hbm), (wide, second_hbm))
        return [
            pltpu.make_async_copy(src.at[rows], dst.at[rows], half_sem.at[half, at])
            for at, (src, dst) in enumerate(pairs)
        ]

    def w_store(pair):
        two = pl.ds(2 * pair, 2)
        return pltpu.make_async_copy(w_buf.at[two], w_out.at[two], out_sem.at[pair])

    def weight(at, cols=slice(None)):
        value = w_buf[at, :, :, :, :, cols]
        return value.reshape(width, value.shape[-1])

    def open_all():
        start([wide_load(part) for part in range(3)])
        sum_ref[...] = jnp.zeros_like(sum_ref)
        vec_ref[0:10, :] = bias_ref[...]
        vec_ref[10:12, :] = gain_ref[...]
        greet(z, in_plane)

    def make_caps():
        for block in range(2):
            cap_ref[block] = attention_caps(counts, lengths, block)
        load(0).wait()
        x_turned[...] = x_then_hidden[...].T
        store(6).start()

    actions = {
        "open": open_all,
        "caps": make_caps,
        "swap": swap,
        "sent": lambda part: swap_wait(part, swap_send),
        "choose": choose,
        "end": z_end,
        "middle": z_middle,
        "total": z_total,
        "mid": give_mid,
        "far": give_far,
        "near": give_near,
        "finish": finish,
        "keep": lambda pair: w_store(pair).start(),
    }

    for at, work in enumerate(FRONT_PLAN):

        @pl.when(step == at)
        def _():
            for name, *rest in work:
                actions[name](*rest)

    quad, block = step // 2, lax.rem(step, 2)
    here = pl.ds(pl.multiple_of(block * ROWS, ROWS), ROWS)

    @pl.when(step < 6)
    def _():
        attend_quad(
            quad,
            weight,
            x_then_hidden.at[here],
            vec_ref,
            cap_ref.at[block],
            q_ref,
            k_ref,
            v_ref,
            p_ref,
            ctx_ref.at[here],
        )

    @pl.when((step >= 4) & (step < 6))
    def _():
        branch = dot(ctx_ref[here, :], weight(3)) + vec_ref[2:3, :]
        hat, inverse = normalize(x_then_hidden[here, :].astype(jnp.float32) + branch)
        hat_ref[here, :] = hat.astype(jnp.bfloat16)
        inverse_ref[here, :] = inverse
        hidden = hat * vec_ref[10:11, :] + vec_ref[8:9, :]
        hidden_low = hidden.astype(jnp.bfloat16)
        x_then_hidden[here, :] = hidden_low
        hidden_turned[:, here] = hidden_low.T
        ctx_turned[:, here] = ctx_ref[here, :].T
        wide[here, :] = hidden + vec_ref[7:8, :]

    @pl.when(step == 5)
    def _():
        start([store(0), store(1), store(2), store(7)])

    turn = step - 6
    slot = lax.rem(turn, 2)

    def tile_stores(source_slot, tile):
        return [
            pltpu.make_async_copy(src.at[source_slot], dst.at[tile], tile_sem.at[source_slot, at])
            for at, (src, dst) in enumerate(((active_buf, active_hbm), (slope_buf, slope_hbm)))
        ]

    @pl.when(turn >= 2)
    def _():
        for copy in tile_stores(slot, 0):
            copy.wait()

    @pl.when(turn >= 0)
    def _():
        for half in range(2):
            rows = slice(ROWS * half, ROWS * half + ROWS)
            up = dot(x_then_hidden[rows, :], weight(4 + 2 * turn)) + vec_ref[pl.ds(3 + turn, 1), :]
            active, slope = gelu_parts(up)
            slope_buf[slot, rows, :] = slope.astype(jnp.bfloat16)
            active_buf[slot, :, rows] = active.T
            wide[rows, :] = wide[rows, :] + dot(active, weight(5 + 2 * turn))
        start(tile_stores(slot, turn))

    @pl.when(step == 9)
    def _():
        load(1).wait()
        for half in range(2):
            rows = slice(ROWS * half, ROWS * half + ROWS)
            at_row = lax.broadcasted_iota(jnp.int32, (ROWS, 1), 0) + half * ROWS
            live = passage_facts(counts, lengths, at_row)[0].astype(jnp.float32)
            hat, inverse = normalize(wide[rows, :])
            mixed = (hat * vec_ref[11:12, :] + vec_ref[9:10, :]) * live
            mixed_ref[rows, :] = mixed.astype(jnp.bfloat16)
            grad_out = cot_then_down[rows, :].astype(jnp.float32) * live
            sum_ref[11:12, :] += columns_total(grad_out * hat)
            sum_ref[9:10, :] += columns_total(grad_out)
            second = normalize_back(grad_out * vec_ref[11:12, :], hat, inverse)
            wide[rows, :] = second
            down_low = second.astype(jnp.bfloat16)
            cot_then_down[rows, :] = down_low
            sum_ref[7:8, :] += columns_total(down_low.astype(jnp.float32))
            start(half_stores(half))
        for at in range(2):
            for copy in tile_stores(at, 0):
                copy.wait()
        for pair in range(PAIRS):
            w_store(pair).wait()
        swap_wait(2, swap_send)
        for unit in range(len(UNITS)):
            for copy in mid_copies(unit) + far_copies(unit) + [near_copy(unit)]:
                copy.wait_send()

            @pl.when(is_end)
            def _():
                for part in z_parts(unit):
                    z_copy(unit, part, 0).wait_send()

            @pl.when(is_middle)
            def _():
                for part in z_parts(unit):
                    z_copy(unit, part, 1).wait_send()
                    z_copy(unit, part, 2).wait_send()

        for at in (0, 1, 2, 6, 7):
            store(at).wait()
        for copy in half_stores(0) + half_stores(1):
            copy.wait()


def gathered_and_forwarded(counts, lengths, owners, bias, gain, x, cotangent, master):
    tokens, width = x.shape
    blocks = tokens // ROWS
    low, high = jnp.bfloat16, jnp.float32
    smem = pl.BlockSpec(memory_space=pltpu.SMEM)
    any_space = pl.BlockSpec(memory_space=pl.ANY)
    dma = pltpu.SemaphoreType.DMA
    shaped = jax.ShapeDtypeStruct

    def at(step):
        step = jnp.minimum(step, 5)
        return lax.rem(step, 2), step // 2

    quad = pl.BlockSpec((ROWS, 256), at)
    rows = shaped((tokens, width), low)
    turned = shaped((width, tokens), low)
    cut = (2, 2, 2, PIECE, width)
    units = len(UNITS)
    return pl.pallas_call(
        gather_and_forward,
        grid=(10,),
        out_shape=(
            rows,
            rows,
            rows,
            shaped((blocks, HEADS, ROWS, ROWS), low),
            rows,
            turned,
            turned,
            turned,
            shaped((4, width, tokens), low),
            shaped((4, tokens, width), low),
            rows,
            rows,
            shaped((tokens, width), high),
            rows,
            shaped((TILES,) + cut, low),
            shaped((tokens, 1), high),
            shaped((16, width), high),
        ),
        in_specs=[smem] * 3
        + [pl.BlockSpec(bias.shape, lambda i: (0, 0)), pl.BlockSpec(gain.shape, lambda i: (0, 0))]
        + [any_space] * 3,
        out_specs=(quad, quad, quad, pl.BlockSpec((1, 4, ROWS, ROWS), lambda i: (*at(i), 0, 0)))
        + (any_space,) * 11
        + (
            pl.BlockSpec((tokens, 1), lambda i: (0, 0), pipeline_mode=pl.Buffered(1)),
            pl.BlockSpec((16, width), lambda i: (0, 0)),
        ),
        scratch_shapes=[
            pltpu.VMEM((VROWS, width), high),
            pltpu.VMEM((2, ROWS, ROWS), high),
            pltpu.VMEM((SLOTS * width, width), high),
            pltpu.VMEM((SLOTS, width, width), low),
            pltpu.VMEM((2 * PLANE, PIECE, 256), low),
            pltpu.VMEM((2 * PLANE, PIECE, 256), low),
            pltpu.VMEM((2 * PLANE, PIECE, 256), low),
            pltpu.VMEM((TILES, PIECE, width), low),
            pltpu.VMEM((TILES, PIECE, width), low),
            pltpu.VMEM((TILES, PIECE, width), low),
            pltpu.VMEM((TILES,) + cut, low),
            pltpu.VMEM((tokens, width), low),
            pltpu.VMEM((width, tokens), low),
            pltpu.VMEM((width, tokens), low),
            pltpu.VMEM((width, tokens), low),
            pltpu.VMEM((tokens, width), low),
            pltpu.VMEM((tokens, width), low),
            pltpu.VMEM((tokens, width), low),
            pltpu.VMEM((tokens, width), low),
            pltpu.VMEM((2, tokens, width), low),
            pltpu.VMEM((2, width, tokens), low),
            dma((3,)),
            dma((2,)),
            dma((8,)),
            dma((2, 3)),
            dma((2, 2)),
            dma((PAIRS,)),
            dma((3,)),
            dma((3,)),
            dma((3, units, 2)),
            dma((3, units, 2)),
            dma((units, 2)),
            dma((units, 2)),
            dma((units, 2)),
            dma((units, 2)),
            dma((units,)),
            dma((units,)),
        ],
        compiler_params=pltpu.CompilerParams(
            collective_id=0, has_side_effects=True, vmem_limit_bytes=63 * 2**20
        ),
        name="gather_and_forward",
    )(counts, lengths, owners, bias, gain, x, cotangent, master.reshape(SLOTS * width, width))


BACK_PLAN = (
    (),
    (),
    (
        ("core", 0),
    ),
    (
        ("far", 0),
    ),
    (
        ("core", 1),
    ),
    (
        ("far", 1),
        ("mid", 0),
    ),
    (
        ("core", 2),
    ),
    (
        ("far", 2),
        ("end", 0),
    ),
    (
        ("mid", 1),
        ("core", 3),
    ),
    (
        ("mid", 2),
    ),
    (
        ("middle", 0),
        ("end", 1),
        ("far", 3),
    ),
    (),
    (
        ("core", 4),
        ("total", 0),
        ("middle", 1),
        ("end", 2),
        ("mid", 3),
    ),
    (),
    (
        ("end", 3),
        ("far", 4),
    ),
    (
        ("middle", 2),
        ("total", 1),
    ),
    (
        ("core", 5),
        ("mid", 4),
        ("middle", 3),
    ),
    (
        ("far", 5),
        ("total", 2),
        ("end", 4),
    ),
    (
        ("core", 6),
        ("middle", 4),
        ("mid", 5),
        ("total", 3),
    ),
    (
        ("far", 6),
        ("take", 0),
        ("end", 5),
    ),
    (
        ("core", 7),
        ("total", 4),
        ("mid", 6),
        ("far", 7),
        ("middle", 5),
        ("take", 3),
        ("sum", 0),
        ("end", 6),
        ("take", 1),
        ("mid", 7),
        ("take", 4),
        ("take", 2),
        ("deliver", 0),
        ("total", 5),
        ("sum", 1),
        ("take", 5),
        ("middle", 6),
        ("end", 7),
        ("deliver", 1),
        ("input", 0),
        ("total", 6),
        ("sum", 2),
        ("take", 6),
        ("deliver", 2),
        ("middle", 7),
        ("total", 7),
        ("take", 7),
        ("deliver", 3),
        ("input", 1),
    ),
)


COLUMNS = ((0, 256), (256, 256), (512, 128), (640, 128))


def backward_and_reduce(
    owners,
    p_ref,
    q_ref,
    k_ref,
    v_ref,
    inverse_ref,
    gain_ref,
    late_ref,
    ctx_hbm,
    x_turned_hbm,
    ctx_turned_hbm,
    hidden_hbm,
    active_hbm,
    slope_hbm,
    down_hbm,
    second_hbm,
    hat_hbm,
    w_hbm,
    input_hbm,
    slot_grad,
    vec_out,
    w_part,
    acc,
    hidden_then_x,
    active_then_ctx,
    down_then_branch,
    ctx_ref,
    grad_ctx_ref,
    hat_ref,
    slope_then_query,
    up_then_key,
    value_buf,
    part,
    from_core,
    from_far,
    from_mid,
    from_end,
    from_middle,
    total,
    snap,
    outbox,
    vec_now,
    vec_in,
    holds,
    keeps,
    load_sem,
    keep_sem,
    w_sem,
    core_send,
    core_recv,
    far_send,
    far_recv,
    mid_send,
    mid_recv,
    z_send,
    z_recv,
    vec_send,
    vec_recv,
    out_send,
    out_recv,
):
    step = pl.program_id(0)
    inner = jnp.maximum(step - 4, 0)
    quad, pair, block = inner // 4, lax.rem(inner, 4) // 2, lax.rem(inner, 2)
    me = lax.axis_index("dp")
    z, y, x, core = place(me)
    in_plane = lax.rem(me, PLANE)
    sibling = me + 1 - 2 * core
    x_peer = me + 2 - 4 * x
    y_peer = me + 4 - 8 * y
    z_targets = along_z(z, in_plane)
    is_end = (z == 0) | (z == 3)
    is_middle = (z == 1) | (z == 2)

    def tiles_of(batch):
        if batch < 4:
            return w_part, 4 + 2 * batch, 2, slice(None)
        return part, 0, 4, pl.ds(*COLUMNS[batch - 4])

    def halves(batch, turned):
        ref, first, count, cols = tiles_of(batch)
        return ref, pl.ds(first + turned * count // 2, count // 2), cols

    def core_copy(batch):
        ref, first, count, cols = tiles_of(batch)
        tiles = pl.ds(first, count)
        return remote(
            ref.at[tiles, 1 - core, :, :, :, cols],
            from_core.at[tiles, :, :, :, cols],
            core_send.at[batch],
            core_recv.at[batch],
            sibling,
        )

    def far_copies(batch):
        copies = []
        for turned in range(2):
            ref, tiles, cols = halves(batch, turned)
            src = ref.at[tiles, core, :, 1 - y, :, cols] if turned else ref.at[tiles, core, 1 - x, :, :, cols]
            copies.append(
                remote(
                    src,
                    from_far.at[tiles, :, :, cols],
                    far_send.at[batch, turned],
                    far_recv.at[batch, turned],
                    y_peer if turned else x_peer,
                )
            )
        return copies

    def mid_copies(batch):
        copies = []
        for turned in range(2):
            ref, tiles, cols = halves(batch, turned)
            src = ref.at[tiles, core, 1 - x, y, :, cols] if turned else ref.at[tiles, core, x, 1 - y, :, cols]
            copies.append(
                remote(
                    src,
                    from_mid.at[tiles, :, cols],
                    mid_send.at[batch, turned],
                    mid_recv.at[batch, turned],
                    x_peer if turned else y_peer,
                )
            )
        return copies

    def z_copy(batch, stage):
        ref, first, count, cols = tiles_of(batch)
        tiles = pl.ds(first, count)
        if stage == 2:
            src, dst = total.at[tiles, :, cols], total.at[tiles, :, cols]
        else:
            src = ref.at[tiles, core, x, y, :, cols]
            dst = (from_middle if stage else from_end).at[tiles, :, cols]
        return remote(src, dst, z_send.at[stage, batch], z_recv.at[stage, batch], z_targets[stage])

    def give_core(batch):
        core_copy(batch).start()

    def give_far(batch):
        core_copy(batch).wait_recv()
        ref, first, count, cols = tiles_of(batch)
        for tile in range(first, first + count):
            ref[tile, core, :, :, :, cols] = ref[tile, core, :, :, :, cols] + from_core[tile, :, :, :, cols]
        start(far_copies(batch))

    def give_mid(batch):
        arrive(far_copies(batch))
        for turned in range(2):
            ref, tiles, cols = halves(batch, turned)
            if turned:
                ref[tiles, core, :, y, :, cols] = ref[tiles, core, :, y, :, cols] + from_far[tiles, :, :, cols]
            else:
                ref[tiles, core, x, :, :, cols] = ref[tiles, core, x, :, :, cols] + from_far[tiles, :, :, cols]
        start(mid_copies(batch))

    def add_piece(batch, other):
        ref, first, count, cols = tiles_of(batch)
        tiles = pl.ds(first, count)
        return ref[tiles, core, x, y, :, cols] + other[tiles, :, cols]

    def give_end(batch):
        arrive(mid_copies(batch))
        ref, first, count, cols = tiles_of(batch)
        ref[pl.ds(first, count), core, x, y, :, cols] = add_piece(batch, from_mid)

        @pl.when(is_end)
        def _():
            z_copy(batch, 0).start()

    def give_middle(batch):
        @pl.when(is_middle)
        def _():
            z_copy(batch, 0).wait_recv()
            ref, first, count, cols = tiles_of(batch)
            ref[pl.ds(first, count), core, x, y, :, cols] = add_piece(batch, from_end)
            z_copy(batch, 1).start()

    def give_total(batch):
        @pl.when(is_middle)
        def _():
            z_copy(batch, 1).wait_recv()
            _, first, count, cols = tiles_of(batch)
            total[pl.ds(first, count), :, cols] = add_piece(batch, from_middle)
            z_copy(batch, 2).start()

    def take_total(batch):
        @pl.when(is_end)
        def _():
            z_copy(batch, 2).wait_recv()

    def deliver(share):
        first, count = COLUMNS[share]
        cols, there = pl.ds(first, count), pl.ds(first % 256, count)
        snap[:, :, 0:count] = total[:, :, cols]

        def fill(at, carry):
            value = snap[holds[at], :, 0:count]
            outbox[first // 256, at, :, there] = jnp.where(keeps[at] > 0, value, jnp.zeros_like(value))
            return carry

        lax.fori_loop(0, 2 * PLANE, fill, 0)

        def send(hop, carry):
            target = lax.rem(in_plane + hop, PLANE)
            remote(
                outbox.at[first // 256, pl.ds(2 * target, 2), :, there],
                slot_grad.at[:, core, x, y, :, cols],
                out_send.at[share],
                out_recv.at[share],
                z * PLANE + target,
            ).start()
            return carry

        lax.fori_loop(1, PLANE, send, 0)
        keep_copy(share).start()

    def keep_copy(share):
        first, count = COLUMNS[share]
        return pltpu.make_async_copy(
            outbox.at[first // 256, pl.ds(2 * in_plane, 2), :, pl.ds(first % 256, count)],
            slot_grad.at[:, core, x, y, :, pl.ds(first, count)],
            keep_sem.at[share],
        )

    def vec_copies(stage):
        if stage < 3:
            hops = [(stage, (sibling, x_peer, y_peer)[stage])]
        else:
            hops = [
                (2 + hop, lax.rem(z + hop, 4) * PLANE + in_plane) for hop in range(1, 4)
            ]
        return [
            remote(vec_now.at[stage], vec_in.at[at], vec_send.at[at], vec_recv.at[at], device)
            for at, device in hops
        ]

    def vec_next(stage):
        arrive(vec_copies(stage))
        vec_now[stage + 1] = vec_now[stage] + vec_in[stage]
        start(vec_copies(stage + 1))

    def input_store():
        return pltpu.make_async_copy(acc, input_hbm, load_sem.at[4])

    def load(at):
        src, dst = (
            (hidden_hbm, hidden_then_x),
            (down_hbm, down_then_branch),
            (second_hbm, acc),
            (hat_hbm, hat_ref),
            None,
            None,
            None,
            None,
            (x_turned_hbm, hidden_then_x),
            (ctx_turned_hbm, active_then_ctx),
            None,
            None,
            (ctx_hbm, ctx_ref),
        )[at]
        return pltpu.make_async_copy(src, dst, load_sem.at[at])

    def tile_load(tile, side):
        src, dst = ((slope_hbm, slope_then_query), (active_hbm, active_then_ctx))[side]
        return pltpu.make_async_copy(src.at[tile], dst, load_sem.at[10 + side])

    def w_load(at):
        return pltpu.make_async_copy(w_hbm.at[at], w_part.at[at], w_sem.at[at])

    def weight(at, cols=slice(None)):
        value = w_part[at, :, :, :, :, cols]
        return value.reshape(8 * PIECE, value.shape[-1])

    def input_rows(half):
        rows = slice(ROWS * half, ROWS * half + ROWS)
        more = acc[rows, :]
        for at, buf in enumerate((slope_then_query, up_then_key, value_buf)):
            more = more + dot_back(buf[rows, :], weight(at))
        acc[rows, :] = more
        if half == 1:
            input_store().start()

    actions = {
        "core": give_core,
        "far": give_far,
        "mid": give_mid,
        "end": give_end,
        "middle": give_middle,
        "total": give_total,
        "take": take_total,
        "deliver": deliver,
        "sum": vec_next,
        "input": input_rows,
    }

    @pl.when(step == 0)
    def _():
        start([load(1), tile_load(0, 0), w_load(5), w_load(4)])
        for at in range(2 * PLANE):
            tile_here, kept = jnp.int32(0), jnp.int32(0)
            for tile in range(TILES):
                place_of = SLOTS * owners[tile] + slot_number(owners, tile)
                match = place_of == z * 2 * PLANE + at
                tile_here = tile_here + jnp.where(match, POSITIONS.index(tile), 0)
                kept = kept + jnp.where(match, 1, 0)
            holds[at] = tile_here
            keeps[at] = kept
        vec_now[0] = late_ref[...]
        greet(z, in_plane)

    def serve(points):
        for at in points:
            if BACK_PLAN[at]:

                @pl.when(step == (at // 2 if at < 8 else at - 4))
                def _():
                    for name, number in BACK_PLAN[at]:
                        actions[name](number)

    serve(range(0, 8, 2))

    @pl.when(step < 4)
    def _():
        tile_load(step, 0).wait()
        w_load(5 + 2 * step).wait()

        @pl.when(step == 0)
        def _():
            load(1).wait()
            start([load(2), tile_load(0, 1), load(0)])

        @pl.when(step < 3)
        def _():
            start([w_load(7 + 2 * step), w_load(6 + 2 * step)])

        @pl.when(step == 1)
        def _():
            load(3).start()

        @pl.when(step == 2)
        def _():
            w_load(3).start()

        @pl.when(step == 3)
        def _():
            start([load(12), w_load(0), w_load(1), w_load(2)])

        for half in range(2):
            rows = slice(ROWS * half, ROWS * half + ROWS)
            back = dot_back(down_then_branch[rows, :], weight(5 + 2 * step))
            up_low = (back * slope_then_query[rows, :].astype(jnp.float32)).astype(jnp.bfloat16)
            up_then_key[rows, :] = up_low
            vec_now[0, pl.ds(3 + step, 1), :] += columns_total(up_low.astype(jnp.float32))

        @pl.when(step < 3)
        def _():
            tile_load(step + 1, 0).start()

        w_load(4 + 2 * step).wait()

        @pl.when(step == 0)
        def _():
            load(2).wait()
            load(0).wait()

        for half in range(2):
            rows = slice(ROWS * half, ROWS * half + ROWS)
            acc[rows, :] = acc[rows, :] + dot_back(up_then_key[rows, :], weight(4 + 2 * step))

    serve(range(1, 8, 2))

    @pl.when(step < 4)
    def _():
        tile_load(step, 1).wait()
        by_down = dot(active_then_ctx[...], down_then_branch[...]).astype(jnp.bfloat16)
        w_part[5 + 2 * step] = by_down.reshape(2, 2, 2, PIECE, 8 * PIECE)

        @pl.when(step < 3)
        def _():
            tile_load(step + 1, 1).start()

        by_up = dot(hidden_then_x[...], up_then_key[...]).astype(jnp.bfloat16)
        w_part[4 + 2 * step] = by_up.reshape(2, 2, 2, PIECE, 8 * PIECE)

    @pl.when(step == 3)
    def _():
        start([load(8), load(9)])
        load(3).wait()
        w_load(3).wait()
        for half in range(2):
            rows = slice(ROWS * half, ROWS * half + ROWS)
            grad_hidden, hat = acc[rows, :], hat_ref[rows, :].astype(jnp.float32)
            vec_now[0, 10:11, :] += columns_total(grad_hidden * hat)
            vec_now[0, 8:9, :] += columns_total(grad_hidden)
            first = normalize_back(grad_hidden * gain_ref[0:1, :], hat, inverse_ref[rows, :])
            acc[rows, :] = first
            branch_low = first.astype(jnp.bfloat16)
            down_then_branch[rows, :] = branch_low
            vec_now[0, 2:3, :] += columns_total(branch_low.astype(jnp.float32))
            grad_ctx_ref[rows, :] = dot_back(branch_low, weight(3)).astype(jnp.bfloat16)

    serve(range(8, 20))

    here = pl.ds(pl.multiple_of(block * ROWS, ROWS), ROWS)
    quad_cols = pl.ds(pl.multiple_of(quad * 256, 256), 256)

    @pl.when(step == 4)
    def _():
        load(12).wait()
        for at in range(3):
            w_load(at).wait()

    pair_cols = pl.ds(pl.multiple_of(quad * 256 + pair * 128, 128), 128)
    grad_bufs = (slope_then_query, up_then_key, value_buf)

    @pl.when(step >= 4)
    def _():
        grads = attend_back_pair(
            grad_ctx_ref[here, pair_cols],
            ctx_ref[here, pair_cols],
            p_ref.at[0],
            q_ref[...],
            k_ref[...],
            v_ref[...],
        )
        for buf, grad in zip(grad_bufs, grads):
            buf[here, pair_cols] = grad
        vec_now[0, 0:1, pair_cols] += columns_total(grads[0].astype(jnp.float32))
        vec_now[0, 1:2, pair_cols] += columns_total(grads[2].astype(jnp.float32))

    @pl.when(step == 7)
    def _():
        load(8).wait()
        load(9).wait()

    def attention_grads(cols):
        for tile in range(4):
            if tile < 3:
                value = dot(hidden_then_x[...], grad_bufs[tile][:, cols])
            else:
                value = dot(active_then_ctx[...], down_then_branch[:, cols])
            value = value.astype(jnp.bfloat16)
            part[tile, :, :, :, :, cols] = value.reshape(2, 2, 2, PIECE, value.shape[-1])

    @pl.when((step >= 4) & (block == 1) & (pair == 1) & (quad < 2))
    def _():
        attention_grads(quad_cols)

    @pl.when((step >= 4) & (block == 1) & (quad == 2))
    def _():
        attention_grads(pair_cols)

    @pl.when(step == 15)
    def _():
        start(vec_copies(0))
        for name, number in BACK_PLAN[-1]:
            actions[name](number)
        arrive(vec_copies(3))
        summed = jnp.zeros(vec_out.shape, jnp.float32)
        for origin in range(4):
            hop = lax.rem(z - origin + 4, 4)
            summed = summed + jnp.where(hop == 0, vec_now[3], vec_in[2 + jnp.maximum(hop, 1)])
        vec_out[...] = summed
        for batch in range(4 + len(COLUMNS)):
            for copy in [core_copy(batch)] + far_copies(batch) + mid_copies(batch):
                copy.wait_send()

            @pl.when(is_end)
            def _():
                z_copy(batch, 0).wait_send()

            @pl.when(is_middle)
            def _():
                z_copy(batch, 1).wait_send()
                z_copy(batch, 2).wait_send()

        for stage in range(4):
            for copy in vec_copies(stage):
                copy.wait_send()
        input_store().wait()
        for share, (first, count) in enumerate(COLUMNS):
            keep_copy(share).wait()
            most = outbox.at[first // 256, pl.ds(0, 2 * PLANE - 2), :, pl.ds(first % 256, count)]
            pltpu.make_async_copy(most, most, out_recv.at[share]).wait()
            pltpu.make_async_copy(most, most, out_send.at[share]).wait()


def backward_and_reduced(
    owners,
    probs,
    query,
    keyed,
    valued,
    inverse,
    gain,
    late_sums,
    context,
    x_turned,
    ctx_turned,
    hidden,
    active,
    slope,
    grad_down,
    grad_second,
    hat,
    weights,
):
    tokens, width = grad_down.shape
    low, high = jnp.bfloat16, jnp.float32
    shaped = jax.ShapeDtypeStruct
    smem = pl.BlockSpec(memory_space=pltpu.SMEM)
    any_space = pl.BlockSpec(memory_space=pl.ANY)
    dma = pltpu.SemaphoreType.DMA
    once = pl.Buffered(1)

    def at(step):
        inner = jnp.maximum(step - 4, 0)
        return lax.rem(inner, 2), inner // 4 * 2 + lax.rem(inner, 4) // 2

    pair = pl.BlockSpec((ROWS, 128), at)
    sums = pl.BlockSpec((16, width), lambda i: (0, 0))
    cut = (2, 2, 2, PIECE, width)
    input_grad, slot_grads, vector_sums = pl.pallas_call(
        backward_and_reduce,
        grid=(16,),
        out_shape=(
            shaped((tokens, width), high),
            shaped((SLOTS,) + cut, low),
            shaped((16, width), high),
        ),
        in_specs=[smem, pl.BlockSpec((1, 2, ROWS, ROWS), lambda i: (*at(i), 0, 0))]
        + [pair] * 3
        + [
            pl.BlockSpec((tokens, 1), lambda i: (0, 0), pipeline_mode=once),
            pl.BlockSpec(gain.shape, lambda i: (0, 0)),
            sums,
        ]
        + [any_space] * 10,
        out_specs=(any_space, any_space, sums),
        scratch_shapes=[
            pltpu.VMEM((TILES,) + cut, low),
            pltpu.VMEM((tokens, width), high),
            pltpu.VMEM((width, tokens), low),
            pltpu.VMEM((width, tokens), low),
            pltpu.VMEM((tokens, width), low),
            pltpu.VMEM((tokens, width), low),
            pltpu.VMEM((tokens, width), low),
            pltpu.VMEM((tokens, width), low),
            pltpu.VMEM((tokens, width), low),
            pltpu.VMEM((tokens, width), low),
            pltpu.VMEM((tokens, width), low),
            pltpu.VMEM((4,) + cut, low),
            pltpu.VMEM((TILES,) + cut[1:], low),
            pltpu.VMEM((TILES,) + cut[2:], low),
            pltpu.VMEM((TILES,) + cut[3:], low),
            pltpu.VMEM((TILES,) + cut[3:], low),
            pltpu.VMEM((TILES,) + cut[3:], low),
            pltpu.VMEM((TILES,) + cut[3:], low),
            pltpu.VMEM((TILES, PIECE, 256), low),
            pltpu.VMEM((3, 2 * PLANE, PIECE, 256), low),
            pltpu.VMEM((4, 16, width), high),
            pltpu.VMEM((6, 16, width), high),
            pltpu.SMEM((2 * PLANE,), jnp.int32),
            pltpu.SMEM((2 * PLANE,), jnp.int32),
            dma((13,)),
            dma((4,)),
            dma((TILES,)),
            dma((8,)),
            dma((8,)),
            dma((8, 2)),
            dma((8, 2)),
            dma((8, 2)),
            dma((8, 2)),
            dma((3, 8)),
            dma((3, 8)),
            dma((6,)),
            dma((6,)),
            dma((4,)),
            dma((4,)),
        ],
        compiler_params=pltpu.CompilerParams(
            collective_id=1, has_side_effects=True, vmem_limit_bytes=63 * 2**20
        ),
        name="backward_and_reduce",
    )(
        owners,
        probs,
        query,
        keyed,
        valued,
        inverse,
        gain,
        late_sums,
        context,
        x_turned,
        ctx_turned,
        hidden,
        active,
        slope,
        grad_down,
        grad_second,
        hat,
        weights,
    )
    return input_grad, slot_grads.reshape(SLOTS, width, width), vector_sums


def collected_tiles(tile_low, owners, slots):
    mine = owners == lax.axis_index("dp")
    local = jnp.where(mine[:, None, None], tile_low[slots], jnp.zeros((), tile_low.dtype))
    return lax.psum(local, "dp")


def summed_over_slice(parts, vector_terms, owners, slots):
    myself = lax.axis_index("dp")

    def add(held, items):
        part, owner, slot = items
        total = lax.psum(part.astype(jnp.float32), "dp")
        here = (owner == myself) & (slot == jnp.arange(SLOTS, dtype=jnp.int32))
        return held + jnp.where(here[:, None, None], total[None], 0.0), None

    empty = jnp.zeros((SLOTS,) + parts.shape[1:], jnp.float32)
    return lax.scan(add, empty, (parts, owners, slots))[0], lax.psum(vector_terms, "dp")


def body(
    inputs,
    cotangent,
    counts,
    lengths,
    owners,
    tile_master,
    tile_first,
    tile_second,
    tile_ema,
    bias_vals,
    gain_vals,
    vector_first,
    vector_second,
    vector_ema,
):
    tokens = inputs.shape[0]
    small = lax.axis_size("dp") == GROUP
    gain_scale = float(tokens * lax.axis_size("dp")) ** (-0.5)
    if small:
        (
            query,
            keyed,
            valued,
            probs,
            context,
            x_turned,
            ctx_turned,
            hidden,
            active,
            slope,
            grad_down,
            mixed,
            grad_second,
            hat,
            weights,
            inverse,
            late_sums,
        ) = gathered_and_forwarded(
            counts,
            lengths,
            owners,
            bias_vals,
            gain_vals,
            inputs,
            cotangent,
            tile_master,
        )
        input_grad, slot_grads, full_sums = backward_and_reduced(
            owners,
            probs,
            query,
            keyed,
            valued,
            inverse,
            gain_vals,
            late_sums,
            context,
            x_turned,
            ctx_turned,
            hidden,
            active,
            slope,
            grad_down,
            grad_second,
            hat,
            weights,
        )
    else:
        slots = tile_slots(owners)
        vectors = jnp.concatenate([bias_vals, gain_vals], 0)
        weights = collected_tiles(tile_master[0].astype(jnp.bfloat16), owners, slots)
        query, keyed, valued, probs, context, hat, inverse = attended(
            counts, lengths, inputs, weights, vectors
        )
        mixed, grad_first, grad_branch, grad_context, up_grads, down_grads, late_sums = fed_forward_both(
            counts, lengths, hat, inverse, cotangent, weights, vectors
        )
        input_grad, early_grads, early_sums = attended_back(
            probs, query, keyed, valued, inputs, context, grad_context, grad_branch, grad_first, weights
        )
        parts = jnp.concatenate([early_grads, up_grads, down_grads], 0)
        slot_grads, full_sums = summed_over_slice(parts, late_sums + early_sums, owners, slots)
    return updated(
        gain_scale,
        slot_grads,
        tile_master,
        tile_first,
        tile_second,
        tile_ema,
        full_sums,
        bias_vals,
        gain_vals,
        vector_first,
        vector_second,
        vector_ema,
        mixed,
        input_grad,
    )


def solution(mesh):
    placed = (
        P("dp", None),
        P("dp", None),
        P("dp", None),
        P("dp", None),
        P(),
        P("dp", None, None, None),
        P("dp", None, None, None),
        P("dp", None, None, None),
        P("dp", None, None, None),
        P(),
        P(),
        P(),
        P(),
        P(),
    )
    return jax.shard_map(
        body,
        mesh=mesh,
        in_specs=placed,
        out_specs=(
            P("dp", None),
            P("dp", None),
            P("dp", None, None, None),
            P("dp", None, None, None),
            P("dp", None, None, None),
            P("dp", None, None, None),
            P("dp", None, None, None),
            P(),
            P(),
            P(),
            P(),
        ),
        check_vma=False,
    )
```

```python
import functools

import jax
import jax.numpy as jnp
from jax import lax
from jax.experimental import pallas as pl
from jax.experimental.pallas import tpu as pltpu
from jax.sharding import PartitionSpec as P

HEADS = 12
BUCKET = 128
SLOTS = 2
TILES = 12
VROWS = 12
STEP = 5

norm_epsilon = 1e-12
tile_rate = 0.03
vector_rate = 0.2
first_decay = 0.5
second_decay = 0.5
adam_epsilon = 1e-08
weight_decay = 0.01
average_rate = 0.9


def tile_slots(owners):
    order = jnp.arange(owners.shape[0], dtype=jnp.int32)
    same = owners[:, None] == owners[None, :]
    earlier = order[None, :] < order[:, None]
    return jnp.sum((same & earlier).astype(jnp.int32), 1)


def adam_update(param, grad, first, second, rate):
    first_new = first_decay * first + (1.0 - first_decay) * grad
    second_new = second_decay * second + (1.0 - second_decay) * grad * grad
    first_hat = first_new / (1.0 - first_decay**STEP)
    second_hat = second_new / (1.0 - second_decay**STEP)
    param_new = param - rate * (
        first_hat / (jnp.sqrt(second_hat) + adam_epsilon) + weight_decay * param
    )
    return (param_new, first_new, second_new)


ROWS = 4 * BUCKET
TAIL_RATE = 0.28
TAIL_SERIES = (
    0.11615256574707405,
    0.06981038475559553,
    0.2631359597579608,
    -0.22983675561378278,
    0.38546775012288165,
    -0.10472989053809521,
)
INV_SQRT_TAU = 0.3989422804014327
ALLOWED = 3.0e38
BARRED = -1000000000.0


def dot(left, right):
    return jnp.dot(left, right, preferred_element_type=jnp.float32)


def dot_back(left, right):
    return lax.dot_general(
        left, right, (((1,), (1,)), ((), ())), preferred_element_type=jnp.float32
    )


def outer(left, right):
    return lax.dot_general(
        left, right, (((0,), (0,)), ((), ())), preferred_element_type=jnp.float32
    )


def passage_facts(counts, lengths, position):
    places = lengths.shape[1]
    big_end = counts[0, 0]
    mid_end = big_end + counts[0, 1]
    all_end = mid_end + counts[0, 2]
    start = jnp.int32(0)
    member = jnp.zeros(position.shape, jnp.int32)
    usable = jnp.zeros(position.shape, jnp.int32)
    for number in range(places):
        size = jnp.where(
            number < big_end,
            4 * BUCKET,
            jnp.where(number < mid_end, 2 * BUCKET, jnp.where(number < all_end, BUCKET, 0)),
        )
        inside = (position >= start) & (position < start + size)
        live = inside & (position < start + lengths[0, number])
        member = jnp.where(inside, number + 1, member)
        usable = jnp.where(live, 1, usable)
        start = start + size
    passage = jnp.where(member > 0, member - 1, places + position // BUCKET)
    return usable, passage


def normalize(values):
    center = jnp.mean(values, -1, keepdims=True)
    centered = values - center
    spread = jnp.mean(centered * centered, -1, keepdims=True)
    inverse = lax.rsqrt(spread + norm_epsilon)
    return centered * inverse, inverse


def normalize_back(grad, hat, inverse):
    center = jnp.mean(grad, -1, keepdims=True)
    along = jnp.mean(grad * hat, -1, keepdims=True)
    return inverse * (grad - center - hat * along)


def columns_total(values):
    return jnp.sum(values, 0, keepdims=True)


def attention_caps(counts, lengths, block):
    at_row = lax.broadcasted_iota(jnp.int32, (ROWS, 1), 0) + block * ROWS
    at_column = lax.broadcasted_iota(jnp.int32, (1, ROWS), 1) + block * ROWS
    _, passage_row = passage_facts(counts, lengths, at_row)
    usable_column, passage_column = passage_facts(counts, lengths, at_column)
    allowed = (passage_row == passage_column) & ((usable_column == 1) | (at_row == at_column))
    return jnp.where(allowed, ALLOWED, BARRED)


def attend_quad(quad, weight, x_ref, vec_ref, cap_ref, q_ref, k_ref, v_ref, p_ref, ctx_ref):
    cols = pl.ds(pl.multiple_of(quad * 256, 256), 256)
    x = x_ref[...]
    query = (dot(x, weight(0, cols)) + vec_ref[0:1, cols]).astype(jnp.bfloat16)
    query = query * jnp.bfloat16(0.125)
    keyed = dot(x, weight(1, cols)).astype(jnp.bfloat16)
    valued = (dot(x, weight(2, cols)) + vec_ref[1:2, cols]).astype(jnp.bfloat16)
    q_ref[...] = query
    k_ref[...] = keyed
    v_ref[...] = valued
    low_half = lax.broadcasted_iota(jnp.int32, (1, 128), 1) < 64
    for pair in range(2):
        part = slice(128 * pair, 128 * pair + 128)
        contexts = []
        for head in range(2):
            here = low_half if head == 0 else ~low_half
            mine = jnp.where(here, query[:, part], jnp.zeros_like(query[:, part]))
            scores = jnp.minimum(dot_back(mine, keyed[:, part]), cap_ref[...])
            exponent = jnp.exp(scores - jnp.max(scores, -1, keepdims=True))
            inverse = 1.0 / jnp.sum(exponent, -1, keepdims=True)
            probability = (exponent * inverse).astype(jnp.bfloat16)
            p_ref[0, 2 * pair + head] = probability
            contexts.append(dot(probability, valued[:, part]))
        both = jnp.where(low_half, contexts[0], contexts[1]).astype(jnp.bfloat16)
        ctx_ref[:, pl.ds(pl.multiple_of(quad * 256 + 128 * pair, 128), 128)] = both


def close_block(w_out, x_ref, vec_ref, ctx_ref, hat_ref, inverse_ref):
    branch = dot(ctx_ref[...], w_out) + vec_ref[2:3, :]
    hat_ref[...], inverse_ref[...] = normalize(x_ref[...].astype(jnp.float32) + branch)


def attend_back_pair(pull, level_from, p_ref, query, keyed, valued):
    low_half = lax.broadcasted_iota(jnp.int32, (1, 128), 1) < 64
    along = pull.astype(jnp.float32) * level_from.astype(jnp.float32)
    by_query, by_key, by_value = [], [], []
    for head in range(2):
        mask = low_half if head == 0 else ~low_half
        mine = jnp.where(mask, pull, jnp.zeros_like(pull))
        level = jnp.sum(jnp.where(mask, along, 0.0), -1, keepdims=True)
        probability = p_ref[head]
        grad_prob = dot_back(mine, valued)
        grad_scores = (probability.astype(jnp.float32) * (grad_prob - level)).astype(jnp.bfloat16)
        by_query.append(dot(grad_scores, keyed))
        by_key.append(outer(grad_scores, query))
        by_value.append(outer(probability, pull))
    grad_query = jnp.where(low_half, by_query[0], by_query[1]) * 0.125
    grad_key = jnp.where(low_half, by_key[0], by_key[1])
    grad_value = jnp.where(low_half, by_value[0], by_value[1])
    return [value.astype(jnp.bfloat16) for value in (grad_query, grad_key, grad_value)]


def gelu_parts(up):
    near = 1.0 / (1.0 + TAIL_RATE * jnp.abs(up))
    decay = jnp.exp(up * up * -0.5)
    series = jnp.full_like(near, TAIL_SERIES[-1])
    for term in TAIL_SERIES[-2::-1]:
        series = series * near + term
    tail = series * near * decay
    share = jnp.where(up < 0.0, tail, 1.0 - tail)
    slope = share + up * (decay * INV_SQRT_TAU)
    return (up * share).astype(jnp.bfloat16), slope


def attend_forward(
    counts,
    lengths,
    x_ref,
    w_hbm,
    vec_ref,
    q_ref,
    k_ref,
    v_ref,
    p_ref,
    ctx_ref,
    hat_ref,
    inverse_ref,
    w_buf,
    cap_ref,
    w_sem,
):
    block, quad = pl.program_id(0), pl.program_id(1)
    loads = [pltpu.make_async_copy(w_hbm.at[at], w_buf.at[at], w_sem.at[at]) for at in range(4)]

    @pl.when((block == 0) & (quad == 0))
    def _():
        for load in loads:
            load.start()
        for load in loads:
            load.wait()

    @pl.when(quad == 0)
    def _():
        cap_ref[...] = attention_caps(counts, lengths, block)

    def weight(at, cols):
        return w_buf[at, :, cols]

    attend_quad(quad, weight, x_ref, vec_ref, cap_ref, q_ref, k_ref, v_ref, p_ref, ctx_ref)

    @pl.when(quad == 2)
    def _():
        close_block(w_buf[3], x_ref, vec_ref, ctx_ref, hat_ref, inverse_ref)


def attended(counts, lengths, x, weights, vectors):
    tokens, width = x.shape
    blocks = tokens // ROWS
    low = jnp.bfloat16
    smem = pl.BlockSpec(memory_space=pltpu.SMEM)
    quad = pl.BlockSpec((ROWS, 256), lambda b, h: (b, h))
    rows = pl.BlockSpec((ROWS, width), lambda b, h: (b, 0))
    shaped = jax.ShapeDtypeStruct
    return pl.pallas_call(
        attend_forward,
        grid=(blocks, 3),
        out_shape=(
            shaped((tokens, width), low),
            shaped((tokens, width), low),
            shaped((tokens, width), low),
            shaped((blocks, HEADS, ROWS, ROWS), low),
            shaped((tokens, width), low),
            shaped((tokens, width), jnp.float32),
            shaped((tokens, 1), jnp.float32),
        ),
        in_specs=[
            smem,
            smem,
            rows,
            pl.BlockSpec(memory_space=pl.ANY),
            pl.BlockSpec((VROWS, width), lambda b, h: (0, 0)),
        ],
        out_specs=(
            quad,
            quad,
            quad,
            pl.BlockSpec((1, 4, ROWS, ROWS), lambda b, h: (b, h, 0, 0)),
            rows,
            rows,
            pl.BlockSpec((ROWS, 1), lambda b, h: (b, 0)),
        ),
        scratch_shapes=[
            pltpu.VMEM((4, width, width), low),
            pltpu.VMEM((ROWS, ROWS), jnp.float32),
            pltpu.SemaphoreType.DMA((4,)),
        ],
        compiler_params=pltpu.CompilerParams(vmem_limit_bytes=56 * 2**20),
        name="attend_forward",
    )(counts, lengths, x, weights, vectors)


def feed_forward_both(
    counts,
    lengths,
    hat_ref,
    inverse_ref,
    cot_ref,
    w_hbm,
    vec_ref,
    mixed_ref,
    first_ref,
    branch_ref,
    context_ref,
    up_grad_ref,
    down_grad_ref,
    sum_ref,
    w_buf,
    active_ref,
    up_ref,
    hidden_ref,
    down_ref,
    slope_ref,
    w_sem,
):
    step = pl.program_id(0)
    blocks = pl.num_programs(0) - 4
    loads = [
        pltpu.make_async_copy(w_hbm.at[3 + at], w_buf.at[at], w_sem.at[at]) for at in range(9)
    ]

    @pl.when(step == 0)
    def _():
        for load in loads[1:] + loads[:1]:
            load.start()
        sum_ref[...] = jnp.zeros_like(sum_ref)
        for load in loads[1:] + loads[:1]:
            load.wait()

    @pl.when(step < blocks)
    def _():
        here = pl.ds(pl.multiple_of(step * ROWS, ROWS), ROWS)
        at_row = lax.broadcasted_iota(jnp.int32, (ROWS, 1), 0) + step * ROWS
        live = passage_facts(counts, lengths, at_row)[0].astype(jnp.float32)
        hat = hat_ref[...]
        hidden = hat * vec_ref[10:11, :] + vec_ref[8:9, :]
        hidden_low = hidden.astype(jnp.bfloat16)
        hidden_ref[here, :] = hidden_low
        total = hidden + vec_ref[7:8, :]
        for tile in range(4):
            up = dot(hidden_low, w_buf[1 + tile]) + vec_ref[3 + tile : 4 + tile, :]
            active, slope = gelu_parts(up)
            slope_ref[tile] = slope.astype(jnp.bfloat16)
            active_ref[tile, here, :] = active
            total = total + dot(active, w_buf[5 + tile])
        hat_two, inverse_two = normalize(total)
        mixed_ref[...] = ((hat_two * vec_ref[11:12, :] + vec_ref[9:10, :]) * live).astype(jnp.bfloat16)
        grad_out = cot_ref[...].astype(jnp.float32) * live
        sum_ref[11:12, :] += columns_total(grad_out * hat_two)
        sum_ref[9:10, :] += columns_total(grad_out)
        second = normalize_back(grad_out * vec_ref[11:12, :], hat_two, inverse_two)
        down_low = second.astype(jnp.bfloat16)
        down_ref[here, :] = down_low
        sum_ref[7:8, :] += columns_total(down_low.astype(jnp.float32))
        grad_hidden = second
        for tile in range(4):
            pulled = dot_back(down_low, w_buf[5 + tile])
            up_low = (pulled * slope_ref[tile].astype(jnp.float32)).astype(jnp.bfloat16)
            up_ref[tile, here, :] = up_low
            sum_ref[3 + tile : 4 + tile, :] += columns_total(up_low.astype(jnp.float32))
            grad_hidden = grad_hidden + dot_back(up_low, w_buf[1 + tile])
        sum_ref[10:11, :] += columns_total(grad_hidden * hat)
        sum_ref[8:9, :] += columns_total(grad_hidden)
        grad_first = normalize_back(grad_hidden * vec_ref[10:11, :], hat, inverse_ref[...])
        first_ref[...] = grad_first
        branch_low = grad_first.astype(jnp.bfloat16)
        branch_ref[...] = branch_low
        sum_ref[2:3, :] += columns_total(branch_low.astype(jnp.float32))
        context_ref[...] = dot_back(branch_low, w_buf[0]).astype(jnp.bfloat16)

    @pl.when(step >= blocks)
    def _():
        tile = step - blocks
        up_grad_ref[0] = outer(hidden_ref[...], up_ref[tile]).astype(jnp.bfloat16)
        down_grad_ref[0] = outer(active_ref[tile], down_ref[...]).astype(jnp.bfloat16)


def fed_forward_both(counts, lengths, hat, inverse, cotangent, weights, vectors):
    tokens, width = hat.shape
    blocks = tokens // ROWS
    low = jnp.bfloat16
    smem = pl.BlockSpec(memory_space=pltpu.SMEM)
    shaped = jax.ShapeDtypeStruct

    def block_of(step):
        return jnp.minimum(step, blocks - 1)

    def tile_of(step):
        return jnp.maximum(step - blocks, 0)

    rows = pl.BlockSpec((ROWS, width), lambda i: (block_of(i), 0))
    tile = pl.BlockSpec((1, width, width), lambda i: (tile_of(i), 0, 0))
    return pl.pallas_call(
        feed_forward_both,
        grid=(blocks + 4,),
        out_shape=(
            shaped((tokens, width), low),
            shaped((tokens, width), jnp.float32),
            shaped((tokens, width), low),
            shaped((tokens, width), low),
            shaped((4, width, width), low),
            shaped((4, width, width), low),
            shaped((16, width), jnp.float32),
        ),
        in_specs=[
            smem,
            smem,
            rows,
            pl.BlockSpec((ROWS, 1), lambda i: (block_of(i), 0)),
            rows,
            pl.BlockSpec(memory_space=pl.ANY),
            pl.BlockSpec((VROWS, width), lambda i: (0, 0)),
        ],
        out_specs=(
            rows,
            rows,
            rows,
            rows,
            tile,
            tile,
            pl.BlockSpec((16, width), lambda i: (0, 0)),
        ),
        scratch_shapes=[
            pltpu.VMEM((9, width, width), low),
            pltpu.VMEM((4, tokens, width), low),
            pltpu.VMEM((4, tokens, width), low),
            pltpu.VMEM((tokens, width), low),
            pltpu.VMEM((tokens, width), low),
            pltpu.VMEM((4, ROWS, width), low),
            pltpu.SemaphoreType.DMA((9,)),
        ],
        compiler_params=pltpu.CompilerParams(vmem_limit_bytes=60 * 2**20),
        name="feed_forward_both",
    )(counts, lengths, hat, inverse, cotangent, weights, vectors)


def attend_backward(
    p_ref,
    q_ref,
    k_ref,
    v_ref,
    x_ref,
    ctx_ref,
    grad_ctx_ref,
    branch_ref,
    first_ref,
    w_ref,
    input_ref,
    grad_ref,
    sum_ref,
    pulled,
):
    step = pl.program_id(0)
    quad, block = step // 2, lax.rem(step, 2)
    here = pl.ds(pl.multiple_of(block * ROWS, ROWS), ROWS)
    cols = pl.ds(pl.multiple_of(quad * 256, 256), 256)

    @pl.when(step == 0)
    def _():
        sum_ref[...] = jnp.zeros_like(sum_ref)
        input_ref[...] = first_ref[...]

    for pair in range(2):
        half = slice(128 * pair, 128 * pair + 128)
        at = pl.ds(pl.multiple_of(quad * 256 + 128 * pair, 128), 128)
        heads = p_ref.at[0, pl.ds(2 * pair, 2)]
        grads = attend_back_pair(
            grad_ctx_ref[here, at], ctx_ref[here, at], heads, q_ref[:, half], k_ref[:, half], v_ref[:, half]
        )
        for number, grad in enumerate(grads):
            pulled[number, here, half] = grad
        sum_ref[0:1, at] += columns_total(grads[0].astype(jnp.float32))
        sum_ref[1:2, at] += columns_total(grads[2].astype(jnp.float32))

    more = input_ref[here, :]
    for at in range(3):
        more = more + dot_back(pulled[at, here, :], w_ref[at, :, cols])
    input_ref[here, :] = more

    @pl.when(block == 1)
    def _():
        for tile in range(3):
            grad_ref[tile, :, cols] = outer(x_ref[...], pulled[tile]).astype(jnp.bfloat16)
        grad_ref[3, :, cols] = outer(ctx_ref[...], branch_ref[:, cols]).astype(jnp.bfloat16)


def attended_back(probs, query, keyed, valued, x, context, grad_context, grad_branch, grad_first, weights):
    tokens, width = x.shape
    low = jnp.bfloat16
    shaped = jax.ShapeDtypeStruct
    once = pl.Buffered(1)
    quad = pl.BlockSpec((ROWS, 256), lambda i: (lax.rem(i, 2), i // 2))
    whole = pl.BlockSpec((tokens, width), lambda i: (0, 0), pipeline_mode=once)
    return pl.pallas_call(
        attend_backward,
        grid=(6,),
        out_shape=(
            shaped((tokens, width), jnp.float32),
            shaped((4, width, width), low),
            shaped((16, width), jnp.float32),
        ),
        in_specs=[
            pl.BlockSpec((1, 4, ROWS, ROWS), lambda i: (lax.rem(i, 2), i // 2, 0, 0)),
            quad,
            quad,
            quad,
            whole,
            whole,
            whole,
            whole,
            whole,
            pl.BlockSpec((3, width, width), lambda i: (0, 0, 0), pipeline_mode=once),
        ],
        out_specs=(
            whole,
            pl.BlockSpec((4, width, width), lambda i: (0, 0, 0), pipeline_mode=once),
            pl.BlockSpec((16, width), lambda i: (0, 0)),
        ),
        scratch_shapes=[pltpu.VMEM((3, tokens, 256), low)],
        compiler_params=pltpu.CompilerParams(vmem_limit_bytes=56 * 2**20),
        name="attend_backward",
    )(probs, query, keyed, valued, x, context, grad_context, grad_branch, grad_first, weights)


def moved(param, grad, first, second, average, rate):
    param_new, first_new, second_new = adam_update(param, grad, first, second, rate)
    return param_new, first_new, second_new, average_rate * average + (1.0 - average_rate) * param_new


def update_kernel(
    gain_scale,
    grad_ref,
    master_ref,
    first_ref,
    second_ref,
    ema_ref,
    mixed_in,
    input_in,
    vec_grad_hbm,
    bias_hbm,
    gain_hbm,
    vec_first_hbm,
    vec_second_hbm,
    vec_ema_hbm,
    master_out,
    first_out,
    second_out,
    ema_out,
    copy_out,
    mixed_out,
    input_out,
    vec_out,
    vec_first_out,
    vec_second_out,
    vec_ema_out,
    vec_grad_buf,
    bias_buf,
    gain_buf,
    vec_buf,
    vec_sem,
):
    step = pl.program_id(0) * pl.num_programs(1) + pl.program_id(1)
    last = pl.num_programs(0) * pl.num_programs(1) - 1

    def loads():
        pairs = (
            (vec_grad_hbm, vec_grad_buf),
            (bias_hbm, bias_buf),
            (gain_hbm, gain_buf),
            (vec_first_hbm, vec_buf.at[1]),
            (vec_second_hbm, vec_buf.at[2]),
            (vec_ema_hbm, vec_buf.at[3]),
        )
        return [pltpu.make_async_copy(src, dst, vec_sem.at[at]) for at, (src, dst) in enumerate(pairs)]

    def stores():
        targets = (vec_out, vec_first_out, vec_second_out, vec_ema_out)
        return [
            pltpu.make_async_copy(vec_buf.at[at], dst, vec_sem.at[6 + at]) for at, dst in enumerate(targets)
        ]

    @pl.when(step == 0)
    def _():
        for load in loads():
            load.start()

    mixed_out[...] = mixed_in[...]
    input_out[...] = input_in[...]
    grad = grad_ref[...].astype(jnp.float32) * gain_scale
    result = moved(master_ref[0], grad, first_ref[0], second_ref[0], ema_ref[0], tile_rate)
    master_out[0], first_out[0], second_out[0], ema_out[0] = result
    copy_out[0] = result[0].astype(jnp.bfloat16)

    @pl.when(step == 1)
    def _():
        for load in loads():
            load.wait()
        vec_buf[0, 0:10, :] = bias_buf[...]
        vec_buf[0, 10:12, :] = gain_buf[...]
        vec_grad = vec_grad_buf[0:VROWS, :] * gain_scale
        vec_buf[0], vec_buf[1], vec_buf[2], vec_buf[3] = moved(
            vec_buf[0], vec_grad, vec_buf[1], vec_buf[2], vec_buf[3], vector_rate
        )
        for store in stores():
            store.start()

    @pl.when(step == last)
    def _():
        for store in stores():
            store.wait()


def updated(
    gain_scale,
    slot_grads,
    master,
    first,
    second,
    ema,
    vec_grad,
    bias,
    gain,
    vec_first,
    vec_second,
    vec_ema,
    mixed,
    input_grad,
):
    width = master.shape[-1]
    chunk = 192
    steps = width // chunk
    tile = pl.BlockSpec((1, 1, chunk, width), lambda s, r: (0, s, r, 0))
    rows = pl.BlockSpec((mixed.shape[0] // (SLOTS * steps), width), lambda s, r: (s * steps + r, 0))
    any_space = pl.BlockSpec(memory_space=pl.ANY)
    shaped = jax.ShapeDtypeStruct
    tile_shape = shaped(master.shape, jnp.float32)
    vec_shape = shaped((VROWS, width), jnp.float32)
    results = pl.pallas_call(
        functools.partial(update_kernel, gain_scale),
        grid=(SLOTS, steps),
        out_shape=(tile_shape,) * 4
        + (shaped(master.shape, jnp.bfloat16),)
        + (shaped(mixed.shape, mixed.dtype), shaped(input_grad.shape, input_grad.dtype))
        + (vec_shape,) * 4,
        in_specs=[pl.BlockSpec((1, chunk, width), lambda s, r: (s, r, 0))]
        + [tile] * 4
        + [rows] * 2
        + [any_space] * 6,
        out_specs=(tile,) * 5 + (rows,) * 2 + (any_space,) * 4,
        scratch_shapes=[
            pltpu.VMEM(vec_grad.shape, jnp.float32),
            pltpu.VMEM(bias.shape, jnp.float32),
            pltpu.VMEM(gain.shape, jnp.float32),
            pltpu.VMEM((4, VROWS, width), jnp.float32),
            pltpu.SemaphoreType.DMA((10,)),
        ],
        compiler_params=pltpu.CompilerParams(vmem_limit_bytes=62 * 2**20),
        name="update",
    )(
        slot_grads,
        master,
        first,
        second,
        ema,
        mixed,
        input_grad,
        vec_grad,
        bias,
        gain,
        vec_first,
        vec_second,
        vec_ema,
    )
    return results[5:7] + results[:5] + results[7:]


MESH = pl.DeviceIdType.MESH
GROUP = 32
PAIRS = TILES // 2
PLANE = 8
PIECE = 96
PAIR_TILES = ((0, 1), (2, 3), (4, 8), (5, 9), (6, 10), (7, 11))


def remote(src, dst, send, recv, device):
    return pltpu.make_async_remote_copy(
        src_ref=src, dst_ref=dst, send_sem=send, recv_sem=recv, device_id=(device,), device_id_type=MESH
    )


def place(device):
    core = lax.rem(device, 2)
    x = lax.rem(device // 2, 2)
    y = lax.rem(device // 4, 2)
    z = device // 8
    return z, y, x, core


def start(copies):
    for copy in copies:
        copy.start()


def arrive(copies):
    for copy in copies:
        copy.wait_recv()


def greet(z, in_plane):
    barrier = pltpu.get_barrier_semaphore()
    for hop in range(1, PLANE):
        other = z * PLANE + lax.rem(in_plane + hop, PLANE)
        pl.semaphore_signal(barrier, inc=1, device_id=(other,), device_id_type=MESH)
    for hop in range(1, 4):
        other = lax.rem(z + hop, 4) * PLANE + in_plane
        pl.semaphore_signal(barrier, inc=1, device_id=(other,), device_id_type=MESH)
    pl.semaphore_wait(barrier, PLANE + 2)


def along_z(z, in_plane):
    inner = (1 + z // 2) * PLANE + in_plane
    other_middle = (3 - z) * PLANE + in_plane
    outer_end = lax.rem(lax.rem(z + 3, 4) * 3, 4) * PLANE + in_plane
    return inner, other_middle, outer_end


def third(part):
    return pl.ds(256 * part, 256)


UNITS = [(0, 4, pl.ds(256 * part, 256)) for part in range(3)]
UNITS += [(2 * pair, 2, pl.ds(0, 768)) for pair in range(2, PAIRS)]
Z_PARTS = (pl.ds(0, 512), pl.ds(512, 256))


POSITIONS = [tile for pair in PAIR_TILES for tile in pair]


def slot_number(owners, tile):
    number = jnp.int32(0)
    for earlier in range(tile):
        number = number + jnp.where(owners[earlier] == owners[tile], 1, 0)
    return number

FRONT_PLAN = (
    (
        ("open",),
        ("swap", 0),
        ("sent", 0),
        ("swap", 1),
        ("choose", 0),
        ("end", 0),
        ("sent", 1),
        ("middle", 0),
        ("choose", 1),
        ("end", 1),
        ("swap", 2),
        ("total", 0),
        ("end", 3, 0),
        ("middle", 1),
        ("mid", 0),
        ("choose", 2),
        ("end", 2),
        ("end", 3, 1),
        ("far", 0),
        ("middle", 3, 0),
        ("total", 1),
        ("caps",),
        ("middle", 3, 1),
        ("end", 4, 0),
        ("mid", 1),
        ("near", 0),
        ("total", 3, 0),
        ("end", 5, 0),
        ("middle", 2),
        ("end", 4, 1),
        ("total", 3, 1),
        ("far", 1),
        ("finish", 0),
    ),
    (
        ("middle", 4, 0),
        ("total", 2),
        ("mid", 3),
        ("middle", 4, 1),
        ("end", 5, 1),
    ),
    (
        ("mid", 2),
        ("end", 6, 0),
        ("middle", 5, 0),
        ("near", 1),
        ("total", 4, 1),
        ("far", 3),
        ("finish", 1),
        ("far", 2),
        ("middle", 5, 1),
        ("end", 6, 1),
        ("total", 4, 0),
    ),
    (
        ("total", 5, 0),
        ("middle", 6, 0),
        ("mid", 4),
        ("total", 5, 1),
        ("middle", 6, 1),
    ),
    (
        ("total", 6, 1),
        ("mid", 5),
        ("near", 2),
        ("far", 4),
        ("total", 6, 0),
        ("finish", 2),
        ("keep", 0),
        ("keep", 1),
    ),
    (
        ("mid", 6),
        ("near", 3),
        ("near", 4),
        ("far", 5),
    ),
    (
        ("far", 6),
        ("finish", 4),
        ("keep", 3),
        ("finish", 3),
        ("keep", 2),
    ),
    (
        ("near", 5),
    ),
    (
        ("near", 6),
        ("finish", 5),
        ("keep", 4),
    ),
    (
        ("finish", 6),
        ("keep", 5),
    ),
)


def gather_and_forward(
    counts,
    lengths,
    owners,
    bias_ref,
    gain_ref,
    x_hbm,
    cot_hbm,
    master_hbm,
    q_ref,
    k_ref,
    v_ref,
    p_ref,
    ctx_hbm,
    x_turned_hbm,
    ctx_turned_hbm,
    hidden_hbm,
    active_hbm,
    slope_hbm,
    down_hbm,
    mixed_hbm,
    second_hbm,
    hat_hbm,
    w_out,
    inverse_ref,
    sum_ref,
    vec_ref,
    cap_ref,
    wide,
    low,
    stage_a,
    stage_b,
    stage_c,
    chosen,
    from_end,
    from_middle,
    w_buf,
    x_then_hidden,
    x_turned,
    ctx_turned,
    hidden_turned,
    ctx_ref,
    cot_then_down,
    mixed_ref,
    hat_ref,
    slope_buf,
    active_buf,
    wide_sem,
    load_sem,
    store_sem,
    half_sem,
    tile_sem,
    out_sem,
    swap_send,
    swap_recv,
    z_send,
    z_recv,
    mid_send,
    mid_recv,
    far_send,
    far_recv,
    near_send,
    near_recv,
):
    step = pl.program_id(0)
    width = 8 * PIECE
    me = lax.axis_index("dp")
    z, y, x, core = place(me)
    in_plane = lax.rem(me, PLANE)
    sibling = me + 1 - 2 * core
    x_peer = me + 2 - 4 * x
    y_peer = me + 4 - 8 * y
    z_targets = along_z(z, in_plane)
    stages = (stage_a, stage_b, stage_c)
    is_end = (z == 0) | (z == 3)
    is_middle = (z == 1) | (z == 2)

    def piece_rows(cell_core, cell_x, cell_y):
        return pl.ds(pl.multiple_of(((cell_core * 2 + cell_x) * 2 + cell_y) * PIECE, 16), PIECE)

    def wide_load(part):
        cols = third(part)
        return pltpu.make_async_copy(master_hbm.at[:, cols], wide.at[:, cols], wide_sem.at[part])

    def swap(part):
        wide_load(part).wait()
        for slot in range(SLOTS):
            master = wide[width * slot : width * (slot + 1), third(part)]
            low[slot, :, third(part)] = master.astype(jnp.bfloat16)

        def send(hop, carry):
            target = lax.rem(in_plane + hop, PLANE)
            _, ty, tx, tc = place(target)
            remote(
                low.at[:, piece_rows(tc, tx, ty), third(part)],
                stages[part].at[pl.ds(2 * in_plane, 2)],
                swap_send.at[part],
                swap_recv.at[part],
                z * PLANE + target,
            ).start()
            return carry

        lax.fori_loop(1, PLANE, send, 0)
        stages[part][pl.ds(2 * in_plane, 2)] = low[:, piece_rows(core, x, y), third(part)]
        if part == 0:
            start([load(0), load(1)])

    def swap_wait(part, sem):
        most = stages[part].at[pl.ds(0, 2 * PLANE - 2)]
        pltpu.make_async_copy(most, most, sem.at[part]).wait()

    def z_copy(unit, part, level):
        first, count, cols = UNITS[unit]
        tiles = pl.ds(first, count)
        cols = cols if count == 4 else Z_PARTS[part]
        src = w_buf.at[tiles, core, x, y, :, cols] if level == 2 else chosen.at[tiles, :, cols]
        dst = (from_end.at[tiles, :, cols], from_middle.at[tiles, :, cols], src)[level]
        at = level, unit, part
        return remote(src, dst, z_send.at[at], z_recv.at[at], z_targets[level])

    def z_parts(unit):
        return range(1 if UNITS[unit][1] == 4 else 2)

    def z_end(unit, part=0):
        @pl.when(is_end)
        def _():
            z_copy(unit, part, 0).start()

    def z_rows(unit, part):
        first, count, cols = UNITS[unit]
        return pl.ds(first, count), cols if count == 4 else Z_PARTS[part]

    def z_middle(unit, part=0):
        @pl.when(is_middle)
        def _():
            z_copy(unit, part, 0).wait_recv()
            tiles, cols = z_rows(unit, part)
            chosen[tiles, :, cols] = chosen[tiles, :, cols] + from_end[tiles, :, cols]
            z_copy(unit, part, 1).start()

    def z_total(unit, part=0):
        @pl.when(is_middle)
        def _():
            z_copy(unit, part, 1).wait_recv()
            tiles, cols = z_rows(unit, part)
            w_buf[tiles, core, x, y, :, cols] = chosen[tiles, :, cols] + from_middle[tiles, :, cols]
            z_copy(unit, part, 2).start()

    def mid_copies(unit):
        first, count, cols = UNITS[unit]
        copies = []
        for n, peer in enumerate((y_peer, x_peer)):
            spot = w_buf.at[pl.ds(first + n * count // 2, count // 2), core, x, y, :, cols]
            copies.append(remote(spot, spot, mid_send.at[unit, n], mid_recv.at[unit, n], peer))
        return copies

    def far_copies(unit):
        first, count, cols = UNITS[unit]
        half = count // 2
        by_row = w_buf.at[pl.ds(first, half), core, x, :, :, cols]
        by_column = w_buf.at[pl.ds(first + half, half), core, :, y, :, cols]
        return [
            remote(spot, spot, far_send.at[unit, n], far_recv.at[unit, n], peer)
            for n, (spot, peer) in enumerate(((by_row, x_peer), (by_column, y_peer)))
        ]

    def near_copy(unit):
        first, count, cols = UNITS[unit]
        spot = w_buf.at[pl.ds(first, count), core, :, :, :, cols]
        return remote(spot, spot, near_send.at[unit], near_recv.at[unit], sibling)

    def give_mid(unit):
        @pl.when(is_end)
        def _():
            arrive([z_copy(unit, part, 2) for part in z_parts(unit)])

        start(mid_copies(unit))

    def give_far(unit):
        arrive(mid_copies(unit))
        start(far_copies(unit))

    def give_near(unit):
        arrive(far_copies(unit))
        near_copy(unit).start()

    def finish(unit):
        near_copy(unit).wait_recv()

    def choose(part):
        swap_wait(part, swap_recv)
        for pair in range(PAIRS):
            for n, tile in enumerate(PAIR_TILES[pair]):
                owner = owners[tile]
                value = stages[part][SLOTS * lax.rem(owner, PLANE) + slot_number(owners, tile)]
                chosen[2 * pair + n, :, third(part)] = jnp.where(
                    owner // PLANE == z, value, jnp.zeros_like(value)
                )

    def load(at):
        src = (x_hbm, cot_hbm)[at]
        dst = (x_then_hidden, cot_then_down)[at]
        return pltpu.make_async_copy(src, dst, load_sem.at[at])

    def store(at):
        src, dst = (
            (hidden_turned, hidden_hbm),
            (ctx_ref, ctx_hbm),
            (hat_ref, hat_hbm),
            None,
            None,
            None,
            (x_turned, x_turned_hbm),
            (ctx_turned, ctx_turned_hbm),
        )[at]
        return pltpu.make_async_copy(src, dst, store_sem.at[at])

    def half_stores(half):
        rows = pl.ds(ROWS * half, ROWS)
        pairs = ((cot_then_down, down_hbm), (mixed_ref, mixed_hbm), (wide, second_hbm))
        return [
            pltpu.make_async_copy(src.at[rows], dst.at[rows], half_sem.at[half, at])
            for at, (src, dst) in enumerate(pairs)
        ]

    def w_store(pair):
        two = pl.ds(2 * pair, 2)
        return pltpu.make_async_copy(w_buf.at[two], w_out.at[two], out_sem.at[pair])

    def weight(at, cols=slice(None)):
        value = w_buf[at, :, :, :, :, cols]
        return value.reshape(width, value.shape[-1])

    def open_all():
        start([wide_load(part) for part in range(3)])
        sum_ref[...] = jnp.zeros_like(sum_ref)
        vec_ref[0:10, :] = bias_ref[...]
        vec_ref[10:12, :] = gain_ref[...]
        greet(z, in_plane)

    def make_caps():
        for block in range(2):
            cap_ref[block] = attention_caps(counts, lengths, block)
        load(0).wait()
        x_turned[...] = x_then_hidden[...].T
        store(6).start()

    actions = {
        "open": open_all,
        "caps": make_caps,
        "swap": swap,
        "sent": lambda part: swap_wait(part, swap_send),
        "choose": choose,
        "end": z_end,
        "middle": z_middle,
        "total": z_total,
        "mid": give_mid,
        "far": give_far,
        "near": give_near,
        "finish": finish,
        "keep": lambda pair: w_store(pair).start(),
    }

    for at, work in enumerate(FRONT_PLAN):

        @pl.when(step == at)
        def _():
            for name, *rest in work:
                actions[name](*rest)

    quad, block = step // 2, lax.rem(step, 2)
    here = pl.ds(pl.multiple_of(block * ROWS, ROWS), ROWS)

    @pl.when(step < 6)
    def _():
        attend_quad(
            quad,
            weight,
            x_then_hidden.at[here],
            vec_ref,
            cap_ref.at[block],
            q_ref,
            k_ref,
            v_ref,
            p_ref,
            ctx_ref.at[here],
        )

    @pl.when((step >= 4) & (step < 6))
    def _():
        branch = dot(ctx_ref[here, :], weight(3)) + vec_ref[2:3, :]
        hat, inverse = normalize(x_then_hidden[here, :].astype(jnp.float32) + branch)
        hat_ref[here, :] = hat.astype(jnp.bfloat16)
        inverse_ref[here, :] = inverse
        hidden = hat * vec_ref[10:11, :] + vec_ref[8:9, :]
        hidden_low = hidden.astype(jnp.bfloat16)
        x_then_hidden[here, :] = hidden_low
        hidden_turned[:, here] = hidden_low.T
        ctx_turned[:, here] = ctx_ref[here, :].T
        wide[here, :] = hidden + vec_ref[7:8, :]

    @pl.when(step == 5)
    def _():
        start([store(0), store(1), store(2), store(7)])

    turn = step - 6
    slot = lax.rem(turn, 2)

    def tile_stores(source_slot, tile):
        return [
            pltpu.make_async_copy(src.at[source_slot], dst.at[tile], tile_sem.at[source_slot, at])
            for at, (src, dst) in enumerate(((active_buf, active_hbm), (slope_buf, slope_hbm)))
        ]

    @pl.when(turn >= 2)
    def _():
        for copy in tile_stores(slot, 0):
            copy.wait()

    @pl.when(turn >= 0)
    def _():
        for half in range(2):
            rows = slice(ROWS * half, ROWS * half + ROWS)
            up = dot(x_then_hidden[rows, :], weight(4 + 2 * turn)) + vec_ref[pl.ds(3 + turn, 1), :]
            active, slope = gelu_parts(up)
            slope_buf[slot, rows, :] = slope.astype(jnp.bfloat16)
            active_buf[slot, :, rows] = active.T
            wide[rows, :] = wide[rows, :] + dot(active, weight(5 + 2 * turn))
        start(tile_stores(slot, turn))

    @pl.when(step == 9)
    def _():
        load(1).wait()
        for half in range(2):
            rows = slice(ROWS * half, ROWS * half + ROWS)
            at_row = lax.broadcasted_iota(jnp.int32, (ROWS, 1), 0) + half * ROWS
            live = passage_facts(counts, lengths, at_row)[0].astype(jnp.float32)
            hat, inverse = normalize(wide[rows, :])
            mixed = (hat * vec_ref[11:12, :] + vec_ref[9:10, :]) * live
            mixed_ref[rows, :] = mixed.astype(jnp.bfloat16)
            grad_out = cot_then_down[rows, :].astype(jnp.float32) * live
            sum_ref[11:12, :] += columns_total(grad_out * hat)
            sum_ref[9:10, :] += columns_total(grad_out)
            second = normalize_back(grad_out * vec_ref[11:12, :], hat, inverse)
            wide[rows, :] = second
            down_low = second.astype(jnp.bfloat16)
            cot_then_down[rows, :] = down_low
            sum_ref[7:8, :] += columns_total(down_low.astype(jnp.float32))
            start(half_stores(half))
        for at in range(2):
            for copy in tile_stores(at, 0):
                copy.wait()
        for pair in range(PAIRS):
            w_store(pair).wait()
        swap_wait(2, swap_send)
        for unit in range(len(UNITS)):
            for copy in mid_copies(unit) + far_copies(unit) + [near_copy(unit)]:
                copy.wait_send()

            @pl.when(is_end)
            def _():
                for part in z_parts(unit):
                    z_copy(unit, part, 0).wait_send()

            @pl.when(is_middle)
            def _():
                for part in z_parts(unit):
                    z_copy(unit, part, 1).wait_send()
                    z_copy(unit, part, 2).wait_send()

        for at in (0, 1, 2, 6, 7):
            store(at).wait()
        for copy in half_stores(0) + half_stores(1):
            copy.wait()


def gathered_and_forwarded(counts, lengths, owners, bias, gain, x, cotangent, master):
    tokens, width = x.shape
    blocks = tokens // ROWS
    low, high = jnp.bfloat16, jnp.float32
    smem = pl.BlockSpec(memory_space=pltpu.SMEM)
    any_space = pl.BlockSpec(memory_space=pl.ANY)
    dma = pltpu.SemaphoreType.DMA
    shaped = jax.ShapeDtypeStruct

    def at(step):
        step = jnp.minimum(step, 5)
        return lax.rem(step, 2), step // 2

    quad = pl.BlockSpec((ROWS, 256), at)
    rows = shaped((tokens, width), low)
    turned = shaped((width, tokens), low)
    cut = (2, 2, 2, PIECE, width)
    units = len(UNITS)
    return pl.pallas_call(
        gather_and_forward,
        grid=(10,),
        out_shape=(
            rows,
            rows,
            rows,
            shaped((blocks, HEADS, ROWS, ROWS), low),
            rows,
            turned,
            turned,
            turned,
            shaped((4, width, tokens), low),
            shaped((4, tokens, width), low),
            rows,
            rows,
            shaped((tokens, width), high),
            rows,
            shaped((TILES,) + cut, low),
            shaped((tokens, 1), high),
            shaped((16, width), high),
        ),
        in_specs=[smem] * 3
        + [pl.BlockSpec(bias.shape, lambda i: (0, 0)), pl.BlockSpec(gain.shape, lambda i: (0, 0))]
        + [any_space] * 3,
        out_specs=(quad, quad, quad, pl.BlockSpec((1, 4, ROWS, ROWS), lambda i: (*at(i), 0, 0)))
        + (any_space,) * 11
        + (
            pl.BlockSpec((tokens, 1), lambda i: (0, 0), pipeline_mode=pl.Buffered(1)),
            pl.BlockSpec((16, width), lambda i: (0, 0)),
        ),
        scratch_shapes=[
            pltpu.VMEM((VROWS, width), high),
            pltpu.VMEM((2, ROWS, ROWS), high),
            pltpu.VMEM((SLOTS * width, width), high),
            pltpu.VMEM((SLOTS, width, width), low),
            pltpu.VMEM((2 * PLANE, PIECE, 256), low),
            pltpu.VMEM((2 * PLANE, PIECE, 256), low),
            pltpu.VMEM((2 * PLANE, PIECE, 256), low),
            pltpu.VMEM((TILES, PIECE, width), low),
            pltpu.VMEM((TILES, PIECE, width), low),
            pltpu.VMEM((TILES, PIECE, width), low),
            pltpu.VMEM((TILES,) + cut, low),
            pltpu.VMEM((tokens, width), low),
            pltpu.VMEM((width, tokens), low),
            pltpu.VMEM((width, tokens), low),
            pltpu.VMEM((width, tokens), low),
            pltpu.VMEM((tokens, width), low),
            pltpu.VMEM((tokens, width), low),
            pltpu.VMEM((tokens, width), low),
            pltpu.VMEM((tokens, width), low),
            pltpu.VMEM((2, tokens, width), low),
            pltpu.VMEM((2, width, tokens), low),
            dma((3,)),
            dma((2,)),
            dma((8,)),
            dma((2, 3)),
            dma((2, 2)),
            dma((PAIRS,)),
            dma((3,)),
            dma((3,)),
            dma((3, units, 2)),
            dma((3, units, 2)),
            dma((units, 2)),
            dma((units, 2)),
            dma((units, 2)),
            dma((units, 2)),
            dma((units,)),
            dma((units,)),
        ],
        compiler_params=pltpu.CompilerParams(
            collective_id=0, has_side_effects=True, vmem_limit_bytes=63 * 2**20
        ),
        name="gather_and_forward",
    )(counts, lengths, owners, bias, gain, x, cotangent, master.reshape(SLOTS * width, width))


BACK_PLAN = (
    (),
    (),
    (
        ("core", 0),
    ),
    (),
    (
        ("core", 1),
        ("far", 0),
    ),
    (),
    (
        ("core", 2),
        ("far", 1),
    ),
    (
        ("mid", 0),
        ("far", 2),
    ),
    (),
    (
        ("core", 3),
        ("mid", 1),
        ("end", 0),
    ),
    (),
    (
        ("far", 3),
        ("end", 1),
        ("mid", 2),
    ),
    (
        ("core", 4),
        ("middle", 0),
    ),
    (),
    (
        ("middle", 1),
        ("end", 2),
        ("mid", 3),
        ("far", 4),
    ),
    (
        ("total", 0),
    ),
    (
        ("middle", 2),
        ("end", 3),
        ("total", 1),
        ("core", 5),
        ("mid", 4),
    ),
    (),
    (
        ("far", 5),
        ("end", 4),
        ("middle", 3),
        ("total", 2),
    ),
    (),
    (
        ("core", 6),
        ("total", 3),
        ("middle", 4),
        ("mid", 5),
        ("far", 6),
        ("total", 4),
        ("sum", 0),
        ("end", 5),
        ("mid", 6),
        ("middle", 5),
        ("end", 6),
        ("take", 4),
        ("take", 0),
        ("sum", 1),
        ("take", 2),
        ("take", 3),
        ("take", 1),
        ("deliver", 0),
        ("total", 5),
        ("middle", 6),
        ("sum", 2),
        ("take", 5),
        ("deliver", 1),
        ("total", 6),
        ("take", 6),
        ("deliver", 2),
        ("input", 0),
        ("input", 1),
    ),
)


def backward_and_reduce(
    owners,
    p_ref,
    q_ref,
    k_ref,
    v_ref,
    inverse_ref,
    gain_ref,
    late_ref,
    ctx_hbm,
    x_turned_hbm,
    ctx_turned_hbm,
    hidden_hbm,
    active_hbm,
    slope_hbm,
    down_hbm,
    second_hbm,
    hat_hbm,
    w_hbm,
    input_hbm,
    slot_grad,
    vec_out,
    w_part,
    acc,
    hidden_then_x,
    active_then_ctx,
    down_then_branch,
    ctx_ref,
    grad_ctx_ref,
    hat_ref,
    slope_then_query,
    up_then_key,
    value_buf,
    part,
    from_core,
    from_far,
    from_mid,
    from_end,
    from_middle,
    total,
    snap,
    outbox,
    vec_now,
    vec_in,
    holds,
    keeps,
    load_sem,
    w_sem,
    core_send,
    core_recv,
    far_send,
    far_recv,
    mid_send,
    mid_recv,
    z_send,
    z_recv,
    vec_send,
    vec_recv,
    out_send,
    out_recv,
):
    step = pl.program_id(0)
    inner = jnp.maximum(step - 4, 0)
    quad, block, pair = inner // 4, lax.rem(inner, 4) // 2, lax.rem(inner, 2)
    me = lax.axis_index("dp")
    z, y, x, core = place(me)
    in_plane = lax.rem(me, PLANE)
    sibling = me + 1 - 2 * core
    x_peer = me + 2 - 4 * x
    y_peer = me + 4 - 8 * y
    z_targets = along_z(z, in_plane)
    is_end = (z == 0) | (z == 3)
    is_middle = (z == 1) | (z == 2)

    def tiles_of(batch):
        if batch < 4:
            return w_part, 4 + 2 * batch, 2, slice(None)
        return part, 0, 4, pl.ds(256 * (batch - 4), 256)

    def halves(batch, turned):
        ref, first, count, cols = tiles_of(batch)
        return ref, pl.ds(first + turned * count // 2, count // 2), cols

    def core_copy(batch):
        ref, first, count, cols = tiles_of(batch)
        tiles = pl.ds(first, count)
        return remote(
            ref.at[tiles, 1 - core, :, :, :, cols],
            from_core.at[tiles, :, :, :, cols],
            core_send.at[batch],
            core_recv.at[batch],
            sibling,
        )

    def far_copies(batch):
        copies = []
        for turned in range(2):
            ref, tiles, cols = halves(batch, turned)
            src = ref.at[tiles, core, :, 1 - y, :, cols] if turned else ref.at[tiles, core, 1 - x, :, :, cols]
            copies.append(
                remote(
                    src,
                    from_far.at[tiles, :, :, cols],
                    far_send.at[batch, turned],
                    far_recv.at[batch, turned],
                    y_peer if turned else x_peer,
                )
            )
        return copies

    def mid_copies(batch):
        copies = []
        for turned in range(2):
            ref, tiles, cols = halves(batch, turned)
            src = ref.at[tiles, core, 1 - x, y, :, cols] if turned else ref.at[tiles, core, x, 1 - y, :, cols]
            copies.append(
                remote(
                    src,
                    from_mid.at[tiles, :, cols],
                    mid_send.at[batch, turned],
                    mid_recv.at[batch, turned],
                    x_peer if turned else y_peer,
                )
            )
        return copies

    def z_copy(batch, stage):
        ref, first, count, cols = tiles_of(batch)
        tiles = pl.ds(first, count)
        if stage == 2:
            src, dst = total.at[tiles, :, cols], total.at[tiles, :, cols]
        else:
            src = ref.at[tiles, core, x, y, :, cols]
            dst = (from_middle if stage else from_end).at[tiles, :, cols]
        return remote(src, dst, z_send.at[stage, batch], z_recv.at[stage, batch], z_targets[stage])

    def give_core(batch):
        core_copy(batch).start()

    def give_far(batch):
        core_copy(batch).wait_recv()
        ref, first, count, cols = tiles_of(batch)
        for tile in range(first, first + count):
            ref[tile, core, :, :, :, cols] = ref[tile, core, :, :, :, cols] + from_core[tile, :, :, :, cols]
        start(far_copies(batch))

    def give_mid(batch):
        arrive(far_copies(batch))
        for turned in range(2):
            ref, tiles, cols = halves(batch, turned)
            if turned:
                ref[tiles, core, :, y, :, cols] = ref[tiles, core, :, y, :, cols] + from_far[tiles, :, :, cols]
            else:
                ref[tiles, core, x, :, :, cols] = ref[tiles, core, x, :, :, cols] + from_far[tiles, :, :, cols]
        start(mid_copies(batch))

    def add_piece(batch, other):
        ref, first, count, cols = tiles_of(batch)
        tiles = pl.ds(first, count)
        return ref[tiles, core, x, y, :, cols] + other[tiles, :, cols]

    def give_end(batch):
        arrive(mid_copies(batch))
        ref, first, count, cols = tiles_of(batch)
        ref[pl.ds(first, count), core, x, y, :, cols] = add_piece(batch, from_mid)

        @pl.when(is_end)
        def _():
            z_copy(batch, 0).start()

    def give_middle(batch):
        @pl.when(is_middle)
        def _():
            z_copy(batch, 0).wait_recv()
            ref, first, count, cols = tiles_of(batch)
            ref[pl.ds(first, count), core, x, y, :, cols] = add_piece(batch, from_end)
            z_copy(batch, 1).start()

    def give_total(batch):
        @pl.when(is_middle)
        def _():
            z_copy(batch, 1).wait_recv()
            _, first, count, cols = tiles_of(batch)
            total[pl.ds(first, count), :, cols] = add_piece(batch, from_middle)
            z_copy(batch, 2).start()

    def take_total(batch):
        @pl.when(is_end)
        def _():
            z_copy(batch, 2).wait_recv()

    def deliver(third):
        cols = pl.ds(256 * third, 256)
        snap[...] = total[:, :, cols]

        def fill(at, carry):
            value = snap[holds[at]]
            outbox[third, at] = jnp.where(keeps[at] > 0, value, jnp.zeros_like(value))
            return carry

        lax.fori_loop(0, 2 * PLANE, fill, 0)

        def send(hop, carry):
            target = lax.rem(in_plane + hop, PLANE)
            remote(
                outbox.at[third, pl.ds(2 * target, 2)],
                slot_grad.at[:, core, x, y, :, cols],
                out_send.at[third],
                out_recv.at[third],
                z * PLANE + target,
            ).start()
            return carry

        lax.fori_loop(1, PLANE, send, 0)
        keep_copy(third).start()

    def keep_copy(third):
        return pltpu.make_async_copy(
            outbox.at[third, pl.ds(2 * in_plane, 2)],
            slot_grad.at[:, core, x, y, :, pl.ds(256 * third, 256)],
            load_sem.at[5 + third],
        )

    def vec_copies(stage):
        if stage < 3:
            hops = [(stage, (sibling, x_peer, y_peer)[stage])]
        else:
            hops = [
                (2 + hop, lax.rem(z + hop, 4) * PLANE + in_plane) for hop in range(1, 4)
            ]
        return [
            remote(vec_now.at[stage], vec_in.at[at], vec_send.at[at], vec_recv.at[at], device)
            for at, device in hops
        ]

    def vec_next(stage):
        arrive(vec_copies(stage))
        vec_now[stage + 1] = vec_now[stage] + vec_in[stage]
        start(vec_copies(stage + 1))

    def input_store():
        return pltpu.make_async_copy(acc, input_hbm, load_sem.at[4])

    def load(at):
        src, dst = (
            (hidden_hbm, hidden_then_x),
            (down_hbm, down_then_branch),
            (second_hbm, acc),
            (hat_hbm, hat_ref),
            None,
            None,
            None,
            None,
            (x_turned_hbm, hidden_then_x),
            (ctx_turned_hbm, active_then_ctx),
            None,
            None,
            (ctx_hbm, ctx_ref),
        )[at]
        return pltpu.make_async_copy(src, dst, load_sem.at[at])

    def tile_load(tile, side):
        src, dst = ((slope_hbm, slope_then_query), (active_hbm, active_then_ctx))[side]
        return pltpu.make_async_copy(src.at[tile], dst, load_sem.at[10 + side])

    def w_load(at):
        return pltpu.make_async_copy(w_hbm.at[at], w_part.at[at], w_sem.at[at])

    def weight(at, cols=slice(None)):
        value = w_part[at, :, :, :, :, cols]
        return value.reshape(8 * PIECE, value.shape[-1])

    def input_rows(half):
        rows = slice(ROWS * half, ROWS * half + ROWS)
        more = acc[rows, :]
        for at, buf in enumerate((slope_then_query, up_then_key, value_buf)):
            more = more + dot_back(buf[rows, :], weight(at))
        acc[rows, :] = more
        if half == 1:
            input_store().start()

    actions = {
        "core": give_core,
        "far": give_far,
        "mid": give_mid,
        "end": give_end,
        "middle": give_middle,
        "total": give_total,
        "take": take_total,
        "deliver": deliver,
        "sum": vec_next,
        "input": input_rows,
    }

    @pl.when(step == 0)
    def _():
        start([load(1), tile_load(0, 0), w_load(5), w_load(4)])
        for at in range(2 * PLANE):
            tile_here, kept = jnp.int32(0), jnp.int32(0)
            for tile in range(TILES):
                place_of = SLOTS * owners[tile] + slot_number(owners, tile)
                match = place_of == z * 2 * PLANE + at
                tile_here = tile_here + jnp.where(match, POSITIONS.index(tile), 0)
                kept = kept + jnp.where(match, 1, 0)
            holds[at] = tile_here
            keeps[at] = kept
        vec_now[0] = late_ref[...]
        greet(z, in_plane)

    def serve(points):
        for at in points:
            if BACK_PLAN[at]:

                @pl.when(step == (at // 2 if at < 8 else at - 4))
                def _():
                    for name, number in BACK_PLAN[at]:
                        actions[name](number)

    serve(range(0, 8, 2))

    @pl.when(step < 4)
    def _():
        tile_load(step, 0).wait()
        w_load(5 + 2 * step).wait()

        @pl.when(step == 0)
        def _():
            load(1).wait()
            start([load(2), tile_load(0, 1), load(0)])

        @pl.when(step < 3)
        def _():
            start([w_load(7 + 2 * step), w_load(6 + 2 * step)])

        @pl.when(step == 1)
        def _():
            load(3).start()

        @pl.when(step == 2)
        def _():
            w_load(3).start()

        @pl.when(step == 3)
        def _():
            start([load(12), w_load(0), w_load(1), w_load(2)])

        for half in range(2):
            rows = slice(ROWS * half, ROWS * half + ROWS)
            back = dot_back(down_then_branch[rows, :], weight(5 + 2 * step))
            up_low = (back * slope_then_query[rows, :].astype(jnp.float32)).astype(jnp.bfloat16)
            up_then_key[rows, :] = up_low
            vec_now[0, pl.ds(3 + step, 1), :] += columns_total(up_low.astype(jnp.float32))

        @pl.when(step < 3)
        def _():
            tile_load(step + 1, 0).start()

        w_load(4 + 2 * step).wait()

        @pl.when(step == 0)
        def _():
            load(2).wait()
            load(0).wait()

        for half in range(2):
            rows = slice(ROWS * half, ROWS * half + ROWS)
            acc[rows, :] = acc[rows, :] + dot_back(up_then_key[rows, :], weight(4 + 2 * step))

    serve(range(1, 8, 2))

    @pl.when(step < 4)
    def _():
        tile_load(step, 1).wait()
        by_down = dot(active_then_ctx[...], down_then_branch[...]).astype(jnp.bfloat16)
        w_part[5 + 2 * step] = by_down.reshape(2, 2, 2, PIECE, 8 * PIECE)

        @pl.when(step < 3)
        def _():
            tile_load(step + 1, 1).start()

        by_up = dot(hidden_then_x[...], up_then_key[...]).astype(jnp.bfloat16)
        w_part[4 + 2 * step] = by_up.reshape(2, 2, 2, PIECE, 8 * PIECE)

    @pl.when(step == 3)
    def _():
        start([load(8), load(9)])
        load(3).wait()
        w_load(3).wait()
        for half in range(2):
            rows = slice(ROWS * half, ROWS * half + ROWS)
            grad_hidden, hat = acc[rows, :], hat_ref[rows, :].astype(jnp.float32)
            vec_now[0, 10:11, :] += columns_total(grad_hidden * hat)
            vec_now[0, 8:9, :] += columns_total(grad_hidden)
            first = normalize_back(grad_hidden * gain_ref[0:1, :], hat, inverse_ref[rows, :])
            acc[rows, :] = first
            branch_low = first.astype(jnp.bfloat16)
            down_then_branch[rows, :] = branch_low
            vec_now[0, 2:3, :] += columns_total(branch_low.astype(jnp.float32))
            grad_ctx_ref[rows, :] = dot_back(branch_low, weight(3)).astype(jnp.bfloat16)

    serve(range(8, 20))

    here = pl.ds(pl.multiple_of(block * ROWS, ROWS), ROWS)
    quad_cols = pl.ds(pl.multiple_of(quad * 256, 256), 256)

    @pl.when(step == 4)
    def _():
        load(12).wait()
        for at in range(3):
            w_load(at).wait()

    pair_cols = pl.ds(pl.multiple_of(quad * 256 + pair * 128, 128), 128)
    grad_bufs = (slope_then_query, up_then_key, value_buf)

    @pl.when(step >= 4)
    def _():
        grads = attend_back_pair(
            grad_ctx_ref[here, pair_cols],
            ctx_ref[here, pair_cols],
            p_ref.at[0],
            q_ref[...],
            k_ref[...],
            v_ref[...],
        )
        for buf, grad in zip(grad_bufs, grads):
            buf[here, pair_cols] = grad
        vec_now[0, 0:1, pair_cols] += columns_total(grads[0].astype(jnp.float32))
        vec_now[0, 1:2, pair_cols] += columns_total(grads[2].astype(jnp.float32))

    @pl.when(step == 7)
    def _():
        load(8).wait()
        load(9).wait()

    @pl.when((step >= 4) & (block == 1) & (pair == 1))
    def _():
        for tile in range(4):
            if tile < 3:
                value = dot(hidden_then_x[...], grad_bufs[tile][:, quad_cols])
            else:
                value = dot(active_then_ctx[...], down_then_branch[:, quad_cols])
            value = value.astype(jnp.bfloat16).reshape(2, 2, 2, PIECE, 256)
            part[tile, :, :, :, :, quad_cols] = value


    @pl.when(step == 15)
    def _():
        start(vec_copies(0))
        for name, number in BACK_PLAN[-1]:
            actions[name](number)
        arrive(vec_copies(3))
        summed = jnp.zeros(vec_out.shape, jnp.float32)
        for origin in range(4):
            hop = lax.rem(z - origin + 4, 4)
            summed = summed + jnp.where(hop == 0, vec_now[3], vec_in[2 + jnp.maximum(hop, 1)])
        vec_out[...] = summed
        for batch in range(7):
            for copy in [core_copy(batch)] + far_copies(batch) + mid_copies(batch):
                copy.wait_send()

            @pl.when(is_end)
            def _():
                z_copy(batch, 0).wait_send()

            @pl.when(is_middle)
            def _():
                z_copy(batch, 1).wait_send()
                z_copy(batch, 2).wait_send()

        for stage in range(4):
            for copy in vec_copies(stage):
                copy.wait_send()
        input_store().wait()
        for third in range(3):
            keep_copy(third).wait()
            most = outbox.at[third, pl.ds(0, 2 * PLANE - 2)]
            pltpu.make_async_copy(most, most, out_recv.at[third]).wait()
            pltpu.make_async_copy(most, most, out_send.at[third]).wait()


def backward_and_reduced(
    owners,
    probs,
    query,
    keyed,
    valued,
    inverse,
    gain,
    late_sums,
    context,
    x_turned,
    ctx_turned,
    hidden,
    active,
    slope,
    grad_down,
    grad_second,
    hat,
    weights,
):
    tokens, width = grad_down.shape
    low, high = jnp.bfloat16, jnp.float32
    shaped = jax.ShapeDtypeStruct
    smem = pl.BlockSpec(memory_space=pltpu.SMEM)
    any_space = pl.BlockSpec(memory_space=pl.ANY)
    dma = pltpu.SemaphoreType.DMA
    once = pl.Buffered(1)

    def at(step):
        inner = jnp.maximum(step - 4, 0)
        return lax.rem(inner, 4) // 2, inner // 4 * 2 + lax.rem(inner, 2)

    pair = pl.BlockSpec((ROWS, 128), at)
    sums = pl.BlockSpec((16, width), lambda i: (0, 0))
    cut = (2, 2, 2, PIECE, width)
    input_grad, slot_grads, vector_sums = pl.pallas_call(
        backward_and_reduce,
        grid=(16,),
        out_shape=(
            shaped((tokens, width), high),
            shaped((SLOTS,) + cut, low),
            shaped((16, width), high),
        ),
        in_specs=[smem, pl.BlockSpec((1, 2, ROWS, ROWS), lambda i: (*at(i), 0, 0))]
        + [pair] * 3
        + [
            pl.BlockSpec((tokens, 1), lambda i: (0, 0), pipeline_mode=once),
            pl.BlockSpec(gain.shape, lambda i: (0, 0)),
            sums,
        ]
        + [any_space] * 10,
        out_specs=(any_space, any_space, sums),
        scratch_shapes=[
            pltpu.VMEM((TILES,) + cut, low),
            pltpu.VMEM((tokens, width), high),
            pltpu.VMEM((width, tokens), low),
            pltpu.VMEM((width, tokens), low),
            pltpu.VMEM((tokens, width), low),
            pltpu.VMEM((tokens, width), low),
            pltpu.VMEM((tokens, width), low),
            pltpu.VMEM((tokens, width), low),
            pltpu.VMEM((tokens, width), low),
            pltpu.VMEM((tokens, width), low),
            pltpu.VMEM((tokens, width), low),
            pltpu.VMEM((4,) + cut, low),
            pltpu.VMEM((TILES,) + cut[1:], low),
            pltpu.VMEM((TILES,) + cut[2:], low),
            pltpu.VMEM((TILES,) + cut[3:], low),
            pltpu.VMEM((TILES,) + cut[3:], low),
            pltpu.VMEM((TILES,) + cut[3:], low),
            pltpu.VMEM((TILES,) + cut[3:], low),
            pltpu.VMEM((TILES, PIECE, 256), low),
            pltpu.VMEM((3, 2 * PLANE, PIECE, 256), low),
            pltpu.VMEM((4, 16, width), high),
            pltpu.VMEM((6, 16, width), high),
            pltpu.SMEM((2 * PLANE,), jnp.int32),
            pltpu.SMEM((2 * PLANE,), jnp.int32),
            dma((13,)),
            dma((TILES,)),
            dma((7,)),
            dma((7,)),
            dma((7, 2)),
            dma((7, 2)),
            dma((7, 2)),
            dma((7, 2)),
            dma((3, 7)),
            dma((3, 7)),
            dma((6,)),
            dma((6,)),
            dma((3,)),
            dma((3,)),
        ],
        compiler_params=pltpu.CompilerParams(
            collective_id=1, has_side_effects=True, vmem_limit_bytes=63 * 2**20
        ),
        name="backward_and_reduce",
    )(
        owners,
        probs,
        query,
        keyed,
        valued,
        inverse,
        gain,
        late_sums,
        context,
        x_turned,
        ctx_turned,
        hidden,
        active,
        slope,
        grad_down,
        grad_second,
        hat,
        weights,
    )
    return input_grad, slot_grads.reshape(SLOTS, width, width), vector_sums


def collected_tiles(tile_low, owners, slots):
    mine = owners == lax.axis_index("dp")
    local = jnp.where(mine[:, None, None], tile_low[slots], jnp.zeros((), tile_low.dtype))
    return lax.psum(local, "dp")


def summed_over_slice(parts, vector_terms, owners, slots):
    myself = lax.axis_index("dp")

    def add(held, items):
        part, owner, slot = items
        total = lax.psum(part.astype(jnp.float32), "dp")
        here = (owner == myself) & (slot == jnp.arange(SLOTS, dtype=jnp.int32))
        return held + jnp.where(here[:, None, None], total[None], 0.0), None

    empty = jnp.zeros((SLOTS,) + parts.shape[1:], jnp.float32)
    return lax.scan(add, empty, (parts, owners, slots))[0], lax.psum(vector_terms, "dp")


def body(
    inputs,
    cotangent,
    counts,
    lengths,
    owners,
    tile_master,
    tile_first,
    tile_second,
    tile_ema,
    bias_vals,
    gain_vals,
    vector_first,
    vector_second,
    vector_ema,
):
    tokens = inputs.shape[0]
    small = lax.axis_size("dp") == GROUP
    gain_scale = float(tokens * lax.axis_size("dp")) ** (-0.5)
    if small:
        (
            query,
            keyed,
            valued,
            probs,
            context,
            x_turned,
            ctx_turned,
            hidden,
            active,
            slope,
            grad_down,
            mixed,
            grad_second,
            hat,
            weights,
            inverse,
            late_sums,
        ) = gathered_and_forwarded(
            counts,
            lengths,
            owners,
            bias_vals,
            gain_vals,
            inputs,
            cotangent,
            tile_master,
        )
        input_grad, slot_grads, full_sums = backward_and_reduced(
            owners,
            probs,
            query,
            keyed,
            valued,
            inverse,
            gain_vals,
            late_sums,
            context,
            x_turned,
            ctx_turned,
            hidden,
            active,
            slope,
            grad_down,
            grad_second,
            hat,
            weights,
        )
    else:
        slots = tile_slots(owners)
        vectors = jnp.concatenate([bias_vals, gain_vals], 0)
        weights = collected_tiles(tile_master[0].astype(jnp.bfloat16), owners, slots)
        query, keyed, valued, probs, context, hat, inverse = attended(
            counts, lengths, inputs, weights, vectors
        )
        mixed, grad_first, grad_branch, grad_context, up_grads, down_grads, late_sums = fed_forward_both(
            counts, lengths, hat, inverse, cotangent, weights, vectors
        )
        input_grad, early_grads, early_sums = attended_back(
            probs, query, keyed, valued, inputs, context, grad_context, grad_branch, grad_first, weights
        )
        parts = jnp.concatenate([early_grads, up_grads, down_grads], 0)
        slot_grads, full_sums = summed_over_slice(parts, late_sums + early_sums, owners, slots)
    return updated(
        gain_scale,
        slot_grads,
        tile_master,
        tile_first,
        tile_second,
        tile_ema,
        full_sums,
        bias_vals,
        gain_vals,
        vector_first,
        vector_second,
        vector_ema,
        mixed,
        input_grad,
    )


def solution(mesh):
    placed = (
        P("dp", None),
        P("dp", None),
        P("dp", None),
        P("dp", None),
        P(),
        P("dp", None, None, None),
        P("dp", None, None, None),
        P("dp", None, None, None),
        P("dp", None, None, None),
        P(),
        P(),
        P(),
        P(),
        P(),
    )
    return jax.shard_map(
        body,
        mesh=mesh,
        in_specs=placed,
        out_specs=(
            P("dp", None),
            P("dp", None),
            P("dp", None, None, None),
            P("dp", None, None, None),
            P("dp", None, None, None),
            P("dp", None, None, None),
            P("dp", None, None, None),
            P(),
            P(),
            P(),
            P(),
        ),
        check_vma=False,
    )
```

```python
import functools

import jax
import jax.numpy as jnp
from jax import lax
from jax.experimental import pallas as pl
from jax.experimental.pallas import tpu as pltpu
from jax.sharding import PartitionSpec as P

HEADS = 12
BUCKET = 128
SLOTS = 2
TILES = 12
VROWS = 12
STEP = 5

norm_epsilon = 1e-12
tile_rate = 0.03
vector_rate = 0.2
first_decay = 0.5
second_decay = 0.5
adam_epsilon = 1e-08
weight_decay = 0.01
average_rate = 0.9


def tile_slots(owners):
    order = jnp.arange(owners.shape[0], dtype=jnp.int32)
    same = owners[:, None] == owners[None, :]
    earlier = order[None, :] < order[:, None]
    return jnp.sum((same & earlier).astype(jnp.int32), 1)


def adam_update(param, grad, first, second, rate):
    first_new = first_decay * first + (1.0 - first_decay) * grad
    second_new = second_decay * second + (1.0 - second_decay) * grad * grad
    first_hat = first_new / (1.0 - first_decay**STEP)
    second_hat = second_new / (1.0 - second_decay**STEP)
    param_new = param - rate * (
        first_hat / (jnp.sqrt(second_hat) + adam_epsilon) + weight_decay * param
    )
    return (param_new, first_new, second_new)


ROWS = 4 * BUCKET
TAIL_RATE = 0.28
TAIL_SERIES = (
    0.11615256574707405,
    0.06981038475559553,
    0.2631359597579608,
    -0.22983675561378278,
    0.38546775012288165,
    -0.10472989053809521,
)
INV_SQRT_TAU = 0.3989422804014327
ALLOWED = 3.0e38
BARRED = -1000000000.0


def dot(left, right):
    return jnp.dot(left, right, preferred_element_type=jnp.float32)


def dot_back(left, right):
    return lax.dot_general(
        left, right, (((1,), (1,)), ((), ())), preferred_element_type=jnp.float32
    )


def outer(left, right):
    return lax.dot_general(
        left, right, (((0,), (0,)), ((), ())), preferred_element_type=jnp.float32
    )


def passage_facts(counts, lengths, position):
    places = lengths.shape[1]
    big_end = counts[0, 0]
    mid_end = big_end + counts[0, 1]
    all_end = mid_end + counts[0, 2]
    start = jnp.int32(0)
    member = jnp.zeros(position.shape, jnp.int32)
    usable = jnp.zeros(position.shape, jnp.int32)
    for number in range(places):
        size = jnp.where(
            number < big_end,
            4 * BUCKET,
            jnp.where(number < mid_end, 2 * BUCKET, jnp.where(number < all_end, BUCKET, 0)),
        )
        inside = (position >= start) & (position < start + size)
        live = inside & (position < start + lengths[0, number])
        member = jnp.where(inside, number + 1, member)
        usable = jnp.where(live, 1, usable)
        start = start + size
    passage = jnp.where(member > 0, member - 1, places + position // BUCKET)
    return usable, passage


def normalize(values):
    center = jnp.mean(values, -1, keepdims=True)
    centered = values - center
    spread = jnp.mean(centered * centered, -1, keepdims=True)
    inverse = lax.rsqrt(spread + norm_epsilon)
    return centered * inverse, inverse


def normalize_back(grad, hat, inverse):
    center = jnp.mean(grad, -1, keepdims=True)
    along = jnp.mean(grad * hat, -1, keepdims=True)
    return inverse * (grad - center - hat * along)


def columns_total(values):
    return jnp.sum(values, 0, keepdims=True)


def attention_caps(counts, lengths, block):
    at_row = lax.broadcasted_iota(jnp.int32, (ROWS, 1), 0) + block * ROWS
    at_column = lax.broadcasted_iota(jnp.int32, (1, ROWS), 1) + block * ROWS
    _, passage_row = passage_facts(counts, lengths, at_row)
    usable_column, passage_column = passage_facts(counts, lengths, at_column)
    allowed = (passage_row == passage_column) & ((usable_column == 1) | (at_row == at_column))
    return jnp.where(allowed, ALLOWED, BARRED)


def attend_quad(quad, weight, x_ref, vec_ref, cap_ref, q_ref, k_ref, v_ref, p_ref, ctx_ref):
    cols = pl.ds(pl.multiple_of(quad * 256, 256), 256)
    x = x_ref[...]
    query = (dot(x, weight(0, cols)) + vec_ref[0:1, cols]).astype(jnp.bfloat16)
    query = query * jnp.bfloat16(0.125)
    keyed = dot(x, weight(1, cols)).astype(jnp.bfloat16)
    valued = (dot(x, weight(2, cols)) + vec_ref[1:2, cols]).astype(jnp.bfloat16)
    q_ref[...] = query
    k_ref[...] = keyed
    v_ref[...] = valued
    low_half = lax.broadcasted_iota(jnp.int32, (1, 128), 1) < 64
    for pair in range(2):
        part = slice(128 * pair, 128 * pair + 128)
        contexts = []
        for head in range(2):
            here = low_half if head == 0 else ~low_half
            mine = jnp.where(here, query[:, part], jnp.zeros_like(query[:, part]))
            scores = jnp.minimum(dot_back(mine, keyed[:, part]), cap_ref[...])
            exponent = jnp.exp(scores - jnp.max(scores, -1, keepdims=True))
            inverse = 1.0 / jnp.sum(exponent, -1, keepdims=True)
            probability = (exponent * inverse).astype(jnp.bfloat16)
            p_ref[0, 2 * pair + head] = probability
            contexts.append(dot(probability, valued[:, part]))
        both = jnp.where(low_half, contexts[0], contexts[1]).astype(jnp.bfloat16)
        ctx_ref[:, pl.ds(pl.multiple_of(quad * 256 + 128 * pair, 128), 128)] = both


def close_block(w_out, x_ref, vec_ref, ctx_ref, hat_ref, inverse_ref):
    branch = dot(ctx_ref[...], w_out) + vec_ref[2:3, :]
    hat_ref[...], inverse_ref[...] = normalize(x_ref[...].astype(jnp.float32) + branch)


def attend_back_pair(pull, level_from, p_ref, query, keyed, valued):
    low_half = lax.broadcasted_iota(jnp.int32, (1, 128), 1) < 64
    along = pull.astype(jnp.float32) * level_from.astype(jnp.float32)
    by_query, by_key, by_value = [], [], []
    for head in range(2):
        mask = low_half if head == 0 else ~low_half
        mine = jnp.where(mask, pull, jnp.zeros_like(pull))
        level = jnp.sum(jnp.where(mask, along, 0.0), -1, keepdims=True)
        probability = p_ref[head]
        grad_prob = dot_back(mine, valued)
        grad_scores = (probability.astype(jnp.float32) * (grad_prob - level)).astype(jnp.bfloat16)
        by_query.append(dot(grad_scores, keyed))
        by_key.append(outer(grad_scores, query))
        by_value.append(outer(probability, pull))
    grad_query = jnp.where(low_half, by_query[0], by_query[1]) * 0.125
    grad_key = jnp.where(low_half, by_key[0], by_key[1])
    grad_value = jnp.where(low_half, by_value[0], by_value[1])
    return [value.astype(jnp.bfloat16) for value in (grad_query, grad_key, grad_value)]


def gelu_parts(up):
    near = 1.0 / (1.0 + TAIL_RATE * jnp.abs(up))
    decay = jnp.exp(up * up * -0.5)
    series = jnp.full_like(near, TAIL_SERIES[-1])
    for term in TAIL_SERIES[-2::-1]:
        series = series * near + term
    tail = series * near * decay
    share = jnp.where(up < 0.0, tail, 1.0 - tail)
    slope = share + up * (decay * INV_SQRT_TAU)
    return (up * share).astype(jnp.bfloat16), slope


def attend_forward(
    counts,
    lengths,
    x_ref,
    w_hbm,
    vec_ref,
    q_ref,
    k_ref,
    v_ref,
    p_ref,
    ctx_ref,
    hat_ref,
    inverse_ref,
    w_buf,
    cap_ref,
    w_sem,
):
    block, quad = pl.program_id(0), pl.program_id(1)
    loads = [pltpu.make_async_copy(w_hbm.at[at], w_buf.at[at], w_sem.at[at]) for at in range(4)]

    @pl.when((block == 0) & (quad == 0))
    def _():
        for load in loads:
            load.start()
        for load in loads:
            load.wait()

    @pl.when(quad == 0)
    def _():
        cap_ref[...] = attention_caps(counts, lengths, block)

    def weight(at, cols):
        return w_buf[at, :, cols]

    attend_quad(quad, weight, x_ref, vec_ref, cap_ref, q_ref, k_ref, v_ref, p_ref, ctx_ref)

    @pl.when(quad == 2)
    def _():
        close_block(w_buf[3], x_ref, vec_ref, ctx_ref, hat_ref, inverse_ref)


def attended(counts, lengths, x, weights, vectors):
    tokens, width = x.shape
    blocks = tokens // ROWS
    low = jnp.bfloat16
    smem = pl.BlockSpec(memory_space=pltpu.SMEM)
    quad = pl.BlockSpec((ROWS, 256), lambda b, h: (b, h))
    rows = pl.BlockSpec((ROWS, width), lambda b, h: (b, 0))
    shaped = jax.ShapeDtypeStruct
    return pl.pallas_call(
        attend_forward,
        grid=(blocks, 3),
        out_shape=(
            shaped((tokens, width), low),
            shaped((tokens, width), low),
            shaped((tokens, width), low),
            shaped((blocks, HEADS, ROWS, ROWS), low),
            shaped((tokens, width), low),
            shaped((tokens, width), jnp.float32),
            shaped((tokens, 1), jnp.float32),
        ),
        in_specs=[
            smem,
            smem,
            rows,
            pl.BlockSpec(memory_space=pl.ANY),
            pl.BlockSpec((VROWS, width), lambda b, h: (0, 0)),
        ],
        out_specs=(
            quad,
            quad,
            quad,
            pl.BlockSpec((1, 4, ROWS, ROWS), lambda b, h: (b, h, 0, 0)),
            rows,
            rows,
            pl.BlockSpec((ROWS, 1), lambda b, h: (b, 0)),
        ),
        scratch_shapes=[
            pltpu.VMEM((4, width, width), low),
            pltpu.VMEM((ROWS, ROWS), jnp.float32),
            pltpu.SemaphoreType.DMA((4,)),
        ],
        compiler_params=pltpu.CompilerParams(vmem_limit_bytes=56 * 2**20),
        name="attend_forward",
    )(counts, lengths, x, weights, vectors)


def feed_forward_both(
    counts,
    lengths,
    hat_ref,
    inverse_ref,
    cot_ref,
    w_hbm,
    vec_ref,
    mixed_ref,
    first_ref,
    branch_ref,
    context_ref,
    up_grad_ref,
    down_grad_ref,
    sum_ref,
    w_buf,
    active_ref,
    up_ref,
    hidden_ref,
    down_ref,
    slope_ref,
    w_sem,
):
    step = pl.program_id(0)
    blocks = pl.num_programs(0) - 4
    loads = [
        pltpu.make_async_copy(w_hbm.at[3 + at], w_buf.at[at], w_sem.at[at]) for at in range(9)
    ]

    @pl.when(step == 0)
    def _():
        for load in loads[1:] + loads[:1]:
            load.start()
        sum_ref[...] = jnp.zeros_like(sum_ref)
        for load in loads[1:] + loads[:1]:
            load.wait()

    @pl.when(step < blocks)
    def _():
        here = pl.ds(pl.multiple_of(step * ROWS, ROWS), ROWS)
        at_row = lax.broadcasted_iota(jnp.int32, (ROWS, 1), 0) + step * ROWS
        live = passage_facts(counts, lengths, at_row)[0].astype(jnp.float32)
        hat = hat_ref[...]
        hidden = hat * vec_ref[10:11, :] + vec_ref[8:9, :]
        hidden_low = hidden.astype(jnp.bfloat16)
        hidden_ref[here, :] = hidden_low
        total = hidden + vec_ref[7:8, :]
        for tile in range(4):
            up = dot(hidden_low, w_buf[1 + tile]) + vec_ref[3 + tile : 4 + tile, :]
            active, slope = gelu_parts(up)
            slope_ref[tile] = slope.astype(jnp.bfloat16)
            active_ref[tile, here, :] = active
            total = total + dot(active, w_buf[5 + tile])
        hat_two, inverse_two = normalize(total)
        mixed_ref[...] = ((hat_two * vec_ref[11:12, :] + vec_ref[9:10, :]) * live).astype(jnp.bfloat16)
        grad_out = cot_ref[...].astype(jnp.float32) * live
        sum_ref[11:12, :] += columns_total(grad_out * hat_two)
        sum_ref[9:10, :] += columns_total(grad_out)
        second = normalize_back(grad_out * vec_ref[11:12, :], hat_two, inverse_two)
        down_low = second.astype(jnp.bfloat16)
        down_ref[here, :] = down_low
        sum_ref[7:8, :] += columns_total(down_low.astype(jnp.float32))
        grad_hidden = second
        for tile in range(4):
            pulled = dot_back(down_low, w_buf[5 + tile])
            up_low = (pulled * slope_ref[tile].astype(jnp.float32)).astype(jnp.bfloat16)
            up_ref[tile, here, :] = up_low
            sum_ref[3 + tile : 4 + tile, :] += columns_total(up_low.astype(jnp.float32))
            grad_hidden = grad_hidden + dot_back(up_low, w_buf[1 + tile])
        sum_ref[10:11, :] += columns_total(grad_hidden * hat)
        sum_ref[8:9, :] += columns_total(grad_hidden)
        grad_first = normalize_back(grad_hidden * vec_ref[10:11, :], hat, inverse_ref[...])
        first_ref[...] = grad_first
        branch_low = grad_first.astype(jnp.bfloat16)
        branch_ref[...] = branch_low
        sum_ref[2:3, :] += columns_total(branch_low.astype(jnp.float32))
        context_ref[...] = dot_back(branch_low, w_buf[0]).astype(jnp.bfloat16)

    @pl.when(step >= blocks)
    def _():
        tile = step - blocks
        up_grad_ref[0] = outer(hidden_ref[...], up_ref[tile]).astype(jnp.bfloat16)
        down_grad_ref[0] = outer(active_ref[tile], down_ref[...]).astype(jnp.bfloat16)


def fed_forward_both(counts, lengths, hat, inverse, cotangent, weights, vectors):
    tokens, width = hat.shape
    blocks = tokens // ROWS
    low = jnp.bfloat16
    smem = pl.BlockSpec(memory_space=pltpu.SMEM)
    shaped = jax.ShapeDtypeStruct

    def block_of(step):
        return jnp.minimum(step, blocks - 1)

    def tile_of(step):
        return jnp.maximum(step - blocks, 0)

    rows = pl.BlockSpec((ROWS, width), lambda i: (block_of(i), 0))
    tile = pl.BlockSpec((1, width, width), lambda i: (tile_of(i), 0, 0))
    return pl.pallas_call(
        feed_forward_both,
        grid=(blocks + 4,),
        out_shape=(
            shaped((tokens, width), low),
            shaped((tokens, width), jnp.float32),
            shaped((tokens, width), low),
            shaped((tokens, width), low),
            shaped((4, width, width), low),
            shaped((4, width, width), low),
            shaped((16, width), jnp.float32),
        ),
        in_specs=[
            smem,
            smem,
            rows,
            pl.BlockSpec((ROWS, 1), lambda i: (block_of(i), 0)),
            rows,
            pl.BlockSpec(memory_space=pl.ANY),
            pl.BlockSpec((VROWS, width), lambda i: (0, 0)),
        ],
        out_specs=(
            rows,
            rows,
            rows,
            rows,
            tile,
            tile,
            pl.BlockSpec((16, width), lambda i: (0, 0)),
        ),
        scratch_shapes=[
            pltpu.VMEM((9, width, width), low),
            pltpu.VMEM((4, tokens, width), low),
            pltpu.VMEM((4, tokens, width), low),
            pltpu.VMEM((tokens, width), low),
            pltpu.VMEM((tokens, width), low),
            pltpu.VMEM((4, ROWS, width), low),
            pltpu.SemaphoreType.DMA((9,)),
        ],
        compiler_params=pltpu.CompilerParams(vmem_limit_bytes=60 * 2**20),
        name="feed_forward_both",
    )(counts, lengths, hat, inverse, cotangent, weights, vectors)


def attend_backward(
    p_ref,
    q_ref,
    k_ref,
    v_ref,
    x_ref,
    ctx_ref,
    grad_ctx_ref,
    branch_ref,
    first_ref,
    w_ref,
    input_ref,
    grad_ref,
    sum_ref,
    pulled,
):
    step = pl.program_id(0)
    quad, block = step // 2, lax.rem(step, 2)
    here = pl.ds(pl.multiple_of(block * ROWS, ROWS), ROWS)
    cols = pl.ds(pl.multiple_of(quad * 256, 256), 256)

    @pl.when(step == 0)
    def _():
        sum_ref[...] = jnp.zeros_like(sum_ref)
        input_ref[...] = first_ref[...]

    for pair in range(2):
        half = slice(128 * pair, 128 * pair + 128)
        at = pl.ds(pl.multiple_of(quad * 256 + 128 * pair, 128), 128)
        heads = p_ref.at[0, pl.ds(2 * pair, 2)]
        grads = attend_back_pair(
            grad_ctx_ref[here, at], ctx_ref[here, at], heads, q_ref[:, half], k_ref[:, half], v_ref[:, half]
        )
        for number, grad in enumerate(grads):
            pulled[number, here, half] = grad
        sum_ref[0:1, at] += columns_total(grads[0].astype(jnp.float32))
        sum_ref[1:2, at] += columns_total(grads[2].astype(jnp.float32))

    more = input_ref[here, :]
    for at in range(3):
        more = more + dot_back(pulled[at, here, :], w_ref[at, :, cols])
    input_ref[here, :] = more

    @pl.when(block == 1)
    def _():
        for tile in range(3):
            grad_ref[tile, :, cols] = outer(x_ref[...], pulled[tile]).astype(jnp.bfloat16)
        grad_ref[3, :, cols] = outer(ctx_ref[...], branch_ref[:, cols]).astype(jnp.bfloat16)


def attended_back(probs, query, keyed, valued, x, context, grad_context, grad_branch, grad_first, weights):
    tokens, width = x.shape
    low = jnp.bfloat16
    shaped = jax.ShapeDtypeStruct
    once = pl.Buffered(1)
    quad = pl.BlockSpec((ROWS, 256), lambda i: (lax.rem(i, 2), i // 2))
    whole = pl.BlockSpec((tokens, width), lambda i: (0, 0), pipeline_mode=once)
    return pl.pallas_call(
        attend_backward,
        grid=(6,),
        out_shape=(
            shaped((tokens, width), jnp.float32),
            shaped((4, width, width), low),
            shaped((16, width), jnp.float32),
        ),
        in_specs=[
            pl.BlockSpec((1, 4, ROWS, ROWS), lambda i: (lax.rem(i, 2), i // 2, 0, 0)),
            quad,
            quad,
            quad,
            whole,
            whole,
            whole,
            whole,
            whole,
            pl.BlockSpec((3, width, width), lambda i: (0, 0, 0), pipeline_mode=once),
        ],
        out_specs=(
            whole,
            pl.BlockSpec((4, width, width), lambda i: (0, 0, 0), pipeline_mode=once),
            pl.BlockSpec((16, width), lambda i: (0, 0)),
        ),
        scratch_shapes=[pltpu.VMEM((3, tokens, 256), low)],
        compiler_params=pltpu.CompilerParams(vmem_limit_bytes=56 * 2**20),
        name="attend_backward",
    )(probs, query, keyed, valued, x, context, grad_context, grad_branch, grad_first, weights)


def moved(param, grad, first, second, average, rate):
    param_new, first_new, second_new = adam_update(param, grad, first, second, rate)
    return param_new, first_new, second_new, average_rate * average + (1.0 - average_rate) * param_new


def update_kernel(
    gain_scale,
    grad_ref,
    master_ref,
    first_ref,
    second_ref,
    ema_ref,
    vec_grad_ref,
    bias_ref,
    gain_ref,
    vec_first_ref,
    vec_second_ref,
    vec_ema_ref,
    mixed_in,
    input_in,
    master_out,
    first_out,
    second_out,
    ema_out,
    copy_out,
    vec_out,
    vec_first_out,
    vec_second_out,
    vec_ema_out,
    mixed_out,
    input_out,
    vec_ref,
):
    mixed_out[...] = mixed_in[...]
    input_out[...] = input_in[...]

    @pl.when((pl.program_id(0) == 0) & (pl.program_id(1) == 0))
    def _():
        vec_ref[0:10, :] = bias_ref[...]
        vec_ref[10:12, :] = gain_ref[...]
        vec_grad = vec_grad_ref[0:VROWS, :] * gain_scale
        vec_out[...], vec_first_out[...], vec_second_out[...], vec_ema_out[...] = moved(
            vec_ref[...], vec_grad, vec_first_ref[...], vec_second_ref[...], vec_ema_ref[...], vector_rate
        )

    grad = grad_ref[...].astype(jnp.float32) * gain_scale
    result = moved(master_ref[0], grad, first_ref[0], second_ref[0], ema_ref[0], tile_rate)
    master_out[0], first_out[0], second_out[0], ema_out[0] = result
    copy_out[0] = result[0].astype(jnp.bfloat16)


def updated(
    gain_scale,
    slot_grads,
    master,
    first,
    second,
    ema,
    vec_grad,
    bias,
    gain,
    vec_first,
    vec_second,
    vec_ema,
    mixed,
    input_grad,
):
    width = master.shape[-1]
    chunk = 192
    tile = pl.BlockSpec((1, 1, chunk, width), lambda s, r: (0, s, r, 0))
    steps = width // chunk
    rows = pl.BlockSpec((mixed.shape[0] // (SLOTS * steps), width), lambda s, r: (s * steps + r, 0))

    def whole(value):
        return pl.BlockSpec(value.shape, lambda s, r: (0, 0))

    shaped = jax.ShapeDtypeStruct
    tile_shape = shaped(master.shape, jnp.float32)
    vec_shape = shaped((VROWS, width), jnp.float32)
    results = pl.pallas_call(
        functools.partial(update_kernel, gain_scale),
        grid=(SLOTS, steps),
        out_shape=(tile_shape,) * 4
        + (shaped(master.shape, jnp.bfloat16),)
        + (vec_shape,) * 4
        + (shaped(mixed.shape, mixed.dtype), shaped(input_grad.shape, input_grad.dtype)),
        in_specs=[pl.BlockSpec((1, chunk, width), lambda s, r: (s, r, 0))]
        + [tile] * 4
        + [whole(value) for value in (vec_grad, bias, gain, vec_first, vec_second, vec_ema)]
        + [rows] * 2,
        out_specs=(tile,) * 5 + (whole(vec_first),) * 4 + (rows,) * 2,
        scratch_shapes=[pltpu.VMEM((VROWS, width), jnp.float32)],
        compiler_params=pltpu.CompilerParams(vmem_limit_bytes=62 * 2**20),
        name="update",
    )(
        slot_grads,
        master,
        first,
        second,
        ema,
        vec_grad,
        bias,
        gain,
        vec_first,
        vec_second,
        vec_ema,
        mixed,
        input_grad,
    )
    return results[-2:] + results[:-2]


MESH = pl.DeviceIdType.MESH
GROUP = 32
PAIRS = TILES // 2
PLANE = 8
PIECE = 96
PAIR_TILES = ((0, 1), (2, 3), (4, 8), (5, 9), (6, 10), (7, 11))


def remote(src, dst, send, recv, device):
    return pltpu.make_async_remote_copy(
        src_ref=src, dst_ref=dst, send_sem=send, recv_sem=recv, device_id=(device,), device_id_type=MESH
    )


def place(device):
    core = lax.rem(device, 2)
    x = lax.rem(device // 2, 2)
    y = lax.rem(device // 4, 2)
    z = device // 8
    return z, y, x, core


def start(copies):
    for copy in copies:
        copy.start()


def arrive(copies):
    for copy in copies:
        copy.wait_recv()


def greet(z, in_plane):
    barrier = pltpu.get_barrier_semaphore()
    for hop in range(1, PLANE):
        other = z * PLANE + lax.rem(in_plane + hop, PLANE)
        pl.semaphore_signal(barrier, inc=1, device_id=(other,), device_id_type=MESH)
    for hop in range(1, 4):
        other = lax.rem(z + hop, 4) * PLANE + in_plane
        pl.semaphore_signal(barrier, inc=1, device_id=(other,), device_id_type=MESH)
    pl.semaphore_wait(barrier, PLANE + 2)


def along_z(z, in_plane):
    inner = (1 + z // 2) * PLANE + in_plane
    other_middle = (3 - z) * PLANE + in_plane
    outer_end = lax.rem(lax.rem(z + 3, 4) * 3, 4) * PLANE + in_plane
    return inner, other_middle, outer_end


def third(part):
    return pl.ds(256 * part, 256)


UNITS = [(0, 4, pl.ds(256 * part, 256)) for part in range(3)]
UNITS += [(2 * pair, 2, pl.ds(0, 768)) for pair in range(2, PAIRS)]
Z_PARTS = (pl.ds(0, 512), pl.ds(512, 256))


POSITIONS = [tile for pair in PAIR_TILES for tile in pair]


def slot_number(owners, tile):
    number = jnp.int32(0)
    for earlier in range(tile):
        number = number + jnp.where(owners[earlier] == owners[tile], 1, 0)
    return number

FRONT_PLAN = (
    (
        ("open",),
        ("swap", 0),
        ("sent", 0),
        ("swap", 1),
        ("choose", 0),
        ("end", 0),
        ("sent", 1),
        ("middle", 0),
        ("choose", 1),
        ("end", 1),
        ("swap", 2),
        ("total", 0),
        ("end", 3, 0),
        ("middle", 1),
        ("mid", 0),
        ("choose", 2),
        ("end", 2),
        ("end", 3, 1),
        ("far", 0),
        ("middle", 3, 0),
        ("total", 1),
        ("caps",),
        ("middle", 3, 1),
        ("end", 4, 0),
        ("mid", 1),
        ("near", 0),
        ("total", 3, 0),
        ("end", 5, 0),
        ("middle", 2),
        ("end", 4, 1),
        ("total", 3, 1),
        ("far", 1),
        ("finish", 0),
    ),
    (
        ("middle", 4, 0),
        ("total", 2),
        ("mid", 3),
        ("middle", 4, 1),
        ("end", 5, 1),
    ),
    (
        ("mid", 2),
        ("end", 6, 0),
        ("middle", 5, 0),
        ("near", 1),
        ("total", 4, 1),
        ("far", 3),
        ("finish", 1),
        ("far", 2),
        ("middle", 5, 1),
        ("end", 6, 1),
        ("total", 4, 0),
    ),
    (
        ("total", 5, 0),
        ("middle", 6, 0),
        ("mid", 4),
        ("total", 5, 1),
        ("middle", 6, 1),
    ),
    (
        ("total", 6, 1),
        ("mid", 5),
        ("near", 2),
        ("far", 4),
        ("total", 6, 0),
        ("finish", 2),
        ("keep", 0),
        ("keep", 1),
    ),
    (
        ("mid", 6),
        ("near", 3),
        ("near", 4),
        ("far", 5),
    ),
    (
        ("far", 6),
        ("finish", 4),
        ("keep", 3),
        ("finish", 3),
        ("keep", 2),
    ),
    (
        ("near", 5),
    ),
    (
        ("near", 6),
        ("finish", 5),
        ("keep", 4),
    ),
    (
        ("finish", 6),
        ("keep", 5),
    ),
)


def gather_and_forward(
    counts,
    lengths,
    owners,
    bias_ref,
    gain_ref,
    x_hbm,
    cot_hbm,
    master_hbm,
    q_ref,
    k_ref,
    v_ref,
    p_ref,
    ctx_hbm,
    x_turned_hbm,
    ctx_turned_hbm,
    hidden_hbm,
    active_hbm,
    slope_hbm,
    down_hbm,
    mixed_hbm,
    second_hbm,
    hat_hbm,
    w_out,
    inverse_ref,
    sum_ref,
    vec_ref,
    cap_ref,
    wide,
    low,
    stage_a,
    stage_b,
    stage_c,
    chosen,
    from_end,
    from_middle,
    w_buf,
    x_then_hidden,
    x_turned,
    ctx_turned,
    hidden_turned,
    ctx_ref,
    cot_then_down,
    mixed_ref,
    hat_ref,
    slope_buf,
    active_buf,
    wide_sem,
    load_sem,
    store_sem,
    half_sem,
    tile_sem,
    out_sem,
    swap_send,
    swap_recv,
    z_send,
    z_recv,
    mid_send,
    mid_recv,
    far_send,
    far_recv,
    near_send,
    near_recv,
):
    step = pl.program_id(0)
    width = 8 * PIECE
    me = lax.axis_index("dp")
    z, y, x, core = place(me)
    in_plane = lax.rem(me, PLANE)
    sibling = me + 1 - 2 * core
    x_peer = me + 2 - 4 * x
    y_peer = me + 4 - 8 * y
    z_targets = along_z(z, in_plane)
    stages = (stage_a, stage_b, stage_c)
    is_end = (z == 0) | (z == 3)
    is_middle = (z == 1) | (z == 2)

    def piece_rows(cell_core, cell_x, cell_y):
        return pl.ds(pl.multiple_of(((cell_core * 2 + cell_x) * 2 + cell_y) * PIECE, 16), PIECE)

    def wide_load(part):
        cols = third(part)
        return pltpu.make_async_copy(master_hbm.at[:, cols], wide.at[:, cols], wide_sem.at[part])

    def swap(part):
        wide_load(part).wait()
        for slot in range(SLOTS):
            master = wide[width * slot : width * (slot + 1), third(part)]
            low[slot, :, third(part)] = master.astype(jnp.bfloat16)

        def send(hop, carry):
            target = lax.rem(in_plane + hop, PLANE)
            _, ty, tx, tc = place(target)
            remote(
                low.at[:, piece_rows(tc, tx, ty), third(part)],
                stages[part].at[pl.ds(2 * in_plane, 2)],
                swap_send.at[part],
                swap_recv.at[part],
                z * PLANE + target,
            ).start()
            return carry

        lax.fori_loop(1, PLANE, send, 0)
        stages[part][pl.ds(2 * in_plane, 2)] = low[:, piece_rows(core, x, y), third(part)]
        if part == 0:
            start([load(0), load(1)])

    def swap_wait(part, sem):
        most = stages[part].at[pl.ds(0, 2 * PLANE - 2)]
        pltpu.make_async_copy(most, most, sem.at[part]).wait()

    def z_copy(unit, part, level):
        first, count, cols = UNITS[unit]
        tiles = pl.ds(first, count)
        cols = cols if count == 4 else Z_PARTS[part]
        src = w_buf.at[tiles, core, x, y, :, cols] if level == 2 else chosen.at[tiles, :, cols]
        dst = (from_end.at[tiles, :, cols], from_middle.at[tiles, :, cols], src)[level]
        at = level, unit, part
        return remote(src, dst, z_send.at[at], z_recv.at[at], z_targets[level])

    def z_parts(unit):
        return range(1 if UNITS[unit][1] == 4 else 2)

    def z_end(unit, part=0):
        @pl.when(is_end)
        def _():
            z_copy(unit, part, 0).start()

    def z_rows(unit, part):
        first, count, cols = UNITS[unit]
        return pl.ds(first, count), cols if count == 4 else Z_PARTS[part]

    def z_middle(unit, part=0):
        @pl.when(is_middle)
        def _():
            z_copy(unit, part, 0).wait_recv()
            tiles, cols = z_rows(unit, part)
            chosen[tiles, :, cols] = chosen[tiles, :, cols] + from_end[tiles, :, cols]
            z_copy(unit, part, 1).start()

    def z_total(unit, part=0):
        @pl.when(is_middle)
        def _():
            z_copy(unit, part, 1).wait_recv()
            tiles, cols = z_rows(unit, part)
            w_buf[tiles, core, x, y, :, cols] = chosen[tiles, :, cols] + from_middle[tiles, :, cols]
            z_copy(unit, part, 2).start()

    def mid_copies(unit):
        first, count, cols = UNITS[unit]
        copies = []
        for n, peer in enumerate((y_peer, x_peer)):
            spot = w_buf.at[pl.ds(first + n * count // 2, count // 2), core, x, y, :, cols]
            copies.append(remote(spot, spot, mid_send.at[unit, n], mid_recv.at[unit, n], peer))
        return copies

    def far_copies(unit):
        first, count, cols = UNITS[unit]
        half = count // 2
        by_row = w_buf.at[pl.ds(first, half), core, x, :, :, cols]
        by_column = w_buf.at[pl.ds(first + half, half), core, :, y, :, cols]
        return [
            remote(spot, spot, far_send.at[unit, n], far_recv.at[unit, n], peer)
            for n, (spot, peer) in enumerate(((by_row, x_peer), (by_column, y_peer)))
        ]

    def near_copy(unit):
        first, count, cols = UNITS[unit]
        spot = w_buf.at[pl.ds(first, count), core, :, :, :, cols]
        return remote(spot, spot, near_send.at[unit], near_recv.at[unit], sibling)

    def give_mid(unit):
        @pl.when(is_end)
        def _():
            arrive([z_copy(unit, part, 2) for part in z_parts(unit)])

        start(mid_copies(unit))

    def give_far(unit):
        arrive(mid_copies(unit))
        start(far_copies(unit))

    def give_near(unit):
        arrive(far_copies(unit))
        near_copy(unit).start()

    def finish(unit):
        near_copy(unit).wait_recv()

    def choose(part):
        swap_wait(part, swap_recv)
        for pair in range(PAIRS):
            for n, tile in enumerate(PAIR_TILES[pair]):
                owner = owners[tile]
                value = stages[part][SLOTS * lax.rem(owner, PLANE) + slot_number(owners, tile)]
                chosen[2 * pair + n, :, third(part)] = jnp.where(
                    owner // PLANE == z, value, jnp.zeros_like(value)
                )

    def load(at):
        src = (x_hbm, cot_hbm)[at]
        dst = (x_then_hidden, cot_then_down)[at]
        return pltpu.make_async_copy(src, dst, load_sem.at[at])

    def store(at):
        src, dst = (
            (hidden_turned, hidden_hbm),
            (ctx_ref, ctx_hbm),
            (hat_ref, hat_hbm),
            None,
            None,
            None,
            (x_turned, x_turned_hbm),
            (ctx_turned, ctx_turned_hbm),
        )[at]
        return pltpu.make_async_copy(src, dst, store_sem.at[at])

    def half_stores(half):
        rows = pl.ds(ROWS * half, ROWS)
        pairs = ((cot_then_down, down_hbm), (mixed_ref, mixed_hbm), (wide, second_hbm))
        return [
            pltpu.make_async_copy(src.at[rows], dst.at[rows], half_sem.at[half, at])
            for at, (src, dst) in enumerate(pairs)
        ]

    def w_store(pair):
        two = pl.ds(2 * pair, 2)
        return pltpu.make_async_copy(w_buf.at[two], w_out.at[two], out_sem.at[pair])

    def weight(at, cols=slice(None)):
        value = w_buf[at, :, :, :, :, cols]
        return value.reshape(width, value.shape[-1])

    def open_all():
        start([wide_load(part) for part in range(3)])
        sum_ref[...] = jnp.zeros_like(sum_ref)
        vec_ref[0:10, :] = bias_ref[...]
        vec_ref[10:12, :] = gain_ref[...]
        greet(z, in_plane)

    def make_caps():
        for block in range(2):
            cap_ref[block] = attention_caps(counts, lengths, block)
        load(0).wait()
        x_turned[...] = x_then_hidden[...].T
        store(6).start()

    actions = {
        "open": open_all,
        "caps": make_caps,
        "swap": swap,
        "sent": lambda part: swap_wait(part, swap_send),
        "choose": choose,
        "end": z_end,
        "middle": z_middle,
        "total": z_total,
        "mid": give_mid,
        "far": give_far,
        "near": give_near,
        "finish": finish,
        "keep": lambda pair: w_store(pair).start(),
    }

    for at, work in enumerate(FRONT_PLAN):

        @pl.when(step == at)
        def _():
            for name, *rest in work:
                actions[name](*rest)

    quad, block = step // 2, lax.rem(step, 2)
    here = pl.ds(pl.multiple_of(block * ROWS, ROWS), ROWS)

    @pl.when(step < 6)
    def _():
        attend_quad(
            quad,
            weight,
            x_then_hidden.at[here],
            vec_ref,
            cap_ref.at[block],
            q_ref,
            k_ref,
            v_ref,
            p_ref,
            ctx_ref.at[here],
        )

    @pl.when((step >= 4) & (step < 6))
    def _():
        branch = dot(ctx_ref[here, :], weight(3)) + vec_ref[2:3, :]
        hat, inverse = normalize(x_then_hidden[here, :].astype(jnp.float32) + branch)
        hat_ref[here, :] = hat.astype(jnp.bfloat16)
        inverse_ref[here, :] = inverse
        hidden = hat * vec_ref[10:11, :] + vec_ref[8:9, :]
        hidden_low = hidden.astype(jnp.bfloat16)
        x_then_hidden[here, :] = hidden_low
        hidden_turned[:, here] = hidden_low.T
        ctx_turned[:, here] = ctx_ref[here, :].T
        wide[here, :] = hidden + vec_ref[7:8, :]

    @pl.when(step == 5)
    def _():
        start([store(0), store(1), store(2), store(7)])

    turn = step - 6
    slot = lax.rem(turn, 2)

    def tile_stores(source_slot, tile):
        return [
            pltpu.make_async_copy(src.at[source_slot], dst.at[tile], tile_sem.at[source_slot, at])
            for at, (src, dst) in enumerate(((active_buf, active_hbm), (slope_buf, slope_hbm)))
        ]

    @pl.when(turn >= 2)
    def _():
        for copy in tile_stores(slot, 0):
            copy.wait()

    @pl.when(turn >= 0)
    def _():
        for half in range(2):
            rows = slice(ROWS * half, ROWS * half + ROWS)
            up = dot(x_then_hidden[rows, :], weight(4 + 2 * turn)) + vec_ref[pl.ds(3 + turn, 1), :]
            active, slope = gelu_parts(up)
            slope_buf[slot, rows, :] = slope.astype(jnp.bfloat16)
            active_buf[slot, :, rows] = active.T
            wide[rows, :] = wide[rows, :] + dot(active, weight(5 + 2 * turn))
        start(tile_stores(slot, turn))

    @pl.when(step == 9)
    def _():
        load(1).wait()
        for half in range(2):
            rows = slice(ROWS * half, ROWS * half + ROWS)
            at_row = lax.broadcasted_iota(jnp.int32, (ROWS, 1), 0) + half * ROWS
            live = passage_facts(counts, lengths, at_row)[0].astype(jnp.float32)
            hat, inverse = normalize(wide[rows, :])
            mixed = (hat * vec_ref[11:12, :] + vec_ref[9:10, :]) * live
            mixed_ref[rows, :] = mixed.astype(jnp.bfloat16)
            grad_out = cot_then_down[rows, :].astype(jnp.float32) * live
            sum_ref[11:12, :] += columns_total(grad_out * hat)
            sum_ref[9:10, :] += columns_total(grad_out)
            second = normalize_back(grad_out * vec_ref[11:12, :], hat, inverse)
            wide[rows, :] = second
            down_low = second.astype(jnp.bfloat16)
            cot_then_down[rows, :] = down_low
            sum_ref[7:8, :] += columns_total(down_low.astype(jnp.float32))
            start(half_stores(half))
        for at in range(2):
            for copy in tile_stores(at, 0):
                copy.wait()
        for pair in range(PAIRS):
            w_store(pair).wait()
        swap_wait(2, swap_send)
        for unit in range(len(UNITS)):
            for copy in mid_copies(unit) + far_copies(unit) + [near_copy(unit)]:
                copy.wait_send()

            @pl.when(is_end)
            def _():
                for part in z_parts(unit):
                    z_copy(unit, part, 0).wait_send()

            @pl.when(is_middle)
            def _():
                for part in z_parts(unit):
                    z_copy(unit, part, 1).wait_send()
                    z_copy(unit, part, 2).wait_send()

        for at in (0, 1, 2, 6, 7):
            store(at).wait()
        for copy in half_stores(0) + half_stores(1):
            copy.wait()


def gathered_and_forwarded(counts, lengths, owners, bias, gain, x, cotangent, master):
    tokens, width = x.shape
    blocks = tokens // ROWS
    low, high = jnp.bfloat16, jnp.float32
    smem = pl.BlockSpec(memory_space=pltpu.SMEM)
    any_space = pl.BlockSpec(memory_space=pl.ANY)
    dma = pltpu.SemaphoreType.DMA
    shaped = jax.ShapeDtypeStruct

    def at(step):
        step = jnp.minimum(step, 5)
        return lax.rem(step, 2), step // 2

    quad = pl.BlockSpec((ROWS, 256), at)
    rows = shaped((tokens, width), low)
    turned = shaped((width, tokens), low)
    cut = (2, 2, 2, PIECE, width)
    units = len(UNITS)
    return pl.pallas_call(
        gather_and_forward,
        grid=(10,),
        out_shape=(
            rows,
            rows,
            rows,
            shaped((blocks, HEADS, ROWS, ROWS), low),
            rows,
            turned,
            turned,
            turned,
            shaped((4, width, tokens), low),
            shaped((4, tokens, width), low),
            rows,
            rows,
            shaped((tokens, width), high),
            rows,
            shaped((TILES,) + cut, low),
            shaped((tokens, 1), high),
            shaped((16, width), high),
        ),
        in_specs=[smem] * 3
        + [pl.BlockSpec(bias.shape, lambda i: (0, 0)), pl.BlockSpec(gain.shape, lambda i: (0, 0))]
        + [any_space] * 3,
        out_specs=(quad, quad, quad, pl.BlockSpec((1, 4, ROWS, ROWS), lambda i: (*at(i), 0, 0)))
        + (any_space,) * 11
        + (
            pl.BlockSpec((tokens, 1), lambda i: (0, 0), pipeline_mode=pl.Buffered(1)),
            pl.BlockSpec((16, width), lambda i: (0, 0)),
        ),
        scratch_shapes=[
            pltpu.VMEM((VROWS, width), high),
            pltpu.VMEM((2, ROWS, ROWS), high),
            pltpu.VMEM((SLOTS * width, width), high),
            pltpu.VMEM((SLOTS, width, width), low),
            pltpu.VMEM((2 * PLANE, PIECE, 256), low),
            pltpu.VMEM((2 * PLANE, PIECE, 256), low),
            pltpu.VMEM((2 * PLANE, PIECE, 256), low),
            pltpu.VMEM((TILES, PIECE, width), low),
            pltpu.VMEM((TILES, PIECE, width), low),
            pltpu.VMEM((TILES, PIECE, width), low),
            pltpu.VMEM((TILES,) + cut, low),
            pltpu.VMEM((tokens, width), low),
            pltpu.VMEM((width, tokens), low),
            pltpu.VMEM((width, tokens), low),
            pltpu.VMEM((width, tokens), low),
            pltpu.VMEM((tokens, width), low),
            pltpu.VMEM((tokens, width), low),
            pltpu.VMEM((tokens, width), low),
            pltpu.VMEM((tokens, width), low),
            pltpu.VMEM((2, tokens, width), low),
            pltpu.VMEM((2, width, tokens), low),
            dma((3,)),
            dma((2,)),
            dma((8,)),
            dma((2, 3)),
            dma((2, 2)),
            dma((PAIRS,)),
            dma((3,)),
            dma((3,)),
            dma((3, units, 2)),
            dma((3, units, 2)),
            dma((units, 2)),
            dma((units, 2)),
            dma((units, 2)),
            dma((units, 2)),
            dma((units,)),
            dma((units,)),
        ],
        compiler_params=pltpu.CompilerParams(
            collective_id=0, has_side_effects=True, vmem_limit_bytes=63 * 2**20
        ),
        name="gather_and_forward",
    )(counts, lengths, owners, bias, gain, x, cotangent, master.reshape(SLOTS * width, width))


BACK_PLAN = (
    (),
    (),
    (
        ("core", 0),
    ),
    (),
    (
        ("core", 1),
        ("far", 0),
    ),
    (),
    (
        ("core", 2),
        ("far", 1),
    ),
    (
        ("mid", 0),
        ("far", 2),
    ),
    (),
    (
        ("core", 3),
        ("mid", 1),
        ("end", 0),
    ),
    (),
    (
        ("far", 3),
        ("end", 1),
        ("mid", 2),
    ),
    (
        ("core", 4),
        ("middle", 0),
    ),
    (),
    (
        ("middle", 1),
        ("end", 2),
        ("mid", 3),
        ("far", 4),
    ),
    (
        ("total", 0),
    ),
    (
        ("middle", 2),
        ("end", 3),
        ("total", 1),
        ("core", 5),
        ("mid", 4),
    ),
    (),
    (
        ("far", 5),
        ("end", 4),
        ("middle", 3),
        ("total", 2),
    ),
    (),
    (
        ("core", 6),
        ("total", 3),
        ("middle", 4),
        ("mid", 5),
        ("far", 6),
        ("total", 4),
        ("end", 5),
        ("mid", 6),
        ("middle", 5),
        ("end", 6),
        ("take", 4),
        ("take", 0),
        ("take", 2),
        ("take", 3),
        ("take", 1),
        ("deliver", 0),
        ("total", 5),
        ("middle", 6),
        ("take", 5),
        ("deliver", 1),
        ("total", 6),
        ("take", 6),
        ("deliver", 2),
        ("sum", 0),
        ("input", 0),
        ("sum", 1),
        ("input", 1),
        ("sum", 2),
    ),
)


def backward_and_reduce(
    owners,
    p_ref,
    q_ref,
    k_ref,
    v_ref,
    inverse_ref,
    gain_ref,
    late_ref,
    ctx_hbm,
    x_turned_hbm,
    ctx_turned_hbm,
    hidden_hbm,
    active_hbm,
    slope_hbm,
    down_hbm,
    second_hbm,
    hat_hbm,
    w_hbm,
    input_hbm,
    slot_grad,
    vec_out,
    w_part,
    acc,
    hidden_then_x,
    active_then_ctx,
    down_then_branch,
    ctx_ref,
    grad_ctx_ref,
    hat_ref,
    slope_then_query,
    up_then_key,
    value_buf,
    part,
    from_core,
    from_far,
    from_mid,
    from_end,
    from_middle,
    total,
    snap,
    outbox,
    vec_now,
    vec_in,
    holds,
    keeps,
    load_sem,
    w_sem,
    core_send,
    core_recv,
    far_send,
    far_recv,
    mid_send,
    mid_recv,
    z_send,
    z_recv,
    vec_send,
    vec_recv,
    out_send,
    out_recv,
):
    step = pl.program_id(0)
    inner = jnp.maximum(step - 4, 0)
    quad, block, pair = inner // 4, lax.rem(inner, 4) // 2, lax.rem(inner, 2)
    me = lax.axis_index("dp")
    z, y, x, core = place(me)
    in_plane = lax.rem(me, PLANE)
    sibling = me + 1 - 2 * core
    x_peer = me + 2 - 4 * x
    y_peer = me + 4 - 8 * y
    z_targets = along_z(z, in_plane)
    is_end = (z == 0) | (z == 3)
    is_middle = (z == 1) | (z == 2)

    def tiles_of(batch):
        if batch < 4:
            return w_part, 4 + 2 * batch, 2, slice(None)
        return part, 0, 4, pl.ds(256 * (batch - 4), 256)

    def halves(batch, turned):
        ref, first, count, cols = tiles_of(batch)
        return ref, pl.ds(first + turned * count // 2, count // 2), cols

    def core_copy(batch):
        ref, first, count, cols = tiles_of(batch)
        tiles = pl.ds(first, count)
        return remote(
            ref.at[tiles, 1 - core, :, :, :, cols],
            from_core.at[tiles, :, :, :, cols],
            core_send.at[batch],
            core_recv.at[batch],
            sibling,
        )

    def far_copies(batch):
        copies = []
        for turned in range(2):
            ref, tiles, cols = halves(batch, turned)
            src = ref.at[tiles, core, :, 1 - y, :, cols] if turned else ref.at[tiles, core, 1 - x, :, :, cols]
            copies.append(
                remote(
                    src,
                    from_far.at[tiles, :, :, cols],
                    far_send.at[batch, turned],
                    far_recv.at[batch, turned],
                    y_peer if turned else x_peer,
                )
            )
        return copies

    def mid_copies(batch):
        copies = []
        for turned in range(2):
            ref, tiles, cols = halves(batch, turned)
            src = ref.at[tiles, core, 1 - x, y, :, cols] if turned else ref.at[tiles, core, x, 1 - y, :, cols]
            copies.append(
                remote(
                    src,
                    from_mid.at[tiles, :, cols],
                    mid_send.at[batch, turned],
                    mid_recv.at[batch, turned],
                    x_peer if turned else y_peer,
                )
            )
        return copies

    def z_copy(batch, stage):
        ref, first, count, cols = tiles_of(batch)
        tiles = pl.ds(first, count)
        if stage == 2:
            src, dst = total.at[tiles, :, cols], total.at[tiles, :, cols]
        else:
            src = ref.at[tiles, core, x, y, :, cols]
            dst = (from_middle if stage else from_end).at[tiles, :, cols]
        return remote(src, dst, z_send.at[stage, batch], z_recv.at[stage, batch], z_targets[stage])

    def give_core(batch):
        core_copy(batch).start()

    def give_far(batch):
        core_copy(batch).wait_recv()
        ref, first, count, cols = tiles_of(batch)
        for tile in range(first, first + count):
            ref[tile, core, :, :, :, cols] = ref[tile, core, :, :, :, cols] + from_core[tile, :, :, :, cols]
        start(far_copies(batch))

    def give_mid(batch):
        arrive(far_copies(batch))
        for turned in range(2):
            ref, tiles, cols = halves(batch, turned)
            if turned:
                ref[tiles, core, :, y, :, cols] = ref[tiles, core, :, y, :, cols] + from_far[tiles, :, :, cols]
            else:
                ref[tiles, core, x, :, :, cols] = ref[tiles, core, x, :, :, cols] + from_far[tiles, :, :, cols]
        start(mid_copies(batch))

    def add_piece(batch, other):
        ref, first, count, cols = tiles_of(batch)
        tiles = pl.ds(first, count)
        return ref[tiles, core, x, y, :, cols] + other[tiles, :, cols]

    def give_end(batch):
        arrive(mid_copies(batch))
        ref, first, count, cols = tiles_of(batch)
        ref[pl.ds(first, count), core, x, y, :, cols] = add_piece(batch, from_mid)

        @pl.when(is_end)
        def _():
            z_copy(batch, 0).start()

    def give_middle(batch):
        @pl.when(is_middle)
        def _():
            z_copy(batch, 0).wait_recv()
            ref, first, count, cols = tiles_of(batch)
            ref[pl.ds(first, count), core, x, y, :, cols] = add_piece(batch, from_end)
            z_copy(batch, 1).start()

    def give_total(batch):
        @pl.when(is_middle)
        def _():
            z_copy(batch, 1).wait_recv()
            _, first, count, cols = tiles_of(batch)
            total[pl.ds(first, count), :, cols] = add_piece(batch, from_middle)
            z_copy(batch, 2).start()

    def take_total(batch):
        @pl.when(is_end)
        def _():
            z_copy(batch, 2).wait_recv()

    def deliver(third):
        cols = pl.ds(256 * third, 256)
        snap[...] = total[:, :, cols]

        def fill(at, carry):
            value = snap[holds[at]]
            outbox[third, at] = jnp.where(keeps[at] > 0, value, jnp.zeros_like(value))
            return carry

        lax.fori_loop(0, 2 * PLANE, fill, 0)

        def send(hop, carry):
            target = lax.rem(in_plane + hop, PLANE)
            remote(
                outbox.at[third, pl.ds(2 * target, 2)],
                slot_grad.at[:, core, x, y, :, cols],
                out_send.at[third],
                out_recv.at[third],
                z * PLANE + target,
            ).start()
            return carry

        lax.fori_loop(1, PLANE, send, 0)
        keep_copy(third).start()

    def keep_copy(third):
        return pltpu.make_async_copy(
            outbox.at[third, pl.ds(2 * in_plane, 2)],
            slot_grad.at[:, core, x, y, :, pl.ds(256 * third, 256)],
            load_sem.at[5 + third],
        )

    def vec_copies(stage):
        if stage < 3:
            hops = [(stage, (sibling, x_peer, y_peer)[stage])]
        else:
            hops = [
                (2 + hop, lax.rem(z + hop, 4) * PLANE + in_plane) for hop in range(1, 4)
            ]
        return [
            remote(vec_now.at[stage], vec_in.at[at], vec_send.at[at], vec_recv.at[at], device)
            for at, device in hops
        ]

    def vec_next(stage):
        arrive(vec_copies(stage))
        vec_now[stage + 1] = vec_now[stage] + vec_in[stage]
        start(vec_copies(stage + 1))

    def input_store():
        return pltpu.make_async_copy(acc, input_hbm, load_sem.at[4])

    def load(at):
        src, dst = (
            (hidden_hbm, hidden_then_x),
            (down_hbm, down_then_branch),
            (second_hbm, acc),
            (hat_hbm, hat_ref),
            None,
            None,
            None,
            None,
            (x_turned_hbm, hidden_then_x),
            (ctx_turned_hbm, active_then_ctx),
            None,
            None,
            (ctx_hbm, ctx_ref),
        )[at]
        return pltpu.make_async_copy(src, dst, load_sem.at[at])

    def tile_load(tile, side):
        src, dst = ((slope_hbm, slope_then_query), (active_hbm, active_then_ctx))[side]
        return pltpu.make_async_copy(src.at[tile], dst, load_sem.at[10 + side])

    def w_load(at):
        return pltpu.make_async_copy(w_hbm.at[at], w_part.at[at], w_sem.at[at])

    def weight(at, cols=slice(None)):
        value = w_part[at, :, :, :, :, cols]
        return value.reshape(8 * PIECE, value.shape[-1])

    def input_rows(half):
        rows = slice(ROWS * half, ROWS * half + ROWS)
        more = acc[rows, :]
        for at, buf in enumerate((slope_then_query, up_then_key, value_buf)):
            more = more + dot_back(buf[rows, :], weight(at))
        acc[rows, :] = more
        if half == 1:
            input_store().start()

    actions = {
        "core": give_core,
        "far": give_far,
        "mid": give_mid,
        "end": give_end,
        "middle": give_middle,
        "total": give_total,
        "take": take_total,
        "deliver": deliver,
        "sum": vec_next,
        "input": input_rows,
    }

    @pl.when(step == 0)
    def _():
        start([load(1), tile_load(0, 0), w_load(5), w_load(4)])
        for at in range(2 * PLANE):
            tile_here, kept = jnp.int32(0), jnp.int32(0)
            for tile in range(TILES):
                place_of = SLOTS * owners[tile] + slot_number(owners, tile)
                match = place_of == z * 2 * PLANE + at
                tile_here = tile_here + jnp.where(match, POSITIONS.index(tile), 0)
                kept = kept + jnp.where(match, 1, 0)
            holds[at] = tile_here
            keeps[at] = kept
        vec_now[0] = late_ref[...]
        greet(z, in_plane)

    def serve(points):
        for at in points:
            if BACK_PLAN[at]:

                @pl.when(step == (at // 2 if at < 8 else at - 4))
                def _():
                    for name, number in BACK_PLAN[at]:
                        actions[name](number)

    serve(range(0, 8, 2))

    @pl.when(step < 4)
    def _():
        tile_load(step, 0).wait()
        w_load(5 + 2 * step).wait()

        @pl.when(step == 0)
        def _():
            load(1).wait()
            start([load(2), tile_load(0, 1), load(0)])

        @pl.when(step < 3)
        def _():
            start([w_load(7 + 2 * step), w_load(6 + 2 * step)])

        @pl.when(step == 1)
        def _():
            load(3).start()

        @pl.when(step == 2)
        def _():
            w_load(3).start()

        @pl.when(step == 3)
        def _():
            start([load(12), w_load(0), w_load(1), w_load(2)])

        for half in range(2):
            rows = slice(ROWS * half, ROWS * half + ROWS)
            back = dot_back(down_then_branch[rows, :], weight(5 + 2 * step))
            up_low = (back * slope_then_query[rows, :].astype(jnp.float32)).astype(jnp.bfloat16)
            up_then_key[rows, :] = up_low
            vec_now[0, pl.ds(3 + step, 1), :] += columns_total(up_low.astype(jnp.float32))

        @pl.when(step < 3)
        def _():
            tile_load(step + 1, 0).start()

        w_load(4 + 2 * step).wait()

        @pl.when(step == 0)
        def _():
            load(2).wait()
            load(0).wait()

        for half in range(2):
            rows = slice(ROWS * half, ROWS * half + ROWS)
            acc[rows, :] = acc[rows, :] + dot_back(up_then_key[rows, :], weight(4 + 2 * step))

    serve(range(1, 8, 2))

    @pl.when(step < 4)
    def _():
        tile_load(step, 1).wait()
        by_down = dot(active_then_ctx[...], down_then_branch[...]).astype(jnp.bfloat16)
        w_part[5 + 2 * step] = by_down.reshape(2, 2, 2, PIECE, 8 * PIECE)

        @pl.when(step < 3)
        def _():
            tile_load(step + 1, 1).start()

        by_up = dot(hidden_then_x[...], up_then_key[...]).astype(jnp.bfloat16)
        w_part[4 + 2 * step] = by_up.reshape(2, 2, 2, PIECE, 8 * PIECE)

    @pl.when(step == 3)
    def _():
        start([load(8), load(9)])
        load(3).wait()
        w_load(3).wait()
        for half in range(2):
            rows = slice(ROWS * half, ROWS * half + ROWS)
            grad_hidden, hat = acc[rows, :], hat_ref[rows, :].astype(jnp.float32)
            vec_now[0, 10:11, :] += columns_total(grad_hidden * hat)
            vec_now[0, 8:9, :] += columns_total(grad_hidden)
            first = normalize_back(grad_hidden * gain_ref[0:1, :], hat, inverse_ref[rows, :])
            acc[rows, :] = first
            branch_low = first.astype(jnp.bfloat16)
            down_then_branch[rows, :] = branch_low
            vec_now[0, 2:3, :] += columns_total(branch_low.astype(jnp.float32))
            grad_ctx_ref[rows, :] = dot_back(branch_low, weight(3)).astype(jnp.bfloat16)

    serve(range(8, 20))

    here = pl.ds(pl.multiple_of(block * ROWS, ROWS), ROWS)
    quad_cols = pl.ds(pl.multiple_of(quad * 256, 256), 256)

    @pl.when(step == 4)
    def _():
        load(12).wait()
        for at in range(3):
            w_load(at).wait()

    pair_cols = pl.ds(pl.multiple_of(quad * 256 + pair * 128, 128), 128)
    grad_bufs = (slope_then_query, up_then_key, value_buf)

    @pl.when(step >= 4)
    def _():
        grads = attend_back_pair(
            grad_ctx_ref[here, pair_cols],
            ctx_ref[here, pair_cols],
            p_ref.at[0],
            q_ref[...],
            k_ref[...],
            v_ref[...],
        )
        for buf, grad in zip(grad_bufs, grads):
            buf[here, pair_cols] = grad
        vec_now[0, 0:1, pair_cols] += columns_total(grads[0].astype(jnp.float32))
        vec_now[0, 1:2, pair_cols] += columns_total(grads[2].astype(jnp.float32))

    @pl.when(step == 7)
    def _():
        load(8).wait()
        load(9).wait()

    @pl.when((step >= 4) & (block == 1) & (pair == 1))
    def _():
        for tile in range(4):
            if tile < 3:
                value = dot(hidden_then_x[...], grad_bufs[tile][:, quad_cols])
            else:
                value = dot(active_then_ctx[...], down_then_branch[:, quad_cols])
            value = value.astype(jnp.bfloat16).reshape(2, 2, 2, PIECE, 256)
            part[tile, :, :, :, :, quad_cols] = value


    @pl.when(step == 15)
    def _():
        start(vec_copies(0))
        for name, number in BACK_PLAN[-1]:
            actions[name](number)
        arrive(vec_copies(3))
        summed = jnp.zeros(vec_out.shape, jnp.float32)
        for origin in range(4):
            hop = lax.rem(z - origin + 4, 4)
            summed = summed + jnp.where(hop == 0, vec_now[3], vec_in[2 + jnp.maximum(hop, 1)])
        vec_out[...] = summed
        for batch in range(7):
            for copy in [core_copy(batch)] + far_copies(batch) + mid_copies(batch):
                copy.wait_send()

            @pl.when(is_end)
            def _():
                z_copy(batch, 0).wait_send()

            @pl.when(is_middle)
            def _():
                z_copy(batch, 1).wait_send()
                z_copy(batch, 2).wait_send()

        for stage in range(4):
            for copy in vec_copies(stage):
                copy.wait_send()
        input_store().wait()
        for third in range(3):
            keep_copy(third).wait()
            most = outbox.at[third, pl.ds(0, 2 * PLANE - 2)]
            pltpu.make_async_copy(most, most, out_recv.at[third]).wait()
            pltpu.make_async_copy(most, most, out_send.at[third]).wait()


def backward_and_reduced(
    owners,
    probs,
    query,
    keyed,
    valued,
    inverse,
    gain,
    late_sums,
    context,
    x_turned,
    ctx_turned,
    hidden,
    active,
    slope,
    grad_down,
    grad_second,
    hat,
    weights,
):
    tokens, width = grad_down.shape
    low, high = jnp.bfloat16, jnp.float32
    shaped = jax.ShapeDtypeStruct
    smem = pl.BlockSpec(memory_space=pltpu.SMEM)
    any_space = pl.BlockSpec(memory_space=pl.ANY)
    dma = pltpu.SemaphoreType.DMA
    once = pl.Buffered(1)

    def at(step):
        inner = jnp.maximum(step - 4, 0)
        return lax.rem(inner, 4) // 2, inner // 4 * 2 + lax.rem(inner, 2)

    pair = pl.BlockSpec((ROWS, 128), at)
    sums = pl.BlockSpec((16, width), lambda i: (0, 0))
    cut = (2, 2, 2, PIECE, width)
    input_grad, slot_grads, vector_sums = pl.pallas_call(
        backward_and_reduce,
        grid=(16,),
        out_shape=(
            shaped((tokens, width), high),
            shaped((SLOTS,) + cut, low),
            shaped((16, width), high),
        ),
        in_specs=[smem, pl.BlockSpec((1, 2, ROWS, ROWS), lambda i: (*at(i), 0, 0))]
        + [pair] * 3
        + [
            pl.BlockSpec((tokens, 1), lambda i: (0, 0), pipeline_mode=once),
            pl.BlockSpec(gain.shape, lambda i: (0, 0)),
            sums,
        ]
        + [any_space] * 10,
        out_specs=(any_space, any_space, sums),
        scratch_shapes=[
            pltpu.VMEM((TILES,) + cut, low),
            pltpu.VMEM((tokens, width), high),
            pltpu.VMEM((width, tokens), low),
            pltpu.VMEM((width, tokens), low),
            pltpu.VMEM((tokens, width), low),
            pltpu.VMEM((tokens, width), low),
            pltpu.VMEM((tokens, width), low),
            pltpu.VMEM((tokens, width), low),
            pltpu.VMEM((tokens, width), low),
            pltpu.VMEM((tokens, width), low),
            pltpu.VMEM((tokens, width), low),
            pltpu.VMEM((4,) + cut, low),
            pltpu.VMEM((TILES,) + cut[1:], low),
            pltpu.VMEM((TILES,) + cut[2:], low),
            pltpu.VMEM((TILES,) + cut[3:], low),
            pltpu.VMEM((TILES,) + cut[3:], low),
            pltpu.VMEM((TILES,) + cut[3:], low),
            pltpu.VMEM((TILES,) + cut[3:], low),
            pltpu.VMEM((TILES, PIECE, 256), low),
            pltpu.VMEM((3, 2 * PLANE, PIECE, 256), low),
            pltpu.VMEM((4, 16, width), high),
            pltpu.VMEM((6, 16, width), high),
            pltpu.SMEM((2 * PLANE,), jnp.int32),
            pltpu.SMEM((2 * PLANE,), jnp.int32),
            dma((13,)),
            dma((TILES,)),
            dma((7,)),
            dma((7,)),
            dma((7, 2)),
            dma((7, 2)),
            dma((7, 2)),
            dma((7, 2)),
            dma((3, 7)),
            dma((3, 7)),
            dma((6,)),
            dma((6,)),
            dma((3,)),
            dma((3,)),
        ],
        compiler_params=pltpu.CompilerParams(
            collective_id=1, has_side_effects=True, vmem_limit_bytes=63 * 2**20
        ),
        name="backward_and_reduce",
    )(
        owners,
        probs,
        query,
        keyed,
        valued,
        inverse,
        gain,
        late_sums,
        context,
        x_turned,
        ctx_turned,
        hidden,
        active,
        slope,
        grad_down,
        grad_second,
        hat,
        weights,
    )
    return input_grad, slot_grads.reshape(SLOTS, width, width), vector_sums


def collected_tiles(tile_low, owners, slots):
    mine = owners == lax.axis_index("dp")
    local = jnp.where(mine[:, None, None], tile_low[slots], jnp.zeros((), tile_low.dtype))
    return lax.psum(local, "dp")


def summed_over_slice(parts, vector_terms, owners, slots):
    myself = lax.axis_index("dp")

    def add(held, items):
        part, owner, slot = items
        total = lax.psum(part.astype(jnp.float32), "dp")
        here = (owner == myself) & (slot == jnp.arange(SLOTS, dtype=jnp.int32))
        return held + jnp.where(here[:, None, None], total[None], 0.0), None

    empty = jnp.zeros((SLOTS,) + parts.shape[1:], jnp.float32)
    return lax.scan(add, empty, (parts, owners, slots))[0], lax.psum(vector_terms, "dp")


def body(
    inputs,
    cotangent,
    counts,
    lengths,
    owners,
    tile_master,
    tile_first,
    tile_second,
    tile_ema,
    bias_vals,
    gain_vals,
    vector_first,
    vector_second,
    vector_ema,
):
    tokens = inputs.shape[0]
    small = lax.axis_size("dp") == GROUP
    gain_scale = float(tokens * lax.axis_size("dp")) ** (-0.5)
    if small:
        (
            query,
            keyed,
            valued,
            probs,
            context,
            x_turned,
            ctx_turned,
            hidden,
            active,
            slope,
            grad_down,
            mixed,
            grad_second,
            hat,
            weights,
            inverse,
            late_sums,
        ) = gathered_and_forwarded(
            counts,
            lengths,
            owners,
            bias_vals,
            gain_vals,
            inputs,
            cotangent,
            tile_master,
        )
        input_grad, slot_grads, full_sums = backward_and_reduced(
            owners,
            probs,
            query,
            keyed,
            valued,
            inverse,
            gain_vals,
            late_sums,
            context,
            x_turned,
            ctx_turned,
            hidden,
            active,
            slope,
            grad_down,
            grad_second,
            hat,
            weights,
        )
    else:
        slots = tile_slots(owners)
        vectors = jnp.concatenate([bias_vals, gain_vals], 0)
        weights = collected_tiles(tile_master[0].astype(jnp.bfloat16), owners, slots)
        query, keyed, valued, probs, context, hat, inverse = attended(
            counts, lengths, inputs, weights, vectors
        )
        mixed, grad_first, grad_branch, grad_context, up_grads, down_grads, late_sums = fed_forward_both(
            counts, lengths, hat, inverse, cotangent, weights, vectors
        )
        input_grad, early_grads, early_sums = attended_back(
            probs, query, keyed, valued, inputs, context, grad_context, grad_branch, grad_first, weights
        )
        parts = jnp.concatenate([early_grads, up_grads, down_grads], 0)
        slot_grads, full_sums = summed_over_slice(parts, late_sums + early_sums, owners, slots)
    return updated(
        gain_scale,
        slot_grads,
        tile_master,
        tile_first,
        tile_second,
        tile_ema,
        full_sums,
        bias_vals,
        gain_vals,
        vector_first,
        vector_second,
        vector_ema,
        mixed,
        input_grad,
    )


def solution(mesh):
    placed = (
        P("dp", None),
        P("dp", None),
        P("dp", None),
        P("dp", None),
        P(),
        P("dp", None, None, None),
        P("dp", None, None, None),
        P("dp", None, None, None),
        P("dp", None, None, None),
        P(),
        P(),
        P(),
        P(),
        P(),
    )
    return jax.shard_map(
        body,
        mesh=mesh,
        in_specs=placed,
        out_specs=(
            P("dp", None),
            P("dp", None),
            P("dp", None, None, None),
            P("dp", None, None, None),
            P("dp", None, None, None),
            P("dp", None, None, None),
            P("dp", None, None, None),
            P(),
            P(),
            P(),
            P(),
        ),
        check_vma=False,
    )
```

```python
import functools

import jax
import jax.numpy as jnp
from jax import lax
from jax.experimental import pallas as pl
from jax.experimental.pallas import tpu as pltpu
from jax.sharding import PartitionSpec as P

HEADS = 12
BUCKET = 128
SLOTS = 2
TILES = 12
VROWS = 12
STEP = 5

norm_epsilon = 1e-12
tile_rate = 0.03
vector_rate = 0.2
first_decay = 0.5
second_decay = 0.5
adam_epsilon = 1e-08
weight_decay = 0.01
average_rate = 0.9


def tile_slots(owners):
    order = jnp.arange(owners.shape[0], dtype=jnp.int32)
    same = owners[:, None] == owners[None, :]
    earlier = order[None, :] < order[:, None]
    return jnp.sum((same & earlier).astype(jnp.int32), 1)


def adam_update(param, grad, first, second, rate):
    first_new = first_decay * first + (1.0 - first_decay) * grad
    second_new = second_decay * second + (1.0 - second_decay) * grad * grad
    first_hat = first_new / (1.0 - first_decay**STEP)
    second_hat = second_new / (1.0 - second_decay**STEP)
    param_new = param - rate * (
        first_hat / (jnp.sqrt(second_hat) + adam_epsilon) + weight_decay * param
    )
    return (param_new, first_new, second_new)


ROWS = 4 * BUCKET
TAIL_RATE = 0.28
TAIL_SERIES = (
    0.11615256574707405,
    0.06981038475559553,
    0.2631359597579608,
    -0.22983675561378278,
    0.38546775012288165,
    -0.10472989053809521,
)
INV_SQRT_TAU = 0.3989422804014327
ALLOWED = 3.0e38
BARRED = -1000000000.0


def dot(left, right):
    return jnp.dot(left, right, preferred_element_type=jnp.float32)


def dot_back(left, right):
    return lax.dot_general(
        left, right, (((1,), (1,)), ((), ())), preferred_element_type=jnp.float32
    )


def outer(left, right):
    return lax.dot_general(
        left, right, (((0,), (0,)), ((), ())), preferred_element_type=jnp.float32
    )


def passage_facts(counts, lengths, position):
    places = lengths.shape[1]
    big_end = counts[0, 0]
    mid_end = big_end + counts[0, 1]
    all_end = mid_end + counts[0, 2]
    start = jnp.int32(0)
    member = jnp.zeros(position.shape, jnp.int32)
    usable = jnp.zeros(position.shape, jnp.int32)
    for number in range(places):
        size = jnp.where(
            number < big_end,
            4 * BUCKET,
            jnp.where(number < mid_end, 2 * BUCKET, jnp.where(number < all_end, BUCKET, 0)),
        )
        inside = (position >= start) & (position < start + size)
        live = inside & (position < start + lengths[0, number])
        member = jnp.where(inside, number + 1, member)
        usable = jnp.where(live, 1, usable)
        start = start + size
    passage = jnp.where(member > 0, member - 1, places + position // BUCKET)
    return usable, passage


def normalize(values):
    center = jnp.mean(values, -1, keepdims=True)
    centered = values - center
    spread = jnp.mean(centered * centered, -1, keepdims=True)
    inverse = lax.rsqrt(spread + norm_epsilon)
    return centered * inverse, inverse


def normalize_back(grad, hat, inverse):
    center = jnp.mean(grad, -1, keepdims=True)
    along = jnp.mean(grad * hat, -1, keepdims=True)
    return inverse * (grad - center - hat * along)


def columns_total(values):
    return jnp.sum(values, 0, keepdims=True)


def attention_caps(counts, lengths, block):
    at_row = lax.broadcasted_iota(jnp.int32, (ROWS, 1), 0) + block * ROWS
    at_column = lax.broadcasted_iota(jnp.int32, (1, ROWS), 1) + block * ROWS
    _, passage_row = passage_facts(counts, lengths, at_row)
    usable_column, passage_column = passage_facts(counts, lengths, at_column)
    allowed = (passage_row == passage_column) & ((usable_column == 1) | (at_row == at_column))
    return jnp.where(allowed, ALLOWED, BARRED)


def attend_quad(quad, weight, x_ref, vec_ref, cap_ref, q_ref, k_ref, v_ref, p_ref, ctx_ref):
    cols = pl.ds(pl.multiple_of(quad * 256, 256), 256)
    x = x_ref[...]
    query = (dot(x, weight(0, cols)) + vec_ref[0:1, cols]).astype(jnp.bfloat16)
    query = query * jnp.bfloat16(0.125)
    keyed = dot(x, weight(1, cols)).astype(jnp.bfloat16)
    valued = (dot(x, weight(2, cols)) + vec_ref[1:2, cols]).astype(jnp.bfloat16)
    q_ref[...] = query
    k_ref[...] = keyed
    v_ref[...] = valued
    low_half = lax.broadcasted_iota(jnp.int32, (1, 128), 1) < 64
    for pair in range(2):
        part = slice(128 * pair, 128 * pair + 128)
        contexts = []
        for head in range(2):
            here = low_half if head == 0 else ~low_half
            mine = jnp.where(here, query[:, part], jnp.zeros_like(query[:, part]))
            scores = jnp.minimum(dot_back(mine, keyed[:, part]), cap_ref[...])
            exponent = jnp.exp(scores - jnp.max(scores, -1, keepdims=True))
            inverse = 1.0 / jnp.sum(exponent, -1, keepdims=True)
            probability = (exponent * inverse).astype(jnp.bfloat16)
            p_ref[0, 2 * pair + head] = probability
            contexts.append(dot(probability, valued[:, part]))
        both = jnp.where(low_half, contexts[0], contexts[1]).astype(jnp.bfloat16)
        ctx_ref[:, pl.ds(pl.multiple_of(quad * 256 + 128 * pair, 128), 128)] = both


def close_block(w_out, x_ref, vec_ref, ctx_ref, hat_ref, inverse_ref):
    branch = dot(ctx_ref[...], w_out) + vec_ref[2:3, :]
    hat_ref[...], inverse_ref[...] = normalize(x_ref[...].astype(jnp.float32) + branch)


def attend_back_pair(pull, level_from, p_ref, query, keyed, valued):
    low_half = lax.broadcasted_iota(jnp.int32, (1, 128), 1) < 64
    along = pull.astype(jnp.float32) * level_from.astype(jnp.float32)
    by_query, by_key, by_value = [], [], []
    for head in range(2):
        mask = low_half if head == 0 else ~low_half
        mine = jnp.where(mask, pull, jnp.zeros_like(pull))
        level = jnp.sum(jnp.where(mask, along, 0.0), -1, keepdims=True)
        probability = p_ref[head]
        grad_prob = dot_back(mine, valued)
        grad_scores = (probability.astype(jnp.float32) * (grad_prob - level)).astype(jnp.bfloat16)
        by_query.append(dot(grad_scores, keyed))
        by_key.append(outer(grad_scores, query))
        by_value.append(outer(probability, pull))
    grad_query = jnp.where(low_half, by_query[0], by_query[1]) * 0.125
    grad_key = jnp.where(low_half, by_key[0], by_key[1])
    grad_value = jnp.where(low_half, by_value[0], by_value[1])
    return [value.astype(jnp.bfloat16) for value in (grad_query, grad_key, grad_value)]


def gelu_parts(up):
    near = 1.0 / (1.0 + TAIL_RATE * jnp.abs(up))
    decay = jnp.exp(up * up * -0.5)
    series = jnp.full_like(near, TAIL_SERIES[-1])
    for term in TAIL_SERIES[-2::-1]:
        series = series * near + term
    tail = series * near * decay
    share = jnp.where(up < 0.0, tail, 1.0 - tail)
    slope = share + up * (decay * INV_SQRT_TAU)
    return (up * share).astype(jnp.bfloat16), slope


def attend_forward(
    counts,
    lengths,
    x_ref,
    w_hbm,
    vec_ref,
    q_ref,
    k_ref,
    v_ref,
    p_ref,
    ctx_ref,
    hat_ref,
    inverse_ref,
    w_buf,
    cap_ref,
    w_sem,
):
    block, quad = pl.program_id(0), pl.program_id(1)
    loads = [pltpu.make_async_copy(w_hbm.at[at], w_buf.at[at], w_sem.at[at]) for at in range(4)]

    @pl.when((block == 0) & (quad == 0))
    def _():
        for load in loads:
            load.start()
        for load in loads:
            load.wait()

    @pl.when(quad == 0)
    def _():
        cap_ref[...] = attention_caps(counts, lengths, block)

    def weight(at, cols):
        return w_buf[at, :, cols]

    attend_quad(quad, weight, x_ref, vec_ref, cap_ref, q_ref, k_ref, v_ref, p_ref, ctx_ref)

    @pl.when(quad == 2)
    def _():
        close_block(w_buf[3], x_ref, vec_ref, ctx_ref, hat_ref, inverse_ref)


def attended(counts, lengths, x, weights, vectors):
    tokens, width = x.shape
    blocks = tokens // ROWS
    low = jnp.bfloat16
    smem = pl.BlockSpec(memory_space=pltpu.SMEM)
    quad = pl.BlockSpec((ROWS, 256), lambda b, h: (b, h))
    rows = pl.BlockSpec((ROWS, width), lambda b, h: (b, 0))
    shaped = jax.ShapeDtypeStruct
    return pl.pallas_call(
        attend_forward,
        grid=(blocks, 3),
        out_shape=(
            shaped((tokens, width), low),
            shaped((tokens, width), low),
            shaped((tokens, width), low),
            shaped((blocks, HEADS, ROWS, ROWS), low),
            shaped((tokens, width), low),
            shaped((tokens, width), jnp.float32),
            shaped((tokens, 1), jnp.float32),
        ),
        in_specs=[
            smem,
            smem,
            rows,
            pl.BlockSpec(memory_space=pl.ANY),
            pl.BlockSpec((VROWS, width), lambda b, h: (0, 0)),
        ],
        out_specs=(
            quad,
            quad,
            quad,
            pl.BlockSpec((1, 4, ROWS, ROWS), lambda b, h: (b, h, 0, 0)),
            rows,
            rows,
            pl.BlockSpec((ROWS, 1), lambda b, h: (b, 0)),
        ),
        scratch_shapes=[
            pltpu.VMEM((4, width, width), low),
            pltpu.VMEM((ROWS, ROWS), jnp.float32),
            pltpu.SemaphoreType.DMA((4,)),
        ],
        compiler_params=pltpu.CompilerParams(vmem_limit_bytes=56 * 2**20),
        name="attend_forward",
    )(counts, lengths, x, weights, vectors)


def feed_forward_both(
    counts,
    lengths,
    hat_ref,
    inverse_ref,
    cot_ref,
    w_hbm,
    vec_ref,
    mixed_ref,
    first_ref,
    branch_ref,
    context_ref,
    up_grad_ref,
    down_grad_ref,
    sum_ref,
    w_buf,
    active_ref,
    up_ref,
    hidden_ref,
    down_ref,
    slope_ref,
    w_sem,
):
    step = pl.program_id(0)
    blocks = pl.num_programs(0) - 4
    loads = [
        pltpu.make_async_copy(w_hbm.at[3 + at], w_buf.at[at], w_sem.at[at]) for at in range(9)
    ]

    @pl.when(step == 0)
    def _():
        for load in loads[1:] + loads[:1]:
            load.start()
        sum_ref[...] = jnp.zeros_like(sum_ref)
        for load in loads[1:] + loads[:1]:
            load.wait()

    @pl.when(step < blocks)
    def _():
        here = pl.ds(pl.multiple_of(step * ROWS, ROWS), ROWS)
        at_row = lax.broadcasted_iota(jnp.int32, (ROWS, 1), 0) + step * ROWS
        live = passage_facts(counts, lengths, at_row)[0].astype(jnp.float32)
        hat = hat_ref[...]
        hidden = hat * vec_ref[10:11, :] + vec_ref[8:9, :]
        hidden_low = hidden.astype(jnp.bfloat16)
        hidden_ref[here, :] = hidden_low
        total = hidden + vec_ref[7:8, :]
        for tile in range(4):
            up = dot(hidden_low, w_buf[1 + tile]) + vec_ref[3 + tile : 4 + tile, :]
            active, slope = gelu_parts(up)
            slope_ref[tile] = slope.astype(jnp.bfloat16)
            active_ref[tile, here, :] = active
            total = total + dot(active, w_buf[5 + tile])
        hat_two, inverse_two = normalize(total)
        mixed_ref[...] = ((hat_two * vec_ref[11:12, :] + vec_ref[9:10, :]) * live).astype(jnp.bfloat16)
        grad_out = cot_ref[...].astype(jnp.float32) * live
        sum_ref[11:12, :] += columns_total(grad_out * hat_two)
        sum_ref[9:10, :] += columns_total(grad_out)
        second = normalize_back(grad_out * vec_ref[11:12, :], hat_two, inverse_two)
        down_low = second.astype(jnp.bfloat16)
        down_ref[here, :] = down_low
        sum_ref[7:8, :] += columns_total(down_low.astype(jnp.float32))
        grad_hidden = second
        for tile in range(4):
            pulled = dot_back(down_low, w_buf[5 + tile])
            up_low = (pulled * slope_ref[tile].astype(jnp.float32)).astype(jnp.bfloat16)
            up_ref[tile, here, :] = up_low
            sum_ref[3 + tile : 4 + tile, :] += columns_total(up_low.astype(jnp.float32))
            grad_hidden = grad_hidden + dot_back(up_low, w_buf[1 + tile])
        sum_ref[10:11, :] += columns_total(grad_hidden * hat)
        sum_ref[8:9, :] += columns_total(grad_hidden)
        grad_first = normalize_back(grad_hidden * vec_ref[10:11, :], hat, inverse_ref[...])
        first_ref[...] = grad_first
        branch_low = grad_first.astype(jnp.bfloat16)
        branch_ref[...] = branch_low
        sum_ref[2:3, :] += columns_total(branch_low.astype(jnp.float32))
        context_ref[...] = dot_back(branch_low, w_buf[0]).astype(jnp.bfloat16)

    @pl.when(step >= blocks)
    def _():
        tile = step - blocks
        up_grad_ref[0] = outer(hidden_ref[...], up_ref[tile]).astype(jnp.bfloat16)
        down_grad_ref[0] = outer(active_ref[tile], down_ref[...]).astype(jnp.bfloat16)


def fed_forward_both(counts, lengths, hat, inverse, cotangent, weights, vectors):
    tokens, width = hat.shape
    blocks = tokens // ROWS
    low = jnp.bfloat16
    smem = pl.BlockSpec(memory_space=pltpu.SMEM)
    shaped = jax.ShapeDtypeStruct

    def block_of(step):
        return jnp.minimum(step, blocks - 1)

    def tile_of(step):
        return jnp.maximum(step - blocks, 0)

    rows = pl.BlockSpec((ROWS, width), lambda i: (block_of(i), 0))
    tile = pl.BlockSpec((1, width, width), lambda i: (tile_of(i), 0, 0))
    return pl.pallas_call(
        feed_forward_both,
        grid=(blocks + 4,),
        out_shape=(
            shaped((tokens, width), low),
            shaped((tokens, width), jnp.float32),
            shaped((tokens, width), low),
            shaped((tokens, width), low),
            shaped((4, width, width), low),
            shaped((4, width, width), low),
            shaped((16, width), jnp.float32),
        ),
        in_specs=[
            smem,
            smem,
            rows,
            pl.BlockSpec((ROWS, 1), lambda i: (block_of(i), 0)),
            rows,
            pl.BlockSpec(memory_space=pl.ANY),
            pl.BlockSpec((VROWS, width), lambda i: (0, 0)),
        ],
        out_specs=(
            rows,
            rows,
            rows,
            rows,
            tile,
            tile,
            pl.BlockSpec((16, width), lambda i: (0, 0)),
        ),
        scratch_shapes=[
            pltpu.VMEM((9, width, width), low),
            pltpu.VMEM((4, tokens, width), low),
            pltpu.VMEM((4, tokens, width), low),
            pltpu.VMEM((tokens, width), low),
            pltpu.VMEM((tokens, width), low),
            pltpu.VMEM((4, ROWS, width), low),
            pltpu.SemaphoreType.DMA((9,)),
        ],
        compiler_params=pltpu.CompilerParams(vmem_limit_bytes=60 * 2**20),
        name="feed_forward_both",
    )(counts, lengths, hat, inverse, cotangent, weights, vectors)


def attend_backward(
    p_ref,
    q_ref,
    k_ref,
    v_ref,
    x_ref,
    ctx_ref,
    grad_ctx_ref,
    branch_ref,
    first_ref,
    w_ref,
    input_ref,
    grad_ref,
    sum_ref,
    pulled,
):
    step = pl.program_id(0)
    quad, block = step // 2, lax.rem(step, 2)
    here = pl.ds(pl.multiple_of(block * ROWS, ROWS), ROWS)
    cols = pl.ds(pl.multiple_of(quad * 256, 256), 256)

    @pl.when(step == 0)
    def _():
        sum_ref[...] = jnp.zeros_like(sum_ref)
        input_ref[...] = first_ref[...]

    for pair in range(2):
        half = slice(128 * pair, 128 * pair + 128)
        at = pl.ds(pl.multiple_of(quad * 256 + 128 * pair, 128), 128)
        heads = p_ref.at[0, pl.ds(2 * pair, 2)]
        grads = attend_back_pair(
            grad_ctx_ref[here, at], ctx_ref[here, at], heads, q_ref[:, half], k_ref[:, half], v_ref[:, half]
        )
        for number, grad in enumerate(grads):
            pulled[number, here, half] = grad
        sum_ref[0:1, at] += columns_total(grads[0].astype(jnp.float32))
        sum_ref[1:2, at] += columns_total(grads[2].astype(jnp.float32))

    more = input_ref[here, :]
    for at in range(3):
        more = more + dot_back(pulled[at, here, :], w_ref[at, :, cols])
    input_ref[here, :] = more

    @pl.when(block == 1)
    def _():
        for tile in range(3):
            grad_ref[tile, :, cols] = outer(x_ref[...], pulled[tile]).astype(jnp.bfloat16)
        grad_ref[3, :, cols] = outer(ctx_ref[...], branch_ref[:, cols]).astype(jnp.bfloat16)


def attended_back(probs, query, keyed, valued, x, context, grad_context, grad_branch, grad_first, weights):
    tokens, width = x.shape
    low = jnp.bfloat16
    shaped = jax.ShapeDtypeStruct
    once = pl.Buffered(1)
    quad = pl.BlockSpec((ROWS, 256), lambda i: (lax.rem(i, 2), i // 2))
    whole = pl.BlockSpec((tokens, width), lambda i: (0, 0), pipeline_mode=once)
    return pl.pallas_call(
        attend_backward,
        grid=(6,),
        out_shape=(
            shaped((tokens, width), jnp.float32),
            shaped((4, width, width), low),
            shaped((16, width), jnp.float32),
        ),
        in_specs=[
            pl.BlockSpec((1, 4, ROWS, ROWS), lambda i: (lax.rem(i, 2), i // 2, 0, 0)),
            quad,
            quad,
            quad,
            whole,
            whole,
            whole,
            whole,
            whole,
            pl.BlockSpec((3, width, width), lambda i: (0, 0, 0), pipeline_mode=once),
        ],
        out_specs=(
            whole,
            pl.BlockSpec((4, width, width), lambda i: (0, 0, 0), pipeline_mode=once),
            pl.BlockSpec((16, width), lambda i: (0, 0)),
        ),
        scratch_shapes=[pltpu.VMEM((3, tokens, 256), low)],
        compiler_params=pltpu.CompilerParams(vmem_limit_bytes=56 * 2**20),
        name="attend_backward",
    )(probs, query, keyed, valued, x, context, grad_context, grad_branch, grad_first, weights)


def moved(param, grad, first, second, average, rate):
    param_new, first_new, second_new = adam_update(param, grad, first, second, rate)
    return param_new, first_new, second_new, average_rate * average + (1.0 - average_rate) * param_new


def update_kernel(
    gain_scale,
    grad_ref,
    master_ref,
    first_ref,
    second_ref,
    ema_ref,
    vec_grad_ref,
    bias_ref,
    gain_ref,
    vec_first_ref,
    vec_second_ref,
    vec_ema_ref,
    mixed_in,
    input_in,
    master_out,
    first_out,
    second_out,
    ema_out,
    copy_out,
    vec_out,
    vec_first_out,
    vec_second_out,
    vec_ema_out,
    mixed_out,
    input_out,
    vec_ref,
):
    mixed_out[...] = mixed_in[...]
    input_out[...] = input_in[...]

    @pl.when((pl.program_id(0) == 0) & (pl.program_id(1) == 0))
    def _():
        vec_ref[0:10, :] = bias_ref[...]
        vec_ref[10:12, :] = gain_ref[...]
        vec_grad = vec_grad_ref[0:VROWS, :] * gain_scale
        vec_out[...], vec_first_out[...], vec_second_out[...], vec_ema_out[...] = moved(
            vec_ref[...], vec_grad, vec_first_ref[...], vec_second_ref[...], vec_ema_ref[...], vector_rate
        )

    grad = grad_ref[...].astype(jnp.float32) * gain_scale
    result = moved(master_ref[0], grad, first_ref[0], second_ref[0], ema_ref[0], tile_rate)
    master_out[0], first_out[0], second_out[0], ema_out[0] = result
    copy_out[0] = result[0].astype(jnp.bfloat16)


def updated(
    gain_scale,
    slot_grads,
    master,
    first,
    second,
    ema,
    vec_grad,
    bias,
    gain,
    vec_first,
    vec_second,
    vec_ema,
    mixed,
    input_grad,
):
    width = master.shape[-1]
    chunk = 192
    tile = pl.BlockSpec((1, 1, chunk, width), lambda s, r: (0, s, r, 0))
    steps = width // chunk
    rows = pl.BlockSpec((mixed.shape[0] // (SLOTS * steps), width), lambda s, r: (s * steps + r, 0))

    def whole(value):
        return pl.BlockSpec(value.shape, lambda s, r: (0, 0))

    shaped = jax.ShapeDtypeStruct
    tile_shape = shaped(master.shape, jnp.float32)
    vec_shape = shaped((VROWS, width), jnp.float32)
    results = pl.pallas_call(
        functools.partial(update_kernel, gain_scale),
        grid=(SLOTS, steps),
        out_shape=(tile_shape,) * 4
        + (shaped(master.shape, jnp.bfloat16),)
        + (vec_shape,) * 4
        + (shaped(mixed.shape, mixed.dtype), shaped(input_grad.shape, input_grad.dtype)),
        in_specs=[pl.BlockSpec((1, chunk, width), lambda s, r: (s, r, 0))]
        + [tile] * 4
        + [whole(value) for value in (vec_grad, bias, gain, vec_first, vec_second, vec_ema)]
        + [rows] * 2,
        out_specs=(tile,) * 5 + (whole(vec_first),) * 4 + (rows,) * 2,
        scratch_shapes=[pltpu.VMEM((VROWS, width), jnp.float32)],
        compiler_params=pltpu.CompilerParams(vmem_limit_bytes=62 * 2**20),
        name="update",
    )(
        slot_grads,
        master,
        first,
        second,
        ema,
        vec_grad,
        bias,
        gain,
        vec_first,
        vec_second,
        vec_ema,
        mixed,
        input_grad,
    )
    return results[-2:] + results[:-2]


MESH = pl.DeviceIdType.MESH
GROUP = 32
PAIRS = TILES // 2
PLANE = 8
PIECE = 96
PAIR_TILES = ((0, 1), (2, 3), (4, 8), (5, 9), (6, 10), (7, 11))


def remote(src, dst, send, recv, device):
    return pltpu.make_async_remote_copy(
        src_ref=src, dst_ref=dst, send_sem=send, recv_sem=recv, device_id=(device,), device_id_type=MESH
    )


def place(device):
    core = lax.rem(device, 2)
    x = lax.rem(device // 2, 2)
    y = lax.rem(device // 4, 2)
    z = device // 8
    return z, y, x, core


def start(copies):
    for copy in copies:
        copy.start()


def arrive(copies):
    for copy in copies:
        copy.wait_recv()


def greet(z, in_plane):
    barrier = pltpu.get_barrier_semaphore()
    for hop in range(1, PLANE):
        other = z * PLANE + lax.rem(in_plane + hop, PLANE)
        pl.semaphore_signal(barrier, inc=1, device_id=(other,), device_id_type=MESH)
    for hop in range(1, 4):
        other = lax.rem(z + hop, 4) * PLANE + in_plane
        pl.semaphore_signal(barrier, inc=1, device_id=(other,), device_id_type=MESH)
    pl.semaphore_wait(barrier, PLANE + 2)


def along_z(z, in_plane):
    inner = (1 + z // 2) * PLANE + in_plane
    other_middle = (3 - z) * PLANE + in_plane
    outer_end = lax.rem(lax.rem(z + 3, 4) * 3, 4) * PLANE + in_plane
    return inner, other_middle, outer_end


def third(part):
    return pl.ds(256 * part, 256)


UNITS = [(0, 4, pl.ds(256 * part, 256)) for part in range(3)]
UNITS += [(2 * pair, 2, pl.ds(0, 768)) for pair in range(2, PAIRS)]
Z_PARTS = (pl.ds(0, 512), pl.ds(512, 256))


POSITIONS = [tile for pair in PAIR_TILES for tile in pair]


def slot_number(owners, tile):
    number = jnp.int32(0)
    for earlier in range(tile):
        number = number + jnp.where(owners[earlier] == owners[tile], 1, 0)
    return number

FRONT_PLAN = (
    (
        ("open",),
        ("swap", 0),
        ("sent", 0),
        ("swap", 1),
        ("choose", 0),
        ("end", 0),
        ("sent", 1),
        ("middle", 0),
        ("choose", 1),
        ("end", 1),
        ("swap", 2),
        ("total", 0),
        ("end", 3, 0),
        ("middle", 1),
        ("mid", 0),
        ("choose", 2),
        ("end", 2),
        ("end", 3, 1),
        ("far", 0),
        ("middle", 3, 0),
        ("total", 1),
        ("caps",),
        ("middle", 3, 1),
        ("end", 4, 0),
        ("mid", 1),
        ("near", 0),
        ("total", 3, 0),
        ("end", 5, 0),
        ("middle", 2),
        ("end", 4, 1),
        ("total", 3, 1),
        ("far", 1),
        ("finish", 0),
    ),
    (
        ("middle", 4, 0),
        ("total", 2),
        ("mid", 3),
        ("middle", 4, 1),
        ("end", 5, 1),
    ),
    (
        ("mid", 2),
        ("end", 6, 0),
        ("middle", 5, 0),
        ("near", 1),
        ("total", 4, 1),
        ("far", 3),
        ("finish", 1),
        ("far", 2),
        ("middle", 5, 1),
        ("end", 6, 1),
        ("total", 4, 0),
    ),
    (
        ("total", 5, 0),
        ("middle", 6, 0),
        ("mid", 4),
        ("total", 5, 1),
        ("middle", 6, 1),
    ),
    (
        ("total", 6, 1),
        ("mid", 5),
        ("near", 2),
        ("far", 4),
        ("total", 6, 0),
        ("finish", 2),
        ("keep", 0),
        ("keep", 1),
    ),
    (
        ("mid", 6),
        ("near", 3),
        ("near", 4),
        ("far", 5),
    ),
    (
        ("far", 6),
        ("finish", 4),
        ("keep", 3),
        ("finish", 3),
        ("keep", 2),
    ),
    (
        ("near", 5),
    ),
    (
        ("near", 6),
        ("finish", 5),
        ("keep", 4),
    ),
    (
        ("finish", 6),
        ("keep", 5),
    ),
)


def gather_and_forward(
    counts,
    lengths,
    owners,
    bias_ref,
    gain_ref,
    x_hbm,
    cot_hbm,
    master_hbm,
    q_ref,
    k_ref,
    v_ref,
    p_ref,
    ctx_hbm,
    x_turned_hbm,
    ctx_turned_hbm,
    hidden_hbm,
    active_hbm,
    slope_hbm,
    down_hbm,
    mixed_hbm,
    second_hbm,
    hat_hbm,
    w_out,
    inverse_ref,
    sum_ref,
    vec_ref,
    cap_ref,
    wide,
    low,
    stage_a,
    stage_b,
    stage_c,
    chosen,
    from_end,
    from_middle,
    w_buf,
    x_then_hidden,
    x_turned,
    ctx_turned,
    hidden_turned,
    ctx_ref,
    cot_then_down,
    mixed_ref,
    hat_ref,
    slope_buf,
    active_buf,
    wide_sem,
    load_sem,
    store_sem,
    half_sem,
    tile_sem,
    out_sem,
    swap_send,
    swap_recv,
    z_send,
    z_recv,
    mid_send,
    mid_recv,
    far_send,
    far_recv,
    near_send,
    near_recv,
):
    step = pl.program_id(0)
    width = 8 * PIECE
    me = lax.axis_index("dp")
    z, y, x, core = place(me)
    in_plane = lax.rem(me, PLANE)
    sibling = me + 1 - 2 * core
    x_peer = me + 2 - 4 * x
    y_peer = me + 4 - 8 * y
    z_targets = along_z(z, in_plane)
    stages = (stage_a, stage_b, stage_c)
    is_end = (z == 0) | (z == 3)
    is_middle = (z == 1) | (z == 2)

    def piece_rows(cell_core, cell_x, cell_y):
        return pl.ds(pl.multiple_of(((cell_core * 2 + cell_x) * 2 + cell_y) * PIECE, 16), PIECE)

    def wide_load(part):
        cols = third(part)
        return pltpu.make_async_copy(master_hbm.at[:, cols], wide.at[:, cols], wide_sem.at[part])

    def swap(part):
        wide_load(part).wait()
        for slot in range(SLOTS):
            master = wide[width * slot : width * (slot + 1), third(part)]
            low[slot, :, third(part)] = master.astype(jnp.bfloat16)

        def send(hop, carry):
            target = lax.rem(in_plane + hop, PLANE)
            _, ty, tx, tc = place(target)
            remote(
                low.at[:, piece_rows(tc, tx, ty), third(part)],
                stages[part].at[pl.ds(2 * in_plane, 2)],
                swap_send.at[part],
                swap_recv.at[part],
                z * PLANE + target,
            ).start()
            return carry

        lax.fori_loop(1, PLANE, send, 0)
        stages[part][pl.ds(2 * in_plane, 2)] = low[:, piece_rows(core, x, y), third(part)]
        if part == 0:
            start([load(0), load(1)])

    def swap_wait(part, sem):
        most = stages[part].at[pl.ds(0, 2 * PLANE - 2)]
        pltpu.make_async_copy(most, most, sem.at[part]).wait()

    def z_copy(unit, part, level):
        first, count, cols = UNITS[unit]
        tiles = pl.ds(first, count)
        cols = cols if count == 4 else Z_PARTS[part]
        src = w_buf.at[tiles, core, x, y, :, cols] if level == 2 else chosen.at[tiles, :, cols]
        dst = (from_end.at[tiles, :, cols], from_middle.at[tiles, :, cols], src)[level]
        at = level, unit, part
        return remote(src, dst, z_send.at[at], z_recv.at[at], z_targets[level])

    def z_parts(unit):
        return range(1 if UNITS[unit][1] == 4 else 2)

    def z_end(unit, part=0):
        @pl.when(is_end)
        def _():
            z_copy(unit, part, 0).start()

    def z_rows(unit, part):
        first, count, cols = UNITS[unit]
        return pl.ds(first, count), cols if count == 4 else Z_PARTS[part]

    def z_middle(unit, part=0):
        @pl.when(is_middle)
        def _():
            z_copy(unit, part, 0).wait_recv()
            tiles, cols = z_rows(unit, part)
            chosen[tiles, :, cols] = chosen[tiles, :, cols] + from_end[tiles, :, cols]
            z_copy(unit, part, 1).start()

    def z_total(unit, part=0):
        @pl.when(is_middle)
        def _():
            z_copy(unit, part, 1).wait_recv()
            tiles, cols = z_rows(unit, part)
            w_buf[tiles, core, x, y, :, cols] = chosen[tiles, :, cols] + from_middle[tiles, :, cols]
            z_copy(unit, part, 2).start()

    def mid_copies(unit):
        first, count, cols = UNITS[unit]
        copies = []
        for n, peer in enumerate((y_peer, x_peer)):
            spot = w_buf.at[pl.ds(first + n * count // 2, count // 2), core, x, y, :, cols]
            copies.append(remote(spot, spot, mid_send.at[unit, n], mid_recv.at[unit, n], peer))
        return copies

    def far_copies(unit):
        first, count, cols = UNITS[unit]
        half = count // 2
        by_row = w_buf.at[pl.ds(first, half), core, x, :, :, cols]
        by_column = w_buf.at[pl.ds(first + half, half), core, :, y, :, cols]
        return [
            remote(spot, spot, far_send.at[unit, n], far_recv.at[unit, n], peer)
            for n, (spot, peer) in enumerate(((by_row, x_peer), (by_column, y_peer)))
        ]

    def near_copy(unit):
        first, count, cols = UNITS[unit]
        spot = w_buf.at[pl.ds(first, count), core, :, :, :, cols]
        return remote(spot, spot, near_send.at[unit], near_recv.at[unit], sibling)

    def give_mid(unit):
        @pl.when(is_end)
        def _():
            arrive([z_copy(unit, part, 2) for part in z_parts(unit)])

        start(mid_copies(unit))

    def give_far(unit):
        arrive(mid_copies(unit))
        start(far_copies(unit))

    def give_near(unit):
        arrive(far_copies(unit))
        near_copy(unit).start()

    def finish(unit):
        near_copy(unit).wait_recv()

    def choose(part):
        swap_wait(part, swap_recv)
        for pair in range(PAIRS):
            for n, tile in enumerate(PAIR_TILES[pair]):
                owner = owners[tile]
                value = stages[part][SLOTS * lax.rem(owner, PLANE) + slot_number(owners, tile)]
                chosen[2 * pair + n, :, third(part)] = jnp.where(
                    owner // PLANE == z, value, jnp.zeros_like(value)
                )

    def load(at):
        src = (x_hbm, cot_hbm)[at]
        dst = (x_then_hidden, cot_then_down)[at]
        return pltpu.make_async_copy(src, dst, load_sem.at[at])

    def store(at):
        src, dst = (
            (hidden_turned, hidden_hbm),
            (ctx_ref, ctx_hbm),
            (hat_ref, hat_hbm),
            None,
            None,
            None,
            (x_turned, x_turned_hbm),
            (ctx_turned, ctx_turned_hbm),
        )[at]
        return pltpu.make_async_copy(src, dst, store_sem.at[at])

    def half_stores(half):
        rows = pl.ds(ROWS * half, ROWS)
        pairs = ((cot_then_down, down_hbm), (mixed_ref, mixed_hbm), (wide, second_hbm))
        return [
            pltpu.make_async_copy(src.at[rows], dst.at[rows], half_sem.at[half, at])
            for at, (src, dst) in enumerate(pairs)
        ]

    def w_store(pair):
        two = pl.ds(2 * pair, 2)
        return pltpu.make_async_copy(w_buf.at[two], w_out.at[two], out_sem.at[pair])

    def weight(at, cols=slice(None)):
        value = w_buf[at, :, :, :, :, cols]
        return value.reshape(width, value.shape[-1])

    def open_all():
        start([wide_load(part) for part in range(3)])
        sum_ref[...] = jnp.zeros_like(sum_ref)
        vec_ref[0:10, :] = bias_ref[...]
        vec_ref[10:12, :] = gain_ref[...]
        greet(z, in_plane)

    def make_caps():
        for block in range(2):
            cap_ref[block] = attention_caps(counts, lengths, block)
        load(0).wait()
        x_turned[...] = x_then_hidden[...].T
        store(6).start()

    actions = {
        "open": open_all,
        "caps": make_caps,
        "swap": swap,
        "sent": lambda part: swap_wait(part, swap_send),
        "choose": choose,
        "end": z_end,
        "middle": z_middle,
        "total": z_total,
        "mid": give_mid,
        "far": give_far,
        "near": give_near,
        "finish": finish,
        "keep": lambda pair: w_store(pair).start(),
    }

    for at, work in enumerate(FRONT_PLAN):

        @pl.when(step == at)
        def _():
            for name, *rest in work:
                actions[name](*rest)

    quad, block = step // 2, lax.rem(step, 2)
    here = pl.ds(pl.multiple_of(block * ROWS, ROWS), ROWS)

    @pl.when(step < 6)
    def _():
        attend_quad(
            quad,
            weight,
            x_then_hidden.at[here],
            vec_ref,
            cap_ref.at[block],
            q_ref,
            k_ref,
            v_ref,
            p_ref,
            ctx_ref.at[here],
        )

    @pl.when((step >= 4) & (step < 6))
    def _():
        branch = dot(ctx_ref[here, :], weight(3)) + vec_ref[2:3, :]
        hat, inverse = normalize(x_then_hidden[here, :].astype(jnp.float32) + branch)
        hat_ref[here, :] = hat.astype(jnp.bfloat16)
        inverse_ref[here, :] = inverse
        hidden = hat * vec_ref[10:11, :] + vec_ref[8:9, :]
        hidden_low = hidden.astype(jnp.bfloat16)
        x_then_hidden[here, :] = hidden_low
        hidden_turned[:, here] = hidden_low.T
        ctx_turned[:, here] = ctx_ref[here, :].T
        wide[here, :] = hidden + vec_ref[7:8, :]

    @pl.when(step == 5)
    def _():
        start([store(0), store(1), store(2), store(7)])

    turn = step - 6
    slot = lax.rem(turn, 2)

    def tile_stores(source_slot, tile):
        return [
            pltpu.make_async_copy(src.at[source_slot], dst.at[tile], tile_sem.at[source_slot, at])
            for at, (src, dst) in enumerate(((active_buf, active_hbm), (slope_buf, slope_hbm)))
        ]

    @pl.when(turn >= 2)
    def _():
        for copy in tile_stores(slot, 0):
            copy.wait()

    @pl.when(turn >= 0)
    def _():
        for half in range(2):
            rows = slice(ROWS * half, ROWS * half + ROWS)
            up = dot(x_then_hidden[rows, :], weight(4 + 2 * turn)) + vec_ref[pl.ds(3 + turn, 1), :]
            active, slope = gelu_parts(up)
            slope_buf[slot, rows, :] = slope.astype(jnp.bfloat16)
            active_buf[slot, :, rows] = active.T
            wide[rows, :] = wide[rows, :] + dot(active, weight(5 + 2 * turn))
        start(tile_stores(slot, turn))

    @pl.when(step == 9)
    def _():
        load(1).wait()
        for half in range(2):
            rows = slice(ROWS * half, ROWS * half + ROWS)
            at_row = lax.broadcasted_iota(jnp.int32, (ROWS, 1), 0) + half * ROWS
            live = passage_facts(counts, lengths, at_row)[0].astype(jnp.float32)
            hat, inverse = normalize(wide[rows, :])
            mixed = (hat * vec_ref[11:12, :] + vec_ref[9:10, :]) * live
            mixed_ref[rows, :] = mixed.astype(jnp.bfloat16)
            grad_out = cot_then_down[rows, :].astype(jnp.float32) * live
            sum_ref[11:12, :] += columns_total(grad_out * hat)
            sum_ref[9:10, :] += columns_total(grad_out)
            second = normalize_back(grad_out * vec_ref[11:12, :], hat, inverse)
            wide[rows, :] = second
            down_low = second.astype(jnp.bfloat16)
            cot_then_down[rows, :] = down_low
            sum_ref[7:8, :] += columns_total(down_low.astype(jnp.float32))
            start(half_stores(half))
        for at in range(2):
            for copy in tile_stores(at, 0):
                copy.wait()
        for pair in range(PAIRS):
            w_store(pair).wait()
        swap_wait(2, swap_send)
        for unit in range(len(UNITS)):
            for copy in mid_copies(unit) + far_copies(unit) + [near_copy(unit)]:
                copy.wait_send()

            @pl.when(is_end)
            def _():
                for part in z_parts(unit):
                    z_copy(unit, part, 0).wait_send()

            @pl.when(is_middle)
            def _():
                for part in z_parts(unit):
                    z_copy(unit, part, 1).wait_send()
                    z_copy(unit, part, 2).wait_send()

        for at in (0, 1, 2, 6, 7):
            store(at).wait()
        for copy in half_stores(0) + half_stores(1):
            copy.wait()


def gathered_and_forwarded(counts, lengths, owners, bias, gain, x, cotangent, master):
    tokens, width = x.shape
    blocks = tokens // ROWS
    low, high = jnp.bfloat16, jnp.float32
    smem = pl.BlockSpec(memory_space=pltpu.SMEM)
    any_space = pl.BlockSpec(memory_space=pl.ANY)
    dma = pltpu.SemaphoreType.DMA
    shaped = jax.ShapeDtypeStruct

    def at(step):
        step = jnp.minimum(step, 5)
        return lax.rem(step, 2), step // 2

    quad = pl.BlockSpec((ROWS, 256), at)
    rows = shaped((tokens, width), low)
    turned = shaped((width, tokens), low)
    cut = (2, 2, 2, PIECE, width)
    units = len(UNITS)
    return pl.pallas_call(
        gather_and_forward,
        grid=(10,),
        out_shape=(
            rows,
            rows,
            rows,
            shaped((blocks, HEADS, ROWS, ROWS), low),
            rows,
            turned,
            turned,
            turned,
            shaped((4, width, tokens), low),
            shaped((4, tokens, width), low),
            rows,
            rows,
            shaped((tokens, width), high),
            rows,
            shaped((TILES,) + cut, low),
            shaped((tokens, 1), high),
            shaped((16, width), high),
        ),
        in_specs=[smem] * 3
        + [pl.BlockSpec(bias.shape, lambda i: (0, 0)), pl.BlockSpec(gain.shape, lambda i: (0, 0))]
        + [any_space] * 3,
        out_specs=(quad, quad, quad, pl.BlockSpec((1, 4, ROWS, ROWS), lambda i: (*at(i), 0, 0)))
        + (any_space,) * 11
        + (
            pl.BlockSpec((tokens, 1), lambda i: (0, 0), pipeline_mode=pl.Buffered(1)),
            pl.BlockSpec((16, width), lambda i: (0, 0)),
        ),
        scratch_shapes=[
            pltpu.VMEM((VROWS, width), high),
            pltpu.VMEM((2, ROWS, ROWS), high),
            pltpu.VMEM((SLOTS * width, width), high),
            pltpu.VMEM((SLOTS, width, width), low),
            pltpu.VMEM((2 * PLANE, PIECE, 256), low),
            pltpu.VMEM((2 * PLANE, PIECE, 256), low),
            pltpu.VMEM((2 * PLANE, PIECE, 256), low),
            pltpu.VMEM((TILES, PIECE, width), low),
            pltpu.VMEM((TILES, PIECE, width), low),
            pltpu.VMEM((TILES, PIECE, width), low),
            pltpu.VMEM((TILES,) + cut, low),
            pltpu.VMEM((tokens, width), low),
            pltpu.VMEM((width, tokens), low),
            pltpu.VMEM((width, tokens), low),
            pltpu.VMEM((width, tokens), low),
            pltpu.VMEM((tokens, width), low),
            pltpu.VMEM((tokens, width), low),
            pltpu.VMEM((tokens, width), low),
            pltpu.VMEM((tokens, width), low),
            pltpu.VMEM((2, tokens, width), low),
            pltpu.VMEM((2, width, tokens), low),
            dma((3,)),
            dma((2,)),
            dma((8,)),
            dma((2, 3)),
            dma((2, 2)),
            dma((PAIRS,)),
            dma((3,)),
            dma((3,)),
            dma((3, units, 2)),
            dma((3, units, 2)),
            dma((units, 2)),
            dma((units, 2)),
            dma((units, 2)),
            dma((units, 2)),
            dma((units,)),
            dma((units,)),
        ],
        compiler_params=pltpu.CompilerParams(
            collective_id=0, has_side_effects=True, vmem_limit_bytes=63 * 2**20
        ),
        name="gather_and_forward",
    )(counts, lengths, owners, bias, gain, x, cotangent, master.reshape(SLOTS * width, width))


BACK_PLAN = (
    (),
    (),
    (
        ("core", 0),
    ),
    (),
    (
        ("core", 1),
        ("far", 0),
    ),
    (),
    (
        ("core", 2),
        ("far", 1),
    ),
    (
        ("mid", 0),
        ("far", 2),
    ),
    (),
    (
        ("core", 3),
        ("mid", 1),
        ("end", 0),
    ),
    (),
    (
        ("far", 3),
        ("end", 1),
        ("mid", 2),
    ),
    (
        ("core", 4),
        ("middle", 0),
    ),
    (),
    (
        ("middle", 1),
        ("end", 2),
        ("mid", 3),
        ("far", 4),
    ),
    (
        ("total", 0),
    ),
    (
        ("middle", 2),
        ("end", 3),
        ("total", 1),
        ("core", 5),
        ("mid", 4),
    ),
    (),
    (
        ("far", 5),
        ("end", 4),
        ("middle", 3),
        ("total", 2),
    ),
    (),
    (
        ("core", 6),
        ("total", 3),
        ("sum", 0),
        ("middle", 4),
        ("mid", 5),
        ("far", 6),
        ("sum", 1),
        ("total", 4),
        ("end", 5),
        ("mid", 6),
        ("sum", 2),
        ("middle", 5),
        ("end", 6),
        ("take", 4),
        ("take", 0),
        ("take", 2),
        ("take", 3),
        ("take", 1),
        ("deliver", 0),
        ("total", 5),
        ("middle", 6),
        ("take", 5),
        ("deliver", 1),
        ("total", 6),
        ("take", 6),
        ("deliver", 2),
        ("input", 0),
        ("input", 1),
    ),
)


def backward_and_reduce(
    owners,
    p_ref,
    q_ref,
    k_ref,
    v_ref,
    inverse_ref,
    gain_ref,
    late_ref,
    ctx_hbm,
    x_turned_hbm,
    ctx_turned_hbm,
    hidden_hbm,
    active_hbm,
    slope_hbm,
    down_hbm,
    second_hbm,
    hat_hbm,
    w_hbm,
    input_hbm,
    slot_grad,
    vec_out,
    w_part,
    acc,
    hidden_then_x,
    active_then_ctx,
    down_then_branch,
    ctx_ref,
    grad_ctx_ref,
    hat_ref,
    slope_then_query,
    up_then_key,
    value_buf,
    part,
    from_core,
    from_far,
    from_mid,
    from_end,
    from_middle,
    total,
    snap,
    outbox,
    vec_now,
    vec_in,
    holds,
    keeps,
    load_sem,
    w_sem,
    core_send,
    core_recv,
    far_send,
    far_recv,
    mid_send,
    mid_recv,
    z_send,
    z_recv,
    vec_send,
    vec_recv,
    out_send,
    out_recv,
):
    step = pl.program_id(0)
    inner = jnp.maximum(step - 4, 0)
    quad, block, pair = inner // 4, lax.rem(inner, 4) // 2, lax.rem(inner, 2)
    me = lax.axis_index("dp")
    z, y, x, core = place(me)
    in_plane = lax.rem(me, PLANE)
    sibling = me + 1 - 2 * core
    x_peer = me + 2 - 4 * x
    y_peer = me + 4 - 8 * y
    z_targets = along_z(z, in_plane)
    is_end = (z == 0) | (z == 3)
    is_middle = (z == 1) | (z == 2)

    def tiles_of(batch):
        if batch < 4:
            return w_part, 4 + 2 * batch, 2, slice(None)
        return part, 0, 4, pl.ds(256 * (batch - 4), 256)

    def halves(batch, turned):
        ref, first, count, cols = tiles_of(batch)
        return ref, pl.ds(first + turned * count // 2, count // 2), cols

    def core_copy(batch):
        ref, first, count, cols = tiles_of(batch)
        tiles = pl.ds(first, count)
        return remote(
            ref.at[tiles, 1 - core, :, :, :, cols],
            from_core.at[tiles, :, :, :, cols],
            core_send.at[batch],
            core_recv.at[batch],
            sibling,
        )

    def far_copies(batch):
        copies = []
        for turned in range(2):
            ref, tiles, cols = halves(batch, turned)
            src = ref.at[tiles, core, :, 1 - y, :, cols] if turned else ref.at[tiles, core, 1 - x, :, :, cols]
            copies.append(
                remote(
                    src,
                    from_far.at[tiles, :, :, cols],
                    far_send.at[batch, turned],
                    far_recv.at[batch, turned],
                    y_peer if turned else x_peer,
                )
            )
        return copies

    def mid_copies(batch):
        copies = []
        for turned in range(2):
            ref, tiles, cols = halves(batch, turned)
            src = ref.at[tiles, core, 1 - x, y, :, cols] if turned else ref.at[tiles, core, x, 1 - y, :, cols]
            copies.append(
                remote(
                    src,
                    from_mid.at[tiles, :, cols],
                    mid_send.at[batch, turned],
                    mid_recv.at[batch, turned],
                    x_peer if turned else y_peer,
                )
            )
        return copies

    def z_copy(batch, stage):
        ref, first, count, cols = tiles_of(batch)
        tiles = pl.ds(first, count)
        if stage == 2:
            src, dst = total.at[tiles, :, cols], total.at[tiles, :, cols]
        else:
            src = ref.at[tiles, core, x, y, :, cols]
            dst = (from_middle if stage else from_end).at[tiles, :, cols]
        return remote(src, dst, z_send.at[stage, batch], z_recv.at[stage, batch], z_targets[stage])

    def give_core(batch):
        core_copy(batch).start()

    def give_far(batch):
        core_copy(batch).wait_recv()
        ref, first, count, cols = tiles_of(batch)
        for tile in range(first, first + count):
            ref[tile, core, :, :, :, cols] = ref[tile, core, :, :, :, cols] + from_core[tile, :, :, :, cols]
        start(far_copies(batch))

    def give_mid(batch):
        arrive(far_copies(batch))
        for turned in range(2):
            ref, tiles, cols = halves(batch, turned)
            if turned:
                ref[tiles, core, :, y, :, cols] = ref[tiles, core, :, y, :, cols] + from_far[tiles, :, :, cols]
            else:
                ref[tiles, core, x, :, :, cols] = ref[tiles, core, x, :, :, cols] + from_far[tiles, :, :, cols]
        start(mid_copies(batch))

    def add_piece(batch, other):
        ref, first, count, cols = tiles_of(batch)
        tiles = pl.ds(first, count)
        return ref[tiles, core, x, y, :, cols] + other[tiles, :, cols]

    def give_end(batch):
        arrive(mid_copies(batch))
        ref, first, count, cols = tiles_of(batch)
        ref[pl.ds(first, count), core, x, y, :, cols] = add_piece(batch, from_mid)

        @pl.when(is_end)
        def _():
            z_copy(batch, 0).start()

    def give_middle(batch):
        @pl.when(is_middle)
        def _():
            z_copy(batch, 0).wait_recv()
            ref, first, count, cols = tiles_of(batch)
            ref[pl.ds(first, count), core, x, y, :, cols] = add_piece(batch, from_end)
            z_copy(batch, 1).start()

    def give_total(batch):
        @pl.when(is_middle)
        def _():
            z_copy(batch, 1).wait_recv()
            _, first, count, cols = tiles_of(batch)
            total[pl.ds(first, count), :, cols] = add_piece(batch, from_middle)
            z_copy(batch, 2).start()

    def take_total(batch):
        @pl.when(is_end)
        def _():
            z_copy(batch, 2).wait_recv()

    def deliver(third):
        cols = pl.ds(256 * third, 256)
        snap[...] = total[:, :, cols]

        def fill(at, carry):
            value = snap[holds[at]]
            outbox[third, at] = jnp.where(keeps[at] > 0, value, jnp.zeros_like(value))
            return carry

        lax.fori_loop(0, 2 * PLANE, fill, 0)

        def send(hop, carry):
            target = lax.rem(in_plane + hop, PLANE)
            remote(
                outbox.at[third, pl.ds(2 * target, 2)],
                slot_grad.at[:, core, x, y, :, cols],
                out_send.at[third],
                out_recv.at[third],
                z * PLANE + target,
            ).start()
            return carry

        lax.fori_loop(1, PLANE, send, 0)
        keep_copy(third).start()

    def keep_copy(third):
        return pltpu.make_async_copy(
            outbox.at[third, pl.ds(2 * in_plane, 2)],
            slot_grad.at[:, core, x, y, :, pl.ds(256 * third, 256)],
            load_sem.at[5 + third],
        )

    def vec_copies(stage):
        if stage < 3:
            hops = [(stage, (sibling, x_peer, y_peer)[stage])]
        else:
            hops = [
                (2 + hop, lax.rem(z + hop, 4) * PLANE + in_plane) for hop in range(1, 4)
            ]
        return [
            remote(vec_now.at[stage], vec_in.at[at], vec_send.at[at], vec_recv.at[at], device)
            for at, device in hops
        ]

    def vec_next(stage):
        arrive(vec_copies(stage))
        vec_now[stage + 1] = vec_now[stage] + vec_in[stage]
        start(vec_copies(stage + 1))

    def input_store():
        return pltpu.make_async_copy(acc, input_hbm, load_sem.at[4])

    def load(at):
        src, dst = (
            (hidden_hbm, hidden_then_x),
            (down_hbm, down_then_branch),
            (second_hbm, acc),
            (hat_hbm, hat_ref),
            None,
            None,
            None,
            None,
            (x_turned_hbm, hidden_then_x),
            (ctx_turned_hbm, active_then_ctx),
            None,
            None,
            (ctx_hbm, ctx_ref),
        )[at]
        return pltpu.make_async_copy(src, dst, load_sem.at[at])

    def tile_load(tile, side):
        src, dst = ((slope_hbm, slope_then_query), (active_hbm, active_then_ctx))[side]
        return pltpu.make_async_copy(src.at[tile], dst, load_sem.at[10 + side])

    def w_load(at):
        return pltpu.make_async_copy(w_hbm.at[at], w_part.at[at], w_sem.at[at])

    def weight(at, cols=slice(None)):
        value = w_part[at, :, :, :, :, cols]
        return value.reshape(8 * PIECE, value.shape[-1])

    def input_rows(half):
        rows = slice(ROWS * half, ROWS * half + ROWS)
        more = acc[rows, :]
        for at, buf in enumerate((slope_then_query, up_then_key, value_buf)):
            more = more + dot_back(buf[rows, :], weight(at))
        acc[rows, :] = more
        if half == 1:
            input_store().start()

    actions = {
        "core": give_core,
        "far": give_far,
        "mid": give_mid,
        "end": give_end,
        "middle": give_middle,
        "total": give_total,
        "take": take_total,
        "deliver": deliver,
        "sum": vec_next,
        "input": input_rows,
    }

    @pl.when(step == 0)
    def _():
        start([load(1), tile_load(0, 0), w_load(5), w_load(4)])
        for at in range(2 * PLANE):
            tile_here, kept = jnp.int32(0), jnp.int32(0)
            for tile in range(TILES):
                place_of = SLOTS * owners[tile] + slot_number(owners, tile)
                match = place_of == z * 2 * PLANE + at
                tile_here = tile_here + jnp.where(match, POSITIONS.index(tile), 0)
                kept = kept + jnp.where(match, 1, 0)
            holds[at] = tile_here
            keeps[at] = kept
        vec_now[0] = late_ref[...]
        greet(z, in_plane)

    def serve(points):
        for at in points:
            if BACK_PLAN[at]:

                @pl.when(step == (at // 2 if at < 8 else at - 4))
                def _():
                    for name, number in BACK_PLAN[at]:
                        actions[name](number)

    serve(range(0, 8, 2))

    @pl.when(step < 4)
    def _():
        tile_load(step, 0).wait()
        w_load(5 + 2 * step).wait()

        @pl.when(step == 0)
        def _():
            load(1).wait()
            start([load(2), tile_load(0, 1), load(0)])

        @pl.when(step < 3)
        def _():
            start([w_load(7 + 2 * step), w_load(6 + 2 * step)])

        @pl.when(step == 1)
        def _():
            load(3).start()

        @pl.when(step == 2)
        def _():
            w_load(3).start()

        @pl.when(step == 3)
        def _():
            start([load(12), w_load(0), w_load(1), w_load(2)])

        for half in range(2):
            rows = slice(ROWS * half, ROWS * half + ROWS)
            back = dot_back(down_then_branch[rows, :], weight(5 + 2 * step))
            up_low = (back * slope_then_query[rows, :].astype(jnp.float32)).astype(jnp.bfloat16)
            up_then_key[rows, :] = up_low
            vec_now[0, pl.ds(3 + step, 1), :] += columns_total(up_low.astype(jnp.float32))

        @pl.when(step < 3)
        def _():
            tile_load(step + 1, 0).start()

        w_load(4 + 2 * step).wait()

        @pl.when(step == 0)
        def _():
            load(2).wait()
            load(0).wait()

        for half in range(2):
            rows = slice(ROWS * half, ROWS * half + ROWS)
            acc[rows, :] = acc[rows, :] + dot_back(up_then_key[rows, :], weight(4 + 2 * step))

    serve(range(1, 8, 2))

    @pl.when(step < 4)
    def _():
        tile_load(step, 1).wait()
        by_down = dot(active_then_ctx[...], down_then_branch[...]).astype(jnp.bfloat16)
        w_part[5 + 2 * step] = by_down.reshape(2, 2, 2, PIECE, 8 * PIECE)

        @pl.when(step < 3)
        def _():
            tile_load(step + 1, 1).start()

        by_up = dot(hidden_then_x[...], up_then_key[...]).astype(jnp.bfloat16)
        w_part[4 + 2 * step] = by_up.reshape(2, 2, 2, PIECE, 8 * PIECE)

    @pl.when(step == 3)
    def _():
        start([load(8), load(9)])
        load(3).wait()
        w_load(3).wait()
        for half in range(2):
            rows = slice(ROWS * half, ROWS * half + ROWS)
            grad_hidden, hat = acc[rows, :], hat_ref[rows, :].astype(jnp.float32)
            vec_now[0, 10:11, :] += columns_total(grad_hidden * hat)
            vec_now[0, 8:9, :] += columns_total(grad_hidden)
            first = normalize_back(grad_hidden * gain_ref[0:1, :], hat, inverse_ref[rows, :])
            acc[rows, :] = first
            branch_low = first.astype(jnp.bfloat16)
            down_then_branch[rows, :] = branch_low
            vec_now[0, 2:3, :] += columns_total(branch_low.astype(jnp.float32))
            grad_ctx_ref[rows, :] = dot_back(branch_low, weight(3)).astype(jnp.bfloat16)

    serve(range(8, 20))

    here = pl.ds(pl.multiple_of(block * ROWS, ROWS), ROWS)
    quad_cols = pl.ds(pl.multiple_of(quad * 256, 256), 256)

    @pl.when(step == 4)
    def _():
        load(12).wait()
        for at in range(3):
            w_load(at).wait()

    pair_cols = pl.ds(pl.multiple_of(quad * 256 + pair * 128, 128), 128)
    grad_bufs = (slope_then_query, up_then_key, value_buf)

    @pl.when(step >= 4)
    def _():
        grads = attend_back_pair(
            grad_ctx_ref[here, pair_cols],
            ctx_ref[here, pair_cols],
            p_ref.at[0],
            q_ref[...],
            k_ref[...],
            v_ref[...],
        )
        for buf, grad in zip(grad_bufs, grads):
            buf[here, pair_cols] = grad
        vec_now[0, 0:1, pair_cols] += columns_total(grads[0].astype(jnp.float32))
        vec_now[0, 1:2, pair_cols] += columns_total(grads[2].astype(jnp.float32))

    @pl.when(step == 7)
    def _():
        load(8).wait()
        load(9).wait()

    @pl.when((step >= 4) & (block == 1) & (pair == 1))
    def _():
        for tile in range(4):
            if tile < 3:
                value = dot(hidden_then_x[...], grad_bufs[tile][:, quad_cols])
            else:
                value = dot(active_then_ctx[...], down_then_branch[:, quad_cols])
            value = value.astype(jnp.bfloat16).reshape(2, 2, 2, PIECE, 256)
            part[tile, :, :, :, :, quad_cols] = value


    @pl.when(step == 15)
    def _():
        start(vec_copies(0))
        for name, number in BACK_PLAN[-1]:
            actions[name](number)
        arrive(vec_copies(3))
        summed = jnp.zeros(vec_out.shape, jnp.float32)
        for origin in range(4):
            hop = lax.rem(z - origin + 4, 4)
            summed = summed + jnp.where(hop == 0, vec_now[3], vec_in[2 + jnp.maximum(hop, 1)])
        vec_out[...] = summed
        for batch in range(7):
            for copy in [core_copy(batch)] + far_copies(batch) + mid_copies(batch):
                copy.wait_send()

            @pl.when(is_end)
            def _():
                z_copy(batch, 0).wait_send()

            @pl.when(is_middle)
            def _():
                z_copy(batch, 1).wait_send()
                z_copy(batch, 2).wait_send()

        for stage in range(4):
            for copy in vec_copies(stage):
                copy.wait_send()
        input_store().wait()
        for third in range(3):
            keep_copy(third).wait()
            most = outbox.at[third, pl.ds(0, 2 * PLANE - 2)]
            pltpu.make_async_copy(most, most, out_recv.at[third]).wait()
            pltpu.make_async_copy(most, most, out_send.at[third]).wait()


def backward_and_reduced(
    owners,
    probs,
    query,
    keyed,
    valued,
    inverse,
    gain,
    late_sums,
    context,
    x_turned,
    ctx_turned,
    hidden,
    active,
    slope,
    grad_down,
    grad_second,
    hat,
    weights,
):
    tokens, width = grad_down.shape
    low, high = jnp.bfloat16, jnp.float32
    shaped = jax.ShapeDtypeStruct
    smem = pl.BlockSpec(memory_space=pltpu.SMEM)
    any_space = pl.BlockSpec(memory_space=pl.ANY)
    dma = pltpu.SemaphoreType.DMA
    once = pl.Buffered(1)

    def at(step):
        inner = jnp.maximum(step - 4, 0)
        return lax.rem(inner, 4) // 2, inner // 4 * 2 + lax.rem(inner, 2)

    pair = pl.BlockSpec((ROWS, 128), at)
    sums = pl.BlockSpec((16, width), lambda i: (0, 0))
    cut = (2, 2, 2, PIECE, width)
    input_grad, slot_grads, vector_sums = pl.pallas_call(
        backward_and_reduce,
        grid=(16,),
        out_shape=(
            shaped((tokens, width), high),
            shaped((SLOTS,) + cut, low),
            shaped((16, width), high),
        ),
        in_specs=[smem, pl.BlockSpec((1, 2, ROWS, ROWS), lambda i: (*at(i), 0, 0))]
        + [pair] * 3
        + [
            pl.BlockSpec((tokens, 1), lambda i: (0, 0), pipeline_mode=once),
            pl.BlockSpec(gain.shape, lambda i: (0, 0)),
            sums,
        ]
        + [any_space] * 10,
        out_specs=(any_space, any_space, sums),
        scratch_shapes=[
            pltpu.VMEM((TILES,) + cut, low),
            pltpu.VMEM((tokens, width), high),
            pltpu.VMEM((width, tokens), low),
            pltpu.VMEM((width, tokens), low),
            pltpu.VMEM((tokens, width), low),
            pltpu.VMEM((tokens, width), low),
            pltpu.VMEM((tokens, width), low),
            pltpu.VMEM((tokens, width), low),
            pltpu.VMEM((tokens, width), low),
            pltpu.VMEM((tokens, width), low),
            pltpu.VMEM((tokens, width), low),
            pltpu.VMEM((4,) + cut, low),
            pltpu.VMEM((TILES,) + cut[1:], low),
            pltpu.VMEM((TILES,) + cut[2:], low),
            pltpu.VMEM((TILES,) + cut[3:], low),
            pltpu.VMEM((TILES,) + cut[3:], low),
            pltpu.VMEM((TILES,) + cut[3:], low),
            pltpu.VMEM((TILES,) + cut[3:], low),
            pltpu.VMEM((TILES, PIECE, 256), low),
            pltpu.VMEM((3, 2 * PLANE, PIECE, 256), low),
            pltpu.VMEM((4, 16, width), high),
            pltpu.VMEM((6, 16, width), high),
            pltpu.SMEM((2 * PLANE,), jnp.int32),
            pltpu.SMEM((2 * PLANE,), jnp.int32),
            dma((13,)),
            dma((TILES,)),
            dma((7,)),
            dma((7,)),
            dma((7, 2)),
            dma((7, 2)),
            dma((7, 2)),
            dma((7, 2)),
            dma((3, 7)),
            dma((3, 7)),
            dma((6,)),
            dma((6,)),
            dma((3,)),
            dma((3,)),
        ],
        compiler_params=pltpu.CompilerParams(
            collective_id=1, has_side_effects=True, vmem_limit_bytes=63 * 2**20
        ),
        name="backward_and_reduce",
    )(
        owners,
        probs,
        query,
        keyed,
        valued,
        inverse,
        gain,
        late_sums,
        context,
        x_turned,
        ctx_turned,
        hidden,
        active,
        slope,
        grad_down,
        grad_second,
        hat,
        weights,
    )
    return input_grad, slot_grads.reshape(SLOTS, width, width), vector_sums


def collected_tiles(tile_low, owners, slots):
    mine = owners == lax.axis_index("dp")
    local = jnp.where(mine[:, None, None], tile_low[slots], jnp.zeros((), tile_low.dtype))
    return lax.psum(local, "dp")


def summed_over_slice(parts, vector_terms, owners, slots):
    myself = lax.axis_index("dp")

    def add(held, items):
        part, owner, slot = items
        total = lax.psum(part.astype(jnp.float32), "dp")
        here = (owner == myself) & (slot == jnp.arange(SLOTS, dtype=jnp.int32))
        return held + jnp.where(here[:, None, None], total[None], 0.0), None

    empty = jnp.zeros((SLOTS,) + parts.shape[1:], jnp.float32)
    return lax.scan(add, empty, (parts, owners, slots))[0], lax.psum(vector_terms, "dp")


def body(
    inputs,
    cotangent,
    counts,
    lengths,
    owners,
    tile_master,
    tile_first,
    tile_second,
    tile_ema,
    bias_vals,
    gain_vals,
    vector_first,
    vector_second,
    vector_ema,
):
    tokens = inputs.shape[0]
    small = lax.axis_size("dp") == GROUP
    gain_scale = float(tokens * lax.axis_size("dp")) ** (-0.5)
    if small:
        (
            query,
            keyed,
            valued,
            probs,
            context,
            x_turned,
            ctx_turned,
            hidden,
            active,
            slope,
            grad_down,
            mixed,
            grad_second,
            hat,
            weights,
            inverse,
            late_sums,
        ) = gathered_and_forwarded(
            counts,
            lengths,
            owners,
            bias_vals,
            gain_vals,
            inputs,
            cotangent,
            tile_master,
        )
        input_grad, slot_grads, full_sums = backward_and_reduced(
            owners,
            probs,
            query,
            keyed,
            valued,
            inverse,
            gain_vals,
            late_sums,
            context,
            x_turned,
            ctx_turned,
            hidden,
            active,
            slope,
            grad_down,
            grad_second,
            hat,
            weights,
        )
    else:
        slots = tile_slots(owners)
        vectors = jnp.concatenate([bias_vals, gain_vals], 0)
        weights = collected_tiles(tile_master[0].astype(jnp.bfloat16), owners, slots)
        query, keyed, valued, probs, context, hat, inverse = attended(
            counts, lengths, inputs, weights, vectors
        )
        mixed, grad_first, grad_branch, grad_context, up_grads, down_grads, late_sums = fed_forward_both(
            counts, lengths, hat, inverse, cotangent, weights, vectors
        )
        input_grad, early_grads, early_sums = attended_back(
            probs, query, keyed, valued, inputs, context, grad_context, grad_branch, grad_first, weights
        )
        parts = jnp.concatenate([early_grads, up_grads, down_grads], 0)
        slot_grads, full_sums = summed_over_slice(parts, late_sums + early_sums, owners, slots)
    return updated(
        gain_scale,
        slot_grads,
        tile_master,
        tile_first,
        tile_second,
        tile_ema,
        full_sums,
        bias_vals,
        gain_vals,
        vector_first,
        vector_second,
        vector_ema,
        mixed,
        input_grad,
    )


def solution(mesh):
    placed = (
        P("dp", None),
        P("dp", None),
        P("dp", None),
        P("dp", None),
        P(),
        P("dp", None, None, None),
        P("dp", None, None, None),
        P("dp", None, None, None),
        P("dp", None, None, None),
        P(),
        P(),
        P(),
        P(),
        P(),
    )
    return jax.shard_map(
        body,
        mesh=mesh,
        in_specs=placed,
        out_specs=(
            P("dp", None),
            P("dp", None),
            P("dp", None, None, None),
            P("dp", None, None, None),
            P("dp", None, None, None),
            P("dp", None, None, None),
            P("dp", None, None, None),
            P(),
            P(),
            P(),
            P(),
        ),
        check_vma=False,
    )
```

```python
import functools

import jax
import jax.numpy as jnp
from jax import lax
from jax.experimental import pallas as pl
from jax.experimental.pallas import tpu as pltpu
from jax.sharding import PartitionSpec as P

HEADS = 12
BUCKET = 128
SLOTS = 2
TILES = 12
VROWS = 12
STEP = 5

norm_epsilon = 1e-12
tile_rate = 0.03
vector_rate = 0.2
first_decay = 0.5
second_decay = 0.5
adam_epsilon = 1e-08
weight_decay = 0.01
average_rate = 0.9


def tile_slots(owners):
    order = jnp.arange(owners.shape[0], dtype=jnp.int32)
    same = owners[:, None] == owners[None, :]
    earlier = order[None, :] < order[:, None]
    return jnp.sum((same & earlier).astype(jnp.int32), 1)


def adam_update(param, grad, first, second, rate):
    first_new = first_decay * first + (1.0 - first_decay) * grad
    second_new = second_decay * second + (1.0 - second_decay) * grad * grad
    first_hat = first_new / (1.0 - first_decay**STEP)
    second_hat = second_new / (1.0 - second_decay**STEP)
    param_new = param - rate * (
        first_hat / (jnp.sqrt(second_hat) + adam_epsilon) + weight_decay * param
    )
    return (param_new, first_new, second_new)


ROWS = 4 * BUCKET
TAIL_RATE = 0.28
TAIL_SERIES = (
    0.11615256574707405,
    0.06981038475559553,
    0.2631359597579608,
    -0.22983675561378278,
    0.38546775012288165,
    -0.10472989053809521,
)
INV_SQRT_TAU = 0.3989422804014327
ALLOWED = 3.0e38
BARRED = -1000000000.0


def dot(left, right):
    return jnp.dot(left, right, preferred_element_type=jnp.float32)


def dot_back(left, right):
    return lax.dot_general(
        left, right, (((1,), (1,)), ((), ())), preferred_element_type=jnp.float32
    )


def outer(left, right):
    return lax.dot_general(
        left, right, (((0,), (0,)), ((), ())), preferred_element_type=jnp.float32
    )


def passage_facts(counts, lengths, position):
    places = lengths.shape[1]
    big_end = counts[0, 0]
    mid_end = big_end + counts[0, 1]
    all_end = mid_end + counts[0, 2]
    start = jnp.int32(0)
    member = jnp.zeros(position.shape, jnp.int32)
    usable = jnp.zeros(position.shape, jnp.int32)
    for number in range(places):
        size = jnp.where(
            number < big_end,
            4 * BUCKET,
            jnp.where(number < mid_end, 2 * BUCKET, jnp.where(number < all_end, BUCKET, 0)),
        )
        inside = (position >= start) & (position < start + size)
        live = inside & (position < start + lengths[0, number])
        member = jnp.where(inside, number + 1, member)
        usable = jnp.where(live, 1, usable)
        start = start + size
    passage = jnp.where(member > 0, member - 1, places + position // BUCKET)
    return usable, passage


def normalize(values):
    center = jnp.mean(values, -1, keepdims=True)
    centered = values - center
    spread = jnp.mean(centered * centered, -1, keepdims=True)
    inverse = lax.rsqrt(spread + norm_epsilon)
    return centered * inverse, inverse


def normalize_back(grad, hat, inverse):
    center = jnp.mean(grad, -1, keepdims=True)
    along = jnp.mean(grad * hat, -1, keepdims=True)
    return inverse * (grad - center - hat * along)


def columns_total(values):
    return jnp.sum(values, 0, keepdims=True)


def attention_caps(counts, lengths, block):
    at_row = lax.broadcasted_iota(jnp.int32, (ROWS, 1), 0) + block * ROWS
    at_column = lax.broadcasted_iota(jnp.int32, (1, ROWS), 1) + block * ROWS
    _, passage_row = passage_facts(counts, lengths, at_row)
    usable_column, passage_column = passage_facts(counts, lengths, at_column)
    allowed = (passage_row == passage_column) & ((usable_column == 1) | (at_row == at_column))
    return jnp.where(allowed, ALLOWED, BARRED)


def attend_quad(quad, weight, x_ref, vec_ref, cap_ref, q_ref, k_ref, v_ref, p_ref, ctx_ref):
    cols = pl.ds(pl.multiple_of(quad * 256, 256), 256)
    x = x_ref[...]
    query = (dot(x, weight(0, cols)) + vec_ref[0:1, cols]).astype(jnp.bfloat16)
    query = query * jnp.bfloat16(0.125)
    keyed = dot(x, weight(1, cols)).astype(jnp.bfloat16)
    valued = (dot(x, weight(2, cols)) + vec_ref[1:2, cols]).astype(jnp.bfloat16)
    q_ref[...] = query
    k_ref[...] = keyed
    v_ref[...] = valued
    low_half = lax.broadcasted_iota(jnp.int32, (1, 128), 1) < 64
    for pair in range(2):
        part = slice(128 * pair, 128 * pair + 128)
        contexts = []
        for head in range(2):
            here = low_half if head == 0 else ~low_half
            mine = jnp.where(here, query[:, part], jnp.zeros_like(query[:, part]))
            scores = jnp.minimum(dot_back(mine, keyed[:, part]), cap_ref[...])
            exponent = jnp.exp(scores - jnp.max(scores, -1, keepdims=True))
            inverse = 1.0 / jnp.sum(exponent, -1, keepdims=True)
            probability = (exponent * inverse).astype(jnp.bfloat16)
            p_ref[0, 2 * pair + head] = probability
            contexts.append(dot(probability, valued[:, part]))
        both = jnp.where(low_half, contexts[0], contexts[1]).astype(jnp.bfloat16)
        ctx_ref[:, pl.ds(pl.multiple_of(quad * 256 + 128 * pair, 128), 128)] = both


def close_block(w_out, x_ref, vec_ref, ctx_ref, hat_ref, inverse_ref):
    branch = dot(ctx_ref[...], w_out) + vec_ref[2:3, :]
    hat_ref[...], inverse_ref[...] = normalize(x_ref[...].astype(jnp.float32) + branch)


def attend_back_pair(pull, level_from, p_ref, query, keyed, valued):
    low_half = lax.broadcasted_iota(jnp.int32, (1, 128), 1) < 64
    along = pull.astype(jnp.float32) * level_from.astype(jnp.float32)
    by_query, by_key, by_value = [], [], []
    for head in range(2):
        mask = low_half if head == 0 else ~low_half
        mine = jnp.where(mask, pull, jnp.zeros_like(pull))
        level = jnp.sum(jnp.where(mask, along, 0.0), -1, keepdims=True)
        probability = p_ref[head]
        grad_prob = dot_back(mine, valued)
        grad_scores = (probability.astype(jnp.float32) * (grad_prob - level)).astype(jnp.bfloat16)
        by_query.append(dot(grad_scores, keyed))
        by_key.append(outer(grad_scores, query))
        by_value.append(outer(probability, pull))
    grad_query = jnp.where(low_half, by_query[0], by_query[1]) * 0.125
    grad_key = jnp.where(low_half, by_key[0], by_key[1])
    grad_value = jnp.where(low_half, by_value[0], by_value[1])
    return [value.astype(jnp.bfloat16) for value in (grad_query, grad_key, grad_value)]


def gelu_parts(up):
    near = 1.0 / (1.0 + TAIL_RATE * jnp.abs(up))
    decay = jnp.exp(up * up * -0.5)
    series = jnp.full_like(near, TAIL_SERIES[-1])
    for term in TAIL_SERIES[-2::-1]:
        series = series * near + term
    tail = series * near * decay
    share = jnp.where(up < 0.0, tail, 1.0 - tail)
    slope = share + up * (decay * INV_SQRT_TAU)
    return (up * share).astype(jnp.bfloat16), slope


def attend_forward(
    counts,
    lengths,
    x_ref,
    w_hbm,
    vec_ref,
    q_ref,
    k_ref,
    v_ref,
    p_ref,
    ctx_ref,
    hat_ref,
    inverse_ref,
    w_buf,
    cap_ref,
    w_sem,
):
    block, quad = pl.program_id(0), pl.program_id(1)
    loads = [pltpu.make_async_copy(w_hbm.at[at], w_buf.at[at], w_sem.at[at]) for at in range(4)]

    @pl.when((block == 0) & (quad == 0))
    def _():
        for load in loads:
            load.start()
        for load in loads:
            load.wait()

    @pl.when(quad == 0)
    def _():
        cap_ref[...] = attention_caps(counts, lengths, block)

    def weight(at, cols):
        return w_buf[at, :, cols]

    attend_quad(quad, weight, x_ref, vec_ref, cap_ref, q_ref, k_ref, v_ref, p_ref, ctx_ref)

    @pl.when(quad == 2)
    def _():
        close_block(w_buf[3], x_ref, vec_ref, ctx_ref, hat_ref, inverse_ref)


def attended(counts, lengths, x, weights, vectors):
    tokens, width = x.shape
    blocks = tokens // ROWS
    low = jnp.bfloat16
    smem = pl.BlockSpec(memory_space=pltpu.SMEM)
    quad = pl.BlockSpec((ROWS, 256), lambda b, h: (b, h))
    rows = pl.BlockSpec((ROWS, width), lambda b, h: (b, 0))
    shaped = jax.ShapeDtypeStruct
    return pl.pallas_call(
        attend_forward,
        grid=(blocks, 3),
        out_shape=(
            shaped((tokens, width), low),
            shaped((tokens, width), low),
            shaped((tokens, width), low),
            shaped((blocks, HEADS, ROWS, ROWS), low),
            shaped((tokens, width), low),
            shaped((tokens, width), jnp.float32),
            shaped((tokens, 1), jnp.float32),
        ),
        in_specs=[
            smem,
            smem,
            rows,
            pl.BlockSpec(memory_space=pl.ANY),
            pl.BlockSpec((VROWS, width), lambda b, h: (0, 0)),
        ],
        out_specs=(
            quad,
            quad,
            quad,
            pl.BlockSpec((1, 4, ROWS, ROWS), lambda b, h: (b, h, 0, 0)),
            rows,
            rows,
            pl.BlockSpec((ROWS, 1), lambda b, h: (b, 0)),
        ),
        scratch_shapes=[
            pltpu.VMEM((4, width, width), low),
            pltpu.VMEM((ROWS, ROWS), jnp.float32),
            pltpu.SemaphoreType.DMA((4,)),
        ],
        compiler_params=pltpu.CompilerParams(vmem_limit_bytes=56 * 2**20),
        name="attend_forward",
    )(counts, lengths, x, weights, vectors)


def feed_forward_both(
    counts,
    lengths,
    hat_ref,
    inverse_ref,
    cot_ref,
    w_hbm,
    vec_ref,
    mixed_ref,
    first_ref,
    branch_ref,
    context_ref,
    up_grad_ref,
    down_grad_ref,
    sum_ref,
    w_buf,
    active_ref,
    up_ref,
    hidden_ref,
    down_ref,
    slope_ref,
    w_sem,
):
    step = pl.program_id(0)
    blocks = pl.num_programs(0) - 4
    loads = [
        pltpu.make_async_copy(w_hbm.at[3 + at], w_buf.at[at], w_sem.at[at]) for at in range(9)
    ]

    @pl.when(step == 0)
    def _():
        for load in loads[1:] + loads[:1]:
            load.start()
        sum_ref[...] = jnp.zeros_like(sum_ref)
        for load in loads[1:] + loads[:1]:
            load.wait()

    @pl.when(step < blocks)
    def _():
        here = pl.ds(pl.multiple_of(step * ROWS, ROWS), ROWS)
        at_row = lax.broadcasted_iota(jnp.int32, (ROWS, 1), 0) + step * ROWS
        live = passage_facts(counts, lengths, at_row)[0].astype(jnp.float32)
        hat = hat_ref[...]
        hidden = hat * vec_ref[10:11, :] + vec_ref[8:9, :]
        hidden_low = hidden.astype(jnp.bfloat16)
        hidden_ref[here, :] = hidden_low
        total = hidden + vec_ref[7:8, :]
        for tile in range(4):
            up = dot(hidden_low, w_buf[1 + tile]) + vec_ref[3 + tile : 4 + tile, :]
            active, slope = gelu_parts(up)
            slope_ref[tile] = slope.astype(jnp.bfloat16)
            active_ref[tile, here, :] = active
            total = total + dot(active, w_buf[5 + tile])
        hat_two, inverse_two = normalize(total)
        mixed_ref[...] = ((hat_two * vec_ref[11:12, :] + vec_ref[9:10, :]) * live).astype(jnp.bfloat16)
        grad_out = cot_ref[...].astype(jnp.float32) * live
        sum_ref[11:12, :] += columns_total(grad_out * hat_two)
        sum_ref[9:10, :] += columns_total(grad_out)
        second = normalize_back(grad_out * vec_ref[11:12, :], hat_two, inverse_two)
        down_low = second.astype(jnp.bfloat16)
        down_ref[here, :] = down_low
        sum_ref[7:8, :] += columns_total(down_low.astype(jnp.float32))
        grad_hidden = second
        for tile in range(4):
            pulled = dot_back(down_low, w_buf[5 + tile])
            up_low = (pulled * slope_ref[tile].astype(jnp.float32)).astype(jnp.bfloat16)
            up_ref[tile, here, :] = up_low
            sum_ref[3 + tile : 4 + tile, :] += columns_total(up_low.astype(jnp.float32))
            grad_hidden = grad_hidden + dot_back(up_low, w_buf[1 + tile])
        sum_ref[10:11, :] += columns_total(grad_hidden * hat)
        sum_ref[8:9, :] += columns_total(grad_hidden)
        grad_first = normalize_back(grad_hidden * vec_ref[10:11, :], hat, inverse_ref[...])
        first_ref[...] = grad_first
        branch_low = grad_first.astype(jnp.bfloat16)
        branch_ref[...] = branch_low
        sum_ref[2:3, :] += columns_total(branch_low.astype(jnp.float32))
        context_ref[...] = dot_back(branch_low, w_buf[0]).astype(jnp.bfloat16)

    @pl.when(step >= blocks)
    def _():
        tile = step - blocks
        up_grad_ref[0] = outer(hidden_ref[...], up_ref[tile]).astype(jnp.bfloat16)
        down_grad_ref[0] = outer(active_ref[tile], down_ref[...]).astype(jnp.bfloat16)


def fed_forward_both(counts, lengths, hat, inverse, cotangent, weights, vectors):
    tokens, width = hat.shape
    blocks = tokens // ROWS
    low = jnp.bfloat16
    smem = pl.BlockSpec(memory_space=pltpu.SMEM)
    shaped = jax.ShapeDtypeStruct

    def block_of(step):
        return jnp.minimum(step, blocks - 1)

    def tile_of(step):
        return jnp.maximum(step - blocks, 0)

    rows = pl.BlockSpec((ROWS, width), lambda i: (block_of(i), 0))
    tile = pl.BlockSpec((1, width, width), lambda i: (tile_of(i), 0, 0))
    return pl.pallas_call(
        feed_forward_both,
        grid=(blocks + 4,),
        out_shape=(
            shaped((tokens, width), low),
            shaped((tokens, width), jnp.float32),
            shaped((tokens, width), low),
            shaped((tokens, width), low),
            shaped((4, width, width), low),
            shaped((4, width, width), low),
            shaped((16, width), jnp.float32),
        ),
        in_specs=[
            smem,
            smem,
            rows,
            pl.BlockSpec((ROWS, 1), lambda i: (block_of(i), 0)),
            rows,
            pl.BlockSpec(memory_space=pl.ANY),
            pl.BlockSpec((VROWS, width), lambda i: (0, 0)),
        ],
        out_specs=(
            rows,
            rows,
            rows,
            rows,
            tile,
            tile,
            pl.BlockSpec((16, width), lambda i: (0, 0)),
        ),
        scratch_shapes=[
            pltpu.VMEM((9, width, width), low),
            pltpu.VMEM((4, tokens, width), low),
            pltpu.VMEM((4, tokens, width), low),
            pltpu.VMEM((tokens, width), low),
            pltpu.VMEM((tokens, width), low),
            pltpu.VMEM((4, ROWS, width), low),
            pltpu.SemaphoreType.DMA((9,)),
        ],
        compiler_params=pltpu.CompilerParams(vmem_limit_bytes=60 * 2**20),
        name="feed_forward_both",
    )(counts, lengths, hat, inverse, cotangent, weights, vectors)


def attend_backward(
    p_ref,
    q_ref,
    k_ref,
    v_ref,
    x_ref,
    ctx_ref,
    grad_ctx_ref,
    branch_ref,
    first_ref,
    w_ref,
    input_ref,
    grad_ref,
    sum_ref,
    pulled,
):
    step = pl.program_id(0)
    quad, block = step // 2, lax.rem(step, 2)
    here = pl.ds(pl.multiple_of(block * ROWS, ROWS), ROWS)
    cols = pl.ds(pl.multiple_of(quad * 256, 256), 256)

    @pl.when(step == 0)
    def _():
        sum_ref[...] = jnp.zeros_like(sum_ref)
        input_ref[...] = first_ref[...]

    for pair in range(2):
        half = slice(128 * pair, 128 * pair + 128)
        at = pl.ds(pl.multiple_of(quad * 256 + 128 * pair, 128), 128)
        heads = p_ref.at[0, pl.ds(2 * pair, 2)]
        grads = attend_back_pair(
            grad_ctx_ref[here, at], ctx_ref[here, at], heads, q_ref[:, half], k_ref[:, half], v_ref[:, half]
        )
        for number, grad in enumerate(grads):
            pulled[number, here, half] = grad
        sum_ref[0:1, at] += columns_total(grads[0].astype(jnp.float32))
        sum_ref[1:2, at] += columns_total(grads[2].astype(jnp.float32))

    more = input_ref[here, :]
    for at in range(3):
        more = more + dot_back(pulled[at, here, :], w_ref[at, :, cols])
    input_ref[here, :] = more

    @pl.when(block == 1)
    def _():
        for tile in range(3):
            grad_ref[tile, :, cols] = outer(x_ref[...], pulled[tile]).astype(jnp.bfloat16)
        grad_ref[3, :, cols] = outer(ctx_ref[...], branch_ref[:, cols]).astype(jnp.bfloat16)


def attended_back(probs, query, keyed, valued, x, context, grad_context, grad_branch, grad_first, weights):
    tokens, width = x.shape
    low = jnp.bfloat16
    shaped = jax.ShapeDtypeStruct
    once = pl.Buffered(1)
    quad = pl.BlockSpec((ROWS, 256), lambda i: (lax.rem(i, 2), i // 2))
    whole = pl.BlockSpec((tokens, width), lambda i: (0, 0), pipeline_mode=once)
    return pl.pallas_call(
        attend_backward,
        grid=(6,),
        out_shape=(
            shaped((tokens, width), jnp.float32),
            shaped((4, width, width), low),
            shaped((16, width), jnp.float32),
        ),
        in_specs=[
            pl.BlockSpec((1, 4, ROWS, ROWS), lambda i: (lax.rem(i, 2), i // 2, 0, 0)),
            quad,
            quad,
            quad,
            whole,
            whole,
            whole,
            whole,
            whole,
            pl.BlockSpec((3, width, width), lambda i: (0, 0, 0), pipeline_mode=once),
        ],
        out_specs=(
            whole,
            pl.BlockSpec((4, width, width), lambda i: (0, 0, 0), pipeline_mode=once),
            pl.BlockSpec((16, width), lambda i: (0, 0)),
        ),
        scratch_shapes=[pltpu.VMEM((3, tokens, 256), low)],
        compiler_params=pltpu.CompilerParams(vmem_limit_bytes=56 * 2**20),
        name="attend_backward",
    )(probs, query, keyed, valued, x, context, grad_context, grad_branch, grad_first, weights)


def moved(param, grad, first, second, average, rate):
    param_new, first_new, second_new = adam_update(param, grad, first, second, rate)
    return param_new, first_new, second_new, average_rate * average + (1.0 - average_rate) * param_new


def update_kernel(
    gain_scale,
    grad_ref,
    master_ref,
    first_ref,
    second_ref,
    ema_ref,
    vec_grad_ref,
    bias_ref,
    gain_ref,
    vec_first_ref,
    vec_second_ref,
    vec_ema_ref,
    mixed_in,
    input_in,
    master_out,
    first_out,
    second_out,
    ema_out,
    copy_out,
    vec_out,
    vec_first_out,
    vec_second_out,
    vec_ema_out,
    mixed_out,
    input_out,
    vec_ref,
):
    mixed_out[...] = mixed_in[...]
    input_out[...] = input_in[...]

    @pl.when((pl.program_id(0) == 0) & (pl.program_id(1) == 0))
    def _():
        vec_ref[0:10, :] = bias_ref[...]
        vec_ref[10:12, :] = gain_ref[...]
        vec_grad = vec_grad_ref[0:VROWS, :] * gain_scale
        vec_out[...], vec_first_out[...], vec_second_out[...], vec_ema_out[...] = moved(
            vec_ref[...], vec_grad, vec_first_ref[...], vec_second_ref[...], vec_ema_ref[...], vector_rate
        )

    grad = grad_ref[...].astype(jnp.float32) * gain_scale
    result = moved(master_ref[0], grad, first_ref[0], second_ref[0], ema_ref[0], tile_rate)
    master_out[0], first_out[0], second_out[0], ema_out[0] = result
    copy_out[0] = result[0].astype(jnp.bfloat16)


def updated(
    gain_scale,
    slot_grads,
    master,
    first,
    second,
    ema,
    vec_grad,
    bias,
    gain,
    vec_first,
    vec_second,
    vec_ema,
    mixed,
    input_grad,
):
    width = master.shape[-1]
    chunk = 192
    tile = pl.BlockSpec((1, 1, chunk, width), lambda s, r: (0, s, r, 0))
    steps = width // chunk
    rows = pl.BlockSpec((mixed.shape[0] // (SLOTS * steps), width), lambda s, r: (s * steps + r, 0))

    def whole(value):
        return pl.BlockSpec(value.shape, lambda s, r: (0, 0))

    shaped = jax.ShapeDtypeStruct
    tile_shape = shaped(master.shape, jnp.float32)
    vec_shape = shaped((VROWS, width), jnp.float32)
    results = pl.pallas_call(
        functools.partial(update_kernel, gain_scale),
        grid=(SLOTS, steps),
        out_shape=(tile_shape,) * 4
        + (shaped(master.shape, jnp.bfloat16),)
        + (vec_shape,) * 4
        + (shaped(mixed.shape, mixed.dtype), shaped(input_grad.shape, input_grad.dtype)),
        in_specs=[pl.BlockSpec((1, chunk, width), lambda s, r: (s, r, 0))]
        + [tile] * 4
        + [whole(value) for value in (vec_grad, bias, gain, vec_first, vec_second, vec_ema)]
        + [rows] * 2,
        out_specs=(tile,) * 5 + (whole(vec_first),) * 4 + (rows,) * 2,
        scratch_shapes=[pltpu.VMEM((VROWS, width), jnp.float32)],
        compiler_params=pltpu.CompilerParams(vmem_limit_bytes=62 * 2**20),
        name="update",
    )(
        slot_grads,
        master,
        first,
        second,
        ema,
        vec_grad,
        bias,
        gain,
        vec_first,
        vec_second,
        vec_ema,
        mixed,
        input_grad,
    )
    return results[-2:] + results[:-2]


MESH = pl.DeviceIdType.MESH
GROUP = 32
PAIRS = TILES // 2
PLANE = 8
PIECE = 96
PAIR_TILES = ((0, 1), (2, 3), (4, 8), (5, 9), (6, 10), (7, 11))


def remote(src, dst, send, recv, device):
    return pltpu.make_async_remote_copy(
        src_ref=src, dst_ref=dst, send_sem=send, recv_sem=recv, device_id=(device,), device_id_type=MESH
    )


def place(device):
    core = lax.rem(device, 2)
    x = lax.rem(device // 2, 2)
    y = lax.rem(device // 4, 2)
    z = device // 8
    return z, y, x, core


def start(copies):
    for copy in copies:
        copy.start()


def arrive(copies):
    for copy in copies:
        copy.wait_recv()


def greet(z, in_plane):
    barrier = pltpu.get_barrier_semaphore()
    for hop in range(1, PLANE):
        other = z * PLANE + lax.rem(in_plane + hop, PLANE)
        pl.semaphore_signal(barrier, inc=1, device_id=(other,), device_id_type=MESH)
    for hop in range(1, 4):
        other = lax.rem(z + hop, 4) * PLANE + in_plane
        pl.semaphore_signal(barrier, inc=1, device_id=(other,), device_id_type=MESH)
    pl.semaphore_wait(barrier, PLANE + 2)


def along_z(z, in_plane):
    inner = (1 + z // 2) * PLANE + in_plane
    other_middle = (3 - z) * PLANE + in_plane
    outer_end = lax.rem(lax.rem(z + 3, 4) * 3, 4) * PLANE + in_plane
    return inner, other_middle, outer_end


def third(part):
    return pl.ds(256 * part, 256)


UNITS = [(0, 4, pl.ds(256 * part, 256)) for part in range(3)]
UNITS += [(2 * pair, 2, pl.ds(0, 768)) for pair in range(2, PAIRS)]
Z_PARTS = (pl.ds(0, 512), pl.ds(512, 256))


POSITIONS = [tile for pair in PAIR_TILES for tile in pair]


def slot_number(owners, tile):
    number = jnp.int32(0)
    for earlier in range(tile):
        number = number + jnp.where(owners[earlier] == owners[tile], 1, 0)
    return number

FRONT_PLAN = (
    (
        ("open",),
        ("swap", 0),
        ("sent", 0),
        ("swap", 1),
        ("choose", 0),
        ("end", 0),
        ("sent", 1),
        ("middle", 0),
        ("choose", 1),
        ("end", 1),
        ("swap", 2),
        ("total", 0),
        ("end", 3, 0),
        ("middle", 1),
        ("mid", 0),
        ("choose", 2),
        ("end", 2),
        ("end", 3, 1),
        ("far", 0),
        ("middle", 3, 0),
        ("total", 1),
        ("caps",),
        ("middle", 3, 1),
        ("end", 4, 0),
        ("mid", 1),
        ("near", 0),
        ("total", 3, 0),
        ("end", 5, 0),
        ("middle", 2),
        ("end", 4, 1),
        ("total", 3, 1),
        ("far", 1),
        ("finish", 0),
    ),
    (
        ("middle", 4, 0),
        ("total", 2),
        ("mid", 3),
        ("middle", 4, 1),
        ("end", 5, 1),
    ),
    (
        ("mid", 2),
        ("end", 6, 0),
        ("middle", 5, 0),
        ("near", 1),
        ("total", 4, 1),
        ("far", 3),
        ("finish", 1),
        ("far", 2),
        ("middle", 5, 1),
        ("end", 6, 1),
        ("total", 4, 0),
    ),
    (
        ("total", 5, 0),
        ("middle", 6, 0),
        ("mid", 4),
        ("total", 5, 1),
        ("middle", 6, 1),
    ),
    (
        ("total", 6, 1),
        ("mid", 5),
        ("near", 2),
        ("far", 4),
        ("total", 6, 0),
        ("finish", 2),
        ("keep", 0),
        ("keep", 1),
    ),
    (
        ("mid", 6),
        ("near", 3),
        ("near", 4),
        ("far", 5),
    ),
    (
        ("far", 6),
        ("finish", 4),
        ("keep", 3),
        ("finish", 3),
        ("keep", 2),
    ),
    (
        ("near", 5),
    ),
    (
        ("near", 6),
        ("finish", 5),
        ("keep", 4),
    ),
    (
        ("finish", 6),
        ("keep", 5),
    ),
)


def gather_and_forward(
    counts,
    lengths,
    owners,
    bias_ref,
    gain_ref,
    x_hbm,
    cot_hbm,
    master_hbm,
    q_ref,
    k_ref,
    v_ref,
    p_ref,
    ctx_hbm,
    x_turned_hbm,
    ctx_turned_hbm,
    hidden_hbm,
    active_hbm,
    slope_hbm,
    down_hbm,
    mixed_hbm,
    second_hbm,
    hat_hbm,
    w_out,
    inverse_ref,
    sum_ref,
    vec_ref,
    cap_ref,
    wide,
    low,
    stage_a,
    stage_b,
    stage_c,
    chosen,
    from_end,
    from_middle,
    w_buf,
    x_then_hidden,
    x_turned,
    ctx_turned,
    hidden_turned,
    ctx_ref,
    cot_then_down,
    mixed_ref,
    hat_ref,
    slope_buf,
    active_buf,
    wide_sem,
    load_sem,
    store_sem,
    half_sem,
    tile_sem,
    out_sem,
    swap_send,
    swap_recv,
    z_send,
    z_recv,
    mid_send,
    mid_recv,
    far_send,
    far_recv,
    near_send,
    near_recv,
):
    step = pl.program_id(0)
    width = 8 * PIECE
    me = lax.axis_index("dp")
    z, y, x, core = place(me)
    in_plane = lax.rem(me, PLANE)
    sibling = me + 1 - 2 * core
    x_peer = me + 2 - 4 * x
    y_peer = me + 4 - 8 * y
    z_targets = along_z(z, in_plane)
    stages = (stage_a, stage_b, stage_c)
    is_end = (z == 0) | (z == 3)
    is_middle = (z == 1) | (z == 2)

    def piece_rows(cell_core, cell_x, cell_y):
        return pl.ds(pl.multiple_of(((cell_core * 2 + cell_x) * 2 + cell_y) * PIECE, 16), PIECE)

    def wide_load(part):
        cols = third(part)
        return pltpu.make_async_copy(master_hbm.at[:, cols], wide.at[:, cols], wide_sem.at[part])

    def swap(part):
        wide_load(part).wait()
        for slot in range(SLOTS):
            master = wide[width * slot : width * (slot + 1), third(part)]
            low[slot, :, third(part)] = master.astype(jnp.bfloat16)

        def send(hop, carry):
            target = lax.rem(in_plane + hop, PLANE)
            _, ty, tx, tc = place(target)
            remote(
                low.at[:, piece_rows(tc, tx, ty), third(part)],
                stages[part].at[pl.ds(2 * in_plane, 2)],
                swap_send.at[part],
                swap_recv.at[part],
                z * PLANE + target,
            ).start()
            return carry

        lax.fori_loop(1, PLANE, send, 0)
        stages[part][pl.ds(2 * in_plane, 2)] = low[:, piece_rows(core, x, y), third(part)]
        if part == 0:
            start([load(0), load(1)])

    def swap_wait(part, sem):
        most = stages[part].at[pl.ds(0, 2 * PLANE - 2)]
        pltpu.make_async_copy(most, most, sem.at[part]).wait()

    def z_copy(unit, part, level):
        first, count, cols = UNITS[unit]
        tiles = pl.ds(first, count)
        cols = cols if count == 4 else Z_PARTS[part]
        src = w_buf.at[tiles, core, x, y, :, cols] if level == 2 else chosen.at[tiles, :, cols]
        dst = (from_end.at[tiles, :, cols], from_middle.at[tiles, :, cols], src)[level]
        at = level, unit, part
        return remote(src, dst, z_send.at[at], z_recv.at[at], z_targets[level])

    def z_parts(unit):
        return range(1 if UNITS[unit][1] == 4 else 2)

    def z_end(unit, part=0):
        @pl.when(is_end)
        def _():
            z_copy(unit, part, 0).start()

    def z_rows(unit, part):
        first, count, cols = UNITS[unit]
        return pl.ds(first, count), cols if count == 4 else Z_PARTS[part]

    def z_middle(unit, part=0):
        @pl.when(is_middle)
        def _():
            z_copy(unit, part, 0).wait_recv()
            tiles, cols = z_rows(unit, part)
            chosen[tiles, :, cols] = chosen[tiles, :, cols] + from_end[tiles, :, cols]
            z_copy(unit, part, 1).start()

    def z_total(unit, part=0):
        @pl.when(is_middle)
        def _():
            z_copy(unit, part, 1).wait_recv()
            tiles, cols = z_rows(unit, part)
            w_buf[tiles, core, x, y, :, cols] = chosen[tiles, :, cols] + from_middle[tiles, :, cols]
            z_copy(unit, part, 2).start()

    def mid_copies(unit):
        first, count, cols = UNITS[unit]
        copies = []
        for n, peer in enumerate((y_peer, x_peer)):
            spot = w_buf.at[pl.ds(first + n * count // 2, count // 2), core, x, y, :, cols]
            copies.append(remote(spot, spot, mid_send.at[unit, n], mid_recv.at[unit, n], peer))
        return copies

    def far_copies(unit):
        first, count, cols = UNITS[unit]
        half = count // 2
        by_row = w_buf.at[pl.ds(first, half), core, x, :, :, cols]
        by_column = w_buf.at[pl.ds(first + half, half), core, :, y, :, cols]
        return [
            remote(spot, spot, far_send.at[unit, n], far_recv.at[unit, n], peer)
            for n, (spot, peer) in enumerate(((by_row, x_peer), (by_column, y_peer)))
        ]

    def near_copy(unit):
        first, count, cols = UNITS[unit]
        spot = w_buf.at[pl.ds(first, count), core, :, :, :, cols]
        return remote(spot, spot, near_send.at[unit], near_recv.at[unit], sibling)

    def give_mid(unit):
        @pl.when(is_end)
        def _():
            arrive([z_copy(unit, part, 2) for part in z_parts(unit)])

        start(mid_copies(unit))

    def give_far(unit):
        arrive(mid_copies(unit))
        start(far_copies(unit))

    def give_near(unit):
        arrive(far_copies(unit))
        near_copy(unit).start()

    def finish(unit):
        near_copy(unit).wait_recv()

    def choose(part):
        swap_wait(part, swap_recv)
        for pair in range(PAIRS):
            for n, tile in enumerate(PAIR_TILES[pair]):
                owner = owners[tile]
                value = stages[part][SLOTS * lax.rem(owner, PLANE) + slot_number(owners, tile)]
                chosen[2 * pair + n, :, third(part)] = jnp.where(
                    owner // PLANE == z, value, jnp.zeros_like(value)
                )

    def load(at):
        src = (x_hbm, cot_hbm)[at]
        dst = (x_then_hidden, cot_then_down)[at]
        return pltpu.make_async_copy(src, dst, load_sem.at[at])

    def store(at):
        src, dst = (
            (hidden_turned, hidden_hbm),
            (ctx_ref, ctx_hbm),
            (hat_ref, hat_hbm),
            None,
            None,
            None,
            (x_turned, x_turned_hbm),
            (ctx_turned, ctx_turned_hbm),
        )[at]
        return pltpu.make_async_copy(src, dst, store_sem.at[at])

    def half_stores(half):
        rows = pl.ds(ROWS * half, ROWS)
        pairs = ((cot_then_down, down_hbm), (mixed_ref, mixed_hbm), (wide, second_hbm))
        return [
            pltpu.make_async_copy(src.at[rows], dst.at[rows], half_sem.at[half, at])
            for at, (src, dst) in enumerate(pairs)
        ]

    def w_store(pair):
        two = pl.ds(2 * pair, 2)
        return pltpu.make_async_copy(w_buf.at[two], w_out.at[two], out_sem.at[pair])

    def weight(at, cols=slice(None)):
        value = w_buf[at, :, :, :, :, cols]
        return value.reshape(width, value.shape[-1])

    def open_all():
        start([wide_load(part) for part in range(3)])
        sum_ref[...] = jnp.zeros_like(sum_ref)
        vec_ref[0:10, :] = bias_ref[...]
        vec_ref[10:12, :] = gain_ref[...]
        greet(z, in_plane)

    def make_caps():
        for block in range(2):
            cap_ref[block] = attention_caps(counts, lengths, block)
        load(0).wait()
        x_turned[...] = x_then_hidden[...].T
        store(6).start()

    actions = {
        "open": open_all,
        "caps": make_caps,
        "swap": swap,
        "sent": lambda part: swap_wait(part, swap_send),
        "choose": choose,
        "end": z_end,
        "middle": z_middle,
        "total": z_total,
        "mid": give_mid,
        "far": give_far,
        "near": give_near,
        "finish": finish,
        "keep": lambda pair: w_store(pair).start(),
    }

    for at, work in enumerate(FRONT_PLAN):

        @pl.when(step == at)
        def _():
            for name, *rest in work:
                actions[name](*rest)

    quad, block = step // 2, lax.rem(step, 2)
    here = pl.ds(pl.multiple_of(block * ROWS, ROWS), ROWS)

    @pl.when(step < 6)
    def _():
        attend_quad(
            quad,
            weight,
            x_then_hidden.at[here],
            vec_ref,
            cap_ref.at[block],
            q_ref,
            k_ref,
            v_ref,
            p_ref,
            ctx_ref.at[here],
        )

    @pl.when((step >= 4) & (step < 6))
    def _():
        branch = dot(ctx_ref[here, :], weight(3)) + vec_ref[2:3, :]
        hat, inverse = normalize(x_then_hidden[here, :].astype(jnp.float32) + branch)
        hat_ref[here, :] = hat.astype(jnp.bfloat16)
        inverse_ref[here, :] = inverse
        hidden = hat * vec_ref[10:11, :] + vec_ref[8:9, :]
        hidden_low = hidden.astype(jnp.bfloat16)
        x_then_hidden[here, :] = hidden_low
        hidden_turned[:, here] = hidden_low.T
        ctx_turned[:, here] = ctx_ref[here, :].T
        wide[here, :] = hidden + vec_ref[7:8, :]

    @pl.when(step == 5)
    def _():
        start([store(0), store(1), store(2), store(7)])

    turn = step - 6
    slot = lax.rem(turn, 2)

    def tile_stores(source_slot, tile):
        return [
            pltpu.make_async_copy(src.at[source_slot], dst.at[tile], tile_sem.at[source_slot, at])
            for at, (src, dst) in enumerate(((active_buf, active_hbm), (slope_buf, slope_hbm)))
        ]

    @pl.when(turn >= 2)
    def _():
        for copy in tile_stores(slot, 0):
            copy.wait()

    @pl.when(turn >= 0)
    def _():
        for half in range(2):
            rows = slice(ROWS * half, ROWS * half + ROWS)
            up = dot(x_then_hidden[rows, :], weight(4 + 2 * turn)) + vec_ref[pl.ds(3 + turn, 1), :]
            active, slope = gelu_parts(up)
            slope_buf[slot, rows, :] = slope.astype(jnp.bfloat16)
            active_buf[slot, :, rows] = active.T
            wide[rows, :] = wide[rows, :] + dot(active, weight(5 + 2 * turn))
        start(tile_stores(slot, turn))

    @pl.when(step == 9)
    def _():
        load(1).wait()
        for half in range(2):
            rows = slice(ROWS * half, ROWS * half + ROWS)
            at_row = lax.broadcasted_iota(jnp.int32, (ROWS, 1), 0) + half * ROWS
            live = passage_facts(counts, lengths, at_row)[0].astype(jnp.float32)
            hat, inverse = normalize(wide[rows, :])
            mixed = (hat * vec_ref[11:12, :] + vec_ref[9:10, :]) * live
            mixed_ref[rows, :] = mixed.astype(jnp.bfloat16)
            grad_out = cot_then_down[rows, :].astype(jnp.float32) * live
            sum_ref[11:12, :] += columns_total(grad_out * hat)
            sum_ref[9:10, :] += columns_total(grad_out)
            second = normalize_back(grad_out * vec_ref[11:12, :], hat, inverse)
            wide[rows, :] = second
            down_low = second.astype(jnp.bfloat16)
            cot_then_down[rows, :] = down_low
            sum_ref[7:8, :] += columns_total(down_low.astype(jnp.float32))
            start(half_stores(half))
        for at in range(2):
            for copy in tile_stores(at, 0):
                copy.wait()
        for pair in range(PAIRS):
            w_store(pair).wait()
        swap_wait(2, swap_send)
        for unit in range(len(UNITS)):
            for copy in mid_copies(unit) + far_copies(unit) + [near_copy(unit)]:
                copy.wait_send()

            @pl.when(is_end)
            def _():
                for part in z_parts(unit):
                    z_copy(unit, part, 0).wait_send()

            @pl.when(is_middle)
            def _():
                for part in z_parts(unit):
                    z_copy(unit, part, 1).wait_send()
                    z_copy(unit, part, 2).wait_send()

        for at in (0, 1, 2, 6, 7):
            store(at).wait()
        for copy in half_stores(0) + half_stores(1):
            copy.wait()


def gathered_and_forwarded(counts, lengths, owners, bias, gain, x, cotangent, master):
    tokens, width = x.shape
    blocks = tokens // ROWS
    low, high = jnp.bfloat16, jnp.float32
    smem = pl.BlockSpec(memory_space=pltpu.SMEM)
    any_space = pl.BlockSpec(memory_space=pl.ANY)
    dma = pltpu.SemaphoreType.DMA
    shaped = jax.ShapeDtypeStruct

    def at(step):
        step = jnp.minimum(step, 5)
        return lax.rem(step, 2), step // 2

    quad = pl.BlockSpec((ROWS, 256), at)
    rows = shaped((tokens, width), low)
    turned = shaped((width, tokens), low)
    cut = (2, 2, 2, PIECE, width)
    units = len(UNITS)
    return pl.pallas_call(
        gather_and_forward,
        grid=(10,),
        out_shape=(
            rows,
            rows,
            rows,
            shaped((blocks, HEADS, ROWS, ROWS), low),
            rows,
            turned,
            turned,
            turned,
            shaped((4, width, tokens), low),
            shaped((4, tokens, width), low),
            rows,
            rows,
            shaped((tokens, width), high),
            rows,
            shaped((TILES,) + cut, low),
            shaped((tokens, 1), high),
            shaped((16, width), high),
        ),
        in_specs=[smem] * 3
        + [pl.BlockSpec(bias.shape, lambda i: (0, 0)), pl.BlockSpec(gain.shape, lambda i: (0, 0))]
        + [any_space] * 3,
        out_specs=(quad, quad, quad, pl.BlockSpec((1, 4, ROWS, ROWS), lambda i: (*at(i), 0, 0)))
        + (any_space,) * 11
        + (
            pl.BlockSpec((tokens, 1), lambda i: (0, 0), pipeline_mode=pl.Buffered(1)),
            pl.BlockSpec((16, width), lambda i: (0, 0)),
        ),
        scratch_shapes=[
            pltpu.VMEM((VROWS, width), high),
            pltpu.VMEM((2, ROWS, ROWS), high),
            pltpu.VMEM((SLOTS * width, width), high),
            pltpu.VMEM((SLOTS, width, width), low),
            pltpu.VMEM((2 * PLANE, PIECE, 256), low),
            pltpu.VMEM((2 * PLANE, PIECE, 256), low),
            pltpu.VMEM((2 * PLANE, PIECE, 256), low),
            pltpu.VMEM((TILES, PIECE, width), low),
            pltpu.VMEM((TILES, PIECE, width), low),
            pltpu.VMEM((TILES, PIECE, width), low),
            pltpu.VMEM((TILES,) + cut, low),
            pltpu.VMEM((tokens, width), low),
            pltpu.VMEM((width, tokens), low),
            pltpu.VMEM((width, tokens), low),
            pltpu.VMEM((width, tokens), low),
            pltpu.VMEM((tokens, width), low),
            pltpu.VMEM((tokens, width), low),
            pltpu.VMEM((tokens, width), low),
            pltpu.VMEM((tokens, width), low),
            pltpu.VMEM((2, tokens, width), low),
            pltpu.VMEM((2, width, tokens), low),
            dma((3,)),
            dma((2,)),
            dma((8,)),
            dma((2, 3)),
            dma((2, 2)),
            dma((PAIRS,)),
            dma((3,)),
            dma((3,)),
            dma((3, units, 2)),
            dma((3, units, 2)),
            dma((units, 2)),
            dma((units, 2)),
            dma((units, 2)),
            dma((units, 2)),
            dma((units,)),
            dma((units,)),
        ],
        compiler_params=pltpu.CompilerParams(
            collective_id=0, has_side_effects=True, vmem_limit_bytes=63 * 2**20
        ),
        name="gather_and_forward",
    )(counts, lengths, owners, bias, gain, x, cotangent, master.reshape(SLOTS * width, width))


BACK_PLAN = (
    (),
    (),
    (
        ("core", 0),
    ),
    (),
    (
        ("core", 1),
        ("far", 0),
    ),
    (),
    (
        ("core", 2),
        ("far", 1),
    ),
    (
        ("mid", 0),
        ("far", 2),
    ),
    (),
    (
        ("core", 3),
        ("mid", 1),
        ("end", 0),
    ),
    (),
    (
        ("far", 3),
        ("end", 1),
        ("mid", 2),
    ),
    (
        ("core", 4),
        ("middle", 0),
    ),
    (),
    (
        ("middle", 1),
        ("end", 2),
        ("mid", 3),
        ("far", 4),
    ),
    (
        ("total", 0),
    ),
    (
        ("middle", 2),
        ("end", 3),
        ("total", 1),
        ("core", 5),
        ("mid", 4),
    ),
    (),
    (
        ("far", 5),
        ("end", 4),
        ("middle", 3),
        ("total", 2),
    ),
    (),
    (
        ("core", 6),
        ("total", 3),
        ("middle", 4),
        ("mid", 5),
        ("far", 6),
        ("total", 4),
        ("sum", 0),
        ("end", 5),
        ("mid", 6),
        ("middle", 5),
        ("end", 6),
        ("take", 4),
        ("take", 0),
        ("sum", 1),
        ("take", 2),
        ("take", 3),
        ("take", 1),
        ("deliver", 0),
        ("total", 5),
        ("middle", 6),
        ("sum", 2),
        ("take", 5),
        ("deliver", 1),
        ("total", 6),
        ("take", 6),
        ("deliver", 2),
        ("input", 0),
        ("input", 1),
    ),
)


def backward_and_reduce(
    owners,
    p_ref,
    q_ref,
    k_ref,
    v_ref,
    inverse_ref,
    gain_ref,
    late_ref,
    ctx_hbm,
    x_turned_hbm,
    ctx_turned_hbm,
    hidden_hbm,
    active_hbm,
    slope_hbm,
    down_hbm,
    second_hbm,
    hat_hbm,
    w_hbm,
    input_hbm,
    slot_grad,
    vec_out,
    w_part,
    acc,
    hidden_then_x,
    active_then_ctx,
    down_then_branch,
    ctx_ref,
    grad_ctx_ref,
    hat_ref,
    slope_then_query,
    up_then_key,
    value_buf,
    part,
    from_core,
    from_far,
    from_mid,
    from_end,
    from_middle,
    total,
    snap,
    outbox,
    vec_now,
    vec_in,
    holds,
    keeps,
    load_sem,
    w_sem,
    core_send,
    core_recv,
    far_send,
    far_recv,
    mid_send,
    mid_recv,
    z_send,
    z_recv,
    vec_send,
    vec_recv,
    out_send,
    out_recv,
):
    step = pl.program_id(0)
    inner = jnp.maximum(step - 4, 0)
    quad, block, pair = inner // 4, lax.rem(inner, 4) // 2, lax.rem(inner, 2)
    me = lax.axis_index("dp")
    z, y, x, core = place(me)
    in_plane = lax.rem(me, PLANE)
    sibling = me + 1 - 2 * core
    x_peer = me + 2 - 4 * x
    y_peer = me + 4 - 8 * y
    z_targets = along_z(z, in_plane)
    is_end = (z == 0) | (z == 3)
    is_middle = (z == 1) | (z == 2)

    def tiles_of(batch):
        if batch < 4:
            return w_part, 4 + 2 * batch, 2, slice(None)
        return part, 0, 4, pl.ds(256 * (batch - 4), 256)

    def halves(batch, turned):
        ref, first, count, cols = tiles_of(batch)
        return ref, pl.ds(first + turned * count // 2, count // 2), cols

    def core_copy(batch):
        ref, first, count, cols = tiles_of(batch)
        tiles = pl.ds(first, count)
        return remote(
            ref.at[tiles, 1 - core, :, :, :, cols],
            from_core.at[tiles, :, :, :, cols],
            core_send.at[batch],
            core_recv.at[batch],
            sibling,
        )

    def far_copies(batch):
        copies = []
        for turned in range(2):
            ref, tiles, cols = halves(batch, turned)
            src = ref.at[tiles, core, :, 1 - y, :, cols] if turned else ref.at[tiles, core, 1 - x, :, :, cols]
            copies.append(
                remote(
                    src,
                    from_far.at[tiles, :, :, cols],
                    far_send.at[batch, turned],
                    far_recv.at[batch, turned],
                    y_peer if turned else x_peer,
                )
            )
        return copies

    def mid_copies(batch):
        copies = []
        for turned in range(2):
            ref, tiles, cols = halves(batch, turned)
            src = ref.at[tiles, core, 1 - x, y, :, cols] if turned else ref.at[tiles, core, x, 1 - y, :, cols]
            copies.append(
                remote(
                    src,
                    from_mid.at[tiles, :, cols],
                    mid_send.at[batch, turned],
                    mid_recv.at[batch, turned],
                    x_peer if turned else y_peer,
                )
            )
        return copies

    def z_copy(batch, stage):
        ref, first, count, cols = tiles_of(batch)
        tiles = pl.ds(first, count)
        if stage == 2:
            src, dst = total.at[tiles, :, cols], total.at[tiles, :, cols]
        else:
            src = ref.at[tiles, core, x, y, :, cols]
            dst = (from_middle if stage else from_end).at[tiles, :, cols]
        return remote(src, dst, z_send.at[stage, batch], z_recv.at[stage, batch], z_targets[stage])

    def give_core(batch):
        core_copy(batch).start()

    def give_far(batch):
        core_copy(batch).wait_recv()
        ref, first, count, cols = tiles_of(batch)
        for tile in range(first, first + count):
            ref[tile, core, :, :, :, cols] = ref[tile, core, :, :, :, cols] + from_core[tile, :, :, :, cols]
        start(far_copies(batch))

    def give_mid(batch):
        arrive(far_copies(batch))
        for turned in range(2):
            ref, tiles, cols = halves(batch, turned)
            if turned:
                ref[tiles, core, :, y, :, cols] = ref[tiles, core, :, y, :, cols] + from_far[tiles, :, :, cols]
            else:
                ref[tiles, core, x, :, :, cols] = ref[tiles, core, x, :, :, cols] + from_far[tiles, :, :, cols]
        start(mid_copies(batch))

    def add_piece(batch, other):
        ref, first, count, cols = tiles_of(batch)
        tiles = pl.ds(first, count)
        return ref[tiles, core, x, y, :, cols] + other[tiles, :, cols]

    def give_end(batch):
        arrive(mid_copies(batch))
        ref, first, count, cols = tiles_of(batch)
        ref[pl.ds(first, count), core, x, y, :, cols] = add_piece(batch, from_mid)

        @pl.when(is_end)
        def _():
            z_copy(batch, 0).start()

    def give_middle(batch):
        @pl.when(is_middle)
        def _():
            z_copy(batch, 0).wait_recv()
            ref, first, count, cols = tiles_of(batch)
            ref[pl.ds(first, count), core, x, y, :, cols] = add_piece(batch, from_end)
            z_copy(batch, 1).start()

    def give_total(batch):
        @pl.when(is_middle)
        def _():
            z_copy(batch, 1).wait_recv()
            _, first, count, cols = tiles_of(batch)
            total[pl.ds(first, count), :, cols] = add_piece(batch, from_middle)
            z_copy(batch, 2).start()

    def take_total(batch):
        @pl.when(is_end)
        def _():
            z_copy(batch, 2).wait_recv()

    def deliver(third):
        cols = pl.ds(256 * third, 256)
        snap[...] = total[:, :, cols]

        def fill(at, carry):
            value = snap[holds[at]]
            outbox[third, at] = jnp.where(keeps[at] > 0, value, jnp.zeros_like(value))
            return carry

        lax.fori_loop(0, 2 * PLANE, fill, 0)

        def send(hop, carry):
            target = lax.rem(in_plane + hop, PLANE)
            remote(
                outbox.at[third, pl.ds(2 * target, 2)],
                slot_grad.at[:, core, x, y, :, cols],
                out_send.at[third],
                out_recv.at[third],
                z * PLANE + target,
            ).start()
            return carry

        lax.fori_loop(1, PLANE, send, 0)
        keep_copy(third).start()

    def keep_copy(third):
        return pltpu.make_async_copy(
            outbox.at[third, pl.ds(2 * in_plane, 2)],
            slot_grad.at[:, core, x, y, :, pl.ds(256 * third, 256)],
            load_sem.at[5 + third],
        )

    def vec_copies(stage):
        if stage < 3:
            hops = [(stage, (sibling, x_peer, y_peer)[stage])]
        else:
            hops = [
                (2 + hop, lax.rem(z + hop, 4) * PLANE + in_plane) for hop in range(1, 4)
            ]
        return [
            remote(vec_now.at[stage], vec_in.at[at], vec_send.at[at], vec_recv.at[at], device)
            for at, device in hops
        ]

    def vec_next(stage):
        arrive(vec_copies(stage))
        vec_now[stage + 1] = vec_now[stage] + vec_in[stage]
        start(vec_copies(stage + 1))

    def input_store():
        return pltpu.make_async_copy(acc, input_hbm, load_sem.at[4])

    def load(at):
        src, dst = (
            (hidden_hbm, hidden_then_x),
            (down_hbm, down_then_branch),
            (second_hbm, acc),
            (hat_hbm, hat_ref),
            None,
            None,
            None,
            None,
            (x_turned_hbm, hidden_then_x),
            (ctx_turned_hbm, active_then_ctx),
            None,
            None,
            (ctx_hbm, ctx_ref),
        )[at]
        return pltpu.make_async_copy(src, dst, load_sem.at[at])

    def tile_load(tile, side):
        src, dst = ((slope_hbm, slope_then_query), (active_hbm, active_then_ctx))[side]
        return pltpu.make_async_copy(src.at[tile], dst, load_sem.at[10 + side])

    def w_load(at):
        return pltpu.make_async_copy(w_hbm.at[at], w_part.at[at], w_sem.at[at])

    def weight(at, cols=slice(None)):
        value = w_part[at, :, :, :, :, cols]
        return value.reshape(8 * PIECE, value.shape[-1])

    def input_rows(half):
        rows = slice(ROWS * half, ROWS * half + ROWS)
        more = acc[rows, :]
        for at, buf in enumerate((slope_then_query, up_then_key, value_buf)):
            more = more + dot_back(buf[rows, :], weight(at))
        acc[rows, :] = more
        if half == 1:
            input_store().start()

    actions = {
        "core": give_core,
        "far": give_far,
        "mid": give_mid,
        "end": give_end,
        "middle": give_middle,
        "total": give_total,
        "take": take_total,
        "deliver": deliver,
        "sum": vec_next,
        "input": input_rows,
    }

    @pl.when(step == 0)
    def _():
        start([load(1), tile_load(0, 0), w_load(5), w_load(4)])
        for at in range(2 * PLANE):
            tile_here, kept = jnp.int32(0), jnp.int32(0)
            for tile in range(TILES):
                place_of = SLOTS * owners[tile] + slot_number(owners, tile)
                match = place_of == z * 2 * PLANE + at
                tile_here = tile_here + jnp.where(match, POSITIONS.index(tile), 0)
                kept = kept + jnp.where(match, 1, 0)
            holds[at] = tile_here
            keeps[at] = kept
        vec_now[0] = late_ref[...]
        greet(z, in_plane)

    def serve(points):
        for at in points:
            if BACK_PLAN[at]:

                @pl.when(step == (at // 2 if at < 8 else at - 4))
                def _():
                    for name, number in BACK_PLAN[at]:
                        actions[name](number)

    serve(range(0, 8, 2))

    @pl.when(step < 4)
    def _():
        tile_load(step, 0).wait()
        w_load(5 + 2 * step).wait()

        @pl.when(step == 0)
        def _():
            load(1).wait()
            start([load(2), tile_load(0, 1), load(0)])

        @pl.when(step < 3)
        def _():
            start([w_load(7 + 2 * step), w_load(6 + 2 * step)])

        @pl.when(step == 1)
        def _():
            load(3).start()

        @pl.when(step == 2)
        def _():
            w_load(3).start()

        @pl.when(step == 3)
        def _():
            start([load(12), w_load(0), w_load(1), w_load(2)])

        for half in range(2):
            rows = slice(ROWS * half, ROWS * half + ROWS)
            back = dot_back(down_then_branch[rows, :], weight(5 + 2 * step))
            up_low = (back * slope_then_query[rows, :].astype(jnp.float32)).astype(jnp.bfloat16)
            up_then_key[rows, :] = up_low
            vec_now[0, pl.ds(3 + step, 1), :] += columns_total(up_low.astype(jnp.float32))

        @pl.when(step < 3)
        def _():
            tile_load(step + 1, 0).start()

        w_load(4 + 2 * step).wait()

        @pl.when(step == 0)
        def _():
            load(2).wait()
            load(0).wait()

        for half in range(2):
            rows = slice(ROWS * half, ROWS * half + ROWS)
            acc[rows, :] = acc[rows, :] + dot_back(up_then_key[rows, :], weight(4 + 2 * step))

    serve(range(1, 8, 2))

    @pl.when(step < 4)
    def _():
        tile_load(step, 1).wait()
        by_down = dot(active_then_ctx[...], down_then_branch[...]).astype(jnp.bfloat16)
        w_part[5 + 2 * step] = by_down.reshape(2, 2, 2, PIECE, 8 * PIECE)

        @pl.when(step < 3)
        def _():
            tile_load(step + 1, 1).start()

        by_up = dot(hidden_then_x[...], up_then_key[...]).astype(jnp.bfloat16)
        w_part[4 + 2 * step] = by_up.reshape(2, 2, 2, PIECE, 8 * PIECE)

    @pl.when(step == 3)
    def _():
        start([load(8), load(9)])
        load(3).wait()
        w_load(3).wait()
        for half in range(2):
            rows = slice(ROWS * half, ROWS * half + ROWS)
            grad_hidden, hat = acc[rows, :], hat_ref[rows, :].astype(jnp.float32)
            vec_now[0, 10:11, :] += columns_total(grad_hidden * hat)
            vec_now[0, 8:9, :] += columns_total(grad_hidden)
            first = normalize_back(grad_hidden * gain_ref[0:1, :], hat, inverse_ref[rows, :])
            acc[rows, :] = first
            branch_low = first.astype(jnp.bfloat16)
            down_then_branch[rows, :] = branch_low
            vec_now[0, 2:3, :] += columns_total(branch_low.astype(jnp.float32))
            grad_ctx_ref[rows, :] = dot_back(branch_low, weight(3)).astype(jnp.bfloat16)

    serve(range(8, 20))

    here = pl.ds(pl.multiple_of(block * ROWS, ROWS), ROWS)
    quad_cols = pl.ds(pl.multiple_of(quad * 256, 256), 256)

    @pl.when(step == 4)
    def _():
        load(12).wait()
        for at in range(3):
            w_load(at).wait()

    pair_cols = pl.ds(pl.multiple_of(quad * 256 + pair * 128, 128), 128)
    grad_bufs = (slope_then_query, up_then_key, value_buf)

    @pl.when(step >= 4)
    def _():
        grads = attend_back_pair(
            grad_ctx_ref[here, pair_cols],
            ctx_ref[here, pair_cols],
            p_ref.at[0],
            q_ref[...],
            k_ref[...],
            v_ref[...],
        )
        for buf, grad in zip(grad_bufs, grads):
            buf[here, pair_cols] = grad
        vec_now[0, 0:1, pair_cols] += columns_total(grads[0].astype(jnp.float32))
        vec_now[0, 1:2, pair_cols] += columns_total(grads[2].astype(jnp.float32))

    @pl.when(step == 7)
    def _():
        load(8).wait()
        load(9).wait()

    @pl.when((step >= 4) & (block == 1) & (pair == 1))
    def _():
        for tile in range(4):
            if tile < 3:
                value = dot(hidden_then_x[...], grad_bufs[tile][:, quad_cols])
            else:
                value = dot(active_then_ctx[...], down_then_branch[:, quad_cols])
            value = value.astype(jnp.bfloat16).reshape(2, 2, 2, PIECE, 256)
            part[tile, :, :, :, :, quad_cols] = value


    @pl.when(step == 15)
    def _():
        start(vec_copies(0))
        for name, number in BACK_PLAN[-1]:
            actions[name](number)
        arrive(vec_copies(3))
        summed = jnp.zeros(vec_out.shape, jnp.float32)
        for origin in range(4):
            hop = lax.rem(z - origin + 4, 4)
            summed = summed + jnp.where(hop == 0, vec_now[3], vec_in[2 + jnp.maximum(hop, 1)])
        vec_out[...] = summed
        for batch in range(7):
            for copy in [core_copy(batch)] + far_copies(batch) + mid_copies(batch):
                copy.wait_send()

            @pl.when(is_end)
            def _():
                z_copy(batch, 0).wait_send()

            @pl.when(is_middle)
            def _():
                z_copy(batch, 1).wait_send()
                z_copy(batch, 2).wait_send()

        for stage in range(4):
            for copy in vec_copies(stage):
                copy.wait_send()
        input_store().wait()
        for third in range(3):
            keep_copy(third).wait()
            most = outbox.at[third, pl.ds(0, 2 * PLANE - 2)]
            pltpu.make_async_copy(most, most, out_recv.at[third]).wait()
            pltpu.make_async_copy(most, most, out_send.at[third]).wait()


def backward_and_reduced(
    owners,
    probs,
    query,
    keyed,
    valued,
    inverse,
    gain,
    late_sums,
    context,
    x_turned,
    ctx_turned,
    hidden,
    active,
    slope,
    grad_down,
    grad_second,
    hat,
    weights,
):
    tokens, width = grad_down.shape
    low, high = jnp.bfloat16, jnp.float32
    shaped = jax.ShapeDtypeStruct
    smem = pl.BlockSpec(memory_space=pltpu.SMEM)
    any_space = pl.BlockSpec(memory_space=pl.ANY)
    dma = pltpu.SemaphoreType.DMA
    once = pl.Buffered(1)

    def at(step):
        inner = jnp.maximum(step - 4, 0)
        return lax.rem(inner, 4) // 2, inner // 4 * 2 + lax.rem(inner, 2)

    pair = pl.BlockSpec((ROWS, 128), at)
    sums = pl.BlockSpec((16, width), lambda i: (0, 0))
    cut = (2, 2, 2, PIECE, width)
    input_grad, slot_grads, vector_sums = pl.pallas_call(
        backward_and_reduce,
        grid=(16,),
        out_shape=(
            shaped((tokens, width), high),
            shaped((SLOTS,) + cut, low),
            shaped((16, width), high),
        ),
        in_specs=[smem, pl.BlockSpec((1, 2, ROWS, ROWS), lambda i: (*at(i), 0, 0))]
        + [pair] * 3
        + [
            pl.BlockSpec((tokens, 1), lambda i: (0, 0), pipeline_mode=once),
            pl.BlockSpec(gain.shape, lambda i: (0, 0)),
            sums,
        ]
        + [any_space] * 10,
        out_specs=(any_space, any_space, sums),
        scratch_shapes=[
            pltpu.VMEM((TILES,) + cut, low),
            pltpu.VMEM((tokens, width), high),
            pltpu.VMEM((width, tokens), low),
            pltpu.VMEM((width, tokens), low),
            pltpu.VMEM((tokens, width), low),
            pltpu.VMEM((tokens, width), low),
            pltpu.VMEM((tokens, width), low),
            pltpu.VMEM((tokens, width), low),
            pltpu.VMEM((tokens, width), low),
            pltpu.VMEM((tokens, width), low),
            pltpu.VMEM((tokens, width), low),
            pltpu.VMEM((4,) + cut, low),
            pltpu.VMEM((TILES,) + cut[1:], low),
            pltpu.VMEM((TILES,) + cut[2:], low),
            pltpu.VMEM((TILES,) + cut[3:], low),
            pltpu.VMEM((TILES,) + cut[3:], low),
            pltpu.VMEM((TILES,) + cut[3:], low),
            pltpu.VMEM((TILES,) + cut[3:], low),
            pltpu.VMEM((TILES, PIECE, 256), low),
            pltpu.VMEM((3, 2 * PLANE, PIECE, 256), low),
            pltpu.VMEM((4, 16, width), high),
            pltpu.VMEM((6, 16, width), high),
            pltpu.SMEM((2 * PLANE,), jnp.int32),
            pltpu.SMEM((2 * PLANE,), jnp.int32),
            dma((13,)),
            dma((TILES,)),
            dma((7,)),
            dma((7,)),
            dma((7, 2)),
            dma((7, 2)),
            dma((7, 2)),
            dma((7, 2)),
            dma((3, 7)),
            dma((3, 7)),
            dma((6,)),
            dma((6,)),
            dma((3,)),
            dma((3,)),
        ],
        compiler_params=pltpu.CompilerParams(
            collective_id=1, has_side_effects=True, vmem_limit_bytes=63 * 2**20
        ),
        name="backward_and_reduce",
    )(
        owners,
        probs,
        query,
        keyed,
        valued,
        inverse,
        gain,
        late_sums,
        context,
        x_turned,
        ctx_turned,
        hidden,
        active,
        slope,
        grad_down,
        grad_second,
        hat,
        weights,
    )
    return input_grad, slot_grads.reshape(SLOTS, width, width), vector_sums


def collected_tiles(tile_low, owners, slots):
    mine = owners == lax.axis_index("dp")
    local = jnp.where(mine[:, None, None], tile_low[slots], jnp.zeros((), tile_low.dtype))
    return lax.psum(local, "dp")


def summed_over_slice(parts, vector_terms, owners, slots):
    myself = lax.axis_index("dp")

    def add(held, items):
        part, owner, slot = items
        total = lax.psum(part.astype(jnp.float32), "dp")
        here = (owner == myself) & (slot == jnp.arange(SLOTS, dtype=jnp.int32))
        return held + jnp.where(here[:, None, None], total[None], 0.0), None

    empty = jnp.zeros((SLOTS,) + parts.shape[1:], jnp.float32)
    return lax.scan(add, empty, (parts, owners, slots))[0], lax.psum(vector_terms, "dp")


def body(
    inputs,
    cotangent,
    counts,
    lengths,
    owners,
    tile_master,
    tile_first,
    tile_second,
    tile_ema,
    bias_vals,
    gain_vals,
    vector_first,
    vector_second,
    vector_ema,
):
    tokens = inputs.shape[0]
    small = lax.axis_size("dp") == GROUP
    gain_scale = float(tokens * lax.axis_size("dp")) ** (-0.5)
    if small:
        (
            query,
            keyed,
            valued,
            probs,
            context,
            x_turned,
            ctx_turned,
            hidden,
            active,
            slope,
            grad_down,
            mixed,
            grad_second,
            hat,
            weights,
            inverse,
            late_sums,
        ) = gathered_and_forwarded(
            counts,
            lengths,
            owners,
            bias_vals,
            gain_vals,
            inputs,
            cotangent,
            tile_master,
        )
        input_grad, slot_grads, full_sums = backward_and_reduced(
            owners,
            probs,
            query,
            keyed,
            valued,
            inverse,
            gain_vals,
            late_sums,
            context,
            x_turned,
            ctx_turned,
            hidden,
            active,
            slope,
            grad_down,
            grad_second,
            hat,
            weights,
        )
    else:
        slots = tile_slots(owners)
        vectors = jnp.concatenate([bias_vals, gain_vals], 0)
        weights = collected_tiles(tile_master[0].astype(jnp.bfloat16), owners, slots)
        query, keyed, valued, probs, context, hat, inverse = attended(
            counts, lengths, inputs, weights, vectors
        )
        mixed, grad_first, grad_branch, grad_context, up_grads, down_grads, late_sums = fed_forward_both(
            counts, lengths, hat, inverse, cotangent, weights, vectors
        )
        input_grad, early_grads, early_sums = attended_back(
            probs, query, keyed, valued, inputs, context, grad_context, grad_branch, grad_first, weights
        )
        parts = jnp.concatenate([early_grads, up_grads, down_grads], 0)
        slot_grads, full_sums = summed_over_slice(parts, late_sums + early_sums, owners, slots)
    return updated(
        gain_scale,
        slot_grads,
        tile_master,
        tile_first,
        tile_second,
        tile_ema,
        full_sums,
        bias_vals,
        gain_vals,
        vector_first,
        vector_second,
        vector_ema,
        mixed,
        input_grad,
    )


def solution(mesh):
    placed = (
        P("dp", None),
        P("dp", None),
        P("dp", None),
        P("dp", None),
        P(),
        P("dp", None, None, None),
        P("dp", None, None, None),
        P("dp", None, None, None),
        P("dp", None, None, None),
        P(),
        P(),
        P(),
        P(),
        P(),
    )
    return jax.shard_map(
        body,
        mesh=mesh,
        in_specs=placed,
        out_specs=(
            P("dp", None),
            P("dp", None),
            P("dp", None, None, None),
            P("dp", None, None, None),
            P("dp", None, None, None),
            P("dp", None, None, None),
            P("dp", None, None, None),
            P(),
            P(),
            P(),
            P(),
        ),
        check_vma=False,
    )
```
